32 devices in a mesh: fsdp: 8 (over y, x, core), tp: 4 (over z).
Axes of the slice: x: 2, y: 2, z: 4, core: 2. Of those that a mesh axis runs over, the one named last changes fastest.
Arguments:
- image_tokens: bfloat16 [16, 1024, 1536], P('fsdp', 'tp'), may hold values from -6 to 6
- text_tokens: bfloat16 [1280, 1536], P(('fsdp', 'tp')), may hold values from -6 to 6
- conditioning: float32 [16, 1536], P('fsdp'), may hold values from -6 to 6
- text_lengths: int32 [8, 2], P('fsdp'), may hold values from 1 to 154, as said below
- adapter_index: int32 [16], P('fsdp'), may hold values from 0 to 7
- adapters: float32 [4, 2260992], P('tp', 'fsdp'), may hold values from -0.24 to 0.24
- mod_weight: bfloat16 [2, 1536, 9216], P(None, 'fsdp', 'tp'), may hold values from -0.15625 to 0.15625
- qkv_weight: bfloat16 [2, 1536, 4608], P(None, 'fsdp', 'tp'), may hold values from -0.15625 to 0.15625
- out_weight: bfloat16 [2, 1536, 1536], P(None, 'tp', 'fsdp'), may hold values from -0.4375 to 0.4375
- fc1_weight: bfloat16 [2, 1536, 6144], P(None, 'fsdp', 'tp'), may hold values from -0.15625 to 0.15625
- fc2_weight: bfloat16 [2, 6144, 1536], P(None, 'tp', 'fsdp'), may hold values from -0.109375 to 0.109375
- image_cot: bfloat16 [16, 1024, 1536], P('fsdp', 'tp'), may hold values from -6 to 6
- text_cot: bfloat16 [1280, 1536], P(('fsdp', 'tp')), may hold values from -6 to 6
Outputs:
- image_out: bfloat16 [16, 1024, 1536], P('fsdp', 'tp')
- text_out: bfloat16 [1280, 1536], P(('fsdp', 'tp'))
- image_grad: float32 [16, 1024, 1536], P('fsdp', 'tp')
- text_grad: float32 [1280, 1536], P(('fsdp', 'tp'))
- cond_grad: float32 [16, 1536], P('fsdp')
- adapter_grad: float32 [4, 2260992], P('tp', 'fsdp')
The draws below stay inside these ranges and needn't reach their ends.
Inputs may be any that keep to these rules, and one draw needn't show every extreme that they name: `text_lengths`: each group's 2 lengths sum to 160, and its largest is exactly 154.
All inputs are finite; a program needn't handle non-finite values.
Results may differ from the reference program's by a relative error of at most 0.015.
The reference program's roundings to bfloat16 on the way count: a program that leaves them out, or rounds other values in their place, can miss the bound.
Values may be sent and summed in bfloat16 or wider, within the bound.
A program may use at most 384 MiB of HBM per device.

```python
import jax
import jax.numpy as jnp
from jax import lax

D = 1536
HEADS = 24
HD = 64
FF = 6144
IMG = 1024
TXT_MEAN = 80
TXT_MOST = 154
NAD = 8
RANK = 16
SLOTS = 2
NSEQ = 16
TXT_G = 160
TXT_ALL = 1280
NPARAM = 9043968
N_FSDP = 8
N_TP = 4


def draw_text_lengths(key, part):
    key = jax.random.fold_in(key, 11)
    move_key, place_key = jax.random.split(key)
    rest = TXT_MEAN * SLOTS - TXT_MOST
    others_count = SLOTS - 1
    base = rest // others_count
    extra = rest % others_count
    others = base + (jnp.arange(others_count) < extra).astype(jnp.int32)
    others = jnp.broadcast_to(others[None, :], (N_FSDP, others_count))
    pair_count = others_count // 2
    if pair_count > 0:
        limit = max(min(base - 1, TXT_MOST - base - 1), 0)
        moves = jax.random.randint(move_key, (N_FSDP, pair_count), -limit, limit + 1)
        delta = jnp.stack([moves, -moves], axis=2).reshape(N_FSDP, 2 * pair_count)
        if others_count > 2 * pair_count:
            delta = jnp.concatenate([delta, jnp.zeros((N_FSDP, 1), jnp.int32)], axis=1)
        others = others + delta
    place = jax.random.randint(place_key, (N_FSDP, 1), 0, SLOTS)
    slot = jnp.arange(SLOTS)[None, :]
    source = jnp.clip(jnp.where(slot > place, slot - 1, slot), 0, others_count - 1)
    values = jnp.take_along_axis(others, jnp.broadcast_to(source, (N_FSDP, SLOTS)), axis=1)
    return jnp.where(slot == place, TXT_MOST, values).astype(jnp.int32)


def with_ends(entries, key, smallest, largest):
    dims = entries.shape
    index_at = [jax.random.randint(jax.random.fold_in(key, axis), (), 0, dims[axis]) for axis in range(len(dims))]
    entries = entries.at[tuple(index_at)].set(smallest)
    longest = dims.index(max(dims))
    index_at[longest] = (index_at[longest] + 1) % dims[longest]
    return entries.at[tuple(index_at)].set(largest)


def steps_of(key, dims, cuts, low, top_value):
    def one(axis_at, blocks):
        heights = jax.random.uniform(jax.random.fold_in(jax.random.fold_in(key, 6), axis_at), (blocks,), jnp.float32, low / len(cuts), top_value / len(cuts))
        return jnp.repeat(jnp.exp(heights), dims[axis_at] // blocks).reshape((-1,) + (1,) * (len(dims) - axis_at - 1))

    loudness = one(*cuts[0])
    for cut in cuts[1:]:
        loudness = loudness * one(*cut)
    return loudness


def bell_draw(own_key, shape, deviation, most, cuts=(), kind=jnp.bfloat16):
    level = steps_of(own_key, shape, cuts, -0.22, 0.18) if cuts else 1.0
    entries = jax.random.normal(own_key, shape, jnp.float32) * deviation * level
    return jnp.minimum(jnp.maximum(entries, -most), most).astype(kind)


def setup_inputs(seed: int = 0) -> dict:
    keys = jax.random.split(jax.random.key(seed), 14)
    image_tokens = bell_draw(keys[0], (NSEQ, IMG, D), 1.0, 6.0, ((0, 8), (1, 4)))
    text_tokens = bell_draw(keys[1], (TXT_ALL, D), 1.0, 6.0, ((0, 32),))
    conditioning = bell_draw(keys[2], (NSEQ, D), 1.0, 6.0, ((0, 8),), jnp.float32)
    text_lengths = draw_text_lengths(jax.random.fold_in(keys[13], 71), 0)
    adapter_index = with_ends(jax.random.randint(keys[4], (NSEQ,), 0, NAD), jax.random.fold_in(keys[4], 1), 0, NAD - 1).astype(jnp.int32)
    adapters = bell_draw(keys[5], (N_TP, NPARAM // N_TP), 0.04, 0.24, ((0, 4), (1, 8)), jnp.float32)
    mod_weight = bell_draw(keys[6], (2, D, 6 * D), D ** -0.5, 0.15625, ((1, 8), (2, 4)))
    qkv_weight = bell_draw(keys[7], (2, D, 3 * D), D ** -0.5, 0.15625, ((1, 8), (2, 4)))
    out_weight = bell_draw(keys[8], (2, D, D), (D // 8) ** -0.5, 0.4375, ((1, 4), (2, 8)))
    fc1_weight = bell_draw(keys[9], (2, D, FF), D ** -0.5, 0.15625, ((1, 8), (2, 4)))
    fc2_weight = bell_draw(keys[10], (2, FF, D), (FF // 2) ** -0.5, 0.109375, ((1, 4), (2, 8)))
    image_cot = bell_draw(keys[11], (NSEQ, IMG, D), 1.0, 6.0, ((0, 8), (1, 4)))
    text_cot = bell_draw(keys[12], (TXT_ALL, D), 1.0, 6.0, ((0, 32),))
    return {"image_tokens": image_tokens, "text_tokens": text_tokens, "conditioning": conditioning, "text_lengths": text_lengths, "adapter_index": adapter_index, "adapters": adapters, "mod_weight": mod_weight, "qkv_weight": qkv_weight, "out_weight": out_weight, "fc1_weight": fc1_weight, "fc2_weight": fc2_weight, "image_cot": image_cot, "text_cot": text_cot}


@jax.custom_vjp
def low(v):
    return lax.optimization_barrier(v.astype(jnp.bfloat16)).astype(jnp.float32)

@jax.custom_vjp
def low_back(v):
    return v

def low_keep(v):
    return (low(v), None)

def low_pass(kept, grad):
    return (grad,)

def back_keep(v):
    return (v, None)

def back_low(kept, grad):
    return (low(grad),)
low.defvjp(low_keep, low_pass)
low_back.defvjp(back_keep, back_low)
HIGH = lax.Precision.HIGHEST

def matmul(left, right):
    return jnp.dot(left, right, precision=HIGH)

def layout(grid):
    parts = grid.shape[0]
    shapes = [(D, 6 * D), (D, 3 * D), (D, D), (D, FF), (FF, D)]
    rank_cols = NAD * RANK
    result = []
    offset = 0
    for stream in range(2):
        pairs = []
        for fan, outer in shapes:
            a_len = fan // parts * rank_cols
            left_mat = grid[:, offset:offset + a_len].reshape(fan, rank_cols)
            offset += a_len
            b_len = rank_cols * (outer // parts)
            right_mat = grid[:, offset:offset + b_len].reshape(parts, rank_cols, outer // parts)
            right_mat = jnp.transpose(right_mat, (1, 0, 2)).reshape(rank_cols, outer)
            offset += b_len
            pairs.append((left_mat, right_mat))
        result.append(pairs)
    return result

def normalize(values):
    center = values - lax.optimization_barrier(jnp.mean(values, axis=-1, keepdims=True))
    spread = lax.optimization_barrier(jnp.mean(center * center, axis=-1, keepdims=True))
    return center * lax.rsqrt(spread + 1e-06)

def adapt(inputs, weight, adapter_pair, mask):
    middle = low(low_back(matmul(inputs, adapter_pair[0]) * mask))
    return matmul(inputs, weight) + matmul(middle, adapter_pair[1])

def attend_slot(member, img_qkv, txt_qkv, segment):
    slot_rows = jnp.concatenate([lax.dynamic_index_in_dim(img_qkv, member, 0, keepdims=False), txt_qkv], axis=0)
    queries = slot_rows[:, :, 0]
    key_rows = slot_rows[:, :, 1]
    value_rows = slot_rows[:, :, 2]
    allowed = jnp.concatenate([jnp.ones((IMG,), bool), segment == member])
    scores = low_back(jnp.einsum('qhd,khd->hqk', queries, key_rows, precision=HIGH) * 0.125)
    scores = jnp.where(allowed[None, None, :], scores, -1e+30)
    row_max = lax.optimization_barrier(jnp.max(scores, axis=-1, keepdims=True))
    exponent = jnp.exp(scores - row_max)
    attention = exponent / lax.optimization_barrier(jnp.sum(exponent, axis=-1, keepdims=True))
    mixture = jnp.einsum('hqk,khd->qhd', low(attention), value_rows, precision=HIGH)
    return mixture.reshape(IMG + TXT_G, D)

def group_forward(group, weights, pieces):
    images, captions, cond_rows, lengths, picks = group
    seg_ends = jnp.cumsum(lengths)
    position = jnp.arange(TXT_G)
    segment = lax.optimization_barrier(jnp.sum((position[:, None] >= seg_ends[None, :]).astype(jnp.int32), axis=1))
    slot_ids = jnp.arange(SLOTS)
    owner_txt = (segment[:, None] == slot_ids[None, :]).astype(jnp.float32)
    owner_img = jnp.repeat(jnp.eye(SLOTS, dtype=jnp.float32), IMG, axis=0)
    owners = [owner_img, owner_txt]
    chosen = (picks[:, None] == jnp.arange(NAD)[None, :]).astype(jnp.float32)
    seq_mask = jnp.repeat(chosen, RANK, axis=1)
    token_masks = [matmul(owner_rows, seq_mask) for owner_rows in owners]
    cond_act = low(jax.nn.silu(cond_rows))
    streams = [images.reshape(SLOTS * IMG, D), captions]
    mod_w, qkv_w, out_w, fc1_w, fc2_w = weights
    mods = []
    qkvs = []
    for stream in range(2):
        modulation = low_back(adapt(cond_act, mod_w[stream], pieces[stream][0], seq_mask))
        per_token = matmul(owners[stream], modulation)
        mods.append(per_token)
        normed = normalize(streams[stream]) * (1.0 + per_token[:, D:2 * D]) + per_token[:, :D]
        qkvs.append(low(low_back(adapt(low(normed), qkv_w[stream], pieces[stream][1], token_masks[stream]))))
    img_qkv = qkvs[0].reshape(SLOTS, IMG, HEADS, 3, HD)
    txt_qkv = qkvs[1].reshape(TXT_G, HEADS, 3, HD)
    mixture = lax.map(jax.checkpoint(lambda member: attend_slot(member, img_qkv, txt_qkv, segment)), slot_ids)
    mixed_img = mixture[:, :IMG].reshape(SLOTS * IMG, D)
    mixed_txt = jnp.einsum('ts,std->td', owner_txt, mixture[:, IMG:], precision=HIGH)
    attended = [low(low_back(mixed_img)), low(low_back(mixed_txt))]
    outputs = []
    for stream in range(2):
        per_token = mods[stream]
        branch = low_back(adapt(attended[stream], out_w[stream], pieces[stream][2], token_masks[stream]))
        after = streams[stream] + per_token[:, 2 * D:3 * D] * branch
        normed = low(normalize(after) * (1.0 + per_token[:, 4 * D:5 * D]) + per_token[:, 3 * D:4 * D])
        hidden = low_back(adapt(normed, fc1_w[stream], pieces[stream][3], token_masks[stream]))
        active = low(jax.nn.gelu(hidden, approximate=True))
        feed = low_back(adapt(active, fc2_w[stream], pieces[stream][4], token_masks[stream]))
        outputs.append(after + per_token[:, 5 * D:] * feed)
    return (outputs[0].reshape(SLOTS, IMG, D), outputs[1])

def reference(image_tokens, text_tokens, conditioning, text_lengths, adapter_index, adapters, mod_weight, qkv_weight, out_weight, fc1_weight, fc2_weight, image_cot, text_cot):
    weights = tuple((w_item.astype(jnp.float32) for w_item in (mod_weight, qkv_weight, out_weight, fc1_weight, fc2_weight)))

    def forward(images, captions, cond_rows, grid):
        pieces = layout(low(grid))
        groups = (images.reshape(N_FSDP, SLOTS, IMG, D), captions.reshape(N_FSDP, TXT_G, D), cond_rows.reshape(N_FSDP, SLOTS, D), text_lengths, adapter_index.reshape(N_FSDP, SLOTS))
        out_img, out_txt = lax.map(jax.checkpoint(lambda group: group_forward(group, weights, pieces)), groups)
        return (out_img.reshape(NSEQ, IMG, D), out_txt.reshape(TXT_ALL, D))
    results, pullback = jax.vjp(forward, image_tokens.astype(jnp.float32), text_tokens.astype(jnp.float32), conditioning, adapters)
    grads = pullback((image_cot.astype(jnp.float32), text_cot.astype(jnp.float32)))
    return (results[0].astype(jnp.bfloat16), results[1].astype(jnp.bfloat16), grads[0], grads[1], grads[2], grads[3])
```

```python
import functools

import jax
import jax.numpy as jnp
from jax import lax
from jax.experimental import pallas as pl
from jax.experimental.pallas import tpu as pltpu
from jax.sharding import PartitionSpec as P

MESH = pl.DeviceIdType.MESH

def bits_of(count):
    return max(count.bit_length() - 1, 0)

def halves(width):
    tiles = width // 128
    first = (tiles + 1) // 2 * 128
    return [(0, first), (first, width - first)]

def gather_kernel(n_f, n_z, full_count, part_count, *refs):
    total = full_count + part_count
    ins, outs = refs[:total], refs[total:2 * total]
    z_send, z_recv, xy_send, xy_recv, core_send, core_recv, own_sem = refs[2 * total:]
    f = lax.axis_index("fsdp")
    z = lax.axis_index("tp")
    chip, core = f // 2, f % 2
    chips = n_f // 2
    nbits = bits_of(chips)
    partner = chip * 2 + (1 - core)

    def peer_of(mask):
        other = 0
        for bit in range(nbits):
            have = (chip // (1 << bit)) % 2
            want = 1 - have if (mask >> bit) & 1 else have
            other = other + want * (1 << bit)
        return other * 2 + core

    barrier = pltpu.get_barrier_semaphore()
    for bit in range(nbits):
        pl.semaphore_signal(barrier, inc=1, device_id=(peer_of(1 << bit), z), device_id_type=MESH)
    pl.semaphore_signal(barrier, inc=1, device_id=(partner, z), device_id_type=MESH)
    @pl.when(z > 0)
    def _():
        pl.semaphore_signal(barrier, inc=1, device_id=(f, z - 1), device_id_type=MESH)
    @pl.when(z < n_z - 1)
    def _():
        pl.semaphore_signal(barrier, inc=1, device_id=(f, z + 1), device_id_type=MESH)
    peers = nbits + 1 + (z > 0).astype(jnp.int32) + (z < n_z - 1).astype(jnp.int32)
    pl.semaphore_wait(barrier, peers)

    def width(m):
        return ins[m].shape[-1]

    def place(m, who, zz, off=0, w=None):
        w = width(m) if w is None else w
        if m < full_count:
            return outs[m].at[who, :, pl.ds(pl.multiple_of(zz * width(m) + off, 128), w)]
        if w == width(m):
            return outs[m].at[who]
        return outs[m].at[who, :, pl.ds(off, w)]

    def piece(m, off, w):
        return ins[m] if w == width(m) else ins[m].at[:, pl.ds(off, w)]

    def remote(src, dst, ssem, rsem, dev):
        return pltpu.make_async_remote_copy(src_ref=src, dst_ref=dst, send_sem=ssem, recv_sem=rsem, device_id=dev, device_id_type=MESH)

    def order_of(half):
        order = list(range(nbits))
        return order if half == 0 else order[::-1]

    def cuts(m):
        if width(m) >= 256:
            return list(enumerate(halves(width(m))))
        return [(m % 2, (0, width(m)))]

    def slot(m, zz):
        return zz if m < full_count else 0

    def xy_copy(m, zz, half, cut, mask, bit, own_piece=False):
        off, w = cut
        who = peer_of(mask)
        source = piece(m, off, w) if own_piece and mask == 0 else place(m, who, zz, off, w)
        return remote(source, place(m, who, zz, off, w),
                      xy_send.at[m, slot(m, zz), half, mask, bit], xy_recv.at[m, slot(m, zz), half, mask | (1 << bit)],
                      (peer_of(1 << bit), z))

    def xy_wait(m, zz, half, cut, mask):
        off, w = cut
        who = peer_of(mask)
        remote(place(m, who, zz, off, w), place(m, who, zz, off, w), xy_send.at[m, slot(m, zz), half, 0, 0],
               xy_recv.at[m, slot(m, zz), half, mask], (partner, z)).wait_recv()

    def core_copy(m, zz, half, cut, mask, own_piece=False):
        off, w = cut
        who = peer_of(mask)
        source = piece(m, off, w) if own_piece and mask == 0 else place(m, who, zz, off, w)
        return remote(source, place(m, who, zz, off, w),
                      core_send.at[m, slot(m, zz), half, mask], core_recv.at[m, slot(m, zz), half, mask], (partner, z))

    def core_wait_recv(m, zz, half, cut, mask):
        off, w = cut
        who = peer_of(mask) - core + (1 - core)
        remote(place(m, who, zz, off, w), place(m, who, zz, off, w),
               core_send.at[m, slot(m, zz), half, mask], core_recv.at[m, slot(m, zz), half, mask], (partner, z)).wait_recv()

    def own(m):
        return pltpu.make_async_copy(ins[m], place(m, f, z), own_sem.at[m])

    def z_copy(m, zz, up, own_piece=False):
        return remote(ins[m] if own_piece else place(m, f, zz), place(m, f, zz), z_send.at[m, zz, up], z_recv.at[m, zz], (f, z + 1 if up else z - 1))

    def launch(m, zz, own_piece=False):
        for half, cut in cuts(m):
            for bit in order_of(half):
                xy_copy(m, zz, half, cut, 0, bit, own_piece).start()
            core_copy(m, zz, half, cut, 0, own_piece).start()

    def masks_in_order(half):
        order = order_of(half)
        def rank(mask):
            return [1 if (mask >> b) & 1 else 0 for b in reversed(order)]
        return sorted(range(1, 1 << nbits), key=rank)

    def forward(m, zz):
        for half, cut in cuts(m):
            order = order_of(half)
            for mask in masks_in_order(half):
                last = max(i for i, b in enumerate(order) if (mask >> b) & 1)
                if last == nbits - 1:
                    continue
                xy_wait(m, zz, half, cut, mask)
                for b in order[last + 1:]:
                    xy_copy(m, zz, half, cut, mask, b).start()
                core_copy(m, zz, half, cut, mask).start()

    def finish(m, zz):
        for half, cut in cuts(m):
            order = order_of(half)
            for mask in masks_in_order(half):
                last = max(i for i, b in enumerate(order) if (mask >> b) & 1)
                if last == nbits - 1:
                    xy_wait(m, zz, half, cut, mask)
                    core_copy(m, zz, half, cut, mask).start()

    def drain(m, zz):
        for half, cut in cuts(m):
            order = order_of(half)
            for mask in [0] + masks_in_order(half):
                last = max([i for i, b in enumerate(order) if (mask >> b) & 1], default=-1)
                for b in order[last + 1:]:
                    xy_copy(m, zz, half, cut, mask, b).wait_send()
                core_copy(m, zz, half, cut, mask).wait_send()
                core_wait_recv(m, zz, half, cut, mask)

    for m in range(total):
        own(m).start()
    for m in range(total):
        if m < full_count:
            @pl.when(z < n_z - 1)
            def _():
                z_copy(m, z, 1, True).start()
            @pl.when(z > 0)
            def _():
                z_copy(m, z, 0, True).start()
        launch(m, z, True)
    for m in range(full_count, total):
        forward(m, z)
    for k in range(1, n_z):
        for m in range(full_count):
            @pl.when(z - k >= 0)
            def _():
                zz = z - k
                z_copy(m, zz, 1).wait_recv()
                @pl.when(z < n_z - 1)
                def _():
                    z_copy(m, zz, 1).start()
                launch(m, zz)
            @pl.when(z + k < n_z)
            def _():
                zz = z + k
                z_copy(m, zz, 0).wait_recv()
                @pl.when(z > 0)
                def _():
                    z_copy(m, zz, 0).start()
                launch(m, zz)
            for sign in ((-1, 1) if k > 1 else (1,)):
                zz = z + sign * (k - 1)
                @pl.when((zz >= 0) & (zz < n_z))
                def _():
                    forward(m, zz)
    for m in range(full_count):
        for sign in (-1, 1):
            zz = z + sign * (n_z - 1)
            @pl.when((zz >= 0) & (zz < n_z))
            def _():
                forward(m, zz)
    for m in range(total):
        if m < full_count:
            def body(zz, _):
                finish(m, zz)
                return 0
            lax.fori_loop(0, n_z, body, 0)
        else:
            finish(m, z)
    for m in range(total):
        own(m).wait()
        if m < full_count:
            def body(zz, _):
                drain(m, zz)
                @pl.when((zz <= z) & (z < n_z - 1))
                def _():
                    z_copy(m, zz, 1).wait_send()
                @pl.when((zz >= z) & (z > 0))
                def _():
                    z_copy(m, zz, 0).wait_send()
                return 0
            lax.fori_loop(0, n_z, body, 0)
        else:
            drain(m, z)

def gather(full, part, n_f, n_z, cid=1):
    arrays = list(full) + list(part)
    total = len(arrays)
    if n_f > 8:
        rows = [lax.all_gather(a, "fsdp", axis=0, tiled=True) for a in arrays]
        return [
            lax.all_gather(a, "tp", axis=1, tiled=True) if i < len(full) else a
            for i, a in enumerate(rows)
        ]
    chips = n_f // 2
    nbits = bits_of(chips)
    shapes = [jax.ShapeDtypeStruct((n_f,) + a.shape[:-1] + (a.shape[-1] * (n_z if i < len(full) else 1),), a.dtype) for i, a in enumerate(arrays)]
    dma = pltpu.SemaphoreType.DMA
    return pl.pallas_call(
        functools.partial(gather_kernel, n_f, n_z, len(full), len(part)),
        out_shape=shapes,
        in_specs=[pl.BlockSpec(memory_space=pl.ANY)] * total,
        out_specs=[pl.BlockSpec(memory_space=pl.ANY)] * total,
        scratch_shapes=[
            dma((total, n_z, 2)), dma((total, n_z)),
            dma((total, n_z, 2, chips, max(nbits, 1))), dma((total, n_z, 2, chips)),
            dma((total, n_z, 2, chips)), dma((total, n_z, 2, chips)), dma((total,)),
        ],
        compiler_params=pltpu.CompilerParams(collective_id=cid, has_side_effects=True),
        name="weight_gather",
    )(*arrays)

def dots(left, right, lc, rc):
    return lax.dot_general(left, right, (((lc,), (rc,)), ((), ())), preferred_element_type=jnp.float32)

def attend_kernel(hd, bq, img_ref, txt_ref, bias_ref, oi_ref, ot_ref, lse_ref):
    img_n, txt_n = img_ref.shape[0], txt_ref.shape[0]
    heads = img_ref.shape[1] // (3 * hd)
    bias = bias_ref[...]
    for h in range(heads):
        base = 3 * hd * h
        ki = img_ref[:, base + hd:base + 2 * hd]
        vi = img_ref[:, base + 2 * hd:base + 3 * hd]
        kt = txt_ref[:, base + hd:base + 2 * hd]
        vt = txt_ref[:, base + 2 * hd:base + 3 * hd]

        def block(q):
            q = q * jnp.bfloat16(0.125)
            si = dots(ki, q, 1, 1)
            st = dots(kt, q, 1, 1) + bias
            top = jnp.maximum(jnp.max(si, axis=0, keepdims=True), jnp.max(st, axis=0, keepdims=True))
            ei = jnp.exp(si - top)
            et = jnp.exp(st - top)
            total = jnp.sum(ei, axis=0, keepdims=True) + jnp.sum(et, axis=0, keepdims=True)
            o = dots(vi, ei.astype(jnp.bfloat16), 0, 0) + dots(vt, et.astype(jnp.bfloat16), 0, 0)
            return (o / total).T.astype(jnp.bfloat16), top + jnp.log(total)

        for i in range(img_n // bq):
            o, lse = block(img_ref[i * bq:(i + 1) * bq, base:base + hd])
            oi_ref[i * bq:(i + 1) * bq, h * hd:(h + 1) * hd] = o
            lse_ref[0, h:h + 1, i * bq:(i + 1) * bq] = lse
        o, lse = block(txt_ref[:, base:base + hd])
        ot_ref[:, h * hd:(h + 1) * hd] = o
        lse_ref[0, h:h + 1, img_n:img_n + txt_n] = lse

def attend(img, txt, bias, hd, bq=512):
    img_n, cols = img.shape
    txt_n = txt.shape[0]
    pairs = cols // (6 * hd)
    return pl.pallas_call(
        functools.partial(attend_kernel, hd, bq),
        grid=(pairs,),
        in_specs=[
            pl.BlockSpec((img_n, 6 * hd), lambda i: (0, i)),
            pl.BlockSpec((txt_n, 6 * hd), lambda i: (0, i)),
            pl.BlockSpec((txt_n, 1), lambda i: (0, 0)),
        ],
        out_specs=[
            pl.BlockSpec((img_n, 2 * hd), lambda i: (0, i)),
            pl.BlockSpec((txt_n, 2 * hd), lambda i: (0, i)),
            pl.BlockSpec((1, 2, img_n + txt_n), lambda i: (i, 0, 0)),
        ],
        out_shape=[
            jax.ShapeDtypeStruct((img_n, pairs * 2 * hd), jnp.bfloat16),
            jax.ShapeDtypeStruct((txt_n, pairs * 2 * hd), jnp.bfloat16),
            jax.ShapeDtypeStruct((pairs, 2, img_n + txt_n), jnp.float32),
        ],
        compiler_params=pltpu.CompilerParams(vmem_limit_bytes=48 * 1024 * 1024),
        name="attend",
    )(img, txt, bias)

def attend_back_kernel(hd, bq, img_ref, txt_ref, bias_ref, doi_ref, dot_ref, lse_ref, di_ref, dt_ref, acc_i, acc_t):
    img_n, txt_n = img_ref.shape[0], txt_ref.shape[0]
    heads = img_ref.shape[1] // (3 * hd)
    bias = bias_ref[...]
    for h in range(heads):
        base = 3 * hd * h
        ki = img_ref[:, base + hd:base + 2 * hd]
        vi = img_ref[:, base + 2 * hd:base + 3 * hd]
        kt = txt_ref[:, base + hd:base + 2 * hd]
        vt = txt_ref[:, base + 2 * hd:base + 3 * hd]

        def block(q, do, lse, first):
            q = q * jnp.bfloat16(0.125)
            pi = jnp.exp(dots(ki, q, 1, 1) - lse)
            pt = jnp.exp(dots(kt, q, 1, 1) + bias - lse)
            dwi = dots(vi, do, 1, 1)
            dwt = dots(vt, do, 1, 1)
            delta = jnp.sum(pi * dwi, axis=0, keepdims=True) + jnp.sum(pt * dwt, axis=0, keepdims=True)
            dsi = (pi * (dwi - delta)).astype(jnp.bfloat16)
            dst = (pt * (dwt - delta)).astype(jnp.bfloat16)
            dvi = dots(pi.astype(jnp.bfloat16), do, 1, 0)
            dvt = dots(pt.astype(jnp.bfloat16), do, 1, 0)
            dki = dots(dsi, q, 1, 0)
            dkt = dots(dst, q, 1, 0)
            if first:
                acc_i[0], acc_i[1], acc_t[0], acc_t[1] = dki, dvi, dkt, dvt
            else:
                acc_i[0] += dki
                acc_i[1] += dvi
                acc_t[0] += dkt
                acc_t[1] += dvt
            dq = dots(ki, dsi, 0, 0) + dots(kt, dst, 0, 0)
            return (dq.T * 0.125).astype(jnp.bfloat16)

        for i in range(img_n // bq):
            rows = slice(i * bq, (i + 1) * bq)
            di_ref[rows, base:base + hd] = block(
                img_ref[rows, base:base + hd], doi_ref[rows, h * hd:(h + 1) * hd], lse_ref[0, h:h + 1, rows], i == 0)
        dt_ref[:, base:base + hd] = block(
            txt_ref[:, base:base + hd], dot_ref[:, h * hd:(h + 1) * hd], lse_ref[0, h:h + 1, img_n:img_n + txt_n], False)
        di_ref[:, base + hd:base + 2 * hd] = acc_i[0].astype(jnp.bfloat16)
        di_ref[:, base + 2 * hd:base + 3 * hd] = acc_i[1].astype(jnp.bfloat16)
        dt_ref[:, base + hd:base + 2 * hd] = acc_t[0].astype(jnp.bfloat16)
        dt_ref[:, base + 2 * hd:base + 3 * hd] = acc_t[1].astype(jnp.bfloat16)

def attend_back(img, txt, bias, doi, dot, lse, hd, bq=512):
    img_n, cols = img.shape
    txt_n = txt.shape[0]
    pairs = cols // (6 * hd)
    wide = pl.BlockSpec((img_n, 6 * hd), lambda i: (0, i))
    wide_t = pl.BlockSpec((txt_n, 6 * hd), lambda i: (0, i))
    return pl.pallas_call(
        functools.partial(attend_back_kernel, hd, bq),
        grid=(pairs,),
        in_specs=[
            wide, wide_t,
            pl.BlockSpec((txt_n, 1), lambda i: (0, 0)),
            pl.BlockSpec((img_n, 2 * hd), lambda i: (0, i)),
            pl.BlockSpec((txt_n, 2 * hd), lambda i: (0, i)),
            pl.BlockSpec((1, 2, img_n + txt_n), lambda i: (i, 0, 0)),
        ],
        out_specs=[wide, wide_t],
        out_shape=[jax.ShapeDtypeStruct(img.shape, jnp.bfloat16), jax.ShapeDtypeStruct(txt.shape, jnp.bfloat16)],
        scratch_shapes=[pltpu.VMEM((2, img_n, hd), jnp.float32), pltpu.VMEM((2, txt_n, hd), jnp.float32)],
        compiler_params=pltpu.CompilerParams(vmem_limit_bytes=48 * 1024 * 1024),
        name="attend_back",
    )(img, txt, bias, doi, dot, lse)

HD = 64
FF = 6144
NAD = 8
RANK = 16
EPS = 1e-06
HIGH = lax.Precision.HIGHEST
F32 = jnp.float32
BF16 = jnp.bfloat16
BOTH = ("fsdp", "tp")


def matmul(left, right):
    return jnp.dot(left, right, preferred_element_type=F32)


def exact(left, right):
    return jnp.dot(left, right, precision=HIGH, preferred_element_type=F32)


def inner_left(left, right):
    return lax.dot_general(left, right, (((0,), (0,)), ((), ())), preferred_element_type=F32)


def inner_right(left, right):
    return lax.dot_general(
        left, right, (((left.ndim - 1,), (right.ndim - 1,)), ((), ())), preferred_element_type=F32
    )


def layer_norm(values):
    center = values - jnp.mean(values, axis=-1, keepdims=True)
    inverse = lax.rsqrt(jnp.mean(center * center, axis=-1, keepdims=True) + EPS)
    return (center * inverse, inverse)


def norm_back(grad_normed, normed, inverse, scale):
    grad_hat = grad_normed * (1.0 + scale)
    return inverse * (
        grad_hat
        - jnp.mean(grad_hat, axis=-1, keepdims=True)
        - normed * jnp.mean(grad_hat * normed, axis=-1, keepdims=True)
    )


def gelu(value):
    return jax.nn.gelu(value, approximate=True)


def gelu_back(value, grad):
    return jax.vjp(gelu, value)[1](grad)[0]


def shards(
    image_tokens,
    text_tokens,
    conditioning,
    text_lengths,
    adapter_index,
    adapters,
    mod_weight,
    qkv_weight,
    out_weight,
    fc1_weight,
    fc2_weight,
    image_cot,
    text_cot,
):
    n_f, n_z = lax.axis_size("fsdp"), lax.axis_size("tp")
    f, z = lax.axis_index("fsdp"), lax.axis_index("tp")
    core = f % 2
    slots, quarter, width = image_tokens.shape
    txt_local = text_tokens.shape[0]
    txt_group = txt_local * n_z
    img_half = 2 * quarter
    img_n = 2 * img_half
    cols = [6 * width, 3 * width, width, FF, width]
    fans = [width, width, width, width, FF]

    def round_pairs(r):
        pairs = []
        for fa in range(n_f):
            for t in range(n_z):
                there = (fa // 2 * 2 + t // 2) * n_z + 2 * (fa % 2) + (r ^ (t % 2))
                pairs.append((fa * n_z + t, there))
        return pairs

    low_bit = z % 2

    def pick(stack, bit):
        return lax.dynamic_index_in_dim(stack, bit, 0, keepdims=False)

    def flip(r):
        return low_bit if r == 0 else 1 - low_bit

    def to_chip(parts):
        got = [lax.ppermute(parts[r], BOTH, round_pairs(r)) for r in range(2)]
        return jnp.where(low_bit == 0, got[0], got[1]), jnp.where(low_bit == 0, got[1], got[0])

    def from_chip(pieces):
        got = []
        for r in range(2):
            mine = jnp.where(flip(r) == 0, pieces[0], pieces[1])
            got.append(lax.ppermute(mine, BOTH, [(b, a) for a, b in round_pairs(r)]))
        return jnp.where(low_bit == 0, got[0], got[1]), jnp.where(low_bit == 0, got[1], got[0])

    def reshard(values):
        return jnp.concatenate(to_chip([pick(values, flip(r)) for r in range(2)]), axis=0)

    def unshard(values):
        return jnp.stack(from_chip([values[:quarter], values[quarter:]]))

    def swap_core(values):
        return lax.ppermute(values, "fsdp", [(i, i ^ 1) for i in range(n_f)])

    def by_core(mine, other, axis):
        first = jnp.where(core == 0, mine, other)
        second = jnp.where(core == 0, other, mine)
        return jnp.concatenate([first, second], axis=axis)

    def to_heads(values):
        half = values.shape[1] // 2
        low, high = values[:, :half], values[:, half:]
        mine = jnp.where(core == 0, low, high)
        return by_core(mine, swap_core(jnp.where(core == 0, high, low)), 0)

    def to_tokens(values):
        low, high = values[:img_half], values[img_half:]
        mine = jnp.where(core == 0, low, high)
        return by_core(mine, swap_core(jnp.where(core == 0, high, low)), 1)

    out_t = jnp.swapaxes(out_weight, 1, 2)
    fc2_t = jnp.swapaxes(fc2_weight, 1, 2)
    local = [qkv_weight, out_t, fc1_weight, fc2_t]
    adapter_rows = adapters.astype(BF16).reshape(-1, 128)
    got = gather([w[0] for w in local], [w[1] for w in local] + [adapter_rows], n_f, n_z)
    got = [g.reshape(-1, g.shape[-1]) for g in got]
    img_w, txt_w, row = got[:4], got[4:8], got[8]
    x_img = reshard(image_tokens).astype(F32)
    g_img = reshard(image_cot).astype(F32)
    x_txt = text_tokens.astype(F32)
    g_txt = text_cot.astype(F32)

    seg_ends = jnp.cumsum(text_lengths[0])
    slot_ids = jnp.arange(slots)

    def owner_of(position):
        segment = jnp.sum((position[:, None] >= seg_ends[None, :]).astype(jnp.int32), axis=1)
        return (segment[:, None] == slot_ids[None, :]).astype(F32)

    owner_group = owner_of(jnp.arange(txt_group))
    owner_local = owner_of(z * txt_local + jnp.arange(txt_local))
    txt_mask = jnp.repeat(owner_group, RANK, axis=1)
    seq_mask = jnp.repeat(jnp.eye(slots, dtype=F32), RANK, axis=1)

    def by_group(mine, other):
        return by_core(mine, other, 0)

    column_picks = by_group(adapter_index, swap_core(adapter_index))
    column_count = 2 * slots
    one_hot = (
        jnp.arange(NAD * RANK)[:, None]
        == (column_picks[:, None] * RANK + jnp.arange(RANK)[None, :]).reshape(1, -1)
    ).astype(F32)
    own_picks = adapter_index
    own_hot = lax.dynamic_slice_in_dim(one_hot, core * slots * RANK, slots * RANK, 1)

    a_rows = [[None] * 5 for stream in range(2)]
    b_rows = [[None] * 5 for stream in range(2)]
    offset = 0
    for stream in range(2):
        for index in range(5):
            count = fans[index] // n_z
            a_rows[stream][index] = row[offset : offset + count]
            offset += count
            count = cols[index] // n_z
            b_rows[stream][index] = row[offset : offset + count]
            offset += count

    def b_pick(stream, index, pick_index):
        part = b_rows[stream][index]
        count = part.shape[0] // NAD
        return lax.dynamic_slice_in_dim(part, pick_index * count, count, 0).reshape(RANK, -1)

    def a_pick(rows, hot):
        return inner_right(hot.T.astype(BF16), rows).astype(BF16)

    img_a = a_pick(jnp.concatenate(a_rows[0], axis=0), one_hot)
    fan_share = sum(fans) // n_z
    img_a = img_a.reshape(column_count, RANK, fan_share)
    img_b = [
        jnp.concatenate([b_pick(0, index, column_picks[s]) for index in range(1, 5)], axis=1)
        for s in range(column_count)
    ]
    img_msg = jnp.concatenate([img_a, jnp.stack(img_b)], axis=2)
    txt_rows = jnp.concatenate(
        [a_rows[0][0], a_rows[1][0], a_rows[1][1], a_rows[1][3]], axis=0
    )
    txt_a = a_pick(txt_rows, own_hot).reshape(slots, RANK, -1)
    txt_b_own = [
        [b_pick(stream, index, own_picks[s]) for s in range(slots)]
        for stream, index in [(0, 0), (1, 0), (1, 1), (1, 2), (1, 3), (1, 4)]
    ]
    txt_b_own = [jnp.concatenate(parts, axis=0) for parts in txt_b_own]
    txt_a_own = a_pick(jnp.concatenate([a_rows[1][2], a_rows[1][4]], axis=0), own_hot)
    txt_msg = jnp.concatenate(
        [txt_a.reshape(slots * RANK, -1), txt_b_own[3], txt_b_own[5]], axis=1
    )
    img_got = lax.all_to_all(img_msg, "tp", 0, 0, tiled=False)
    txt_got = lax.all_gather(txt_msg, "tp", axis=0, tiled=False)

    def join(part):
        return jnp.swapaxes(part, 0, 1).reshape(part.shape[1], -1)

    img_pairs = []
    offset, b_offset = 0, fan_share
    for index in range(5):
        count = fans[index] // n_z
        a_full = join(img_got[:, :, offset : offset + count])
        offset += count
        if index == 0:
            img_pairs.append(None)
            continue
        count = cols[index] // n_z
        b_full = join(img_got[:, :, b_offset : b_offset + count])
        b_offset += count
        img_pairs.append((a_full, b_full))
    txt_full = []
    offset = 0
    for count in [width // n_z] * 6:
        txt_full.append(join(txt_got[:, :, offset : offset + count]))
        offset += count
    mod_a = [txt_full[0], txt_full[1]]
    mod_b = [txt_b_own[0], txt_b_own[1]]
    txt_pairs = [
        None,
        (txt_full[2], txt_b_own[2]),
        (txt_a_own[:, : width // n_z], txt_full[4]),
        (txt_full[3], txt_b_own[4]),
        (txt_a_own[:, width // n_z :], txt_full[5]),
    ]

    k_local = mod_weight.shape[1]
    cond_act = jax.nn.silu(conditioning).astype(BF16)
    cond_all = lax.all_gather(cond_act, "fsdp", axis=0, tiled=True)
    cond_slice = lax.dynamic_slice_in_dim(cond_all, f * k_local, k_local, 1)
    mod_part = jnp.stack([matmul(cond_slice, mod_weight[stream]) for stream in range(2)], axis=1)
    mod_part = lax.psum_scatter(mod_part, "fsdp", scatter_dimension=0, tiled=True)
    mod_mid = []
    mod_terms = []
    for stream in range(2):
        middle = (inner_right(cond_act, mod_a[stream]) * seq_mask).astype(BF16)
        mod_mid.append(middle)
        mod_terms.append(mod_part[:, stream] + matmul(middle, mod_b[stream]))
    mods = lax.all_gather(jnp.stack(mod_terms, axis=1), "tp", axis=2, tiled=True)
    img_mods = by_group(mods[:, 0], swap_core(mods[:, 0]))
    img_mod = lax.dynamic_slice_in_dim(img_mods, z, 1, 0)
    txt_mods = mods[:, 1]

    def stretch(stream, index):
        if stream == 0:
            return img_mod[:, index * width : (index + 1) * width]
        return exact(owner_local, txt_mods[:, index * width : (index + 1) * width])

    def collapse(stream, values):
        if stream == 0:
            return jnp.sum(values, axis=0, keepdims=True)
        return exact(owner_local.T, values)

    def share(values):
        return lax.all_gather(values, "tp", axis=0, tiled=True)

    def give(values):
        return lax.psum_scatter(values, "tp", scatter_dimension=0, tiled=True)

    def mine(values):
        return lax.dynamic_slice_in_dim(values, z * txt_local, txt_local, 0)

    def lanes(values):
        count = values.shape[1] // n_z
        return lax.dynamic_slice_in_dim(values, z * count, count, 1)

    inputs = [x_img, x_txt]
    cots = [g_img, g_txt]
    norm_one = [layer_norm(values) for values in inputs]
    heads_in = [
        (norm_one[s][0] * (1.0 + stretch(s, 1)) + stretch(s, 0)).astype(BF16) for s in range(2)
    ]

    def project(values, weight, pair, mask, flipped):
        middle = inner_right(values, pair[0])
        if mask is not None:
            middle = middle * mask
        middle = middle.astype(BF16)
        main = inner_right(values, weight) if flipped else matmul(values, weight)
        return middle, main + matmul(middle, pair[1])

    txt_in = share(heads_in[1])
    txt_qkv_mid, txt_qkv = project(txt_in, txt_w[0], txt_pairs[1], txt_mask, False)
    img_qkv_mid, img_qkv = project(heads_in[0], img_w[0], img_pairs[1], None, False)
    txt_qkv, img_qkv = txt_qkv.astype(BF16), img_qkv.astype(BF16)
    img_heads = to_heads(img_qkv)
    txt_heads = jnp.concatenate(to_chip([txt_qkv, txt_qkv]), axis=1)
    lengths = by_group(text_lengths[0:1], swap_core(text_lengths[0:1]))
    chip_lengths = jnp.cumsum(lax.dynamic_index_in_dim(lengths, z // slots, 0, keepdims=False))
    chip_slot = z % slots
    chip_segment = jnp.sum(
        (jnp.arange(txt_group)[:, None] >= chip_lengths[None, :]).astype(jnp.int32),
        axis=1,
        keepdims=True,
    )
    chip_owner = chip_segment == chip_slot
    bias = jnp.where(chip_owner, 0.0, -1e30).astype(F32)
    o_img, o_txt, lse = attend(img_heads, txt_heads, bias, HD)

    def txt_home(values):
        half = values.shape[1] // 2
        got = from_chip([values[:, :half], values[:, half:]])
        return jnp.where(owner_group[:, 0:1] > 0, got[0], got[1])

    attended = [to_tokens(o_img), txt_home(o_txt)]

    txt_rank = lax.psum(inner_right(attended[1], txt_pairs[2][0]), "tp")
    txt_out_mid = (txt_rank * txt_mask).astype(BF16)
    txt_branch = give(inner_right(attended[1], txt_w[1])) + matmul(
        mine(txt_out_mid), txt_pairs[2][1]
    )
    img_out_mid, img_branch = project(attended[0], img_w[1], img_pairs[2], None, True)
    branch = [img_branch, txt_branch]
    after = [inputs[s] + stretch(s, 2) * branch[s] for s in range(2)]
    norm_two = [layer_norm(values) for values in after]
    mlp_in = [
        (norm_two[s][0] * (1.0 + stretch(s, 4)) + stretch(s, 3)).astype(BF16) for s in range(2)
    ]

    txt_mlp = share(mlp_in[1])
    txt_fc1_mid, txt_pre = project(txt_mlp, txt_w[2], txt_pairs[3], txt_mask, False)
    txt_act = gelu(txt_pre).astype(BF16)
    txt_rank = lax.psum(inner_right(txt_act, txt_pairs[4][0]), "tp")
    txt_fc2_mid = (txt_rank * txt_mask).astype(BF16)
    txt_feed = give(inner_right(txt_act, txt_w[3])) + matmul(mine(txt_fc2_mid), txt_pairs[4][1])
    img_fc1_mid, img_pre = project(mlp_in[0], img_w[2], img_pairs[3], None, False)
    img_act = gelu(img_pre).astype(BF16)
    img_fc2_mid, img_feed = project(img_act, img_w[3], img_pairs[4], None, True)
    feed = [img_feed, txt_feed]
    results = [(after[s] + stretch(s, 5) * feed[s]).astype(BF16) for s in range(2)]
    image_out = unshard(results[0])

    grad_feed = [(stretch(s, 5) * cots[s]).astype(BF16) for s in range(2)]
    grads = [[None] * 5 for stream in range(2)]

    def project_back(grad, weight, pair, mask, flipped):
        middle = inner_right(grad, pair[1])
        if mask is not None:
            middle = middle * mask
        middle = middle.astype(BF16)
        main = matmul(grad, weight) if flipped else inner_right(grad, weight)
        return middle, main + matmul(middle, pair[0])

    img_back_mid, img_grad_act = project_back(grad_feed[0], img_w[3], img_pairs[4], None, True)
    grads[0][4] = (inner_left(img_back_mid, img_act), inner_left(img_fc2_mid, grad_feed[0]))
    img_grad_pre = gelu_back(img_pre, img_grad_act).astype(BF16)
    img_back_mid, img_grad_norm = project_back(img_grad_pre, img_w[2], img_pairs[3], None, False)
    grads[0][3] = (inner_left(img_back_mid, mlp_in[0]), inner_left(img_fc1_mid, img_grad_pre))

    txt_feed_full = share(grad_feed[1])
    txt_back_mid, txt_grad_act = project_back(txt_feed_full, txt_w[3], txt_pairs[4], txt_mask, True)
    grads[1][4] = (
        inner_left(txt_back_mid, txt_act),
        inner_left(txt_fc2_mid, lanes(txt_feed_full)),
    )
    txt_grad_pre = gelu_back(txt_pre, txt_grad_act).astype(BF16)
    txt_back_mid = lax.psum(inner_right(txt_grad_pre, txt_pairs[3][1]), "tp")
    txt_back_mid = (txt_back_mid * txt_mask).astype(BF16)
    grads[1][3] = (
        inner_left(txt_back_mid, lanes(txt_mlp)),
        inner_left(txt_fc1_mid, txt_grad_pre),
    )
    txt_grad_norm = give(inner_right(txt_grad_pre, txt_w[2])) + matmul(
        mine(txt_back_mid), txt_pairs[3][0]
    )
    grad_norm = [img_grad_norm, txt_grad_norm]
    mod_parts = [[None] * 6 for stream in range(2)]
    grad_after = []
    for s in range(2):
        grad_after.append(
            cots[s] + norm_back(grad_norm[s], norm_two[s][0], norm_two[s][1], stretch(s, 4))
        )
        mod_parts[s][3] = collapse(s, grad_norm[s])
        mod_parts[s][4] = collapse(s, grad_norm[s] * norm_two[s][0])
        mod_parts[s][5] = collapse(s, cots[s] * feed[s])
        mod_parts[s][2] = collapse(s, grad_after[s] * branch[s])
    grad_branch = [(stretch(s, 2) * grad_after[s]).astype(BF16) for s in range(2)]

    img_back_mid, img_grad_att = project_back(grad_branch[0], img_w[1], img_pairs[2], None, True)
    grads[0][2] = (inner_left(img_back_mid, attended[0]), inner_left(img_out_mid, grad_branch[0]))
    txt_branch_full = share(grad_branch[1])
    txt_back_mid, txt_grad_att = project_back(
        txt_branch_full, txt_w[1], txt_pairs[2], txt_mask, True
    )
    grads[1][2] = (
        inner_left(txt_back_mid, attended[1]),
        inner_left(txt_out_mid, lanes(txt_branch_full)),
    )
    txt_grad_att = txt_grad_att.astype(BF16)
    do_img = to_heads(img_grad_att.astype(BF16))
    do_txt = jnp.concatenate(to_chip([txt_grad_att, txt_grad_att]), axis=1)
    do_txt = jnp.where(chip_owner, do_txt, jnp.zeros_like(do_txt))
    d_img, d_txt = attend_back(img_heads, txt_heads, bias, do_img, do_txt, lse, HD)
    img_grad_qkv = to_tokens(d_img)
    txt_grad_qkv = txt_home(d_txt)

    img_back_mid, img_grad_norm = project_back(img_grad_qkv, img_w[0], img_pairs[1], None, False)
    grads[0][1] = (inner_left(img_back_mid, heads_in[0]), inner_left(img_qkv_mid, img_grad_qkv))
    txt_back_mid = lax.psum(inner_right(txt_grad_qkv, txt_pairs[1][1]), "tp")
    txt_back_mid = (txt_back_mid * txt_mask).astype(BF16)
    grads[1][1] = (
        inner_left(txt_back_mid, lanes(txt_in)),
        inner_left(txt_qkv_mid, txt_grad_qkv),
    )
    txt_grad_norm = give(inner_right(txt_grad_qkv, txt_w[0])) + matmul(
        mine(txt_back_mid), txt_pairs[1][0]
    )
    grad_norm = [img_grad_norm, txt_grad_norm]
    grad_inputs = []
    for s in range(2):
        grad_inputs.append(
            grad_after[s]
            + norm_back(grad_norm[s], norm_one[s][0], norm_one[s][1], stretch(s, 1))
        )
        mod_parts[s][0] = collapse(s, grad_norm[s])
        mod_parts[s][1] = collapse(s, grad_norm[s] * norm_one[s][0])
    image_grad = unshard(grad_inputs[0])

    img_dmod = jnp.concatenate(mod_parts[0], axis=1)
    img_dmod = (img_dmod + swap_core(img_dmod)).astype(BF16)
    img_dmods = lax.all_gather(img_dmod, "tp", axis=0, tiled=True)
    img_dmods = lax.dynamic_slice_in_dim(img_dmods, core * slots, slots, 0)
    img_dmods = lanes(img_dmods)
    txt_dmod = jnp.concatenate(mod_parts[1], axis=1)
    txt_dmods = lax.psum_scatter(txt_dmod, "tp", scatter_dimension=1, tiled=True).astype(BF16)
    dmods = jnp.stack([img_dmods, txt_dmods], axis=1)
    dmods_all = lax.all_gather(dmods, "fsdp", axis=0, tiled=True)
    cond_part = sum(inner_right(dmods_all[:, s], mod_weight[s]) for s in range(2))
    mod_back = [inner_right(dmods[:, s], mod_b[s]) for s in range(2)]
    cond_slices, mod_rank = lax.psum((cond_part, jnp.stack(mod_back)), "tp")
    cond_rows = lax.all_to_all(cond_slices, "fsdp", 0, 1, tiled=True)
    for s in range(2):
        back_mid = (mod_rank[s] * seq_mask).astype(BF16)
        cond_rows = cond_rows + matmul(back_mid, mod_a[s])
        grads[s][0] = (inner_left(back_mid, lanes(cond_act)), inner_left(mod_mid[s], dmods[:, s]))
    cond_grad = jax.vjp(jax.nn.silu, conditioning)[1](cond_rows)[0]

    def spread(values):
        return jnp.swapaxes(values.reshape(RANK, n_z, -1), 0, 1)

    img_parts = [spread(grads[0][index][side]) for side in range(2) for index in range(1, 5)]
    img_parts = lax.all_to_all(jnp.concatenate(img_parts, axis=2), "tp", 0, 0, tiled=False)
    img_parts = img_parts.reshape(column_count * RANK, -1)
    offset = 0
    img_rows = []
    for sizes in (fans, cols):
        for index in range(1, 5):
            count = sizes[index] // n_z
            img_rows.append(img_parts[:, offset : offset + count])
            offset += count
    flat = []
    for stream in range(2):
        for index in range(5):
            if stream == 0 and index > 0:
                part_a, part_b = img_rows[index - 1], img_rows[index + 3]
                hot = one_hot
            else:
                part_a, part_b = grads[stream][index]
                hot = own_hot
            flat.append(
                lax.dot_general(
                    part_a, hot, (((0,), (1,)), ((), ())),
                    precision=HIGH, preferred_element_type=F32,
                )
            )
            flat.append(exact(hot, part_b).reshape(-1, 128))
    total = jnp.concatenate(flat, axis=0).reshape(n_f, -1, 128)
    step = 1
    while step < n_f:
        bit = (f // step) % 2
        pairs = total.reshape((-1, 2) + total.shape[1:])
        keep = lax.dynamic_index_in_dim(pairs, bit, 1, keepdims=False)
        send = lax.dynamic_index_in_dim(pairs, 1 - bit, 1, keepdims=False)
        sent = lax.ppermute(send.astype(BF16), "fsdp", [(i, i ^ step) for i in range(n_f)])
        total = keep + sent.astype(F32)
        step *= 2
    adapter_grad = total.reshape(1, -1)
    return (image_out, results[1], image_grad, grad_inputs[1], cond_grad, adapter_grad)


def solution(mesh):
    return jax.shard_map(
        shards,
        mesh=mesh,
        in_specs=(
            P("fsdp", "tp", None),
            P(("fsdp", "tp"), None),
            P("fsdp", None),
            P("fsdp", None),
            P("fsdp"),
            P("tp", "fsdp"),
            P(None, "fsdp", "tp"),
            P(None, "fsdp", "tp"),
            P(None, "tp", "fsdp"),
            P(None, "fsdp", "tp"),
            P(None, "tp", "fsdp"),
            P("fsdp", "tp", None),
            P(("fsdp", "tp"), None),
        ),
        out_specs=(
            P("fsdp", "tp", None),
            P(("fsdp", "tp"), None),
            P("fsdp", "tp", None),
            P(("fsdp", "tp"), None),
            P("fsdp", None),
            P("tp", "fsdp"),
        ),
        check_vma=False,
    )
```

```python
import functools

import jax
import jax.numpy as jnp
from jax import lax
from jax.experimental import pallas as pl
from jax.experimental.pallas import tpu as pltpu
from jax.sharding import PartitionSpec as P

MESH = pl.DeviceIdType.MESH

def bits_of(count):
    return max(count.bit_length() - 1, 0)

def halves(width):
    tiles = width // 128
    first = (tiles + 1) // 2 * 128
    return [(0, first), (first, width - first)]

def gather_kernel(n_f, n_z, full_count, part_count, *refs):
    total = full_count + part_count
    ins, outs = refs[:total], refs[total:2 * total]
    z_send, z_recv, xy_send, xy_recv, core_send, core_recv, own_sem = refs[2 * total:]
    f = lax.axis_index("fsdp")
    z = lax.axis_index("tp")
    chip, core = f // 2, f % 2
    chips = n_f // 2
    nbits = bits_of(chips)
    partner = chip * 2 + (1 - core)

    def peer_of(mask):
        other = 0
        for bit in range(nbits):
            have = (chip // (1 << bit)) % 2
            want = 1 - have if (mask >> bit) & 1 else have
            other = other + want * (1 << bit)
        return other * 2 + core

    barrier = pltpu.get_barrier_semaphore()
    for bit in range(nbits):
        pl.semaphore_signal(barrier, inc=1, device_id=(peer_of(1 << bit), z), device_id_type=MESH)
    pl.semaphore_signal(barrier, inc=1, device_id=(partner, z), device_id_type=MESH)
    @pl.when(z > 0)
    def _():
        pl.semaphore_signal(barrier, inc=1, device_id=(f, z - 1), device_id_type=MESH)
    @pl.when(z < n_z - 1)
    def _():
        pl.semaphore_signal(barrier, inc=1, device_id=(f, z + 1), device_id_type=MESH)
    peers = nbits + 1 + (z > 0).astype(jnp.int32) + (z < n_z - 1).astype(jnp.int32)
    pl.semaphore_wait(barrier, peers)

    def width(m):
        return ins[m].shape[-1]

    def place(m, who, zz, off=0, w=None):
        w = width(m) if w is None else w
        if m < full_count:
            return outs[m].at[who, :, pl.ds(pl.multiple_of(zz * width(m) + off, 128), w)]
        if w == width(m):
            return outs[m].at[who]
        return outs[m].at[who, :, pl.ds(off, w)]

    def piece(m, off, w):
        return ins[m] if w == width(m) else ins[m].at[:, pl.ds(off, w)]

    def remote(src, dst, ssem, rsem, dev):
        return pltpu.make_async_remote_copy(src_ref=src, dst_ref=dst, send_sem=ssem, recv_sem=rsem, device_id=dev, device_id_type=MESH)

    def order_of(half):
        order = list(range(nbits))
        return order if half == 0 else order[::-1]

    def cuts(m):
        if width(m) >= 256:
            return list(enumerate(halves(width(m))))
        return [(m % 2, (0, width(m)))]

    def slot(m, zz):
        return zz if m < full_count else 0

    def xy_copy(m, zz, half, cut, mask, bit, own_piece=False):
        off, w = cut
        who = peer_of(mask)
        source = piece(m, off, w) if own_piece and mask == 0 else place(m, who, zz, off, w)
        return remote(source, place(m, who, zz, off, w),
                      xy_send.at[m, slot(m, zz), half, mask, bit], xy_recv.at[m, slot(m, zz), half, mask | (1 << bit)],
                      (peer_of(1 << bit), z))

    def xy_wait(m, zz, half, cut, mask):
        off, w = cut
        who = peer_of(mask)
        remote(place(m, who, zz, off, w), place(m, who, zz, off, w), xy_send.at[m, slot(m, zz), half, 0, 0],
               xy_recv.at[m, slot(m, zz), half, mask], (partner, z)).wait_recv()

    def core_copy(m, zz, half, cut, mask, own_piece=False):
        off, w = cut
        who = peer_of(mask)
        source = piece(m, off, w) if own_piece and mask == 0 else place(m, who, zz, off, w)
        return remote(source, place(m, who, zz, off, w),
                      core_send.at[m, slot(m, zz), half, mask], core_recv.at[m, slot(m, zz), half, mask], (partner, z))

    def core_wait_recv(m, zz, half, cut, mask):
        off, w = cut
        who = peer_of(mask) - core + (1 - core)
        remote(place(m, who, zz, off, w), place(m, who, zz, off, w),
               core_send.at[m, slot(m, zz), half, mask], core_recv.at[m, slot(m, zz), half, mask], (partner, z)).wait_recv()

    def own(m):
        return pltpu.make_async_copy(ins[m], place(m, f, z), own_sem.at[m])

    def z_copy(m, zz, up, own_piece=False):
        return remote(ins[m] if own_piece else place(m, f, zz), place(m, f, zz), z_send.at[m, zz, up], z_recv.at[m, zz], (f, z + 1 if up else z - 1))

    def launch(m, zz, own_piece=False):
        for half, cut in cuts(m):
            for bit in order_of(half):
                xy_copy(m, zz, half, cut, 0, bit, own_piece).start()
            core_copy(m, zz, half, cut, 0, own_piece).start()

    def masks_in_order(half):
        order = order_of(half)
        def rank(mask):
            return [1 if (mask >> b) & 1 else 0 for b in reversed(order)]
        return sorted(range(1, 1 << nbits), key=rank)

    def forward(m, zz):
        for half, cut in cuts(m):
            order = order_of(half)
            for mask in masks_in_order(half):
                last = max(i for i, b in enumerate(order) if (mask >> b) & 1)
                if last == nbits - 1:
                    continue
                xy_wait(m, zz, half, cut, mask)
                for b in order[last + 1:]:
                    xy_copy(m, zz, half, cut, mask, b).start()
                core_copy(m, zz, half, cut, mask).start()

    def finish(m, zz):
        for half, cut in cuts(m):
            order = order_of(half)
            for mask in masks_in_order(half):
                last = max(i for i, b in enumerate(order) if (mask >> b) & 1)
                if last == nbits - 1:
                    xy_wait(m, zz, half, cut, mask)
                    core_copy(m, zz, half, cut, mask).start()

    def drain(m, zz):
        for half, cut in cuts(m):
            order = order_of(half)
            for mask in [0] + masks_in_order(half):
                last = max([i for i, b in enumerate(order) if (mask >> b) & 1], default=-1)
                for b in order[last + 1:]:
                    xy_copy(m, zz, half, cut, mask, b).wait_send()
                core_copy(m, zz, half, cut, mask).wait_send()
                core_wait_recv(m, zz, half, cut, mask)

    for m in range(total):
        own(m).start()
    for m in range(total):
        if m < full_count:
            @pl.when(z < n_z - 1)
            def _():
                z_copy(m, z, 1, True).start()
            @pl.when(z > 0)
            def _():
                z_copy(m, z, 0, True).start()
        launch(m, z, True)
    for m in range(full_count, total):
        forward(m, z)
    for k in range(1, n_z):
        for m in range(full_count):
            @pl.when(z - k >= 0)
            def _():
                zz = z - k
                z_copy(m, zz, 1).wait_recv()
                @pl.when(z < n_z - 1)
                def _():
                    z_copy(m, zz, 1).start()
                launch(m, zz)
            @pl.when(z + k < n_z)
            def _():
                zz = z + k
                z_copy(m, zz, 0).wait_recv()
                @pl.when(z > 0)
                def _():
                    z_copy(m, zz, 0).start()
                launch(m, zz)
            for sign in ((-1, 1) if k > 1 else (1,)):
                zz = z + sign * (k - 1)
                @pl.when((zz >= 0) & (zz < n_z))
                def _():
                    forward(m, zz)
    for m in range(full_count):
        for sign in (-1, 1):
            zz = z + sign * (n_z - 1)
            @pl.when((zz >= 0) & (zz < n_z))
            def _():
                forward(m, zz)
    for m in range(total):
        if m < full_count:
            def body(zz, _):
                finish(m, zz)
                return 0
            lax.fori_loop(0, n_z, body, 0)
        else:
            finish(m, z)
    for m in range(total):
        own(m).wait()
        if m < full_count:
            def body(zz, _):
                drain(m, zz)
                @pl.when((zz <= z) & (z < n_z - 1))
                def _():
                    z_copy(m, zz, 1).wait_send()
                @pl.when((zz >= z) & (z > 0))
                def _():
                    z_copy(m, zz, 0).wait_send()
                return 0
            lax.fori_loop(0, n_z, body, 0)
        else:
            drain(m, z)

def gather(full, part, n_f, n_z, cid=1):
    arrays = list(full) + list(part)
    total = len(arrays)
    if n_f > 8:
        rows = [lax.all_gather(a, "fsdp", axis=0, tiled=True) for a in arrays]
        return [
            lax.all_gather(a, "tp", axis=1, tiled=True) if i < len(full) else a
            for i, a in enumerate(rows)
        ]
    chips = n_f // 2
    nbits = bits_of(chips)
    shapes = [jax.ShapeDtypeStruct((n_f,) + a.shape[:-1] + (a.shape[-1] * (n_z if i < len(full) else 1),), a.dtype) for i, a in enumerate(arrays)]
    dma = pltpu.SemaphoreType.DMA
    return pl.pallas_call(
        functools.partial(gather_kernel, n_f, n_z, len(full), len(part)),
        out_shape=shapes,
        in_specs=[pl.BlockSpec(memory_space=pl.ANY)] * total,
        out_specs=[pl.BlockSpec(memory_space=pl.ANY)] * total,
        scratch_shapes=[
            dma((total, n_z, 2)), dma((total, n_z)),
            dma((total, n_z, 2, chips, max(nbits, 1))), dma((total, n_z, 2, chips)),
            dma((total, n_z, 2, chips)), dma((total, n_z, 2, chips)), dma((total,)),
        ],
        compiler_params=pltpu.CompilerParams(collective_id=cid, has_side_effects=True),
        name="weight_gather",
    )(*arrays)

def dots(left, right, lc, rc):
    return lax.dot_general(left, right, (((lc,), (rc,)), ((), ())), preferred_element_type=jnp.float32)

def attend_kernel(hd, bq, img_ref, txt_ref, bias_ref, oi_ref, ot_ref, lse_ref):
    img_n, txt_n = img_ref.shape[0], txt_ref.shape[0]
    heads = img_ref.shape[1] // (3 * hd)
    bias = bias_ref[...]
    for h in range(heads):
        base = 3 * hd * h
        ki = img_ref[:, base + hd:base + 2 * hd]
        vi = img_ref[:, base + 2 * hd:base + 3 * hd]
        kt = txt_ref[:, base + hd:base + 2 * hd]
        vt = txt_ref[:, base + 2 * hd:base + 3 * hd]

        def block(q):
            q = q * jnp.bfloat16(0.125)
            si = dots(ki, q, 1, 1)
            st = dots(kt, q, 1, 1) + bias
            top = jnp.maximum(jnp.max(si, axis=0, keepdims=True), jnp.max(st, axis=0, keepdims=True))
            ei = jnp.exp(si - top)
            et = jnp.exp(st - top)
            total = jnp.sum(ei, axis=0, keepdims=True) + jnp.sum(et, axis=0, keepdims=True)
            o = dots(vi, ei.astype(jnp.bfloat16), 0, 0) + dots(vt, et.astype(jnp.bfloat16), 0, 0)
            return (o / total).T.astype(jnp.bfloat16), top + jnp.log(total)

        for i in range(img_n // bq):
            o, lse = block(img_ref[i * bq:(i + 1) * bq, base:base + hd])
            oi_ref[i * bq:(i + 1) * bq, h * hd:(h + 1) * hd] = o
            lse_ref[0, h:h + 1, i * bq:(i + 1) * bq] = lse
        o, lse = block(txt_ref[:, base:base + hd])
        ot_ref[:, h * hd:(h + 1) * hd] = o
        lse_ref[0, h:h + 1, img_n:img_n + txt_n] = lse

def attend(img, txt, bias, hd, bq=512):
    img_n, cols = img.shape
    txt_n = txt.shape[0]
    pairs = cols // (6 * hd)
    return pl.pallas_call(
        functools.partial(attend_kernel, hd, bq),
        grid=(pairs,),
        in_specs=[
            pl.BlockSpec((img_n, 6 * hd), lambda i: (0, i)),
            pl.BlockSpec((txt_n, 6 * hd), lambda i: (0, i)),
            pl.BlockSpec((txt_n, 1), lambda i: (0, 0)),
        ],
        out_specs=[
            pl.BlockSpec((img_n, 2 * hd), lambda i: (0, i)),
            pl.BlockSpec((txt_n, 2 * hd), lambda i: (0, i)),
            pl.BlockSpec((1, 2, img_n + txt_n), lambda i: (i, 0, 0)),
        ],
        out_shape=[
            jax.ShapeDtypeStruct((img_n, pairs * 2 * hd), jnp.bfloat16),
            jax.ShapeDtypeStruct((txt_n, pairs * 2 * hd), jnp.bfloat16),
            jax.ShapeDtypeStruct((pairs, 2, img_n + txt_n), jnp.float32),
        ],
        compiler_params=pltpu.CompilerParams(vmem_limit_bytes=48 * 1024 * 1024),
        name="attend",
    )(img, txt, bias)

def attend_back_kernel(hd, bq, img_ref, txt_ref, bias_ref, doi_ref, dot_ref, lse_ref, di_ref, dt_ref, acc_i, acc_t):
    img_n, txt_n = img_ref.shape[0], txt_ref.shape[0]
    heads = img_ref.shape[1] // (3 * hd)
    bias = bias_ref[...]
    for h in range(heads):
        base = 3 * hd * h
        ki = img_ref[:, base + hd:base + 2 * hd]
        vi = img_ref[:, base + 2 * hd:base + 3 * hd]
        kt = txt_ref[:, base + hd:base + 2 * hd]
        vt = txt_ref[:, base + 2 * hd:base + 3 * hd]

        def block(q, do, lse, first):
            q = q * jnp.bfloat16(0.125)
            pi = jnp.exp(dots(ki, q, 1, 1) - lse)
            pt = jnp.exp(dots(kt, q, 1, 1) + bias - lse)
            dwi = dots(vi, do, 1, 1)
            dwt = dots(vt, do, 1, 1)
            delta = jnp.sum(pi * dwi, axis=0, keepdims=True) + jnp.sum(pt * dwt, axis=0, keepdims=True)
            dsi = (pi * (dwi - delta)).astype(jnp.bfloat16)
            dst = (pt * (dwt - delta)).astype(jnp.bfloat16)
            dvi = dots(pi.astype(jnp.bfloat16), do, 1, 0)
            dvt = dots(pt.astype(jnp.bfloat16), do, 1, 0)
            dki = dots(dsi, q, 1, 0)
            dkt = dots(dst, q, 1, 0)
            if first:
                acc_i[0], acc_i[1], acc_t[0], acc_t[1] = dki, dvi, dkt, dvt
            else:
                acc_i[0] += dki
                acc_i[1] += dvi
                acc_t[0] += dkt
                acc_t[1] += dvt
            dq = dots(ki, dsi, 0, 0) + dots(kt, dst, 0, 0)
            return (dq.T * 0.125).astype(jnp.bfloat16)

        for i in range(img_n // bq):
            rows = slice(i * bq, (i + 1) * bq)
            di_ref[rows, base:base + hd] = block(
                img_ref[rows, base:base + hd], doi_ref[rows, h * hd:(h + 1) * hd], lse_ref[0, h:h + 1, rows], i == 0)
        dt_ref[:, base:base + hd] = block(
            txt_ref[:, base:base + hd], dot_ref[:, h * hd:(h + 1) * hd], lse_ref[0, h:h + 1, img_n:img_n + txt_n], False)
        di_ref[:, base + hd:base + 2 * hd] = acc_i[0].astype(jnp.bfloat16)
        di_ref[:, base + 2 * hd:base + 3 * hd] = acc_i[1].astype(jnp.bfloat16)
        dt_ref[:, base + hd:base + 2 * hd] = acc_t[0].astype(jnp.bfloat16)
        dt_ref[:, base + 2 * hd:base + 3 * hd] = acc_t[1].astype(jnp.bfloat16)

def attend_back(img, txt, bias, doi, dot, lse, hd, bq=512):
    img_n, cols = img.shape
    txt_n = txt.shape[0]
    pairs = cols // (6 * hd)
    wide = pl.BlockSpec((img_n, 6 * hd), lambda i: (0, i))
    wide_t = pl.BlockSpec((txt_n, 6 * hd), lambda i: (0, i))
    return pl.pallas_call(
        functools.partial(attend_back_kernel, hd, bq),
        grid=(pairs,),
        in_specs=[
            wide, wide_t,
            pl.BlockSpec((txt_n, 1), lambda i: (0, 0)),
            pl.BlockSpec((img_n, 2 * hd), lambda i: (0, i)),
            pl.BlockSpec((txt_n, 2 * hd), lambda i: (0, i)),
            pl.BlockSpec((1, 2, img_n + txt_n), lambda i: (i, 0, 0)),
        ],
        out_specs=[wide, wide_t],
        out_shape=[jax.ShapeDtypeStruct(img.shape, jnp.bfloat16), jax.ShapeDtypeStruct(txt.shape, jnp.bfloat16)],
        scratch_shapes=[pltpu.VMEM((2, img_n, hd), jnp.float32), pltpu.VMEM((2, txt_n, hd), jnp.float32)],
        compiler_params=pltpu.CompilerParams(vmem_limit_bytes=48 * 1024 * 1024),
        name="attend_back",
    )(img, txt, bias, doi, dot, lse)

HD = 64
FF = 6144
NAD = 8
RANK = 16
EPS = 1e-06
HIGH = lax.Precision.HIGHEST
F32 = jnp.float32
BF16 = jnp.bfloat16
BOTH = ("fsdp", "tp")


def matmul(left, right):
    return jnp.dot(left, right, preferred_element_type=F32)


def exact(left, right):
    return jnp.dot(left, right, precision=HIGH, preferred_element_type=F32)


def inner_left(left, right):
    return lax.dot_general(left, right, (((0,), (0,)), ((), ())), preferred_element_type=F32)


def inner_right(left, right):
    return lax.dot_general(
        left, right, (((left.ndim - 1,), (right.ndim - 1,)), ((), ())), preferred_element_type=F32
    )


def layer_norm(values):
    center = values - jnp.mean(values, axis=-1, keepdims=True)
    inverse = lax.rsqrt(jnp.mean(center * center, axis=-1, keepdims=True) + EPS)
    return (center * inverse, inverse)


def norm_back(grad_normed, normed, inverse, scale):
    grad_hat = grad_normed * (1.0 + scale)
    return inverse * (
        grad_hat
        - jnp.mean(grad_hat, axis=-1, keepdims=True)
        - normed * jnp.mean(grad_hat * normed, axis=-1, keepdims=True)
    )


def gelu(value):
    return jax.nn.gelu(value, approximate=True)


def gelu_back(value, grad):
    return jax.vjp(gelu, value)[1](grad)[0]


def shards(
    image_tokens,
    text_tokens,
    conditioning,
    text_lengths,
    adapter_index,
    adapters,
    mod_weight,
    qkv_weight,
    out_weight,
    fc1_weight,
    fc2_weight,
    image_cot,
    text_cot,
):
    n_f, n_z = lax.axis_size("fsdp"), lax.axis_size("tp")
    f, z = lax.axis_index("fsdp"), lax.axis_index("tp")
    core = f % 2
    slots, quarter, width = image_tokens.shape
    txt_local = text_tokens.shape[0]
    txt_group = txt_local * n_z
    img_half = 2 * quarter
    img_n = 2 * img_half
    cols = [6 * width, 3 * width, width, FF, width]
    fans = [width, width, width, width, FF]

    def round_pairs(r):
        pairs = []
        for fa in range(n_f):
            for t in range(n_z):
                there = (fa // 2 * 2 + t // 2) * n_z + 2 * (fa % 2) + (r ^ (t % 2))
                pairs.append((fa * n_z + t, there))
        return pairs

    low_bit = z % 2

    def pick(stack, bit):
        return lax.dynamic_index_in_dim(stack, bit, 0, keepdims=False)

    def flip(r):
        return low_bit if r == 0 else 1 - low_bit

    def to_chip(parts):
        got = [lax.ppermute(parts[r], BOTH, round_pairs(r)) for r in range(2)]
        return jnp.where(low_bit == 0, got[0], got[1]), jnp.where(low_bit == 0, got[1], got[0])

    def from_chip(pieces):
        got = []
        for r in range(2):
            mine = jnp.where(flip(r) == 0, pieces[0], pieces[1])
            got.append(lax.ppermute(mine, BOTH, [(b, a) for a, b in round_pairs(r)]))
        return jnp.where(low_bit == 0, got[0], got[1]), jnp.where(low_bit == 0, got[1], got[0])

    def reshard(values):
        return jnp.concatenate(to_chip([pick(values, flip(r)) for r in range(2)]), axis=0)

    def unshard(values):
        return jnp.stack(from_chip([values[:quarter], values[quarter:]]))

    def swap_core(values):
        return lax.ppermute(values, "fsdp", [(i, i ^ 1) for i in range(n_f)])

    def by_core(mine, other, axis):
        first = jnp.where(core == 0, mine, other)
        second = jnp.where(core == 0, other, mine)
        return jnp.concatenate([first, second], axis=axis)

    def z_swap(values, step):
        return lax.ppermute(values, "tp", [(i, i ^ step) for i in range(n_z)])

    def z_order(pieces):
        stack = jnp.stack(pieces)
        return [pick(stack, z ^ a) for a in range(n_z)]

    def z_gather(values):
        return z_order([values] + [z_swap(values, j) for j in range(1, n_z)])

    def z_exchange(blocks):
        return z_order([pick(blocks, z ^ j) if j == 0 else z_swap(pick(blocks, z ^ j), j) for j in range(n_z)])

    def z_scatter(values):
        count = values.shape[0] // n_z
        mine = lax.dynamic_slice_in_dim(values, z * count, count, 0)
        for j in range(1, n_z):
            part = lax.dynamic_slice_in_dim(values, (z ^ j) * count, count, 0)
            mine = mine + z_swap(part.astype(BF16), j).astype(F32)
        return mine

    def to_heads(values):
        half = values.shape[1] // 2
        low, high = values[:, :half], values[:, half:]
        mine = jnp.where(core == 0, low, high)
        return by_core(mine, swap_core(jnp.where(core == 0, high, low)), 0)

    def to_tokens(values):
        low, high = values[:img_half], values[img_half:]
        mine = jnp.where(core == 0, low, high)
        return by_core(mine, swap_core(jnp.where(core == 0, high, low)), 1)

    out_t = jnp.swapaxes(out_weight, 1, 2)
    fc2_t = jnp.swapaxes(fc2_weight, 1, 2)
    local = [qkv_weight, out_t, fc1_weight, fc2_t]
    adapter_rows = adapters.astype(BF16).reshape(-1, 128)
    got = gather([w[0] for w in local], [w[1] for w in local] + [adapter_rows], n_f, n_z)
    got = [g.reshape(-1, g.shape[-1]) for g in got]
    img_w, txt_w, row = got[:4], got[4:8], got[8]
    x_img = reshard(image_tokens).astype(F32)
    g_img = reshard(image_cot).astype(F32)
    x_txt = text_tokens.astype(F32)
    g_txt = text_cot.astype(F32)

    seg_ends = jnp.cumsum(text_lengths[0])
    slot_ids = jnp.arange(slots)

    def owner_of(position):
        segment = jnp.sum((position[:, None] >= seg_ends[None, :]).astype(jnp.int32), axis=1)
        return (segment[:, None] == slot_ids[None, :]).astype(F32)

    owner_group = owner_of(jnp.arange(txt_group))
    owner_local = owner_of(z * txt_local + jnp.arange(txt_local))
    txt_mask = jnp.repeat(owner_group, RANK, axis=1)
    txt_mask_local = jnp.repeat(owner_local, RANK, axis=1)
    rank_cols = slots * RANK
    seq_mask = jnp.repeat(jnp.eye(slots, dtype=F32), RANK, axis=1)

    def by_group(mine, other):
        return by_core(mine, other, 0)

    column_picks = by_group(adapter_index, swap_core(adapter_index))
    column_count = 2 * slots
    one_hot = (
        jnp.arange(NAD * RANK)[:, None]
        == (column_picks[:, None] * RANK + jnp.arange(RANK)[None, :]).reshape(1, -1)
    ).astype(F32)
    own_picks = adapter_index
    own_hot = lax.dynamic_slice_in_dim(one_hot, core * slots * RANK, slots * RANK, 1)

    a_rows = [[None] * 5 for stream in range(2)]
    b_rows = [[None] * 5 for stream in range(2)]
    offset = 0
    for stream in range(2):
        for index in range(5):
            count = fans[index] // n_z
            a_rows[stream][index] = row[offset : offset + count]
            offset += count
            count = cols[index] // n_z
            b_rows[stream][index] = row[offset : offset + count]
            offset += count

    def b_pick(stream, index, pick_index):
        part = b_rows[stream][index]
        count = part.shape[0] // NAD
        return lax.dynamic_slice_in_dim(part, pick_index * count, count, 0).reshape(RANK, -1)

    def a_pick(rows, hot):
        return inner_right(hot.T.astype(BF16), rows).astype(BF16)

    img_a = a_pick(jnp.concatenate(a_rows[0], axis=0), one_hot)
    fan_share = sum(fans) // n_z
    img_a = img_a.reshape(column_count, RANK, fan_share)
    img_b = [
        jnp.concatenate([b_pick(0, index, column_picks[s]) for index in range(1, 5)], axis=1)
        for s in range(column_count)
    ]
    img_msg = jnp.concatenate([img_a, jnp.stack(img_b)], axis=2)
    txt_rows = jnp.concatenate(
        [a_rows[0][0], a_rows[1][0], a_rows[1][1], a_rows[1][3]], axis=0
    )
    txt_a = a_pick(txt_rows, own_hot).reshape(slots, RANK, -1)
    txt_b_own = [
        [b_pick(stream, index, own_picks[s]) for s in range(slots)]
        for stream, index in [(0, 0), (1, 0), (1, 1), (1, 2), (1, 3), (1, 4)]
    ]
    txt_b_own = [jnp.concatenate(parts, axis=0) for parts in txt_b_own]
    txt_a_own = a_pick(jnp.concatenate([a_rows[1][2], a_rows[1][4]], axis=0), own_hot)
    txt_msg = jnp.concatenate(
        [txt_a.reshape(slots * RANK, -1), txt_b_own[3], txt_b_own[5]], axis=1
    )
    img_got = jnp.stack(z_exchange(img_msg))
    txt_got = jnp.stack(z_gather(txt_msg))

    def join(part):
        return jnp.swapaxes(part, 0, 1).reshape(part.shape[1], -1)

    img_pairs = []
    offset, b_offset = 0, fan_share
    for index in range(5):
        count = fans[index] // n_z
        a_full = join(img_got[:, :, offset : offset + count])
        offset += count
        if index == 0:
            img_pairs.append(None)
            continue
        count = cols[index] // n_z
        b_full = join(img_got[:, :, b_offset : b_offset + count])
        b_offset += count
        img_pairs.append((a_full, b_full))
    txt_full = []
    offset = 0
    for count in [width // n_z] * 6:
        txt_full.append(join(txt_got[:, :, offset : offset + count]))
        offset += count
    mod_a = [txt_full[0], txt_full[1]]
    mod_b = [txt_b_own[0], txt_b_own[1]]
    txt_pairs = [
        None,
        (txt_full[2], txt_b_own[2]),
        (txt_a_own[:, : width // n_z], txt_full[4]),
        (txt_full[3], txt_b_own[4]),
        (txt_a_own[:, width // n_z :], txt_full[5]),
    ]

    k_local = mod_weight.shape[1]
    cond_act = jax.nn.silu(conditioning).astype(BF16)
    cond_all = lax.all_gather(cond_act, "fsdp", axis=0, tiled=True)
    cond_slice = lax.dynamic_slice_in_dim(cond_all, f * k_local, k_local, 1)
    mod_part = jnp.stack([matmul(cond_slice, mod_weight[stream]) for stream in range(2)], axis=1)
    mod_part = lax.psum_scatter(mod_part, "fsdp", scatter_dimension=0, tiled=True)
    mod_mid = []
    mod_terms = []
    for stream in range(2):
        middle = (inner_right(cond_act, mod_a[stream]) * seq_mask).astype(BF16)
        mod_mid.append(middle)
        mod_terms.append(mod_part[:, stream] + matmul(middle, mod_b[stream]))
    mods = jnp.concatenate(z_gather(jnp.stack(mod_terms, axis=1)), axis=2)
    img_mods = by_group(mods[:, 0], swap_core(mods[:, 0]))
    img_mod = lax.dynamic_slice_in_dim(img_mods, z, 1, 0)
    txt_mods = mods[:, 1]

    def stretch(stream, index):
        if stream == 0:
            return img_mod[:, index * width : (index + 1) * width]
        return exact(owner_local, txt_mods[:, index * width : (index + 1) * width])

    def collapse(stream, values):
        if stream == 0:
            return jnp.sum(values, axis=0, keepdims=True)
        return exact(owner_local.T, values)

    def share(values):
        return jnp.concatenate(z_gather(values), axis=0)

    def give(values, rank_part):
        got = z_scatter(jnp.concatenate([values, rank_part], axis=1))
        return got[:, :width], (got[:, width:] * txt_mask_local).astype(BF16)

    def lanes(values):
        count = values.shape[1] // n_z
        return lax.dynamic_slice_in_dim(values, z * count, count, 1)

    inputs = [x_img, x_txt]
    cots = [g_img, g_txt]
    norm_one = [layer_norm(values) for values in inputs]
    heads_in = [
        (norm_one[s][0] * (1.0 + stretch(s, 1)) + stretch(s, 0)).astype(BF16) for s in range(2)
    ]

    def project(values, weight, pair, mask, flipped):
        middle = inner_right(values, pair[0])
        if mask is not None:
            middle = middle * mask
        middle = middle.astype(BF16)
        main = inner_right(values, weight) if flipped else matmul(values, weight)
        return middle, main + matmul(middle, pair[1])

    txt_in = share(heads_in[1])
    txt_qkv_mid, txt_qkv = project(txt_in, txt_w[0], txt_pairs[1], txt_mask, False)
    img_qkv_mid, img_qkv = project(heads_in[0], img_w[0], img_pairs[1], None, False)
    txt_qkv, img_qkv = txt_qkv.astype(BF16), img_qkv.astype(BF16)
    img_heads = to_heads(img_qkv)
    txt_heads = jnp.concatenate(to_chip([txt_qkv, txt_qkv]), axis=1)
    lengths = by_group(text_lengths[0:1], swap_core(text_lengths[0:1]))
    chip_lengths = jnp.cumsum(lax.dynamic_index_in_dim(lengths, z // slots, 0, keepdims=False))
    chip_slot = z % slots
    chip_segment = jnp.sum(
        (jnp.arange(txt_group)[:, None] >= chip_lengths[None, :]).astype(jnp.int32),
        axis=1,
        keepdims=True,
    )
    chip_owner = chip_segment == chip_slot
    bias = jnp.where(chip_owner, 0.0, -1e30).astype(F32)
    o_img, o_txt, lse = attend(img_heads, txt_heads, bias, HD)

    def txt_home(values):
        half = values.shape[1] // 2
        got = from_chip([values[:, :half], values[:, half:]])
        return jnp.where(owner_group[:, 0:1] > 0, got[0], got[1])

    attended = [to_tokens(o_img), txt_home(o_txt)]

    txt_branch, txt_out_mid = give(
        inner_right(attended[1], txt_w[1]), inner_right(attended[1], txt_pairs[2][0])
    )
    txt_branch = txt_branch + matmul(txt_out_mid, txt_pairs[2][1])
    img_out_mid, img_branch = project(attended[0], img_w[1], img_pairs[2], None, True)
    branch = [img_branch, txt_branch]
    after = [inputs[s] + stretch(s, 2) * branch[s] for s in range(2)]
    norm_two = [layer_norm(values) for values in after]
    mlp_in = [
        (norm_two[s][0] * (1.0 + stretch(s, 4)) + stretch(s, 3)).astype(BF16) for s in range(2)
    ]

    txt_mlp = share(jnp.concatenate([mlp_in[1], txt_out_mid], axis=1))
    txt_mlp, txt_out_mid = txt_mlp[:, :width], txt_mlp[:, width:]
    txt_fc1_mid, txt_pre = project(txt_mlp, txt_w[2], txt_pairs[3], txt_mask, False)
    txt_act = gelu(txt_pre).astype(BF16)
    txt_feed, txt_fc2_mid = give(
        inner_right(txt_act, txt_w[3]), inner_right(txt_act, txt_pairs[4][0])
    )
    txt_feed = txt_feed + matmul(txt_fc2_mid, txt_pairs[4][1])
    img_fc1_mid, img_pre = project(mlp_in[0], img_w[2], img_pairs[3], None, False)
    img_act = gelu(img_pre).astype(BF16)
    img_fc2_mid, img_feed = project(img_act, img_w[3], img_pairs[4], None, True)
    feed = [img_feed, txt_feed]
    results = [(after[s] + stretch(s, 5) * feed[s]).astype(BF16) for s in range(2)]
    image_out = unshard(results[0])

    grad_feed = [(stretch(s, 5) * cots[s]).astype(BF16) for s in range(2)]
    grads = [[None] * 5 for stream in range(2)]

    def project_back(grad, weight, pair, mask, flipped):
        middle = inner_right(grad, pair[1])
        if mask is not None:
            middle = middle * mask
        middle = middle.astype(BF16)
        main = matmul(grad, weight) if flipped else inner_right(grad, weight)
        return middle, main + matmul(middle, pair[0])

    img_back_mid, img_grad_act = project_back(grad_feed[0], img_w[3], img_pairs[4], None, True)
    grads[0][4] = (inner_left(img_back_mid, img_act), inner_left(img_fc2_mid, grad_feed[0]))
    img_grad_pre = gelu_back(img_pre, img_grad_act).astype(BF16)
    img_back_mid, img_grad_norm = project_back(img_grad_pre, img_w[2], img_pairs[3], None, False)
    grads[0][3] = (inner_left(img_back_mid, mlp_in[0]), inner_left(img_fc1_mid, img_grad_pre))

    txt_feed_full = share(grad_feed[1])
    txt_back_mid, txt_grad_act = project_back(txt_feed_full, txt_w[3], txt_pairs[4], txt_mask, True)
    txt_fc2_grad_a = inner_left(txt_back_mid, txt_act)
    txt_grad_pre = gelu_back(txt_pre, txt_grad_act).astype(BF16)
    txt_grad_norm, txt_fc1_back = give(
        inner_right(txt_grad_pre, txt_w[2]), inner_right(txt_grad_pre, txt_pairs[3][1])
    )
    txt_grad_norm = txt_grad_norm + matmul(txt_fc1_back, txt_pairs[3][0])
    grad_norm = [img_grad_norm, txt_grad_norm]
    mod_parts = [[None] * 6 for stream in range(2)]
    grad_after = []
    for s in range(2):
        grad_after.append(
            cots[s] + norm_back(grad_norm[s], norm_two[s][0], norm_two[s][1], stretch(s, 4))
        )
        mod_parts[s][3] = collapse(s, grad_norm[s])
        mod_parts[s][4] = collapse(s, grad_norm[s] * norm_two[s][0])
        mod_parts[s][5] = collapse(s, cots[s] * feed[s])
        mod_parts[s][2] = collapse(s, grad_after[s] * branch[s])
    grad_branch = [(stretch(s, 2) * grad_after[s]).astype(BF16) for s in range(2)]

    img_back_mid, img_grad_att = project_back(grad_branch[0], img_w[1], img_pairs[2], None, True)
    grads[0][2] = (inner_left(img_back_mid, attended[0]), inner_left(img_out_mid, grad_branch[0]))
    shared = share(jnp.concatenate([grad_branch[1], txt_fc1_back, txt_fc2_mid], axis=1))
    txt_branch_full = shared[:, :width]
    txt_fc1_back = shared[:, width : width + rank_cols]
    txt_fc2_mid = shared[:, width + rank_cols :]
    grads[1][4] = (txt_fc2_grad_a, inner_left(txt_fc2_mid, lanes(txt_feed_full)))
    grads[1][3] = (
        inner_left(txt_fc1_back, lanes(txt_mlp)),
        inner_left(txt_fc1_mid, txt_grad_pre),
    )
    txt_back_mid, txt_grad_att = project_back(
        txt_branch_full, txt_w[1], txt_pairs[2], txt_mask, True
    )
    grads[1][2] = (
        inner_left(txt_back_mid, attended[1]),
        inner_left(txt_out_mid, lanes(txt_branch_full)),
    )
    txt_grad_att = txt_grad_att.astype(BF16)
    do_img = to_heads(img_grad_att.astype(BF16))
    do_txt = jnp.concatenate(to_chip([txt_grad_att, txt_grad_att]), axis=1)
    do_txt = jnp.where(chip_owner, do_txt, jnp.zeros_like(do_txt))
    d_img, d_txt = attend_back(img_heads, txt_heads, bias, do_img, do_txt, lse, HD)
    img_grad_qkv = to_tokens(d_img)
    txt_grad_qkv = txt_home(d_txt)

    img_back_mid, img_grad_norm = project_back(img_grad_qkv, img_w[0], img_pairs[1], None, False)
    grads[0][1] = (inner_left(img_back_mid, heads_in[0]), inner_left(img_qkv_mid, img_grad_qkv))
    txt_grad_norm, txt_qkv_back = give(
        inner_right(txt_grad_qkv, txt_w[0]), inner_right(txt_grad_qkv, txt_pairs[1][1])
    )
    txt_grad_norm = txt_grad_norm + matmul(txt_qkv_back, txt_pairs[1][0])
    grads[1][1] = (
        inner_left(share(txt_qkv_back), lanes(txt_in)),
        inner_left(txt_qkv_mid, txt_grad_qkv),
    )
    grad_norm = [img_grad_norm, txt_grad_norm]
    grad_inputs = []
    for s in range(2):
        grad_inputs.append(
            grad_after[s]
            + norm_back(grad_norm[s], norm_one[s][0], norm_one[s][1], stretch(s, 1))
        )
        mod_parts[s][0] = collapse(s, grad_norm[s])
        mod_parts[s][1] = collapse(s, grad_norm[s] * norm_one[s][0])
    image_grad = unshard(grad_inputs[0].astype(BF16)).astype(F32)

    img_dmod = jnp.concatenate(mod_parts[0], axis=1)
    img_dmod = (img_dmod + swap_core(img_dmod)).astype(BF16)
    def lane_blocks(values):
        return jnp.swapaxes(values.reshape(values.shape[0], n_z, -1), 0, 1)

    img_dmods = jnp.concatenate(z_exchange(lane_blocks(img_dmod)), axis=0)
    img_dmods = lax.dynamic_slice_in_dim(img_dmods, core * slots, slots, 0)
    txt_dmod = jnp.concatenate(mod_parts[1], axis=1)
    txt_dmods = sum(z_exchange(lane_blocks(txt_dmod))).astype(BF16)
    dmods = jnp.stack([img_dmods, txt_dmods], axis=1)
    dmods_all = lax.all_gather(dmods, "fsdp", axis=0, tiled=True)
    cond_part = sum(inner_right(dmods_all[:, s], mod_weight[s]) for s in range(2))
    mod_back = [inner_right(dmods[:, s], mod_b[s]) for s in range(2)]
    cond_part = cond_part.reshape(-1, width // n_f)
    joined = jnp.concatenate([cond_part.reshape(-1), jnp.stack(mod_back).reshape(-1)])
    joined = sum(z_gather(joined))
    cond_slices = joined[: cond_part.size].reshape(n_f, -1, width // n_f)
    mod_rank = joined[cond_part.size :].reshape(2, slots, -1)
    cond_rows = lax.all_to_all(cond_slices, "fsdp", 0, 2, tiled=True)[0]
    for s in range(2):
        back_mid = (mod_rank[s] * seq_mask).astype(BF16)
        cond_rows = cond_rows + matmul(back_mid, mod_a[s])
        grads[s][0] = (inner_left(back_mid, lanes(cond_act)), inner_left(mod_mid[s], dmods[:, s]))
    cond_grad = jax.vjp(jax.nn.silu, conditioning)[1](cond_rows)[0]

    def spread(values):
        return jnp.swapaxes(values.reshape(RANK, n_z, -1), 0, 1)

    img_rows = {}
    for group in ((2, 3, 4), (1,)):
        parts = [spread(grads[0][index][side]) for side in range(2) for index in group]
        parts = jnp.concatenate(z_exchange(jnp.concatenate(parts, axis=2)), axis=0)
        offset = 0
        for side, sizes in enumerate((fans, cols)):
            for index in group:
                count = sizes[index] // n_z
                img_rows[side, index] = parts[:, offset : offset + count]
                offset += count
    flat = []
    for stream in range(2):
        for index in range(5):
            if stream == 0 and index > 0:
                part_a, part_b = img_rows[0, index], img_rows[1, index]
                hot = one_hot
            else:
                part_a, part_b = grads[stream][index]
                hot = own_hot
            flat.append(
                lax.dot_general(
                    part_a, hot, (((0,), (1,)), ((), ())),
                    precision=HIGH, preferred_element_type=F32,
                )
            )
            flat.append(exact(hot, part_b).reshape(-1, 128))
    total = jnp.concatenate(flat, axis=0).reshape(n_f, -1, 128)
    step = 1
    while step < n_f:
        bit = (f // step) % 2
        pairs = total.reshape((-1, 2) + total.shape[1:])
        keep = lax.dynamic_index_in_dim(pairs, bit, 1, keepdims=False)
        send = lax.dynamic_index_in_dim(pairs, 1 - bit, 1, keepdims=False)
        sent = lax.ppermute(send.astype(BF16), "fsdp", [(i, i ^ step) for i in range(n_f)])
        total = keep + sent.astype(F32)
        step *= 2
    adapter_grad = total.reshape(1, -1)
    return (image_out, results[1], image_grad, grad_inputs[1], cond_grad, adapter_grad)


def solution(mesh):
    return jax.shard_map(
        shards,
        mesh=mesh,
        in_specs=(
            P("fsdp", "tp", None),
            P(("fsdp", "tp"), None),
            P("fsdp", None),
            P("fsdp", None),
            P("fsdp"),
            P("tp", "fsdp"),
            P(None, "fsdp", "tp"),
            P(None, "fsdp", "tp"),
            P(None, "tp", "fsdp"),
            P(None, "fsdp", "tp"),
            P(None, "tp", "fsdp"),
            P("fsdp", "tp", None),
            P(("fsdp", "tp"), None),
        ),
        out_specs=(
            P("fsdp", "tp", None),
            P(("fsdp", "tp"), None),
            P("fsdp", "tp", None),
            P(("fsdp", "tp"), None),
            P("fsdp", None),
            P("tp", "fsdp"),
        ),
        check_vma=False,
    )
```

```python
import functools

import jax
import jax.numpy as jnp
from jax import lax
from jax.experimental import pallas as pl
from jax.experimental.pallas import tpu as pltpu
from jax.sharding import PartitionSpec as P

MESH = pl.DeviceIdType.MESH

def bits_of(count):
    return max(count.bit_length() - 1, 0)

def halves(width):
    tiles = width // 128
    first = (tiles + 1) // 2 * 128
    return [(0, first), (first, width - first)]

def gather_kernel(n_f, n_z, full_count, part_count, *refs):
    total = full_count + part_count
    ins, outs = refs[:total], refs[total:2 * total]
    z_send, z_recv, xy_send, xy_recv, core_send, core_recv, own_sem = refs[2 * total:]
    f = lax.axis_index("fsdp")
    z = lax.axis_index("tp")
    chip, core = f // 2, f % 2
    chips = n_f // 2
    nbits = bits_of(chips)
    partner = chip * 2 + (1 - core)

    def peer_of(mask):
        other = 0
        for bit in range(nbits):
            have = (chip // (1 << bit)) % 2
            want = 1 - have if (mask >> bit) & 1 else have
            other = other + want * (1 << bit)
        return other * 2 + core

    barrier = pltpu.get_barrier_semaphore()
    for bit in range(nbits):
        pl.semaphore_signal(barrier, inc=1, device_id=(peer_of(1 << bit), z), device_id_type=MESH)
    pl.semaphore_signal(barrier, inc=1, device_id=(partner, z), device_id_type=MESH)
    @pl.when(z > 0)
    def _():
        pl.semaphore_signal(barrier, inc=1, device_id=(f, z - 1), device_id_type=MESH)
    @pl.when(z < n_z - 1)
    def _():
        pl.semaphore_signal(barrier, inc=1, device_id=(f, z + 1), device_id_type=MESH)
    peers = nbits + 1 + (z > 0).astype(jnp.int32) + (z < n_z - 1).astype(jnp.int32)
    pl.semaphore_wait(barrier, peers)

    def width(m):
        return ins[m].shape[-1]

    def place(m, who, zz, off=0, w=None):
        w = width(m) if w is None else w
        if m < full_count:
            return outs[m].at[who, :, pl.ds(pl.multiple_of(zz * width(m) + off, 128), w)]
        if w == width(m):
            return outs[m].at[who]
        return outs[m].at[who, :, pl.ds(off, w)]

    def piece(m, off, w):
        return ins[m] if w == width(m) else ins[m].at[:, pl.ds(off, w)]

    def remote(src, dst, ssem, rsem, dev):
        return pltpu.make_async_remote_copy(src_ref=src, dst_ref=dst, send_sem=ssem, recv_sem=rsem, device_id=dev, device_id_type=MESH)

    def order_of(half):
        order = list(range(nbits))
        return order if half == 0 else order[::-1]

    def cuts(m):
        if width(m) >= 256:
            return list(enumerate(halves(width(m))))
        return [(m % 2, (0, width(m)))]

    def slot(m, zz):
        return zz if m < full_count else 0

    def xy_copy(m, zz, half, cut, mask, bit, own_piece=False):
        off, w = cut
        who = peer_of(mask)
        source = piece(m, off, w) if own_piece and mask == 0 else place(m, who, zz, off, w)
        return remote(source, place(m, who, zz, off, w),
                      xy_send.at[m, slot(m, zz), half, mask, bit], xy_recv.at[m, slot(m, zz), half, mask | (1 << bit)],
                      (peer_of(1 << bit), z))

    def xy_wait(m, zz, half, cut, mask):
        off, w = cut
        who = peer_of(mask)
        remote(place(m, who, zz, off, w), place(m, who, zz, off, w), xy_send.at[m, slot(m, zz), half, 0, 0],
               xy_recv.at[m, slot(m, zz), half, mask], (partner, z)).wait_recv()

    def core_copy(m, zz, half, cut, mask, own_piece=False):
        off, w = cut
        who = peer_of(mask)
        source = piece(m, off, w) if own_piece and mask == 0 else place(m, who, zz, off, w)
        return remote(source, place(m, who, zz, off, w),
                      core_send.at[m, slot(m, zz), half, mask], core_recv.at[m, slot(m, zz), half, mask], (partner, z))

    def core_wait_recv(m, zz, half, cut, mask):
        off, w = cut
        who = peer_of(mask) - core + (1 - core)
        remote(place(m, who, zz, off, w), place(m, who, zz, off, w),
               core_send.at[m, slot(m, zz), half, mask], core_recv.at[m, slot(m, zz), half, mask], (partner, z)).wait_recv()

    def own(m):
        return pltpu.make_async_copy(ins[m], place(m, f, z), own_sem.at[m])

    def z_copy(m, zz, up, own_piece=False):
        return remote(ins[m] if own_piece else place(m, f, zz), place(m, f, zz), z_send.at[m, zz, up], z_recv.at[m, zz], (f, z + 1 if up else z - 1))

    def launch(m, zz, own_piece=False):
        for half, cut in cuts(m):
            for bit in order_of(half):
                xy_copy(m, zz, half, cut, 0, bit, own_piece).start()
            core_copy(m, zz, half, cut, 0, own_piece).start()

    def masks_in_order(half):
        order = order_of(half)
        def rank(mask):
            return [1 if (mask >> b) & 1 else 0 for b in reversed(order)]
        return sorted(range(1, 1 << nbits), key=rank)

    def forward(m, zz):
        for half, cut in cuts(m):
            order = order_of(half)
            for mask in masks_in_order(half):
                last = max(i for i, b in enumerate(order) if (mask >> b) & 1)
                if last == nbits - 1:
                    continue
                xy_wait(m, zz, half, cut, mask)
                for b in order[last + 1:]:
                    xy_copy(m, zz, half, cut, mask, b).start()
                core_copy(m, zz, half, cut, mask).start()

    def finish(m, zz):
        for half, cut in cuts(m):
            order = order_of(half)
            for mask in masks_in_order(half):
                last = max(i for i, b in enumerate(order) if (mask >> b) & 1)
                if last == nbits - 1:
                    xy_wait(m, zz, half, cut, mask)
                    core_copy(m, zz, half, cut, mask).start()

    def drain(m, zz):
        for half, cut in cuts(m):
            order = order_of(half)
            for mask in [0] + masks_in_order(half):
                last = max([i for i, b in enumerate(order) if (mask >> b) & 1], default=-1)
                for b in order[last + 1:]:
                    xy_copy(m, zz, half, cut, mask, b).wait_send()
                core_copy(m, zz, half, cut, mask).wait_send()
                core_wait_recv(m, zz, half, cut, mask)

    for m in range(total):
        own(m).start()
    for m in range(total):
        if m < full_count:
            @pl.when(z < n_z - 1)
            def _():
                z_copy(m, z, 1, True).start()
            @pl.when(z > 0)
            def _():
                z_copy(m, z, 0, True).start()
        launch(m, z, True)
    for m in range(full_count, total):
        forward(m, z)
    for k in range(1, n_z):
        for m in range(full_count):
            @pl.when(z - k >= 0)
            def _():
                zz = z - k
                z_copy(m, zz, 1).wait_recv()
                @pl.when(z < n_z - 1)
                def _():
                    z_copy(m, zz, 1).start()
                launch(m, zz)
            @pl.when(z + k < n_z)
            def _():
                zz = z + k
                z_copy(m, zz, 0).wait_recv()
                @pl.when(z > 0)
                def _():
                    z_copy(m, zz, 0).start()
                launch(m, zz)
            for sign in ((-1, 1) if k > 1 else (1,)):
                zz = z + sign * (k - 1)
                @pl.when((zz >= 0) & (zz < n_z))
                def _():
                    forward(m, zz)
    for m in range(full_count):
        for sign in (-1, 1):
            zz = z + sign * (n_z - 1)
            @pl.when((zz >= 0) & (zz < n_z))
            def _():
                forward(m, zz)
    for m in range(total):
        if m < full_count:
            def body(zz, _):
                finish(m, zz)
                return 0
            lax.fori_loop(0, n_z, body, 0)
        else:
            finish(m, z)
    for m in range(total):
        own(m).wait()
        if m < full_count:
            def body(zz, _):
                drain(m, zz)
                @pl.when((zz <= z) & (z < n_z - 1))
                def _():
                    z_copy(m, zz, 1).wait_send()
                @pl.when((zz >= z) & (z > 0))
                def _():
                    z_copy(m, zz, 0).wait_send()
                return 0
            lax.fori_loop(0, n_z, body, 0)
        else:
            drain(m, z)

def gather(full, part, n_f, n_z, cid=1):
    arrays = list(full) + list(part)
    total = len(arrays)
    if n_f > 8:
        rows = [lax.all_gather(a, "fsdp", axis=0, tiled=True) for a in arrays]
        return [
            lax.all_gather(a, "tp", axis=1, tiled=True) if i < len(full) else a
            for i, a in enumerate(rows)
        ]
    chips = n_f // 2
    nbits = bits_of(chips)
    shapes = [jax.ShapeDtypeStruct((n_f,) + a.shape[:-1] + (a.shape[-1] * (n_z if i < len(full) else 1),), a.dtype) for i, a in enumerate(arrays)]
    dma = pltpu.SemaphoreType.DMA
    return pl.pallas_call(
        functools.partial(gather_kernel, n_f, n_z, len(full), len(part)),
        out_shape=shapes,
        in_specs=[pl.BlockSpec(memory_space=pl.ANY)] * total,
        out_specs=[pl.BlockSpec(memory_space=pl.ANY)] * total,
        scratch_shapes=[
            dma((total, n_z, 2)), dma((total, n_z)),
            dma((total, n_z, 2, chips, max(nbits, 1))), dma((total, n_z, 2, chips)),
            dma((total, n_z, 2, chips)), dma((total, n_z, 2, chips)), dma((total,)),
        ],
        compiler_params=pltpu.CompilerParams(collective_id=cid, has_side_effects=True),
        name="weight_gather",
    )(*arrays)

def dots(left, right, lc, rc):
    return lax.dot_general(left, right, (((lc,), (rc,)), ((), ())), preferred_element_type=jnp.float32)

def attend_kernel(hd, bq, img_ref, txt_ref, bias_ref, oi_ref, ot_ref, lse_ref):
    img_n, txt_n = img_ref.shape[0], txt_ref.shape[1]
    heads = img_ref.shape[1] // (3 * hd)
    bias = bias_ref[...]
    for h in range(heads):
        base = 3 * hd * h
        ki = img_ref[:, base + hd:base + 2 * hd]
        vi = img_ref[:, base + 2 * hd:base + 3 * hd]
        kt = txt_ref[0, :, base + hd:base + 2 * hd]
        vt = txt_ref[0, :, base + 2 * hd:base + 3 * hd]

        def block(q):
            q = q * jnp.bfloat16(0.125)
            si = dots(ki, q, 1, 1)
            st = dots(kt, q, 1, 1) + bias
            top = jnp.maximum(jnp.max(si, axis=0, keepdims=True), jnp.max(st, axis=0, keepdims=True))
            ei = jnp.exp(si - top)
            et = jnp.exp(st - top)
            total = jnp.sum(ei, axis=0, keepdims=True) + jnp.sum(et, axis=0, keepdims=True)
            o = dots(vi, ei.astype(jnp.bfloat16), 0, 0) + dots(vt, et.astype(jnp.bfloat16), 0, 0)
            return (o / total).T.astype(jnp.bfloat16), top + jnp.log(total)

        for i in range(img_n // bq):
            o, lse = block(img_ref[i * bq:(i + 1) * bq, base:base + hd])
            oi_ref[i * bq:(i + 1) * bq, h * hd:(h + 1) * hd] = o
            lse_ref[0, h:h + 1, i * bq:(i + 1) * bq] = lse
        o, lse = block(txt_ref[0, :, base:base + hd])
        ot_ref[0, :, h * hd:(h + 1) * hd] = o
        lse_ref[0, h:h + 1, img_n:img_n + txt_n] = lse

def attend(img, txt, bias, hd, bq=512):
    img_n, cols = img.shape
    parts, txt_n, _ = txt.shape
    pairs = cols // (6 * hd)
    per = pairs // parts
    return pl.pallas_call(
        functools.partial(attend_kernel, hd, bq),
        grid=(pairs,),
        in_specs=[
            pl.BlockSpec((img_n, 6 * hd), lambda i: (0, i)),
            pl.BlockSpec((1, txt_n, 6 * hd), lambda i: (i // per, 0, i % per)),
            pl.BlockSpec((txt_n, 1), lambda i: (0, 0)),
        ],
        out_specs=[
            pl.BlockSpec((img_n, 2 * hd), lambda i: (0, i)),
            pl.BlockSpec((1, txt_n, 2 * hd), lambda i: (i // per, 0, i % per)),
            pl.BlockSpec((1, 2, img_n + txt_n), lambda i: (i, 0, 0)),
        ],
        out_shape=[
            jax.ShapeDtypeStruct((img_n, pairs * 2 * hd), jnp.bfloat16),
            jax.ShapeDtypeStruct((parts, txt_n, per * 2 * hd), jnp.bfloat16),
            jax.ShapeDtypeStruct((pairs, 2, img_n + txt_n), jnp.float32),
        ],
        compiler_params=pltpu.CompilerParams(vmem_limit_bytes=48 * 1024 * 1024),
        name="attend",
    )(img, txt, bias)

def attend_back_kernel(hd, bq, img_ref, txt_ref, bias_ref, doi_ref, dot_ref, lse_ref, di_ref, dt_ref, acc_i, acc_t):
    img_n, txt_n = img_ref.shape[0], txt_ref.shape[1]
    heads = img_ref.shape[1] // (3 * hd)
    bias = bias_ref[...]
    for h in range(heads):
        base = 3 * hd * h
        ki = img_ref[:, base + hd:base + 2 * hd]
        vi = img_ref[:, base + 2 * hd:base + 3 * hd]
        kt = txt_ref[0, :, base + hd:base + 2 * hd]
        vt = txt_ref[0, :, base + 2 * hd:base + 3 * hd]

        def block(q, do, lse, first):
            q = q * jnp.bfloat16(0.125)
            pi = jnp.exp(dots(ki, q, 1, 1) - lse)
            pt = jnp.exp(dots(kt, q, 1, 1) + bias - lse)
            dwi = dots(vi, do, 1, 1)
            dwt = dots(vt, do, 1, 1)
            delta = jnp.sum(pi * dwi, axis=0, keepdims=True) + jnp.sum(pt * dwt, axis=0, keepdims=True)
            dsi = (pi * (dwi - delta)).astype(jnp.bfloat16)
            dst = (pt * (dwt - delta)).astype(jnp.bfloat16)
            dvi = dots(pi.astype(jnp.bfloat16), do, 1, 0)
            dvt = dots(pt.astype(jnp.bfloat16), do, 1, 0)
            dki = dots(dsi, q, 1, 0)
            dkt = dots(dst, q, 1, 0)
            if first:
                acc_i[0], acc_i[1], acc_t[0], acc_t[1] = dki, dvi, dkt, dvt
            else:
                acc_i[0] += dki
                acc_i[1] += dvi
                acc_t[0] += dkt
                acc_t[1] += dvt
            dq = dots(ki, dsi, 0, 0) + dots(kt, dst, 0, 0)
            return (dq.T * 0.125).astype(jnp.bfloat16)

        for i in range(img_n // bq):
            rows = slice(i * bq, (i + 1) * bq)
            di_ref[rows, base:base + hd] = block(
                img_ref[rows, base:base + hd], doi_ref[rows, h * hd:(h + 1) * hd], lse_ref[0, h:h + 1, rows], i == 0)
        grad = jnp.where(bias < 0, 0.0, dot_ref[0, :, h * hd:(h + 1) * hd].astype(jnp.float32)).astype(jnp.bfloat16)
        dt_ref[0, :, base:base + hd] = block(
            txt_ref[0, :, base:base + hd], grad, lse_ref[0, h:h + 1, img_n:img_n + txt_n], False)
        di_ref[:, base + hd:base + 2 * hd] = acc_i[0].astype(jnp.bfloat16)
        di_ref[:, base + 2 * hd:base + 3 * hd] = acc_i[1].astype(jnp.bfloat16)
        dt_ref[0, :, base + hd:base + 2 * hd] = acc_t[0].astype(jnp.bfloat16)
        dt_ref[0, :, base + 2 * hd:base + 3 * hd] = acc_t[1].astype(jnp.bfloat16)

def attend_back(img, txt, bias, doi, dot, lse, hd, bq=512):
    img_n, cols = img.shape
    parts, txt_n, _ = txt.shape
    pairs = cols // (6 * hd)
    per = pairs // parts
    wide = pl.BlockSpec((img_n, 6 * hd), lambda i: (0, i))
    wide_t = pl.BlockSpec((1, txt_n, 6 * hd), lambda i: (i // per, 0, i % per))
    return pl.pallas_call(
        functools.partial(attend_back_kernel, hd, bq),
        grid=(pairs,),
        in_specs=[
            wide, wide_t,
            pl.BlockSpec((txt_n, 1), lambda i: (0, 0)),
            pl.BlockSpec((img_n, 2 * hd), lambda i: (0, i)),
            pl.BlockSpec((1, txt_n, 2 * hd), lambda i: (i // per, 0, i % per)),
            pl.BlockSpec((1, 2, img_n + txt_n), lambda i: (i, 0, 0)),
        ],
        out_specs=[wide, wide_t],
        out_shape=[jax.ShapeDtypeStruct(img.shape, jnp.bfloat16), jax.ShapeDtypeStruct(txt.shape, jnp.bfloat16)],
        scratch_shapes=[pltpu.VMEM((2, img_n, hd), jnp.float32), pltpu.VMEM((2, txt_n, hd), jnp.float32)],
        compiler_params=pltpu.CompilerParams(vmem_limit_bytes=48 * 1024 * 1024),
        name="attend_back",
    )(img, txt, bias, doi, dot, lse)

ROWS = 64


def mm(left, right):
    return dots(left, right, 1, 0)


def mm_t(left, right):
    return dots(left, right, 1, 1)


def t_mm(left, right):
    return dots(left, right, 0, 0)


def gelu_parts(u):
    scale = 0.7978845608028654
    square = u * u
    tanh = jnp.tanh(scale * (u + 0.044715 * u * square))
    half = 0.5 * (1.0 + tanh)
    slope = half + 0.5 * u * (1.0 - tanh * tanh) * (scale * (1.0 + 3 * 0.044715 * square))
    return u * half, slope


def norm_rows(v):
    center = v - jnp.mean(v, axis=-1, keepdims=True)
    inverse = lax.rsqrt(jnp.mean(center * center, axis=-1, keepdims=True) + 1e-06)
    return center * inverse, inverse


def block_fwd_kernel(tiles, o_ref, x_ref, g_ref, mod_ref, wo_ref, ao_ref, bo_ref, a1_ref, b1_ref, w1_ref, a2_ref, w2_ref, b2_ref,
                     a_out, x1_out, h2_out, u_out, y_out, to_out, t1_out, t2_out, gate_out, m_acc, t2_acc):
    step = pl.program_id(0)
    rows = o_ref.shape[0]
    width = o_ref.shape[1]

    @pl.when(step == 0)
    def _():
        to = mm_t(o_ref[...], ao_ref[...]).astype(jnp.bfloat16)
        to_out[...] = to

        def cols(n, _):
            sl = pl.ds(pl.multiple_of(n * 256, 256), 256)
            a_out[:, sl] = mm_t(o_ref[...], wo_ref[sl, :]) + mm(to_out[...], bo_ref[:, sl])
            return 0

        lax.fori_loop(0, width // 256, cols, 0)

        def norm(r, _):
            sl = pl.ds(pl.multiple_of(r * ROWS, ROWS), ROWS)
            x1 = x_ref[sl, :].astype(jnp.float32) + mod_ref[2:3, :] * a_out[sl, :]
            x1_out[sl, :] = x1
            xh, _inv = norm_rows(x1)
            h2_out[sl, :] = (xh * (1.0 + mod_ref[4:5, :]) + mod_ref[3:4, :]).astype(jnp.bfloat16)
            return 0

        lax.fori_loop(0, rows // ROWS, norm, 0)
        t1_out[...] = mm_t(h2_out[...], a1_ref[...]).astype(jnp.bfloat16)
        m_acc[...] = jnp.zeros_like(m_acc)
        t2_acc[...] = jnp.zeros_like(t2_acc)

    u = mm(h2_out[...], w1_ref[...]) + mm(t1_out[...], b1_ref[...])
    u_out[...] = u
    f = gelu_parts(u)[0].astype(jnp.bfloat16)
    m_acc[...] += mm_t(f, w2_ref[...])
    t2_acc[...] += mm_t(f, a2_ref[...])

    @pl.when(step == tiles - 1)
    def _():
        t2_out[...] = t2_acc[...].astype(jnp.bfloat16)
        gate_out[...] = jnp.zeros_like(gate_out)

        def last(r, _):
            sl = pl.ds(pl.multiple_of(r * ROWS, ROWS), ROWS)
            m = m_acc[sl, :] + mm(t2_out[sl, :], b2_ref[...])
            y_out[sl, :] = (x1_out[sl, :] + mod_ref[5:6, :] * m).astype(jnp.bfloat16)
            gm = g_ref[sl, :].astype(jnp.float32) * m
            gate_out[...] += sum(gm[8 * i:8 * i + 8, :] for i in range(ROWS // 8))
            return 0

        lax.fori_loop(0, rows // ROWS, last, 0)


def block_fwd(o, x, g, mod, wo, pair_o, pair_1, w1, pair_2, w2, tn=512):
    rows, width = o.shape
    hidden = w1.shape[1]
    tiles = hidden // tn
    rank = pair_o[0].shape[0]
    whole = lambda shape: pl.BlockSpec(shape, lambda n: (0,) * len(shape))
    once = lambda shape: pl.BlockSpec(shape, lambda n: (0,) * len(shape), pipeline_mode=pl.Buffered(1))
    tile = lambda height: pl.BlockSpec((height, tn), lambda n: (0, n))
    f32, bf16 = jnp.float32, jnp.bfloat16
    act = (rows, width)
    return pl.pallas_call(
        functools.partial(block_fwd_kernel, tiles),
        grid=(tiles,),
        in_specs=[once(act), once(act), once(act), once(mod.shape), once((width, width)), once((rank, width)), once((rank, width)),
                  once((rank, width)), tile(rank), tile(width), tile(rank), tile(width), once((rank, width))],
        out_specs=[whole(act), whole(act), whole(act), tile(rows), whole(act), whole((rows, rank)), whole((rows, rank)),
                   whole((rows, rank)), whole((8, width))],
        out_shape=[jax.ShapeDtypeStruct(act, f32), jax.ShapeDtypeStruct(act, f32), jax.ShapeDtypeStruct(act, bf16),
                   jax.ShapeDtypeStruct((rows, hidden), f32), jax.ShapeDtypeStruct(act, bf16)]
        + [jax.ShapeDtypeStruct((rows, rank), bf16)] * 3 + [jax.ShapeDtypeStruct((8, width), f32)],
        scratch_shapes=[pltpu.VMEM(act, f32), pltpu.VMEM((rows, rank), f32)],
        compiler_params=pltpu.CompilerParams(vmem_limit_bytes=58 * 1024 * 1024),
        cost_estimate=pl.CostEstimate(flops=2 * rows * width * (width + 2 * hidden), bytes_accessed=4 * width * hidden, transcendentals=0),
        name="block_forward",
    )(o, x, g, mod, wo, *pair_o, pair_1[0], pair_1[1], w1, pair_2[0], w2, pair_2[1])


def block_back_kernel(tiles, g_ref, x1_ref, a_ref, h2_ref, o_ref, mod_ref, u_ref, w2_ref, a2_ref, b2_ref, w1_ref, a1_ref, b1_ref,
                      wo_ref, ao_ref, bo_ref, to_ref, t1_ref, t2_ref,
                      dx1_out, do_out, sums_out, ga2_out, gb1_out, ga1_out, gb2_out, gao_out, gbo_out,
                      dm_ref, dt2_ref, dh_acc, dt1_acc, da_ref):
    step = pl.program_id(0)
    rows, width = g_ref.shape
    bf16 = jnp.bfloat16

    @pl.when(step == 0)
    def _():
        def start(r, _):
            sl = pl.ds(pl.multiple_of(r * ROWS, ROWS), ROWS)
            dm_ref[sl, :] = (mod_ref[5:6, :] * g_ref[sl, :].astype(jnp.float32)).astype(bf16)
            return 0

        lax.fori_loop(0, rows // ROWS, start, 0)
        dt2_ref[...] = mm_t(dm_ref[...], b2_ref[...]).astype(bf16)
        gb2_out[...] = t_mm(t2_ref[...], dm_ref[...])
        dh_acc[...] = jnp.zeros_like(dh_acc)
        dt1_acc[...] = jnp.zeros_like(dt1_acc)

    act, slope = gelu_parts(u_ref[...])
    df = mm(dm_ref[...], w2_ref[...]) + mm(dt2_ref[...], a2_ref[...])
    ga2_out[...] = t_mm(dt2_ref[...], act.astype(bf16))
    du = (df * slope).astype(bf16)
    gb1_out[...] = t_mm(t1_ref[...], du)
    dh_acc[...] += mm_t(du, w1_ref[...])
    dt1_acc[...] += mm_t(du, b1_ref[...])

    @pl.when(step == tiles - 1)
    def _():
        dt1 = dt1_acc[...].astype(bf16)
        dt2_ref[...] = dt1
        ga1_out[...] = t_mm(dt1, h2_ref[...])
        sums_out[...] = jnp.zeros_like(sums_out)

        def last(r, _):
            sl = pl.ds(pl.multiple_of(r * ROWS, ROWS), ROWS)
            dh = dh_acc[sl, :] + mm(dt2_ref[sl, :], a1_ref[...])
            xh, inverse = norm_rows(x1_ref[sl, :])
            dz = dh * (1.0 + mod_ref[4:5, :])
            dx1 = g_ref[sl, :].astype(jnp.float32) + inverse * (
                dz - jnp.mean(dz, axis=-1, keepdims=True) - xh * jnp.mean(dz * xh, axis=-1, keepdims=True))
            dx1_out[sl, :] = dx1
            da_ref[sl, :] = (mod_ref[2:3, :] * dx1).astype(bf16)
            fold = lambda v: sum(v[8 * i:8 * i + 8, :] for i in range(ROWS // 8))
            sums_out[0:8, :] += fold(dx1 * a_ref[sl, :])
            sums_out[8:16, :] += fold(dh)
            sums_out[16:24, :] += fold(dh * xh)
            return 0

        lax.fori_loop(0, rows // ROWS, last, 0)
        dto = mm_t(da_ref[...], bo_ref[...]).astype(bf16)
        dt2_ref[...] = dto
        gao_out[...] = t_mm(dto, o_ref[...])
        gbo_out[...] = t_mm(to_ref[...], da_ref[...])

        def cols(n, _):
            sl = pl.ds(pl.multiple_of(n * 256, 256), 256)
            do_out[:, sl] = (mm(da_ref[...], wo_ref[:, sl]) + mm(dt2_ref[...], ao_ref[:, sl])).astype(bf16)
            return 0

        lax.fori_loop(0, width // 256, cols, 0)


def block_back(g, x1, a, h2, o, mod, u, w2, pair_2, w1, pair_1, wo, pair_o, mids, tn=512):
    rows, width = o.shape
    hidden = w1.shape[1]
    tiles = hidden // tn
    rank = pair_o[0].shape[0]
    whole = lambda shape: pl.BlockSpec(shape, lambda n: (0,) * len(shape))
    once = lambda shape: pl.BlockSpec(shape, lambda n: (0,) * len(shape), pipeline_mode=pl.Buffered(1))
    tile = lambda height: pl.BlockSpec((height, tn), lambda n: (0, n))
    f32, bf16 = jnp.float32, jnp.bfloat16
    act = (rows, width)
    side = (rank, width)
    thin = (rows, rank)
    return pl.pallas_call(
        functools.partial(block_back_kernel, tiles),
        grid=(tiles,),
        in_specs=[once(act)] * 5 + [once(mod.shape), tile(rows), tile(width), tile(rank), once(side), tile(width), once(side), tile(rank),
                  once((width, width)), once(side), once(side)] + [once(thin)] * 3,
        out_specs=[whole(act), whole(act), whole((24, width)), tile(rank), tile(rank)] + [whole(side)] * 4,
        out_shape=[jax.ShapeDtypeStruct(act, f32), jax.ShapeDtypeStruct(act, bf16), jax.ShapeDtypeStruct((24, width), f32)]
        + [jax.ShapeDtypeStruct((rank, hidden), f32)] * 2 + [jax.ShapeDtypeStruct(side, f32)] * 4,
        scratch_shapes=[pltpu.VMEM(act, bf16), pltpu.VMEM(thin, bf16), pltpu.VMEM(act, f32), pltpu.VMEM(thin, f32), pltpu.VMEM(act, bf16)],
        compiler_params=pltpu.CompilerParams(vmem_limit_bytes=58 * 1024 * 1024),
        cost_estimate=pl.CostEstimate(flops=2 * rows * width * (width + 2 * hidden), bytes_accessed=4 * width * hidden, transcendentals=0),
        name="block_backward",
    )(g, x1, a, h2, o, mod, u, w2, pair_2[0], pair_2[1], w1, pair_1[0], pair_1[1], wo, *pair_o, *mids)


def column_peers(n_z):
    f, z = lax.axis_index("fsdp"), lax.axis_index("tp")
    core = f % 2
    base = f - core
    peers = [(f, (z + j) % n_z) for j in range(1, n_z)]
    peers += [(base + 1 - core, (z + j) % n_z) for j in range(n_z)]
    return f, z, core, base, peers


def meet(peers):
    barrier = pltpu.get_barrier_semaphore()
    for peer in peers:
        pl.semaphore_signal(barrier, inc=1, device_id=peer, device_id_type=MESH)
    pl.semaphore_wait(barrier, len(peers))


def push(src, dst, send, recv, peer):
    return pltpu.make_async_remote_copy(
        src_ref=src, dst_ref=dst, send_sem=send, recv_sem=recv, device_id=peer, device_id_type=MESH)


class ZRing:
    def __init__(self, f, z, n_z):
        self.f, self.z, self.n_z = f, z, n_z

    def start(self, source_of, buf, send, recv):
        for j in range(1, self.n_z):
            to = (self.z + j) % self.n_z
            push(source_of(to), buf.at[self.z], send.at[j], recv.at[self.z], (self.f, to)).start()

    def wait(self, buf, send, recv):
        for j in range(1, self.n_z):
            came = (self.z + j) % self.n_z
            push(buf.at[came], buf.at[came], send.at[j], recv.at[came], (self.f, came)).wait_recv()

    def drain(self, source_of, buf, send, recv):
        for j in range(1, self.n_z):
            to = (self.z + j) % self.n_z
            push(source_of(to), buf.at[self.z], send.at[j], recv.at[self.z], (self.f, to)).wait_send()


def text_mid_kernel(n_z, o_ref, x_ref, g_ref, mod_ref, owner_ref, own_ref, mask_ref, lmask_ref, wo_ref, w1_ref, w2_ref,
                    ao_ref, bo_ref, a1_ref, b1_ref, a2_ref, b2_ref,
                    y_out, dx1_out, do_out, sums_out, gao_out, gbo_out, ga1_out, gb1_out, ga2_out, gb2_out,
                    o_got, part_ref, out_buf, in_buf, ag_ref, da_ref, dm_ref, u_ref, f_ref, att_ref, do_buf, x1_ref, br_ref, t_ref,
                    o_send, o_recv, rs_send, rs_recv, ag_send, ag_recv, dm_send, dm_recv, do_send, do_recv):
    f, z, core, base, peers = column_peers(n_z)
    ring = ZRing(f, z, n_z)
    bf16, f32 = jnp.bfloat16, jnp.float32
    pad, width = x_ref.shape
    rank = ao_ref.shape[0]
    share = ao_ref.shape[1]
    meet(peers)

    def modulation(row):
        return jnp.where(own_ref[...] > 0, mod_ref[row:row + 1, :], mod_ref[8 + row:9 + row, :])

    home = [(base + z // 2, 2 * core + i) for i in range(2)]
    for i in range(2):
        here = (z // 2 == core) & (2 * core + i == z)

        @pl.when(here)
        def _():
            copy = pltpu.make_async_copy(o_ref.at[i], o_got.at[z % 2], o_recv.at[z % 2])
            copy.start()
            copy.wait()

        @pl.when(jnp.logical_not(here))
        def _():
            push(o_ref.at[i], o_got.at[z % 2], o_send.at[i], o_recv.at[z % 2], home[i]).start()

    dm_ref[z, :, :] = (modulation(5) * g_ref[...].astype(f32)).astype(bf16)
    ring.start(lambda to: dm_ref.at[z], dm_ref, dm_send, dm_recv)

    for s in range(2):
        here = (z // 2 == core) & (2 * core + s == z)

        @pl.when(jnp.logical_not(here))
        def _():
            push(o_got.at[s], o_got.at[s], o_send.at[s], o_recv.at[s], home[s]).wait_recv()

    owner = owner_ref[...]
    att_ref[...] = jnp.where(
        owner > 0, o_got[0].astype(f32), jnp.where(owner < 0, o_got[1].astype(f32), 0.0)).astype(bf16)

    def scatter(turn, main, rank_part):
        full = jnp.concatenate([main, rank_part], axis=1)
        full = full.reshape(n_z, pad, full.shape[1])
        part_ref[...] = full
        out_buf[...] = full.astype(bf16)
        ring.start(lambda to: out_buf.at[to], in_buf.at[turn], rs_send.at[turn], rs_recv.at[turn])

    def collect(turn):
        ring.wait(in_buf.at[turn], rs_send.at[turn], rs_recv.at[turn])
        total = part_ref[z]
        for j in range(1, n_z):
            total = total + in_buf[turn, (z + j) % n_z].astype(f32)
        ring.drain(lambda to: out_buf.at[to], in_buf.at[turn], rs_send.at[turn], rs_recv.at[turn])
        return total[:, :width], (total[:, width:] * lmask_ref[...]).astype(bf16)

    def spread(turn, ref, *parts):
        offset = 0
        for part in parts:
            ref[z, :, offset:offset + part.shape[1]] = part
            offset += part.shape[1]
        ring.start(lambda to: ref.at[z], ref, ag_send.at[turn], ag_recv.at[turn])

    def spread_end(turn, ref):
        ring.wait(ref, ag_send.at[turn], ag_recv.at[turn])
        ring.drain(lambda to: ref.at[z], ref, ag_send.at[turn], ag_recv.at[turn])

    def gathered(ref, start, count):
        return ref[:, :, start:start + count].reshape(n_z * pad, count)

    def own_lanes(ref):
        at = pl.ds(pl.multiple_of(z * share, 128), share)
        return ref[:, :, at].reshape(n_z * pad, share)

    mask = mask_ref[...]
    att = att_ref[...]
    scatter(0, mm_t(att, wo_ref[...]), mm_t(att, ao_ref[...]))
    branch, to_mine = collect(0)
    branch = branch + mm(to_mine, bo_ref[...])
    br_ref[...] = branch
    x1 = x_ref[...].astype(f32) + modulation(2) * branch
    x1_ref[...] = x1
    xh, _inv = norm_rows(x1)
    h2 = (xh * (1.0 + modulation(4)) + modulation(3)).astype(bf16)
    spread(0, ag_ref, h2, to_mine)
    spread_end(0, ag_ref)
    h2_all = gathered(ag_ref, 0, width)
    to_all = gathered(ag_ref, width, rank)
    t1 = (mm_t(h2_all, a1_ref[...]) * mask).astype(bf16)
    u = mm(h2_all, w1_ref[...]) + mm(t1, b1_ref[...])
    u_ref[...] = u
    act = gelu_parts(u)[0].astype(bf16)
    f_ref[...] = act
    scatter(1, mm_t(act, w2_ref[...]), mm_t(act, a2_ref[...]))
    t_ref[0] = to_all
    t_ref[1] = t1
    feed, t2_mine = collect(1)
    feed = feed + mm(t2_mine, b2_ref[...])
    y_out[...] = (x1_ref[...] + modulation(5) * feed).astype(bf16)

    def collapse(place, values):
        for s in range(2):
            sums_out[2 * place + s:2 * place + s + 1, :] = jnp.sum(
                jnp.where(own_ref[...] == (1.0 if s == 0 else -1.0), values, 0.0), axis=0, keepdims=True)

    collapse(3, g_ref[...].astype(f32) * feed)

    ring.wait(dm_ref, dm_send, dm_recv)
    ring.drain(lambda to: dm_ref.at[z], dm_ref, dm_send, dm_recv)
    dm_all = dm_ref[...].reshape(n_z * pad, width)
    dt2 = (mm_t(dm_all, b2_ref[...]) * mask).astype(bf16)
    df = mm(dm_all, w2_ref[...]) + mm(dt2, a2_ref[...])
    ga2_out[...] = t_mm(dt2, f_ref[...])
    du = (df * gelu_parts(u_ref[...])[1]).astype(bf16)
    scatter(2, mm_t(du, w1_ref[...]), mm_t(du, b1_ref[...]))
    gb1_out[...] = t_mm(t_ref[1], du)
    dh, dt1_mine = collect(2)
    dh = dh + mm(dt1_mine, a1_ref[...])
    xh, inverse = norm_rows(x1_ref[...])
    dz = dh * (1.0 + modulation(4))
    dx1 = g_ref[...].astype(f32) + inverse * (
        dz - jnp.mean(dz, axis=-1, keepdims=True) - xh * jnp.mean(dz * xh, axis=-1, keepdims=True))
    spread(1, da_ref, (modulation(2) * dx1).astype(bf16), dt1_mine, t2_mine)
    dx1_out[...] = dx1
    collapse(0, dx1 * br_ref[...])
    collapse(1, dh)
    collapse(2, dh * xh)
    spread_end(1, da_ref)
    da_all = gathered(da_ref, 0, width)
    dt1 = gathered(da_ref, width, rank)
    t2 = gathered(da_ref, width + rank, rank)
    dto = (mm_t(da_all, bo_ref[...]) * mask).astype(bf16)
    do_buf[...] = (mm(da_all, wo_ref[...]) + mm(dto, ao_ref[...])).astype(bf16)
    for s in range(2):
        here = (z // 2 == core) & (2 * core + s == z)

        @pl.when(here)
        def _():
            copy = pltpu.make_async_copy(do_buf, do_out.at[z % 2], do_recv.at[z % 2])
            copy.start()
            copy.wait()

        @pl.when(jnp.logical_not(here))
        def _():
            push(do_buf, do_out.at[z % 2], do_send.at[s], do_recv.at[z % 2], (base + z // 2, 2 * core + s)).start()

    gao_out[...] = t_mm(dto, att_ref[...])
    gbo_out[...] = t_mm(t_ref[0], own_lanes(da_ref))
    gb2_out[...] = t_mm(t2, own_lanes(dm_ref))
    ga1_out[...] = t_mm(dt1, own_lanes(ag_ref))
    for i in range(2):
        here = (z // 2 == core) & (2 * core + i == z)

        @pl.when(jnp.logical_not(here))
        def _():
            push(do_out.at[i], do_out.at[i], do_send.at[i], do_recv.at[i], home[i]).wait_recv()
            push(do_buf, do_out.at[i], do_send.at[i], do_recv.at[i], home[i]).wait_send()
            push(o_ref.at[i], o_got.at[z % 2], o_send.at[i], o_recv.at[z % 2], home[i]).wait_send()


def text_mid(o, x, g, mod, owner, own, mask, lmask, wo, w1, w2, pair_o, pair_1, pair_2, n_z, cid):
    pad, width = x.shape
    rank, share = pair_o[0].shape
    total = n_z * pad
    hidden = w1.shape[1]
    wide = width + rank
    f32, bf16 = jnp.float32, jnp.bfloat16
    shape = jax.ShapeDtypeStruct
    vmem = pltpu.VMEM
    dma = pltpu.SemaphoreType.DMA
    args = (o, x, g, mod, owner, own, mask, lmask, wo, w1, w2, *pair_o, *pair_1, *pair_2)
    out_shape = [
        shape((pad, width), bf16), shape((pad, width), f32), shape((2, total, share), bf16), shape((8, width), f32),
        shape((rank, share), f32), shape((rank, share), f32), shape((rank, share), f32), shape((rank, hidden), f32),
        shape((rank, hidden), f32), shape((rank, share), f32),
    ]
    return pl.pallas_call(
        functools.partial(text_mid_kernel, n_z),
        out_shape=out_shape,
        in_specs=[pl.BlockSpec(memory_space=vmem)] * len(args),
        out_specs=[pl.BlockSpec(memory_space=vmem)] * len(out_shape),
        scratch_shapes=[
            vmem((2, total, share), bf16), vmem((n_z, pad, wide), f32), vmem((n_z, pad, wide), bf16),
            vmem((3, n_z, pad, wide), bf16), vmem((n_z, pad, wide), bf16), vmem((n_z, pad, wide + rank), bf16),
            vmem((n_z, pad, width), bf16),
            vmem((total, hidden), f32), vmem((total, hidden), bf16), vmem((total, share), bf16),
            vmem((total, share), bf16), vmem((pad, width), f32), vmem((pad, width), f32), vmem((2, total, rank), bf16),
            dma((2,)), dma((2,)), dma((3, n_z)), dma((3, n_z)), dma((2, n_z)), dma((2, n_z)), dma((n_z,)), dma((n_z,)),
            dma((2,)), dma((2,)),
        ],
        compiler_params=pltpu.CompilerParams(collective_id=cid, has_side_effects=True, vmem_limit_bytes=50 * 1024 * 1024),
        name="text_block",
    )(*args)

HD = 64
FF = 6144
NAD = 8
RANK = 16
EPS = 1e-06
HIGH = lax.Precision.HIGHEST
F32 = jnp.float32
BF16 = jnp.bfloat16
BOTH = ("fsdp", "tp")


def matmul(left, right):
    return jnp.dot(left, right, preferred_element_type=F32)


def exact(left, right):
    return jnp.dot(left, right, precision=HIGH, preferred_element_type=F32)


def inner_left(left, right):
    return lax.dot_general(left, right, (((0,), (0,)), ((), ())), preferred_element_type=F32)


def inner_right(left, right):
    return lax.dot_general(
        left, right, (((left.ndim - 1,), (right.ndim - 1,)), ((), ())), preferred_element_type=F32
    )


def layer_norm(values):
    center = values - jnp.mean(values, axis=-1, keepdims=True)
    inverse = lax.rsqrt(jnp.mean(center * center, axis=-1, keepdims=True) + EPS)
    return (center * inverse, inverse)


def norm_back(grad_normed, normed, inverse, scale):
    grad_hat = grad_normed * (1.0 + scale)
    return inverse * (
        grad_hat
        - jnp.mean(grad_hat, axis=-1, keepdims=True)
        - normed * jnp.mean(grad_hat * normed, axis=-1, keepdims=True)
    )


def gelu(value):
    return jax.nn.gelu(value, approximate=True)


def gelu_back(value, grad):
    return jax.vjp(gelu, value)[1](grad)[0]


def shards(
    image_tokens,
    text_tokens,
    conditioning,
    text_lengths,
    adapter_index,
    adapters,
    mod_weight,
    qkv_weight,
    out_weight,
    fc1_weight,
    fc2_weight,
    image_cot,
    text_cot,
):
    n_f, n_z = lax.axis_size("fsdp"), lax.axis_size("tp")
    f, z = lax.axis_index("fsdp"), lax.axis_index("tp")
    core = f % 2
    slots, quarter, width = image_tokens.shape
    txt_local = text_tokens.shape[0]
    txt_group = txt_local * n_z
    img_half = 2 * quarter
    img_n = 2 * img_half
    cols = [6 * width, 3 * width, width, FF, width]
    fans = [width, width, width, width, FF]

    def round_pairs(r):
        pairs = []
        for fa in range(n_f):
            for t in range(n_z):
                there = (fa // 2 * 2 + t // 2) * n_z + 2 * (fa % 2) + (r ^ (t % 2))
                pairs.append((fa * n_z + t, there))
        return pairs

    low_bit = z % 2

    def pick(stack, bit):
        return lax.dynamic_index_in_dim(stack, bit, 0, keepdims=False)

    def flip(r):
        return low_bit if r == 0 else 1 - low_bit

    def to_chip(parts):
        got = [lax.ppermute(parts[r], BOTH, round_pairs(r)) for r in range(2)]
        return jnp.where(low_bit == 0, got[0], got[1]), jnp.where(low_bit == 0, got[1], got[0])

    def from_chip(pieces):
        got = []
        for r in range(2):
            mine = jnp.where(flip(r) == 0, pieces[0], pieces[1])
            got.append(lax.ppermute(mine, BOTH, [(b, a) for a, b in round_pairs(r)]))
        return jnp.where(low_bit == 0, got[0], got[1]), jnp.where(low_bit == 0, got[1], got[0])

    def reshard(values):
        return jnp.concatenate(to_chip([pick(values, flip(r)) for r in range(2)]), axis=0)

    def unshard(values):
        return jnp.stack(from_chip([values[:quarter], values[quarter:]]))

    def swap_core(values):
        return lax.ppermute(values, "fsdp", [(i, i ^ 1) for i in range(n_f)])

    def by_core(mine, other, axis):
        first = jnp.where(core == 0, mine, other)
        second = jnp.where(core == 0, other, mine)
        return jnp.concatenate([first, second], axis=axis)

    def z_swap(values, step):
        return lax.ppermute(values, "tp", [(i, i ^ step) for i in range(n_z)])

    def z_order(pieces):
        stack = jnp.stack(pieces)
        return [pick(stack, z ^ a) for a in range(n_z)]

    def z_gather(values):
        return z_order([values] + [z_swap(values, j) for j in range(1, n_z)])

    def z_exchange(blocks):
        return z_order([pick(blocks, z ^ j) if j == 0 else z_swap(pick(blocks, z ^ j), j) for j in range(n_z)])

    def z_scatter(values):
        count = values.shape[0] // n_z
        mine = lax.dynamic_slice_in_dim(values, z * count, count, 0)
        for j in range(1, n_z):
            part = lax.dynamic_slice_in_dim(values, (z ^ j) * count, count, 0)
            mine = mine + z_swap(part.astype(BF16), j).astype(F32)
        return mine

    def to_heads(values):
        half = values.shape[1] // 2
        low, high = values[:, :half], values[:, half:]
        mine = jnp.where(core == 0, low, high)
        return by_core(mine, swap_core(jnp.where(core == 0, high, low)), 0)

    def to_tokens(values):
        low, high = values[:img_half], values[img_half:]
        mine = jnp.where(core == 0, low, high)
        return by_core(mine, swap_core(jnp.where(core == 0, high, low)), 1)

    out_t = jnp.swapaxes(out_weight, 1, 2)
    fc2_t = jnp.swapaxes(fc2_weight, 1, 2)
    local = [qkv_weight, out_t, fc1_weight, fc2_t]
    adapter_rows = adapters.astype(BF16).reshape(-1, 128)
    got = gather([w[0] for w in local], [w[1] for w in local] + [adapter_rows], n_f, n_z)
    got = [g.reshape(-1, g.shape[-1]) for g in got]
    img_w, txt_w, row = got[:4], got[4:8], got[8]
    x_img = reshard(image_tokens)
    g_img = reshard(image_cot)
    txt_pad = (txt_local + 15) // 16 * 16

    def padded(values):
        return jnp.pad(values, ((0, txt_pad - txt_local), (0, 0)))

    x_txt_low, g_txt_low = padded(text_tokens), padded(text_cot)
    x_txt = x_txt_low.astype(F32)

    seg_ends = jnp.cumsum(text_lengths[0])
    slot_ids = jnp.arange(slots)

    def owner_of(position):
        segment = jnp.sum((position[:, None] >= seg_ends[None, :]).astype(jnp.int32), axis=1)
        return (segment[:, None] == slot_ids[None, :]).astype(F32)

    def real(owner):
        place = jnp.arange(owner.shape[0]) % txt_pad
        return jnp.where((place < txt_local)[:, None], owner, 0.0)

    def position(rows):
        return rows // txt_pad * txt_local + rows % txt_pad

    txt_rows = jnp.arange(n_z * txt_pad)
    owner_group = real(owner_of(position(txt_rows)))
    owner_local = real(owner_of(z * txt_local + jnp.arange(txt_pad)))
    txt_mask = jnp.repeat(owner_group, RANK, axis=1)
    txt_mask_local = jnp.repeat(owner_local, RANK, axis=1)
    rank_cols = slots * RANK
    seq_mask = jnp.repeat(jnp.eye(slots, dtype=F32), RANK, axis=1)

    def by_group(mine, other):
        return by_core(mine, other, 0)

    column_picks = by_group(adapter_index, swap_core(adapter_index))
    column_count = 2 * slots
    one_hot = (
        jnp.arange(NAD * RANK)[:, None]
        == (column_picks[:, None] * RANK + jnp.arange(RANK)[None, :]).reshape(1, -1)
    ).astype(F32)
    own_picks = adapter_index
    own_hot = lax.dynamic_slice_in_dim(one_hot, core * slots * RANK, slots * RANK, 1)

    a_rows = [[None] * 5 for stream in range(2)]
    b_rows = [[None] * 5 for stream in range(2)]
    offset = 0
    for stream in range(2):
        for index in range(5):
            count = fans[index] // n_z
            a_rows[stream][index] = row[offset : offset + count]
            offset += count
            count = cols[index] // n_z
            b_rows[stream][index] = row[offset : offset + count]
            offset += count

    def b_pick(stream, index, pick_index):
        part = b_rows[stream][index]
        count = part.shape[0] // NAD
        return lax.dynamic_slice_in_dim(part, pick_index * count, count, 0).reshape(RANK, -1)

    def a_pick(rows, hot):
        return inner_right(hot.T.astype(BF16), rows).astype(BF16)

    img_a = a_pick(jnp.concatenate(a_rows[0], axis=0), one_hot)
    fan_share = sum(fans) // n_z
    img_a = img_a.reshape(column_count, RANK, fan_share)
    img_b = [
        jnp.concatenate([b_pick(0, index, column_picks[s]) for index in range(1, 5)], axis=1)
        for s in range(column_count)
    ]
    img_msg = jnp.concatenate([img_a, jnp.stack(img_b)], axis=2)
    txt_a_rows = jnp.concatenate(
        [a_rows[0][0], a_rows[1][0], a_rows[1][1], a_rows[1][3]], axis=0
    )
    txt_a = a_pick(txt_a_rows, own_hot).reshape(slots, RANK, -1)
    txt_b_own = [
        [b_pick(stream, index, own_picks[s]) for s in range(slots)]
        for stream, index in [(0, 0), (1, 0), (1, 1), (1, 2), (1, 3), (1, 4)]
    ]
    txt_b_own = [jnp.concatenate(parts, axis=0) for parts in txt_b_own]
    txt_a_own = a_pick(jnp.concatenate([a_rows[1][2], a_rows[1][4]], axis=0), own_hot)
    txt_msg = jnp.concatenate(
        [txt_a.reshape(slots * RANK, -1), txt_b_own[3], txt_b_own[5]], axis=1
    )
    img_got = jnp.stack(z_exchange(img_msg))
    txt_got = jnp.stack(z_gather(txt_msg))

    def join(part):
        return jnp.swapaxes(part, 0, 1).reshape(part.shape[1], -1)

    img_pairs = []
    offset, b_offset = 0, fan_share
    for index in range(5):
        count = fans[index] // n_z
        a_full = join(img_got[:, :, offset : offset + count])
        offset += count
        if index == 0:
            img_pairs.append(None)
            continue
        count = cols[index] // n_z
        b_full = join(img_got[:, :, b_offset : b_offset + count])
        b_offset += count
        img_pairs.append((a_full, b_full))
    txt_full = []
    offset = 0
    for count in [width // n_z] * 6:
        txt_full.append(join(txt_got[:, :, offset : offset + count]))
        offset += count
    mod_a = [txt_full[0], txt_full[1]]
    mod_b = [txt_b_own[0], txt_b_own[1]]
    txt_pairs = [
        None,
        (txt_full[2], txt_b_own[2]),
        (txt_a_own[:, : width // n_z], txt_full[4]),
        (txt_full[3], txt_b_own[4]),
        (txt_a_own[:, width // n_z :], txt_full[5]),
    ]

    k_local = mod_weight.shape[1]
    cond_act = jax.nn.silu(conditioning).astype(BF16)
    cond_all = lax.all_gather(cond_act, "fsdp", axis=0, tiled=True)
    cond_slice = lax.dynamic_slice_in_dim(cond_all, f * k_local, k_local, 1)
    mod_part = jnp.stack([matmul(cond_slice, mod_weight[stream]) for stream in range(2)], axis=1)
    mod_part = lax.psum_scatter(mod_part, "fsdp", scatter_dimension=0, tiled=True)
    mod_mid = []
    mod_terms = []
    for stream in range(2):
        middle = (inner_right(cond_act, mod_a[stream]) * seq_mask).astype(BF16)
        mod_mid.append(middle)
        mod_terms.append(mod_part[:, stream] + matmul(middle, mod_b[stream]))
    mods = jnp.concatenate(z_gather(jnp.stack(mod_terms, axis=1)), axis=2)
    img_mods = by_group(mods[:, 0], swap_core(mods[:, 0]))
    img_mod = lax.dynamic_slice_in_dim(img_mods, z, 1, 0)
    txt_mods = mods[:, 1]

    def stretch(stream, index):
        if stream == 0:
            return img_mod[:, index * width : (index + 1) * width]
        return exact(owner_local, txt_mods[:, index * width : (index + 1) * width])

    def collapse(stream, values):
        if stream == 0:
            return jnp.sum(values, axis=0, keepdims=True)
        return exact(owner_local.T, values)

    def share(values):
        return jnp.concatenate(z_gather(values), axis=0)

    def give(values, rank_part):
        got = z_scatter(jnp.concatenate([values, rank_part], axis=1))
        return got[:, :width], (got[:, width:] * txt_mask_local).astype(BF16)

    def lanes(values):
        count = values.shape[1] // n_z
        return lax.dynamic_slice_in_dim(values, z * count, count, 1)

    inputs = [x_img.astype(F32), x_txt]
    norm_one = [layer_norm(values) for values in inputs]
    heads_in = [
        (norm_one[s][0] * (1.0 + stretch(s, 1)) + stretch(s, 0)).astype(BF16) for s in range(2)
    ]

    def project(values, weight, pair, mask, flipped):
        middle = inner_right(values, pair[0])
        if mask is not None:
            middle = middle * mask
        middle = middle.astype(BF16)
        main = inner_right(values, weight) if flipped else matmul(values, weight)
        return middle, main + matmul(middle, pair[1])

    txt_in = share(heads_in[1])
    txt_qkv_mid, txt_qkv = project(txt_in, txt_w[0], txt_pairs[1], txt_mask, False)
    img_qkv_mid, img_qkv = project(heads_in[0], img_w[0], img_pairs[1], None, False)
    txt_qkv, img_qkv = txt_qkv.astype(BF16), img_qkv.astype(BF16)
    img_heads = to_heads(img_qkv)
    txt_heads = jnp.stack(to_chip([txt_qkv, txt_qkv]))
    lengths = by_group(text_lengths[0:1], swap_core(text_lengths[0:1]))
    chip_lengths = jnp.cumsum(lax.dynamic_index_in_dim(lengths, z // slots, 0, keepdims=False))
    chip_slot = z % slots
    chip_segment = jnp.sum(
        (position(txt_rows)[:, None] >= chip_lengths[None, :]).astype(jnp.int32),
        axis=1,
        keepdims=True,
    )
    chip_owner = (chip_segment == chip_slot) & (txt_rows % txt_pad < txt_local)[:, None]
    bias = jnp.where(chip_owner, 0.0, -1e30).astype(F32)
    o_img, o_txt, lse = attend(img_heads, txt_heads, bias, HD)

    def txt_home(values):
        got = from_chip([values[0], values[1]])
        return jnp.where(owner_group[:, 0:1] > 0, got[0], jnp.where(owner_group[:, 1:2] > 0, got[1], 0))

    attended = to_tokens(o_img)
    thick = 128

    def thicker(part):
        return jnp.concatenate([part, jnp.zeros((thick - part.shape[0], part.shape[1]), part.dtype)], axis=0)

    def sign(owner):
        return owner[:, 0:1] - owner[:, 1:2]

    def lanes_pad(mask):
        return jnp.pad(mask, ((0, 0), (0, thick - mask.shape[1])))

    txt_mod = jnp.pad(txt_mods.reshape(slots, 6, width), ((0, 0), (0, 2), (0, 0))).reshape(-1, width)
    thick_pairs = [None] + [tuple(thicker(part) for part in txt_pairs[index]) for index in range(1, 5)]
    (txt_result, txt_grad_after, do_txt, txt_sums, *txt_sides) = text_mid(
        o_txt, x_txt_low, g_txt_low, txt_mod, sign(owner_group), sign(owner_local), lanes_pad(txt_mask),
        lanes_pad(txt_mask_local), txt_w[1], txt_w[2], txt_w[3], thick_pairs[2], thick_pairs[3], thick_pairs[4],
        n_z, 2,
    )
    txt_sides = [part[:rank_cols] for part in txt_sides]
    txt_sums = txt_sums.reshape(4, slots, width)

    img_rows_mod = jnp.concatenate([img_mod.reshape(6, width), jnp.zeros((2, width), F32)], axis=0)
    (img_branch, img_after, img_mlp, img_pre, img_result, *img_mids, img_gate) = block_fwd(
        attended, x_img, g_img, img_rows_mod, img_w[1], img_pairs[2], img_pairs[3], img_w[2],
        img_pairs[4], img_w[3],
    )
    image_out = unshard(img_result)

    grads = [[None] * 5 for stream in range(2)]

    def project_back(grad, weight, pair, mask, flipped):
        middle = inner_right(grad, pair[1])
        if mask is not None:
            middle = middle * mask
        middle = middle.astype(BF16)
        main = matmul(grad, weight) if flipped else inner_right(grad, weight)
        return middle, main + matmul(middle, pair[0])

    (img_grad_after, img_grad_att, img_sums, *sides) = block_back(
        g_img, img_after, img_branch, img_mlp, attended, img_rows_mod, img_pre, img_w[3],
        img_pairs[4], img_w[2], img_pairs[3], img_w[1], img_pairs[2], img_mids,
    )
    grads[0][4] = (sides[0], sides[3])
    grads[0][3] = (sides[2], sides[1])
    grads[0][2] = (sides[4], sides[5])
    mod_parts = [[None] * 6 for stream in range(2)]
    for place in range(4):
        mod_parts[1][2 + place] = txt_sums[place]
    grads[1][2] = (txt_sides[0], txt_sides[1])
    grads[1][3] = (txt_sides[2], txt_sides[3])
    grads[1][4] = (txt_sides[4], txt_sides[5])
    img_sums = jnp.sum(jnp.concatenate([img_sums, img_gate]).reshape(4, 8, width), axis=1)
    for place in range(4):
        mod_parts[0][2 + place] = img_sums[place : place + 1]
    grad_after = [img_grad_after, txt_grad_after]

    do_img = to_heads(img_grad_att)
    d_img, d_txt = attend_back(img_heads, txt_heads, bias, do_img, do_txt, lse, HD)
    img_grad_qkv = to_tokens(d_img)
    txt_grad_qkv = txt_home(d_txt)

    img_back_mid, img_grad_norm = project_back(img_grad_qkv, img_w[0], img_pairs[1], None, False)
    grads[0][1] = (inner_left(img_back_mid, heads_in[0]), inner_left(img_qkv_mid, img_grad_qkv))
    txt_grad_norm, txt_qkv_back = give(
        inner_right(txt_grad_qkv, txt_w[0]), inner_right(txt_grad_qkv, txt_pairs[1][1])
    )
    txt_grad_norm = txt_grad_norm + matmul(txt_qkv_back, txt_pairs[1][0])
    grads[1][1] = (
        inner_left(share(txt_qkv_back), lanes(txt_in)),
        inner_left(txt_qkv_mid, txt_grad_qkv),
    )
    grad_norm = [img_grad_norm, txt_grad_norm]
    grad_inputs = []
    for s in range(2):
        grad_inputs.append(
            grad_after[s]
            + norm_back(grad_norm[s], norm_one[s][0], norm_one[s][1], stretch(s, 1))
        )
        mod_parts[s][0] = collapse(s, grad_norm[s])
        mod_parts[s][1] = collapse(s, grad_norm[s] * norm_one[s][0])
    image_grad = unshard(grad_inputs[0].astype(BF16)).astype(F32)

    img_dmod = jnp.concatenate(mod_parts[0], axis=1)
    img_dmod = (img_dmod + swap_core(img_dmod)).astype(BF16)
    def lane_blocks(values):
        return jnp.swapaxes(values.reshape(values.shape[0], n_z, -1), 0, 1)

    img_dmods = jnp.concatenate(z_exchange(lane_blocks(img_dmod)), axis=0)
    img_dmods = lax.dynamic_slice_in_dim(img_dmods, core * slots, slots, 0)
    txt_dmod = jnp.concatenate(mod_parts[1], axis=1)
    txt_dmods = sum(z_exchange(lane_blocks(txt_dmod))).astype(BF16)
    dmods = jnp.stack([img_dmods, txt_dmods], axis=1)
    dmods_all = lax.all_gather(dmods, "fsdp", axis=0, tiled=True)
    cond_part = sum(inner_right(dmods_all[:, s], mod_weight[s]) for s in range(2))
    mod_back = [inner_right(dmods[:, s], mod_b[s]) for s in range(2)]
    cond_part = cond_part.reshape(-1, width // n_f)
    joined = jnp.concatenate([cond_part.reshape(-1), jnp.stack(mod_back).reshape(-1)])
    joined = sum(z_gather(joined))
    cond_slices = joined[: cond_part.size].reshape(n_f, -1, width // n_f)
    mod_rank = joined[cond_part.size :].reshape(2, slots, -1)
    cond_rows = lax.all_to_all(cond_slices, "fsdp", 0, 2, tiled=True)[0]
    for s in range(2):
        back_mid = (mod_rank[s] * seq_mask).astype(BF16)
        cond_rows = cond_rows + matmul(back_mid, mod_a[s])
        grads[s][0] = (inner_left(back_mid, lanes(cond_act)), inner_left(mod_mid[s], dmods[:, s]))
    cond_grad = jax.vjp(jax.nn.silu, conditioning)[1](cond_rows)[0]

    def spread(values):
        return jnp.swapaxes(values.reshape(RANK, n_z, -1), 0, 1)

    img_rows = {}
    for group in ((2, 3, 4), (1,)):
        parts = [spread(grads[0][index][side]) for side in range(2) for index in group]
        parts = jnp.concatenate(z_exchange(jnp.concatenate(parts, axis=2)), axis=0)
        offset = 0
        for side, sizes in enumerate((fans, cols)):
            for index in group:
                count = sizes[index] // n_z
                img_rows[side, index] = parts[:, offset : offset + count]
                offset += count
    flat = []
    for stream in range(2):
        for index in range(5):
            if stream == 0 and index > 0:
                part_a, part_b = img_rows[0, index], img_rows[1, index]
                hot = one_hot
            else:
                part_a, part_b = grads[stream][index]
                hot = own_hot
            flat.append(
                lax.dot_general(
                    part_a, hot, (((0,), (1,)), ((), ())),
                    precision=HIGH, preferred_element_type=F32,
                )
            )
            flat.append(exact(hot, part_b).reshape(-1, 128))
    total = jnp.concatenate(flat, axis=0).reshape(n_f, -1, 128)
    step = 1
    while step < n_f:
        bit = (f // step) % 2
        pairs = total.reshape((-1, 2) + total.shape[1:])
        keep = lax.dynamic_index_in_dim(pairs, bit, 1, keepdims=False)
        send = lax.dynamic_index_in_dim(pairs, 1 - bit, 1, keepdims=False)
        sent = lax.ppermute(send.astype(BF16), "fsdp", [(i, i ^ step) for i in range(n_f)])
        total = keep + sent.astype(F32)
        step *= 2
    adapter_grad = total.reshape(1, -1)
    return (
        image_out, txt_result[:txt_local], image_grad, grad_inputs[1][:txt_local], cond_grad, adapter_grad
    )


def solution(mesh):
    return jax.shard_map(
        shards,
        mesh=mesh,
        in_specs=(
            P("fsdp", "tp", None),
            P(("fsdp", "tp"), None),
            P("fsdp", None),
            P("fsdp", None),
            P("fsdp"),
            P("tp", "fsdp"),
            P(None, "fsdp", "tp"),
            P(None, "fsdp", "tp"),
            P(None, "tp", "fsdp"),
            P(None, "fsdp", "tp"),
            P(None, "tp", "fsdp"),
            P("fsdp", "tp", None),
            P(("fsdp", "tp"), None),
        ),
        out_specs=(
            P("fsdp", "tp", None),
            P(("fsdp", "tp"), None),
            P("fsdp", "tp", None),
            P(("fsdp", "tp"), None),
            P("fsdp", None),
            P("tp", "fsdp"),
        ),
        check_vma=False,
    )
```

```python
import functools

import jax
import jax.numpy as jnp
from jax import lax
from jax.experimental import pallas as pl
from jax.experimental.pallas import tpu as pltpu
from jax.sharding import PartitionSpec as P

MESH = pl.DeviceIdType.MESH

def bits_of(count):
    return max(count.bit_length() - 1, 0)

def halves(width):
    tiles = width // 128
    first = (tiles + 1) // 2 * 128
    return [(0, first), (first, width - first)]

def gather_kernel(n_f, n_z, full_count, part_count, *refs):
    total = full_count + part_count
    ins, outs = refs[:total], refs[total:2 * total]
    z_send, z_recv, xy_send, xy_recv, core_send, core_recv, own_sem = refs[2 * total:]
    f = lax.axis_index("fsdp")
    z = lax.axis_index("tp")
    chip, core = f // 2, f % 2
    chips = n_f // 2
    nbits = bits_of(chips)
    partner = chip * 2 + (1 - core)

    def peer_of(mask):
        other = 0
        for bit in range(nbits):
            have = (chip // (1 << bit)) % 2
            want = 1 - have if (mask >> bit) & 1 else have
            other = other + want * (1 << bit)
        return other * 2 + core

    barrier = pltpu.get_barrier_semaphore()
    for bit in range(nbits):
        pl.semaphore_signal(barrier, inc=1, device_id=(peer_of(1 << bit), z), device_id_type=MESH)
    pl.semaphore_signal(barrier, inc=1, device_id=(partner, z), device_id_type=MESH)
    @pl.when(z > 0)
    def _():
        pl.semaphore_signal(barrier, inc=1, device_id=(f, z - 1), device_id_type=MESH)
    @pl.when(z < n_z - 1)
    def _():
        pl.semaphore_signal(barrier, inc=1, device_id=(f, z + 1), device_id_type=MESH)
    peers = nbits + 1 + (z > 0).astype(jnp.int32) + (z < n_z - 1).astype(jnp.int32)
    pl.semaphore_wait(barrier, peers)

    def width(m):
        return ins[m].shape[-1]

    def place(m, who, zz, off=0, w=None):
        w = width(m) if w is None else w
        if m < full_count:
            return outs[m].at[who, :, pl.ds(pl.multiple_of(zz * width(m) + off, 128), w)]
        if w == width(m):
            return outs[m].at[who]
        return outs[m].at[who, :, pl.ds(off, w)]

    def piece(m, off, w):
        return ins[m] if w == width(m) else ins[m].at[:, pl.ds(off, w)]

    def remote(src, dst, ssem, rsem, dev):
        return pltpu.make_async_remote_copy(src_ref=src, dst_ref=dst, send_sem=ssem, recv_sem=rsem, device_id=dev, device_id_type=MESH)

    def order_of(half):
        order = list(range(nbits))
        return order if half == 0 else order[::-1]

    def cuts(m):
        if width(m) >= 256:
            return list(enumerate(halves(width(m))))
        return [(m % 2, (0, width(m)))]

    def slot(m, zz):
        return zz if m < full_count else 0

    def xy_copy(m, zz, half, cut, mask, bit, own_piece=False):
        off, w = cut
        who = peer_of(mask)
        source = piece(m, off, w) if own_piece and mask == 0 else place(m, who, zz, off, w)
        return remote(source, place(m, who, zz, off, w),
                      xy_send.at[m, slot(m, zz), half, mask, bit], xy_recv.at[m, slot(m, zz), half, mask | (1 << bit)],
                      (peer_of(1 << bit), z))

    def xy_wait(m, zz, half, cut, mask):
        off, w = cut
        who = peer_of(mask)
        remote(place(m, who, zz, off, w), place(m, who, zz, off, w), xy_send.at[m, slot(m, zz), half, 0, 0],
               xy_recv.at[m, slot(m, zz), half, mask], (partner, z)).wait_recv()

    def core_copy(m, zz, half, cut, mask, own_piece=False):
        off, w = cut
        who = peer_of(mask)
        source = piece(m, off, w) if own_piece and mask == 0 else place(m, who, zz, off, w)
        return remote(source, place(m, who, zz, off, w),
                      core_send.at[m, slot(m, zz), half, mask], core_recv.at[m, slot(m, zz), half, mask], (partner, z))

    def core_wait_recv(m, zz, half, cut, mask):
        off, w = cut
        who = peer_of(mask) - core + (1 - core)
        remote(place(m, who, zz, off, w), place(m, who, zz, off, w),
               core_send.at[m, slot(m, zz), half, mask], core_recv.at[m, slot(m, zz), half, mask], (partner, z)).wait_recv()

    def own(m):
        return pltpu.make_async_copy(ins[m], place(m, f, z), own_sem.at[m])

    def z_copy(m, zz, up, own_piece=False):
        return remote(ins[m] if own_piece else place(m, f, zz), place(m, f, zz), z_send.at[m, zz, up], z_recv.at[m, zz], (f, z + 1 if up else z - 1))

    def launch(m, zz, own_piece=False):
        for half, cut in cuts(m):
            for bit in order_of(half):
                xy_copy(m, zz, half, cut, 0, bit, own_piece).start()
            core_copy(m, zz, half, cut, 0, own_piece).start()

    def masks_in_order(half):
        order = order_of(half)
        def rank(mask):
            return [1 if (mask >> b) & 1 else 0 for b in reversed(order)]
        return sorted(range(1, 1 << nbits), key=rank)

    def forward(m, zz):
        for half, cut in cuts(m):
            order = order_of(half)
            for mask in masks_in_order(half):
                last = max(i for i, b in enumerate(order) if (mask >> b) & 1)
                if last == nbits - 1:
                    continue
                xy_wait(m, zz, half, cut, mask)
                for b in order[last + 1:]:
                    xy_copy(m, zz, half, cut, mask, b).start()
                core_copy(m, zz, half, cut, mask).start()

    def finish(m, zz):
        for half, cut in cuts(m):
            order = order_of(half)
            for mask in masks_in_order(half):
                last = max(i for i, b in enumerate(order) if (mask >> b) & 1)
                if last == nbits - 1:
                    xy_wait(m, zz, half, cut, mask)
                    core_copy(m, zz, half, cut, mask).start()

    def drain(m, zz):
        for half, cut in cuts(m):
            order = order_of(half)
            for mask in [0] + masks_in_order(half):
                last = max([i for i, b in enumerate(order) if (mask >> b) & 1], default=-1)
                for b in order[last + 1:]:
                    xy_copy(m, zz, half, cut, mask, b).wait_send()
                core_copy(m, zz, half, cut, mask).wait_send()
                core_wait_recv(m, zz, half, cut, mask)

    for m in range(total):
        own(m).start()
    for m in range(total):
        if m < full_count:
            @pl.when(z < n_z - 1)
            def _():
                z_copy(m, z, 1, True).start()
            @pl.when(z > 0)
            def _():
                z_copy(m, z, 0, True).start()
        launch(m, z, True)
    for m in range(full_count, total):
        forward(m, z)
    for k in range(1, n_z):
        for m in range(full_count):
            @pl.when(z - k >= 0)
            def _():
                zz = z - k
                z_copy(m, zz, 1).wait_recv()
                @pl.when(z < n_z - 1)
                def _():
                    z_copy(m, zz, 1).start()
                launch(m, zz)
            @pl.when(z + k < n_z)
            def _():
                zz = z + k
                z_copy(m, zz, 0).wait_recv()
                @pl.when(z > 0)
                def _():
                    z_copy(m, zz, 0).start()
                launch(m, zz)
            for sign in ((-1, 1) if k > 1 else (1,)):
                zz = z + sign * (k - 1)
                @pl.when((zz >= 0) & (zz < n_z))
                def _():
                    forward(m, zz)
    for m in range(full_count):
        for sign in (-1, 1):
            zz = z + sign * (n_z - 1)
            @pl.when((zz >= 0) & (zz < n_z))
            def _():
                forward(m, zz)
    for m in range(total):
        if m < full_count:
            def body(zz, _):
                finish(m, zz)
                return 0
            lax.fori_loop(0, n_z, body, 0)
        else:
            finish(m, z)
    for m in range(total):
        own(m).wait()
        if m < full_count:
            def body(zz, _):
                drain(m, zz)
                @pl.when((zz <= z) & (z < n_z - 1))
                def _():
                    z_copy(m, zz, 1).wait_send()
                @pl.when((zz >= z) & (z > 0))
                def _():
                    z_copy(m, zz, 0).wait_send()
                return 0
            lax.fori_loop(0, n_z, body, 0)
        else:
            drain(m, z)

def gather(full, part, n_f, n_z, cid=1):
    arrays = list(full) + list(part)
    total = len(arrays)
    if n_f > 8:
        rows = [lax.all_gather(a, "fsdp", axis=0, tiled=True) for a in arrays]
        return [
            lax.all_gather(a, "tp", axis=1, tiled=True) if i < len(full) else a
            for i, a in enumerate(rows)
        ]
    chips = n_f // 2
    nbits = bits_of(chips)
    shapes = [jax.ShapeDtypeStruct((n_f,) + a.shape[:-1] + (a.shape[-1] * (n_z if i < len(full) else 1),), a.dtype) for i, a in enumerate(arrays)]
    dma = pltpu.SemaphoreType.DMA
    return pl.pallas_call(
        functools.partial(gather_kernel, n_f, n_z, len(full), len(part)),
        out_shape=shapes,
        in_specs=[pl.BlockSpec(memory_space=pl.ANY)] * total,
        out_specs=[pl.BlockSpec(memory_space=pl.ANY)] * total,
        scratch_shapes=[
            dma((total, n_z, 2)), dma((total, n_z)),
            dma((total, n_z, 2, chips, max(nbits, 1))), dma((total, n_z, 2, chips)),
            dma((total, n_z, 2, chips)), dma((total, n_z, 2, chips)), dma((total,)),
        ],
        compiler_params=pltpu.CompilerParams(collective_id=cid, has_side_effects=True),
        name="weight_gather",
    )(*arrays)

def dots(left, right, lc, rc):
    return lax.dot_general(left, right, (((lc,), (rc,)), ((), ())), preferred_element_type=jnp.float32)

def attend_kernel(hd, bq, img_ref, txt_ref, bias_ref, oi_ref, ot_ref, lse_ref):
    img_n, txt_n = img_ref.shape[0], txt_ref.shape[1]
    heads = img_ref.shape[1] // (3 * hd)
    bias = bias_ref[...]
    for h in range(heads):
        base = 3 * hd * h
        ki = img_ref[:, base + hd:base + 2 * hd]
        vi = img_ref[:, base + 2 * hd:base + 3 * hd]
        kt = txt_ref[0, :, base + hd:base + 2 * hd]
        vt = txt_ref[0, :, base + 2 * hd:base + 3 * hd]

        def block(q):
            q = q * jnp.bfloat16(0.125)
            si = dots(ki, q, 1, 1)
            st = dots(kt, q, 1, 1) + bias
            top = jnp.maximum(jnp.max(si, axis=0, keepdims=True), jnp.max(st, axis=0, keepdims=True))
            ei = jnp.exp(si - top)
            et = jnp.exp(st - top)
            total = jnp.sum(ei, axis=0, keepdims=True) + jnp.sum(et, axis=0, keepdims=True)
            o = dots(vi, ei.astype(jnp.bfloat16), 0, 0) + dots(vt, et.astype(jnp.bfloat16), 0, 0)
            return (o / total).T.astype(jnp.bfloat16), top + jnp.log(total)

        for i in range(img_n // bq):
            o, lse = block(img_ref[i * bq:(i + 1) * bq, base:base + hd])
            oi_ref[i * bq:(i + 1) * bq, h * hd:(h + 1) * hd] = o
            lse_ref[0, h:h + 1, i * bq:(i + 1) * bq] = lse
        o, lse = block(txt_ref[0, :, base:base + hd])
        ot_ref[0, :, h * hd:(h + 1) * hd] = o
        lse_ref[0, h:h + 1, img_n:img_n + txt_n] = lse

def attend(img, txt, bias, hd, bq=512):
    img_n, cols = img.shape
    parts, txt_n, _ = txt.shape
    pairs = cols // (6 * hd)
    per = pairs // parts
    return pl.pallas_call(
        functools.partial(attend_kernel, hd, bq),
        grid=(pairs,),
        in_specs=[
            pl.BlockSpec((img_n, 6 * hd), lambda i: (0, i)),
            pl.BlockSpec((1, txt_n, 6 * hd), lambda i: (i // per, 0, i % per)),
            pl.BlockSpec((txt_n, 1), lambda i: (0, 0)),
        ],
        out_specs=[
            pl.BlockSpec((img_n, 2 * hd), lambda i: (0, i)),
            pl.BlockSpec((1, txt_n, 2 * hd), lambda i: (i // per, 0, i % per)),
            pl.BlockSpec((1, 2, img_n + txt_n), lambda i: (i, 0, 0)),
        ],
        out_shape=[
            jax.ShapeDtypeStruct((img_n, pairs * 2 * hd), jnp.bfloat16),
            jax.ShapeDtypeStruct((parts, txt_n, per * 2 * hd), jnp.bfloat16),
            jax.ShapeDtypeStruct((pairs, 2, img_n + txt_n), jnp.float32),
        ],
        compiler_params=pltpu.CompilerParams(vmem_limit_bytes=48 * 1024 * 1024),
        name="attend",
    )(img, txt, bias)

def attend_back_kernel(hd, bq, img_ref, txt_ref, bias_ref, doi_ref, dot_ref, lse_ref, di_ref, dt_ref, acc_i, acc_t):
    img_n, txt_n = img_ref.shape[0], txt_ref.shape[1]
    heads = img_ref.shape[1] // (3 * hd)
    bias = bias_ref[...]
    for h in range(heads):
        base = 3 * hd * h
        ki = img_ref[:, base + hd:base + 2 * hd]
        vi = img_ref[:, base + 2 * hd:base + 3 * hd]
        kt = txt_ref[0, :, base + hd:base + 2 * hd]
        vt = txt_ref[0, :, base + 2 * hd:base + 3 * hd]

        def block(q, do, lse, first):
            q = q * jnp.bfloat16(0.125)
            pi = jnp.exp(dots(ki, q, 1, 1) - lse)
            pt = jnp.exp(dots(kt, q, 1, 1) + bias - lse)
            dwi = dots(vi, do, 1, 1)
            dwt = dots(vt, do, 1, 1)
            delta = jnp.sum(pi * dwi, axis=0, keepdims=True) + jnp.sum(pt * dwt, axis=0, keepdims=True)
            dsi = (pi * (dwi - delta)).astype(jnp.bfloat16)
            dst = (pt * (dwt - delta)).astype(jnp.bfloat16)
            dvi = dots(pi.astype(jnp.bfloat16), do, 1, 0)
            dvt = dots(pt.astype(jnp.bfloat16), do, 1, 0)
            dki = dots(dsi, q, 1, 0)
            dkt = dots(dst, q, 1, 0)
            if first:
                acc_i[0], acc_i[1], acc_t[0], acc_t[1] = dki, dvi, dkt, dvt
            else:
                acc_i[0] += dki
                acc_i[1] += dvi
                acc_t[0] += dkt
                acc_t[1] += dvt
            dq = dots(ki, dsi, 0, 0) + dots(kt, dst, 0, 0)
            return (dq.T * 0.125).astype(jnp.bfloat16)

        for i in range(img_n // bq):
            rows = slice(i * bq, (i + 1) * bq)
            di_ref[rows, base:base + hd] = block(
                img_ref[rows, base:base + hd], doi_ref[rows, h * hd:(h + 1) * hd], lse_ref[0, h:h + 1, rows], i == 0)
        grad = jnp.where(bias < 0, 0.0, dot_ref[0, :, h * hd:(h + 1) * hd].astype(jnp.float32)).astype(jnp.bfloat16)
        dt_ref[0, :, base:base + hd] = block(
            txt_ref[0, :, base:base + hd], grad, lse_ref[0, h:h + 1, img_n:img_n + txt_n], False)
        di_ref[:, base + hd:base + 2 * hd] = acc_i[0].astype(jnp.bfloat16)
        di_ref[:, base + 2 * hd:base + 3 * hd] = acc_i[1].astype(jnp.bfloat16)
        dt_ref[0, :, base + hd:base + 2 * hd] = acc_t[0].astype(jnp.bfloat16)
        dt_ref[0, :, base + 2 * hd:base + 3 * hd] = acc_t[1].astype(jnp.bfloat16)

def attend_back(img, txt, bias, doi, dot, lse, hd, bq=512):
    img_n, cols = img.shape
    parts, txt_n, _ = txt.shape
    pairs = cols // (6 * hd)
    per = pairs // parts
    wide = pl.BlockSpec((img_n, 6 * hd), lambda i: (0, i))
    wide_t = pl.BlockSpec((1, txt_n, 6 * hd), lambda i: (i // per, 0, i % per))
    return pl.pallas_call(
        functools.partial(attend_back_kernel, hd, bq),
        grid=(pairs,),
        in_specs=[
            wide, wide_t,
            pl.BlockSpec((txt_n, 1), lambda i: (0, 0)),
            pl.BlockSpec((img_n, 2 * hd), lambda i: (0, i)),
            pl.BlockSpec((1, txt_n, 2 * hd), lambda i: (i // per, 0, i % per)),
            pl.BlockSpec((1, 2, img_n + txt_n), lambda i: (i, 0, 0)),
        ],
        out_specs=[wide, wide_t],
        out_shape=[jax.ShapeDtypeStruct(img.shape, jnp.bfloat16), jax.ShapeDtypeStruct(txt.shape, jnp.bfloat16)],
        scratch_shapes=[pltpu.VMEM((2, img_n, hd), jnp.float32), pltpu.VMEM((2, txt_n, hd), jnp.float32)],
        compiler_params=pltpu.CompilerParams(vmem_limit_bytes=48 * 1024 * 1024),
        name="attend_back",
    )(img, txt, bias, doi, dot, lse)

ROWS = 64


def mm(left, right):
    return dots(left, right, 1, 0)


def mm_t(left, right):
    return dots(left, right, 1, 1)


def t_mm(left, right):
    return dots(left, right, 0, 0)


def gelu_parts(u):
    scale = 0.7978845608028654
    square = u * u
    tanh = jnp.tanh(scale * (u + 0.044715 * u * square))
    half = 0.5 * (1.0 + tanh)
    slope = half + 0.5 * u * (1.0 - tanh * tanh) * (scale * (1.0 + 3 * 0.044715 * square))
    return u * half, slope


def norm_rows(v):
    center = v - jnp.mean(v, axis=-1, keepdims=True)
    inverse = lax.rsqrt(jnp.mean(center * center, axis=-1, keepdims=True) + 1e-06)
    return center * inverse, inverse


def block_fwd_kernel(tiles, o_ref, x_ref, g_ref, mod_ref, wo_ref, ao_ref, bo_ref, a1_ref, b1_ref, w1_ref, a2_ref, w2_ref, b2_ref,
                     a_out, x1_out, h2_out, u_out, y_out, to_out, t1_out, t2_out, gate_out, m_acc, t2_acc):
    step = pl.program_id(0)
    rows = o_ref.shape[0]
    width = o_ref.shape[1]

    @pl.when(step == 0)
    def _():
        to = mm_t(o_ref[...], ao_ref[...]).astype(jnp.bfloat16)
        to_out[...] = to

        def cols(n, _):
            sl = pl.ds(pl.multiple_of(n * 256, 256), 256)
            a_out[:, sl] = mm_t(o_ref[...], wo_ref[sl, :]) + mm(to_out[...], bo_ref[:, sl])
            return 0

        lax.fori_loop(0, width // 256, cols, 0)

        def norm(r, _):
            sl = pl.ds(pl.multiple_of(r * ROWS, ROWS), ROWS)
            x1 = x_ref[sl, :].astype(jnp.float32) + mod_ref[2:3, :] * a_out[sl, :]
            x1_out[sl, :] = x1
            xh, _inv = norm_rows(x1)
            h2_out[sl, :] = (xh * (1.0 + mod_ref[4:5, :]) + mod_ref[3:4, :]).astype(jnp.bfloat16)
            return 0

        lax.fori_loop(0, rows // ROWS, norm, 0)
        t1_out[...] = mm_t(h2_out[...], a1_ref[...]).astype(jnp.bfloat16)
        m_acc[...] = jnp.zeros_like(m_acc)
        t2_acc[...] = jnp.zeros_like(t2_acc)

    u = mm(h2_out[...], w1_ref[...]) + mm(t1_out[...], b1_ref[...])
    u_out[...] = u
    f = gelu_parts(u)[0].astype(jnp.bfloat16)
    m_acc[...] += mm_t(f, w2_ref[...])
    t2_acc[...] += mm_t(f, a2_ref[...])

    @pl.when(step == tiles - 1)
    def _():
        t2_out[...] = t2_acc[...].astype(jnp.bfloat16)
        gate_out[...] = jnp.zeros_like(gate_out)

        def last(r, _):
            sl = pl.ds(pl.multiple_of(r * ROWS, ROWS), ROWS)
            m = m_acc[sl, :] + mm(t2_out[sl, :], b2_ref[...])
            y_out[sl, :] = (x1_out[sl, :] + mod_ref[5:6, :] * m).astype(jnp.bfloat16)
            gm = g_ref[sl, :].astype(jnp.float32) * m
            gate_out[...] += sum(gm[8 * i:8 * i + 8, :] for i in range(ROWS // 8))
            return 0

        lax.fori_loop(0, rows // ROWS, last, 0)


def block_fwd(o, x, g, mod, wo, pair_o, pair_1, w1, pair_2, w2, tn=512):
    rows, width = o.shape
    hidden = w1.shape[1]
    tiles = hidden // tn
    rank = pair_o[0].shape[0]
    whole = lambda shape: pl.BlockSpec(shape, lambda n: (0,) * len(shape))
    once = lambda shape: pl.BlockSpec(shape, lambda n: (0,) * len(shape), pipeline_mode=pl.Buffered(1))
    tile = lambda height: pl.BlockSpec((height, tn), lambda n: (0, n))
    f32, bf16 = jnp.float32, jnp.bfloat16
    act = (rows, width)
    return pl.pallas_call(
        functools.partial(block_fwd_kernel, tiles),
        grid=(tiles,),
        in_specs=[once(act), once(act), once(act), once(mod.shape), once((width, width)), once((rank, width)), once((rank, width)),
                  once((rank, width)), tile(rank), tile(width), tile(rank), tile(width), once((rank, width))],
        out_specs=[whole(act), whole(act), whole(act), tile(rows), whole(act), whole((rows, rank)), whole((rows, rank)),
                   whole((rows, rank)), whole((8, width))],
        out_shape=[jax.ShapeDtypeStruct(act, f32), jax.ShapeDtypeStruct(act, f32), jax.ShapeDtypeStruct(act, bf16),
                   jax.ShapeDtypeStruct((rows, hidden), f32), jax.ShapeDtypeStruct(act, bf16)]
        + [jax.ShapeDtypeStruct((rows, rank), bf16)] * 3 + [jax.ShapeDtypeStruct((8, width), f32)],
        scratch_shapes=[pltpu.VMEM(act, f32), pltpu.VMEM((rows, rank), f32)],
        compiler_params=pltpu.CompilerParams(vmem_limit_bytes=58 * 1024 * 1024),
        cost_estimate=pl.CostEstimate(flops=2 * rows * width * (width + 2 * hidden), bytes_accessed=4 * width * hidden, transcendentals=0),
        name="block_forward",
    )(o, x, g, mod, wo, *pair_o, pair_1[0], pair_1[1], w1, pair_2[0], w2, pair_2[1])


def block_back_kernel(tiles, g_ref, x1_ref, a_ref, h2_ref, o_ref, mod_ref, u_ref, w2_ref, a2_ref, b2_ref, w1_ref, a1_ref, b1_ref,
                      wo_ref, ao_ref, bo_ref, to_ref, t1_ref, t2_ref,
                      dx1_out, do_out, sums_out, ga2_out, gb1_out, ga1_out, gb2_out, gao_out, gbo_out,
                      dm_ref, dt2_ref, dh_acc, dt1_acc, da_ref):
    step = pl.program_id(0)
    rows, width = g_ref.shape
    bf16 = jnp.bfloat16

    @pl.when(step == 0)
    def _():
        def start(r, _):
            sl = pl.ds(pl.multiple_of(r * ROWS, ROWS), ROWS)
            dm_ref[sl, :] = (mod_ref[5:6, :] * g_ref[sl, :].astype(jnp.float32)).astype(bf16)
            return 0

        lax.fori_loop(0, rows // ROWS, start, 0)
        dt2_ref[...] = mm_t(dm_ref[...], b2_ref[...]).astype(bf16)
        gb2_out[...] = t_mm(t2_ref[...], dm_ref[...])
        dh_acc[...] = jnp.zeros_like(dh_acc)
        dt1_acc[...] = jnp.zeros_like(dt1_acc)

    act, slope = gelu_parts(u_ref[...])
    df = mm(dm_ref[...], w2_ref[...]) + mm(dt2_ref[...], a2_ref[...])
    ga2_out[...] = t_mm(dt2_ref[...], act.astype(bf16))
    du = (df * slope).astype(bf16)
    gb1_out[...] = t_mm(t1_ref[...], du)
    dh_acc[...] += mm_t(du, w1_ref[...])
    dt1_acc[...] += mm_t(du, b1_ref[...])

    @pl.when(step == tiles - 1)
    def _():
        dt1 = dt1_acc[...].astype(bf16)
        dt2_ref[...] = dt1
        ga1_out[...] = t_mm(dt1, h2_ref[...])
        sums_out[...] = jnp.zeros_like(sums_out)

        def last(r, _):
            sl = pl.ds(pl.multiple_of(r * ROWS, ROWS), ROWS)
            dh = dh_acc[sl, :] + mm(dt2_ref[sl, :], a1_ref[...])
            xh, inverse = norm_rows(x1_ref[sl, :])
            dz = dh * (1.0 + mod_ref[4:5, :])
            dx1 = g_ref[sl, :].astype(jnp.float32) + inverse * (
                dz - jnp.mean(dz, axis=-1, keepdims=True) - xh * jnp.mean(dz * xh, axis=-1, keepdims=True))
            dx1_out[sl, :] = dx1
            da_ref[sl, :] = (mod_ref[2:3, :] * dx1).astype(bf16)
            fold = lambda v: sum(v[8 * i:8 * i + 8, :] for i in range(ROWS // 8))
            sums_out[0:8, :] += fold(dx1 * a_ref[sl, :])
            sums_out[8:16, :] += fold(dh)
            sums_out[16:24, :] += fold(dh * xh)
            return 0

        lax.fori_loop(0, rows // ROWS, last, 0)
        dto = mm_t(da_ref[...], bo_ref[...]).astype(bf16)
        dt2_ref[...] = dto
        gao_out[...] = t_mm(dto, o_ref[...])
        gbo_out[...] = t_mm(to_ref[...], da_ref[...])

        def cols(n, _):
            sl = pl.ds(pl.multiple_of(n * 256, 256), 256)
            do_out[:, sl] = (mm(da_ref[...], wo_ref[:, sl]) + mm(dt2_ref[...], ao_ref[:, sl])).astype(bf16)
            return 0

        lax.fori_loop(0, width // 256, cols, 0)


def block_back(g, x1, a, h2, o, mod, u, w2, pair_2, w1, pair_1, wo, pair_o, mids, tn=512):
    rows, width = o.shape
    hidden = w1.shape[1]
    tiles = hidden // tn
    rank = pair_o[0].shape[0]
    whole = lambda shape: pl.BlockSpec(shape, lambda n: (0,) * len(shape))
    once = lambda shape: pl.BlockSpec(shape, lambda n: (0,) * len(shape), pipeline_mode=pl.Buffered(1))
    tile = lambda height: pl.BlockSpec((height, tn), lambda n: (0, n))
    f32, bf16 = jnp.float32, jnp.bfloat16
    act = (rows, width)
    side = (rank, width)
    thin = (rows, rank)
    return pl.pallas_call(
        functools.partial(block_back_kernel, tiles),
        grid=(tiles,),
        in_specs=[once(act)] * 5 + [once(mod.shape), tile(rows), tile(width), tile(rank), once(side), tile(width), once(side), tile(rank),
                  once((width, width)), once(side), once(side)] + [once(thin)] * 3,
        out_specs=[whole(act), whole(act), whole((24, width)), tile(rank), tile(rank)] + [whole(side)] * 4,
        out_shape=[jax.ShapeDtypeStruct(act, f32), jax.ShapeDtypeStruct(act, bf16), jax.ShapeDtypeStruct((24, width), f32)]
        + [jax.ShapeDtypeStruct((rank, hidden), f32)] * 2 + [jax.ShapeDtypeStruct(side, f32)] * 4,
        scratch_shapes=[pltpu.VMEM(act, bf16), pltpu.VMEM(thin, bf16), pltpu.VMEM(act, f32), pltpu.VMEM(thin, f32), pltpu.VMEM(act, bf16)],
        compiler_params=pltpu.CompilerParams(vmem_limit_bytes=58 * 1024 * 1024),
        cost_estimate=pl.CostEstimate(flops=2 * rows * width * (width + 2 * hidden), bytes_accessed=4 * width * hidden, transcendentals=0),
        name="block_backward",
    )(g, x1, a, h2, o, mod, u, w2, pair_2[0], pair_2[1], w1, pair_1[0], pair_1[1], wo, *pair_o, *mids)


def column_peers(n_z):
    f, z = lax.axis_index("fsdp"), lax.axis_index("tp")
    core = f % 2
    base = f - core
    peers = [(f, (z + j) % n_z) for j in range(1, n_z)]
    peers += [(base + 1 - core, (z + j) % n_z) for j in range(n_z)]
    return f, z, core, base, peers


def meet(peers):
    barrier = pltpu.get_barrier_semaphore()
    for peer in peers:
        pl.semaphore_signal(barrier, inc=1, device_id=peer, device_id_type=MESH)
    pl.semaphore_wait(barrier, len(peers))


def push(src, dst, send, recv, peer):
    return pltpu.make_async_remote_copy(
        src_ref=src, dst_ref=dst, send_sem=send, recv_sem=recv, device_id=peer, device_id_type=MESH)


class ZRing:
    def __init__(self, f, z, n_z):
        self.f, self.z, self.n_z = f, z, n_z

    def start(self, source_of, buf, send, recv):
        for j in range(1, self.n_z):
            to = (self.z + j) % self.n_z
            push(source_of(to), buf.at[self.z], send.at[j], recv.at[self.z], (self.f, to)).start()

    def wait(self, buf, send, recv):
        for j in range(1, self.n_z):
            came = (self.z + j) % self.n_z
            push(buf.at[came], buf.at[came], send.at[j], recv.at[came], (self.f, came)).wait_recv()

    def drain(self, source_of, buf, send, recv):
        for j in range(1, self.n_z):
            to = (self.z + j) % self.n_z
            push(source_of(to), buf.at[self.z], send.at[j], recv.at[self.z], (self.f, to)).wait_send()


def text_mid_kernel(n_z, o_ref, x_ref, g_ref, mod_ref, owner_ref, own_ref, mask_ref, lmask_ref, wo_ref, w1_ref, w2_ref,
                    ao_ref, bo_ref, a1_ref, b1_ref, a2_ref, b2_ref,
                    y_out, dx1_out, do_out, sums_out, gao_out, gbo_out, ga1_out, gb1_out, ga2_out, gb2_out,
                    o_got, part_ref, out_buf, in_buf, ag_ref, da_ref, dm_ref, u_ref, f_ref, att_ref, do_buf, x1_ref, br_ref, t_ref,
                    o_send, o_recv, rs_send, rs_recv, ag_send, ag_recv, dm_send, dm_recv, do_send, do_recv):
    f, z, core, base, peers = column_peers(n_z)
    ring = ZRing(f, z, n_z)
    bf16, f32 = jnp.bfloat16, jnp.float32
    pad, width = x_ref.shape
    rank = ao_ref.shape[0]
    share = ao_ref.shape[1]
    meet(peers)

    def modulation(row):
        return jnp.where(own_ref[...] > 0, mod_ref[row:row + 1, :], mod_ref[8 + row:9 + row, :])

    home = [(base + z // 2, 2 * core + i) for i in range(2)]
    for i in range(2):
        here = (z // 2 == core) & (2 * core + i == z)

        @pl.when(here)
        def _():
            copy = pltpu.make_async_copy(o_ref.at[i], o_got.at[z % 2], o_recv.at[z % 2])
            copy.start()
            copy.wait()

        @pl.when(jnp.logical_not(here))
        def _():
            push(o_ref.at[i], o_got.at[z % 2], o_send.at[i], o_recv.at[z % 2], home[i]).start()

    dm_ref[z, :, :] = (modulation(5) * g_ref[...].astype(f32)).astype(bf16)
    ring.start(lambda to: dm_ref.at[z], dm_ref, dm_send, dm_recv)

    for s in range(2):
        here = (z // 2 == core) & (2 * core + s == z)

        @pl.when(jnp.logical_not(here))
        def _():
            push(o_got.at[s], o_got.at[s], o_send.at[s], o_recv.at[s], home[s]).wait_recv()

    owner = owner_ref[...]
    att_ref[...] = jnp.where(
        owner > 0, o_got[0].astype(f32), jnp.where(owner < 0, o_got[1].astype(f32), 0.0)).astype(bf16)

    def scatter(turn, main, rank_part):
        full = jnp.concatenate([main, rank_part], axis=1)
        full = full.reshape(n_z, pad, full.shape[1])
        part_ref[...] = full
        out_buf[...] = full.astype(bf16)
        ring.start(lambda to: out_buf.at[to], in_buf.at[turn], rs_send.at[turn], rs_recv.at[turn])

    def collect(turn):
        ring.wait(in_buf.at[turn], rs_send.at[turn], rs_recv.at[turn])
        total = part_ref[z]
        for j in range(1, n_z):
            total = total + in_buf[turn, (z + j) % n_z].astype(f32)
        ring.drain(lambda to: out_buf.at[to], in_buf.at[turn], rs_send.at[turn], rs_recv.at[turn])
        return total[:, :width], (total[:, width:] * lmask_ref[...]).astype(bf16)

    def spread(turn, ref, *parts):
        offset = 0
        for part in parts:
            ref[z, :, offset:offset + part.shape[1]] = part
            offset += part.shape[1]
        ring.start(lambda to: ref.at[z], ref, ag_send.at[turn], ag_recv.at[turn])

    def spread_end(turn, ref):
        ring.wait(ref, ag_send.at[turn], ag_recv.at[turn])
        ring.drain(lambda to: ref.at[z], ref, ag_send.at[turn], ag_recv.at[turn])

    def gathered(ref, start, count):
        return ref[:, :, start:start + count].reshape(n_z * pad, count)

    def own_lanes(ref):
        at = pl.ds(pl.multiple_of(z * share, 128), share)
        return ref[:, :, at].reshape(n_z * pad, share)

    mask = mask_ref[...]
    att = att_ref[...]
    scatter(0, mm_t(att, wo_ref[...]), mm_t(att, ao_ref[...]))
    branch, to_mine = collect(0)
    branch = branch + mm(to_mine, bo_ref[...])
    br_ref[...] = branch
    x1 = x_ref[...].astype(f32) + modulation(2) * branch
    x1_ref[...] = x1
    xh, _inv = norm_rows(x1)
    h2 = (xh * (1.0 + modulation(4)) + modulation(3)).astype(bf16)
    spread(0, ag_ref, h2, to_mine)
    spread_end(0, ag_ref)
    h2_all = gathered(ag_ref, 0, width)
    to_all = gathered(ag_ref, width, rank)
    t1 = (mm_t(h2_all, a1_ref[...]) * mask).astype(bf16)
    u = mm(h2_all, w1_ref[...]) + mm(t1, b1_ref[...])
    u_ref[...] = u
    act = gelu_parts(u)[0].astype(bf16)
    f_ref[...] = act
    scatter(1, mm_t(act, w2_ref[...]), mm_t(act, a2_ref[...]))
    t_ref[0] = to_all
    t_ref[1] = t1
    feed, t2_mine = collect(1)
    feed = feed + mm(t2_mine, b2_ref[...])
    y_out[...] = (x1_ref[...] + modulation(5) * feed).astype(bf16)

    def collapse(place, values):
        for s in range(2):
            sums_out[2 * place + s:2 * place + s + 1, :] = jnp.sum(
                jnp.where(own_ref[...] == (1.0 if s == 0 else -1.0), values, 0.0), axis=0, keepdims=True)

    collapse(3, g_ref[...].astype(f32) * feed)

    ring.wait(dm_ref, dm_send, dm_recv)
    ring.drain(lambda to: dm_ref.at[z], dm_ref, dm_send, dm_recv)
    dm_all = dm_ref[...].reshape(n_z * pad, width)
    dt2 = (mm_t(dm_all, b2_ref[...]) * mask).astype(bf16)
    df = mm(dm_all, w2_ref[...]) + mm(dt2, a2_ref[...])
    ga2_out[...] = t_mm(dt2, f_ref[...])
    du = (df * gelu_parts(u_ref[...])[1]).astype(bf16)
    scatter(2, mm_t(du, w1_ref[...]), mm_t(du, b1_ref[...]))
    gb1_out[...] = t_mm(t_ref[1], du)
    dh, dt1_mine = collect(2)
    dh = dh + mm(dt1_mine, a1_ref[...])
    xh, inverse = norm_rows(x1_ref[...])
    dz = dh * (1.0 + modulation(4))
    dx1 = g_ref[...].astype(f32) + inverse * (
        dz - jnp.mean(dz, axis=-1, keepdims=True) - xh * jnp.mean(dz * xh, axis=-1, keepdims=True))
    spread(1, da_ref, (modulation(2) * dx1).astype(bf16), dt1_mine, t2_mine)
    dx1_out[...] = dx1
    collapse(0, dx1 * br_ref[...])
    collapse(1, dh)
    collapse(2, dh * xh)
    spread_end(1, da_ref)
    da_all = gathered(da_ref, 0, width)
    dt1 = gathered(da_ref, width, rank)
    t2 = gathered(da_ref, width + rank, rank)
    dto = (mm_t(da_all, bo_ref[...]) * mask).astype(bf16)
    do_buf[...] = (mm(da_all, wo_ref[...]) + mm(dto, ao_ref[...])).astype(bf16)
    for s in range(2):
        here = (z // 2 == core) & (2 * core + s == z)

        @pl.when(here)
        def _():
            copy = pltpu.make_async_copy(do_buf, do_out.at[z % 2], do_recv.at[z % 2])
            copy.start()
            copy.wait()

        @pl.when(jnp.logical_not(here))
        def _():
            push(do_buf, do_out.at[z % 2], do_send.at[s], do_recv.at[z % 2], (base + z // 2, 2 * core + s)).start()

    gao_out[...] = t_mm(dto, att_ref[...])
    gbo_out[...] = t_mm(t_ref[0], own_lanes(da_ref))
    gb2_out[...] = t_mm(t2, own_lanes(dm_ref))
    ga1_out[...] = t_mm(dt1, own_lanes(ag_ref))
    for i in range(2):
        here = (z // 2 == core) & (2 * core + i == z)

        @pl.when(jnp.logical_not(here))
        def _():
            push(do_out.at[i], do_out.at[i], do_send.at[i], do_recv.at[i], home[i]).wait_recv()
            push(do_buf, do_out.at[i], do_send.at[i], do_recv.at[i], home[i]).wait_send()
            push(o_ref.at[i], o_got.at[z % 2], o_send.at[i], o_recv.at[z % 2], home[i]).wait_send()


def text_mid(o, x, g, mod, owner, own, mask, lmask, wo, w1, w2, pair_o, pair_1, pair_2, n_z, cid):
    pad, width = x.shape
    rank, share = pair_o[0].shape
    total = n_z * pad
    hidden = w1.shape[1]
    wide = width + rank
    f32, bf16 = jnp.float32, jnp.bfloat16
    shape = jax.ShapeDtypeStruct
    vmem = pltpu.VMEM
    dma = pltpu.SemaphoreType.DMA
    args = (o, x, g, mod, owner, own, mask, lmask, wo, w1, w2, *pair_o, *pair_1, *pair_2)
    out_shape = [
        shape((pad, width), bf16), shape((pad, width), f32), shape((2, total, share), bf16), shape((8, width), f32),
        shape((rank, share), f32), shape((rank, share), f32), shape((rank, share), f32), shape((rank, hidden), f32),
        shape((rank, hidden), f32), shape((rank, share), f32),
    ]
    return pl.pallas_call(
        functools.partial(text_mid_kernel, n_z),
        out_shape=out_shape,
        in_specs=[pl.BlockSpec(memory_space=vmem)] * len(args),
        out_specs=[pl.BlockSpec(memory_space=vmem)] * len(out_shape),
        scratch_shapes=[
            vmem((2, total, share), bf16), vmem((n_z, pad, wide), f32), vmem((n_z, pad, wide), bf16),
            vmem((3, n_z, pad, wide), bf16), vmem((n_z, pad, wide), bf16), vmem((n_z, pad, wide + rank), bf16),
            vmem((n_z, pad, width), bf16),
            vmem((total, hidden), f32), vmem((total, hidden), bf16), vmem((total, share), bf16),
            vmem((total, share), bf16), vmem((pad, width), f32), vmem((pad, width), f32), vmem((2, total, rank), bf16),
            dma((2,)), dma((2,)), dma((3, n_z)), dma((3, n_z)), dma((2, n_z)), dma((2, n_z)), dma((n_z,)), dma((n_z,)),
            dma((2,)), dma((2,)),
        ],
        compiler_params=pltpu.CompilerParams(collective_id=cid, has_side_effects=True, vmem_limit_bytes=50 * 1024 * 1024),
        name="text_block",
    )(*args)


def flip_bits(chip, mask, nbits):
    other = 0
    for bit in range(nbits):
        have = (chip // (1 << bit)) % 2
        other = other + (1 - have if (mask >> bit) & 1 else have) * (1 << bit)
    return other


def tail_kernel(n_f, n_z, fans, cols, *refs):
    it = iter(refs)
    take = lambda count: [next(it) for _ in range(count)]
    grad_ref, = take(1)
    img_a, img_b, txt_a, txt_b = take(4), take(4), take(4), take(4)
    hot4_ref, hot2_ref, dmod_ref, wmod_ref, bmod_ref, tmod_ref, cond_ref, smask_ref = take(8)
    grad_out, cond_out, rank_out, shard_out = take(4)
    zmsg, zgot, dense, snd1, rcv1, snd2, rcv2, dgot, own_dm, all_dm, cpart, cgot, zsum, zall, dts = take(15)
    (g_send, g_recv, z_send, z_recv, c_send, c_recv, s_send, s_recv, d_send, d_recv, f_send, f_recv, p_send, p_recv,
     q_send, q_recv, t_send, t_recv) = take(18)
    f32, bf16 = jnp.float32, jnp.bfloat16
    f, z, core, base, column = column_peers(n_z)
    chip = f // 2
    chips = n_f // 2
    nbits = bits_of(chips)
    partner = base + 1 - core
    around = [((f + j) % n_f, z) for j in range(1, n_f)]
    others = [(flip_bits(chip, mask, nbits) * 2 + side, z) for mask in range(1, chips) for side in range(2)]
    meet(column + others)
    ring = ZRing(f, z, n_z)
    blk = shard_out.shape[0]
    hidden_rank = hot2_ref.shape[0]

    def dmod_copy(index, peer):
        return push(dmod_ref.at[peer[1]], dgot.at[core * n_z + z], d_send.at[index], d_recv.at[core * n_z + z], peer)

    for index, peer in enumerate(column):
        dmod_copy(index, peer).start()
    dgot[core * n_z + z] = dmod_ref[z]

    offset = 0
    spans = []
    for part, sizes in ((img_a, fans), (img_b, cols)):
        for index in range(4):
            count = sizes[index + 1] // n_z
            for t in range(n_z):
                zmsg[t, :, offset:offset + count] = part[index][:, t * count:(t + 1) * count].astype(bf16)
            spans.append((offset, count))
            offset += count
    ring.start(lambda to: zmsg.at[to], zgot, z_send, z_recv)
    zgot[z] = zmsg[z]

    for index, peer in enumerate(column):
        place = peer[0] % 2 * n_z + peer[1]
        push(dgot.at[place], dgot.at[place], d_send.at[index], d_recv.at[place], peer).wait_recv()
    rows = []
    for slot in range(2):
        rows.append(dgot[2 * core + slot, 0] + dgot[n_z + 2 * core + slot, 0])
    for slot in range(2):
        total = dgot[core * n_z, 1 + slot]
        for t in range(1, n_z):
            total = total + dgot[core * n_z + t, 1 + slot]
        rows.append(total)
    chunk = dmod_ref.shape[-1]
    own_dm[...] = jnp.zeros_like(own_dm)
    for r, total in enumerate(rows):
        for j in range(own_dm.shape[1] // chunk):
            own_dm[r:r + 1, j * chunk:(j + 1) * chunk] = total[j:j + 1, :].astype(bf16).astype(f32)
    for j in range(1, n_f):
        push(own_dm, all_dm.at[f], f_send.at[j], f_recv.at[f], around[j - 1]).start()
    all_dm[f] = own_dm[...]
    dm_low = own_dm[...].astype(bf16)
    tmod = [tmod_ref[s].astype(bf16) for s in range(2)]
    gb_mod = [t_mm(tmod[s], dm_low) for s in range(2)]
    rank_img = mm_t(dm_low, bmod_ref[0])
    rank_txt = mm_t(dm_low, bmod_ref[1])
    row = lax.broadcasted_iota(jnp.int32, rank_img.shape, 0)
    rank_part = jnp.where(row < 2, rank_img, rank_txt)

    hot2 = hot2_ref[...]
    starts = []
    offset = 0
    for stream in range(2):
        for index in range(5):
            starts.append((stream, index, offset, offset + fans[index] // n_z))
            offset += fans[index] // n_z + cols[index] // n_z

    def put_a(at, part, hot):
        dense[at:at + part.shape[1], :] = dots(part, hot, 0, 0)

    def put_b(at, part, hot):
        full = dots(hot, part, 0, 0)
        blocks = part.shape[1] // 128
        for j in range(blocks):
            dense[pl.ds(at + j, 128, stride=blocks), :] = full[:, j * 128:(j + 1) * 128]

    for stream, index, at_a, at_b in starts:
        if index == 0:
            dense[at_a:at_b, :] = jnp.zeros((at_b - at_a, 128), f32)
            put_b(at_b, gb_mod[stream].astype(bf16), hot2)
        elif stream == 1:
            put_a(at_a, txt_a[index - 1][...].astype(bf16), hot2)
            put_b(at_b, txt_b[index - 1][...].astype(bf16), hot2)

    ring.wait(zgot, z_send, z_recv)
    hot4 = hot4_ref[...]
    for stream, index, at_a, at_b in starts:
        if stream == 0 and index > 0:
            for at, put, (begin, count) in ((at_a, put_a, spans[index - 1]), (at_b, put_b, spans[index + 3])):
                part = zgot[:, :, begin:begin + count].reshape(hot4.shape[0], count)
                put(at, part, hot4)

    home = [(base + z // 2, 2 * core + i) for i in range(2)]

    def is_here(i):
        return (z // 2 == core) & (2 * core + i == z)

    for i in range(2):
        @pl.when(is_here(i))
        def _():
            pltpu.make_async_copy(grad_ref.at[i], grad_out.at[z % 2], g_recv.at[z % 2]).start()

        @pl.when(jnp.logical_not(is_here(i)))
        def _():
            push(grad_ref.at[i], grad_out.at[z % 2], g_send.at[i], g_recv.at[z % 2], home[i]).start()

    def block(number):
        return pl.ds(pl.multiple_of(number * blk, 16), blk)

    for p in range(chips):
        snd1[p] = dense[block(2 * p + 1 - core), :].astype(bf16)
        push(snd1.at[p], rcv1.at[p], c_send.at[p], c_recv.at[p], (partner, z)).start()

    for j in range(1, n_f):
        came = (f - j + n_f) % n_f
        push(own_dm, all_dm.at[came], f_send.at[j], f_recv.at[came], (came, z)).wait_recv()
    everyone = all_dm[...].reshape(n_f * 8, own_dm.shape[1]).astype(bf16)
    part = mm_t(everyone, wmod_ref[0]) + pltpu.roll(mm_t(everyone, wmod_ref[1]), n_f * 8 - 2, 0)
    k_local = part.shape[1]
    cpart[...] = jnp.zeros_like(cpart)
    cpart[:, :, :k_local] = part.reshape(n_f, 8, k_local)
    for j in range(1, n_f):
        to = (f + j) % n_f
        push(cpart.at[to], cgot.at[f], p_send.at[j], p_recv.at[f], (to, z)).start()
    cgot[f] = cpart[f]

    for p in range(chips):
        push(snd1.at[p], rcv1.at[p], c_send.at[p], c_recv.at[p], (partner, z)).wait_recv()

    def mine_of(p):
        return block(2 * p + core)

    for p in range(chips):
        dense[mine_of(p), :] += rcv1[p].astype(f32)

    half = blk // 2
    orders = [list(range(nbits)), list(range(nbits))[::-1]]

    def masks_at(side, turn):
        left = orders[side][turn:]
        return [sum(1 << b for i, b in enumerate(left) if (m >> i) & 1) for m in range(1 << len(left))]

    def rs_copy(side, turn, index):
        slot = turn * 2 + index
        peer = flip_bits(chip, 1 << orders[side][turn], nbits) * 2 + core
        return push(snd2.at[side, slot], rcv2.at[side, slot], s_send.at[side, slot], s_recv.at[side, slot], (peer, z))

    def half_of(number, side):
        return pl.ds(pl.multiple_of((2 * number + core) * blk + side * half, 16), half)

    def rs_start(turn):
        for side in range(2):
            bit = 1 << orders[side][turn]
            for index, mask in enumerate(masks_at(side, turn + 1)):
                number = flip_bits(chip, bit | mask, nbits)
                snd2[side, turn * 2 + index] = dense[half_of(number, side), :].astype(bf16)
                rs_copy(side, turn, index).start()

    def rs_end(turn):
        for side in range(2):
            for index, mask in enumerate(masks_at(side, turn + 1)):
                number = flip_bits(chip, mask, nbits)
                rs_copy(side, turn, index).wait_recv()
                dense[half_of(number, side), :] += rcv2[side, turn * 2 + index].astype(f32)

    rs_start(0)

    for j in range(1, n_f):
        came = (f - j + n_f) % n_f
        push(cpart.at[came], cgot.at[came], p_send.at[j], p_recv.at[came], (came, z)).wait_recv()
    zsum[:n_f] = cgot[...]
    zsum[n_f] = jnp.zeros(zsum.shape[1:], f32)
    zsum[n_f, :, :hidden_rank] = rank_part
    zall[z] = zsum[...]
    ring.start(lambda to: zsum, zall, q_send, q_recv)
    ring.wait(zall, q_send, q_recv)
    total = zall[0]
    for t in range(1, n_z):
        total = total + zall[t]
    cond_out[...] = total[:n_f]
    dt = (total[n_f][:, :hidden_rank] * smask_ref[...]).astype(bf16)
    rank_out[...] = dt.astype(f32)
    wide = mm(dt, hot2)
    dts[f] = wide
    for j in range(1, n_f):
        push(dts.at[f], dts.at[f], t_send.at[j], t_recv.at[f], around[j - 1]).start()

    rs_end(0)
    if nbits > 1:
        rs_start(1)
    for j in range(1, n_f):
        came = (f - j + n_f) % n_f
        push(dts.at[came], dts.at[came], t_send.at[j], t_recv.at[came], (came, z)).wait_recv()
    all_dt = dts[...].reshape(n_f * 8, 128)
    row = lax.broadcasted_iota(jnp.int32, all_dt.shape, 0) % 8
    act = cond_ref[...].reshape(n_f * 8, cond_ref.shape[-1]).astype(bf16)
    mod_a = [
        dots(act, jnp.where(row < 2, all_dt, 0.0).astype(bf16), 0, 0),
        dots(act, pltpu.roll(jnp.where((row >= 2) & (row < 4), all_dt, 0.0), n_f * 8 - 2, 0).astype(bf16), 0, 0),
    ]
    if nbits > 1:
        rs_end(1)
    shard_out[...] = dense[block(f), :]
    for stream in range(2):
        first = starts[5 * stream][2]
        own = jnp.where(f == first // blk, 1.0, 0.0)
        count = mod_a[stream].shape[0]
        shard_out[:count, :] += own * mod_a[stream]

    ring.drain(lambda to: zmsg.at[to], zgot, z_send, z_recv)
    ring.drain(lambda to: zsum, zall, q_send, q_recv)
    for index, peer in enumerate(column):
        dmod_copy(index, peer).wait_send()
    for j in range(1, n_f):
        to = (f + j) % n_f
        push(own_dm, all_dm.at[f], f_send.at[j], f_recv.at[f], (to, z)).wait_send()
        push(cpart.at[to], cgot.at[f], p_send.at[j], p_recv.at[f], (to, z)).wait_send()
        push(dts.at[f], dts.at[f], t_send.at[j], t_recv.at[f], (to, z)).wait_send()
    for p in range(chips):
        push(snd1.at[p], rcv1.at[p], c_send.at[p], c_recv.at[p], (partner, z)).wait_send()
    for turn in range(nbits):
        for side in range(2):
            for index in range(len(masks_at(side, turn + 1))):
                rs_copy(side, turn, index).wait_send()
    for i in range(2):
        @pl.when(is_here(i))
        def _():
            pltpu.make_async_copy(grad_ref.at[i], grad_out.at[z % 2], g_recv.at[z % 2]).wait()

        @pl.when(jnp.logical_not(is_here(i)))
        def _():
            push(grad_out.at[i], grad_out.at[i], g_send.at[i], g_recv.at[i], home[i]).wait_recv()
            push(grad_ref.at[i], grad_out.at[z % 2], g_send.at[i], g_recv.at[z % 2], home[i]).wait_send()


def tail(grad, img_a, img_b, txt_a, txt_b, hot4, hot2, dmod, wmod, bmod, tmod, cond, smask, n_f, n_z, fans, cols, cid):
    f32, bf16 = jnp.float32, jnp.bfloat16
    vmem, dma = pltpu.VMEM, pltpu.SemaphoreType.DMA
    shape = jax.ShapeDtypeStruct
    args = (grad, *img_a, *img_b, *txt_a, *txt_b, hot4, hot2, dmod, wmod, bmod, tmod, cond, smask)
    lanes = (sum(fans[1:]) + sum(cols[1:])) // n_z
    rows = 2 * (sum(fans) + sum(cols)) // n_z
    blk = rows // n_f
    chips = n_f // 2
    cut = cols[0] // n_z
    rank = hot2.shape[0]
    inside = pl.BlockSpec(memory_space=vmem)
    return pl.pallas_call(
        functools.partial(tail_kernel, n_f, n_z, tuple(fans), tuple(cols)),
        out_shape=[shape(grad.shape, bf16), shape((n_f, 8, 256), f32), shape((8, rank), f32), shape((blk, 128), f32)],
        in_specs=[pl.BlockSpec(memory_space=pl.ANY)] + [inside] * (len(args) - 1),
        out_specs=[pl.BlockSpec(memory_space=pl.ANY)] + [inside] * 3,
        scratch_shapes=[
            vmem((n_z, RANK, lanes), bf16), vmem((n_z, RANK, lanes), bf16), vmem((rows, 128), f32),
            vmem((chips, blk, 128), bf16), vmem((chips, blk, 128), bf16),
            vmem((2, 4, blk // 2, 128), bf16), vmem((2, 4, blk // 2, 128), bf16),
            vmem((2 * n_z,) + dmod.shape[1:], f32), vmem((8, cut), f32), vmem((n_f, 8, cut), f32),
            vmem((n_f, 8, 256), f32), vmem((n_f, 8, 256), f32), vmem((n_f + 1, 8, 256), f32),
            vmem((n_z, n_f + 1, 8, 256), f32), vmem((n_f, 8, 128), f32),
            dma((2,)), dma((2,)), dma((n_z,)), dma((n_z,)), dma((chips,)), dma((chips,)), dma((2, 4)), dma((2, 4)),
            dma((2 * n_z,)), dma((2 * n_z,)), dma((n_f,)), dma((n_f,)), dma((n_f,)), dma((n_f,)), dma((n_z,)), dma((n_z,)),
            dma((n_f,)), dma((n_f,)),
        ],
        compiler_params=pltpu.CompilerParams(collective_id=cid, has_side_effects=True, vmem_limit_bytes=56 * 1024 * 1024),
        name="gradient_exchange",
    )(*args)

HD = 64
FF = 6144
NAD = 8
RANK = 16
EPS = 1e-06
HIGH = lax.Precision.HIGHEST
F32 = jnp.float32
BF16 = jnp.bfloat16
BOTH = ("fsdp", "tp")


def matmul(left, right):
    return jnp.dot(left, right, preferred_element_type=F32)


def exact(left, right):
    return jnp.dot(left, right, precision=HIGH, preferred_element_type=F32)


def inner_left(left, right):
    return lax.dot_general(left, right, (((0,), (0,)), ((), ())), preferred_element_type=F32)


def inner_right(left, right):
    return lax.dot_general(
        left, right, (((left.ndim - 1,), (right.ndim - 1,)), ((), ())), preferred_element_type=F32
    )


def layer_norm(values):
    center = values - jnp.mean(values, axis=-1, keepdims=True)
    inverse = lax.rsqrt(jnp.mean(center * center, axis=-1, keepdims=True) + EPS)
    return (center * inverse, inverse)


def norm_back(grad_normed, normed, inverse, scale):
    grad_hat = grad_normed * (1.0 + scale)
    return inverse * (
        grad_hat
        - jnp.mean(grad_hat, axis=-1, keepdims=True)
        - normed * jnp.mean(grad_hat * normed, axis=-1, keepdims=True)
    )


def gelu(value):
    return jax.nn.gelu(value, approximate=True)


def gelu_back(value, grad):
    return jax.vjp(gelu, value)[1](grad)[0]


def shards(
    image_tokens,
    text_tokens,
    conditioning,
    text_lengths,
    adapter_index,
    adapters,
    mod_weight,
    qkv_weight,
    out_weight,
    fc1_weight,
    fc2_weight,
    image_cot,
    text_cot,
):
    n_f, n_z = lax.axis_size("fsdp"), lax.axis_size("tp")
    f, z = lax.axis_index("fsdp"), lax.axis_index("tp")
    core = f % 2
    slots, quarter, width = image_tokens.shape
    txt_local = text_tokens.shape[0]
    txt_group = txt_local * n_z
    img_half = 2 * quarter
    img_n = 2 * img_half
    cols = [6 * width, 3 * width, width, FF, width]
    fans = [width, width, width, width, FF]

    def round_pairs(r):
        pairs = []
        for fa in range(n_f):
            for t in range(n_z):
                there = (fa // 2 * 2 + t // 2) * n_z + 2 * (fa % 2) + (r ^ (t % 2))
                pairs.append((fa * n_z + t, there))
        return pairs

    low_bit = z % 2

    def pick(stack, bit):
        return lax.dynamic_index_in_dim(stack, bit, 0, keepdims=False)

    def flip(r):
        return low_bit if r == 0 else 1 - low_bit

    def to_chip(parts):
        got = [lax.ppermute(parts[r], BOTH, round_pairs(r)) for r in range(2)]
        return jnp.where(low_bit == 0, got[0], got[1]), jnp.where(low_bit == 0, got[1], got[0])

    def from_chip(pieces):
        got = []
        for r in range(2):
            mine = jnp.where(flip(r) == 0, pieces[0], pieces[1])
            got.append(lax.ppermute(mine, BOTH, [(b, a) for a, b in round_pairs(r)]))
        return jnp.where(low_bit == 0, got[0], got[1]), jnp.where(low_bit == 0, got[1], got[0])

    def reshard(values):
        return jnp.concatenate(to_chip([pick(values, flip(r)) for r in range(2)]), axis=0)

    def unshard(values):
        return jnp.stack(from_chip([values[:quarter], values[quarter:]]))

    def swap_core(values):
        return lax.ppermute(values, "fsdp", [(i, i ^ 1) for i in range(n_f)])

    def by_core(mine, other, axis):
        first = jnp.where(core == 0, mine, other)
        second = jnp.where(core == 0, other, mine)
        return jnp.concatenate([first, second], axis=axis)

    def z_swap(values, step):
        return lax.ppermute(values, "tp", [(i, i ^ step) for i in range(n_z)])

    def z_order(pieces):
        stack = jnp.stack(pieces)
        return [pick(stack, z ^ a) for a in range(n_z)]

    def z_gather(values):
        return z_order([values] + [z_swap(values, j) for j in range(1, n_z)])

    def z_exchange(blocks):
        return z_order([pick(blocks, z ^ j) if j == 0 else z_swap(pick(blocks, z ^ j), j) for j in range(n_z)])

    def z_scatter(values):
        count = values.shape[0] // n_z
        mine = lax.dynamic_slice_in_dim(values, z * count, count, 0)
        for j in range(1, n_z):
            part = lax.dynamic_slice_in_dim(values, (z ^ j) * count, count, 0)
            mine = mine + z_swap(part.astype(BF16), j).astype(F32)
        return mine

    def to_heads(values):
        half = values.shape[1] // 2
        low, high = values[:, :half], values[:, half:]
        mine = jnp.where(core == 0, low, high)
        return by_core(mine, swap_core(jnp.where(core == 0, high, low)), 0)

    def to_tokens(values):
        low, high = values[:img_half], values[img_half:]
        mine = jnp.where(core == 0, low, high)
        return by_core(mine, swap_core(jnp.where(core == 0, high, low)), 1)

    out_t = jnp.swapaxes(out_weight, 1, 2)
    fc2_t = jnp.swapaxes(fc2_weight, 1, 2)
    local = [qkv_weight, out_t, fc1_weight, fc2_t]
    adapter_rows = adapters.astype(BF16).reshape(-1, 128)
    got = gather([w[0] for w in local], [w[1] for w in local] + [adapter_rows], n_f, n_z)
    got = [g.reshape(-1, g.shape[-1]) for g in got]
    img_w, txt_w, row = got[:4], got[4:8], got[8]
    x_img = reshard(image_tokens)
    g_img = reshard(image_cot)
    txt_pad = (txt_local + 15) // 16 * 16

    def padded(values):
        return jnp.pad(values, ((0, txt_pad - txt_local), (0, 0)))

    x_txt_low, g_txt_low = padded(text_tokens), padded(text_cot)
    x_txt = x_txt_low.astype(F32)

    seg_ends = jnp.cumsum(text_lengths[0])
    slot_ids = jnp.arange(slots)

    def owner_of(position):
        segment = jnp.sum((position[:, None] >= seg_ends[None, :]).astype(jnp.int32), axis=1)
        return (segment[:, None] == slot_ids[None, :]).astype(F32)

    def real(owner):
        place = jnp.arange(owner.shape[0]) % txt_pad
        return jnp.where((place < txt_local)[:, None], owner, 0.0)

    def position(rows):
        return rows // txt_pad * txt_local + rows % txt_pad

    txt_rows = jnp.arange(n_z * txt_pad)
    owner_group = real(owner_of(position(txt_rows)))
    owner_local = real(owner_of(z * txt_local + jnp.arange(txt_pad)))
    txt_mask = jnp.repeat(owner_group, RANK, axis=1)
    txt_mask_local = jnp.repeat(owner_local, RANK, axis=1)
    rank_cols = slots * RANK
    seq_mask = jnp.repeat(jnp.eye(slots, dtype=F32), RANK, axis=1)

    def by_group(mine, other):
        return by_core(mine, other, 0)

    column_picks = by_group(adapter_index, swap_core(adapter_index))
    column_count = 2 * slots
    one_hot = (
        jnp.arange(NAD * RANK)[:, None]
        == (column_picks[:, None] * RANK + jnp.arange(RANK)[None, :]).reshape(1, -1)
    ).astype(F32)
    own_picks = adapter_index
    own_hot = lax.dynamic_slice_in_dim(one_hot, core * slots * RANK, slots * RANK, 1)

    a_rows = [[None] * 5 for stream in range(2)]
    b_rows = [[None] * 5 for stream in range(2)]
    offset = 0
    for stream in range(2):
        for index in range(5):
            count = fans[index] // n_z
            a_rows[stream][index] = row[offset : offset + count]
            offset += count
            count = cols[index] // n_z
            b_rows[stream][index] = row[offset : offset + count]
            offset += count

    def b_pick(stream, index, pick_index):
        part = b_rows[stream][index]
        count = part.shape[0] // NAD
        return lax.dynamic_slice_in_dim(part, pick_index * count, count, 0).reshape(RANK, -1)

    def a_pick(rows, hot):
        return inner_right(hot.T.astype(BF16), rows).astype(BF16)

    img_a = a_pick(jnp.concatenate(a_rows[0], axis=0), one_hot)
    fan_share = sum(fans) // n_z
    img_a = img_a.reshape(column_count, RANK, fan_share)
    img_b = [
        jnp.concatenate([b_pick(0, index, column_picks[s]) for index in range(1, 5)], axis=1)
        for s in range(column_count)
    ]
    img_msg = jnp.concatenate([img_a, jnp.stack(img_b)], axis=2)
    txt_a_rows = jnp.concatenate(
        [a_rows[0][0], a_rows[1][0], a_rows[1][1], a_rows[1][3]], axis=0
    )
    txt_a = a_pick(txt_a_rows, own_hot).reshape(slots, RANK, -1)
    txt_b_own = [
        [b_pick(stream, index, own_picks[s]) for s in range(slots)]
        for stream, index in [(0, 0), (1, 0), (1, 1), (1, 2), (1, 3), (1, 4)]
    ]
    txt_b_own = [jnp.concatenate(parts, axis=0) for parts in txt_b_own]
    txt_a_own = a_pick(jnp.concatenate([a_rows[1][2], a_rows[1][4]], axis=0), own_hot)
    txt_msg = jnp.concatenate(
        [txt_a.reshape(slots * RANK, -1), txt_b_own[3], txt_b_own[5]], axis=1
    )
    img_got = jnp.stack(z_exchange(img_msg))
    txt_got = jnp.stack(z_gather(txt_msg))

    def join(part):
        return jnp.swapaxes(part, 0, 1).reshape(part.shape[1], -1)

    img_pairs = []
    offset, b_offset = 0, fan_share
    for index in range(5):
        count = fans[index] // n_z
        a_full = join(img_got[:, :, offset : offset + count])
        offset += count
        if index == 0:
            img_pairs.append(None)
            continue
        count = cols[index] // n_z
        b_full = join(img_got[:, :, b_offset : b_offset + count])
        b_offset += count
        img_pairs.append((a_full, b_full))
    txt_full = []
    offset = 0
    for count in [width // n_z] * 6:
        txt_full.append(join(txt_got[:, :, offset : offset + count]))
        offset += count
    mod_a = [txt_full[0], txt_full[1]]
    mod_b = [txt_b_own[0], txt_b_own[1]]
    txt_pairs = [
        None,
        (txt_full[2], txt_b_own[2]),
        (txt_a_own[:, : width // n_z], txt_full[4]),
        (txt_full[3], txt_b_own[4]),
        (txt_a_own[:, width // n_z :], txt_full[5]),
    ]

    k_local = mod_weight.shape[1]
    cond_act = jax.nn.silu(conditioning).astype(BF16)
    cond_all = lax.all_gather(cond_act, "fsdp", axis=0, tiled=True)
    cond_slice = lax.dynamic_slice_in_dim(cond_all, f * k_local, k_local, 1)
    mod_part = jnp.stack([matmul(cond_slice, mod_weight[stream]) for stream in range(2)], axis=1)
    mod_part = lax.psum_scatter(mod_part, "fsdp", scatter_dimension=0, tiled=True)
    mod_mid = []
    mod_terms = []
    for stream in range(2):
        middle = (inner_right(cond_act, mod_a[stream]) * seq_mask).astype(BF16)
        mod_mid.append(middle)
        mod_terms.append(mod_part[:, stream] + matmul(middle, mod_b[stream]))
    mods = jnp.concatenate(z_gather(jnp.stack(mod_terms, axis=1)), axis=2)
    img_mods = by_group(mods[:, 0], swap_core(mods[:, 0]))
    img_mod = lax.dynamic_slice_in_dim(img_mods, z, 1, 0)
    txt_mods = mods[:, 1]

    def stretch(stream, index):
        if stream == 0:
            return img_mod[:, index * width : (index + 1) * width]
        return exact(owner_local, txt_mods[:, index * width : (index + 1) * width])

    def collapse(stream, values):
        if stream == 0:
            return jnp.sum(values, axis=0, keepdims=True)
        return exact(owner_local.T, values)

    def share(values):
        return jnp.concatenate(z_gather(values), axis=0)

    def give(values, rank_part):
        got = z_scatter(jnp.concatenate([values, rank_part], axis=1))
        return got[:, :width], (got[:, width:] * txt_mask_local).astype(BF16)

    def lanes(values):
        count = values.shape[1] // n_z
        return lax.dynamic_slice_in_dim(values, z * count, count, 1)

    inputs = [x_img.astype(F32), x_txt]
    norm_one = [layer_norm(values) for values in inputs]
    heads_in = [
        (norm_one[s][0] * (1.0 + stretch(s, 1)) + stretch(s, 0)).astype(BF16) for s in range(2)
    ]

    def project(values, weight, pair, mask, flipped):
        middle = inner_right(values, pair[0])
        if mask is not None:
            middle = middle * mask
        middle = middle.astype(BF16)
        main = inner_right(values, weight) if flipped else matmul(values, weight)
        return middle, main + matmul(middle, pair[1])

    txt_in = share(heads_in[1])
    txt_qkv_mid, txt_qkv = project(txt_in, txt_w[0], txt_pairs[1], txt_mask, False)
    img_qkv_mid, img_qkv = project(heads_in[0], img_w[0], img_pairs[1], None, False)
    txt_qkv, img_qkv = txt_qkv.astype(BF16), img_qkv.astype(BF16)
    img_heads = to_heads(img_qkv)
    txt_heads = jnp.stack(to_chip([txt_qkv, txt_qkv]))
    lengths = by_group(text_lengths[0:1], swap_core(text_lengths[0:1]))
    chip_lengths = jnp.cumsum(lax.dynamic_index_in_dim(lengths, z // slots, 0, keepdims=False))
    chip_slot = z % slots
    chip_segment = jnp.sum(
        (position(txt_rows)[:, None] >= chip_lengths[None, :]).astype(jnp.int32),
        axis=1,
        keepdims=True,
    )
    chip_owner = (chip_segment == chip_slot) & (txt_rows % txt_pad < txt_local)[:, None]
    bias = jnp.where(chip_owner, 0.0, -1e30).astype(F32)
    o_img, o_txt, lse = attend(img_heads, txt_heads, bias, HD)

    def txt_home(values):
        got = from_chip([values[0], values[1]])
        return jnp.where(owner_group[:, 0:1] > 0, got[0], jnp.where(owner_group[:, 1:2] > 0, got[1], 0))

    attended = to_tokens(o_img)
    thick = 128

    def thicker(part):
        return jnp.concatenate([part, jnp.zeros((thick - part.shape[0], part.shape[1]), part.dtype)], axis=0)

    def sign(owner):
        return owner[:, 0:1] - owner[:, 1:2]

    def lanes_pad(mask):
        return jnp.pad(mask, ((0, 0), (0, thick - mask.shape[1])))

    txt_mod = jnp.pad(txt_mods.reshape(slots, 6, width), ((0, 0), (0, 2), (0, 0))).reshape(-1, width)
    thick_pairs = [None] + [tuple(thicker(part) for part in txt_pairs[index]) for index in range(1, 5)]
    (txt_result, txt_grad_after, do_txt, txt_sums, *txt_sides) = text_mid(
        o_txt, x_txt_low, g_txt_low, txt_mod, sign(owner_group), sign(owner_local), lanes_pad(txt_mask),
        lanes_pad(txt_mask_local), txt_w[1], txt_w[2], txt_w[3], thick_pairs[2], thick_pairs[3], thick_pairs[4],
        n_z, 2,
    )
    txt_sides = [part[:rank_cols] for part in txt_sides]
    txt_sums = txt_sums.reshape(4, slots, width)

    img_rows_mod = jnp.concatenate([img_mod.reshape(6, width), jnp.zeros((2, width), F32)], axis=0)
    (img_branch, img_after, img_mlp, img_pre, img_result, *img_mids, img_gate) = block_fwd(
        attended, x_img, g_img, img_rows_mod, img_w[1], img_pairs[2], img_pairs[3], img_w[2],
        img_pairs[4], img_w[3],
    )
    image_out = unshard(img_result)

    grads = [[None] * 5 for stream in range(2)]

    def project_back(grad, weight, pair, mask, flipped):
        middle = inner_right(grad, pair[1])
        if mask is not None:
            middle = middle * mask
        middle = middle.astype(BF16)
        main = matmul(grad, weight) if flipped else inner_right(grad, weight)
        return middle, main + matmul(middle, pair[0])

    (img_grad_after, img_grad_att, img_sums, *sides) = block_back(
        g_img, img_after, img_branch, img_mlp, attended, img_rows_mod, img_pre, img_w[3],
        img_pairs[4], img_w[2], img_pairs[3], img_w[1], img_pairs[2], img_mids,
    )
    grads[0][4] = (sides[0], sides[3])
    grads[0][3] = (sides[2], sides[1])
    grads[0][2] = (sides[4], sides[5])
    mod_parts = [[None] * 6 for stream in range(2)]
    for place in range(4):
        mod_parts[1][2 + place] = txt_sums[place]
    grads[1][2] = (txt_sides[0], txt_sides[1])
    grads[1][3] = (txt_sides[2], txt_sides[3])
    grads[1][4] = (txt_sides[4], txt_sides[5])
    img_sums = jnp.sum(jnp.concatenate([img_sums, img_gate]).reshape(4, 8, width), axis=1)
    for place in range(4):
        mod_parts[0][2 + place] = img_sums[place : place + 1]
    grad_after = [img_grad_after, txt_grad_after]

    do_img = to_heads(img_grad_att)
    d_img, d_txt = attend_back(img_heads, txt_heads, bias, do_img, do_txt, lse, HD)
    img_grad_qkv = to_tokens(d_img)
    txt_grad_qkv = txt_home(d_txt)

    img_back_mid, img_grad_norm = project_back(img_grad_qkv, img_w[0], img_pairs[1], None, False)
    grads[0][1] = (inner_left(img_back_mid, heads_in[0]), inner_left(img_qkv_mid, img_grad_qkv))
    txt_grad_norm, txt_qkv_back = give(
        inner_right(txt_grad_qkv, txt_w[0]), inner_right(txt_grad_qkv, txt_pairs[1][1])
    )
    txt_grad_norm = txt_grad_norm + matmul(txt_qkv_back, txt_pairs[1][0])
    grads[1][1] = (
        inner_left(share(txt_qkv_back), lanes(txt_in)),
        inner_left(txt_qkv_mid, txt_grad_qkv),
    )
    grad_norm = [img_grad_norm, txt_grad_norm]
    grad_inputs = []
    for s in range(2):
        grad_inputs.append(
            grad_after[s]
            + norm_back(grad_norm[s], norm_one[s][0], norm_one[s][1], stretch(s, 1))
        )
        mod_parts[s][0] = collapse(s, grad_norm[s])
        mod_parts[s][1] = collapse(s, grad_norm[s] * norm_one[s][0])
    img_dmod = jnp.concatenate(mod_parts[0], axis=1)
    txt_dmod = jnp.concatenate(mod_parts[1], axis=1)
    if n_f == 8:
        cut = width // n_z
        dmod = jnp.concatenate([img_dmod, txt_dmod]).reshape(1 + slots, n_z, -1, cut)
        dmod = jnp.pad(jnp.swapaxes(dmod, 0, 1), ((0, 0), (0, 0), (0, 8 - dmod.shape[2]), (0, 0)))
        tmod = jnp.stack([jnp.pad(mod_mid[s].astype(F32), ((2 * s, 6 - 2 * s), (0, 0))) for s in range(2)])
        cond_own = jnp.pad(lanes(cond_all).astype(F32).reshape(n_f, slots, -1), ((0, 0), (0, 6), (0, 0)))
        sides_of = lambda stream, side: [grads[stream][index][side] for index in range(1, 5)]
        image_low, cond_slices, mod_rank, shard = tail(
            grad_inputs[0].astype(BF16).reshape(2, quarter, width),
            sides_of(0, 0), sides_of(0, 1), sides_of(1, 0), sides_of(1, 1),
            one_hot.T.astype(BF16), own_hot.T.astype(BF16), dmod, mod_weight, jnp.stack(mod_b), tmod, cond_own,
            jnp.pad(jnp.concatenate([seq_mask, seq_mask]), ((0, 4), (0, 0))),
            n_f, n_z, fans, cols, 3,
        )
        image_grad = image_low.astype(F32)
        cond_rows = jnp.swapaxes(cond_slices[:, :slots, :k_local], 0, 1).reshape(slots, width)
        for s in range(2):
            cond_rows = cond_rows + matmul(mod_rank[2 * s : 2 * s + 2].astype(BF16), mod_a[s])
        cond_grad = jax.vjp(jax.nn.silu, conditioning)[1](cond_rows)[0]
        adapter_grad = shard.reshape(1, -1)
        return (
            image_out, txt_result[:txt_local], image_grad, grad_inputs[1][:txt_local], cond_grad, adapter_grad
        )
    image_grad = unshard(grad_inputs[0].astype(BF16)).astype(F32)

    img_dmod = (img_dmod + swap_core(img_dmod)).astype(BF16)
    def lane_blocks(values):
        return jnp.swapaxes(values.reshape(values.shape[0], n_z, -1), 0, 1)

    img_dmods = jnp.concatenate(z_exchange(lane_blocks(img_dmod)), axis=0)
    img_dmods = lax.dynamic_slice_in_dim(img_dmods, core * slots, slots, 0)
    txt_dmods = sum(z_exchange(lane_blocks(txt_dmod))).astype(BF16)
    dmods = jnp.stack([img_dmods, txt_dmods], axis=1)
    dmods_all = lax.all_gather(dmods, "fsdp", axis=0, tiled=True)
    cond_part = sum(inner_right(dmods_all[:, s], mod_weight[s]) for s in range(2))
    mod_back = [inner_right(dmods[:, s], mod_b[s]) for s in range(2)]
    cond_part = cond_part.reshape(-1, width // n_f)
    joined = jnp.concatenate([cond_part.reshape(-1), jnp.stack(mod_back).reshape(-1)])
    joined = sum(z_gather(joined))
    cond_slices = joined[: cond_part.size].reshape(n_f, -1, width // n_f)
    mod_rank = joined[cond_part.size :].reshape(2, slots, -1)
    cond_rows = lax.all_to_all(cond_slices, "fsdp", 0, 2, tiled=True)[0]
    for s in range(2):
        back_mid = (mod_rank[s] * seq_mask).astype(BF16)
        cond_rows = cond_rows + matmul(back_mid, mod_a[s])
        grads[s][0] = (inner_left(back_mid, lanes(cond_act)), inner_left(mod_mid[s], dmods[:, s]))
    cond_grad = jax.vjp(jax.nn.silu, conditioning)[1](cond_rows)[0]

    def spread(values):
        return jnp.swapaxes(values.reshape(RANK, n_z, -1), 0, 1)

    img_rows = {}
    for group in ((2, 3, 4), (1,)):
        parts = [spread(grads[0][index][side]) for side in range(2) for index in group]
        parts = jnp.concatenate(z_exchange(jnp.concatenate(parts, axis=2)), axis=0)
        offset = 0
        for side, sizes in enumerate((fans, cols)):
            for index in group:
                count = sizes[index] // n_z
                img_rows[side, index] = parts[:, offset : offset + count]
                offset += count
    flat = []
    for stream in range(2):
        for index in range(5):
            if stream == 0 and index > 0:
                part_a, part_b = img_rows[0, index], img_rows[1, index]
                hot = one_hot
            else:
                part_a, part_b = grads[stream][index]
                hot = own_hot
            flat.append(
                lax.dot_general(
                    part_a, hot, (((0,), (1,)), ((), ())),
                    precision=HIGH, preferred_element_type=F32,
                )
            )
            flat.append(exact(hot, part_b).reshape(-1, 128))
    total = jnp.concatenate(flat, axis=0).reshape(n_f, -1, 128)
    step = 1
    while step < n_f:
        bit = (f // step) % 2
        pairs = total.reshape((-1, 2) + total.shape[1:])
        keep = lax.dynamic_index_in_dim(pairs, bit, 1, keepdims=False)
        send = lax.dynamic_index_in_dim(pairs, 1 - bit, 1, keepdims=False)
        sent = lax.ppermute(send.astype(BF16), "fsdp", [(i, i ^ step) for i in range(n_f)])
        total = keep + sent.astype(F32)
        step *= 2
    adapter_grad = total.reshape(1, -1)
    return (
        image_out, txt_result[:txt_local], image_grad, grad_inputs[1][:txt_local], cond_grad, adapter_grad
    )


def solution(mesh):
    return jax.shard_map(
        shards,
        mesh=mesh,
        in_specs=(
            P("fsdp", "tp", None),
            P(("fsdp", "tp"), None),
            P("fsdp", None),
            P("fsdp", None),
            P("fsdp"),
            P("tp", "fsdp"),
            P(None, "fsdp", "tp"),
            P(None, "fsdp", "tp"),
            P(None, "tp", "fsdp"),
            P(None, "fsdp", "tp"),
            P(None, "tp", "fsdp"),
            P("fsdp", "tp", None),
            P(("fsdp", "tp"), None),
        ),
        out_specs=(
            P("fsdp", "tp", None),
            P(("fsdp", "tp"), None),
            P("fsdp", "tp", None),
            P(("fsdp", "tp"), None),
            P("fsdp", None),
            P("tp", "fsdp"),
        ),
        check_vma=False,
    )
```

```python
import functools

import jax
import jax.numpy as jnp
from jax import lax
from jax.experimental import pallas as pl
from jax.experimental.pallas import tpu as pltpu
from jax.sharding import PartitionSpec as P

MESH = pl.DeviceIdType.MESH

def bits_of(count):
    return max(count.bit_length() - 1, 0)

def halves(width):
    tiles = width // 128
    first = (tiles + 1) // 2 * 128
    return [(0, first), (first, width - first)]

def gather_kernel(n_f, n_z, full_count, part_count, *refs):
    total = full_count + part_count
    ins, outs = refs[:total], refs[total:2 * total]
    z_send, z_recv, xy_send, xy_recv, core_send, core_recv, own_sem = refs[2 * total:]
    f = lax.axis_index("fsdp")
    z = lax.axis_index("tp")
    chip, core = f // 2, f % 2
    chips = n_f // 2
    nbits = bits_of(chips)
    partner = chip * 2 + (1 - core)

    def peer_of(mask):
        other = 0
        for bit in range(nbits):
            have = (chip // (1 << bit)) % 2
            want = 1 - have if (mask >> bit) & 1 else have
            other = other + want * (1 << bit)
        return other * 2 + core

    barrier = pltpu.get_barrier_semaphore()
    for bit in range(nbits):
        pl.semaphore_signal(barrier, inc=1, device_id=(peer_of(1 << bit), z), device_id_type=MESH)
    pl.semaphore_signal(barrier, inc=1, device_id=(partner, z), device_id_type=MESH)
    @pl.when(z > 0)
    def _():
        pl.semaphore_signal(barrier, inc=1, device_id=(f, z - 1), device_id_type=MESH)
    @pl.when(z < n_z - 1)
    def _():
        pl.semaphore_signal(barrier, inc=1, device_id=(f, z + 1), device_id_type=MESH)
    peers = nbits + 1 + (z > 0).astype(jnp.int32) + (z < n_z - 1).astype(jnp.int32)
    pl.semaphore_wait(barrier, peers)

    def width(m):
        return ins[m].shape[-1]

    def place(m, who, zz, off=0, w=None):
        w = width(m) if w is None else w
        if m < full_count:
            return outs[m].at[who, :, pl.ds(pl.multiple_of(zz * width(m) + off, 128), w)]
        if w == width(m):
            return outs[m].at[who]
        return outs[m].at[who, :, pl.ds(off, w)]

    def piece(m, off, w):
        return ins[m] if w == width(m) else ins[m].at[:, pl.ds(off, w)]

    def remote(src, dst, ssem, rsem, dev):
        return pltpu.make_async_remote_copy(src_ref=src, dst_ref=dst, send_sem=ssem, recv_sem=rsem, device_id=dev, device_id_type=MESH)

    def order_of(half):
        order = list(range(nbits))
        return order if half == 0 else order[::-1]

    def cuts(m):
        if width(m) >= 256:
            return list(enumerate(halves(width(m))))
        return [(m % 2, (0, width(m)))]

    def slot(m, zz):
        return zz if m < full_count else 0

    def xy_copy(m, zz, half, cut, mask, bit, own_piece=False):
        off, w = cut
        who = peer_of(mask)
        source = piece(m, off, w) if own_piece and mask == 0 else place(m, who, zz, off, w)
        return remote(source, place(m, who, zz, off, w),
                      xy_send.at[m, slot(m, zz), half, mask, bit], xy_recv.at[m, slot(m, zz), half, mask | (1 << bit)],
                      (peer_of(1 << bit), z))

    def xy_wait(m, zz, half, cut, mask):
        off, w = cut
        who = peer_of(mask)
        remote(place(m, who, zz, off, w), place(m, who, zz, off, w), xy_send.at[m, slot(m, zz), half, 0, 0],
               xy_recv.at[m, slot(m, zz), half, mask], (partner, z)).wait_recv()

    def core_copy(m, zz, half, cut, mask, own_piece=False):
        off, w = cut
        who = peer_of(mask)
        source = piece(m, off, w) if own_piece and mask == 0 else place(m, who, zz, off, w)
        return remote(source, place(m, who, zz, off, w),
                      core_send.at[m, slot(m, zz), half, mask], core_recv.at[m, slot(m, zz), half, mask], (partner, z))

    def core_wait_recv(m, zz, half, cut, mask):
        off, w = cut
        who = peer_of(mask) - core + (1 - core)
        remote(place(m, who, zz, off, w), place(m, who, zz, off, w),
               core_send.at[m, slot(m, zz), half, mask], core_recv.at[m, slot(m, zz), half, mask], (partner, z)).wait_recv()

    def own(m):
        return pltpu.make_async_copy(ins[m], place(m, f, z), own_sem.at[m])

    def z_copy(m, zz, up, own_piece=False):
        return remote(ins[m] if own_piece else place(m, f, zz), place(m, f, zz), z_send.at[m, zz, up], z_recv.at[m, zz], (f, z + 1 if up else z - 1))

    def launch(m, zz, own_piece=False):
        for half, cut in cuts(m):
            for bit in order_of(half):
                xy_copy(m, zz, half, cut, 0, bit, own_piece).start()
            core_copy(m, zz, half, cut, 0, own_piece).start()

    def masks_in_order(half):
        order = order_of(half)
        def rank(mask):
            return [1 if (mask >> b) & 1 else 0 for b in reversed(order)]
        return sorted(range(1, 1 << nbits), key=rank)

    def forward(m, zz):
        for half, cut in cuts(m):
            order = order_of(half)
            for mask in masks_in_order(half):
                last = max(i for i, b in enumerate(order) if (mask >> b) & 1)
                if last == nbits - 1:
                    continue
                xy_wait(m, zz, half, cut, mask)
                for b in order[last + 1:]:
                    xy_copy(m, zz, half, cut, mask, b).start()
                core_copy(m, zz, half, cut, mask).start()

    def finish(m, zz):
        for half, cut in cuts(m):
            order = order_of(half)
            for mask in masks_in_order(half):
                last = max(i for i, b in enumerate(order) if (mask >> b) & 1)
                if last == nbits - 1:
                    xy_wait(m, zz, half, cut, mask)
                    core_copy(m, zz, half, cut, mask).start()

    def drain(m, zz):
        for half, cut in cuts(m):
            order = order_of(half)
            for mask in [0] + masks_in_order(half):
                last = max([i for i, b in enumerate(order) if (mask >> b) & 1], default=-1)
                for b in order[last + 1:]:
                    xy_copy(m, zz, half, cut, mask, b).wait_send()
                core_copy(m, zz, half, cut, mask).wait_send()
                core_wait_recv(m, zz, half, cut, mask)

    for m in range(total):
        own(m).start()
    for m in range(total):
        if m < full_count:
            @pl.when(z < n_z - 1)
            def _():
                z_copy(m, z, 1, True).start()
            @pl.when(z > 0)
            def _():
                z_copy(m, z, 0, True).start()
        launch(m, z, True)
    for m in range(full_count, total):
        forward(m, z)
    for k in range(1, n_z):
        for m in range(full_count):
            @pl.when(z - k >= 0)
            def _():
                zz = z - k
                z_copy(m, zz, 1).wait_recv()
                @pl.when(z < n_z - 1)
                def _():
                    z_copy(m, zz, 1).start()
                launch(m, zz)
            @pl.when(z + k < n_z)
            def _():
                zz = z + k
                z_copy(m, zz, 0).wait_recv()
                @pl.when(z > 0)
                def _():
                    z_copy(m, zz, 0).start()
                launch(m, zz)
            for sign in ((-1, 1) if k > 1 else (1,)):
                zz = z + sign * (k - 1)
                @pl.when((zz >= 0) & (zz < n_z))
                def _():
                    forward(m, zz)
    for m in range(full_count):
        for sign in (-1, 1):
            zz = z + sign * (n_z - 1)
            @pl.when((zz >= 0) & (zz < n_z))
            def _():
                forward(m, zz)
    for m in range(total):
        if m < full_count:
            def body(zz, _):
                finish(m, zz)
                return 0
            lax.fori_loop(0, n_z, body, 0)
        else:
            finish(m, z)
    for m in range(total):
        own(m).wait()
        if m < full_count:
            def body(zz, _):
                drain(m, zz)
                @pl.when((zz <= z) & (z < n_z - 1))
                def _():
                    z_copy(m, zz, 1).wait_send()
                @pl.when((zz >= z) & (z > 0))
                def _():
                    z_copy(m, zz, 0).wait_send()
                return 0
            lax.fori_loop(0, n_z, body, 0)
        else:
            drain(m, z)

def gather(full, part, n_f, n_z, cid=1):
    arrays = list(full) + list(part)
    total = len(arrays)
    if n_f > 8:
        rows = [lax.all_gather(a, "fsdp", axis=0, tiled=True) for a in arrays]
        return [
            lax.all_gather(a, "tp", axis=1, tiled=True) if i < len(full) else a
            for i, a in enumerate(rows)
        ]
    chips = n_f // 2
    nbits = bits_of(chips)
    shapes = [jax.ShapeDtypeStruct((n_f,) + a.shape[:-1] + (a.shape[-1] * (n_z if i < len(full) else 1),), a.dtype) for i, a in enumerate(arrays)]
    dma = pltpu.SemaphoreType.DMA
    return pl.pallas_call(
        functools.partial(gather_kernel, n_f, n_z, len(full), len(part)),
        out_shape=shapes,
        in_specs=[pl.BlockSpec(memory_space=pl.ANY)] * total,
        out_specs=[pl.BlockSpec(memory_space=pl.ANY)] * total,
        scratch_shapes=[
            dma((total, n_z, 2)), dma((total, n_z)),
            dma((total, n_z, 2, chips, max(nbits, 1))), dma((total, n_z, 2, chips)),
            dma((total, n_z, 2, chips)), dma((total, n_z, 2, chips)), dma((total,)),
        ],
        compiler_params=pltpu.CompilerParams(collective_id=cid, has_side_effects=True),
        name="weight_gather",
    )(*arrays)

def dots(left, right, lc, rc):
    return lax.dot_general(left, right, (((lc,), (rc,)), ((), ())), preferred_element_type=jnp.float32)

def attend_kernel(hd, bq, img_ref, txt_ref, bias_ref, oi_ref, ot_ref, lse_ref):
    img_n, txt_n = img_ref.shape[0], txt_ref.shape[1]
    heads = img_ref.shape[1] // (3 * hd)
    bias = bias_ref[...]
    for h in range(heads):
        base = 3 * hd * h
        ki = img_ref[:, base + hd:base + 2 * hd]
        vi = img_ref[:, base + 2 * hd:base + 3 * hd]
        kt = txt_ref[0, :, base + hd:base + 2 * hd]
        vt = txt_ref[0, :, base + 2 * hd:base + 3 * hd]

        def block(q):
            q = q * jnp.bfloat16(0.125)
            si = dots(ki, q, 1, 1)
            st = dots(kt, q, 1, 1) + bias
            top = jnp.maximum(jnp.max(si, axis=0, keepdims=True), jnp.max(st, axis=0, keepdims=True))
            ei = jnp.exp(si - top)
            et = jnp.exp(st - top)
            total = jnp.sum(ei, axis=0, keepdims=True) + jnp.sum(et, axis=0, keepdims=True)
            o = dots(vi, ei.astype(jnp.bfloat16), 0, 0) + dots(vt, et.astype(jnp.bfloat16), 0, 0)
            return (o / total).T.astype(jnp.bfloat16), top + jnp.log(total)

        for i in range(img_n // bq):
            o, lse = block(img_ref[i * bq:(i + 1) * bq, base:base + hd])
            oi_ref[i * bq:(i + 1) * bq, h * hd:(h + 1) * hd] = o
            lse_ref[0, h:h + 1, i * bq:(i + 1) * bq] = lse
        o, lse = block(txt_ref[0, :, base:base + hd])
        ot_ref[0, :, h * hd:(h + 1) * hd] = o
        lse_ref[0, h:h + 1, img_n:img_n + txt_n] = lse

def attend(img, txt, bias, hd, bq=512):
    img_n, cols = img.shape
    parts, txt_n, _ = txt.shape
    pairs = cols // (6 * hd)
    per = pairs // parts
    return pl.pallas_call(
        functools.partial(attend_kernel, hd, bq),
        grid=(pairs,),
        in_specs=[
            pl.BlockSpec((img_n, 6 * hd), lambda i: (0, i)),
            pl.BlockSpec((1, txt_n, 6 * hd), lambda i: (i // per, 0, i % per)),
            pl.BlockSpec((txt_n, 1), lambda i: (0, 0)),
        ],
        out_specs=[
            pl.BlockSpec((img_n, 2 * hd), lambda i: (0, i)),
            pl.BlockSpec((1, txt_n, 2 * hd), lambda i: (i // per, 0, i % per)),
            pl.BlockSpec((1, 2, img_n + txt_n), lambda i: (i, 0, 0)),
        ],
        out_shape=[
            jax.ShapeDtypeStruct((img_n, pairs * 2 * hd), jnp.bfloat16),
            jax.ShapeDtypeStruct((parts, txt_n, per * 2 * hd), jnp.bfloat16),
            jax.ShapeDtypeStruct((pairs, 2, img_n + txt_n), jnp.float32),
        ],
        compiler_params=pltpu.CompilerParams(vmem_limit_bytes=48 * 1024 * 1024),
        name="attend",
    )(img, txt, bias)

def attend_back_kernel(hd, bq, img_ref, txt_ref, bias_ref, doi_ref, dot_ref, lse_ref, di_ref, dt_ref, acc_i, acc_t):
    img_n, txt_n = img_ref.shape[0], txt_ref.shape[1]
    heads = img_ref.shape[1] // (3 * hd)
    bias = bias_ref[...]
    for h in range(heads):
        base = 3 * hd * h
        ki = img_ref[:, base + hd:base + 2 * hd]
        vi = img_ref[:, base + 2 * hd:base + 3 * hd]
        kt = txt_ref[0, :, base + hd:base + 2 * hd]
        vt = txt_ref[0, :, base + 2 * hd:base + 3 * hd]

        def block(q, do, lse, first):
            q = q * jnp.bfloat16(0.125)
            pi = jnp.exp(dots(ki, q, 1, 1) - lse)
            pt = jnp.exp(dots(kt, q, 1, 1) + bias - lse)
            dwi = dots(vi, do, 1, 1)
            dwt = dots(vt, do, 1, 1)
            delta = jnp.sum(pi * dwi, axis=0, keepdims=True) + jnp.sum(pt * dwt, axis=0, keepdims=True)
            dsi = (pi * (dwi - delta)).astype(jnp.bfloat16)
            dst = (pt * (dwt - delta)).astype(jnp.bfloat16)
            dvi = dots(pi.astype(jnp.bfloat16), do, 1, 0)
            dvt = dots(pt.astype(jnp.bfloat16), do, 1, 0)
            dki = dots(dsi, q, 1, 0)
            dkt = dots(dst, q, 1, 0)
            if first:
                acc_i[0], acc_i[1], acc_t[0], acc_t[1] = dki, dvi, dkt, dvt
            else:
                acc_i[0] += dki
                acc_i[1] += dvi
                acc_t[0] += dkt
                acc_t[1] += dvt
            dq = dots(ki, dsi, 0, 0) + dots(kt, dst, 0, 0)
            return (dq.T * 0.125).astype(jnp.bfloat16)

        for i in range(img_n // bq):
            rows = slice(i * bq, (i + 1) * bq)
            di_ref[rows, base:base + hd] = block(
                img_ref[rows, base:base + hd], doi_ref[rows, h * hd:(h + 1) * hd], lse_ref[0, h:h + 1, rows], i == 0)
        grad = jnp.where(bias < 0, 0.0, dot_ref[0, :, h * hd:(h + 1) * hd].astype(jnp.float32)).astype(jnp.bfloat16)
        dt_ref[0, :, base:base + hd] = block(
            txt_ref[0, :, base:base + hd], grad, lse_ref[0, h:h + 1, img_n:img_n + txt_n], False)
        di_ref[:, base + hd:base + 2 * hd] = acc_i[0].astype(jnp.bfloat16)
        di_ref[:, base + 2 * hd:base + 3 * hd] = acc_i[1].astype(jnp.bfloat16)
        dt_ref[0, :, base + hd:base + 2 * hd] = acc_t[0].astype(jnp.bfloat16)
        dt_ref[0, :, base + 2 * hd:base + 3 * hd] = acc_t[1].astype(jnp.bfloat16)

def attend_back(img, txt, bias, doi, dot, lse, hd, bq=512):
    img_n, cols = img.shape
    parts, txt_n, _ = txt.shape
    pairs = cols // (6 * hd)
    per = pairs // parts
    wide = pl.BlockSpec((img_n, 6 * hd), lambda i: (0, i))
    wide_t = pl.BlockSpec((1, txt_n, 6 * hd), lambda i: (i // per, 0, i % per))
    return pl.pallas_call(
        functools.partial(attend_back_kernel, hd, bq),
        grid=(pairs,),
        in_specs=[
            wide, wide_t,
            pl.BlockSpec((txt_n, 1), lambda i: (0, 0)),
            pl.BlockSpec((img_n, 2 * hd), lambda i: (0, i)),
            pl.BlockSpec((1, txt_n, 2 * hd), lambda i: (i // per, 0, i % per)),
            pl.BlockSpec((1, 2, img_n + txt_n), lambda i: (i, 0, 0)),
        ],
        out_specs=[wide, wide_t],
        out_shape=[jax.ShapeDtypeStruct(img.shape, jnp.bfloat16), jax.ShapeDtypeStruct(txt.shape, jnp.bfloat16)],
        scratch_shapes=[pltpu.VMEM((2, img_n, hd), jnp.float32), pltpu.VMEM((2, txt_n, hd), jnp.float32)],
        compiler_params=pltpu.CompilerParams(vmem_limit_bytes=48 * 1024 * 1024),
        name="attend_back",
    )(img, txt, bias, doi, dot, lse)

ROWS = 64


def mm(left, right):
    return dots(left, right, 1, 0)


def mm_t(left, right):
    return dots(left, right, 1, 1)


def t_mm(left, right):
    return dots(left, right, 0, 0)


def gelu_parts(u):
    scale = 0.7978845608028654
    square = u * u
    tanh = jnp.tanh(scale * (u + 0.044715 * u * square))
    half = 0.5 * (1.0 + tanh)
    slope = half + 0.5 * u * (1.0 - tanh * tanh) * (scale * (1.0 + 3 * 0.044715 * square))
    return u * half, slope


def norm_rows(v):
    center = v - jnp.mean(v, axis=-1, keepdims=True)
    inverse = lax.rsqrt(jnp.mean(center * center, axis=-1, keepdims=True) + 1e-06)
    return center * inverse, inverse


def block_fwd_kernel(tiles, o_ref, x_ref, g_ref, mod_ref, wo_ref, ao_ref, bo_ref, a1_ref, b1_ref, w1_ref, a2_ref, w2_ref, b2_ref,
                     a_out, x1_out, h2_out, u_out, y_out, to_out, t1_out, t2_out, gate_out, m_acc, t2_acc):
    step = pl.program_id(0)
    rows = o_ref.shape[0]
    width = o_ref.shape[1]

    @pl.when(step == 0)
    def _():
        to = mm_t(o_ref[...], ao_ref[...]).astype(jnp.bfloat16)
        to_out[...] = to

        def cols(n, _):
            sl = pl.ds(pl.multiple_of(n * 256, 256), 256)
            a_out[:, sl] = mm_t(o_ref[...], wo_ref[sl, :]) + mm(to_out[...], bo_ref[:, sl])
            return 0

        lax.fori_loop(0, width // 256, cols, 0)

        def norm(r, _):
            sl = pl.ds(pl.multiple_of(r * ROWS, ROWS), ROWS)
            x1 = x_ref[sl, :].astype(jnp.float32) + mod_ref[2:3, :] * a_out[sl, :]
            x1_out[sl, :] = x1
            xh, _inv = norm_rows(x1)
            h2_out[sl, :] = (xh * (1.0 + mod_ref[4:5, :]) + mod_ref[3:4, :]).astype(jnp.bfloat16)
            return 0

        lax.fori_loop(0, rows // ROWS, norm, 0)
        t1_out[...] = mm_t(h2_out[...], a1_ref[...]).astype(jnp.bfloat16)
        m_acc[...] = jnp.zeros_like(m_acc)
        t2_acc[...] = jnp.zeros_like(t2_acc)

    u = mm(h2_out[...], w1_ref[...]) + mm(t1_out[...], b1_ref[...])
    u_out[...] = u
    f = gelu_parts(u)[0].astype(jnp.bfloat16)
    m_acc[...] += mm_t(f, w2_ref[...])
    t2_acc[...] += mm_t(f, a2_ref[...])

    @pl.when(step == tiles - 1)
    def _():
        t2_out[...] = t2_acc[...].astype(jnp.bfloat16)
        gate_out[...] = jnp.zeros_like(gate_out)

        def last(r, _):
            sl = pl.ds(pl.multiple_of(r * ROWS, ROWS), ROWS)
            m = m_acc[sl, :] + mm(t2_out[sl, :], b2_ref[...])
            y_out[sl, :] = (x1_out[sl, :] + mod_ref[5:6, :] * m).astype(jnp.bfloat16)
            gm = g_ref[sl, :].astype(jnp.float32) * m
            gate_out[...] += sum(gm[8 * i:8 * i + 8, :] for i in range(ROWS // 8))
            return 0

        lax.fori_loop(0, rows // ROWS, last, 0)


def block_fwd(o, x, g, mod, wo, pair_o, pair_1, w1, pair_2, w2, tn=512):
    rows, width = o.shape
    hidden = w1.shape[1]
    tiles = hidden // tn
    rank = pair_o[0].shape[0]
    whole = lambda shape: pl.BlockSpec(shape, lambda n: (0,) * len(shape))
    once = lambda shape: pl.BlockSpec(shape, lambda n: (0,) * len(shape), pipeline_mode=pl.Buffered(1))
    tile = lambda height: pl.BlockSpec((height, tn), lambda n: (0, n))
    f32, bf16 = jnp.float32, jnp.bfloat16
    act = (rows, width)
    return pl.pallas_call(
        functools.partial(block_fwd_kernel, tiles),
        grid=(tiles,),
        in_specs=[once(act), once(act), once(act), once(mod.shape), once((width, width)), once((rank, width)), once((rank, width)),
                  once((rank, width)), tile(rank), tile(width), tile(rank), tile(width), once((rank, width))],
        out_specs=[whole(act), whole(act), whole(act), tile(rows), whole(act), whole((rows, rank)), whole((rows, rank)),
                   whole((rows, rank)), whole((8, width))],
        out_shape=[jax.ShapeDtypeStruct(act, f32), jax.ShapeDtypeStruct(act, f32), jax.ShapeDtypeStruct(act, bf16),
                   jax.ShapeDtypeStruct((rows, hidden), f32), jax.ShapeDtypeStruct(act, bf16)]
        + [jax.ShapeDtypeStruct((rows, rank), bf16)] * 3 + [jax.ShapeDtypeStruct((8, width), f32)],
        scratch_shapes=[pltpu.VMEM(act, f32), pltpu.VMEM((rows, rank), f32)],
        compiler_params=pltpu.CompilerParams(vmem_limit_bytes=58 * 1024 * 1024),
        cost_estimate=pl.CostEstimate(flops=2 * rows * width * (width + 2 * hidden), bytes_accessed=4 * width * hidden, transcendentals=0),
        name="block_forward",
    )(o, x, g, mod, wo, *pair_o, pair_1[0], pair_1[1], w1, pair_2[0], w2, pair_2[1])


def block_back_kernel(tiles, g_ref, x1_ref, a_ref, h2_ref, o_ref, mod_ref, u_ref, w2_ref, a2_ref, b2_ref, w1_ref, a1_ref, b1_ref,
                      wo_ref, ao_ref, bo_ref, to_ref, t1_ref, t2_ref,
                      dx1_out, do_out, sums_out, ga2_out, gb1_out, ga1_out, gb2_out, gao_out, gbo_out,
                      dm_ref, dt2_ref, dh_acc, dt1_acc, da_ref):
    step = pl.program_id(0)
    rows, width = g_ref.shape
    bf16 = jnp.bfloat16

    @pl.when(step == 0)
    def _():
        def start(r, _):
            sl = pl.ds(pl.multiple_of(r * ROWS, ROWS), ROWS)
            dm_ref[sl, :] = (mod_ref[5:6, :] * g_ref[sl, :].astype(jnp.float32)).astype(bf16)
            return 0

        lax.fori_loop(0, rows // ROWS, start, 0)
        dt2_ref[...] = mm_t(dm_ref[...], b2_ref[...]).astype(bf16)
        gb2_out[...] = t_mm(t2_ref[...], dm_ref[...])
        dh_acc[...] = jnp.zeros_like(dh_acc)
        dt1_acc[...] = jnp.zeros_like(dt1_acc)

    act, slope = gelu_parts(u_ref[...])
    df = mm(dm_ref[...], w2_ref[...]) + mm(dt2_ref[...], a2_ref[...])
    ga2_out[...] = t_mm(dt2_ref[...], act.astype(bf16))
    du = (df * slope).astype(bf16)
    gb1_out[...] = t_mm(t1_ref[...], du)
    dh_acc[...] += mm_t(du, w1_ref[...])
    dt1_acc[...] += mm_t(du, b1_ref[...])

    @pl.when(step == tiles - 1)
    def _():
        dt1 = dt1_acc[...].astype(bf16)
        dt2_ref[...] = dt1
        ga1_out[...] = t_mm(dt1, h2_ref[...])
        sums_out[...] = jnp.zeros_like(sums_out)

        def last(r, _):
            sl = pl.ds(pl.multiple_of(r * ROWS, ROWS), ROWS)
            dh = dh_acc[sl, :] + mm(dt2_ref[sl, :], a1_ref[...])
            xh, inverse = norm_rows(x1_ref[sl, :])
            dz = dh * (1.0 + mod_ref[4:5, :])
            dx1 = g_ref[sl, :].astype(jnp.float32) + inverse * (
                dz - jnp.mean(dz, axis=-1, keepdims=True) - xh * jnp.mean(dz * xh, axis=-1, keepdims=True))
            dx1_out[sl, :] = dx1
            da_ref[sl, :] = (mod_ref[2:3, :] * dx1).astype(bf16)
            fold = lambda v: sum(v[8 * i:8 * i + 8, :] for i in range(ROWS // 8))
            sums_out[0:8, :] += fold(dx1 * a_ref[sl, :])
            sums_out[8:16, :] += fold(dh)
            sums_out[16:24, :] += fold(dh * xh)
            return 0

        lax.fori_loop(0, rows // ROWS, last, 0)
        dto = mm_t(da_ref[...], bo_ref[...]).astype(bf16)
        dt2_ref[...] = dto
        gao_out[...] = t_mm(dto, o_ref[...])
        gbo_out[...] = t_mm(to_ref[...], da_ref[...])

        def cols(n, _):
            sl = pl.ds(pl.multiple_of(n * 256, 256), 256)
            do_out[:, sl] = (mm(da_ref[...], wo_ref[:, sl]) + mm(dt2_ref[...], ao_ref[:, sl])).astype(bf16)
            return 0

        lax.fori_loop(0, width // 256, cols, 0)


def block_back(g, x1, a, h2, o, mod, u, w2, pair_2, w1, pair_1, wo, pair_o, mids, tn=512):
    rows, width = o.shape
    hidden = w1.shape[1]
    tiles = hidden // tn
    rank = pair_o[0].shape[0]
    whole = lambda shape: pl.BlockSpec(shape, lambda n: (0,) * len(shape))
    once = lambda shape: pl.BlockSpec(shape, lambda n: (0,) * len(shape), pipeline_mode=pl.Buffered(1))
    tile = lambda height: pl.BlockSpec((height, tn), lambda n: (0, n))
    f32, bf16 = jnp.float32, jnp.bfloat16
    act = (rows, width)
    side = (rank, width)
    thin = (rows, rank)
    return pl.pallas_call(
        functools.partial(block_back_kernel, tiles),
        grid=(tiles,),
        in_specs=[once(act)] * 5 + [once(mod.shape), tile(rows), tile(width), tile(rank), once(side), tile(width), once(side), tile(rank),
                  once((width, width)), once(side), once(side)] + [once(thin)] * 3,
        out_specs=[whole(act), whole(act), whole((24, width)), tile(rank), tile(rank)] + [whole(side)] * 4,
        out_shape=[jax.ShapeDtypeStruct(act, f32), jax.ShapeDtypeStruct(act, bf16), jax.ShapeDtypeStruct((24, width), f32)]
        + [jax.ShapeDtypeStruct((rank, hidden), f32)] * 2 + [jax.ShapeDtypeStruct(side, f32)] * 4,
        scratch_shapes=[pltpu.VMEM(act, bf16), pltpu.VMEM(thin, bf16), pltpu.VMEM(act, f32), pltpu.VMEM(thin, f32), pltpu.VMEM(act, bf16)],
        compiler_params=pltpu.CompilerParams(vmem_limit_bytes=58 * 1024 * 1024),
        cost_estimate=pl.CostEstimate(flops=2 * rows * width * (width + 2 * hidden), bytes_accessed=4 * width * hidden, transcendentals=0),
        name="block_backward",
    )(g, x1, a, h2, o, mod, u, w2, pair_2[0], pair_2[1], w1, pair_1[0], pair_1[1], wo, *pair_o, *mids)


def column_peers(n_z):
    f, z = lax.axis_index("fsdp"), lax.axis_index("tp")
    core = f % 2
    base = f - core
    peers = [(f, (z + j) % n_z) for j in range(1, n_z)]
    peers += [(base + 1 - core, (z + j) % n_z) for j in range(n_z)]
    return f, z, core, base, peers


def meet(peers):
    barrier = pltpu.get_barrier_semaphore()
    for peer in peers:
        pl.semaphore_signal(barrier, inc=1, device_id=peer, device_id_type=MESH)
    pl.semaphore_wait(barrier, len(peers))


def push(src, dst, send, recv, peer):
    return pltpu.make_async_remote_copy(
        src_ref=src, dst_ref=dst, send_sem=send, recv_sem=recv, device_id=peer, device_id_type=MESH)


class ZRing:
    def __init__(self, f, z, n_z):
        self.f, self.z, self.n_z = f, z, n_z

    def start(self, source_of, buf, send, recv):
        for j in range(1, self.n_z):
            to = (self.z + j) % self.n_z
            push(source_of(to), buf.at[self.z], send.at[j], recv.at[self.z], (self.f, to)).start()

    def wait(self, buf, send, recv):
        for j in range(1, self.n_z):
            came = (self.z + j) % self.n_z
            push(buf.at[came], buf.at[came], send.at[j], recv.at[came], (self.f, came)).wait_recv()

    def drain(self, source_of, buf, send, recv):
        for j in range(1, self.n_z):
            to = (self.z + j) % self.n_z
            push(source_of(to), buf.at[self.z], send.at[j], recv.at[self.z], (self.f, to)).wait_send()


def text_mid_kernel(n_z, o_ref, x_ref, g_ref, mod_ref, owner_ref, own_ref, mask_ref, lmask_ref, wo_ref, w1_ref, w2_ref,
                    ao_ref, bo_ref, a1_ref, b1_ref, a2_ref, b2_ref,
                    y_out, dx1_out, do_out, sums_out, gao_out, gbo_out, ga1_out, gb1_out, ga2_out, gb2_out,
                    o_got, part_ref, out_buf, in_buf, ag_ref, da_ref, dm_ref, u_ref, f_ref, att_ref, do_buf, x1_ref, br_ref, t_ref,
                    o_send, o_recv, rs_send, rs_recv, ag_send, ag_recv, dm_send, dm_recv, do_send, do_recv):
    f, z, core, base, peers = column_peers(n_z)
    ring = ZRing(f, z, n_z)
    bf16, f32 = jnp.bfloat16, jnp.float32
    pad, width = x_ref.shape
    rank = ao_ref.shape[0]
    share = ao_ref.shape[1]
    meet(peers)

    def modulation(row):
        return jnp.where(own_ref[...] > 0, mod_ref[row:row + 1, :], mod_ref[8 + row:9 + row, :])

    home = [(base + z // 2, 2 * core + i) for i in range(2)]
    for i in range(2):
        here = (z // 2 == core) & (2 * core + i == z)

        @pl.when(here)
        def _():
            copy = pltpu.make_async_copy(o_ref.at[i], o_got.at[z % 2], o_recv.at[z % 2])
            copy.start()
            copy.wait()

        @pl.when(jnp.logical_not(here))
        def _():
            push(o_ref.at[i], o_got.at[z % 2], o_send.at[i], o_recv.at[z % 2], home[i]).start()

    dm_ref[z, :, :] = (modulation(5) * g_ref[...].astype(f32)).astype(bf16)
    ring.start(lambda to: dm_ref.at[z], dm_ref, dm_send, dm_recv)

    for s in range(2):
        here = (z // 2 == core) & (2 * core + s == z)

        @pl.when(jnp.logical_not(here))
        def _():
            push(o_got.at[s], o_got.at[s], o_send.at[s], o_recv.at[s], home[s]).wait_recv()

    owner = owner_ref[...]
    att_ref[...] = jnp.where(
        owner > 0, o_got[0].astype(f32), jnp.where(owner < 0, o_got[1].astype(f32), 0.0)).astype(bf16)

    def scatter(turn, main, rank_part):
        full = jnp.concatenate([main, rank_part], axis=1)
        full = full.reshape(n_z, pad, full.shape[1])
        part_ref[...] = full
        out_buf[...] = full.astype(bf16)
        ring.start(lambda to: out_buf.at[to], in_buf.at[turn], rs_send.at[turn], rs_recv.at[turn])

    def collect(turn):
        ring.wait(in_buf.at[turn], rs_send.at[turn], rs_recv.at[turn])
        total = part_ref[z]
        for j in range(1, n_z):
            total = total + in_buf[turn, (z + j) % n_z].astype(f32)
        ring.drain(lambda to: out_buf.at[to], in_buf.at[turn], rs_send.at[turn], rs_recv.at[turn])
        return total[:, :width], (total[:, width:] * lmask_ref[...]).astype(bf16)

    def spread(turn, ref, *parts):
        offset = 0
        for part in parts:
            ref[z, :, offset:offset + part.shape[1]] = part
            offset += part.shape[1]
        ring.start(lambda to: ref.at[z], ref, ag_send.at[turn], ag_recv.at[turn])

    def spread_end(turn, ref):
        ring.wait(ref, ag_send.at[turn], ag_recv.at[turn])
        ring.drain(lambda to: ref.at[z], ref, ag_send.at[turn], ag_recv.at[turn])

    def gathered(ref, start, count):
        return ref[:, :, start:start + count].reshape(n_z * pad, count)

    def own_lanes(ref):
        at = pl.ds(pl.multiple_of(z * share, 128), share)
        return ref[:, :, at].reshape(n_z * pad, share)

    mask = mask_ref[...]
    att = att_ref[...]
    scatter(0, mm_t(att, wo_ref[...]), mm_t(att, ao_ref[...]))
    branch, to_mine = collect(0)
    branch = branch + mm(to_mine, bo_ref[...])
    br_ref[...] = branch
    x1 = x_ref[...].astype(f32) + modulation(2) * branch
    x1_ref[...] = x1
    xh, _inv = norm_rows(x1)
    h2 = (xh * (1.0 + modulation(4)) + modulation(3)).astype(bf16)
    spread(0, ag_ref, h2, to_mine)
    spread_end(0, ag_ref)
    h2_all = gathered(ag_ref, 0, width)
    to_all = gathered(ag_ref, width, rank)
    t1 = (mm_t(h2_all, a1_ref[...]) * mask).astype(bf16)
    u = mm(h2_all, w1_ref[...]) + mm(t1, b1_ref[...])
    u_ref[...] = u
    act = gelu_parts(u)[0].astype(bf16)
    f_ref[...] = act
    scatter(1, mm_t(act, w2_ref[...]), mm_t(act, a2_ref[...]))
    t_ref[0] = to_all
    t_ref[1] = t1
    feed, t2_mine = collect(1)
    feed = feed + mm(t2_mine, b2_ref[...])
    y_out[...] = (x1_ref[...] + modulation(5) * feed).astype(bf16)

    def collapse(place, values):
        for s in range(2):
            sums_out[2 * place + s:2 * place + s + 1, :] = jnp.sum(
                jnp.where(own_ref[...] == (1.0 if s == 0 else -1.0), values, 0.0), axis=0, keepdims=True)

    collapse(3, g_ref[...].astype(f32) * feed)

    ring.wait(dm_ref, dm_send, dm_recv)
    ring.drain(lambda to: dm_ref.at[z], dm_ref, dm_send, dm_recv)
    dm_all = dm_ref[...].reshape(n_z * pad, width)
    dt2 = (mm_t(dm_all, b2_ref[...]) * mask).astype(bf16)
    df = mm(dm_all, w2_ref[...]) + mm(dt2, a2_ref[...])
    ga2_out[...] = t_mm(dt2, f_ref[...])
    du = (df * gelu_parts(u_ref[...])[1]).astype(bf16)
    scatter(2, mm_t(du, w1_ref[...]), mm_t(du, b1_ref[...]))
    gb1_out[...] = t_mm(t_ref[1], du)
    dh, dt1_mine = collect(2)
    dh = dh + mm(dt1_mine, a1_ref[...])
    xh, inverse = norm_rows(x1_ref[...])
    dz = dh * (1.0 + modulation(4))
    dx1 = g_ref[...].astype(f32) + inverse * (
        dz - jnp.mean(dz, axis=-1, keepdims=True) - xh * jnp.mean(dz * xh, axis=-1, keepdims=True))
    spread(1, da_ref, (modulation(2) * dx1).astype(bf16), dt1_mine, t2_mine)
    dx1_out[...] = dx1
    collapse(0, dx1 * br_ref[...])
    collapse(1, dh)
    collapse(2, dh * xh)
    spread_end(1, da_ref)
    da_all = gathered(da_ref, 0, width)
    dt1 = gathered(da_ref, width, rank)
    t2 = gathered(da_ref, width + rank, rank)
    dto = (mm_t(da_all, bo_ref[...]) * mask).astype(bf16)
    do_buf[...] = (mm(da_all, wo_ref[...]) + mm(dto, ao_ref[...])).astype(bf16)
    for s in range(2):
        here = (z // 2 == core) & (2 * core + s == z)

        @pl.when(here)
        def _():
            copy = pltpu.make_async_copy(do_buf, do_out.at[z % 2], do_recv.at[z % 2])
            copy.start()
            copy.wait()

        @pl.when(jnp.logical_not(here))
        def _():
            push(do_buf, do_out.at[z % 2], do_send.at[s], do_recv.at[z % 2], (base + z // 2, 2 * core + s)).start()

    gao_out[...] = t_mm(dto, att_ref[...])
    gbo_out[...] = t_mm(t_ref[0], own_lanes(da_ref))
    gb2_out[...] = t_mm(t2, own_lanes(dm_ref))
    ga1_out[...] = t_mm(dt1, own_lanes(ag_ref))
    for i in range(2):
        here = (z // 2 == core) & (2 * core + i == z)

        @pl.when(jnp.logical_not(here))
        def _():
            push(do_out.at[i], do_out.at[i], do_send.at[i], do_recv.at[i], home[i]).wait_recv()
            push(do_buf, do_out.at[i], do_send.at[i], do_recv.at[i], home[i]).wait_send()
            push(o_ref.at[i], o_got.at[z % 2], o_send.at[i], o_recv.at[z % 2], home[i]).wait_send()


def text_mid(o, x, g, mod, owner, own, mask, lmask, wo, w1, w2, pair_o, pair_1, pair_2, n_z, cid):
    pad, width = x.shape
    rank, share = pair_o[0].shape
    total = n_z * pad
    hidden = w1.shape[1]
    wide = width + rank
    f32, bf16 = jnp.float32, jnp.bfloat16
    shape = jax.ShapeDtypeStruct
    vmem = pltpu.VMEM
    dma = pltpu.SemaphoreType.DMA
    args = (o, x, g, mod, owner, own, mask, lmask, wo, w1, w2, *pair_o, *pair_1, *pair_2)
    out_shape = [
        shape((pad, width), bf16), shape((pad, width), f32), shape((2, total, share), bf16), shape((8, width), f32),
        shape((rank, share), f32), shape((rank, share), f32), shape((rank, share), f32), shape((rank, hidden), f32),
        shape((rank, hidden), f32), shape((rank, share), f32),
    ]
    return pl.pallas_call(
        functools.partial(text_mid_kernel, n_z),
        out_shape=out_shape,
        in_specs=[pl.BlockSpec(memory_space=vmem)] * len(args),
        out_specs=[pl.BlockSpec(memory_space=vmem)] * len(out_shape),
        scratch_shapes=[
            vmem((2, total, share), bf16), vmem((n_z, pad, wide), f32), vmem((n_z, pad, wide), bf16),
            vmem((3, n_z, pad, wide), bf16), vmem((n_z, pad, wide), bf16), vmem((n_z, pad, wide + rank), bf16),
            vmem((n_z, pad, width), bf16),
            vmem((total, hidden), f32), vmem((total, hidden), bf16), vmem((total, share), bf16),
            vmem((total, share), bf16), vmem((pad, width), f32), vmem((pad, width), f32), vmem((2, total, rank), bf16),
            dma((2,)), dma((2,)), dma((3, n_z)), dma((3, n_z)), dma((2, n_z)), dma((2, n_z)), dma((n_z,)), dma((n_z,)),
            dma((2,)), dma((2,)),
        ],
        compiler_params=pltpu.CompilerParams(collective_id=cid, has_side_effects=True, vmem_limit_bytes=50 * 1024 * 1024),
        name="text_block",
    )(*args)


def flip_bits(chip, mask, nbits):
    other = 0
    for bit in range(nbits):
        have = (chip // (1 << bit)) % 2
        other = other + (1 - have if (mask >> bit) & 1 else have) * (1 << bit)
    return other


def tail_kernel(n_f, n_z, fans, cols, *refs):
    it = iter(refs)
    take = lambda count: [next(it) for _ in range(count)]
    grad_ref, = take(1)
    img_a, img_b, txt_a, txt_b = take(4), take(4), take(4), take(4)
    hot4_ref, hot2_ref, dmod_ref, wmod_ref, bmod_ref, tmod_ref, cond_ref, smask_ref = take(8)
    grad_out, cond_out, rank_out, shard_out = take(4)
    zmsg, zgot, dense, snd1, rcv1, snd2, rcv2, dgot, own_dm, all_dm, cpart, cgot, zsum, zall, dts = take(15)
    (g_send, g_recv, z_send, z_recv, c_send, c_recv, s_send, s_recv, d_send, d_recv, f_send, f_recv, p_send, p_recv,
     q_send, q_recv, t_send, t_recv) = take(18)
    f32, bf16 = jnp.float32, jnp.bfloat16
    f, z, core, base, column = column_peers(n_z)
    chip = f // 2
    chips = n_f // 2
    nbits = bits_of(chips)
    partner = base + 1 - core
    around = [((f + j) % n_f, z) for j in range(1, n_f)]
    others = [(flip_bits(chip, mask, nbits) * 2 + side, z) for mask in range(1, chips) for side in range(2)]
    meet(column + others)
    ring = ZRing(f, z, n_z)
    blk = shard_out.shape[0]
    hidden_rank = hot2_ref.shape[0]

    def dmod_copy(index, peer):
        return push(dmod_ref.at[peer[1]], dgot.at[core * n_z + z], d_send.at[index], d_recv.at[core * n_z + z], peer)

    for index, peer in enumerate(column):
        dmod_copy(index, peer).start()
    dgot[core * n_z + z] = dmod_ref[z]

    offset = 0
    spans = []
    for part, sizes in ((img_a, fans), (img_b, cols)):
        for index in range(4):
            count = sizes[index + 1] // n_z
            for t in range(n_z):
                zmsg[t, :, offset:offset + count] = part[index][:, t * count:(t + 1) * count].astype(bf16)
            spans.append((offset, count))
            offset += count
    ring.start(lambda to: zmsg.at[to], zgot, z_send, z_recv)
    zgot[z] = zmsg[z]

    for index, peer in enumerate(column):
        place = peer[0] % 2 * n_z + peer[1]
        push(dgot.at[place], dgot.at[place], d_send.at[index], d_recv.at[place], peer).wait_recv()
    rows = []
    for slot in range(2):
        rows.append(dgot[2 * core + slot, 0] + dgot[n_z + 2 * core + slot, 0])
    for slot in range(2):
        total = dgot[core * n_z, 1 + slot]
        for t in range(1, n_z):
            total = total + dgot[core * n_z + t, 1 + slot]
        rows.append(total)
    chunk = dmod_ref.shape[-1]
    own_dm[...] = jnp.zeros_like(own_dm)
    for r, total in enumerate(rows):
        for j in range(own_dm.shape[1] // chunk):
            own_dm[r:r + 1, j * chunk:(j + 1) * chunk] = total[j:j + 1, :].astype(bf16).astype(f32)
    for j in range(1, n_f):
        push(own_dm, all_dm.at[f], f_send.at[j], f_recv.at[f], around[j - 1]).start()
    all_dm[f] = own_dm[...]
    dm_low = own_dm[...].astype(bf16)
    tmod = [tmod_ref[s].astype(bf16) for s in range(2)]
    gb_mod = [t_mm(tmod[s], dm_low) for s in range(2)]
    rank_img = mm_t(dm_low, bmod_ref[0])
    rank_txt = mm_t(dm_low, bmod_ref[1])
    row = lax.broadcasted_iota(jnp.int32, rank_img.shape, 0)
    rank_part = jnp.where(row < 2, rank_img, rank_txt)

    hot2 = hot2_ref[...]
    starts = []
    offset = 0
    for stream in range(2):
        for index in range(5):
            starts.append((stream, index, offset, offset + fans[index] // n_z))
            offset += fans[index] // n_z + cols[index] // n_z

    def put_a(at, part, hot):
        dense[at:at + part.shape[1], :] = dots(part, hot, 0, 0)

    def put_b(at, part, hot):
        full = dots(hot, part, 0, 0)
        blocks = part.shape[1] // 128
        for j in range(blocks):
            dense[pl.ds(at + j, 128, stride=blocks), :] = full[:, j * 128:(j + 1) * 128]

    for stream, index, at_a, at_b in starts:
        if index == 0:
            dense[at_a:at_b, :] = jnp.zeros((at_b - at_a, 128), f32)
            put_b(at_b, gb_mod[stream].astype(bf16), hot2)
        elif stream == 1:
            put_a(at_a, txt_a[index - 1][...].astype(bf16), hot2)
            put_b(at_b, txt_b[index - 1][...].astype(bf16), hot2)

    ring.wait(zgot, z_send, z_recv)
    hot4 = hot4_ref[...]
    for stream, index, at_a, at_b in starts:
        if stream == 0 and index > 0:
            for at, put, (begin, count) in ((at_a, put_a, spans[index - 1]), (at_b, put_b, spans[index + 3])):
                part = zgot[:, :, begin:begin + count].reshape(hot4.shape[0], count)
                put(at, part, hot4)

    home = [(base + z // 2, 2 * core + i) for i in range(2)]

    def is_here(i):
        return (z // 2 == core) & (2 * core + i == z)

    for i in range(2):
        @pl.when(is_here(i))
        def _():
            pltpu.make_async_copy(grad_ref.at[i], grad_out.at[z % 2], g_recv.at[z % 2]).start()

        @pl.when(jnp.logical_not(is_here(i)))
        def _():
            push(grad_ref.at[i], grad_out.at[z % 2], g_send.at[i], g_recv.at[z % 2], home[i]).start()

    def block(number):
        return pl.ds(pl.multiple_of(number * blk, 16), blk)

    for p in range(chips):
        snd1[p] = dense[block(2 * p + 1 - core), :].astype(bf16)
        push(snd1.at[p], rcv1.at[p], c_send.at[p], c_recv.at[p], (partner, z)).start()

    for j in range(1, n_f):
        came = (f - j + n_f) % n_f
        push(own_dm, all_dm.at[came], f_send.at[j], f_recv.at[came], (came, z)).wait_recv()
    everyone = all_dm[...].reshape(n_f * 8, own_dm.shape[1]).astype(bf16)
    part = mm_t(everyone, wmod_ref[0]) + pltpu.roll(mm_t(everyone, wmod_ref[1]), n_f * 8 - 2, 0)
    k_local = part.shape[1]
    cpart[...] = jnp.zeros_like(cpart)
    cpart[:, :, :k_local] = part.reshape(n_f, 8, k_local)
    for j in range(1, n_f):
        to = (f + j) % n_f
        push(cpart.at[to], cgot.at[f], p_send.at[j], p_recv.at[f], (to, z)).start()
    cgot[f] = cpart[f]

    for p in range(chips):
        push(snd1.at[p], rcv1.at[p], c_send.at[p], c_recv.at[p], (partner, z)).wait_recv()

    def mine_of(p):
        return block(2 * p + core)

    for p in range(chips):
        dense[mine_of(p), :] += rcv1[p].astype(f32)

    half = blk // 2
    orders = [list(range(nbits)), list(range(nbits))[::-1]]

    def masks_at(side, turn):
        left = orders[side][turn:]
        return [sum(1 << b for i, b in enumerate(left) if (m >> i) & 1) for m in range(1 << len(left))]

    def rs_copy(side, turn, index):
        slot = turn * 2 + index
        peer = flip_bits(chip, 1 << orders[side][turn], nbits) * 2 + core
        return push(snd2.at[side, slot], rcv2.at[side, slot], s_send.at[side, slot], s_recv.at[side, slot], (peer, z))

    def half_of(number, side):
        return pl.ds(pl.multiple_of((2 * number + core) * blk + side * half, 16), half)

    def rs_start(turn):
        for side in range(2):
            bit = 1 << orders[side][turn]
            for index, mask in enumerate(masks_at(side, turn + 1)):
                number = flip_bits(chip, bit | mask, nbits)
                snd2[side, turn * 2 + index] = dense[half_of(number, side), :].astype(bf16)
                rs_copy(side, turn, index).start()

    def rs_end(turn):
        for side in range(2):
            for index, mask in enumerate(masks_at(side, turn + 1)):
                number = flip_bits(chip, mask, nbits)
                rs_copy(side, turn, index).wait_recv()
                dense[half_of(number, side), :] += rcv2[side, turn * 2 + index].astype(f32)

    rs_start(0)

    for j in range(1, n_f):
        came = (f - j + n_f) % n_f
        push(cpart.at[came], cgot.at[came], p_send.at[j], p_recv.at[came], (came, z)).wait_recv()
    zsum[:n_f] = cgot[...]
    zsum[n_f] = jnp.zeros(zsum.shape[1:], f32)
    zsum[n_f, :, :hidden_rank] = rank_part
    zall[z] = zsum[...]
    ring.start(lambda to: zsum, zall, q_send, q_recv)
    ring.wait(zall, q_send, q_recv)
    total = zall[0]
    for t in range(1, n_z):
        total = total + zall[t]
    cond_out[...] = total[:n_f]
    dt = (total[n_f][:, :hidden_rank] * smask_ref[...]).astype(bf16)
    rank_out[...] = dt.astype(f32)
    wide = mm(dt, hot2)
    dts[f] = wide
    for j in range(1, n_f):
        push(dts.at[f], dts.at[f], t_send.at[j], t_recv.at[f], around[j - 1]).start()

    rs_end(0)
    if nbits > 1:
        rs_start(1)
    for j in range(1, n_f):
        came = (f - j + n_f) % n_f
        push(dts.at[came], dts.at[came], t_send.at[j], t_recv.at[came], (came, z)).wait_recv()
    all_dt = dts[...].reshape(n_f * 8, 128)
    row = lax.broadcasted_iota(jnp.int32, all_dt.shape, 0) % 8
    act = cond_ref[...].reshape(n_f * 8, cond_ref.shape[-1]).astype(bf16)
    mod_a = [
        dots(act, jnp.where(row < 2, all_dt, 0.0).astype(bf16), 0, 0),
        dots(act, pltpu.roll(jnp.where((row >= 2) & (row < 4), all_dt, 0.0), n_f * 8 - 2, 0).astype(bf16), 0, 0),
    ]
    if nbits > 1:
        rs_end(1)
    shard_out[...] = dense[block(f), :]
    for stream in range(2):
        first = starts[5 * stream][2]
        own = jnp.where(f == first // blk, 1.0, 0.0)
        count = mod_a[stream].shape[0]
        shard_out[:count, :] += own * mod_a[stream]

    ring.drain(lambda to: zmsg.at[to], zgot, z_send, z_recv)
    ring.drain(lambda to: zsum, zall, q_send, q_recv)
    for index, peer in enumerate(column):
        dmod_copy(index, peer).wait_send()
    for j in range(1, n_f):
        to = (f + j) % n_f
        push(own_dm, all_dm.at[f], f_send.at[j], f_recv.at[f], (to, z)).wait_send()
        push(cpart.at[to], cgot.at[f], p_send.at[j], p_recv.at[f], (to, z)).wait_send()
        push(dts.at[f], dts.at[f], t_send.at[j], t_recv.at[f], (to, z)).wait_send()
    for p in range(chips):
        push(snd1.at[p], rcv1.at[p], c_send.at[p], c_recv.at[p], (partner, z)).wait_send()
    for turn in range(nbits):
        for side in range(2):
            for index in range(len(masks_at(side, turn + 1))):
                rs_copy(side, turn, index).wait_send()
    for i in range(2):
        @pl.when(is_here(i))
        def _():
            pltpu.make_async_copy(grad_ref.at[i], grad_out.at[z % 2], g_recv.at[z % 2]).wait()

        @pl.when(jnp.logical_not(is_here(i)))
        def _():
            push(grad_out.at[i], grad_out.at[i], g_send.at[i], g_recv.at[i], home[i]).wait_recv()
            push(grad_ref.at[i], grad_out.at[z % 2], g_send.at[i], g_recv.at[z % 2], home[i]).wait_send()


def tail(grad, img_a, img_b, txt_a, txt_b, hot4, hot2, dmod, wmod, bmod, tmod, cond, smask, n_f, n_z, fans, cols, cid):
    f32, bf16 = jnp.float32, jnp.bfloat16
    vmem, dma = pltpu.VMEM, pltpu.SemaphoreType.DMA
    shape = jax.ShapeDtypeStruct
    args = (grad, *img_a, *img_b, *txt_a, *txt_b, hot4, hot2, dmod, wmod, bmod, tmod, cond, smask)
    lanes = (sum(fans[1:]) + sum(cols[1:])) // n_z
    rows = 2 * (sum(fans) + sum(cols)) // n_z
    blk = rows // n_f
    chips = n_f // 2
    cut = cols[0] // n_z
    rank = hot2.shape[0]
    inside = pl.BlockSpec(memory_space=vmem)
    return pl.pallas_call(
        functools.partial(tail_kernel, n_f, n_z, tuple(fans), tuple(cols)),
        out_shape=[shape(grad.shape, bf16), shape((n_f, 8, 256), f32), shape((8, rank), f32), shape((blk, 128), f32)],
        in_specs=[pl.BlockSpec(memory_space=pl.ANY)] + [inside] * (len(args) - 1),
        out_specs=[pl.BlockSpec(memory_space=pl.ANY)] + [inside] * 3,
        scratch_shapes=[
            vmem((n_z, RANK, lanes), bf16), vmem((n_z, RANK, lanes), bf16), vmem((rows, 128), f32),
            vmem((chips, blk, 128), bf16), vmem((chips, blk, 128), bf16),
            vmem((2, 4, blk // 2, 128), bf16), vmem((2, 4, blk // 2, 128), bf16),
            vmem((2 * n_z,) + dmod.shape[1:], f32), vmem((8, cut), f32), vmem((n_f, 8, cut), f32),
            vmem((n_f, 8, 256), f32), vmem((n_f, 8, 256), f32), vmem((n_f + 1, 8, 256), f32),
            vmem((n_z, n_f + 1, 8, 256), f32), vmem((n_f, 8, 128), f32),
            dma((2,)), dma((2,)), dma((n_z,)), dma((n_z,)), dma((chips,)), dma((chips,)), dma((2, 4)), dma((2, 4)),
            dma((2 * n_z,)), dma((2 * n_z,)), dma((n_f,)), dma((n_f,)), dma((n_f,)), dma((n_f,)), dma((n_z,)), dma((n_z,)),
            dma((n_f,)), dma((n_f,)),
        ],
        compiler_params=pltpu.CompilerParams(collective_id=cid, has_side_effects=True, vmem_limit_bytes=56 * 1024 * 1024),
        name="gradient_exchange",
    )(*args)

FULL = 4
PART = 4


def front_kernel(n_f, n_z, fans, cols, *refs):
    it = iter(refs)
    take = lambda count: [next(it) for _ in range(count)]
    ins = take(FULL + PART + 1)
    (x_ref, g_ref, picks_ref, hot2_ref, cblk_ref, clane_ref, c8_ref, smask_ref, wmod_ref, xt_ref, own_ref, tmask_ref) = take(12)
    outs = take(FULL + PART)
    x_out, g_out, imod_out, tmod_out = take(4)
    img_a, img_b, txt_a, txt_b = take(4), take(4), take(4), take(4)
    moda_out, modb_out, midm_out, cond_out = take(4)
    h_out, mid_out, heads_out, th_out, tmid_out, theads_out = take(6)
    (row_ref, fl_ref, img_msg, img_got, txt_msg, txt_got, cgot, mpart, mgot, own_mod, mod_got, wtile, wtxt, stage, tq_ref) = take(15)
    (z_send, z_recv, xy_send, xy_recv, core_send, core_recv, own_sem, x_send, x_recv, g_send, g_recv, c_send, c_recv, l_send,
     l_recv, m_send, m_recv, i_send, i_recv, t_send, t_recv, d_send, d_recv, a_send, a_recv, w_sem, tw_sem, h_send, h_recv,
     h_sem, q_send, q_recv) = take(32)
    f32, bf16 = jnp.float32, jnp.bfloat16
    f, z, core, base, column = column_peers(n_z)
    chip = f // 2
    chips = n_f // 2
    nbits = bits_of(chips)
    partner = base + 1 - core
    others = [(flip_bits(chip, mask, nbits) * 2 + side, z) for mask in range(1, chips) for side in range(2)]
    meet(column + others)
    ring = ZRing(f, z, n_z)
    total = FULL + PART + 1
    adapters = total - 1
    blk = ins[adapters].shape[0]
    width = x_ref.shape[2]
    rank2 = hot2_ref.shape[0]

    def peer_of(mask):
        return flip_bits(chip, mask, nbits) * 2 + core

    def wide_of(m):
        return ins[m].shape[-1]

    def cuts(m):
        if m == adapters:
            return [(0, (0, blk // 2)), (1, (blk // 2, blk // 2))]
        return list(enumerate(halves(wide_of(m))))

    def place(m, who, zz, cut):
        off, w = cut
        if m == adapters:
            return row_ref.at[pl.ds(pl.multiple_of(who * blk + off, 16), w), :]
        if m < FULL:
            return outs[m].at[who, :, pl.ds(pl.multiple_of(zz * wide_of(m) + off, 128), w)]
        return outs[m].at[who, :, pl.ds(off, w)]

    def piece(m, cut):
        off, w = cut
        if m == adapters:
            return ins[m].at[pl.ds(off, w), :]
        return ins[m].at[:, pl.ds(off, w)]

    def whole_place(m, who, zz):
        return place(m, who, zz, (0, blk if m == adapters else wide_of(m)))

    def slot(m, zz):
        return zz if m < FULL else 0

    def order_of(half):
        order = list(range(nbits))
        return order if half == 0 else order[::-1]

    def xy_copy(m, zz, half, cut, mask, bit, own_piece=False):
        where = place(m, peer_of(mask), zz, cut)
        return push(piece(m, cut) if own_piece else where, where, xy_send.at[m, slot(m, zz), half, mask, bit],
                    xy_recv.at[m, slot(m, zz), half, mask | (1 << bit)], (peer_of(1 << bit), z))

    def xy_wait(m, zz, half, cut, mask):
        where = place(m, peer_of(mask), zz, cut)
        push(where, where, xy_send.at[m, slot(m, zz), half, 0, 0], xy_recv.at[m, slot(m, zz), half, mask], (partner, z)).wait_recv()

    def core_copy(m, zz, half, cut, mask, own_piece=False):
        where = place(m, peer_of(mask), zz, cut)
        return push(piece(m, cut) if own_piece else where, where, core_send.at[m, slot(m, zz), half, mask],
                    core_recv.at[m, slot(m, zz), half, mask], (partner, z))

    def core_wait(m, zz, half, cut, mask):
        where = place(m, peer_of(mask) - core + (1 - core), zz, cut)
        push(where, where, core_send.at[m, slot(m, zz), half, mask], core_recv.at[m, slot(m, zz), half, mask], (partner, z)).wait_recv()

    def own_copy(m):
        return pltpu.make_async_copy(ins[m], whole_place(m, f, z), own_sem.at[m])

    def z_copy(m, zz, up, own_piece=False):
        where = whole_place(m, f, zz)
        return push(ins[m] if own_piece else where, where, z_send.at[m, zz, up], z_recv.at[m, zz], (f, z + 1 if up else z - 1))

    def last_of(order, mask):
        return max([i for i, b in enumerate(order) if (mask >> b) & 1], default=-1)

    def masks_in_order(half):
        order = order_of(half)
        return sorted(range(1, 1 << nbits), key=lambda mask: [1 if (mask >> b) & 1 else 0 for b in reversed(order)])

    def launch(m, zz, own_piece=False):
        for half, cut in cuts(m):
            for bit in order_of(half):
                xy_copy(m, zz, half, cut, 0, bit, own_piece).start()
            core_copy(m, zz, half, cut, 0, own_piece).start()

    def launch_own(m):
        if m < FULL:
            @pl.when(z < n_z - 1)
            def _():
                z_copy(m, z, 1, True).start()

            @pl.when(z > 0)
            def _():
                z_copy(m, z, 0, True).start()
        launch(m, z, True)
        own_copy(m).start()

    def forward(m, zz):
        for half, cut in cuts(m):
            order = order_of(half)
            for mask in masks_in_order(half):
                if last_of(order, mask) < nbits - 1:
                    xy_wait(m, zz, half, cut, mask)
                    for b in order[last_of(order, mask) + 1:]:
                        xy_copy(m, zz, half, cut, mask, b).start()
                    core_copy(m, zz, half, cut, mask).start()

    def finish(m, zz):
        for half, cut in cuts(m):
            order = order_of(half)
            for mask in masks_in_order(half):
                if last_of(order, mask) == nbits - 1:
                    xy_wait(m, zz, half, cut, mask)
                    core_copy(m, zz, half, cut, mask).start()

    def settle(m, zz):
        for half, cut in cuts(m):
            for mask in range(1 << nbits):
                core_wait(m, zz, half, cut, mask)

    def drain(m, zz):
        for half, cut in cuts(m):
            order = order_of(half)
            for mask in range(1 << nbits):
                for b in order[last_of(order, mask) + 1:]:
                    xy_copy(m, zz, half, cut, mask, b).wait_send()
                core_copy(m, zz, half, cut, mask).wait_send()

    def at_distance(k, body):
        for sign in ((-1, 1) if k else (1,)):
            zz = z + sign * k

            @pl.when((zz >= 0) & (zz < n_z))
            def _():
                body(zz)

    def arrive(m, k):
        @pl.when(z - k >= 0)
        def _():
            zz = z - k
            z_copy(m, zz, 1).wait_recv()

            @pl.when(z < n_z - 1)
            def _():
                z_copy(m, zz, 1).start()

            launch(m, zz)

        @pl.when(z + k < n_z)
        def _():
            zz = z + k
            z_copy(m, zz, 0).wait_recv()

            @pl.when(z > 0)
            def _():
                z_copy(m, zz, 0).start()

            launch(m, zz)

    def every_z(m, body):
        if m < FULL:
            def step(zz, _):
                body(m, zz)
                return 0

            lax.fori_loop(0, n_z, step, 0)
        else:
            body(m, z)

    there = [(base + z // 2, 2 * core + s) for s in range(2)]

    def is_here(s):
        return (z // 2 == core) & (2 * core + s == z)

    def token_push(src, dst, send, recv, s):
        return push(src.at[s], dst.at[z % 2], send.at[s], recv.at[z % 2], there[s])

    def tokens_start(src, dst, send, recv):
        for s in range(2):
            @pl.when(is_here(s))
            def _():
                pltpu.make_async_copy(src.at[s], dst.at[z % 2], recv.at[z % 2]).start()

            @pl.when(jnp.logical_not(is_here(s)))
            def _():
                token_push(src, dst, send, recv, s).start()

    def tokens_wait(src, dst, send, recv):
        for i in range(2):
            @pl.when(is_here(i))
            def _():
                pltpu.make_async_copy(src.at[i], dst.at[z % 2], recv.at[z % 2]).wait()

            @pl.when(jnp.logical_not(is_here(i)))
            def _():
                push(dst.at[i], dst.at[i], send.at[i], recv.at[i], there[i]).wait_recv()

    def tokens_drain(src, dst, send, recv):
        for s in range(2):
            @pl.when(jnp.logical_not(is_here(s)))
            def _():
                token_push(src, dst, send, recv, s).wait_send()

    def around(src_of, dst, send, recv):
        return [push(src_of((f + j) % n_f), dst.at[f], send.at[j], recv.at[f], ((f + j) % n_f, z)) for j in range(1, n_f)]

    def around_wait(dst, send, recv):
        for j in range(1, n_f):
            came = (f - j + n_f) % n_f
            push(dst.at[came], dst.at[came], send.at[j], recv.at[came], (came, z)).wait_recv()

    cond_sends = around(lambda to: cblk_ref.at[to], cgot, c_send, c_recv)
    lane_sends = around(lambda to: clane_ref, cond_out, l_send, l_recv)
    mod_sends = around(lambda to: mpart.at[to], mgot, m_send, m_recv)

    for copy in cond_sends + lane_sends:
        copy.start()
    launch_own(adapters)
    tokens_start(x_ref, x_out, x_send, x_recv)
    launch_own(FULL)
    launch_own(0)
    cgot[f] = cblk_ref[f]
    cond_out[f] = clane_ref[...]

    around_wait(cgot, c_send, c_recv)
    k_local = wmod_ref.shape[1]
    everyone = cgot[...].reshape(n_f * 8, cgot.shape[2])[:, :k_local].astype(bf16)
    mpart[...] = (mm(everyone, wmod_ref[0]) + pltpu.roll(mm(everyone, wmod_ref[1]), 2, 0)).reshape(mpart.shape)
    for copy in mod_sends:
        copy.start()
    mgot[f] = mpart[f]

    forward(adapters, z)
    forward(FULL, z)
    for m in (1, 2, 3):
        launch_own(m)
    for m in (FULL + 1, FULL + 2, FULL + 3):
        launch_own(m)
    for k in range(1, n_z):
        arrive(0, k)
        at_distance(k - 1, lambda zz: forward(0, zz))
    for m in (1, 2, 3):
        arrive(m, 1)
        at_distance(0, lambda zz: forward(m, zz))
    at_distance(n_z - 1, lambda zz: forward(0, zz))
    for m in (FULL + 1, FULL + 2, FULL + 3):
        forward(m, z)

    finish(adapters, z)
    settle(adapters, z)
    own_copy(adapters).wait()
    hot2 = hot2_ref[...]
    starts = {}
    offset = 0
    for stream in range(2):
        for index in range(5):
            starts[stream, index] = (offset, offset + fans[index] // n_z)
            offset += fans[index] // n_z + cols[index] // n_z

    def pick_a(stream, index):
        at = starts[stream, index][0]
        return mm_t(hot2, row_ref[at:at + fans[index] // n_z, :]).astype(bf16)

    def pick_b(stream, index, s, put):
        at = starts[stream, index][1]
        count = cols[index] // n_z // NAD
        flat = row_ref[at:at + count, :].astype(f32) * picks_ref[s * NAD:s * NAD + 1, :]
        for k in range(1, NAD):
            begin = at + k * count
            flat = flat + row_ref[begin:begin + count, :].astype(f32) * picks_ref[s * NAD + k:s * NAD + k + 1, :]
        fl_ref[:count, :] = flat
        blocks = count // RANK
        for j in range(blocks):
            put(j * 128, fl_ref[pl.ds(j, RANK, stride=blocks), :].astype(bf16))

    spans_a, spans_b = [], []
    offset = 0
    for index in range(1, 5):
        count = fans[index] // n_z
        picked = pick_a(0, index)
        for s in range(2):
            img_msg[s, :, offset:offset + count] = picked[s * RANK:(s + 1) * RANK]
        spans_a.append((offset, count))
        offset += count
    for index in range(1, 5):
        count = cols[index] // n_z
        for s in range(2):
            def put(at, value, s=s, offset=offset):
                img_msg[s, :, offset + at:offset + at + 128] = value
            pick_b(0, index, s, put)
        spans_b.append((offset, count))
        offset += count

    def img_push(s, side):
        return push(img_msg.at[s], img_got.at[z], i_send.at[s, side], i_recv.at[z], (base + side, 2 * core + s))

    for s in range(2):
        for side in range(2):
            self_here = (side == core) & (2 * core + s == z)

            @pl.when(self_here)
            def _():
                img_got[z] = img_msg[s]

            @pl.when(jnp.logical_not(self_here))
            def _():
                img_push(s, side).start()

    share = width // n_z
    for place_at, (stream, index) in enumerate([(0, 0), (1, 0), (1, 1), (1, 3)]):
        txt_msg[:, place_at * share:(place_at + 1) * share] = pick_a(stream, index)
    for place_at, index in ((4, 2), (5, 4)):
        for s in range(2):
            def put(at, value, s=s, place_at=place_at):
                txt_msg[s * RANK:(s + 1) * RANK, place_at * share + at:place_at * share + at + 128] = value
            pick_b(1, index, s, put)
    txt_got[z] = txt_msg[...]
    ring.start(lambda to: txt_msg, txt_got, t_send, t_recv)
    for ref in txt_a + txt_b:
        ref[...] = jnp.zeros_like(ref)
    for index in (2, 4):
        txt_a[index - 1][:rank2, :] = pick_a(1, index)
    for ref, stream, index in ((txt_b[0], 1, 1), (txt_b[2], 1, 3), (modb_out.at[0], 0, 0), (modb_out.at[1], 1, 0)):
        for s in range(2):
            def put(at, value, ref=ref, s=s):
                ref[s * RANK:(s + 1) * RANK, at:at + 128] = value
            pick_b(stream, index, s, put)

    for m in (1, 2, 3):
        arrive(m, 2)
        at_distance(1, lambda zz: forward(m, zz))

    ring.wait(txt_got, t_send, t_recv)
    for t in range(n_z):
        lanes = slice(t * share, (t + 1) * share)
        got = lambda number: txt_got[t, :, number * share:(number + 1) * share]
        moda_out[0, :, lanes] = got(0)
        moda_out[1, :, lanes] = got(1)
        txt_a[0][:rank2, lanes] = got(2)
        txt_a[2][:rank2, lanes] = got(3)
        txt_b[1][:rank2, lanes] = got(4)
        txt_b[3][:rank2, lanes] = got(5)
    around_wait(mgot, m_send, m_recv)
    mod_sum = mgot[0]
    for j in range(1, n_f):
        mod_sum = mod_sum + mgot[j]
    c8 = c8_ref[...].astype(bf16)
    thin = mm_t(c8, moda_out[0])
    row = lax.broadcasted_iota(jnp.int32, thin.shape, 0)
    middle = (jnp.where(row < 2, thin, mm_t(c8, moda_out[1])) * smask_ref[...]).astype(bf16)
    low = jnp.where(row < 2, middle.astype(f32), 0.0)
    high = jnp.where((row >= 2) & (row < 4), middle.astype(f32), 0.0)
    midm_out[0] = low
    midm_out[1] = high
    own_mod[...] = mod_sum + mm(low.astype(bf16), modb_out[0]) + mm(high.astype(bf16), modb_out[1])

    def mod_push(index, peer):
        return push(own_mod, mod_got.at[core * n_z + z], d_send.at[index], d_recv.at[core * n_z + z], peer)

    for index, peer in enumerate(column):
        mod_push(index, peer).start()
    mod_got[core * n_z + z] = own_mod[...]

    for t in range(n_z):
        @pl.when(jnp.logical_not((z // 2 == core) & (t == z)))
        def _():
            push(img_got.at[t], img_got.at[t], i_send.at[0, 0], i_recv.at[t], (base + z // 2, t)).wait_recv()
    for t in range(n_z):
        for refs_of, spans in ((img_a, spans_a), (img_b, spans_b)):
            for ref, (begin, count) in zip(refs_of, spans):
                ref[:, t * count:(t + 1) * count] = img_got[t, :, begin:begin + count]

    for index, peer in enumerate(column):
        place_at = peer[0] % 2 * n_z + peer[1]
        push(mod_got.at[place_at], mod_got.at[place_at], d_send.at[index], d_recv.at[place_at], peer).wait_recv()
    step = width // 2
    per = own_mod.shape[1] // step
    imod_out[...] = jnp.zeros_like(imod_out)
    tmod_out[...] = jnp.zeros_like(tmod_out)
    for q in range(12):
        t, lanes = q // per, slice(q % per * step, (q % per + 1) * step)
        into = slice(q % 2 * step, (q % 2 + 1) * step)
        here = mod_got[z // 2 * n_z + t]
        imod_out[q // 2:q // 2 + 1, into] = jnp.where(z % 2 == 0, here[0:1, lanes], here[1:2, lanes])
        ours = mod_got[core * n_z + t]
        for s in range(2):
            tmod_out[8 * s + q // 2:8 * s + q // 2 + 1, into] = ours[2 + s:3 + s, lanes]

    own = own_ref[...]
    pick = lambda r: jnp.where(own > 0, tmod_out[r:r + 1, :], tmod_out[8 + r:9 + r, :])
    hat, _inv = norm_rows(xt_ref[...].astype(f32))
    th_out[z] = (hat * (1.0 + pick(1)) + pick(0)).astype(bf16)
    ring.start(lambda to: th_out.at[z], th_out, a_send, a_recv)
    tokens_wait(x_ref, x_out, x_send, x_recv)
    quarter = x_ref.shape[1]
    for i in range(2):
        def norm(r, _):
            sl = pl.ds(pl.multiple_of(r * ROWS, ROWS), ROWS)
            hat, _inv = norm_rows(x_out[i, sl, :].astype(f32))
            h_out[pl.ds(pl.multiple_of(i * quarter + r * ROWS, ROWS), ROWS), :] = (
                hat * (1.0 + imod_out[1:2, :]) + imod_out[0:1, :]).astype(bf16)
            return 0

        lax.fori_loop(0, quarter // ROWS, norm, 0)
    tokens_start(g_ref, g_out, g_send, g_recv)

    for m in (1, 2, 3):
        arrive(m, 3)
        at_distance(2, lambda zz: forward(m, zz))

    finish(FULL, z)
    settle(FULL, z)
    own_copy(FULL).wait()
    load = pltpu.make_async_copy(outs[FULL], wtxt, tw_sem)
    load.start()
    ring.wait(th_out, a_send, a_recv)
    pad = xt_ref.shape[0]
    h_txt = th_out[...].reshape(n_z * pad, width)
    tmid = (mm_t(h_txt, txt_a[0][...]) * tmask_ref[...]).astype(bf16)
    tmid_out[...] = tmid
    load.wait()
    tq_ref[...] = (mm(h_txt, wtxt[...].reshape(width, wtxt.shape[2])) + mm(tmid, txt_b[0][...])).astype(bf16)
    for s in range(2):
        @pl.when(is_here(s))
        def _():
            copy = pltpu.make_async_copy(tq_ref, theads_out.at[z % 2], q_recv.at[z % 2])
            copy.start()
            copy.wait()

        @pl.when(jnp.logical_not(is_here(s)))
        def _():
            push(tq_ref, theads_out.at[z % 2], q_send.at[s], q_recv.at[z % 2], there[s]).start()

    every_z(0, finish)
    every_z(0, settle)
    own_copy(0).wait()
    mid = mm_t(h_out[...], img_a[0][...]).astype(bf16)
    mid_out[...] = mid
    tn = wtile.shape[3]
    per_half = stage.shape[2] // tn

    def tile_of(n):
        side = 1 - core if n < per_half else core
        return side, side * per_half + n % per_half

    def tile_load(n):
        at = pl.ds(pl.multiple_of(tile_of(n)[1] * tn, 128), tn)
        return pltpu.make_async_copy(outs[0].at[:, :, at], wtile.at[n % 2], w_sem.at[n % 2])

    def heads_push():
        return push(stage.at[0], heads_out.at[core], h_send, h_recv, (partner, z))

    tile_load(0).start()
    for n in range(2 * per_half):
        if n + 1 < 2 * per_half:
            tile_load(n + 1).start()
        tile_load(n).wait()
        at = pl.ds(pl.multiple_of(tile_of(n)[1] * tn, 128), tn)
        lanes = slice(n % per_half * tn, (n % per_half + 1) * tn)
        stage[n // per_half, :, lanes] = (
            mm(h_out[...], wtile[n % 2].reshape(width, tn)) + mm(mid, img_b[0][:, at])).astype(bf16)
        if n == per_half - 1:
            heads_push().start()
    keep = pltpu.make_async_copy(stage.at[1], heads_out.at[core], h_sem)
    keep.start()

    for m in (1, 2, 3):
        at_distance(n_z - 1, lambda zz: forward(m, zz))
    for m in range(total - 1):
        if m not in (0, FULL):
            every_z(m, finish)
    for m in range(total - 1):
        if m not in (0, FULL):
            every_z(m, settle)
            own_copy(m).wait()
    for m in range(total):
        every_z(m, drain)
        if m < FULL:
            def sent(zz, _):
                @pl.when((zz <= z) & (z < n_z - 1))
                def _():
                    z_copy(m, zz, 1).wait_send()

                @pl.when((zz >= z) & (z > 0))
                def _():
                    z_copy(m, zz, 0).wait_send()

                return 0

            lax.fori_loop(0, n_z, sent, 0)
    for copy in cond_sends + lane_sends + mod_sends:
        copy.wait_send()
    around_wait(cond_out, l_send, l_recv)
    ring.drain(lambda to: txt_msg, txt_got, t_send, t_recv)
    ring.drain(lambda to: th_out.at[z], th_out, a_send, a_recv)
    for index, peer in enumerate(column):
        mod_push(index, peer).wait_send()
    for s in range(2):
        for side in range(2):
            @pl.when(jnp.logical_not((side == core) & (2 * core + s == z)))
            def _():
                img_push(s, side).wait_send()
    tokens_wait(g_ref, g_out, g_send, g_recv)
    tokens_drain(x_ref, x_out, x_send, x_recv)
    tokens_drain(g_ref, g_out, g_send, g_recv)
    keep.wait()
    heads_push().wait_send()
    push(stage.at[0], heads_out.at[1 - core], h_send, h_recv, (partner, z)).wait_recv()
    for s in range(2):
        @pl.when(jnp.logical_not(is_here(s)))
        def _():
            push(theads_out.at[s], theads_out.at[s], q_send.at[s], q_recv.at[s], there[s]).wait_recv()
            push(tq_ref, theads_out.at[z % 2], q_send.at[s], q_recv.at[z % 2], there[s]).wait_send()


def front(full, part, adapter_rows, x, g, picks, hot2, cond, wmod, x_txt, own, tmask, smask, n_f, n_z, fans, cols, cid):
    f32, bf16 = jnp.float32, jnp.bfloat16
    vmem, dma = pltpu.VMEM, pltpu.SemaphoreType.DMA
    shape = jax.ShapeDtypeStruct
    slots, width = cond.shape
    k_local = wmod.shape[1]
    z = lax.axis_index("tp")
    blocks = jnp.pad(jnp.swapaxes(cond.reshape(slots, n_f, k_local), 0, 1), ((0, 0), (0, 6), (0, 256 - k_local)))
    cond8 = jnp.concatenate([cond, cond, jnp.zeros((4, width), f32)])
    lane = jnp.pad(lax.dynamic_slice_in_dim(cond, z * (width // n_z), width // n_z, 1), ((0, 6), (0, 0)))
    chosen = (picks[:, None] == jnp.arange(NAD)[None, :]).astype(f32).reshape(-1, 1)
    smalls = (jnp.broadcast_to(chosen, (slots * NAD, 128)), hot2, blocks, lane, cond8, smask, wmod, x_txt, own, tmask)
    args = (*full, *part, adapter_rows, x, g, *smalls)
    any_spec, in_vmem = pl.BlockSpec(memory_space=pl.ANY), pl.BlockSpec(memory_space=vmem)
    rows = 2 * (sum(fans) + sum(cols)) // n_z
    chips = n_f // 2
    nbits = bits_of(chips)
    total = len(full) + len(part) + 1
    pad = x_txt.shape[0]
    img_rows = 2 * x.shape[1]
    cut = cols[0] // n_z
    qkv_part = cols[1] // n_z
    thick = tmask.shape[1]
    rank2 = hot2.shape[0]
    own_a = [fans[1], fans[2] // n_z, fans[3], fans[4] // n_z]
    own_b = [cols[1] // n_z, cols[2], cols[3] // n_z, cols[4]]
    lanes = (sum(fans[1:]) + sum(cols[1:])) // n_z
    share = width // n_z
    outs = [shape((n_f,) + a.shape[:-1] + (a.shape[-1] * (n_z if i < len(full) else 1),), a.dtype) for i, a in enumerate(full + part)]
    in_hbm = len(outs)
    outs += [shape(x.shape, bf16), shape(g.shape, bf16), shape((8, width), f32), shape((16, width), f32)]
    outs += [shape((RANK, n), bf16) for n in fans[1:]] + [shape((RANK, n), bf16) for n in cols[1:]]
    outs += [shape((thick, n), bf16) for n in own_a] + [shape((thick, n), bf16) for n in own_b]
    outs += [shape((2, rank2, width), bf16), shape((2, rank2, cut), bf16), shape((2, 8, rank2), f32), shape((n_f, 8, share), f32)]
    outs += [shape((img_rows, width), bf16), shape((img_rows, RANK), bf16), shape((2, img_rows, cols[1] // 2), bf16),
             shape((n_z, pad, width), bf16), shape((n_z * pad, thick), bf16), shape((2, n_z * pad, qkv_part), bf16)]
    specs = [any_spec] * in_hbm + [in_vmem, any_spec] + [in_vmem] * (len(outs) - in_hbm - 2)
    specs[len(outs) - 4] = any_spec
    specs[len(outs) - 1] = any_spec
    return pl.pallas_call(
        functools.partial(front_kernel, n_f, n_z, tuple(fans), tuple(cols)),
        out_shape=outs,
        in_specs=[any_spec] * (total + 2) + [in_vmem] * len(smalls),
        out_specs=specs,
        scratch_shapes=[
            vmem((rows, 128), bf16), vmem((cut // NAD, 128), f32), vmem((2, RANK, lanes), bf16), vmem((n_z, RANK, lanes), bf16),
            vmem((rank2, 6 * share), bf16), vmem((n_z, rank2, 6 * share), bf16), vmem((n_f, 8, 256), f32),
            vmem((n_f, 8, cut), f32), vmem((n_f, 8, cut), f32), vmem((8, cut), f32), vmem((2 * n_z, 8, cut), f32),
            vmem((2, n_f, k_local, 768), bf16), vmem((n_f, k_local, qkv_part), bf16), vmem((2, img_rows, cols[1] // 2), bf16),
            vmem((n_z * pad, qkv_part), bf16),
            dma((total, n_z, 2)), dma((total, n_z)), dma((total, n_z, 2, chips, nbits)), dma((total, n_z, 2, chips)),
            dma((total, n_z, 2, chips)), dma((total, n_z, 2, chips)), dma((total,)),
            dma((2,)), dma((2,)), dma((2,)), dma((2,)), dma((n_f,)), dma((n_f,)), dma((n_f,)), dma((n_f,)), dma((n_f,)), dma((n_f,)),
            dma((2, 2)), dma((n_z,)), dma((n_z,)), dma((n_z,)), dma((2 * n_z,)), dma((2 * n_z,)), dma((n_z,)), dma((n_z,)),
            dma((2,)), dma, dma, dma, dma, dma((2,)), dma((2,)),
        ],
        compiler_params=pltpu.CompilerParams(collective_id=cid, has_side_effects=True, vmem_limit_bytes=58 * 1024 * 1024),
        name="front",
    )(*args)

HD = 64
FF = 6144
NAD = 8
RANK = 16
EPS = 1e-06
HIGH = lax.Precision.HIGHEST
F32 = jnp.float32
BF16 = jnp.bfloat16
BOTH = ("fsdp", "tp")


def matmul(left, right):
    return jnp.dot(left, right, preferred_element_type=F32)


def exact(left, right):
    return jnp.dot(left, right, precision=HIGH, preferred_element_type=F32)


def inner_left(left, right):
    return lax.dot_general(left, right, (((0,), (0,)), ((), ())), preferred_element_type=F32)


def inner_right(left, right):
    return lax.dot_general(
        left, right, (((left.ndim - 1,), (right.ndim - 1,)), ((), ())), preferred_element_type=F32
    )


def layer_norm(values):
    center = values - jnp.mean(values, axis=-1, keepdims=True)
    inverse = lax.rsqrt(jnp.mean(center * center, axis=-1, keepdims=True) + EPS)
    return (center * inverse, inverse)


def norm_back(grad_normed, normed, inverse, scale):
    grad_hat = grad_normed * (1.0 + scale)
    return inverse * (
        grad_hat
        - jnp.mean(grad_hat, axis=-1, keepdims=True)
        - normed * jnp.mean(grad_hat * normed, axis=-1, keepdims=True)
    )


def gelu(value):
    return jax.nn.gelu(value, approximate=True)


def gelu_back(value, grad):
    return jax.vjp(gelu, value)[1](grad)[0]


def shards(
    image_tokens,
    text_tokens,
    conditioning,
    text_lengths,
    adapter_index,
    adapters,
    mod_weight,
    qkv_weight,
    out_weight,
    fc1_weight,
    fc2_weight,
    image_cot,
    text_cot,
):
    n_f, n_z = lax.axis_size("fsdp"), lax.axis_size("tp")
    f, z = lax.axis_index("fsdp"), lax.axis_index("tp")
    core = f % 2
    slots, quarter, width = image_tokens.shape
    txt_local = text_tokens.shape[0]
    txt_group = txt_local * n_z
    img_half = 2 * quarter
    img_n = 2 * img_half
    cols = [6 * width, 3 * width, width, FF, width]
    fans = [width, width, width, width, FF]

    def round_pairs(r):
        pairs = []
        for fa in range(n_f):
            for t in range(n_z):
                there = (fa // 2 * 2 + t // 2) * n_z + 2 * (fa % 2) + (r ^ (t % 2))
                pairs.append((fa * n_z + t, there))
        return pairs

    low_bit = z % 2

    def pick(stack, bit):
        return lax.dynamic_index_in_dim(stack, bit, 0, keepdims=False)

    def flip(r):
        return low_bit if r == 0 else 1 - low_bit

    def to_chip(parts):
        got = [lax.ppermute(parts[r], BOTH, round_pairs(r)) for r in range(2)]
        return jnp.where(low_bit == 0, got[0], got[1]), jnp.where(low_bit == 0, got[1], got[0])

    def from_chip(pieces):
        got = []
        for r in range(2):
            mine = jnp.where(flip(r) == 0, pieces[0], pieces[1])
            got.append(lax.ppermute(mine, BOTH, [(b, a) for a, b in round_pairs(r)]))
        return jnp.where(low_bit == 0, got[0], got[1]), jnp.where(low_bit == 0, got[1], got[0])

    def reshard(values):
        return jnp.concatenate(to_chip([pick(values, flip(r)) for r in range(2)]), axis=0)

    def unshard(values):
        return jnp.stack(from_chip([values[:quarter], values[quarter:]]))

    def swap_core(values):
        return lax.ppermute(values, "fsdp", [(i, i ^ 1) for i in range(n_f)])

    def by_core(mine, other, axis):
        first = jnp.where(core == 0, mine, other)
        second = jnp.where(core == 0, other, mine)
        return jnp.concatenate([first, second], axis=axis)

    def z_swap(values, step):
        return lax.ppermute(values, "tp", [(i, i ^ step) for i in range(n_z)])

    def z_order(pieces):
        stack = jnp.stack(pieces)
        return [pick(stack, z ^ a) for a in range(n_z)]

    def z_gather(values):
        return z_order([values] + [z_swap(values, j) for j in range(1, n_z)])

    def z_exchange(blocks):
        return z_order([pick(blocks, z ^ j) if j == 0 else z_swap(pick(blocks, z ^ j), j) for j in range(n_z)])

    def z_scatter(values):
        count = values.shape[0] // n_z
        mine = lax.dynamic_slice_in_dim(values, z * count, count, 0)
        for j in range(1, n_z):
            part = lax.dynamic_slice_in_dim(values, (z ^ j) * count, count, 0)
            mine = mine + z_swap(part.astype(BF16), j).astype(F32)
        return mine

    def to_heads(values):
        half = values.shape[1] // 2
        low, high = values[:, :half], values[:, half:]
        mine = jnp.where(core == 0, low, high)
        return by_core(mine, swap_core(jnp.where(core == 0, high, low)), 0)

    def to_tokens(values):
        low, high = values[:img_half], values[img_half:]
        mine = jnp.where(core == 0, low, high)
        return by_core(mine, swap_core(jnp.where(core == 0, high, low)), 1)

    out_t = jnp.swapaxes(out_weight, 1, 2)
    fc2_t = jnp.swapaxes(fc2_weight, 1, 2)
    local = [qkv_weight, out_t, fc1_weight, fc2_t]
    adapter_rows = adapters.astype(BF16).reshape(-1, 128)
    txt_pad = (txt_local + 15) // 16 * 16

    def padded(values):
        return jnp.pad(values, ((0, txt_pad - txt_local), (0, 0)))

    x_txt_low, g_txt_low = padded(text_tokens), padded(text_cot)
    x_txt = x_txt_low.astype(F32)

    seg_ends = jnp.cumsum(text_lengths[0])
    slot_ids = jnp.arange(slots)

    def owner_of(position):
        segment = jnp.sum((position[:, None] >= seg_ends[None, :]).astype(jnp.int32), axis=1)
        return (segment[:, None] == slot_ids[None, :]).astype(F32)

    def real(owner):
        place = jnp.arange(owner.shape[0]) % txt_pad
        return jnp.where((place < txt_local)[:, None], owner, 0.0)

    def position(rows):
        return rows // txt_pad * txt_local + rows % txt_pad

    txt_rows = jnp.arange(n_z * txt_pad)
    owner_group = real(owner_of(position(txt_rows)))
    owner_local = real(owner_of(z * txt_local + jnp.arange(txt_pad)))
    txt_mask = jnp.repeat(owner_group, RANK, axis=1)
    txt_mask_local = jnp.repeat(owner_local, RANK, axis=1)
    rank_cols = slots * RANK
    seq_mask = jnp.repeat(jnp.eye(slots, dtype=F32), RANK, axis=1)

    def by_group(mine, other):
        return by_core(mine, other, 0)

    column_picks = by_group(adapter_index, swap_core(adapter_index))
    column_count = 2 * slots
    one_hot = (
        jnp.arange(NAD * RANK)[:, None]
        == (column_picks[:, None] * RANK + jnp.arange(RANK)[None, :]).reshape(1, -1)
    ).astype(F32)
    def stretch(stream, index):
        if stream == 0:
            return img_mod[:, index * width : (index + 1) * width]
        return exact(owner_local, txt_mods[:, index * width : (index + 1) * width])

    def collapse(stream, values):
        if stream == 0:
            return jnp.sum(values, axis=0, keepdims=True)
        return exact(owner_local.T, values)

    def share(values):
        return jnp.concatenate(z_gather(values), axis=0)

    def give(values, rank_part):
        got = z_scatter(jnp.concatenate([values, rank_part], axis=1))
        return got[:, :width], (got[:, width:] * txt_mask_local).astype(BF16)

    def lanes(values):
        count = values.shape[1] // n_z
        return lax.dynamic_slice_in_dim(values, z * count, count, 1)

    def project(values, weight, pair, mask, flipped):
        middle = inner_right(values, pair[0])
        if mask is not None:
            middle = middle * mask
        middle = middle.astype(BF16)
        main = inner_right(values, weight) if flipped else matmul(values, weight)
        return middle, main + matmul(middle, pair[1])

    own_hot = (
        jnp.arange(NAD * RANK)[:, None]
        == (adapter_index[:, None] * RANK + jnp.arange(RANK)[None, :]).reshape(1, -1)
    ).astype(F32)
    k_local = mod_weight.shape[1]
    cond_act = jax.nn.silu(conditioning).astype(BF16)
    thick = 128

    def thicker(part):
        return jnp.concatenate([part, jnp.zeros((thick - part.shape[0], part.shape[1]), part.dtype)], axis=0)

    def sign(owner):
        return owner[:, 0:1] - owner[:, 1:2]

    def lanes_pad(mask):
        return jnp.pad(mask, ((0, 0), (0, thick - mask.shape[1])))

    if n_f == 8:
        slot_mask = jnp.pad(jnp.concatenate([seq_mask, seq_mask]), ((0, 4), (0, 0)))
        made = front(
            [w[0] for w in local], [w[1] for w in local], adapter_rows, image_tokens, image_cot,
            adapter_index, own_hot.T.astype(BF16), cond_act.astype(F32), mod_weight, x_txt_low,
            sign(owner_local), lanes_pad(txt_mask), slot_mask, n_f, n_z, fans, cols, 1,
        )
        made = iter(made)
        take = lambda count: [next(made) for _ in range(count)]
        img_w = [w.reshape(-1, w.shape[-1]) for w in take(4)]
        txt_w = [w.reshape(-1, w.shape[-1]) for w in take(4)]
        x_img, g_img = [v.reshape(-1, width) for v in take(2)]
        img_rows_mod, txt_mod = take(2)
        img_pairs = [None] + list(zip(take(4), take(4)))
        thick_pairs = [None] + list(zip(take(4), take(4)))
        mod_a, mod_b, tmod, cond_own = take(4)
        img_in, img_qkv_mid, img_heads, txt_in, txt_qkv_mid, txt_heads = take(6)
        img_heads = img_heads.reshape(img_n, -1)
        txt_in = txt_in.reshape(-1, width)
        txt_qkv_mid = txt_qkv_mid[:, :rank_cols]
        txt_pairs = [None, tuple(part[:rank_cols] for part in thick_pairs[1])]
        img_mod = img_rows_mod[:6].reshape(1, -1)
        txt_mods = txt_mod.reshape(slots, 8, width)[:, :6].reshape(slots, -1)
    else:
        got = gather([w[0] for w in local], [w[1] for w in local] + [adapter_rows], n_f, n_z)
        got = [g.reshape(-1, g.shape[-1]) for g in got]
        img_w, txt_w, row = got[:4], got[4:8], got[8]
        x_img = reshard(image_tokens)
        g_img = reshard(image_cot)
        own_picks = adapter_index

        a_rows = [[None] * 5 for stream in range(2)]
        b_rows = [[None] * 5 for stream in range(2)]
        offset = 0
        for stream in range(2):
            for index in range(5):
                count = fans[index] // n_z
                a_rows[stream][index] = row[offset : offset + count]
                offset += count
                count = cols[index] // n_z
                b_rows[stream][index] = row[offset : offset + count]
                offset += count

        def b_pick(stream, index, pick_index):
            part = b_rows[stream][index]
            count = part.shape[0] // NAD
            return lax.dynamic_slice_in_dim(part, pick_index * count, count, 0).reshape(RANK, -1)

        def a_pick(rows, hot):
            return inner_right(hot.T.astype(BF16), rows).astype(BF16)

        img_a = a_pick(jnp.concatenate(a_rows[0], axis=0), one_hot)
        fan_share = sum(fans) // n_z
        img_a = img_a.reshape(column_count, RANK, fan_share)
        img_b = [
            jnp.concatenate([b_pick(0, index, column_picks[s]) for index in range(1, 5)], axis=1)
            for s in range(column_count)
        ]
        img_msg = jnp.concatenate([img_a, jnp.stack(img_b)], axis=2)
        txt_a_rows = jnp.concatenate(
            [a_rows[0][0], a_rows[1][0], a_rows[1][1], a_rows[1][3]], axis=0
        )
        txt_a = a_pick(txt_a_rows, own_hot).reshape(slots, RANK, -1)
        txt_b_own = [
            [b_pick(stream, index, own_picks[s]) for s in range(slots)]
            for stream, index in [(0, 0), (1, 0), (1, 1), (1, 2), (1, 3), (1, 4)]
        ]
        txt_b_own = [jnp.concatenate(parts, axis=0) for parts in txt_b_own]
        txt_a_own = a_pick(jnp.concatenate([a_rows[1][2], a_rows[1][4]], axis=0), own_hot)
        txt_msg = jnp.concatenate(
            [txt_a.reshape(slots * RANK, -1), txt_b_own[3], txt_b_own[5]], axis=1
        )
        img_got = jnp.stack(z_exchange(img_msg))
        txt_got = jnp.stack(z_gather(txt_msg))

        def join(part):
            return jnp.swapaxes(part, 0, 1).reshape(part.shape[1], -1)

        img_pairs = []
        offset, b_offset = 0, fan_share
        for index in range(5):
            count = fans[index] // n_z
            a_full = join(img_got[:, :, offset : offset + count])
            offset += count
            if index == 0:
                img_pairs.append(None)
                continue
            count = cols[index] // n_z
            b_full = join(img_got[:, :, b_offset : b_offset + count])
            b_offset += count
            img_pairs.append((a_full, b_full))
        txt_full = []
        offset = 0
        for count in [width // n_z] * 6:
            txt_full.append(join(txt_got[:, :, offset : offset + count]))
            offset += count
        mod_a = [txt_full[0], txt_full[1]]
        mod_b = [txt_b_own[0], txt_b_own[1]]
        txt_pairs = [
            None,
            (txt_full[2], txt_b_own[2]),
            (txt_a_own[:, : width // n_z], txt_full[4]),
            (txt_full[3], txt_b_own[4]),
            (txt_a_own[:, width // n_z :], txt_full[5]),
        ]

        cond_all = lax.all_gather(cond_act, "fsdp", axis=0, tiled=True)
        cond_slice = lax.dynamic_slice_in_dim(cond_all, f * k_local, k_local, 1)
        mod_part = jnp.stack([matmul(cond_slice, mod_weight[stream]) for stream in range(2)], axis=1)
        mod_part = lax.psum_scatter(mod_part, "fsdp", scatter_dimension=0, tiled=True)
        mod_mid = []
        mod_terms = []
        for stream in range(2):
            middle = (inner_right(cond_act, mod_a[stream]) * seq_mask).astype(BF16)
            mod_mid.append(middle)
            mod_terms.append(mod_part[:, stream] + matmul(middle, mod_b[stream]))
        mods = jnp.concatenate(z_gather(jnp.stack(mod_terms, axis=1)), axis=2)
        img_mods = by_group(mods[:, 0], swap_core(mods[:, 0]))
        img_mod = lax.dynamic_slice_in_dim(img_mods, z, 1, 0)
        txt_mods = mods[:, 1]

        img_rows_mod = jnp.concatenate([img_mod.reshape(6, width), jnp.zeros((2, width), F32)], axis=0)
        txt_mod = jnp.pad(txt_mods.reshape(slots, 6, width), ((0, 0), (0, 2), (0, 0))).reshape(-1, width)
        thick_pairs = [None] + [tuple(thicker(part) for part in txt_pairs[index]) for index in range(1, 5)]
        norm_first = [layer_norm(v.astype(F32)) for v in (x_img, x_txt)]
        heads_in = [
            (norm_first[s][0] * (1.0 + stretch(s, 1)) + stretch(s, 0)).astype(BF16) for s in range(2)
        ]

        txt_in = share(heads_in[1])
        txt_qkv_mid, txt_qkv = project(txt_in, txt_w[0], txt_pairs[1], txt_mask, False)
        img_qkv_mid, img_qkv = project(heads_in[0], img_w[0], img_pairs[1], None, False)
        txt_qkv, img_qkv = txt_qkv.astype(BF16), img_qkv.astype(BF16)
        img_heads = to_heads(img_qkv)
        txt_heads = jnp.stack(to_chip([txt_qkv, txt_qkv]))
        img_in = heads_in[0]

    inputs = [x_img.astype(F32), x_txt]
    norm_one = [layer_norm(values) for values in inputs]
    lengths = by_group(text_lengths[0:1], swap_core(text_lengths[0:1]))
    chip_lengths = jnp.cumsum(lax.dynamic_index_in_dim(lengths, z // slots, 0, keepdims=False))
    chip_slot = z % slots
    chip_segment = jnp.sum(
        (position(txt_rows)[:, None] >= chip_lengths[None, :]).astype(jnp.int32),
        axis=1,
        keepdims=True,
    )
    chip_owner = (chip_segment == chip_slot) & (txt_rows % txt_pad < txt_local)[:, None]
    bias = jnp.where(chip_owner, 0.0, -1e30).astype(F32)
    o_img, o_txt, lse = attend(img_heads, txt_heads, bias, HD)

    def txt_home(values):
        got = from_chip([values[0], values[1]])
        return jnp.where(owner_group[:, 0:1] > 0, got[0], jnp.where(owner_group[:, 1:2] > 0, got[1], 0))

    attended = to_tokens(o_img)
    (txt_result, txt_grad_after, do_txt, txt_sums, *txt_sides) = text_mid(
        o_txt, x_txt_low, g_txt_low, txt_mod, sign(owner_group), sign(owner_local), lanes_pad(txt_mask),
        lanes_pad(txt_mask_local), txt_w[1], txt_w[2], txt_w[3], thick_pairs[2], thick_pairs[3], thick_pairs[4],
        n_z, 2,
    )
    txt_sides = [part[:rank_cols] for part in txt_sides]
    txt_sums = txt_sums.reshape(4, slots, width)

    (img_branch, img_after, img_mlp, img_pre, img_result, *img_mids, img_gate) = block_fwd(
        attended, x_img, g_img, img_rows_mod, img_w[1], img_pairs[2], img_pairs[3], img_w[2],
        img_pairs[4], img_w[3],
    )
    image_out = unshard(img_result)

    grads = [[None] * 5 for stream in range(2)]

    def project_back(grad, weight, pair, mask, flipped):
        middle = inner_right(grad, pair[1])
        if mask is not None:
            middle = middle * mask
        middle = middle.astype(BF16)
        main = matmul(grad, weight) if flipped else inner_right(grad, weight)
        return middle, main + matmul(middle, pair[0])

    (img_grad_after, img_grad_att, img_sums, *sides) = block_back(
        g_img, img_after, img_branch, img_mlp, attended, img_rows_mod, img_pre, img_w[3],
        img_pairs[4], img_w[2], img_pairs[3], img_w[1], img_pairs[2], img_mids,
    )
    grads[0][4] = (sides[0], sides[3])
    grads[0][3] = (sides[2], sides[1])
    grads[0][2] = (sides[4], sides[5])
    mod_parts = [[None] * 6 for stream in range(2)]
    for place in range(4):
        mod_parts[1][2 + place] = txt_sums[place]
    grads[1][2] = (txt_sides[0], txt_sides[1])
    grads[1][3] = (txt_sides[2], txt_sides[3])
    grads[1][4] = (txt_sides[4], txt_sides[5])
    img_sums = jnp.sum(jnp.concatenate([img_sums, img_gate]).reshape(4, 8, width), axis=1)
    for place in range(4):
        mod_parts[0][2 + place] = img_sums[place : place + 1]
    grad_after = [img_grad_after, txt_grad_after]

    do_img = to_heads(img_grad_att)
    d_img, d_txt = attend_back(img_heads, txt_heads, bias, do_img, do_txt, lse, HD)
    img_grad_qkv = to_tokens(d_img)
    txt_grad_qkv = txt_home(d_txt)

    img_back_mid, img_grad_norm = project_back(img_grad_qkv, img_w[0], img_pairs[1], None, False)
    grads[0][1] = (inner_left(img_back_mid, img_in), inner_left(img_qkv_mid, img_grad_qkv))
    txt_grad_norm, txt_qkv_back = give(
        inner_right(txt_grad_qkv, txt_w[0]), inner_right(txt_grad_qkv, txt_pairs[1][1])
    )
    txt_grad_norm = txt_grad_norm + matmul(txt_qkv_back, txt_pairs[1][0])
    grads[1][1] = (
        inner_left(share(txt_qkv_back), lanes(txt_in)),
        inner_left(txt_qkv_mid, txt_grad_qkv),
    )
    grad_norm = [img_grad_norm, txt_grad_norm]
    grad_inputs = []
    for s in range(2):
        grad_inputs.append(
            grad_after[s]
            + norm_back(grad_norm[s], norm_one[s][0], norm_one[s][1], stretch(s, 1))
        )
        mod_parts[s][0] = collapse(s, grad_norm[s])
        mod_parts[s][1] = collapse(s, grad_norm[s] * norm_one[s][0])
    img_dmod = jnp.concatenate(mod_parts[0], axis=1)
    txt_dmod = jnp.concatenate(mod_parts[1], axis=1)
    if n_f == 8:
        cut = width // n_z
        dmod = jnp.concatenate([img_dmod, txt_dmod]).reshape(1 + slots, n_z, -1, cut)
        dmod = jnp.pad(jnp.swapaxes(dmod, 0, 1), ((0, 0), (0, 0), (0, 8 - dmod.shape[2]), (0, 0)))
        sides_of = lambda stream, side: [grads[stream][index][side] for index in range(1, 5)]
        image_low, cond_slices, mod_rank, shard = tail(
            grad_inputs[0].astype(BF16).reshape(2, quarter, width),
            sides_of(0, 0), sides_of(0, 1), sides_of(1, 0), sides_of(1, 1),
            one_hot.T.astype(BF16), own_hot.T.astype(BF16), dmod, mod_weight, mod_b, tmod, cond_own,
            slot_mask,
            n_f, n_z, fans, cols, 3,
        )
        image_grad = image_low.astype(F32)
        cond_rows = jnp.swapaxes(cond_slices[:, :slots, :k_local], 0, 1).reshape(slots, width)
        for s in range(2):
            cond_rows = cond_rows + matmul(mod_rank[2 * s : 2 * s + 2].astype(BF16), mod_a[s])
        cond_grad = jax.vjp(jax.nn.silu, conditioning)[1](cond_rows)[0]
        adapter_grad = shard.reshape(1, -1)
        return (
            image_out, txt_result[:txt_local], image_grad, grad_inputs[1][:txt_local], cond_grad, adapter_grad
        )
    image_grad = unshard(grad_inputs[0].astype(BF16)).astype(F32)

    img_dmod = (img_dmod + swap_core(img_dmod)).astype(BF16)
    def lane_blocks(values):
        return jnp.swapaxes(values.reshape(values.shape[0], n_z, -1), 0, 1)

    img_dmods = jnp.concatenate(z_exchange(lane_blocks(img_dmod)), axis=0)
    img_dmods = lax.dynamic_slice_in_dim(img_dmods, core * slots, slots, 0)
    txt_dmods = sum(z_exchange(lane_blocks(txt_dmod))).astype(BF16)
    dmods = jnp.stack([img_dmods, txt_dmods], axis=1)
    dmods_all = lax.all_gather(dmods, "fsdp", axis=0, tiled=True)
    cond_part = sum(inner_right(dmods_all[:, s], mod_weight[s]) for s in range(2))
    mod_back = [inner_right(dmods[:, s], mod_b[s]) for s in range(2)]
    cond_part = cond_part.reshape(-1, width // n_f)
    joined = jnp.concatenate([cond_part.reshape(-1), jnp.stack(mod_back).reshape(-1)])
    joined = sum(z_gather(joined))
    cond_slices = joined[: cond_part.size].reshape(n_f, -1, width // n_f)
    mod_rank = joined[cond_part.size :].reshape(2, slots, -1)
    cond_rows = lax.all_to_all(cond_slices, "fsdp", 0, 2, tiled=True)[0]
    for s in range(2):
        back_mid = (mod_rank[s] * seq_mask).astype(BF16)
        cond_rows = cond_rows + matmul(back_mid, mod_a[s])
        grads[s][0] = (inner_left(back_mid, lanes(cond_act)), inner_left(mod_mid[s], dmods[:, s]))
    cond_grad = jax.vjp(jax.nn.silu, conditioning)[1](cond_rows)[0]

    def spread(values):
        return jnp.swapaxes(values.reshape(RANK, n_z, -1), 0, 1)

    img_rows = {}
    for group in ((2, 3, 4), (1,)):
        parts = [spread(grads[0][index][side]) for side in range(2) for index in group]
        parts = jnp.concatenate(z_exchange(jnp.concatenate(parts, axis=2)), axis=0)
        offset = 0
        for side, sizes in enumerate((fans, cols)):
            for index in group:
                count = sizes[index] // n_z
                img_rows[side, index] = parts[:, offset : offset + count]
                offset += count
    flat = []
    for stream in range(2):
        for index in range(5):
            if stream == 0 and index > 0:
                part_a, part_b = img_rows[0, index], img_rows[1, index]
                hot = one_hot
            else:
                part_a, part_b = grads[stream][index]
                hot = own_hot
            flat.append(
                lax.dot_general(
                    part_a, hot, (((0,), (1,)), ((), ())),
                    precision=HIGH, preferred_element_type=F32,
                )
            )
            flat.append(exact(hot, part_b).reshape(-1, 128))
    total = jnp.concatenate(flat, axis=0).reshape(n_f, -1, 128)
    step = 1
    while step < n_f:
        bit = (f // step) % 2
        pairs = total.reshape((-1, 2) + total.shape[1:])
        keep = lax.dynamic_index_in_dim(pairs, bit, 1, keepdims=False)
        send = lax.dynamic_index_in_dim(pairs, 1 - bit, 1, keepdims=False)
        sent = lax.ppermute(send.astype(BF16), "fsdp", [(i, i ^ step) for i in range(n_f)])
        total = keep + sent.astype(F32)
        step *= 2
    adapter_grad = total.reshape(1, -1)
    return (
        image_out, txt_result[:txt_local], image_grad, grad_inputs[1][:txt_local], cond_grad, adapter_grad
    )


def solution(mesh):
    return jax.shard_map(
        shards,
        mesh=mesh,
        in_specs=(
            P("fsdp", "tp", None),
            P(("fsdp", "tp"), None),
            P("fsdp", None),
            P("fsdp", None),
            P("fsdp"),
            P("tp", "fsdp"),
            P(None, "fsdp", "tp"),
            P(None, "fsdp", "tp"),
            P(None, "tp", "fsdp"),
            P(None, "fsdp", "tp"),
            P(None, "tp", "fsdp"),
            P("fsdp", "tp", None),
            P(("fsdp", "tp"), None),
        ),
        out_specs=(
            P("fsdp", "tp", None),
            P(("fsdp", "tp"), None),
            P("fsdp", "tp", None),
            P(("fsdp", "tp"), None),
            P("fsdp", None),
            P("tp", "fsdp"),
        ),
        check_vma=False,
    )
```

```python
import functools

import jax
import jax.numpy as jnp
from jax import lax
from jax.experimental import pallas as pl
from jax.experimental.pallas import tpu as pltpu
from jax.sharding import PartitionSpec as P

MESH = pl.DeviceIdType.MESH

def bits_of(count):
    return max(count.bit_length() - 1, 0)

def halves(width):
    tiles = width // 128
    first = (tiles + 1) // 2 * 128
    return [(0, first), (first, width - first)]

def gather_kernel(n_f, n_z, full_count, part_count, *refs):
    total = full_count + part_count
    ins, outs = refs[:total], refs[total:2 * total]
    z_send, z_recv, xy_send, xy_recv, core_send, core_recv, own_sem = refs[2 * total:]
    f = lax.axis_index("fsdp")
    z = lax.axis_index("tp")
    chip, core = f // 2, f % 2
    chips = n_f // 2
    nbits = bits_of(chips)
    partner = chip * 2 + (1 - core)

    def peer_of(mask):
        other = 0
        for bit in range(nbits):
            have = (chip // (1 << bit)) % 2
            want = 1 - have if (mask >> bit) & 1 else have
            other = other + want * (1 << bit)
        return other * 2 + core

    barrier = pltpu.get_barrier_semaphore()
    for bit in range(nbits):
        pl.semaphore_signal(barrier, inc=1, device_id=(peer_of(1 << bit), z), device_id_type=MESH)
    pl.semaphore_signal(barrier, inc=1, device_id=(partner, z), device_id_type=MESH)
    @pl.when(z > 0)
    def _():
        pl.semaphore_signal(barrier, inc=1, device_id=(f, z - 1), device_id_type=MESH)
    @pl.when(z < n_z - 1)
    def _():
        pl.semaphore_signal(barrier, inc=1, device_id=(f, z + 1), device_id_type=MESH)
    peers = nbits + 1 + (z > 0).astype(jnp.int32) + (z < n_z - 1).astype(jnp.int32)
    pl.semaphore_wait(barrier, peers)

    def width(m):
        return ins[m].shape[-1]

    def place(m, who, zz, off=0, w=None):
        w = width(m) if w is None else w
        if m < full_count:
            return outs[m].at[who, :, pl.ds(pl.multiple_of(zz * width(m) + off, 128), w)]
        if w == width(m):
            return outs[m].at[who]
        return outs[m].at[who, :, pl.ds(off, w)]

    def piece(m, off, w):
        return ins[m] if w == width(m) else ins[m].at[:, pl.ds(off, w)]

    def remote(src, dst, ssem, rsem, dev):
        return pltpu.make_async_remote_copy(src_ref=src, dst_ref=dst, send_sem=ssem, recv_sem=rsem, device_id=dev, device_id_type=MESH)

    def order_of(half):
        order = list(range(nbits))
        return order if half == 0 else order[::-1]

    def cuts(m):
        if width(m) >= 256:
            return list(enumerate(halves(width(m))))
        return [(m % 2, (0, width(m)))]

    def slot(m, zz):
        return zz if m < full_count else 0

    def xy_copy(m, zz, half, cut, mask, bit, own_piece=False):
        off, w = cut
        who = peer_of(mask)
        source = piece(m, off, w) if own_piece and mask == 0 else place(m, who, zz, off, w)
        return remote(source, place(m, who, zz, off, w),
                      xy_send.at[m, slot(m, zz), half, mask, bit], xy_recv.at[m, slot(m, zz), half, mask | (1 << bit)],
                      (peer_of(1 << bit), z))

    def xy_wait(m, zz, half, cut, mask):
        off, w = cut
        who = peer_of(mask)
        remote(place(m, who, zz, off, w), place(m, who, zz, off, w), xy_send.at[m, slot(m, zz), half, 0, 0],
               xy_recv.at[m, slot(m, zz), half, mask], (partner, z)).wait_recv()

    def core_copy(m, zz, half, cut, mask, own_piece=False):
        off, w = cut
        who = peer_of(mask)
        source = piece(m, off, w) if own_piece and mask == 0 else place(m, who, zz, off, w)
        return remote(source, place(m, who, zz, off, w),
                      core_send.at[m, slot(m, zz), half, mask], core_recv.at[m, slot(m, zz), half, mask], (partner, z))

    def core_wait_recv(m, zz, half, cut, mask):
        off, w = cut
        who = peer_of(mask) - core + (1 - core)
        remote(place(m, who, zz, off, w), place(m, who, zz, off, w),
               core_send.at[m, slot(m, zz), half, mask], core_recv.at[m, slot(m, zz), half, mask], (partner, z)).wait_recv()

    def own(m):
        return pltpu.make_async_copy(ins[m], place(m, f, z), own_sem.at[m])

    def z_copy(m, zz, up, own_piece=False):
        return remote(ins[m] if own_piece else place(m, f, zz), place(m, f, zz), z_send.at[m, zz, up], z_recv.at[m, zz], (f, z + 1 if up else z - 1))

    def launch(m, zz, own_piece=False):
        for half, cut in cuts(m):
            for bit in order_of(half):
                xy_copy(m, zz, half, cut, 0, bit, own_piece).start()
            core_copy(m, zz, half, cut, 0, own_piece).start()

    def masks_in_order(half):
        order = order_of(half)
        def rank(mask):
            return [1 if (mask >> b) & 1 else 0 for b in reversed(order)]
        return sorted(range(1, 1 << nbits), key=rank)

    def forward(m, zz):
        for half, cut in cuts(m):
            order = order_of(half)
            for mask in masks_in_order(half):
                last = max(i for i, b in enumerate(order) if (mask >> b) & 1)
                if last == nbits - 1:
                    continue
                xy_wait(m, zz, half, cut, mask)
                for b in order[last + 1:]:
                    xy_copy(m, zz, half, cut, mask, b).start()
                core_copy(m, zz, half, cut, mask).start()

    def finish(m, zz):
        for half, cut in cuts(m):
            order = order_of(half)
            for mask in masks_in_order(half):
                last = max(i for i, b in enumerate(order) if (mask >> b) & 1)
                if last == nbits - 1:
                    xy_wait(m, zz, half, cut, mask)
                    core_copy(m, zz, half, cut, mask).start()

    def drain(m, zz):
        for half, cut in cuts(m):
            order = order_of(half)
            for mask in [0] + masks_in_order(half):
                last = max([i for i, b in enumerate(order) if (mask >> b) & 1], default=-1)
                for b in order[last + 1:]:
                    xy_copy(m, zz, half, cut, mask, b).wait_send()
                core_copy(m, zz, half, cut, mask).wait_send()
                core_wait_recv(m, zz, half, cut, mask)

    for m in range(total):
        own(m).start()
    for m in range(total):
        if m < full_count:
            @pl.when(z < n_z - 1)
            def _():
                z_copy(m, z, 1, True).start()
            @pl.when(z > 0)
            def _():
                z_copy(m, z, 0, True).start()
        launch(m, z, True)
    for m in range(full_count, total):
        forward(m, z)
    for k in range(1, n_z):
        for m in range(full_count):
            @pl.when(z - k >= 0)
            def _():
                zz = z - k
                z_copy(m, zz, 1).wait_recv()
                @pl.when(z < n_z - 1)
                def _():
                    z_copy(m, zz, 1).start()
                launch(m, zz)
            @pl.when(z + k < n_z)
            def _():
                zz = z + k
                z_copy(m, zz, 0).wait_recv()
                @pl.when(z > 0)
                def _():
                    z_copy(m, zz, 0).start()
                launch(m, zz)
            for sign in ((-1, 1) if k > 1 else (1,)):
                zz = z + sign * (k - 1)
                @pl.when((zz >= 0) & (zz < n_z))
                def _():
                    forward(m, zz)
    for m in range(full_count):
        for sign in (-1, 1):
            zz = z + sign * (n_z - 1)
            @pl.when((zz >= 0) & (zz < n_z))
            def _():
                forward(m, zz)
    for m in range(total):
        if m < full_count:
            def body(zz, _):
                finish(m, zz)
                return 0
            lax.fori_loop(0, n_z, body, 0)
        else:
            finish(m, z)
    for m in range(total):
        own(m).wait()
        if m < full_count:
            def body(zz, _):
                drain(m, zz)
                @pl.when((zz <= z) & (z < n_z - 1))
                def _():
                    z_copy(m, zz, 1).wait_send()
                @pl.when((zz >= z) & (z > 0))
                def _():
                    z_copy(m, zz, 0).wait_send()
                return 0
            lax.fori_loop(0, n_z, body, 0)
        else:
            drain(m, z)

def gather(full, part, n_f, n_z, cid=1):
    arrays = list(full) + list(part)
    total = len(arrays)
    if n_f > 8:
        rows = [lax.all_gather(a, "fsdp", axis=0, tiled=True) for a in arrays]
        return [
            lax.all_gather(a, "tp", axis=1, tiled=True) if i < len(full) else a
            for i, a in enumerate(rows)
        ]
    chips = n_f // 2
    nbits = bits_of(chips)
    shapes = [jax.ShapeDtypeStruct((n_f,) + a.shape[:-1] + (a.shape[-1] * (n_z if i < len(full) else 1),), a.dtype) for i, a in enumerate(arrays)]
    dma = pltpu.SemaphoreType.DMA
    return pl.pallas_call(
        functools.partial(gather_kernel, n_f, n_z, len(full), len(part)),
        out_shape=shapes,
        in_specs=[pl.BlockSpec(memory_space=pl.ANY)] * total,
        out_specs=[pl.BlockSpec(memory_space=pl.ANY)] * total,
        scratch_shapes=[
            dma((total, n_z, 2)), dma((total, n_z)),
            dma((total, n_z, 2, chips, max(nbits, 1))), dma((total, n_z, 2, chips)),
            dma((total, n_z, 2, chips)), dma((total, n_z, 2, chips)), dma((total,)),
        ],
        compiler_params=pltpu.CompilerParams(collective_id=cid, has_side_effects=True),
        name="weight_gather",
    )(*arrays)

def dots(left, right, lc, rc):
    return lax.dot_general(left, right, (((lc,), (rc,)), ((), ())), preferred_element_type=jnp.float32)

def attend_kernel(hd, bq, img_ref, txt_ref, bias_ref, oi_ref, ot_ref, lse_ref):
    img_n, txt_n = img_ref.shape[0], txt_ref.shape[1]
    heads = img_ref.shape[1] // (3 * hd)
    bias = bias_ref[...]
    for h in range(heads):
        base = 3 * hd * h
        ki = img_ref[:, base + hd:base + 2 * hd]
        vi = img_ref[:, base + 2 * hd:base + 3 * hd]
        kt = txt_ref[0, :, base + hd:base + 2 * hd]
        vt = txt_ref[0, :, base + 2 * hd:base + 3 * hd]

        def block(q):
            q = q * jnp.bfloat16(0.125)
            si = dots(ki, q, 1, 1)
            st = dots(kt, q, 1, 1) + bias
            top = jnp.maximum(jnp.max(si, axis=0, keepdims=True), jnp.max(st, axis=0, keepdims=True))
            ei = jnp.exp(si - top)
            et = jnp.exp(st - top)
            total = jnp.sum(ei, axis=0, keepdims=True) + jnp.sum(et, axis=0, keepdims=True)
            o = dots(vi, ei.astype(jnp.bfloat16), 0, 0) + dots(vt, et.astype(jnp.bfloat16), 0, 0)
            return (o / total).T.astype(jnp.bfloat16), top + jnp.log(total)

        for i in range(img_n // bq):
            o, lse = block(img_ref[i * bq:(i + 1) * bq, base:base + hd])
            oi_ref[i * bq:(i + 1) * bq, h * hd:(h + 1) * hd] = o
            lse_ref[0, h:h + 1, i * bq:(i + 1) * bq] = lse
        o, lse = block(txt_ref[0, :, base:base + hd])
        ot_ref[0, :, h * hd:(h + 1) * hd] = o
        lse_ref[0, h:h + 1, img_n:img_n + txt_n] = lse

def attend(img, txt, bias, hd, bq=512):
    img_n, cols = img.shape
    parts, txt_n, _ = txt.shape
    pairs = cols // (6 * hd)
    per = pairs // parts
    return pl.pallas_call(
        functools.partial(attend_kernel, hd, bq),
        grid=(pairs,),
        in_specs=[
            pl.BlockSpec((img_n, 6 * hd), lambda i: (0, i)),
            pl.BlockSpec((1, txt_n, 6 * hd), lambda i: (i // per, 0, i % per)),
            pl.BlockSpec((txt_n, 1), lambda i: (0, 0)),
        ],
        out_specs=[
            pl.BlockSpec((img_n, 2 * hd), lambda i: (0, i)),
            pl.BlockSpec((1, txt_n, 2 * hd), lambda i: (i // per, 0, i % per)),
            pl.BlockSpec((1, 2, img_n + txt_n), lambda i: (i, 0, 0)),
        ],
        out_shape=[
            jax.ShapeDtypeStruct((img_n, pairs * 2 * hd), jnp.bfloat16),
            jax.ShapeDtypeStruct((parts, txt_n, per * 2 * hd), jnp.bfloat16),
            jax.ShapeDtypeStruct((pairs, 2, img_n + txt_n), jnp.float32),
        ],
        compiler_params=pltpu.CompilerParams(vmem_limit_bytes=48 * 1024 * 1024),
        name="attend",
    )(img, txt, bias)

def attend_back_kernel(hd, bq, img_ref, txt_ref, bias_ref, doi_ref, dot_ref, lse_ref, di_ref, dt_ref, acc_i, acc_t):
    img_n, txt_n = img_ref.shape[0], txt_ref.shape[1]
    heads = img_ref.shape[1] // (3 * hd)
    bias = bias_ref[...]
    for h in range(heads):
        base = 3 * hd * h
        ki = img_ref[:, base + hd:base + 2 * hd]
        vi = img_ref[:, base + 2 * hd:base + 3 * hd]
        kt = txt_ref[0, :, base + hd:base + 2 * hd]
        vt = txt_ref[0, :, base + 2 * hd:base + 3 * hd]

        def block(q, do, lse, first):
            q = q * jnp.bfloat16(0.125)
            pi = jnp.exp(dots(ki, q, 1, 1) - lse)
            pt = jnp.exp(dots(kt, q, 1, 1) + bias - lse)
            dwi = dots(vi, do, 1, 1)
            dwt = dots(vt, do, 1, 1)
            delta = jnp.sum(pi * dwi, axis=0, keepdims=True) + jnp.sum(pt * dwt, axis=0, keepdims=True)
            dsi = (pi * (dwi - delta)).astype(jnp.bfloat16)
            dst = (pt * (dwt - delta)).astype(jnp.bfloat16)
            dvi = dots(pi.astype(jnp.bfloat16), do, 1, 0)
            dvt = dots(pt.astype(jnp.bfloat16), do, 1, 0)
            dki = dots(dsi, q, 1, 0)
            dkt = dots(dst, q, 1, 0)
            if first:
                acc_i[0], acc_i[1], acc_t[0], acc_t[1] = dki, dvi, dkt, dvt
            else:
                acc_i[0] += dki
                acc_i[1] += dvi
                acc_t[0] += dkt
                acc_t[1] += dvt
            dq = dots(ki, dsi, 0, 0) + dots(kt, dst, 0, 0)
            return (dq.T * 0.125).astype(jnp.bfloat16)

        for i in range(img_n // bq):
            rows = slice(i * bq, (i + 1) * bq)
            di_ref[rows, base:base + hd] = block(
                img_ref[rows, base:base + hd], doi_ref[rows, h * hd:(h + 1) * hd], lse_ref[0, h:h + 1, rows], i == 0)
        grad = jnp.where(bias < 0, 0.0, dot_ref[0, :, h * hd:(h + 1) * hd].astype(jnp.float32)).astype(jnp.bfloat16)
        dt_ref[0, :, base:base + hd] = block(
            txt_ref[0, :, base:base + hd], grad, lse_ref[0, h:h + 1, img_n:img_n + txt_n], False)
        di_ref[:, base + hd:base + 2 * hd] = acc_i[0].astype(jnp.bfloat16)
        di_ref[:, base + 2 * hd:base + 3 * hd] = acc_i[1].astype(jnp.bfloat16)
        dt_ref[0, :, base + hd:base + 2 * hd] = acc_t[0].astype(jnp.bfloat16)
        dt_ref[0, :, base + 2 * hd:base + 3 * hd] = acc_t[1].astype(jnp.bfloat16)

def attend_back(img, txt, bias, doi, dot, lse, hd, bq=512):
    img_n, cols = img.shape
    parts, txt_n, _ = txt.shape
    pairs = cols // (6 * hd)
    per = pairs // parts
    wide = pl.BlockSpec((img_n, 6 * hd), lambda i: (0, i))
    wide_t = pl.BlockSpec((1, txt_n, 6 * hd), lambda i: (i // per, 0, i % per))
    return pl.pallas_call(
        functools.partial(attend_back_kernel, hd, bq),
        grid=(pairs,),
        in_specs=[
            wide, wide_t,
            pl.BlockSpec((txt_n, 1), lambda i: (0, 0)),
            pl.BlockSpec((img_n, 2 * hd), lambda i: (0, i)),
            pl.BlockSpec((1, txt_n, 2 * hd), lambda i: (i // per, 0, i % per)),
            pl.BlockSpec((1, 2, img_n + txt_n), lambda i: (i, 0, 0)),
        ],
        out_specs=[wide, wide_t],
        out_shape=[jax.ShapeDtypeStruct(img.shape, jnp.bfloat16), jax.ShapeDtypeStruct(txt.shape, jnp.bfloat16)],
        scratch_shapes=[pltpu.VMEM((2, img_n, hd), jnp.float32), pltpu.VMEM((2, txt_n, hd), jnp.float32)],
        compiler_params=pltpu.CompilerParams(vmem_limit_bytes=48 * 1024 * 1024),
        name="attend_back",
    )(img, txt, bias, doi, dot, lse)

ROWS = 64


def mm(left, right):
    return dots(left, right, 1, 0)


def mm_t(left, right):
    return dots(left, right, 1, 1)


def t_mm(left, right):
    return dots(left, right, 0, 0)


def gelu_parts(u):
    scale = 0.7978845608028654
    square = u * u
    tanh = jnp.tanh(scale * (u + 0.044715 * u * square))
    half = 0.5 * (1.0 + tanh)
    slope = half + 0.5 * u * (1.0 - tanh * tanh) * (scale * (1.0 + 3 * 0.044715 * square))
    return u * half, slope


def norm_rows(v):
    center = v - jnp.mean(v, axis=-1, keepdims=True)
    inverse = lax.rsqrt(jnp.mean(center * center, axis=-1, keepdims=True) + 1e-06)
    return center * inverse, inverse


def column_peers(n_z):
    f, z = lax.axis_index("fsdp"), lax.axis_index("tp")
    core = f % 2
    base = f - core
    peers = [(f, (z + j) % n_z) for j in range(1, n_z)]
    peers += [(base + 1 - core, (z + j) % n_z) for j in range(n_z)]
    return f, z, core, base, peers


def meet(peers):
    barrier = pltpu.get_barrier_semaphore()
    for peer in peers:
        pl.semaphore_signal(barrier, inc=1, device_id=peer, device_id_type=MESH)
    pl.semaphore_wait(barrier, len(peers))


def push(src, dst, send, recv, peer):
    return pltpu.make_async_remote_copy(
        src_ref=src, dst_ref=dst, send_sem=send, recv_sem=recv, device_id=peer, device_id_type=MESH)


class ZRing:
    def __init__(self, f, z, n_z):
        self.f, self.z, self.n_z = f, z, n_z

    def start(self, source_of, buf, send, recv):
        for j in range(1, self.n_z):
            to = (self.z + j) % self.n_z
            push(source_of(to), buf.at[self.z], send.at[j], recv.at[self.z], (self.f, to)).start()

    def wait(self, buf, send, recv):
        for j in range(1, self.n_z):
            came = (self.z + j) % self.n_z
            push(buf.at[came], buf.at[came], send.at[j], recv.at[came], (self.f, came)).wait_recv()

    def drain(self, source_of, buf, send, recv):
        for j in range(1, self.n_z):
            to = (self.z + j) % self.n_z
            push(source_of(to), buf.at[self.z], send.at[j], recv.at[self.z], (self.f, to)).wait_send()


def text_tools(n_z, pad, width, f, z, lmask_ref, part_ref, mine_ref, out_buf, in_buf, rs_send, rs_recv, ag_send, ag_recv):
    ring = ZRing(f, z, n_z)
    bf16, f32 = jnp.bfloat16, jnp.float32

    def scatter(turn, main, rank_part):
        full = jnp.concatenate([main, rank_part], axis=1)
        full = full.reshape(n_z, pad, full.shape[1])
        part_ref[...] = full
        mine_ref[turn] = part_ref[z]
        out_buf[turn] = full.astype(bf16)
        ring.start(lambda to: out_buf.at[turn, to], in_buf.at[turn], rs_send.at[turn], rs_recv.at[turn])

    def collect(turn):
        ring.wait(in_buf.at[turn], rs_send.at[turn], rs_recv.at[turn])
        total = mine_ref[turn]
        for j in range(1, n_z):
            total = total + in_buf[turn, (z + j) % n_z].astype(f32)
        ring.drain(lambda to: out_buf.at[turn, to], in_buf.at[turn], rs_send.at[turn], rs_recv.at[turn])
        return total[:, :width], (total[:, width:] * lmask_ref[...]).astype(bf16)

    def spread(ref, *parts):
        offset = 0
        for part in parts:
            ref[z, :, offset:offset + part.shape[1]] = part
            offset += part.shape[1]
        ring.start(lambda to: ref.at[z], ref, ag_send, ag_recv)

    def spread_end(ref):
        ring.wait(ref, ag_send, ag_recv)
        ring.drain(lambda to: ref.at[z], ref, ag_send, ag_recv)

    def gathered(ref, start, count):
        return ref[:, :, start:start + count].reshape(n_z * pad, count)

    def own_lanes(ref, share):
        at = pl.ds(pl.multiple_of(z * share, 128), share)
        return ref[:, :, at].reshape(n_z * pad, share)

    return scatter, collect, spread, spread_end, gathered, own_lanes


def rows_of(mod_ref, own_ref):
    return lambda row: jnp.where(own_ref[...] > 0, mod_ref[row:row + 1, :], mod_ref[8 + row:9 + row, :])


def both_fwd_kernel(tiles, n_z, turns, o_ref, x_ref, g_ref, mod_ref, wo_ref, ao_ref, bo_ref, a1_ref, b1_ref, w1_ref, a2_ref, w2_ref, b2_ref,
                    ot_ref, xt_ref, tmod_ref, owner_ref, own_ref, lmask_ref, two_ref, tao_ref, tbo_ref,
                    a_out, x1_out, h2_out, u_out, y_out, to_out, t1_out, t2_out, gate_out,
                    tall_out, att_out, tx1_out, tbr_out,
                    m_acc, t2_acc, o_got, part_ref, mine_ref, out_buf, in_buf, ag_ref, o_send, o_recv, rs_send, rs_recv, ag_send, ag_recv):
    step = pl.program_id(0)
    f, z, core, base, column = column_peers(n_z)
    pad, width_t = xt_ref.shape
    f32, bf16 = jnp.float32, jnp.bfloat16
    scatter, collect, spread, spread_end, gathered, own_lanes = text_tools(
        n_z, pad, width_t, f, z, lmask_ref, part_ref, mine_ref, out_buf, in_buf, rs_send, rs_recv, ag_send, ag_recv)
    home = [(base + z // 2, 2 * core + i) for i in range(2)]

    def is_here(i):
        return (z // 2 == core) & (2 * core + i == z)

    def o_push(i):
        return push(ot_ref.at[i], o_got.at[z % 2], o_send.at[i], o_recv.at[z % 2], home[i])

    @pl.when(step == 0)
    def _():
        meet(column)
        for i in range(2):
            @pl.when(is_here(i))
            def _():
                copy = pltpu.make_async_copy(ot_ref.at[i], o_got.at[z % 2], o_recv.at[z % 2])
                copy.start()
                copy.wait()

            @pl.when(jnp.logical_not(is_here(i)))
            def _():
                o_push(i).start()

    rows = o_ref.shape[0]
    width = o_ref.shape[1]


    @pl.when(step == 0)
    def _():
        to = mm_t(o_ref[...], ao_ref[...]).astype(jnp.bfloat16)
        to_out[...] = to

        def cols(n, _):
            sl = pl.ds(pl.multiple_of(n * 256, 256), 256)
            a = mm_t(o_ref[...], wo_ref[sl, :]) + mm(to_out[...], bo_ref[:, sl])
            a_out[:, sl] = a.astype(jnp.bfloat16)
            x1_out[:, sl] = x_ref[:, sl].astype(jnp.float32) + mod_ref[2:3, sl] * a
            return 0

        lax.fori_loop(0, width // 256, cols, 0)

        def norm(r, _):
            sl = pl.ds(pl.multiple_of(r * ROWS, ROWS), ROWS)
            xh, _inv = norm_rows(x1_out[sl, :])
            h2_out[sl, :] = (xh * (1.0 + mod_ref[4:5, :]) + mod_ref[3:4, :]).astype(jnp.bfloat16)
            return 0

        lax.fori_loop(0, rows // ROWS, norm, 0)
        t1_out[...] = mm_t(h2_out[...], a1_ref[...]).astype(jnp.bfloat16)
        m_acc[...] = jnp.zeros_like(m_acc)
        t2_acc[...] = jnp.zeros_like(t2_acc)

    u = mm(h2_out[...], w1_ref[...]) + mm(t1_out[...], b1_ref[...])
    u_out[...] = u
    f = gelu_parts(u)[0].astype(jnp.bfloat16)
    m_acc[...] += mm_t(f, w2_ref[...])
    t2_acc[...] += mm_t(f, a2_ref[...])


    @pl.when(step == turns[0])
    def _():
        for i in range(2):
            @pl.when(jnp.logical_not(is_here(i)))
            def _():
                push(o_got.at[i], o_got.at[i], o_send.at[i], o_recv.at[i], home[i]).wait_recv()
                o_push(i).wait_send()
        owner = owner_ref[...]
        att = jnp.where(owner > 0, o_got[0].astype(f32), jnp.where(owner < 0, o_got[1].astype(f32), 0.0)).astype(bf16)
        att_out[...] = att
        scatter(0, mm_t(att, two_ref[...]), mm_t(att, tao_ref[...]))

    @pl.when(step == turns[1])
    def _():
        modulation = rows_of(tmod_ref, own_ref)
        branch, to_mine = collect(0)
        branch = branch + mm(to_mine, tbo_ref[...])
        tbr_out[...] = branch
        x1 = xt_ref[...].astype(f32) + modulation(2) * branch
        tx1_out[...] = x1
        hat, _inv = norm_rows(x1)
        spread(ag_ref, (hat * (1.0 + modulation(4)) + modulation(3)).astype(bf16), to_mine)

    @pl.when(step == tiles - 1)
    def _():
        spread_end(ag_ref)
        tall_out[...] = ag_ref[...]

    @pl.when(step == tiles - 1)
    def _():
        t2_out[...] = t2_acc[...].astype(jnp.bfloat16)
        gate_out[...] = jnp.zeros_like(gate_out)

        def last(r, _):
            sl = pl.ds(pl.multiple_of(r * ROWS, ROWS), ROWS)
            m = m_acc[sl, :] + mm(t2_out[sl, :], b2_ref[...])
            y_out[sl, :] = (x1_out[sl, :] + mod_ref[5:6, :] * m).astype(jnp.bfloat16)
            gm = g_ref[sl, :].astype(jnp.float32) * m
            gate_out[...] += sum(gm[8 * i:8 * i + 8, :] for i in range(ROWS // 8))
            return 0

        lax.fori_loop(0, rows // ROWS, last, 0)


def both_back_kernel(tiles, n_z, turns, g_ref, x1_ref, a_ref, h2_ref, o_ref, mod_ref, u_ref, w2_ref, a2_ref, b2_ref, w1_ref, a1_ref, b1_ref,
                     wo_ref, ao_ref, bo_ref, to_ref, t1_ref, t2_ref,
                     gt_ref, tx1_ref, tbr_ref, tmod_ref, own_ref, mask_ref, lmask_ref, tall_ref, att_ref, tdm_ref, two_ref, tw1_ref, tw2_ref,
                     tao_ref, tbo_ref, ta1_ref, tb1_ref, ta2_ref, tb2_ref,
                     dx1_out, do_out, sums_out, ga2_out, gb1_out, ga1_out, gb2_out, gao_out, gbo_out,
                     ty_out, tdx1_out, tdo_out, tsums_out, tgao_out, tgbo_out, tga1_out, tgb1_out, tga2_out, tgb2_out,
                     dm_ref, dt2_ref, dh_acc, dt1_acc, part_ref, mine_ref, out_buf, in_buf, tda_ref, tdo_buf,
                     do_send, do_recv, rs_send, rs_recv, ag_send, ag_recv):
    step = pl.program_id(0)
    f, z, core, base, column = column_peers(n_z)
    pad, width_t = gt_ref.shape
    rank = tao_ref.shape[0]
    share = tao_ref.shape[1]
    f32, bf16 = jnp.float32, jnp.bfloat16
    scatter, collect, spread, spread_end, gathered, own_lanes = text_tools(
        n_z, pad, width_t, f, z, lmask_ref, part_ref, mine_ref, out_buf, in_buf, rs_send, rs_recv, ag_send, ag_recv)
    home = [(base + z // 2, 2 * core + i) for i in range(2)]

    def is_here(i):
        return (z // 2 == core) & (2 * core + i == z)

    def do_push(s):
        return push(tdo_buf, tdo_out.at[z % 2], do_send.at[s], do_recv.at[z % 2], home[s])

    def collapse(place, values):
        for s in range(2):
            tsums_out[2 * place + s:2 * place + s + 1, :] = jnp.sum(
                jnp.where(own_ref[...] == (1.0 if s == 0 else -1.0), values, 0.0), axis=0, keepdims=True)

    @pl.when(step == 0)
    def _():
        meet(column)
        h2_all = gathered(tall_ref, 0, width_t)
        t1 = (mm_t(h2_all, ta1_ref[...]) * mask_ref[...]).astype(bf16)
        u = mm(h2_all, tw1_ref[...]) + mm(t1, tb1_ref[...])
        act, slope = gelu_parts(u)
        act = act.astype(bf16)
        dm_all = tdm_ref[...].reshape(n_z * pad, width_t)
        dt2 = (mm_t(dm_all, tb2_ref[...]) * mask_ref[...]).astype(bf16)
        du = ((mm(dm_all, tw2_ref[...]) + mm(dt2, ta2_ref[...])) * slope).astype(bf16)
        scatter(1, mm_t(du, tw1_ref[...]), mm_t(du, tb1_ref[...]))
        scatter(0, mm_t(act, tw2_ref[...]), mm_t(act, ta2_ref[...]))
        tga2_out[...] = t_mm(dt2, act)
        tgb1_out[...] = t_mm(t1, du)

    rows, width = g_ref.shape
    bf16 = jnp.bfloat16


    @pl.when(step == 0)
    def _():
        def start(r, _):
            sl = pl.ds(pl.multiple_of(r * ROWS, ROWS), ROWS)
            dm_ref[sl, :] = (mod_ref[5:6, :] * g_ref[sl, :].astype(jnp.float32)).astype(bf16)
            return 0

        lax.fori_loop(0, rows // ROWS, start, 0)
        dt2_ref[...] = mm_t(dm_ref[...], b2_ref[...]).astype(bf16)
        gb2_out[...] = t_mm(t2_ref[...], dm_ref[...])
        dh_acc[...] = jnp.zeros_like(dh_acc)
        dt1_acc[...] = jnp.zeros_like(dt1_acc)

    act, slope = gelu_parts(u_ref[...])
    df = mm(dm_ref[...], w2_ref[...]) + mm(dt2_ref[...], a2_ref[...])
    ga2_out[...] = t_mm(dt2_ref[...], act.astype(bf16))
    du = (df * slope).astype(bf16)
    gb1_out[...] = t_mm(t1_ref[...], du)
    dh_acc[...] += mm_t(du, w1_ref[...])
    dt1_acc[...] += mm_t(du, b1_ref[...])


    @pl.when(step == turns[0])
    def _():
        modulation = rows_of(tmod_ref, own_ref)
        dh, dt1_mine = collect(1)
        dh = dh + mm(dt1_mine, ta1_ref[...])
        hat, inverse = norm_rows(tx1_ref[...])
        dz = dh * (1.0 + modulation(4))
        dx1 = gt_ref[...].astype(f32) + inverse * (
            dz - jnp.mean(dz, axis=-1, keepdims=True) - hat * jnp.mean(dz * hat, axis=-1, keepdims=True))
        feed, t2_mine = collect(0)
        spread(tda_ref, (modulation(2) * dx1).astype(bf16), dt1_mine, t2_mine)
        tdx1_out[...] = dx1
        collapse(0, dx1 * tbr_ref[...])
        collapse(1, dh)
        collapse(2, dh * hat)
        feed = feed + mm(t2_mine, tb2_ref[...])
        ty_out[...] = (tx1_ref[...] + modulation(5) * feed).astype(bf16)
        collapse(3, gt_ref[...].astype(f32) * feed)

    @pl.when(step == turns[1])
    def _():
        spread_end(tda_ref)
        da_all = gathered(tda_ref, 0, width_t)
        dt1 = gathered(tda_ref, width_t, rank)
        t2 = gathered(tda_ref, width_t + rank, rank)
        dto = (mm_t(da_all, tbo_ref[...]) * mask_ref[...]).astype(bf16)
        tdo_buf[...] = (mm(da_all, two_ref[...]) + mm(dto, tao_ref[...])).astype(bf16)
        for s in range(2):
            @pl.when(is_here(s))
            def _():
                copy = pltpu.make_async_copy(tdo_buf, tdo_out.at[z % 2], do_recv.at[z % 2])
                copy.start()
                copy.wait()

            @pl.when(jnp.logical_not(is_here(s)))
            def _():
                do_push(s).start()
        tgao_out[...] = t_mm(dto, att_ref[...])
        tgbo_out[...] = t_mm(gathered(tall_ref, width_t, rank), own_lanes(tda_ref, share))
        tgb2_out[...] = t_mm(t2, own_lanes(tdm_ref, share))
        tga1_out[...] = t_mm(dt1, own_lanes(tall_ref, share))

    @pl.when(step == tiles - 1)
    def _():
        dt1 = dt1_acc[...].astype(bf16)
        dt2_ref[...] = dt1
        ga1_out[...] = t_mm(dt1, h2_ref[...])
        sums_out[...] = jnp.zeros_like(sums_out)

        def last(r, _):
            sl = pl.ds(pl.multiple_of(r * ROWS, ROWS), ROWS)
            dh = dh_acc[sl, :] + mm(dt2_ref[sl, :], a1_ref[...])
            xh, inverse = norm_rows(x1_ref[sl, :])
            dz = dh * (1.0 + mod_ref[4:5, :])
            dx1 = g_ref[sl, :].astype(jnp.float32) + inverse * (
                dz - jnp.mean(dz, axis=-1, keepdims=True) - xh * jnp.mean(dz * xh, axis=-1, keepdims=True))
            dx1_out[sl, :] = dx1
            dm_ref[sl, :] = (mod_ref[2:3, :] * dx1).astype(bf16)
            fold = lambda v: sum(v[8 * i:8 * i + 8, :] for i in range(ROWS // 8))
            sums_out[0:8, :] += fold(dx1 * a_ref[sl, :].astype(jnp.float32))
            sums_out[8:16, :] += fold(dh)
            sums_out[16:24, :] += fold(dh * xh)
            return 0

        lax.fori_loop(0, rows // ROWS, last, 0)
        dto = mm_t(dm_ref[...], bo_ref[...]).astype(bf16)
        dt2_ref[...] = dto
        gao_out[...] = t_mm(dto, o_ref[...])
        gbo_out[...] = t_mm(to_ref[...], dm_ref[...])

        def cols(n, _):
            sl = pl.ds(pl.multiple_of(n * 256, 256), 256)
            do_out[:, sl] = (mm(dm_ref[...], wo_ref[:, sl]) + mm(dt2_ref[...], ao_ref[:, sl])).astype(bf16)
            return 0

        lax.fori_loop(0, width // 256, cols, 0)

    @pl.when(step == tiles - 1)
    def _():
        for i in range(2):
            @pl.when(jnp.logical_not(is_here(i)))
            def _():
                push(tdo_out.at[i], tdo_out.at[i], do_send.at[i], do_recv.at[i], home[i]).wait_recv()
                do_push(i).wait_send()


def both_fwd(o, x, g, mod, wo, pair_o, pair_1, w1, pair_2, w2, ot, xt, tmod, owner, own, lmask, two, tpair_o, n_z, cid, tn=512, turns=(2, 7)):
    rows, width = o.shape
    hidden = w1.shape[1]
    tiles = hidden // tn
    rank = pair_o[0].shape[0]
    once = lambda shape: pl.BlockSpec(shape, lambda n: (0,) * len(shape), pipeline_mode=pl.Buffered(1))
    whole = once
    tile = lambda height: pl.BlockSpec((height, tn), lambda n: (0, n))
    f32, bf16 = jnp.float32, jnp.bfloat16
    shape, vmem, dma = jax.ShapeDtypeStruct, pltpu.VMEM, pltpu.SemaphoreType.DMA
    act = (rows, width)
    pad = xt.shape[0]
    total, share = n_z * pad, two.shape[1]
    thick = tpair_o[0].shape[0]
    wide = width + thick
    texts = (xt, tmod, owner, own, lmask, two, *tpair_o)
    return pl.pallas_call(
        functools.partial(both_fwd_kernel, tiles, n_z, turns),
        grid=(tiles,),
        in_specs=[once(act), once(act), once(act), once(mod.shape), once((width, width)), once((rank, width)), once((rank, width)),
                  once((rank, width)), tile(rank), tile(width), tile(rank), tile(width), once((rank, width)),
                  pl.BlockSpec(memory_space=pl.ANY)] + [once(v.shape) for v in texts],
        out_specs=[whole(act), whole(act), whole(act), tile(rows), whole(act), whole((rows, rank)), whole((rows, rank)),
                   whole((rows, rank)), whole((8, width)), whole((n_z, pad, wide)), whole((total, share)), whole((pad, width)),
                   whole((pad, width))],
        out_shape=[shape(act, bf16), shape(act, f32), shape(act, bf16), shape((rows, hidden), f32), shape(act, bf16)]
        + [shape((rows, rank), bf16)] * 3
        + [shape((8, width), f32), shape((n_z, pad, wide), bf16), shape((total, share), bf16), shape((pad, width), f32),
           shape((pad, width), f32)],
        scratch_shapes=[vmem(act, f32), vmem((rows, rank), f32), vmem((2, total, share), bf16), vmem((n_z, pad, wide), f32), vmem((1, pad, wide), f32),
                        vmem((1, n_z, pad, wide), bf16), vmem((1, n_z, pad, wide), bf16), vmem((n_z, pad, wide), bf16),
                        dma((2,)), dma((2,)), dma((1, n_z)), dma((1, n_z)), dma((n_z,)), dma((n_z,))],
        compiler_params=pltpu.CompilerParams(collective_id=cid, has_side_effects=True, vmem_limit_bytes=60 * 1024 * 1024),
        name="block_forward",
    )(o, x, g, mod, wo, *pair_o, pair_1[0], pair_1[1], w1, pair_2[0], w2, pair_2[1], ot, *texts)


def both_back(g, x1, a, h2, o, mod, u, w2, pair_2, w1, pair_1, wo, pair_o, mids,
              gt, tx1, tbr, tmod, own, mask, lmask, tall, att, tdm, two, tw1, tw2, tpair_o, tpair_1, tpair_2, n_z, cid, tn=512, turns=(5, 9)):
    rows, width = o.shape
    hidden = w1.shape[1]
    tiles = hidden // tn
    rank = pair_o[0].shape[0]
    once = lambda shape: pl.BlockSpec(shape, lambda n: (0,) * len(shape), pipeline_mode=pl.Buffered(1))
    whole = once
    tile = lambda height: pl.BlockSpec((height, tn), lambda n: (0, n))
    f32, bf16 = jnp.float32, jnp.bfloat16
    shape, vmem, dma = jax.ShapeDtypeStruct, pltpu.VMEM, pltpu.SemaphoreType.DMA
    act = (rows, width)
    side = (rank, width)
    thin = (rows, rank)
    pad = gt.shape[0]
    total, share = n_z * pad, two.shape[1]
    thick = tpair_o[0].shape[0]
    t_hidden = tw1.shape[1]
    wide = width + thick
    texts = (gt, tx1, tbr, tmod, own, mask, lmask, tall, att, tdm, two, tw1, tw2, *tpair_o, *tpair_1, *tpair_2)
    return pl.pallas_call(
        functools.partial(both_back_kernel, tiles, n_z, turns),
        grid=(tiles,),
        in_specs=[once(act)] * 5 + [once(mod.shape), tile(rows), tile(width), tile(rank), once(side), tile(width), once(side), tile(rank),
                  once((width, width)), once(side), once(side)] + [once(thin)] * 3 + [once(v.shape) for v in texts],
        out_specs=[whole(act), whole(act), whole((24, width)), tile(rank), tile(rank)] + [whole(side)] * 4
        + [whole((pad, width)), whole((pad, width)), pl.BlockSpec(memory_space=pl.ANY), whole((8, width)), whole((thick, share)),
           whole((thick, share)), whole((thick, share)), whole((thick, t_hidden)), whole((thick, t_hidden)), whole((thick, share))],
        out_shape=[shape(act, f32), shape(act, bf16), shape((24, width), f32)] + [shape((rank, hidden), f32)] * 2 + [shape(side, f32)] * 4
        + [shape((pad, width), bf16), shape((pad, width), f32), shape((2, total, share), bf16), shape((8, width), f32),
           shape((thick, share), f32), shape((thick, share), f32), shape((thick, share), f32), shape((thick, t_hidden), f32),
           shape((thick, t_hidden), f32), shape((thick, share), f32)],
        scratch_shapes=[vmem(act, bf16), vmem(thin, bf16), vmem(act, f32), vmem(thin, f32),
                        vmem((n_z, pad, wide), f32), vmem((2, pad, wide), f32), vmem((2, n_z, pad, wide), bf16), vmem((2, n_z, pad, wide), bf16),
                        vmem((n_z, pad, wide + thick), bf16), vmem((total, share), bf16),
                        dma((2,)), dma((2,)), dma((2, n_z)), dma((2, n_z)), dma((n_z,)), dma((n_z,))],
        compiler_params=pltpu.CompilerParams(collective_id=cid, has_side_effects=True, vmem_limit_bytes=60 * 1024 * 1024),
        name="block_backward",
    )(g, x1, a, h2, o, mod, u, w2, pair_2[0], pair_2[1], w1, pair_1[0], pair_1[1], wo, *pair_o, *mids, *texts)


def flip_bits(chip, mask, nbits):
    other = 0
    for bit in range(nbits):
        have = (chip // (1 << bit)) % 2
        other = other + (1 - have if (mask >> bit) & 1 else have) * (1 << bit)
    return other


def tail_kernel(n_f, n_z, fans, cols, *refs):
    it = iter(refs)
    take = lambda count: [next(it) for _ in range(count)]
    dq_in, tdq_in, wq_ref = take(3)
    (x_ref, dx1_ref, h_ref, imod_ref, mid_ref, qa_ref, qb_ref, isum_ref, igate_ref, tx_ref, tdx1_ref, th_ref, tmodr_ref, owner_ref,
     own_ref, lmask_ref, tmid_ref, twq_ref, tqa_ref, tqb_ref, tsum_ref) = take(21)
    img_a, img_b, txt_a, txt_b = take(3), take(3), take(3), take(3)
    hot4_ref, hot2_ref, wmod_ref, bmod_ref, tmod_ref, cond_ref, smask_ref = take(7)
    grad_out, tgrad_out, cond_out, rank_out, shard_out = take(5)
    (dq_ref, wtile, dh_ref, dt_ref, grad_ref, gaq_ref, gbq_ref, tgot, part_ref, mine_ref, out_buf, in_buf, dt_ag, tgb_ref, dmod_ref,
     isums) = take(16)
    zmsg, zgot, dense, snd1, rcv1, snd2, rcv2, dgot, own_dm, all_dm, cpart, cgot, zsum, zall, dts = take(15)
    (g_send, g_recv, z_send, z_recv, c_send, c_recv, s_send, s_recv, d_send, d_recv, f_send, f_recv, p_send, p_recv,
     q_send, q_recv, t_send, t_recv, dq_send, dq_recv, dq_own, w_sem, h_send, h_recv, rs_send, rs_recv, ag_send, ag_recv) = take(28)
    f32, bf16 = jnp.float32, jnp.bfloat16
    f, z, core, base, column = column_peers(n_z)
    chip = f // 2
    chips = n_f // 2
    nbits = bits_of(chips)
    partner = base + 1 - core
    around = [((f + j) % n_f, z) for j in range(1, n_f)]
    others = [(flip_bits(chip, mask, nbits) * 2 + side, z) for mask in range(1, chips) for side in range(2)]
    meet(column + others)
    ring = ZRing(f, z, n_z)
    blk = shard_out.shape[0]
    hidden_rank = hot2_ref.shape[0]

    home = [(base + z // 2, 2 * core + i) for i in range(2)]

    def is_here(i):
        return (z // 2 == core) & (2 * core + i == z)

    swap = push(dq_in.at[1 - core], dq_ref.at[core], dq_send, dq_recv, (partner, z))
    swap.start()
    keep = pltpu.make_async_copy(dq_in.at[core], dq_ref.at[core], dq_own)
    keep.start()

    def t_push(i):
        return push(tdq_in.at[i], tgot.at[z % 2], h_send.at[i], h_recv.at[z % 2], home[i])

    for i in range(2):
        @pl.when(is_here(i))
        def _():
            copy = pltpu.make_async_copy(tdq_in.at[i], tgot.at[z % 2], h_recv.at[z % 2])
            copy.start()
            copy.wait()

        @pl.when(jnp.logical_not(is_here(i)))
        def _():
            t_push(i).start()

    pad, width = tx_ref.shape
    thick = tqa_ref.shape[0]
    scatter, collect, spread, spread_end, gathered, own_lanes = text_tools(
        n_z, pad, width, f, z, lmask_ref, part_ref, mine_ref, out_buf, in_buf, rs_send, rs_recv, ag_send, ag_recv)
    tn = wtile.shape[3]
    per_half = dq_ref.shape[2] // tn

    def tile_of(n):
        side = core if n < per_half else 1 - core
        return side, side * per_half + n % per_half

    def tile_load(n):
        at = pl.ds(pl.multiple_of(tile_of(n)[1] * tn, 128), tn)
        return pltpu.make_async_copy(wq_ref.at[:, :, at], wtile.at[n % 2], w_sem.at[n % 2])

    def tile_back(n):
        if n + 1 < 2 * per_half:
            tile_load(n + 1).start()
        tile_load(n).wait()
        side, number = tile_of(n)
        at = pl.ds(pl.multiple_of(number * tn, 128), tn)
        part = dq_ref[side, :, n % per_half * tn:(n % per_half + 1) * tn]
        main = mm_t(part, wtile[n % 2].reshape(width, tn))
        thin = mm_t(part, qb_ref[:, at])
        if n == 0:
            dh_ref[...] = main
            dt_ref[...] = thin
        else:
            dh_ref[...] += main
            dt_ref[...] += thin
        gbq_ref[:, at] = t_mm(mid_ref[...], part)

    tile_load(0).start()
    keep.wait()
    for n in range(per_half):
        tile_back(n)

    for i in range(2):
        @pl.when(jnp.logical_not(is_here(i)))
        def _():
            push(tgot.at[i], tgot.at[i], h_send.at[i], h_recv.at[i], home[i]).wait_recv()
            t_push(i).wait_send()
    owner = owner_ref[...]
    tdq = jnp.where(owner > 0, tgot[0].astype(f32), jnp.where(owner < 0, tgot[1].astype(f32), 0.0)).astype(bf16)
    scatter(0, mm_t(tdq, twq_ref[...]), mm_t(tdq, tqb_ref[...]))
    tgb_ref[...] = t_mm(tmid_ref[...], tdq)

    push(dq_in.at[1 - core], dq_ref.at[1 - core], dq_send, dq_recv, (partner, z)).wait_recv()
    for n in range(per_half, 2 * per_half):
        tile_back(n)
    dt_low = dt_ref[...].astype(bf16)
    gaq_ref[...] = t_mm(dt_low, h_ref[...])

    offset = 0
    spans = []
    for part, sizes in (([gaq_ref] + img_a, fans), ([gbq_ref] + img_b, cols)):
        for index in range(4):
            count = sizes[index + 1] // n_z
            for t in range(n_z):
                zmsg[t, :, offset:offset + count] = part[index][:, t * count:(t + 1) * count].astype(bf16)
            spans.append((offset, count))
            offset += count
    ring.start(lambda to: zmsg.at[to], zgot, z_send, z_recv)
    zgot[z] = zmsg[z]

    isums[...] = jnp.zeros_like(isums)
    quarter = grad_ref.shape[1]
    dh_ref[...] += mm(dt_low, qa_ref[...])
    for i in range(2):
        def last(r, _):
            sl = pl.ds(pl.multiple_of(i * quarter + r * ROWS, ROWS), ROWS)
            dh = dh_ref[sl, :]
            xh, inverse = norm_rows(x_ref[sl, :].astype(f32))
            dz = dh * (1.0 + imod_ref[1:2, :])
            dx = dx1_ref[sl, :] + inverse * (
                dz - jnp.mean(dz, axis=-1, keepdims=True) - xh * jnp.mean(dz * xh, axis=-1, keepdims=True))
            grad_ref[i, pl.ds(pl.multiple_of(r * ROWS, ROWS), ROWS), :] = dx.astype(bf16)
            fold = lambda v: sum(v[8 * j:8 * j + 8, :] for j in range(ROWS // 8))
            isums[0:8, :] += fold(dh)
            isums[8:16, :] += fold(dh * xh)
            return 0

        lax.fori_loop(0, quarter // ROWS, last, 0)

    pick = rows_of(tmodr_ref, own_ref)
    tdh, tdt = collect(0)
    spread(dt_ag, tdt)
    tdh = tdh + mm(tdt, tqa_ref[...])
    hat, inverse = norm_rows(tx_ref[...].astype(f32))
    dz = tdh * (1.0 + pick(1))
    tgrad_out[...] = tdx1_ref[...] + inverse * (
        dz - jnp.mean(dz, axis=-1, keepdims=True) - hat * jnp.mean(dz * hat, axis=-1, keepdims=True))

    def total_of(v):
        return jnp.sum(v, axis=0, keepdims=True)

    rows_img = [total_of(isums[0:8, :]), total_of(isums[8:16, :])]
    rows_img += [total_of(isum_ref[8 * p:8 * p + 8, :]) for p in range(3)] + [total_of(igate_ref[...])]
    rows_txt = []
    for s in range(2):
        chosen = own_ref[...] == (1.0 if s == 0 else -1.0)
        rows_txt.append([total_of(jnp.where(chosen, tdh, 0.0)), total_of(jnp.where(chosen, tdh * hat, 0.0))]
                        + [tsum_ref[2 * p + s:2 * p + s + 1, :] for p in range(4)])
    dmod_ref[...] = jnp.zeros_like(dmod_ref)
    chunk = dmod_ref.shape[-1]
    per_row = width // chunk
    per_block = 6 * per_row // n_z
    for r, parts in enumerate([rows_img] + rows_txt):
        for q in range(6 * per_row):
            dmod_ref[q // per_block, r, q % per_block:q % per_block + 1, :] = (
                parts[q // per_row][:, q % per_row * chunk:(q % per_row + 1) * chunk])

    def dmod_copy(index, peer):
        return push(dmod_ref.at[peer[1]], dgot.at[core * n_z + z], d_send.at[index], d_recv.at[core * n_z + z], peer)

    for index, peer in enumerate(column):
        dmod_copy(index, peer).start()
    dgot[core * n_z + z] = dmod_ref[z]

    for index, peer in enumerate(column):
        place = peer[0] % 2 * n_z + peer[1]
        push(dgot.at[place], dgot.at[place], d_send.at[index], d_recv.at[place], peer).wait_recv()
    rows = []
    for slot in range(2):
        rows.append(dgot[2 * core + slot, 0] + dgot[n_z + 2 * core + slot, 0])
    for slot in range(2):
        total = dgot[core * n_z, 1 + slot]
        for t in range(1, n_z):
            total = total + dgot[core * n_z + t, 1 + slot]
        rows.append(total)
    own_dm[...] = jnp.zeros_like(own_dm)
    for r, total in enumerate(rows):
        for j in range(own_dm.shape[1] // chunk):
            own_dm[r:r + 1, j * chunk:(j + 1) * chunk] = total[j:j + 1, :].astype(bf16).astype(f32)
    for j in range(1, n_f):
        push(own_dm, all_dm.at[f], f_send.at[j], f_recv.at[f], around[j - 1]).start()
    all_dm[f] = own_dm[...]
    dm_low = own_dm[...].astype(bf16)
    tmod = [tmod_ref[s].astype(bf16) for s in range(2)]
    gb_mod = [t_mm(tmod[s], dm_low) for s in range(2)]
    rank_img = mm_t(dm_low, bmod_ref[0])
    rank_txt = mm_t(dm_low, bmod_ref[1])
    row = lax.broadcasted_iota(jnp.int32, rank_img.shape, 0)
    rank_part = jnp.where(row < 2, rank_img, rank_txt)

    spread_end(dt_ag)
    tga = t_mm(gathered(dt_ag, 0, thick), own_lanes(th_ref, cols[2] // n_z))
    txt_a = [tga[:hidden_rank]] + [ref[...] for ref in txt_a]
    txt_b = [tgb_ref[:hidden_rank, :]] + [ref[...] for ref in txt_b]
    hot2 = hot2_ref[...]
    starts = []
    offset = 0
    for stream in range(2):
        for index in range(5):
            starts.append((stream, index, offset, offset + fans[index] // n_z))
            offset += fans[index] // n_z + cols[index] // n_z

    def put_a(at, part, hot):
        dense[at:at + part.shape[1], :] = dots(part, hot, 0, 0)

    def put_b(at, part, hot):
        full = dots(hot, part, 0, 0)
        blocks = part.shape[1] // 128
        for j in range(blocks):
            dense[pl.ds(at + j, 128, stride=blocks), :] = full[:, j * 128:(j + 1) * 128]

    for stream, index, at_a, at_b in starts:
        if index == 0:
            dense[at_a:at_b, :] = jnp.zeros((at_b - at_a, 128), f32)
            put_b(at_b, gb_mod[stream].astype(bf16), hot2)
        elif stream == 1:
            put_a(at_a, txt_a[index - 1].astype(bf16), hot2)
            put_b(at_b, txt_b[index - 1].astype(bf16), hot2)

    ring.wait(zgot, z_send, z_recv)
    hot4 = hot4_ref[...]
    for stream, index, at_a, at_b in starts:
        if stream == 0 and index > 0:
            for at, put, (begin, count) in ((at_a, put_a, spans[index - 1]), (at_b, put_b, spans[index + 3])):
                part = zgot[:, :, begin:begin + count].reshape(hot4.shape[0], count)
                put(at, part, hot4)

    for i in range(2):
        @pl.when(is_here(i))
        def _():
            pltpu.make_async_copy(grad_ref.at[i], grad_out.at[z % 2], g_recv.at[z % 2]).start()

        @pl.when(jnp.logical_not(is_here(i)))
        def _():
            push(grad_ref.at[i], grad_out.at[z % 2], g_send.at[i], g_recv.at[z % 2], home[i]).start()

    def block(number):
        return pl.ds(pl.multiple_of(number * blk, 16), blk)

    for p in range(chips):
        snd1[p] = dense[block(2 * p + 1 - core), :].astype(bf16)
        push(snd1.at[p], rcv1.at[p], c_send.at[p], c_recv.at[p], (partner, z)).start()

    for j in range(1, n_f):
        came = (f - j + n_f) % n_f
        push(own_dm, all_dm.at[came], f_send.at[j], f_recv.at[came], (came, z)).wait_recv()
    everyone = all_dm[...].reshape(n_f * 8, own_dm.shape[1]).astype(bf16)
    part = mm_t(everyone, wmod_ref[0]) + pltpu.roll(mm_t(everyone, wmod_ref[1]), n_f * 8 - 2, 0)
    k_local = part.shape[1]
    cpart[...] = jnp.zeros_like(cpart)
    cpart[:, :, :k_local] = part.reshape(n_f, 8, k_local)
    for j in range(1, n_f):
        to = (f + j) % n_f
        push(cpart.at[to], cgot.at[f], p_send.at[j], p_recv.at[f], (to, z)).start()
    cgot[f] = cpart[f]

    for p in range(chips):
        push(snd1.at[p], rcv1.at[p], c_send.at[p], c_recv.at[p], (partner, z)).wait_recv()

    def mine_of(p):
        return block(2 * p + core)

    for p in range(chips):
        dense[mine_of(p), :] += rcv1[p].astype(f32)

    half = blk // 2
    orders = [list(range(nbits)), list(range(nbits))[::-1]]

    def masks_at(side, turn):
        left = orders[side][turn:]
        return [sum(1 << b for i, b in enumerate(left) if (m >> i) & 1) for m in range(1 << len(left))]

    def rs_copy(side, turn, index):
        slot = turn * 2 + index
        peer = flip_bits(chip, 1 << orders[side][turn], nbits) * 2 + core
        return push(snd2.at[side, slot], rcv2.at[side, slot], s_send.at[side, slot], s_recv.at[side, slot], (peer, z))

    def half_of(number, side):
        return pl.ds(pl.multiple_of((2 * number + core) * blk + side * half, 16), half)

    def rs_start(turn):
        for side in range(2):
            bit = 1 << orders[side][turn]
            for index, mask in enumerate(masks_at(side, turn + 1)):
                number = flip_bits(chip, bit | mask, nbits)
                snd2[side, turn * 2 + index] = dense[half_of(number, side), :].astype(bf16)
                rs_copy(side, turn, index).start()

    def rs_end(turn):
        for side in range(2):
            for index, mask in enumerate(masks_at(side, turn + 1)):
                number = flip_bits(chip, mask, nbits)
                rs_copy(side, turn, index).wait_recv()
                dense[half_of(number, side), :] += rcv2[side, turn * 2 + index].astype(f32)

    rs_start(0)

    for j in range(1, n_f):
        came = (f - j + n_f) % n_f
        push(cpart.at[came], cgot.at[came], p_send.at[j], p_recv.at[came], (came, z)).wait_recv()
    zsum[:n_f] = cgot[...]
    zsum[n_f] = jnp.zeros(zsum.shape[1:], f32)
    zsum[n_f, :, :hidden_rank] = rank_part
    zall[z] = zsum[...]
    ring.start(lambda to: zsum, zall, q_send, q_recv)
    ring.wait(zall, q_send, q_recv)
    total = zall[0]
    for t in range(1, n_z):
        total = total + zall[t]
    cond_out[...] = total[:n_f]
    dt = (total[n_f][:, :hidden_rank] * smask_ref[...]).astype(bf16)
    rank_out[...] = dt.astype(f32)
    wide = mm(dt, hot2)
    dts[f] = wide
    for j in range(1, n_f):
        push(dts.at[f], dts.at[f], t_send.at[j], t_recv.at[f], around[j - 1]).start()

    rs_end(0)
    if nbits > 1:
        rs_start(1)
    for j in range(1, n_f):
        came = (f - j + n_f) % n_f
        push(dts.at[came], dts.at[came], t_send.at[j], t_recv.at[came], (came, z)).wait_recv()
    all_dt = dts[...].reshape(n_f * 8, 128)
    row = lax.broadcasted_iota(jnp.int32, all_dt.shape, 0) % 8
    act = cond_ref[...].reshape(n_f * 8, cond_ref.shape[-1]).astype(bf16)
    mod_a = [
        dots(act, jnp.where(row < 2, all_dt, 0.0).astype(bf16), 0, 0),
        dots(act, pltpu.roll(jnp.where((row >= 2) & (row < 4), all_dt, 0.0), n_f * 8 - 2, 0).astype(bf16), 0, 0),
    ]
    if nbits > 1:
        rs_end(1)
    shard_out[...] = dense[block(f), :]
    for stream in range(2):
        first = starts[5 * stream][2]
        own = jnp.where(f == first // blk, 1.0, 0.0)
        count = mod_a[stream].shape[0]
        shard_out[:count, :] += own * mod_a[stream]

    swap.wait_send()
    ring.drain(lambda to: zmsg.at[to], zgot, z_send, z_recv)
    ring.drain(lambda to: zsum, zall, q_send, q_recv)
    for index, peer in enumerate(column):
        dmod_copy(index, peer).wait_send()
    for j in range(1, n_f):
        to = (f + j) % n_f
        push(own_dm, all_dm.at[f], f_send.at[j], f_recv.at[f], (to, z)).wait_send()
        push(cpart.at[to], cgot.at[f], p_send.at[j], p_recv.at[f], (to, z)).wait_send()
        push(dts.at[f], dts.at[f], t_send.at[j], t_recv.at[f], (to, z)).wait_send()
    for p in range(chips):
        push(snd1.at[p], rcv1.at[p], c_send.at[p], c_recv.at[p], (partner, z)).wait_send()
    for turn in range(nbits):
        for side in range(2):
            for index in range(len(masks_at(side, turn + 1))):
                rs_copy(side, turn, index).wait_send()
    for i in range(2):
        @pl.when(is_here(i))
        def _():
            pltpu.make_async_copy(grad_ref.at[i], grad_out.at[z % 2], g_recv.at[z % 2]).wait()

        @pl.when(jnp.logical_not(is_here(i)))
        def _():
            push(grad_out.at[i], grad_out.at[i], g_send.at[i], g_recv.at[i], home[i]).wait_recv()
            push(grad_ref.at[i], grad_out.at[z % 2], g_send.at[i], g_recv.at[z % 2], home[i]).wait_send()


def tail(dq, tdq, wq, smalls, img_a, img_b, txt_a, txt_b, hot4, hot2, wmod, bmod, tmod, cond, smask, n_f, n_z, fans, cols, cid, tn=768):
    f32, bf16 = jnp.float32, jnp.bfloat16
    vmem, dma = pltpu.VMEM, pltpu.SemaphoreType.DMA
    shape = jax.ShapeDtypeStruct
    args = (dq, tdq, wq, *smalls, *img_a, *img_b, *txt_a, *txt_b, hot4, hot2, wmod, bmod, tmod, cond, smask)
    lanes = (sum(fans[1:]) + sum(cols[1:])) // n_z
    rows = 2 * (sum(fans) + sum(cols)) // n_z
    blk = rows // n_f
    chips = n_f // 2
    cut = cols[0] // n_z
    rank = hot2.shape[0]
    _, img_rows, half = dq.shape
    _, k_local, _ = wq.shape
    width = cols[2]
    tx = smalls[9]
    thick = smalls[18].shape[0]
    pad = tx.shape[0]
    wide = width + thick
    inside, outside = pl.BlockSpec(memory_space=vmem), pl.BlockSpec(memory_space=pl.ANY)
    return pl.pallas_call(
        functools.partial(tail_kernel, n_f, n_z, tuple(fans), tuple(cols)),
        out_shape=[shape((2, img_rows // 2, width), bf16), shape((pad, width), f32), shape((n_f, 8, 256), f32), shape((8, rank), f32),
                   shape((blk, 128), f32)],
        in_specs=[outside] * 3 + [inside] * (len(args) - 3),
        out_specs=[outside] + [inside] * 4,
        scratch_shapes=[
            vmem((2, img_rows, half), bf16), vmem((2, n_f, k_local, tn), bf16), vmem((img_rows, width), f32), vmem((img_rows, RANK), f32),
            vmem((2, img_rows // 2, width), bf16), vmem((RANK, fans[1]), f32), vmem((RANK, cols[1]), f32), vmem(tdq.shape, bf16),
            vmem((n_z, pad, wide), f32), vmem((1, pad, wide), f32), vmem((1, n_z, pad, wide), bf16), vmem((1, n_z, pad, wide), bf16),
            vmem((n_z, pad, thick), bf16), vmem((thick, cols[1] // n_z), f32), vmem((n_z, 3, 8, width // n_z), f32), vmem((16, width), f32),
            vmem((n_z, RANK, lanes), bf16), vmem((n_z, RANK, lanes), bf16), vmem((rows, 128), f32),
            vmem((chips, blk, 128), bf16), vmem((chips, blk, 128), bf16),
            vmem((2, 3, blk // 2, 128), bf16), vmem((2, 3, blk // 2, 128), bf16),
            vmem((2 * n_z, 3, 8, width // n_z), f32), vmem((8, cut), f32), vmem((n_f, 8, cut), f32),
            vmem((n_f, 8, 256), f32), vmem((n_f, 8, 256), f32), vmem((n_f + 1, 8, 256), f32),
            vmem((n_z, n_f + 1, 8, 256), f32), vmem((n_f, 8, 128), f32),
            dma((2,)), dma((2,)), dma((n_z,)), dma((n_z,)), dma((chips,)), dma((chips,)), dma((2, 3)), dma((2, 3)),
            dma((2 * n_z,)), dma((2 * n_z,)), dma((n_f,)), dma((n_f,)), dma((n_f,)), dma((n_f,)), dma((n_z,)), dma((n_z,)),
            dma((n_f,)), dma((n_f,)), dma, dma, dma, dma((2,)), dma((2,)), dma((2,)), dma((1, n_z)), dma((1, n_z)), dma((n_z,)), dma((n_z,)),
        ],
        compiler_params=pltpu.CompilerParams(collective_id=cid, has_side_effects=True, vmem_limit_bytes=60 * 1024 * 1024),
        name="gradient_exchange",
    )(*args)

FULL = 4
PART = 4


def front_kernel(n_f, n_z, fans, cols, *refs):
    it = iter(refs)
    take = lambda count: [next(it) for _ in range(count)]
    ins = take(FULL + PART + 1)
    (x_ref, g_ref, picks_ref, hot2_ref, cblk_ref, clane_ref, c8_ref, smask_ref, wmod_ref, xt_ref, gt_ref, own_ref, tmask_ref) = take(13)
    outs = take(FULL + PART)
    x_out, g_out, imod_out, tmod_out = take(4)
    img_a, img_b, txt_a, txt_b = take(4), take(4), take(4), take(4)
    moda_out, modb_out, midm_out, cond_out, dm_out = take(5)
    h_out, mid_out, heads_out, th_out, tmid_out, theads_out = take(6)
    (row_ref, fl_ref, img_msg, img_got, txt_msg, txt_got, cgot, mpart, mgot, own_mod, mod_got, wtile, wtxt, stage, tq_ref) = take(15)
    (z_send, z_recv, xy_send, xy_recv, core_send, core_recv, own_sem, x_send, x_recv, g_send, g_recv, c_send, c_recv, l_send,
     l_recv, m_send, m_recv, i_send, i_recv, t_send, t_recv, d_send, d_recv, a_send, a_recv, w_sem, tw_sem, h_send, h_recv,
     h_sem, q_send, q_recv, dm_send, dm_recv) = take(34)
    f32, bf16 = jnp.float32, jnp.bfloat16
    f, z, core, base, column = column_peers(n_z)
    chip = f // 2
    chips = n_f // 2
    nbits = bits_of(chips)
    partner = base + 1 - core
    others = [(flip_bits(chip, mask, nbits) * 2 + side, z) for mask in range(1, chips) for side in range(2)]
    meet(column + others)
    ring = ZRing(f, z, n_z)
    total = FULL + PART + 1
    adapters = total - 1
    blk = ins[adapters].shape[0]
    width = x_ref.shape[2]
    rank2 = hot2_ref.shape[0]

    def peer_of(mask):
        return flip_bits(chip, mask, nbits) * 2 + core

    def wide_of(m):
        return ins[m].shape[-1]

    def cuts(m):
        if m == adapters:
            return [(0, (0, blk // 2)), (1, (blk // 2, blk // 2))]
        return list(enumerate(halves(wide_of(m))))

    def place(m, who, zz, cut):
        off, w = cut
        if m == adapters:
            return row_ref.at[pl.ds(pl.multiple_of(who * blk + off, 16), w), :]
        if m < FULL:
            return outs[m].at[who, :, pl.ds(pl.multiple_of(zz * wide_of(m) + off, 128), w)]
        return outs[m].at[who, :, pl.ds(off, w)]

    def piece(m, cut):
        off, w = cut
        if m == adapters:
            return ins[m].at[pl.ds(off, w), :]
        return ins[m].at[:, pl.ds(off, w)]

    def whole_place(m, who, zz):
        return place(m, who, zz, (0, blk if m == adapters else wide_of(m)))

    def slot(m, zz):
        return zz if m < FULL else 0

    def order_of(half):
        order = list(range(nbits))
        return order if half == 0 else order[::-1]

    def xy_copy(m, zz, half, cut, mask, bit, own_piece=False):
        where = place(m, peer_of(mask), zz, cut)
        return push(piece(m, cut) if own_piece else where, where, xy_send.at[m, slot(m, zz), half, mask, bit],
                    xy_recv.at[m, slot(m, zz), half, mask | (1 << bit)], (peer_of(1 << bit), z))

    def xy_wait(m, zz, half, cut, mask):
        where = place(m, peer_of(mask), zz, cut)
        push(where, where, xy_send.at[m, slot(m, zz), half, 0, 0], xy_recv.at[m, slot(m, zz), half, mask], (partner, z)).wait_recv()

    def core_copy(m, zz, half, cut, mask, own_piece=False):
        where = place(m, peer_of(mask), zz, cut)
        return push(piece(m, cut) if own_piece else where, where, core_send.at[m, slot(m, zz), half, mask],
                    core_recv.at[m, slot(m, zz), half, mask], (partner, z))

    def core_wait(m, zz, half, cut, mask):
        where = place(m, peer_of(mask) - core + (1 - core), zz, cut)
        push(where, where, core_send.at[m, slot(m, zz), half, mask], core_recv.at[m, slot(m, zz), half, mask], (partner, z)).wait_recv()

    def own_copy(m):
        return pltpu.make_async_copy(ins[m], whole_place(m, f, z), own_sem.at[m])

    def z_copy(m, zz, up, own_piece=False):
        where = whole_place(m, f, zz)
        return push(ins[m] if own_piece else where, where, z_send.at[m, zz, up], z_recv.at[m, zz], (f, z + 1 if up else z - 1))

    def last_of(order, mask):
        return max([i for i, b in enumerate(order) if (mask >> b) & 1], default=-1)

    def masks_in_order(half):
        order = order_of(half)
        return sorted(range(1, 1 << nbits), key=lambda mask: [1 if (mask >> b) & 1 else 0 for b in reversed(order)])

    def launch(m, zz, own_piece=False):
        for half, cut in cuts(m):
            for bit in order_of(half):
                xy_copy(m, zz, half, cut, 0, bit, own_piece).start()
            core_copy(m, zz, half, cut, 0, own_piece).start()

    def launch_own(m):
        if m < FULL:
            @pl.when(z < n_z - 1)
            def _():
                z_copy(m, z, 1, True).start()

            @pl.when(z > 0)
            def _():
                z_copy(m, z, 0, True).start()
        launch(m, z, True)
        own_copy(m).start()

    def forward(m, zz):
        for half, cut in cuts(m):
            order = order_of(half)
            for mask in masks_in_order(half):
                if last_of(order, mask) < nbits - 1:
                    xy_wait(m, zz, half, cut, mask)
                    for b in order[last_of(order, mask) + 1:]:
                        xy_copy(m, zz, half, cut, mask, b).start()
                    core_copy(m, zz, half, cut, mask).start()

    def finish(m, zz):
        for half, cut in cuts(m):
            order = order_of(half)
            for mask in masks_in_order(half):
                if last_of(order, mask) == nbits - 1:
                    xy_wait(m, zz, half, cut, mask)
                    core_copy(m, zz, half, cut, mask).start()

    def settle(m, zz):
        for half, cut in cuts(m):
            for mask in range(1 << nbits):
                core_wait(m, zz, half, cut, mask)

    def drain(m, zz):
        for half, cut in cuts(m):
            order = order_of(half)
            for mask in range(1 << nbits):
                for b in order[last_of(order, mask) + 1:]:
                    xy_copy(m, zz, half, cut, mask, b).wait_send()
                core_copy(m, zz, half, cut, mask).wait_send()

    def at_distance(k, body):
        for sign in ((-1, 1) if k else (1,)):
            zz = z + sign * k

            @pl.when((zz >= 0) & (zz < n_z))
            def _():
                body(zz)

    def arrive(m, k):
        @pl.when(z - k >= 0)
        def _():
            zz = z - k
            z_copy(m, zz, 1).wait_recv()

            @pl.when(z < n_z - 1)
            def _():
                z_copy(m, zz, 1).start()

            launch(m, zz)

        @pl.when(z + k < n_z)
        def _():
            zz = z + k
            z_copy(m, zz, 0).wait_recv()

            @pl.when(z > 0)
            def _():
                z_copy(m, zz, 0).start()

            launch(m, zz)

    def every_z(m, body):
        if m < FULL:
            def step(zz, _):
                body(m, zz)
                return 0

            lax.fori_loop(0, n_z, step, 0)
        else:
            body(m, z)

    there = [(base + z // 2, 2 * core + s) for s in range(2)]

    def is_here(s):
        return (z // 2 == core) & (2 * core + s == z)

    def token_push(src, dst, send, recv, s):
        return push(src.at[s], dst.at[z % 2], send.at[s], recv.at[z % 2], there[s])

    def tokens_start(src, dst, send, recv):
        for s in range(2):
            @pl.when(is_here(s))
            def _():
                pltpu.make_async_copy(src.at[s], dst.at[z % 2], recv.at[z % 2]).start()

            @pl.when(jnp.logical_not(is_here(s)))
            def _():
                token_push(src, dst, send, recv, s).start()

    def tokens_wait(src, dst, send, recv):
        for i in range(2):
            @pl.when(is_here(i))
            def _():
                pltpu.make_async_copy(src.at[i], dst.at[z % 2], recv.at[z % 2]).wait()

            @pl.when(jnp.logical_not(is_here(i)))
            def _():
                push(dst.at[i], dst.at[i], send.at[i], recv.at[i], there[i]).wait_recv()

    def tokens_drain(src, dst, send, recv):
        for s in range(2):
            @pl.when(jnp.logical_not(is_here(s)))
            def _():
                token_push(src, dst, send, recv, s).wait_send()

    def around(src_of, dst, send, recv):
        return [push(src_of((f + j) % n_f), dst.at[f], send.at[j], recv.at[f], ((f + j) % n_f, z)) for j in range(1, n_f)]

    def around_wait(dst, send, recv):
        for j in range(1, n_f):
            came = (f - j + n_f) % n_f
            push(dst.at[came], dst.at[came], send.at[j], recv.at[came], (came, z)).wait_recv()

    cond_sends = around(lambda to: cblk_ref.at[to], cgot, c_send, c_recv)
    lane_sends = around(lambda to: clane_ref, cond_out, l_send, l_recv)
    mod_sends = around(lambda to: mpart.at[to], mgot, m_send, m_recv)

    for copy in cond_sends + lane_sends:
        copy.start()
    launch_own(adapters)
    tokens_start(x_ref, x_out, x_send, x_recv)
    launch_own(FULL)
    launch_own(0)
    cgot[f] = cblk_ref[f]
    cond_out[f] = clane_ref[...]

    around_wait(cgot, c_send, c_recv)
    k_local = wmod_ref.shape[1]
    everyone = cgot[...].reshape(n_f * 8, cgot.shape[2])[:, :k_local].astype(bf16)
    mpart[...] = (mm(everyone, wmod_ref[0]) + pltpu.roll(mm(everyone, wmod_ref[1]), 2, 0)).reshape(mpart.shape)
    for copy in mod_sends:
        copy.start()
    mgot[f] = mpart[f]

    forward(adapters, z)
    forward(FULL, z)
    for m in (1, 2, 3):
        launch_own(m)
    for m in (FULL + 1, FULL + 2, FULL + 3):
        launch_own(m)
    for k in range(1, n_z):
        arrive(0, k)
        at_distance(k - 1, lambda zz: forward(0, zz))
    for m in (1, 2, 3):
        arrive(m, 1)
        at_distance(0, lambda zz: forward(m, zz))
    at_distance(n_z - 1, lambda zz: forward(0, zz))
    for m in (FULL + 1, FULL + 2, FULL + 3):
        forward(m, z)

    finish(adapters, z)
    settle(adapters, z)
    own_copy(adapters).wait()
    hot2 = hot2_ref[...]
    starts = {}
    offset = 0
    for stream in range(2):
        for index in range(5):
            starts[stream, index] = (offset, offset + fans[index] // n_z)
            offset += fans[index] // n_z + cols[index] // n_z

    def pick_a(stream, index):
        at = starts[stream, index][0]
        return mm_t(hot2, row_ref[at:at + fans[index] // n_z, :]).astype(bf16)

    def pick_b(stream, index, s, put):
        at = starts[stream, index][1]
        count = cols[index] // n_z // NAD
        flat = row_ref[at:at + count, :].astype(f32) * picks_ref[s * NAD:s * NAD + 1, :]
        for k in range(1, NAD):
            begin = at + k * count
            flat = flat + row_ref[begin:begin + count, :].astype(f32) * picks_ref[s * NAD + k:s * NAD + k + 1, :]
        fl_ref[:count, :] = flat
        blocks = count // RANK
        for j in range(blocks):
            put(j * 128, fl_ref[pl.ds(j, RANK, stride=blocks), :].astype(bf16))

    spans_a, spans_b = [], []
    offset = 0
    for index in range(1, 5):
        count = fans[index] // n_z
        picked = pick_a(0, index)
        for s in range(2):
            img_msg[s, :, offset:offset + count] = picked[s * RANK:(s + 1) * RANK]
        spans_a.append((offset, count))
        offset += count
    for index in range(1, 5):
        count = cols[index] // n_z
        for s in range(2):
            def put(at, value, s=s, offset=offset):
                img_msg[s, :, offset + at:offset + at + 128] = value
            pick_b(0, index, s, put)
        spans_b.append((offset, count))
        offset += count

    def img_push(s, side):
        return push(img_msg.at[s], img_got.at[z], i_send.at[s, side], i_recv.at[z], (base + side, 2 * core + s))

    for s in range(2):
        for side in range(2):
            self_here = (side == core) & (2 * core + s == z)

            @pl.when(self_here)
            def _():
                img_got[z] = img_msg[s]

            @pl.when(jnp.logical_not(self_here))
            def _():
                img_push(s, side).start()

    share = width // n_z
    for place_at, (stream, index) in enumerate([(0, 0), (1, 0), (1, 1), (1, 3)]):
        txt_msg[:, place_at * share:(place_at + 1) * share] = pick_a(stream, index)
    for place_at, index in ((4, 2), (5, 4)):
        for s in range(2):
            def put(at, value, s=s, place_at=place_at):
                txt_msg[s * RANK:(s + 1) * RANK, place_at * share + at:place_at * share + at + 128] = value
            pick_b(1, index, s, put)
    txt_got[z] = txt_msg[...]
    ring.start(lambda to: txt_msg, txt_got, t_send, t_recv)
    for ref in txt_a + txt_b:
        ref[...] = jnp.zeros_like(ref)
    for index in (2, 4):
        txt_a[index - 1][:rank2, :] = pick_a(1, index)
    for ref, stream, index in ((txt_b[0], 1, 1), (txt_b[2], 1, 3), (modb_out.at[0], 0, 0), (modb_out.at[1], 1, 0)):
        for s in range(2):
            def put(at, value, ref=ref, s=s):
                ref[s * RANK:(s + 1) * RANK, at:at + 128] = value
            pick_b(stream, index, s, put)

    for m in (1, 2, 3):
        arrive(m, 2)
        at_distance(1, lambda zz: forward(m, zz))

    ring.wait(txt_got, t_send, t_recv)
    for t in range(n_z):
        lanes = slice(t * share, (t + 1) * share)
        got = lambda number: txt_got[t, :, number * share:(number + 1) * share]
        moda_out[0, :, lanes] = got(0)
        moda_out[1, :, lanes] = got(1)
        txt_a[0][:rank2, lanes] = got(2)
        txt_a[2][:rank2, lanes] = got(3)
        txt_b[1][:rank2, lanes] = got(4)
        txt_b[3][:rank2, lanes] = got(5)
    around_wait(mgot, m_send, m_recv)
    mod_sum = mgot[0]
    for j in range(1, n_f):
        mod_sum = mod_sum + mgot[j]
    c8 = c8_ref[...].astype(bf16)
    thin = mm_t(c8, moda_out[0])
    row = lax.broadcasted_iota(jnp.int32, thin.shape, 0)
    middle = (jnp.where(row < 2, thin, mm_t(c8, moda_out[1])) * smask_ref[...]).astype(bf16)
    low = jnp.where(row < 2, middle.astype(f32), 0.0)
    high = jnp.where((row >= 2) & (row < 4), middle.astype(f32), 0.0)
    midm_out[0] = low
    midm_out[1] = high
    own_mod[...] = mod_sum + mm(low.astype(bf16), modb_out[0]) + mm(high.astype(bf16), modb_out[1])

    def mod_push(index, peer):
        return push(own_mod, mod_got.at[core * n_z + z], d_send.at[index], d_recv.at[core * n_z + z], peer)

    for index, peer in enumerate(column):
        mod_push(index, peer).start()
    mod_got[core * n_z + z] = own_mod[...]

    for t in range(n_z):
        @pl.when(jnp.logical_not((z // 2 == core) & (t == z)))
        def _():
            push(img_got.at[t], img_got.at[t], i_send.at[0, 0], i_recv.at[t], (base + z // 2, t)).wait_recv()
    for t in range(n_z):
        for refs_of, spans in ((img_a, spans_a), (img_b, spans_b)):
            for ref, (begin, count) in zip(refs_of, spans):
                ref[:, t * count:(t + 1) * count] = img_got[t, :, begin:begin + count]

    for index, peer in enumerate(column):
        place_at = peer[0] % 2 * n_z + peer[1]
        push(mod_got.at[place_at], mod_got.at[place_at], d_send.at[index], d_recv.at[place_at], peer).wait_recv()
    step = width // 2
    per = own_mod.shape[1] // step
    imod_out[...] = jnp.zeros_like(imod_out)
    tmod_out[...] = jnp.zeros_like(tmod_out)
    for q in range(12):
        t, lanes = q // per, slice(q % per * step, (q % per + 1) * step)
        into = slice(q % 2 * step, (q % 2 + 1) * step)
        here = mod_got[z // 2 * n_z + t]
        imod_out[q // 2:q // 2 + 1, into] = jnp.where(z % 2 == 0, here[0:1, lanes], here[1:2, lanes])
        ours = mod_got[core * n_z + t]
        for s in range(2):
            tmod_out[8 * s + q // 2:8 * s + q // 2 + 1, into] = ours[2 + s:3 + s, lanes]

    own = own_ref[...]
    pick = lambda r: jnp.where(own > 0, tmod_out[r:r + 1, :], tmod_out[8 + r:9 + r, :])
    hat, _inv = norm_rows(xt_ref[...].astype(f32))
    th_out[z] = (hat * (1.0 + pick(1)) + pick(0)).astype(bf16)
    ring.start(lambda to: th_out.at[z], th_out, a_send, a_recv)
    dm_out[z] = (pick(5) * gt_ref[...].astype(f32)).astype(bf16)
    ring.start(lambda to: dm_out.at[z], dm_out, dm_send, dm_recv)
    tokens_wait(x_ref, x_out, x_send, x_recv)
    quarter = x_ref.shape[1]
    for i in range(2):
        def norm(r, _):
            sl = pl.ds(pl.multiple_of(r * ROWS, ROWS), ROWS)
            hat, _inv = norm_rows(x_out[i, sl, :].astype(f32))
            h_out[pl.ds(pl.multiple_of(i * quarter + r * ROWS, ROWS), ROWS), :] = (
                hat * (1.0 + imod_out[1:2, :]) + imod_out[0:1, :]).astype(bf16)
            return 0

        lax.fori_loop(0, quarter // ROWS, norm, 0)
    tokens_start(g_ref, g_out, g_send, g_recv)

    for m in (1, 2, 3):
        arrive(m, 3)
        at_distance(2, lambda zz: forward(m, zz))

    finish(FULL, z)
    settle(FULL, z)
    own_copy(FULL).wait()
    load = pltpu.make_async_copy(outs[FULL], wtxt, tw_sem)
    load.start()
    ring.wait(th_out, a_send, a_recv)
    pad = xt_ref.shape[0]
    h_txt = th_out[...].reshape(n_z * pad, width)
    tmid = (mm_t(h_txt, txt_a[0][...]) * tmask_ref[...]).astype(bf16)
    tmid_out[...] = tmid
    load.wait()
    tq_ref[...] = (mm(h_txt, wtxt[...].reshape(width, wtxt.shape[2])) + mm(tmid, txt_b[0][...])).astype(bf16)
    for s in range(2):
        @pl.when(is_here(s))
        def _():
            copy = pltpu.make_async_copy(tq_ref, theads_out.at[z % 2], q_recv.at[z % 2])
            copy.start()
            copy.wait()

        @pl.when(jnp.logical_not(is_here(s)))
        def _():
            push(tq_ref, theads_out.at[z % 2], q_send.at[s], q_recv.at[z % 2], there[s]).start()

    every_z(0, finish)
    every_z(0, settle)
    own_copy(0).wait()
    mid = mm_t(h_out[...], img_a[0][...]).astype(bf16)
    mid_out[...] = mid
    tn = wtile.shape[3]
    per_half = stage.shape[2] // tn

    def tile_of(n):
        side = 1 - core if n < per_half else core
        return side, side * per_half + n % per_half

    def tile_load(n):
        at = pl.ds(pl.multiple_of(tile_of(n)[1] * tn, 128), tn)
        return pltpu.make_async_copy(outs[0].at[:, :, at], wtile.at[n % 2], w_sem.at[n % 2])

    def heads_push():
        return push(stage.at[0], heads_out.at[core], h_send, h_recv, (partner, z))

    tile_load(0).start()
    for n in range(2 * per_half):
        if n + 1 < 2 * per_half:
            tile_load(n + 1).start()
        tile_load(n).wait()
        at = pl.ds(pl.multiple_of(tile_of(n)[1] * tn, 128), tn)
        lanes = slice(n % per_half * tn, (n % per_half + 1) * tn)
        stage[n // per_half, :, lanes] = (
            mm(h_out[...], wtile[n % 2].reshape(width, tn)) + mm(mid, img_b[0][:, at])).astype(bf16)
        if n == per_half - 1:
            heads_push().start()
    keep = pltpu.make_async_copy(stage.at[1], heads_out.at[core], h_sem)
    keep.start()

    for m in (1, 2, 3):
        at_distance(n_z - 1, lambda zz: forward(m, zz))
    for m in range(total - 1):
        if m not in (0, FULL):
            every_z(m, finish)
    for m in range(total - 1):
        if m not in (0, FULL):
            every_z(m, settle)
            own_copy(m).wait()
    for m in range(total):
        every_z(m, drain)
        if m < FULL:
            def sent(zz, _):
                @pl.when((zz <= z) & (z < n_z - 1))
                def _():
                    z_copy(m, zz, 1).wait_send()

                @pl.when((zz >= z) & (z > 0))
                def _():
                    z_copy(m, zz, 0).wait_send()

                return 0

            lax.fori_loop(0, n_z, sent, 0)
    for copy in cond_sends + lane_sends + mod_sends:
        copy.wait_send()
    around_wait(cond_out, l_send, l_recv)
    ring.drain(lambda to: txt_msg, txt_got, t_send, t_recv)
    ring.drain(lambda to: th_out.at[z], th_out, a_send, a_recv)
    ring.wait(dm_out, dm_send, dm_recv)
    ring.drain(lambda to: dm_out.at[z], dm_out, dm_send, dm_recv)
    for index, peer in enumerate(column):
        mod_push(index, peer).wait_send()
    for s in range(2):
        for side in range(2):
            @pl.when(jnp.logical_not((side == core) & (2 * core + s == z)))
            def _():
                img_push(s, side).wait_send()
    tokens_wait(g_ref, g_out, g_send, g_recv)
    tokens_drain(x_ref, x_out, x_send, x_recv)
    tokens_drain(g_ref, g_out, g_send, g_recv)
    keep.wait()
    heads_push().wait_send()
    push(stage.at[0], heads_out.at[1 - core], h_send, h_recv, (partner, z)).wait_recv()
    for s in range(2):
        @pl.when(jnp.logical_not(is_here(s)))
        def _():
            push(theads_out.at[s], theads_out.at[s], q_send.at[s], q_recv.at[s], there[s]).wait_recv()
            push(tq_ref, theads_out.at[z % 2], q_send.at[s], q_recv.at[z % 2], there[s]).wait_send()


def front(full, part, adapter_rows, x, g, picks, hot2, cond, wmod, x_txt, g_txt, own, tmask, smask, n_f, n_z, fans, cols, cid):
    f32, bf16 = jnp.float32, jnp.bfloat16
    vmem, dma = pltpu.VMEM, pltpu.SemaphoreType.DMA
    shape = jax.ShapeDtypeStruct
    slots, width = cond.shape
    k_local = wmod.shape[1]
    z = lax.axis_index("tp")
    blocks = jnp.pad(jnp.swapaxes(cond.reshape(slots, n_f, k_local), 0, 1), ((0, 0), (0, 6), (0, 256 - k_local)))
    cond8 = jnp.concatenate([cond, cond, jnp.zeros((4, width), f32)])
    lane = jnp.pad(lax.dynamic_slice_in_dim(cond, z * (width // n_z), width // n_z, 1), ((0, 6), (0, 0)))
    chosen = (picks[:, None] == jnp.arange(NAD)[None, :]).astype(f32).reshape(-1, 1)
    smalls = (jnp.broadcast_to(chosen, (slots * NAD, 128)), hot2, blocks, lane, cond8, smask, wmod, x_txt, g_txt, own, tmask)
    args = (*full, *part, adapter_rows, x, g, *smalls)
    any_spec, in_vmem = pl.BlockSpec(memory_space=pl.ANY), pl.BlockSpec(memory_space=vmem)
    rows = 2 * (sum(fans) + sum(cols)) // n_z
    chips = n_f // 2
    nbits = bits_of(chips)
    total = len(full) + len(part) + 1
    pad = x_txt.shape[0]
    img_rows = 2 * x.shape[1]
    cut = cols[0] // n_z
    qkv_part = cols[1] // n_z
    thick = tmask.shape[1]
    rank2 = hot2.shape[0]
    own_a = [fans[1], fans[2] // n_z, fans[3], fans[4] // n_z]
    own_b = [cols[1] // n_z, cols[2], cols[3] // n_z, cols[4]]
    lanes = (sum(fans[1:]) + sum(cols[1:])) // n_z
    share = width // n_z
    outs = [shape((n_f,) + a.shape[:-1] + (a.shape[-1] * (n_z if i < len(full) else 1),), a.dtype) for i, a in enumerate(full + part)]
    in_hbm = len(outs)
    outs += [shape(x.shape, bf16), shape(g.shape, bf16), shape((8, width), f32), shape((16, width), f32)]
    outs += [shape((RANK, n), bf16) for n in fans[1:]] + [shape((RANK, n), bf16) for n in cols[1:]]
    outs += [shape((thick, n), bf16) for n in own_a] + [shape((thick, n), bf16) for n in own_b]
    outs += [shape((2, rank2, width), bf16), shape((2, rank2, cut), bf16), shape((2, 8, rank2), f32), shape((n_f, 8, share), f32), shape((n_z, pad, width), bf16)]
    outs += [shape((img_rows, width), bf16), shape((img_rows, RANK), bf16), shape((2, img_rows, cols[1] // 2), bf16),
             shape((n_z, pad, width), bf16), shape((n_z * pad, thick), bf16), shape((2, n_z * pad, qkv_part), bf16)]
    specs = [any_spec] * in_hbm + [in_vmem, any_spec] + [in_vmem] * (len(outs) - in_hbm - 2)
    specs[len(outs) - 4] = any_spec
    specs[len(outs) - 1] = any_spec
    return pl.pallas_call(
        functools.partial(front_kernel, n_f, n_z, tuple(fans), tuple(cols)),
        out_shape=outs,
        in_specs=[any_spec] * (total + 2) + [in_vmem] * len(smalls),
        out_specs=specs,
        scratch_shapes=[
            vmem((rows, 128), bf16), vmem((cut // NAD, 128), f32), vmem((2, RANK, lanes), bf16), vmem((n_z, RANK, lanes), bf16),
            vmem((rank2, 6 * share), bf16), vmem((n_z, rank2, 6 * share), bf16), vmem((n_f, 8, 256), f32),
            vmem((n_f, 8, cut), f32), vmem((n_f, 8, cut), f32), vmem((8, cut), f32), vmem((2 * n_z, 8, cut), f32),
            vmem((2, n_f, k_local, 768), bf16), vmem((n_f, k_local, qkv_part), bf16), vmem((2, img_rows, cols[1] // 2), bf16),
            vmem((n_z * pad, qkv_part), bf16),
            dma((total, n_z, 2)), dma((total, n_z)), dma((total, n_z, 2, chips, nbits)), dma((total, n_z, 2, chips)),
            dma((total, n_z, 2, chips)), dma((total, n_z, 2, chips)), dma((total,)),
            dma((2,)), dma((2,)), dma((2,)), dma((2,)), dma((n_f,)), dma((n_f,)), dma((n_f,)), dma((n_f,)), dma((n_f,)), dma((n_f,)),
            dma((2, 2)), dma((n_z,)), dma((n_z,)), dma((n_z,)), dma((2 * n_z,)), dma((2 * n_z,)), dma((n_z,)), dma((n_z,)),
            dma((2,)), dma, dma, dma, dma, dma((2,)), dma((2,)), dma((n_z,)), dma((n_z,)),
        ],
        compiler_params=pltpu.CompilerParams(collective_id=cid, has_side_effects=True, vmem_limit_bytes=58 * 1024 * 1024),
        name="front",
    )(*args)

HD = 64
FF = 6144
NAD = 8
RANK = 16
EPS = 1e-06
HIGH = lax.Precision.HIGHEST
F32 = jnp.float32
BF16 = jnp.bfloat16
BOTH = ("fsdp", "tp")


def matmul(left, right):
    return jnp.dot(left, right, preferred_element_type=F32)


def exact(left, right):
    return jnp.dot(left, right, precision=HIGH, preferred_element_type=F32)


def inner_left(left, right):
    return lax.dot_general(left, right, (((0,), (0,)), ((), ())), preferred_element_type=F32)


def inner_right(left, right):
    return lax.dot_general(
        left, right, (((left.ndim - 1,), (right.ndim - 1,)), ((), ())), preferred_element_type=F32
    )


def layer_norm(values):
    center = values - jnp.mean(values, axis=-1, keepdims=True)
    inverse = lax.rsqrt(jnp.mean(center * center, axis=-1, keepdims=True) + EPS)
    return (center * inverse, inverse)


def norm_back(grad_normed, normed, inverse, scale):
    grad_hat = grad_normed * (1.0 + scale)
    return inverse * (
        grad_hat
        - jnp.mean(grad_hat, axis=-1, keepdims=True)
        - normed * jnp.mean(grad_hat * normed, axis=-1, keepdims=True)
    )


def gelu(value):
    return jax.nn.gelu(value, approximate=True)


def gelu_back(value, grad):
    return jax.vjp(gelu, value)[1](grad)[0]


def shards(
    image_tokens,
    text_tokens,
    conditioning,
    text_lengths,
    adapter_index,
    adapters,
    mod_weight,
    qkv_weight,
    out_weight,
    fc1_weight,
    fc2_weight,
    image_cot,
    text_cot,
):
    n_f, n_z = lax.axis_size("fsdp"), lax.axis_size("tp")
    f, z = lax.axis_index("fsdp"), lax.axis_index("tp")
    core = f % 2
    slots, quarter, width = image_tokens.shape
    txt_local = text_tokens.shape[0]
    txt_group = txt_local * n_z
    img_half = 2 * quarter
    img_n = 2 * img_half
    cols = [6 * width, 3 * width, width, FF, width]
    fans = [width, width, width, width, FF]

    def round_pairs(r):
        pairs = []
        for fa in range(n_f):
            for t in range(n_z):
                there = (fa // 2 * 2 + t // 2) * n_z + 2 * (fa % 2) + (r ^ (t % 2))
                pairs.append((fa * n_z + t, there))
        return pairs

    low_bit = z % 2

    def pick(stack, bit):
        return lax.dynamic_index_in_dim(stack, bit, 0, keepdims=False)

    def flip(r):
        return low_bit if r == 0 else 1 - low_bit

    def to_chip(parts):
        got = [lax.ppermute(parts[r], BOTH, round_pairs(r)) for r in range(2)]
        return jnp.where(low_bit == 0, got[0], got[1]), jnp.where(low_bit == 0, got[1], got[0])

    def from_chip(pieces):
        got = []
        for r in range(2):
            mine = jnp.where(flip(r) == 0, pieces[0], pieces[1])
            got.append(lax.ppermute(mine, BOTH, [(b, a) for a, b in round_pairs(r)]))
        return jnp.where(low_bit == 0, got[0], got[1]), jnp.where(low_bit == 0, got[1], got[0])

    def reshard(values):
        return jnp.concatenate(to_chip([pick(values, flip(r)) for r in range(2)]), axis=0)

    def unshard(values):
        return jnp.stack(from_chip([values[:quarter], values[quarter:]]))

    def swap_core(values):
        return lax.ppermute(values, "fsdp", [(i, i ^ 1) for i in range(n_f)])

    def by_core(mine, other, axis):
        first = jnp.where(core == 0, mine, other)
        second = jnp.where(core == 0, other, mine)
        return jnp.concatenate([first, second], axis=axis)

    def z_swap(values, step):
        return lax.ppermute(values, "tp", [(i, i ^ step) for i in range(n_z)])

    def z_order(pieces):
        stack = jnp.stack(pieces)
        return [pick(stack, z ^ a) for a in range(n_z)]

    def z_gather(values):
        return z_order([values] + [z_swap(values, j) for j in range(1, n_z)])

    def z_exchange(blocks):
        return z_order([pick(blocks, z ^ j) if j == 0 else z_swap(pick(blocks, z ^ j), j) for j in range(n_z)])

    def z_scatter(values):
        count = values.shape[0] // n_z
        mine = lax.dynamic_slice_in_dim(values, z * count, count, 0)
        for j in range(1, n_z):
            part = lax.dynamic_slice_in_dim(values, (z ^ j) * count, count, 0)
            mine = mine + z_swap(part.astype(BF16), j).astype(F32)
        return mine

    def to_heads(values):
        half = values.shape[1] // 2
        low, high = values[:, :half], values[:, half:]
        mine = jnp.where(core == 0, low, high)
        return by_core(mine, swap_core(jnp.where(core == 0, high, low)), 0)

    def to_tokens(values):
        low, high = values[:img_half], values[img_half:]
        mine = jnp.where(core == 0, low, high)
        return by_core(mine, swap_core(jnp.where(core == 0, high, low)), 1)

    out_t = jnp.swapaxes(out_weight, 1, 2)
    fc2_t = jnp.swapaxes(fc2_weight, 1, 2)
    local = [qkv_weight, out_t, fc1_weight, fc2_t]
    adapter_rows = lax.optimization_barrier(adapters.reshape(-1, 128)).astype(BF16)
    txt_pad = (txt_local + 15) // 16 * 16

    def padded(values):
        return jnp.pad(values, ((0, txt_pad - txt_local), (0, 0)))

    x_txt_low, g_txt_low = padded(text_tokens), padded(text_cot)
    x_txt = x_txt_low.astype(F32)

    seg_ends = jnp.cumsum(text_lengths[0])
    slot_ids = jnp.arange(slots)

    def owner_of(position):
        segment = jnp.sum((position[:, None] >= seg_ends[None, :]).astype(jnp.int32), axis=1)
        return (segment[:, None] == slot_ids[None, :]).astype(F32)

    def real(owner):
        place = jnp.arange(owner.shape[0]) % txt_pad
        return jnp.where((place < txt_local)[:, None], owner, 0.0)

    def position(rows):
        return rows // txt_pad * txt_local + rows % txt_pad

    txt_rows = jnp.arange(n_z * txt_pad)
    owner_group = real(owner_of(position(txt_rows)))
    owner_local = real(owner_of(z * txt_local + jnp.arange(txt_pad)))
    txt_mask = jnp.repeat(owner_group, RANK, axis=1)
    txt_mask_local = jnp.repeat(owner_local, RANK, axis=1)
    rank_cols = slots * RANK
    seq_mask = jnp.repeat(jnp.eye(slots, dtype=F32), RANK, axis=1)

    def by_group(mine, other):
        return by_core(mine, other, 0)

    column_picks = by_group(adapter_index, swap_core(adapter_index))
    column_count = 2 * slots
    one_hot = (
        jnp.arange(NAD * RANK)[:, None]
        == (column_picks[:, None] * RANK + jnp.arange(RANK)[None, :]).reshape(1, -1)
    ).astype(F32)
    def stretch(stream, index):
        if stream == 0:
            return img_mod[:, index * width : (index + 1) * width]
        return exact(owner_local, txt_mods[:, index * width : (index + 1) * width])

    def collapse(stream, values):
        if stream == 0:
            return jnp.sum(values, axis=0, keepdims=True)
        return exact(owner_local.T, values)

    def share(values):
        return jnp.concatenate(z_gather(values), axis=0)

    def give(values, rank_part):
        got = z_scatter(jnp.concatenate([values, rank_part], axis=1))
        return got[:, :width], (got[:, width:] * txt_mask_local).astype(BF16)

    def lanes(values):
        count = values.shape[1] // n_z
        return lax.dynamic_slice_in_dim(values, z * count, count, 1)

    def project(values, weight, pair, mask, flipped):
        middle = inner_right(values, pair[0])
        if mask is not None:
            middle = middle * mask
        middle = middle.astype(BF16)
        main = inner_right(values, weight) if flipped else matmul(values, weight)
        return middle, main + matmul(middle, pair[1])

    own_hot = (
        jnp.arange(NAD * RANK)[:, None]
        == (adapter_index[:, None] * RANK + jnp.arange(RANK)[None, :]).reshape(1, -1)
    ).astype(F32)
    k_local = mod_weight.shape[1]
    cond_act = jax.nn.silu(conditioning).astype(BF16)
    thick = 128

    def thicker(part):
        return jnp.concatenate([part, jnp.zeros((thick - part.shape[0], part.shape[1]), part.dtype)], axis=0)

    def sign(owner):
        return owner[:, 0:1] - owner[:, 1:2]

    def lanes_pad(mask):
        return jnp.pad(mask, ((0, 0), (0, thick - mask.shape[1])))

    if n_f == 8:
        slot_mask = jnp.pad(jnp.concatenate([seq_mask, seq_mask]), ((0, 4), (0, 0)))
        made = front(
            [w[0] for w in local], [w[1] for w in local], adapter_rows, image_tokens, image_cot,
            adapter_index, own_hot.T.astype(BF16), cond_act.astype(F32), mod_weight, x_txt_low,
            g_txt_low, sign(owner_local), lanes_pad(txt_mask), slot_mask, n_f, n_z, fans, cols, 1,
        )
        made = iter(made)
        take = lambda count: [next(made) for _ in range(count)]
        img_w = [w.reshape(-1, w.shape[-1]) for w in take(4)]
        txt_w = [w.reshape(-1, w.shape[-1]) for w in take(4)]
        x_img, g_img = [v.reshape(-1, width) for v in take(2)]
        img_rows_mod, txt_mod = take(2)
        img_pairs = [None] + list(zip(take(4), take(4)))
        thick_pairs = [None] + list(zip(take(4), take(4)))
        mod_a, mod_b, tmod, cond_own, txt_dm = take(5)
        img_in, img_qkv_mid, img_heads, txt_in, txt_qkv_mid, txt_heads = take(6)
        img_heads = img_heads.reshape(img_n, -1)
        txt_in = txt_in.reshape(-1, width)
        txt_pairs = [None, tuple(part[:rank_cols] for part in thick_pairs[1])]
        img_mod = img_rows_mod[:6].reshape(1, -1)
        txt_mods = txt_mod.reshape(slots, 8, width)[:, :6].reshape(slots, -1)
    else:
        got = gather([w[0] for w in local], [w[1] for w in local] + [adapter_rows], n_f, n_z)
        got = [g.reshape(-1, g.shape[-1]) for g in got]
        img_w, txt_w, row = got[:4], got[4:8], got[8]
        x_img = reshard(image_tokens)
        g_img = reshard(image_cot)
        own_picks = adapter_index

        a_rows = [[None] * 5 for stream in range(2)]
        b_rows = [[None] * 5 for stream in range(2)]
        offset = 0
        for stream in range(2):
            for index in range(5):
                count = fans[index] // n_z
                a_rows[stream][index] = row[offset : offset + count]
                offset += count
                count = cols[index] // n_z
                b_rows[stream][index] = row[offset : offset + count]
                offset += count

        def b_pick(stream, index, pick_index):
            part = b_rows[stream][index]
            count = part.shape[0] // NAD
            return lax.dynamic_slice_in_dim(part, pick_index * count, count, 0).reshape(RANK, -1)

        def a_pick(rows, hot):
            return inner_right(hot.T.astype(BF16), rows).astype(BF16)

        img_a = a_pick(jnp.concatenate(a_rows[0], axis=0), one_hot)
        fan_share = sum(fans) // n_z
        img_a = img_a.reshape(column_count, RANK, fan_share)
        img_b = [
            jnp.concatenate([b_pick(0, index, column_picks[s]) for index in range(1, 5)], axis=1)
            for s in range(column_count)
        ]
        img_msg = jnp.concatenate([img_a, jnp.stack(img_b)], axis=2)
        txt_a_rows = jnp.concatenate(
            [a_rows[0][0], a_rows[1][0], a_rows[1][1], a_rows[1][3]], axis=0
        )
        txt_a = a_pick(txt_a_rows, own_hot).reshape(slots, RANK, -1)
        txt_b_own = [
            [b_pick(stream, index, own_picks[s]) for s in range(slots)]
            for stream, index in [(0, 0), (1, 0), (1, 1), (1, 2), (1, 3), (1, 4)]
        ]
        txt_b_own = [jnp.concatenate(parts, axis=0) for parts in txt_b_own]
        txt_a_own = a_pick(jnp.concatenate([a_rows[1][2], a_rows[1][4]], axis=0), own_hot)
        txt_msg = jnp.concatenate(
            [txt_a.reshape(slots * RANK, -1), txt_b_own[3], txt_b_own[5]], axis=1
        )
        img_got = jnp.stack(z_exchange(img_msg))
        txt_got = jnp.stack(z_gather(txt_msg))

        def join(part):
            return jnp.swapaxes(part, 0, 1).reshape(part.shape[1], -1)

        img_pairs = []
        offset, b_offset = 0, fan_share
        for index in range(5):
            count = fans[index] // n_z
            a_full = join(img_got[:, :, offset : offset + count])
            offset += count
            if index == 0:
                img_pairs.append(None)
                continue
            count = cols[index] // n_z
            b_full = join(img_got[:, :, b_offset : b_offset + count])
            b_offset += count
            img_pairs.append((a_full, b_full))
        txt_full = []
        offset = 0
        for count in [width // n_z] * 6:
            txt_full.append(join(txt_got[:, :, offset : offset + count]))
            offset += count
        mod_a = [txt_full[0], txt_full[1]]
        mod_b = [txt_b_own[0], txt_b_own[1]]
        txt_pairs = [
            None,
            (txt_full[2], txt_b_own[2]),
            (txt_a_own[:, : width // n_z], txt_full[4]),
            (txt_full[3], txt_b_own[4]),
            (txt_a_own[:, width // n_z :], txt_full[5]),
        ]

        cond_all = lax.all_gather(cond_act, "fsdp", axis=0, tiled=True)
        cond_slice = lax.dynamic_slice_in_dim(cond_all, f * k_local, k_local, 1)
        mod_part = jnp.stack([matmul(cond_slice, mod_weight[stream]) for stream in range(2)], axis=1)
        mod_part = lax.psum_scatter(mod_part, "fsdp", scatter_dimension=0, tiled=True)
        mod_mid = []
        mod_terms = []
        for stream in range(2):
            middle = (inner_right(cond_act, mod_a[stream]) * seq_mask).astype(BF16)
            mod_mid.append(middle)
            mod_terms.append(mod_part[:, stream] + matmul(middle, mod_b[stream]))
        mods = jnp.concatenate(z_gather(jnp.stack(mod_terms, axis=1)), axis=2)
        img_mods = by_group(mods[:, 0], swap_core(mods[:, 0]))
        img_mod = lax.dynamic_slice_in_dim(img_mods, z, 1, 0)
        txt_mods = mods[:, 1]

        img_rows_mod = jnp.concatenate([img_mod.reshape(6, width), jnp.zeros((2, width), F32)], axis=0)
        txt_mod = jnp.pad(txt_mods.reshape(slots, 6, width), ((0, 0), (0, 2), (0, 0))).reshape(-1, width)
        thick_pairs = [None] + [tuple(thicker(part) for part in txt_pairs[index]) for index in range(1, 5)]
        norm_first = [layer_norm(v.astype(F32)) for v in (x_img, x_txt)]
        heads_in = [
            (norm_first[s][0] * (1.0 + stretch(s, 1)) + stretch(s, 0)).astype(BF16) for s in range(2)
        ]

        txt_in = share(heads_in[1])
        txt_qkv_mid, txt_qkv = project(txt_in, txt_w[0], txt_pairs[1], txt_mask, False)
        img_qkv_mid, img_qkv = project(heads_in[0], img_w[0], img_pairs[1], None, False)
        txt_qkv, img_qkv = txt_qkv.astype(BF16), img_qkv.astype(BF16)
        img_heads = to_heads(img_qkv)
        txt_heads = jnp.stack(to_chip([txt_qkv, txt_qkv]))
        img_in = heads_in[0]
        txt_dm = jnp.stack(z_gather((stretch(1, 5) * g_txt_low.astype(F32)).astype(BF16)))

    inputs = [x_img.astype(F32), x_txt]
    norm_one = [layer_norm(values) for values in inputs]
    lengths = by_group(text_lengths[0:1], swap_core(text_lengths[0:1]))
    chip_lengths = jnp.cumsum(lax.dynamic_index_in_dim(lengths, z // slots, 0, keepdims=False))
    chip_slot = z % slots
    chip_segment = jnp.sum(
        (position(txt_rows)[:, None] >= chip_lengths[None, :]).astype(jnp.int32),
        axis=1,
        keepdims=True,
    )
    chip_owner = (chip_segment == chip_slot) & (txt_rows % txt_pad < txt_local)[:, None]
    bias = jnp.where(chip_owner, 0.0, -1e30).astype(F32)
    o_img, o_txt, lse = attend(img_heads, txt_heads, bias, HD)

    def txt_home(values):
        got = from_chip([values[0], values[1]])
        return jnp.where(owner_group[:, 0:1] > 0, got[0], jnp.where(owner_group[:, 1:2] > 0, got[1], 0))

    attended = to_tokens(o_img)
    (img_branch, img_after, img_mlp, img_pre, img_result, *img_mids, img_gate, txt_mlp, txt_att, txt_after, txt_branch) = both_fwd(
        attended, x_img, g_img, img_rows_mod, img_w[1], img_pairs[2], img_pairs[3], img_w[2], img_pairs[4], img_w[3],
        o_txt, x_txt_low, txt_mod, sign(owner_group), sign(owner_local), lanes_pad(txt_mask_local), txt_w[1], thick_pairs[2],
        n_z, 2,
    )
    made = both_back(
        g_img, img_after, img_branch, img_mlp, attended, img_rows_mod, img_pre, img_w[3], img_pairs[4], img_w[2], img_pairs[3],
        img_w[1], img_pairs[2], img_mids, g_txt_low, txt_after, txt_branch, txt_mod, sign(owner_local), lanes_pad(txt_mask),
        lanes_pad(txt_mask_local), txt_mlp, txt_att, txt_dm, txt_w[1], txt_w[2], txt_w[3], thick_pairs[2], thick_pairs[3],
        thick_pairs[4], n_z, 4,
    )
    img_grad_after, img_grad_att, img_sums, *sides = made[:9]
    txt_result, txt_grad_after, do_txt, txt_sums, *txt_sides = made[9:]
    txt_sides = [part[:rank_cols] for part in txt_sides]
    txt_sum_rows = txt_sums
    txt_sums = txt_sums.reshape(4, slots, width)
    image_out = unshard(img_result)

    grads = [[None] * 5 for stream in range(2)]

    def project_back(grad, weight, pair, mask, flipped):
        middle = inner_right(grad, pair[1])
        if mask is not None:
            middle = middle * mask
        middle = middle.astype(BF16)
        main = matmul(grad, weight) if flipped else inner_right(grad, weight)
        return middle, main + matmul(middle, pair[0])

    grads[0][4] = (sides[0], sides[3])
    grads[0][3] = (sides[2], sides[1])
    grads[0][2] = (sides[4], sides[5])
    mod_parts = [[None] * 6 for stream in range(2)]
    for place in range(4):
        mod_parts[1][2 + place] = txt_sums[place]
    grads[1][2] = (txt_sides[0], txt_sides[1])
    grads[1][3] = (txt_sides[2], txt_sides[3])
    grads[1][4] = (txt_sides[4], txt_sides[5])
    img_sum_rows = img_sums
    img_sums = jnp.sum(jnp.concatenate([img_sums, img_gate]).reshape(4, 8, width), axis=1)
    for place in range(4):
        mod_parts[0][2 + place] = img_sums[place : place + 1]
    grad_after = [img_grad_after, txt_grad_after]

    do_img = to_heads(img_grad_att)
    d_img, d_txt = attend_back(img_heads, txt_heads, bias, do_img, do_txt, lse, HD)
    if n_f == 8:
        sides_of = lambda stream, side: [grads[stream][index][side] for index in range(2, 5)]
        smalls = (
            x_img, img_grad_after, img_in, img_rows_mod, img_qkv_mid, *img_pairs[1], img_sum_rows, img_gate,
            x_txt_low, txt_grad_after, txt_in.reshape(n_z, txt_pad, width), txt_mod, sign(owner_group), sign(owner_local),
            lanes_pad(txt_mask_local), txt_qkv_mid, txt_w[0], *thick_pairs[1], txt_sum_rows,
        )
        image_low, txt_grad, cond_slices, mod_rank, shard = tail(
            d_img.reshape(2, img_half, -1), d_txt, img_w[0].reshape(n_f, k_local, -1), smalls,
            sides_of(0, 0), sides_of(0, 1), sides_of(1, 0), sides_of(1, 1),
            one_hot.T.astype(BF16), own_hot.T.astype(BF16), mod_weight, mod_b, tmod, cond_own, slot_mask,
            n_f, n_z, fans, cols, 3,
        )
        image_grad = image_low.astype(F32)
        cond_rows = jnp.swapaxes(cond_slices[:, :slots, :k_local], 0, 1).reshape(slots, width)
        for s in range(2):
            cond_rows = cond_rows + matmul(mod_rank[2 * s : 2 * s + 2].astype(BF16), mod_a[s])
        cond_grad = jax.vjp(jax.nn.silu, conditioning)[1](cond_rows)[0]
        adapter_grad = shard.reshape(1, -1)
        return (image_out, txt_result[:txt_local], image_grad, txt_grad[:txt_local], cond_grad, adapter_grad)
    img_grad_qkv = to_tokens(d_img)
    txt_grad_qkv = txt_home(d_txt)

    img_back_mid, img_grad_norm = project_back(img_grad_qkv, img_w[0], img_pairs[1], None, False)
    grads[0][1] = (inner_left(img_back_mid, img_in), inner_left(img_qkv_mid, img_grad_qkv))
    txt_grad_norm, txt_qkv_back = give(
        inner_right(txt_grad_qkv, txt_w[0]), inner_right(txt_grad_qkv, txt_pairs[1][1])
    )
    txt_grad_norm = txt_grad_norm + matmul(txt_qkv_back, txt_pairs[1][0])
    grads[1][1] = (
        inner_left(share(txt_qkv_back), lanes(txt_in)),
        inner_left(txt_qkv_mid, txt_grad_qkv),
    )
    grad_norm = [img_grad_norm, txt_grad_norm]
    grad_inputs = []
    for s in range(2):
        grad_inputs.append(
            grad_after[s]
            + norm_back(grad_norm[s], norm_one[s][0], norm_one[s][1], stretch(s, 1))
        )
        mod_parts[s][0] = collapse(s, grad_norm[s])
        mod_parts[s][1] = collapse(s, grad_norm[s] * norm_one[s][0])
    img_dmod = jnp.concatenate(mod_parts[0], axis=1)
    txt_dmod = jnp.concatenate(mod_parts[1], axis=1)
    image_grad = unshard(grad_inputs[0].astype(BF16)).astype(F32)

    img_dmod = (img_dmod + swap_core(img_dmod)).astype(BF16)
    def lane_blocks(values):
        return jnp.swapaxes(values.reshape(values.shape[0], n_z, -1), 0, 1)

    img_dmods = jnp.concatenate(z_exchange(lane_blocks(img_dmod)), axis=0)
    img_dmods = lax.dynamic_slice_in_dim(img_dmods, core * slots, slots, 0)
    txt_dmods = sum(z_exchange(lane_blocks(txt_dmod))).astype(BF16)
    dmods = jnp.stack([img_dmods, txt_dmods], axis=1)
    dmods_all = lax.all_gather(dmods, "fsdp", axis=0, tiled=True)
    cond_part = sum(inner_right(dmods_all[:, s], mod_weight[s]) for s in range(2))
    mod_back = [inner_right(dmods[:, s], mod_b[s]) for s in range(2)]
    cond_part = cond_part.reshape(-1, width // n_f)
    joined = jnp.concatenate([cond_part.reshape(-1), jnp.stack(mod_back).reshape(-1)])
    joined = sum(z_gather(joined))
    cond_slices = joined[: cond_part.size].reshape(n_f, -1, width // n_f)
    mod_rank = joined[cond_part.size :].reshape(2, slots, -1)
    cond_rows = lax.all_to_all(cond_slices, "fsdp", 0, 2, tiled=True)[0]
    for s in range(2):
        back_mid = (mod_rank[s] * seq_mask).astype(BF16)
        cond_rows = cond_rows + matmul(back_mid, mod_a[s])
        grads[s][0] = (inner_left(back_mid, lanes(cond_act)), inner_left(mod_mid[s], dmods[:, s]))
    cond_grad = jax.vjp(jax.nn.silu, conditioning)[1](cond_rows)[0]

    def spread(values):
        return jnp.swapaxes(values.reshape(RANK, n_z, -1), 0, 1)

    img_rows = {}
    for group in ((2, 3, 4), (1,)):
        parts = [spread(grads[0][index][side]) for side in range(2) for index in group]
        parts = jnp.concatenate(z_exchange(jnp.concatenate(parts, axis=2)), axis=0)
        offset = 0
        for side, sizes in enumerate((fans, cols)):
            for index in group:
                count = sizes[index] // n_z
                img_rows[side, index] = parts[:, offset : offset + count]
                offset += count
    flat = []
    for stream in range(2):
        for index in range(5):
            if stream == 0 and index > 0:
                part_a, part_b = img_rows[0, index], img_rows[1, index]
                hot = one_hot
            else:
                part_a, part_b = grads[stream][index]
                hot = own_hot
            flat.append(
                lax.dot_general(
                    part_a, hot, (((0,), (1,)), ((), ())),
                    precision=HIGH, preferred_element_type=F32,
                )
            )
            flat.append(exact(hot, part_b).reshape(-1, 128))
    total = jnp.concatenate(flat, axis=0).reshape(n_f, -1, 128)
    step = 1
    while step < n_f:
        bit = (f // step) % 2
        pairs = total.reshape((-1, 2) + total.shape[1:])
        keep = lax.dynamic_index_in_dim(pairs, bit, 1, keepdims=False)
        send = lax.dynamic_index_in_dim(pairs, 1 - bit, 1, keepdims=False)
        sent = lax.ppermute(send.astype(BF16), "fsdp", [(i, i ^ step) for i in range(n_f)])
        total = keep + sent.astype(F32)
        step *= 2
    adapter_grad = total.reshape(1, -1)
    return (
        image_out, txt_result[:txt_local], image_grad, grad_inputs[1][:txt_local], cond_grad, adapter_grad
    )


def solution(mesh):
    return jax.shard_map(
        shards,
        mesh=mesh,
        in_specs=(
            P("fsdp", "tp", None),
            P(("fsdp", "tp"), None),
            P("fsdp", None),
            P("fsdp", None),
            P("fsdp"),
            P("tp", "fsdp"),
            P(None, "fsdp", "tp"),
            P(None, "fsdp", "tp"),
            P(None, "tp", "fsdp"),
            P(None, "fsdp", "tp"),
            P(None, "tp", "fsdp"),
            P("fsdp", "tp", None),
            P(("fsdp", "tp"), None),
        ),
        out_specs=(
            P("fsdp", "tp", None),
            P(("fsdp", "tp"), None),
            P("fsdp", "tp", None),
            P(("fsdp", "tp"), None),
            P("fsdp", None),
            P("tp", "fsdp"),
        ),
        check_vma=False,
    )
```

```python
import functools

import jax
import jax.numpy as jnp
from jax import lax
from jax.experimental import pallas as pl
from jax.experimental.pallas import tpu as pltpu
from jax.sharding import PartitionSpec as P

MESH = pl.DeviceIdType.MESH

def bits_of(count):
    return max(count.bit_length() - 1, 0)

def halves(width):
    tiles = width // 128
    first = (tiles + 1) // 2 * 128
    return [(0, first), (first, width - first)]

def gather_kernel(n_f, n_z, full_count, part_count, *refs):
    total = full_count + part_count
    ins, outs = refs[:total], refs[total:2 * total]
    z_send, z_recv, xy_send, xy_recv, core_send, core_recv, own_sem = refs[2 * total:]
    f = lax.axis_index("fsdp")
    z = lax.axis_index("tp")
    chip, core = f // 2, f % 2
    chips = n_f // 2
    nbits = bits_of(chips)
    partner = chip * 2 + (1 - core)

    def peer_of(mask):
        other = 0
        for bit in range(nbits):
            have = (chip // (1 << bit)) % 2
            want = 1 - have if (mask >> bit) & 1 else have
            other = other + want * (1 << bit)
        return other * 2 + core

    barrier = pltpu.get_barrier_semaphore()
    for bit in range(nbits):
        pl.semaphore_signal(barrier, inc=1, device_id=(peer_of(1 << bit), z), device_id_type=MESH)
    pl.semaphore_signal(barrier, inc=1, device_id=(partner, z), device_id_type=MESH)
    @pl.when(z > 0)
    def _():
        pl.semaphore_signal(barrier, inc=1, device_id=(f, z - 1), device_id_type=MESH)
    @pl.when(z < n_z - 1)
    def _():
        pl.semaphore_signal(barrier, inc=1, device_id=(f, z + 1), device_id_type=MESH)
    peers = nbits + 1 + (z > 0).astype(jnp.int32) + (z < n_z - 1).astype(jnp.int32)
    pl.semaphore_wait(barrier, peers)

    def width(m):
        return ins[m].shape[-1]

    def place(m, who, zz, off=0, w=None):
        w = width(m) if w is None else w
        if m < full_count:
            return outs[m].at[who, :, pl.ds(pl.multiple_of(zz * width(m) + off, 128), w)]
        if w == width(m):
            return outs[m].at[who]
        return outs[m].at[who, :, pl.ds(off, w)]

    def piece(m, off, w):
        return ins[m] if w == width(m) else ins[m].at[:, pl.ds(off, w)]

    def remote(src, dst, ssem, rsem, dev):
        return pltpu.make_async_remote_copy(src_ref=src, dst_ref=dst, send_sem=ssem, recv_sem=rsem, device_id=dev, device_id_type=MESH)

    def order_of(half):
        order = list(range(nbits))
        return order if half == 0 else order[::-1]

    def cuts(m):
        if width(m) >= 256:
            return list(enumerate(halves(width(m))))
        return [(m % 2, (0, width(m)))]

    def slot(m, zz):
        return zz if m < full_count else 0

    def xy_copy(m, zz, half, cut, mask, bit, own_piece=False):
        off, w = cut
        who = peer_of(mask)
        source = piece(m, off, w) if own_piece and mask == 0 else place(m, who, zz, off, w)
        return remote(source, place(m, who, zz, off, w),
                      xy_send.at[m, slot(m, zz), half, mask, bit], xy_recv.at[m, slot(m, zz), half, mask | (1 << bit)],
                      (peer_of(1 << bit), z))

    def xy_wait(m, zz, half, cut, mask):
        off, w = cut
        who = peer_of(mask)
        remote(place(m, who, zz, off, w), place(m, who, zz, off, w), xy_send.at[m, slot(m, zz), half, 0, 0],
               xy_recv.at[m, slot(m, zz), half, mask], (partner, z)).wait_recv()

    def core_copy(m, zz, half, cut, mask, own_piece=False):
        off, w = cut
        who = peer_of(mask)
        source = piece(m, off, w) if own_piece and mask == 0 else place(m, who, zz, off, w)
        return remote(source, place(m, who, zz, off, w),
                      core_send.at[m, slot(m, zz), half, mask], core_recv.at[m, slot(m, zz), half, mask], (partner, z))

    def core_wait_recv(m, zz, half, cut, mask):
        off, w = cut
        who = peer_of(mask) - core + (1 - core)
        remote(place(m, who, zz, off, w), place(m, who, zz, off, w),
               core_send.at[m, slot(m, zz), half, mask], core_recv.at[m, slot(m, zz), half, mask], (partner, z)).wait_recv()

    def own(m):
        return pltpu.make_async_copy(ins[m], place(m, f, z), own_sem.at[m])

    def z_copy(m, zz, up, own_piece=False):
        return remote(ins[m] if own_piece else place(m, f, zz), place(m, f, zz), z_send.at[m, zz, up], z_recv.at[m, zz], (f, z + 1 if up else z - 1))

    def launch(m, zz, own_piece=False):
        for half, cut in cuts(m):
            for bit in order_of(half):
                xy_copy(m, zz, half, cut, 0, bit, own_piece).start()
            core_copy(m, zz, half, cut, 0, own_piece).start()

    def masks_in_order(half):
        order = order_of(half)
        def rank(mask):
            return [1 if (mask >> b) & 1 else 0 for b in reversed(order)]
        return sorted(range(1, 1 << nbits), key=rank)

    def forward(m, zz):
        for half, cut in cuts(m):
            order = order_of(half)
            for mask in masks_in_order(half):
                last = max(i for i, b in enumerate(order) if (mask >> b) & 1)
                if last == nbits - 1:
                    continue
                xy_wait(m, zz, half, cut, mask)
                for b in order[last + 1:]:
                    xy_copy(m, zz, half, cut, mask, b).start()
                core_copy(m, zz, half, cut, mask).start()

    def finish(m, zz):
        for half, cut in cuts(m):
            order = order_of(half)
            for mask in masks_in_order(half):
                last = max(i for i, b in enumerate(order) if (mask >> b) & 1)
                if last == nbits - 1:
                    xy_wait(m, zz, half, cut, mask)
                    core_copy(m, zz, half, cut, mask).start()

    def drain(m, zz):
        for half, cut in cuts(m):
            order = order_of(half)
            for mask in [0] + masks_in_order(half):
                last = max([i for i, b in enumerate(order) if (mask >> b) & 1], default=-1)
                for b in order[last + 1:]:
                    xy_copy(m, zz, half, cut, mask, b).wait_send()
                core_copy(m, zz, half, cut, mask).wait_send()
                core_wait_recv(m, zz, half, cut, mask)

    for m in range(total):
        own(m).start()
    for m in range(total):
        if m < full_count:
            @pl.when(z < n_z - 1)
            def _():
                z_copy(m, z, 1, True).start()
            @pl.when(z > 0)
            def _():
                z_copy(m, z, 0, True).start()
        launch(m, z, True)
    for m in range(full_count, total):
        forward(m, z)
    for k in range(1, n_z):
        for m in range(full_count):
            @pl.when(z - k >= 0)
            def _():
                zz = z - k
                z_copy(m, zz, 1).wait_recv()
                @pl.when(z < n_z - 1)
                def _():
                    z_copy(m, zz, 1).start()
                launch(m, zz)
            @pl.when(z + k < n_z)
            def _():
                zz = z + k
                z_copy(m, zz, 0).wait_recv()
                @pl.when(z > 0)
                def _():
                    z_copy(m, zz, 0).start()
                launch(m, zz)
            for sign in ((-1, 1) if k > 1 else (1,)):
                zz = z + sign * (k - 1)
                @pl.when((zz >= 0) & (zz < n_z))
                def _():
                    forward(m, zz)
    for m in range(full_count):
        for sign in (-1, 1):
            zz = z + sign * (n_z - 1)
            @pl.when((zz >= 0) & (zz < n_z))
            def _():
                forward(m, zz)
    for m in range(total):
        if m < full_count:
            def body(zz, _):
                finish(m, zz)
                return 0
            lax.fori_loop(0, n_z, body, 0)
        else:
            finish(m, z)
    for m in range(total):
        own(m).wait()
        if m < full_count:
            def body(zz, _):
                drain(m, zz)
                @pl.when((zz <= z) & (z < n_z - 1))
                def _():
                    z_copy(m, zz, 1).wait_send()
                @pl.when((zz >= z) & (z > 0))
                def _():
                    z_copy(m, zz, 0).wait_send()
                return 0
            lax.fori_loop(0, n_z, body, 0)
        else:
            drain(m, z)

def gather(full, part, n_f, n_z, cid=1):
    arrays = list(full) + list(part)
    total = len(arrays)
    if n_f > 8:
        rows = [lax.all_gather(a, "fsdp", axis=0, tiled=True) for a in arrays]
        return [
            lax.all_gather(a, "tp", axis=1, tiled=True) if i < len(full) else a
            for i, a in enumerate(rows)
        ]
    chips = n_f // 2
    nbits = bits_of(chips)
    shapes = [jax.ShapeDtypeStruct((n_f,) + a.shape[:-1] + (a.shape[-1] * (n_z if i < len(full) else 1),), a.dtype) for i, a in enumerate(arrays)]
    dma = pltpu.SemaphoreType.DMA
    return pl.pallas_call(
        functools.partial(gather_kernel, n_f, n_z, len(full), len(part)),
        out_shape=shapes,
        in_specs=[pl.BlockSpec(memory_space=pl.ANY)] * total,
        out_specs=[pl.BlockSpec(memory_space=pl.ANY)] * total,
        scratch_shapes=[
            dma((total, n_z, 2)), dma((total, n_z)),
            dma((total, n_z, 2, chips, max(nbits, 1))), dma((total, n_z, 2, chips)),
            dma((total, n_z, 2, chips)), dma((total, n_z, 2, chips)), dma((total,)),
        ],
        compiler_params=pltpu.CompilerParams(collective_id=cid, has_side_effects=True),
        name="weight_gather",
    )(*arrays)

def dots(left, right, lc, rc):
    return lax.dot_general(left, right, (((lc,), (rc,)), ((), ())), preferred_element_type=jnp.float32)

def attend_block(q, ki, vi, kt, vt, bias):
    q = q * jnp.bfloat16(0.125)
    si = dots(ki, q, 1, 1)
    st = dots(kt, q, 1, 1) + bias
    top = jnp.maximum(jnp.max(si, axis=0, keepdims=True), jnp.max(st, axis=0, keepdims=True))
    ei = jnp.exp(si - top)
    et = jnp.exp(st - top)
    total = jnp.sum(ei, axis=0, keepdims=True) + jnp.sum(et, axis=0, keepdims=True)
    o = dots(vi, ei.astype(jnp.bfloat16), 0, 0) + dots(vt, et.astype(jnp.bfloat16), 0, 0)
    return (o / total).T.astype(jnp.bfloat16), top + jnp.log(total)


def attend_kernel(hd, bq, img_ref, txt_ref, bias_ref, oi_ref, ot_ref, lse_ref):
    img_n, txt_n = img_ref.shape[0], txt_ref.shape[1]
    heads = img_ref.shape[1] // (3 * hd)
    bias = bias_ref[...]
    for h in range(heads):
        base = 3 * hd * h
        ki = img_ref[:, base + hd:base + 2 * hd]
        vi = img_ref[:, base + 2 * hd:base + 3 * hd]
        kt = txt_ref[0, :, base + hd:base + 2 * hd]
        vt = txt_ref[0, :, base + 2 * hd:base + 3 * hd]

        def block(q):
            q = q * jnp.bfloat16(0.125)
            si = dots(ki, q, 1, 1)
            st = dots(kt, q, 1, 1) + bias
            top = jnp.maximum(jnp.max(si, axis=0, keepdims=True), jnp.max(st, axis=0, keepdims=True))
            ei = jnp.exp(si - top)
            et = jnp.exp(st - top)
            total = jnp.sum(ei, axis=0, keepdims=True) + jnp.sum(et, axis=0, keepdims=True)
            o = dots(vi, ei.astype(jnp.bfloat16), 0, 0) + dots(vt, et.astype(jnp.bfloat16), 0, 0)
            return (o / total).T.astype(jnp.bfloat16), top + jnp.log(total)

        for i in range(img_n // bq):
            o, lse = block(img_ref[i * bq:(i + 1) * bq, base:base + hd])
            oi_ref[i * bq:(i + 1) * bq, h * hd:(h + 1) * hd] = o
            lse_ref[0, h:h + 1, i * bq:(i + 1) * bq] = lse
        o, lse = block(txt_ref[0, :, base:base + hd])
        ot_ref[0, :, h * hd:(h + 1) * hd] = o
        lse_ref[0, h:h + 1, img_n:img_n + txt_n] = lse

def attend(img, txt, bias, hd, bq=512):
    img_n, cols = img.shape
    parts, txt_n, _ = txt.shape
    pairs = cols // (6 * hd)
    per = pairs // parts
    return pl.pallas_call(
        functools.partial(attend_kernel, hd, bq),
        grid=(pairs,),
        in_specs=[
            pl.BlockSpec((img_n, 6 * hd), lambda i: (0, i)),
            pl.BlockSpec((1, txt_n, 6 * hd), lambda i: (i // per, 0, i % per)),
            pl.BlockSpec((txt_n, 1), lambda i: (0, 0)),
        ],
        out_specs=[
            pl.BlockSpec((img_n, 2 * hd), lambda i: (0, i)),
            pl.BlockSpec((1, txt_n, 2 * hd), lambda i: (i // per, 0, i % per)),
            pl.BlockSpec((1, 2, img_n + txt_n), lambda i: (i, 0, 0)),
        ],
        out_shape=[
            jax.ShapeDtypeStruct((img_n, pairs * 2 * hd), jnp.bfloat16),
            jax.ShapeDtypeStruct((parts, txt_n, per * 2 * hd), jnp.bfloat16),
            jax.ShapeDtypeStruct((pairs, 2, img_n + txt_n), jnp.float32),
        ],
        compiler_params=pltpu.CompilerParams(vmem_limit_bytes=48 * 1024 * 1024),
        name="attend",
    )(img, txt, bias)

def attend_back_kernel(hd, bq, img_ref, txt_ref, bias_ref, doi_ref, dot_ref, lse_ref, di_ref, dt_ref, acc_i, acc_t):
    img_n, txt_n = img_ref.shape[0], txt_ref.shape[1]
    heads = img_ref.shape[1] // (3 * hd)
    bias = bias_ref[...]
    for h in range(heads):
        base = 3 * hd * h
        ki = img_ref[:, base + hd:base + 2 * hd]
        vi = img_ref[:, base + 2 * hd:base + 3 * hd]
        kt = txt_ref[0, :, base + hd:base + 2 * hd]
        vt = txt_ref[0, :, base + 2 * hd:base + 3 * hd]

        def block(q, do, lse, first):
            q = q * jnp.bfloat16(0.125)
            pi = jnp.exp(dots(ki, q, 1, 1) - lse)
            pt = jnp.exp(dots(kt, q, 1, 1) + bias - lse)
            dwi = dots(vi, do, 1, 1)
            dwt = dots(vt, do, 1, 1)
            delta = jnp.sum(pi * dwi, axis=0, keepdims=True) + jnp.sum(pt * dwt, axis=0, keepdims=True)
            dsi = (pi * (dwi - delta)).astype(jnp.bfloat16)
            dst = (pt * (dwt - delta)).astype(jnp.bfloat16)
            dvi = dots(pi.astype(jnp.bfloat16), do, 1, 0)
            dvt = dots(pt.astype(jnp.bfloat16), do, 1, 0)
            dki = dots(dsi, q, 1, 0)
            dkt = dots(dst, q, 1, 0)
            if first:
                acc_i[0], acc_i[1], acc_t[0], acc_t[1] = dki, dvi, dkt, dvt
            else:
                acc_i[0] += dki
                acc_i[1] += dvi
                acc_t[0] += dkt
                acc_t[1] += dvt
            dq = dots(ki, dsi, 0, 0) + dots(kt, dst, 0, 0)
            return (dq.T * 0.125).astype(jnp.bfloat16)

        for i in range(img_n // bq):
            rows = slice(i * bq, (i + 1) * bq)
            di_ref[rows, base:base + hd] = block(
                img_ref[rows, base:base + hd], doi_ref[rows, h * hd:(h + 1) * hd], lse_ref[0, h:h + 1, rows], i == 0)
        grad = jnp.where(bias < 0, 0.0, dot_ref[0, :, h * hd:(h + 1) * hd].astype(jnp.float32)).astype(jnp.bfloat16)
        dt_ref[0, :, base:base + hd] = block(
            txt_ref[0, :, base:base + hd], grad, lse_ref[0, h:h + 1, img_n:img_n + txt_n], False)
        di_ref[:, base + hd:base + 2 * hd] = acc_i[0].astype(jnp.bfloat16)
        di_ref[:, base + 2 * hd:base + 3 * hd] = acc_i[1].astype(jnp.bfloat16)
        dt_ref[0, :, base + hd:base + 2 * hd] = acc_t[0].astype(jnp.bfloat16)
        dt_ref[0, :, base + 2 * hd:base + 3 * hd] = acc_t[1].astype(jnp.bfloat16)

def attend_back(img, txt, bias, doi, dot, lse, hd, bq=512):
    img_n, cols = img.shape
    parts, txt_n, _ = txt.shape
    pairs = cols // (6 * hd)
    per = pairs // parts
    wide = pl.BlockSpec((img_n, 6 * hd), lambda i: (0, i))
    wide_t = pl.BlockSpec((1, txt_n, 6 * hd), lambda i: (i // per, 0, i % per))
    return pl.pallas_call(
        functools.partial(attend_back_kernel, hd, bq),
        grid=(pairs,),
        in_specs=[
            wide, wide_t,
            pl.BlockSpec((txt_n, 1), lambda i: (0, 0)),
            pl.BlockSpec((img_n, 2 * hd), lambda i: (0, i)),
            pl.BlockSpec((1, txt_n, 2 * hd), lambda i: (i // per, 0, i % per)),
            pl.BlockSpec((1, 2, img_n + txt_n), lambda i: (i, 0, 0)),
        ],
        out_specs=[wide, wide_t],
        out_shape=[jax.ShapeDtypeStruct(img.shape, jnp.bfloat16), jax.ShapeDtypeStruct(txt.shape, jnp.bfloat16)],
        scratch_shapes=[pltpu.VMEM((2, img_n, hd), jnp.float32), pltpu.VMEM((2, txt_n, hd), jnp.float32)],
        compiler_params=pltpu.CompilerParams(vmem_limit_bytes=48 * 1024 * 1024),
        name="attend_back",
    )(img, txt, bias, doi, dot, lse)

ROWS = 64


def mm(left, right):
    return dots(left, right, 1, 0)


def mm_t(left, right):
    return dots(left, right, 1, 1)


def t_mm(left, right):
    return dots(left, right, 0, 0)


def gelu_parts(u):
    scale = 0.7978845608028654
    square = u * u
    tanh = jnp.tanh(scale * (u + 0.044715 * u * square))
    half = 0.5 * (1.0 + tanh)
    slope = half + 0.5 * u * (1.0 - tanh * tanh) * (scale * (1.0 + 3 * 0.044715 * square))
    return u * half, slope


def norm_rows(v):
    center = v - jnp.mean(v, axis=-1, keepdims=True)
    inverse = lax.rsqrt(jnp.mean(center * center, axis=-1, keepdims=True) + 1e-06)
    return center * inverse, inverse


def column_peers(n_z):
    f, z = lax.axis_index("fsdp"), lax.axis_index("tp")
    core = f % 2
    base = f - core
    peers = [(f, (z + j) % n_z) for j in range(1, n_z)]
    peers += [(base + 1 - core, (z + j) % n_z) for j in range(n_z)]
    return f, z, core, base, peers


def meet(peers):
    barrier = pltpu.get_barrier_semaphore()
    for peer in peers:
        pl.semaphore_signal(barrier, inc=1, device_id=peer, device_id_type=MESH)
    pl.semaphore_wait(barrier, len(peers))


def push(src, dst, send, recv, peer):
    return pltpu.make_async_remote_copy(
        src_ref=src, dst_ref=dst, send_sem=send, recv_sem=recv, device_id=peer, device_id_type=MESH)


class ZRing:
    def __init__(self, f, z, n_z):
        self.f, self.z, self.n_z = f, z, n_z

    def start(self, source_of, buf, send, recv):
        for j in range(1, self.n_z):
            to = (self.z + j) % self.n_z
            push(source_of(to), buf.at[self.z], send.at[j], recv.at[self.z], (self.f, to)).start()

    def wait(self, buf, send, recv):
        for j in range(1, self.n_z):
            came = (self.z + j) % self.n_z
            push(buf.at[came], buf.at[came], send.at[j], recv.at[came], (self.f, came)).wait_recv()

    def drain(self, source_of, buf, send, recv):
        for j in range(1, self.n_z):
            to = (self.z + j) % self.n_z
            push(source_of(to), buf.at[self.z], send.at[j], recv.at[self.z], (self.f, to)).wait_send()


def text_tools(n_z, pad, width, f, z, lmask_ref, part_ref, mine_ref, out_buf, in_buf, rs_send, rs_recv, ag_send, ag_recv):
    ring = ZRing(f, z, n_z)
    bf16, f32 = jnp.bfloat16, jnp.float32

    def scatter(turn, main, rank_part):
        full = jnp.concatenate([main, rank_part], axis=1)
        full = full.reshape(n_z, pad, full.shape[1])
        part_ref[...] = full
        mine_ref[turn] = part_ref[z]
        out_buf[turn] = full.astype(bf16)
        ring.start(lambda to: out_buf.at[turn, to], in_buf.at[turn], rs_send.at[turn], rs_recv.at[turn])

    def collect(turn):
        ring.wait(in_buf.at[turn], rs_send.at[turn], rs_recv.at[turn])
        total = mine_ref[turn]
        for j in range(1, n_z):
            total = total + in_buf[turn, (z + j) % n_z].astype(f32)
        ring.drain(lambda to: out_buf.at[turn, to], in_buf.at[turn], rs_send.at[turn], rs_recv.at[turn])
        return total[:, :width], (total[:, width:] * lmask_ref[...]).astype(bf16)

    def spread(ref, *parts):
        offset = 0
        for part in parts:
            ref[z, :, offset:offset + part.shape[1]] = part
            offset += part.shape[1]
        ring.start(lambda to: ref.at[z], ref, ag_send, ag_recv)

    def spread_end(ref):
        ring.wait(ref, ag_send, ag_recv)
        ring.drain(lambda to: ref.at[z], ref, ag_send, ag_recv)

    def gathered(ref, start, count):
        return ref[:, :, start:start + count].reshape(n_z * pad, count)

    def own_lanes(ref, share):
        at = pl.ds(pl.multiple_of(z * share, 128), share)
        return ref[:, :, at].reshape(n_z * pad, share)

    return scatter, collect, spread, spread_end, gathered, own_lanes


def rows_of(mod_ref, own_ref):
    return lambda row: jnp.where(own_ref[...] > 0, mod_ref[row:row + 1, :], mod_ref[8 + row:9 + row, :])


def both_fwd_kernel(tiles, n_z, turns, o_ref, x_ref, g_ref, mod_ref, wo_ref, ao_ref, bo_ref, a1_ref, b1_ref, w1_ref, a2_ref, w2_ref, b2_ref,
                    ot_ref, xt_ref, tmod_ref, owner_ref, own_ref, lmask_ref, two_ref, tao_ref, tbo_ref,
                    a_out, x1_out, h2_out, u_out, y_out, to_out, t1_out, t2_out, gate_out,
                    tall_out, att_out, tx1_out, tbr_out,
                    m_acc, t2_acc, o_got, part_ref, mine_ref, out_buf, in_buf, ag_ref, o_send, o_recv, rs_send, rs_recv, ag_send, ag_recv):
    step = pl.program_id(0)
    f, z, core, base, column = column_peers(n_z)
    pad, width_t = xt_ref.shape
    f32, bf16 = jnp.float32, jnp.bfloat16
    scatter, collect, spread, spread_end, gathered, own_lanes = text_tools(
        n_z, pad, width_t, f, z, lmask_ref, part_ref, mine_ref, out_buf, in_buf, rs_send, rs_recv, ag_send, ag_recv)
    home = [(base + z // 2, 2 * core + i) for i in range(2)]

    def is_here(i):
        return (z // 2 == core) & (2 * core + i == z)

    def o_push(i):
        return push(ot_ref.at[i], o_got.at[z % 2], o_send.at[i], o_recv.at[z % 2], home[i])

    @pl.when(step == 0)
    def _():
        meet(column)
        for i in range(2):
            @pl.when(is_here(i))
            def _():
                copy = pltpu.make_async_copy(ot_ref.at[i], o_got.at[z % 2], o_recv.at[z % 2])
                copy.start()
                copy.wait()

            @pl.when(jnp.logical_not(is_here(i)))
            def _():
                o_push(i).start()

    rows = o_ref.shape[0]
    width = o_ref.shape[1]


    @pl.when(step == 0)
    def _():
        to = mm_t(o_ref[...], ao_ref[...]).astype(jnp.bfloat16)
        to_out[...] = to

        def cols(n, _):
            sl = pl.ds(pl.multiple_of(n * 256, 256), 256)
            a = mm_t(o_ref[...], wo_ref[sl, :]) + mm(to_out[...], bo_ref[:, sl])
            a_out[:, sl] = a.astype(jnp.bfloat16)
            x1_out[:, sl] = x_ref[:, sl].astype(jnp.float32) + mod_ref[2:3, sl] * a
            return 0

        lax.fori_loop(0, width // 256, cols, 0)

        def norm(r, _):
            sl = pl.ds(pl.multiple_of(r * ROWS, ROWS), ROWS)
            xh, _inv = norm_rows(x1_out[sl, :])
            h2_out[sl, :] = (xh * (1.0 + mod_ref[4:5, :]) + mod_ref[3:4, :]).astype(jnp.bfloat16)
            return 0

        lax.fori_loop(0, rows // ROWS, norm, 0)
        t1_out[...] = mm_t(h2_out[...], a1_ref[...]).astype(jnp.bfloat16)
        m_acc[...] = jnp.zeros_like(m_acc)
        t2_acc[...] = jnp.zeros_like(t2_acc)

    u = mm(h2_out[...], w1_ref[...]) + mm(t1_out[...], b1_ref[...])
    u_out[...] = u
    f = gelu_parts(u)[0].astype(jnp.bfloat16)
    m_acc[...] += mm_t(f, w2_ref[...])
    t2_acc[...] += mm_t(f, a2_ref[...])


    @pl.when(step == turns[0])
    def _():
        for i in range(2):
            @pl.when(jnp.logical_not(is_here(i)))
            def _():
                push(o_got.at[i], o_got.at[i], o_send.at[i], o_recv.at[i], home[i]).wait_recv()
                o_push(i).wait_send()
        owner = owner_ref[...]
        att = jnp.where(owner > 0, o_got[0].astype(f32), jnp.where(owner < 0, o_got[1].astype(f32), 0.0)).astype(bf16)
        att_out[...] = att
        scatter(0, mm_t(att, two_ref[...]), mm_t(att, tao_ref[...]))

    @pl.when(step == turns[1])
    def _():
        modulation = rows_of(tmod_ref, own_ref)
        branch, to_mine = collect(0)
        branch = branch + mm(to_mine, tbo_ref[...])
        tbr_out[...] = branch
        x1 = xt_ref[...].astype(f32) + modulation(2) * branch
        tx1_out[...] = x1
        hat, _inv = norm_rows(x1)
        spread(ag_ref, (hat * (1.0 + modulation(4)) + modulation(3)).astype(bf16), to_mine)

    @pl.when(step == tiles - 1)
    def _():
        spread_end(ag_ref)
        tall_out[...] = ag_ref[...]

    @pl.when(step == tiles - 1)
    def _():
        t2_out[...] = t2_acc[...].astype(jnp.bfloat16)
        gate_out[...] = jnp.zeros_like(gate_out)

        def last(r, _):
            sl = pl.ds(pl.multiple_of(r * ROWS, ROWS), ROWS)
            m = m_acc[sl, :] + mm(t2_out[sl, :], b2_ref[...])
            y_out[sl, :] = (x1_out[sl, :] + mod_ref[5:6, :] * m).astype(jnp.bfloat16)
            gm = g_ref[sl, :].astype(jnp.float32) * m
            gate_out[...] += sum(gm[8 * i:8 * i + 8, :] for i in range(ROWS // 8))
            return 0

        lax.fori_loop(0, rows // ROWS, last, 0)


def both_back_kernel(tiles, n_z, turns, g_ref, x1_ref, a_ref, h2_ref, o_ref, mod_ref, u_ref, w2_ref, a2_ref, b2_ref, w1_ref, a1_ref, b1_ref,
                     wo_ref, ao_ref, bo_ref, to_ref, t1_ref, t2_ref,
                     gt_ref, tx1_ref, tbr_ref, tmod_ref, own_ref, mask_ref, lmask_ref, tall_ref, att_ref, tdm_ref, two_ref, tw1_ref, tw2_ref,
                     tao_ref, tbo_ref, ta1_ref, tb1_ref, ta2_ref, tb2_ref,
                     dx1_out, do_out, sums_out, ga2_out, gb1_out, ga1_out, gb2_out, gao_out, gbo_out,
                     ty_out, tdx1_out, tdo_out, tsums_out, tgao_out, tgbo_out, tga1_out, tgb1_out, tga2_out, tgb2_out,
                     dm_ref, dt2_ref, dh_acc, dt1_acc, part_ref, mine_ref, out_buf, in_buf, tda_ref, tdo_buf,
                     do_send, do_recv, rs_send, rs_recv, ag_send, ag_recv):
    step = pl.program_id(0)
    f, z, core, base, column = column_peers(n_z)
    pad, width_t = gt_ref.shape
    rank = tao_ref.shape[0]
    share = tao_ref.shape[1]
    f32, bf16 = jnp.float32, jnp.bfloat16
    scatter, collect, spread, spread_end, gathered, own_lanes = text_tools(
        n_z, pad, width_t, f, z, lmask_ref, part_ref, mine_ref, out_buf, in_buf, rs_send, rs_recv, ag_send, ag_recv)
    home = [(base + z // 2, 2 * core + i) for i in range(2)]

    def is_here(i):
        return (z // 2 == core) & (2 * core + i == z)

    def do_push(s):
        return push(tdo_buf, tdo_out.at[z % 2], do_send.at[s], do_recv.at[z % 2], home[s])

    def collapse(place, values):
        for s in range(2):
            tsums_out[2 * place + s:2 * place + s + 1, :] = jnp.sum(
                jnp.where(own_ref[...] == (1.0 if s == 0 else -1.0), values, 0.0), axis=0, keepdims=True)

    @pl.when(step == 0)
    def _():
        meet(column)
        h2_all = gathered(tall_ref, 0, width_t)
        t1 = (mm_t(h2_all, ta1_ref[...]) * mask_ref[...]).astype(bf16)
        u = mm(h2_all, tw1_ref[...]) + mm(t1, tb1_ref[...])
        act, slope = gelu_parts(u)
        act = act.astype(bf16)
        dm_all = tdm_ref[...].reshape(n_z * pad, width_t)
        dt2 = (mm_t(dm_all, tb2_ref[...]) * mask_ref[...]).astype(bf16)
        du = ((mm(dm_all, tw2_ref[...]) + mm(dt2, ta2_ref[...])) * slope).astype(bf16)
        scatter(1, mm_t(du, tw1_ref[...]), mm_t(du, tb1_ref[...]))
        scatter(0, mm_t(act, tw2_ref[...]), mm_t(act, ta2_ref[...]))
        tga2_out[...] = t_mm(dt2, act)
        tgb1_out[...] = t_mm(t1, du)

    rows, width = g_ref.shape
    bf16 = jnp.bfloat16


    @pl.when(step == 0)
    def _():
        def start(r, _):
            sl = pl.ds(pl.multiple_of(r * ROWS, ROWS), ROWS)
            dm_ref[sl, :] = (mod_ref[5:6, :] * g_ref[sl, :].astype(jnp.float32)).astype(bf16)
            return 0

        lax.fori_loop(0, rows // ROWS, start, 0)
        dt2_ref[...] = mm_t(dm_ref[...], b2_ref[...]).astype(bf16)
        gb2_out[...] = t_mm(t2_ref[...], dm_ref[...])
        dh_acc[...] = jnp.zeros_like(dh_acc)
        dt1_acc[...] = jnp.zeros_like(dt1_acc)

    act, slope = gelu_parts(u_ref[...])
    df = mm(dm_ref[...], w2_ref[...]) + mm(dt2_ref[...], a2_ref[...])
    ga2_out[...] = t_mm(dt2_ref[...], act.astype(bf16))
    du = (df * slope).astype(bf16)
    gb1_out[...] = t_mm(t1_ref[...], du)
    dh_acc[...] += mm_t(du, w1_ref[...])
    dt1_acc[...] += mm_t(du, b1_ref[...])


    @pl.when(step == turns[0])
    def _():
        modulation = rows_of(tmod_ref, own_ref)
        dh, dt1_mine = collect(1)
        dh = dh + mm(dt1_mine, ta1_ref[...])
        hat, inverse = norm_rows(tx1_ref[...])
        dz = dh * (1.0 + modulation(4))
        dx1 = gt_ref[...].astype(f32) + inverse * (
            dz - jnp.mean(dz, axis=-1, keepdims=True) - hat * jnp.mean(dz * hat, axis=-1, keepdims=True))
        feed, t2_mine = collect(0)
        spread(tda_ref, (modulation(2) * dx1).astype(bf16), dt1_mine, t2_mine)
        tdx1_out[...] = dx1
        collapse(0, dx1 * tbr_ref[...])
        collapse(1, dh)
        collapse(2, dh * hat)
        feed = feed + mm(t2_mine, tb2_ref[...])
        ty_out[...] = (tx1_ref[...] + modulation(5) * feed).astype(bf16)
        collapse(3, gt_ref[...].astype(f32) * feed)

    @pl.when(step == turns[1])
    def _():
        spread_end(tda_ref)
        da_all = gathered(tda_ref, 0, width_t)
        dt1 = gathered(tda_ref, width_t, rank)
        t2 = gathered(tda_ref, width_t + rank, rank)
        dto = (mm_t(da_all, tbo_ref[...]) * mask_ref[...]).astype(bf16)
        tdo_buf[...] = (mm(da_all, two_ref[...]) + mm(dto, tao_ref[...])).astype(bf16)
        for s in range(2):
            @pl.when(is_here(s))
            def _():
                copy = pltpu.make_async_copy(tdo_buf, tdo_out.at[z % 2], do_recv.at[z % 2])
                copy.start()
                copy.wait()

            @pl.when(jnp.logical_not(is_here(s)))
            def _():
                do_push(s).start()
        tgao_out[...] = t_mm(dto, att_ref[...])
        tgbo_out[...] = t_mm(gathered(tall_ref, width_t, rank), own_lanes(tda_ref, share))
        tgb2_out[...] = t_mm(t2, own_lanes(tdm_ref, share))
        tga1_out[...] = t_mm(dt1, own_lanes(tall_ref, share))

    @pl.when(step == tiles - 1)
    def _():
        dt1 = dt1_acc[...].astype(bf16)
        dt2_ref[...] = dt1
        ga1_out[...] = t_mm(dt1, h2_ref[...])
        sums_out[...] = jnp.zeros_like(sums_out)

        def last(r, _):
            sl = pl.ds(pl.multiple_of(r * ROWS, ROWS), ROWS)
            dh = dh_acc[sl, :] + mm(dt2_ref[sl, :], a1_ref[...])
            xh, inverse = norm_rows(x1_ref[sl, :])
            dz = dh * (1.0 + mod_ref[4:5, :])
            dx1 = g_ref[sl, :].astype(jnp.float32) + inverse * (
                dz - jnp.mean(dz, axis=-1, keepdims=True) - xh * jnp.mean(dz * xh, axis=-1, keepdims=True))
            dx1_out[sl, :] = dx1
            dm_ref[sl, :] = (mod_ref[2:3, :] * dx1).astype(bf16)
            fold = lambda v: sum(v[8 * i:8 * i + 8, :] for i in range(ROWS // 8))
            sums_out[0:8, :] += fold(dx1 * a_ref[sl, :].astype(jnp.float32))
            sums_out[8:16, :] += fold(dh)
            sums_out[16:24, :] += fold(dh * xh)
            return 0

        lax.fori_loop(0, rows // ROWS, last, 0)
        dto = mm_t(dm_ref[...], bo_ref[...]).astype(bf16)
        dt2_ref[...] = dto
        gao_out[...] = t_mm(dto, o_ref[...])
        gbo_out[...] = t_mm(to_ref[...], dm_ref[...])

        def cols(n, _):
            sl = pl.ds(pl.multiple_of(n * 256, 256), 256)
            do_out[:, sl] = (mm(dm_ref[...], wo_ref[:, sl]) + mm(dt2_ref[...], ao_ref[:, sl])).astype(bf16)
            return 0

        lax.fori_loop(0, width // 256, cols, 0)

    @pl.when(step == tiles - 1)
    def _():
        for i in range(2):
            @pl.when(jnp.logical_not(is_here(i)))
            def _():
                push(tdo_out.at[i], tdo_out.at[i], do_send.at[i], do_recv.at[i], home[i]).wait_recv()
                do_push(i).wait_send()


def both_fwd(o, x, g, mod, wo, pair_o, pair_1, w1, pair_2, w2, ot, xt, tmod, owner, own, lmask, two, tpair_o, n_z, cid, tn=512, turns=(2, 7)):
    rows, width = o.shape
    hidden = w1.shape[1]
    tiles = hidden // tn
    rank = pair_o[0].shape[0]
    once = lambda shape: pl.BlockSpec(shape, lambda n: (0,) * len(shape), pipeline_mode=pl.Buffered(1))
    whole = once
    tile = lambda height: pl.BlockSpec((height, tn), lambda n: (0, n))
    f32, bf16 = jnp.float32, jnp.bfloat16
    shape, vmem, dma = jax.ShapeDtypeStruct, pltpu.VMEM, pltpu.SemaphoreType.DMA
    act = (rows, width)
    pad = xt.shape[0]
    total, share = n_z * pad, two.shape[1]
    thick = tpair_o[0].shape[0]
    wide = width + thick
    texts = (xt, tmod, owner, own, lmask, two, *tpair_o)
    return pl.pallas_call(
        functools.partial(both_fwd_kernel, tiles, n_z, turns),
        grid=(tiles,),
        in_specs=[once(act), once(act), once(act), once(mod.shape), once((width, width)), once((rank, width)), once((rank, width)),
                  once((rank, width)), tile(rank), tile(width), tile(rank), tile(width), once((rank, width)),
                  pl.BlockSpec(memory_space=pl.ANY)] + [once(v.shape) for v in texts],
        out_specs=[whole(act), whole(act), whole(act), tile(rows), whole(act), whole((rows, rank)), whole((rows, rank)),
                   whole((rows, rank)), whole((8, width)), whole((n_z, pad, wide)), whole((total, share)), whole((pad, width)),
                   whole((pad, width))],
        out_shape=[shape(act, bf16), shape(act, f32), shape(act, bf16), shape((rows, hidden), f32), shape(act, bf16)]
        + [shape((rows, rank), bf16)] * 3
        + [shape((8, width), f32), shape((n_z, pad, wide), bf16), shape((total, share), bf16), shape((pad, width), f32),
           shape((pad, width), f32)],
        scratch_shapes=[vmem(act, f32), vmem((rows, rank), f32), vmem((2, total, share), bf16), vmem((n_z, pad, wide), f32), vmem((1, pad, wide), f32),
                        vmem((1, n_z, pad, wide), bf16), vmem((1, n_z, pad, wide), bf16), vmem((n_z, pad, wide), bf16),
                        dma((2,)), dma((2,)), dma((1, n_z)), dma((1, n_z)), dma((n_z,)), dma((n_z,))],
        compiler_params=pltpu.CompilerParams(collective_id=cid, has_side_effects=True, vmem_limit_bytes=60 * 1024 * 1024),
        name="block_forward",
    )(o, x, g, mod, wo, *pair_o, pair_1[0], pair_1[1], w1, pair_2[0], w2, pair_2[1], ot, *texts)


def both_back(g, x1, a, h2, o, mod, u, w2, pair_2, w1, pair_1, wo, pair_o, mids,
              gt, tx1, tbr, tmod, own, mask, lmask, tall, att, tdm, two, tw1, tw2, tpair_o, tpair_1, tpair_2, n_z, cid, tn=512, turns=(5, 9)):
    rows, width = o.shape
    hidden = w1.shape[1]
    tiles = hidden // tn
    rank = pair_o[0].shape[0]
    once = lambda shape: pl.BlockSpec(shape, lambda n: (0,) * len(shape), pipeline_mode=pl.Buffered(1))
    whole = once
    tile = lambda height: pl.BlockSpec((height, tn), lambda n: (0, n))
    f32, bf16 = jnp.float32, jnp.bfloat16
    shape, vmem, dma = jax.ShapeDtypeStruct, pltpu.VMEM, pltpu.SemaphoreType.DMA
    act = (rows, width)
    side = (rank, width)
    thin = (rows, rank)
    pad = gt.shape[0]
    total, share = n_z * pad, two.shape[1]
    thick = tpair_o[0].shape[0]
    t_hidden = tw1.shape[1]
    wide = width + thick
    texts = (gt, tx1, tbr, tmod, own, mask, lmask, tall, att, tdm, two, tw1, tw2, *tpair_o, *tpair_1, *tpair_2)
    return pl.pallas_call(
        functools.partial(both_back_kernel, tiles, n_z, turns),
        grid=(tiles,),
        in_specs=[once(act)] * 5 + [once(mod.shape), tile(rows), tile(width), tile(rank), once(side), tile(width), once(side), tile(rank),
                  once((width, width)), once(side), once(side)] + [once(thin)] * 3 + [once(v.shape) for v in texts],
        out_specs=[whole(act), whole(act), whole((24, width)), tile(rank), tile(rank)] + [whole(side)] * 4
        + [whole((pad, width)), whole((pad, width)), pl.BlockSpec(memory_space=pl.ANY), whole((8, width)), whole((thick, share)),
           whole((thick, share)), whole((thick, share)), whole((thick, t_hidden)), whole((thick, t_hidden)), whole((thick, share))],
        out_shape=[shape(act, f32), shape(act, bf16), shape((24, width), f32)] + [shape((rank, hidden), f32)] * 2 + [shape(side, f32)] * 4
        + [shape((pad, width), bf16), shape((pad, width), f32), shape((2, total, share), bf16), shape((8, width), f32),
           shape((thick, share), f32), shape((thick, share), f32), shape((thick, share), f32), shape((thick, t_hidden), f32),
           shape((thick, t_hidden), f32), shape((thick, share), f32)],
        scratch_shapes=[vmem(act, bf16), vmem(thin, bf16), vmem(act, f32), vmem(thin, f32),
                        vmem((n_z, pad, wide), f32), vmem((2, pad, wide), f32), vmem((2, n_z, pad, wide), bf16), vmem((2, n_z, pad, wide), bf16),
                        vmem((n_z, pad, wide + thick), bf16), vmem((total, share), bf16),
                        dma((2,)), dma((2,)), dma((2, n_z)), dma((2, n_z)), dma((n_z,)), dma((n_z,))],
        compiler_params=pltpu.CompilerParams(collective_id=cid, has_side_effects=True, vmem_limit_bytes=60 * 1024 * 1024),
        name="block_backward",
    )(g, x1, a, h2, o, mod, u, w2, pair_2[0], pair_2[1], w1, pair_1[0], pair_1[1], wo, *pair_o, *mids, *texts)


def flip_bits(chip, mask, nbits):
    other = 0
    for bit in range(nbits):
        have = (chip // (1 << bit)) % 2
        other = other + (1 - have if (mask >> bit) & 1 else have) * (1 << bit)
    return other


def tail_kernel(n_f, n_z, fans, cols, *refs):
    it = iter(refs)
    take = lambda count: [next(it) for _ in range(count)]
    dq_in, tdq_in, wq_ref = take(3)
    (x_ref, dx1_ref, h_ref, imod_ref, mid_ref, qa_ref, qb_ref, isum_ref, igate_ref, tx_ref, tdx1_ref, th_ref, tmodr_ref, owner_ref,
     own_ref, lmask_ref, tmid_ref, twq_ref, tqa_ref, tqb_ref, tsum_ref) = take(21)
    img_a, img_b, txt_a, txt_b = take(3), take(3), take(3), take(3)
    hot4_ref, hot2_ref, wmod_ref, bmod_ref, tmod_ref, cond_ref, smask_ref = take(7)
    grad_out, tgrad_out, cond_out, rank_out, shard_out = take(5)
    (dq_ref, wtile, dh_ref, dt_ref, grad_ref, gaq_ref, gbq_ref, tgot, part_ref, mine_ref, out_buf, in_buf, dt_ag, tgb_ref, dmod_ref,
     isums) = take(16)
    zmsg, zgot, dense, snd1, rcv1, snd2, rcv2, dgot, own_dm, all_dm, cpart, cgot, zsum, zall, dts = take(15)
    (g_send, g_recv, z_send, z_recv, c_send, c_recv, s_send, s_recv, d_send, d_recv, f_send, f_recv, p_send, p_recv,
     q_send, q_recv, t_send, t_recv, dq_send, dq_recv, dq_own, w_sem, h_send, h_recv, rs_send, rs_recv, ag_send, ag_recv) = take(28)
    f32, bf16 = jnp.float32, jnp.bfloat16
    f, z, core, base, column = column_peers(n_z)
    chip = f // 2
    chips = n_f // 2
    nbits = bits_of(chips)
    partner = base + 1 - core
    around = [((f + j) % n_f, z) for j in range(1, n_f)]
    others = [(flip_bits(chip, mask, nbits) * 2 + side, z) for mask in range(1, chips) for side in range(2)]
    meet(column + others)
    ring = ZRing(f, z, n_z)
    blk = shard_out.shape[0]
    hidden_rank = hot2_ref.shape[0]

    home = [(base + z // 2, 2 * core + i) for i in range(2)]

    def is_here(i):
        return (z // 2 == core) & (2 * core + i == z)

    swap = push(dq_in.at[1 - core], dq_ref.at[core], dq_send, dq_recv, (partner, z))
    swap.start()
    keep = pltpu.make_async_copy(dq_in.at[core], dq_ref.at[core], dq_own)
    keep.start()

    def t_push(i):
        return push(tdq_in.at[i], tgot.at[z % 2], h_send.at[i], h_recv.at[z % 2], home[i])

    for i in range(2):
        @pl.when(is_here(i))
        def _():
            copy = pltpu.make_async_copy(tdq_in.at[i], tgot.at[z % 2], h_recv.at[z % 2])
            copy.start()
            copy.wait()

        @pl.when(jnp.logical_not(is_here(i)))
        def _():
            t_push(i).start()

    pad, width = tx_ref.shape
    thick = tqa_ref.shape[0]
    scatter, collect, spread, spread_end, gathered, own_lanes = text_tools(
        n_z, pad, width, f, z, lmask_ref, part_ref, mine_ref, out_buf, in_buf, rs_send, rs_recv, ag_send, ag_recv)
    tn = wtile.shape[3]
    per_half = dq_ref.shape[2] // tn

    def tile_of(n):
        side = core if n < per_half else 1 - core
        return side, side * per_half + n % per_half

    def tile_load(n):
        at = pl.ds(pl.multiple_of(tile_of(n)[1] * tn, 128), tn)
        return pltpu.make_async_copy(wq_ref.at[:, :, at], wtile.at[n % 2], w_sem.at[n % 2])

    def tile_back(n):
        if n + 1 < 2 * per_half:
            tile_load(n + 1).start()
        tile_load(n).wait()
        side, number = tile_of(n)
        at = pl.ds(pl.multiple_of(number * tn, 128), tn)
        part = dq_ref[side, :, n % per_half * tn:(n % per_half + 1) * tn]
        main = mm_t(part, wtile[n % 2].reshape(width, tn))
        thin = mm_t(part, qb_ref[:, at])
        if n == 0:
            dh_ref[...] = main
            dt_ref[...] = thin
        else:
            dh_ref[...] += main
            dt_ref[...] += thin
        gbq_ref[:, at] = t_mm(mid_ref[...], part)

    tile_load(0).start()
    keep.wait()
    for n in range(per_half):
        tile_back(n)

    for i in range(2):
        @pl.when(jnp.logical_not(is_here(i)))
        def _():
            push(tgot.at[i], tgot.at[i], h_send.at[i], h_recv.at[i], home[i]).wait_recv()
            t_push(i).wait_send()
    owner = owner_ref[...]
    tdq = jnp.where(owner > 0, tgot[0].astype(f32), jnp.where(owner < 0, tgot[1].astype(f32), 0.0)).astype(bf16)
    scatter(0, mm_t(tdq, twq_ref[...]), mm_t(tdq, tqb_ref[...]))
    tgb_ref[...] = t_mm(tmid_ref[...], tdq)

    push(dq_in.at[1 - core], dq_ref.at[1 - core], dq_send, dq_recv, (partner, z)).wait_recv()
    for n in range(per_half, 2 * per_half):
        tile_back(n)
    dt_low = dt_ref[...].astype(bf16)
    gaq_ref[...] = t_mm(dt_low, h_ref[...])

    offset = 0
    spans = []
    for part, sizes in (([gaq_ref] + img_a, fans), ([gbq_ref] + img_b, cols)):
        for index in range(4):
            count = sizes[index + 1] // n_z
            for t in range(n_z):
                zmsg[t, :, offset:offset + count] = part[index][:, t * count:(t + 1) * count].astype(bf16)
            spans.append((offset, count))
            offset += count
    ring.start(lambda to: zmsg.at[to], zgot, z_send, z_recv)
    zgot[z] = zmsg[z]

    isums[...] = jnp.zeros_like(isums)
    quarter = grad_ref.shape[1]
    dh_ref[...] += mm(dt_low, qa_ref[...])
    for i in range(2):
        def last(r, _):
            sl = pl.ds(pl.multiple_of(i * quarter + r * ROWS, ROWS), ROWS)
            dh = dh_ref[sl, :]
            xh, inverse = norm_rows(x_ref[sl, :].astype(f32))
            dz = dh * (1.0 + imod_ref[1:2, :])
            dx = dx1_ref[sl, :] + inverse * (
                dz - jnp.mean(dz, axis=-1, keepdims=True) - xh * jnp.mean(dz * xh, axis=-1, keepdims=True))
            grad_ref[i, pl.ds(pl.multiple_of(r * ROWS, ROWS), ROWS), :] = dx.astype(bf16)
            fold = lambda v: sum(v[8 * j:8 * j + 8, :] for j in range(ROWS // 8))
            isums[0:8, :] += fold(dh)
            isums[8:16, :] += fold(dh * xh)
            return 0

        lax.fori_loop(0, quarter // ROWS, last, 0)

    pick = rows_of(tmodr_ref, own_ref)
    tdh, tdt = collect(0)
    spread(dt_ag, tdt)
    tdh = tdh + mm(tdt, tqa_ref[...])
    hat, inverse = norm_rows(tx_ref[...].astype(f32))
    dz = tdh * (1.0 + pick(1))
    tgrad_out[...] = tdx1_ref[...] + inverse * (
        dz - jnp.mean(dz, axis=-1, keepdims=True) - hat * jnp.mean(dz * hat, axis=-1, keepdims=True))

    def total_of(v):
        return jnp.sum(v, axis=0, keepdims=True)

    rows_img = [total_of(isums[0:8, :]), total_of(isums[8:16, :])]
    rows_img += [total_of(isum_ref[8 * p:8 * p + 8, :]) for p in range(3)] + [total_of(igate_ref[...])]
    rows_txt = []
    for s in range(2):
        chosen = own_ref[...] == (1.0 if s == 0 else -1.0)
        rows_txt.append([total_of(jnp.where(chosen, tdh, 0.0)), total_of(jnp.where(chosen, tdh * hat, 0.0))]
                        + [tsum_ref[2 * p + s:2 * p + s + 1, :] for p in range(4)])
    dmod_ref[...] = jnp.zeros_like(dmod_ref)
    chunk = dmod_ref.shape[-1]
    per_row = width // chunk
    per_block = 6 * per_row // n_z
    for r, parts in enumerate([rows_img] + rows_txt):
        for q in range(6 * per_row):
            dmod_ref[q // per_block, r, q % per_block:q % per_block + 1, :] = (
                parts[q // per_row][:, q % per_row * chunk:(q % per_row + 1) * chunk])

    def dmod_copy(index, peer):
        return push(dmod_ref.at[peer[1]], dgot.at[core * n_z + z], d_send.at[index], d_recv.at[core * n_z + z], peer)

    for index, peer in enumerate(column):
        dmod_copy(index, peer).start()
    dgot[core * n_z + z] = dmod_ref[z]

    for index, peer in enumerate(column):
        place = peer[0] % 2 * n_z + peer[1]
        push(dgot.at[place], dgot.at[place], d_send.at[index], d_recv.at[place], peer).wait_recv()
    rows = []
    for slot in range(2):
        rows.append(dgot[2 * core + slot, 0] + dgot[n_z + 2 * core + slot, 0])
    for slot in range(2):
        total = dgot[core * n_z, 1 + slot]
        for t in range(1, n_z):
            total = total + dgot[core * n_z + t, 1 + slot]
        rows.append(total)
    own_dm[...] = jnp.zeros_like(own_dm)
    for r, total in enumerate(rows):
        for j in range(own_dm.shape[1] // chunk):
            own_dm[r:r + 1, j * chunk:(j + 1) * chunk] = total[j:j + 1, :].astype(bf16).astype(f32)
    for j in range(1, n_f):
        push(own_dm, all_dm.at[f], f_send.at[j], f_recv.at[f], around[j - 1]).start()
    all_dm[f] = own_dm[...]
    dm_low = own_dm[...].astype(bf16)
    tmod = [tmod_ref[s].astype(bf16) for s in range(2)]
    gb_mod = [t_mm(tmod[s], dm_low) for s in range(2)]
    rank_img = mm_t(dm_low, bmod_ref[0])
    rank_txt = mm_t(dm_low, bmod_ref[1])
    row = lax.broadcasted_iota(jnp.int32, rank_img.shape, 0)
    rank_part = jnp.where(row < 2, rank_img, rank_txt)

    spread_end(dt_ag)
    tga = t_mm(gathered(dt_ag, 0, thick), own_lanes(th_ref, cols[2] // n_z))
    txt_a = [tga[:hidden_rank]] + [ref[:hidden_rank, :] for ref in txt_a]
    txt_b = [tgb_ref[:hidden_rank, :]] + [ref[:hidden_rank, :] for ref in txt_b]
    hot2 = hot2_ref[...]
    starts = []
    offset = 0
    for stream in range(2):
        for index in range(5):
            starts.append((stream, index, offset, offset + fans[index] // n_z))
            offset += fans[index] // n_z + cols[index] // n_z

    def put_a(at, part, hot):
        dense[at:at + part.shape[1], :] = dots(part, hot, 0, 0)

    def put_b(at, part, hot):
        full = dots(hot, part, 0, 0)
        blocks = part.shape[1] // 128
        for j in range(blocks):
            dense[pl.ds(at + j, 128, stride=blocks), :] = full[:, j * 128:(j + 1) * 128]

    for stream, index, at_a, at_b in starts:
        if index == 0:
            dense[at_a:at_b, :] = jnp.zeros((at_b - at_a, 128), f32)
            put_b(at_b, gb_mod[stream].astype(bf16), hot2)
        elif stream == 1:
            put_a(at_a, txt_a[index - 1].astype(bf16), hot2)
            put_b(at_b, txt_b[index - 1].astype(bf16), hot2)

    ring.wait(zgot, z_send, z_recv)
    hot4 = hot4_ref[...]
    for stream, index, at_a, at_b in starts:
        if stream == 0 and index > 0:
            for at, put, (begin, count) in ((at_a, put_a, spans[index - 1]), (at_b, put_b, spans[index + 3])):
                part = zgot[:, :, begin:begin + count].reshape(hot4.shape[0], count)
                put(at, part, hot4)

    for i in range(2):
        @pl.when(is_here(i))
        def _():
            pltpu.make_async_copy(grad_ref.at[i], grad_out.at[z % 2], g_recv.at[z % 2]).start()

        @pl.when(jnp.logical_not(is_here(i)))
        def _():
            push(grad_ref.at[i], grad_out.at[z % 2], g_send.at[i], g_recv.at[z % 2], home[i]).start()

    def block(number):
        return pl.ds(pl.multiple_of(number * blk, 16), blk)

    for p in range(chips):
        snd1[p] = dense[block(2 * p + 1 - core), :].astype(bf16)
        push(snd1.at[p], rcv1.at[p], c_send.at[p], c_recv.at[p], (partner, z)).start()

    for j in range(1, n_f):
        came = (f - j + n_f) % n_f
        push(own_dm, all_dm.at[came], f_send.at[j], f_recv.at[came], (came, z)).wait_recv()
    everyone = all_dm[...].reshape(n_f * 8, own_dm.shape[1]).astype(bf16)
    part = mm_t(everyone, wmod_ref[0]) + pltpu.roll(mm_t(everyone, wmod_ref[1]), n_f * 8 - 2, 0)
    k_local = part.shape[1]
    cpart[...] = jnp.zeros_like(cpart)
    cpart[:, :, :k_local] = part.reshape(n_f, 8, k_local)
    for j in range(1, n_f):
        to = (f + j) % n_f
        push(cpart.at[to], cgot.at[f], p_send.at[j], p_recv.at[f], (to, z)).start()
    cgot[f] = cpart[f]

    for p in range(chips):
        push(snd1.at[p], rcv1.at[p], c_send.at[p], c_recv.at[p], (partner, z)).wait_recv()

    def mine_of(p):
        return block(2 * p + core)

    for p in range(chips):
        dense[mine_of(p), :] += rcv1[p].astype(f32)

    half = blk // 2
    orders = [list(range(nbits)), list(range(nbits))[::-1]]

    def masks_at(side, turn):
        left = orders[side][turn:]
        return [sum(1 << b for i, b in enumerate(left) if (m >> i) & 1) for m in range(1 << len(left))]

    def rs_copy(side, turn, index):
        slot = turn * 2 + index
        peer = flip_bits(chip, 1 << orders[side][turn], nbits) * 2 + core
        return push(snd2.at[side, slot], rcv2.at[side, slot], s_send.at[side, slot], s_recv.at[side, slot], (peer, z))

    def half_of(number, side):
        return pl.ds(pl.multiple_of((2 * number + core) * blk + side * half, 16), half)

    def rs_start(turn):
        for side in range(2):
            bit = 1 << orders[side][turn]
            for index, mask in enumerate(masks_at(side, turn + 1)):
                number = flip_bits(chip, bit | mask, nbits)
                snd2[side, turn * 2 + index] = dense[half_of(number, side), :].astype(bf16)
                rs_copy(side, turn, index).start()

    def rs_end(turn):
        for side in range(2):
            for index, mask in enumerate(masks_at(side, turn + 1)):
                number = flip_bits(chip, mask, nbits)
                rs_copy(side, turn, index).wait_recv()
                dense[half_of(number, side), :] += rcv2[side, turn * 2 + index].astype(f32)

    rs_start(0)

    for j in range(1, n_f):
        came = (f - j + n_f) % n_f
        push(cpart.at[came], cgot.at[came], p_send.at[j], p_recv.at[came], (came, z)).wait_recv()
    zsum[:n_f] = cgot[...]
    zsum[n_f] = jnp.zeros(zsum.shape[1:], f32)
    zsum[n_f, :, :hidden_rank] = rank_part
    zall[z] = zsum[...]
    ring.start(lambda to: zsum, zall, q_send, q_recv)
    ring.wait(zall, q_send, q_recv)
    total = zall[0]
    for t in range(1, n_z):
        total = total + zall[t]
    cond_out[...] = total[:n_f]
    dt = (total[n_f][:, :hidden_rank] * smask_ref[...]).astype(bf16)
    rank_out[...] = dt.astype(f32)
    wide = mm(dt, hot2)
    dts[f] = wide
    for j in range(1, n_f):
        push(dts.at[f], dts.at[f], t_send.at[j], t_recv.at[f], around[j - 1]).start()

    rs_end(0)
    if nbits > 1:
        rs_start(1)
    for j in range(1, n_f):
        came = (f - j + n_f) % n_f
        push(dts.at[came], dts.at[came], t_send.at[j], t_recv.at[came], (came, z)).wait_recv()
    all_dt = dts[...].reshape(n_f * 8, 128)
    row = lax.broadcasted_iota(jnp.int32, all_dt.shape, 0) % 8
    act = cond_ref[...].reshape(n_f * 8, cond_ref.shape[-1]).astype(bf16)
    mod_a = [
        dots(act, jnp.where(row < 2, all_dt, 0.0).astype(bf16), 0, 0),
        dots(act, pltpu.roll(jnp.where((row >= 2) & (row < 4), all_dt, 0.0), n_f * 8 - 2, 0).astype(bf16), 0, 0),
    ]
    if nbits > 1:
        rs_end(1)
    shard_out[...] = dense[block(f), :]
    for stream in range(2):
        first = starts[5 * stream][2]
        own = jnp.where(f == first // blk, 1.0, 0.0)
        count = mod_a[stream].shape[0]
        shard_out[:count, :] += own * mod_a[stream]

    swap.wait_send()
    ring.drain(lambda to: zmsg.at[to], zgot, z_send, z_recv)
    ring.drain(lambda to: zsum, zall, q_send, q_recv)
    for index, peer in enumerate(column):
        dmod_copy(index, peer).wait_send()
    for j in range(1, n_f):
        to = (f + j) % n_f
        push(own_dm, all_dm.at[f], f_send.at[j], f_recv.at[f], (to, z)).wait_send()
        push(cpart.at[to], cgot.at[f], p_send.at[j], p_recv.at[f], (to, z)).wait_send()
        push(dts.at[f], dts.at[f], t_send.at[j], t_recv.at[f], (to, z)).wait_send()
    for p in range(chips):
        push(snd1.at[p], rcv1.at[p], c_send.at[p], c_recv.at[p], (partner, z)).wait_send()
    for turn in range(nbits):
        for side in range(2):
            for index in range(len(masks_at(side, turn + 1))):
                rs_copy(side, turn, index).wait_send()
    for i in range(2):
        @pl.when(is_here(i))
        def _():
            pltpu.make_async_copy(grad_ref.at[i], grad_out.at[z % 2], g_recv.at[z % 2]).wait()

        @pl.when(jnp.logical_not(is_here(i)))
        def _():
            push(grad_out.at[i], grad_out.at[i], g_send.at[i], g_recv.at[i], home[i]).wait_recv()
            push(grad_ref.at[i], grad_out.at[z % 2], g_send.at[i], g_recv.at[z % 2], home[i]).wait_send()


def tail(dq, tdq, wq, smalls, img_a, img_b, txt_a, txt_b, hot4, hot2, wmod, bmod, tmod, cond, smask, n_f, n_z, fans, cols, cid, tn=768):
    f32, bf16 = jnp.float32, jnp.bfloat16
    vmem, dma = pltpu.VMEM, pltpu.SemaphoreType.DMA
    shape = jax.ShapeDtypeStruct
    args = (dq, tdq, wq, *smalls, *img_a, *img_b, *txt_a, *txt_b, hot4, hot2, wmod, bmod, tmod, cond, smask)
    lanes = (sum(fans[1:]) + sum(cols[1:])) // n_z
    rows = 2 * (sum(fans) + sum(cols)) // n_z
    blk = rows // n_f
    chips = n_f // 2
    cut = cols[0] // n_z
    rank = hot2.shape[0]
    _, img_rows, half = dq.shape
    _, k_local, _ = wq.shape
    width = cols[2]
    tx = smalls[9]
    thick = smalls[18].shape[0]
    pad = tx.shape[0]
    wide = width + thick
    inside, outside = pl.BlockSpec(memory_space=vmem), pl.BlockSpec(memory_space=pl.ANY)
    return pl.pallas_call(
        functools.partial(tail_kernel, n_f, n_z, tuple(fans), tuple(cols)),
        out_shape=[shape((2, img_rows // 2, width), bf16), shape((pad, width), f32), shape((n_f, 8, 256), f32), shape((8, rank), f32),
                   shape((blk, 128), f32)],
        in_specs=[outside] * 3 + [inside] * (len(args) - 3),
        out_specs=[outside] + [inside] * 4,
        scratch_shapes=[
            vmem((2, img_rows, half), bf16), vmem((2, n_f, k_local, tn), bf16), vmem((img_rows, width), f32), vmem((img_rows, RANK), f32),
            vmem((2, img_rows // 2, width), bf16), vmem((RANK, fans[1]), f32), vmem((RANK, cols[1]), f32), vmem(tdq.shape, bf16),
            vmem((n_z, pad, wide), f32), vmem((1, pad, wide), f32), vmem((1, n_z, pad, wide), bf16), vmem((1, n_z, pad, wide), bf16),
            vmem((n_z, pad, thick), bf16), vmem((thick, cols[1] // n_z), f32), vmem((n_z, 3, 8, width // n_z), f32), vmem((16, width), f32),
            vmem((n_z, RANK, lanes), bf16), vmem((n_z, RANK, lanes), bf16), vmem((rows, 128), f32),
            vmem((chips, blk, 128), bf16), vmem((chips, blk, 128), bf16),
            vmem((2, 3, blk // 2, 128), bf16), vmem((2, 3, blk // 2, 128), bf16),
            vmem((2 * n_z, 3, 8, width // n_z), f32), vmem((8, cut), f32), vmem((n_f, 8, cut), f32),
            vmem((n_f, 8, 256), f32), vmem((n_f, 8, 256), f32), vmem((n_f + 1, 8, 256), f32),
            vmem((n_z, n_f + 1, 8, 256), f32), vmem((n_f, 8, 128), f32),
            dma((2,)), dma((2,)), dma((n_z,)), dma((n_z,)), dma((chips,)), dma((chips,)), dma((2, 3)), dma((2, 3)),
            dma((2 * n_z,)), dma((2 * n_z,)), dma((n_f,)), dma((n_f,)), dma((n_f,)), dma((n_f,)), dma((n_z,)), dma((n_z,)),
            dma((n_f,)), dma((n_f,)), dma, dma, dma, dma((2,)), dma((2,)), dma((2,)), dma((1, n_z)), dma((1, n_z)), dma((n_z,)), dma((n_z,)),
        ],
        compiler_params=pltpu.CompilerParams(collective_id=cid, has_side_effects=True, vmem_limit_bytes=60 * 1024 * 1024),
        name="gradient_exchange",
    )(*args)

FULL = 4
PART = 4


def front_kernel(n_f, n_z, fans, cols, *refs):
    it = iter(refs)
    take = lambda count: [next(it) for _ in range(count)]
    ins = take(FULL + PART + 1)
    (x_ref, g_ref, picks_ref, hot2_ref, cblk_ref, clane_ref, c8_ref, smask_ref, wmod_ref, xt_ref, gt_ref, own_ref, tmask_ref, sign_ref) = take(14)
    outs = take(FULL + PART)
    x_out, g_out, imod_out, tmod_out = take(4)
    img_a, img_b, txt_a, txt_b = take(4), take(4), take(4), take(4)
    moda_out, modb_out, midm_out, cond_out, dm_out = take(5)
    ot_out, lse_out, bias_out, hot4_out = take(4)
    h_out, mid_out, heads_out, th_out, tmid_out, theads_out, att_out = take(7)
    (row_ref, fl_ref, img_msg, img_got, txt_msg, txt_got, cgot, mpart, mgot, own_mod, mod_got, wtile, wtxt, stage, tq_ref, sign_got, hot_got, img_buf, txt_buf, o_stage) = take(20)
    (z_send, z_recv, xy_send, xy_recv, core_send, core_recv, own_sem, x_send, x_recv, g_send, g_recv, c_send, c_recv, l_send,
     l_recv, m_send, m_recv, i_send, i_recv, t_send, t_recv, d_send, d_recv, a_send, a_recv, w_sem, tw_sem, h_send, h_recv,
     h_sem, q_send, q_recv, dm_send, dm_recv, s_send, s_recv, b_sem, o_send, o_recv, o_sem) = take(40)
    f32, bf16 = jnp.float32, jnp.bfloat16
    f, z, core, base, column = column_peers(n_z)
    chip = f // 2
    chips = n_f // 2
    nbits = bits_of(chips)
    partner = base + 1 - core
    others = [(flip_bits(chip, mask, nbits) * 2 + side, z) for mask in range(1, chips) for side in range(2)]
    meet(column + others)
    ring = ZRing(f, z, n_z)
    total = FULL + PART + 1
    adapters = total - 1
    blk = ins[adapters].shape[0]
    width = x_ref.shape[2]
    rank2 = hot2_ref.shape[0]

    def peer_of(mask):
        return flip_bits(chip, mask, nbits) * 2 + core

    def wide_of(m):
        return ins[m].shape[-1]

    def cuts(m):
        if m == adapters:
            return [(0, (0, blk // 2)), (1, (blk // 2, blk // 2))]
        return list(enumerate(halves(wide_of(m))))

    def place(m, who, zz, cut):
        off, w = cut
        if m == adapters:
            return row_ref.at[pl.ds(pl.multiple_of(who * blk + off, 16), w), :]
        if m < FULL:
            return outs[m].at[who, :, pl.ds(pl.multiple_of(zz * wide_of(m) + off, 128), w)]
        return outs[m].at[who, :, pl.ds(off, w)]

    def piece(m, cut):
        off, w = cut
        if m == adapters:
            return ins[m].at[pl.ds(off, w), :]
        return ins[m].at[:, pl.ds(off, w)]

    def whole_place(m, who, zz):
        return place(m, who, zz, (0, blk if m == adapters else wide_of(m)))

    def slot(m, zz):
        return zz if m < FULL else 0

    def order_of(half):
        order = list(range(nbits))
        return order if half == 0 else order[::-1]

    def xy_copy(m, zz, half, cut, mask, bit, own_piece=False):
        where = place(m, peer_of(mask), zz, cut)
        return push(piece(m, cut) if own_piece else where, where, xy_send.at[m, slot(m, zz), half, mask, bit],
                    xy_recv.at[m, slot(m, zz), half, mask | (1 << bit)], (peer_of(1 << bit), z))

    def xy_wait(m, zz, half, cut, mask):
        where = place(m, peer_of(mask), zz, cut)
        push(where, where, xy_send.at[m, slot(m, zz), half, 0, 0], xy_recv.at[m, slot(m, zz), half, mask], (partner, z)).wait_recv()

    def core_copy(m, zz, half, cut, mask, own_piece=False):
        where = place(m, peer_of(mask), zz, cut)
        return push(piece(m, cut) if own_piece else where, where, core_send.at[m, slot(m, zz), half, mask],
                    core_recv.at[m, slot(m, zz), half, mask], (partner, z))

    def core_wait(m, zz, half, cut, mask):
        where = place(m, peer_of(mask) - core + (1 - core), zz, cut)
        push(where, where, core_send.at[m, slot(m, zz), half, mask], core_recv.at[m, slot(m, zz), half, mask], (partner, z)).wait_recv()

    def own_copy(m):
        return pltpu.make_async_copy(ins[m], whole_place(m, f, z), own_sem.at[m])

    def z_copy(m, zz, up, own_piece=False):
        where = whole_place(m, f, zz)
        return push(ins[m] if own_piece else where, where, z_send.at[m, zz, up], z_recv.at[m, zz], (f, z + 1 if up else z - 1))

    def last_of(order, mask):
        return max([i for i, b in enumerate(order) if (mask >> b) & 1], default=-1)

    def masks_in_order(half):
        order = order_of(half)
        return sorted(range(1, 1 << nbits), key=lambda mask: [1 if (mask >> b) & 1 else 0 for b in reversed(order)])

    def launch(m, zz, own_piece=False):
        for half, cut in cuts(m):
            for bit in order_of(half):
                xy_copy(m, zz, half, cut, 0, bit, own_piece).start()
            core_copy(m, zz, half, cut, 0, own_piece).start()

    def launch_own(m):
        if m < FULL:
            @pl.when(z < n_z - 1)
            def _():
                z_copy(m, z, 1, True).start()

            @pl.when(z > 0)
            def _():
                z_copy(m, z, 0, True).start()
        launch(m, z, True)
        own_copy(m).start()

    def forward(m, zz):
        for half, cut in cuts(m):
            order = order_of(half)
            for mask in masks_in_order(half):
                if last_of(order, mask) < nbits - 1:
                    xy_wait(m, zz, half, cut, mask)
                    for b in order[last_of(order, mask) + 1:]:
                        xy_copy(m, zz, half, cut, mask, b).start()
                    core_copy(m, zz, half, cut, mask).start()

    def finish(m, zz):
        for half, cut in cuts(m):
            order = order_of(half)
            for mask in masks_in_order(half):
                if last_of(order, mask) == nbits - 1:
                    xy_wait(m, zz, half, cut, mask)
                    core_copy(m, zz, half, cut, mask).start()

    def settle(m, zz):
        for half, cut in cuts(m):
            for mask in range(1 << nbits):
                core_wait(m, zz, half, cut, mask)

    def drain(m, zz):
        for half, cut in cuts(m):
            order = order_of(half)
            for mask in range(1 << nbits):
                for b in order[last_of(order, mask) + 1:]:
                    xy_copy(m, zz, half, cut, mask, b).wait_send()
                core_copy(m, zz, half, cut, mask).wait_send()

    def at_distance(k, body):
        for sign in ((-1, 1) if k else (1,)):
            zz = z + sign * k

            @pl.when((zz >= 0) & (zz < n_z))
            def _():
                body(zz)

    def arrive(m, k):
        @pl.when(z - k >= 0)
        def _():
            zz = z - k
            z_copy(m, zz, 1).wait_recv()

            @pl.when(z < n_z - 1)
            def _():
                z_copy(m, zz, 1).start()

            launch(m, zz)

        @pl.when(z + k < n_z)
        def _():
            zz = z + k
            z_copy(m, zz, 0).wait_recv()

            @pl.when(z > 0)
            def _():
                z_copy(m, zz, 0).start()

            launch(m, zz)

    def every_z(m, body):
        if m < FULL:
            def step(zz, _):
                body(m, zz)
                return 0

            lax.fori_loop(0, n_z, step, 0)
        else:
            body(m, z)

    there = [(base + z // 2, 2 * core + s) for s in range(2)]

    def is_here(s):
        return (z // 2 == core) & (2 * core + s == z)

    def token_push(src, dst, send, recv, s):
        return push(src.at[s], dst.at[z % 2], send.at[s], recv.at[z % 2], there[s])

    def tokens_start(src, dst, send, recv):
        for s in range(2):
            @pl.when(is_here(s))
            def _():
                pltpu.make_async_copy(src.at[s], dst.at[z % 2], recv.at[z % 2]).start()

            @pl.when(jnp.logical_not(is_here(s)))
            def _():
                token_push(src, dst, send, recv, s).start()

    def tokens_wait(src, dst, send, recv):
        for i in range(2):
            @pl.when(is_here(i))
            def _():
                pltpu.make_async_copy(src.at[i], dst.at[z % 2], recv.at[z % 2]).wait()

            @pl.when(jnp.logical_not(is_here(i)))
            def _():
                push(dst.at[i], dst.at[i], send.at[i], recv.at[i], there[i]).wait_recv()

    def tokens_drain(src, dst, send, recv):
        for s in range(2):
            @pl.when(jnp.logical_not(is_here(s)))
            def _():
                token_push(src, dst, send, recv, s).wait_send()

    def around(src_of, dst, send, recv):
        return [push(src_of((f + j) % n_f), dst.at[f], send.at[j], recv.at[f], ((f + j) % n_f, z)) for j in range(1, n_f)]

    def around_wait(dst, send, recv):
        for j in range(1, n_f):
            came = (f - j + n_f) % n_f
            push(dst.at[came], dst.at[came], send.at[j], recv.at[came], (came, z)).wait_recv()

    cond_sends = around(lambda to: cblk_ref.at[to], cgot, c_send, c_recv)
    lane_sends = around(lambda to: clane_ref, cond_out, l_send, l_recv)
    mod_sends = around(lambda to: mpart.at[to], mgot, m_send, m_recv)

    sign_push = push(sign_ref, sign_got, s_send.at[0], s_recv.at[0], (partner, z))
    hot_push = push(hot2_ref, hot_got, s_send.at[1], s_recv.at[1], (partner, z))

    sign_push.start()
    hot_push.start()
    for copy in cond_sends + lane_sends:
        copy.start()
    launch_own(adapters)
    tokens_start(x_ref, x_out, x_send, x_recv)
    launch_own(FULL)
    launch_own(0)
    cgot[f] = cblk_ref[f]
    cond_out[f] = clane_ref[...]

    around_wait(cgot, c_send, c_recv)
    k_local = wmod_ref.shape[1]
    everyone = cgot[...].reshape(n_f * 8, cgot.shape[2])[:, :k_local].astype(bf16)
    mpart[...] = (mm(everyone, wmod_ref[0]) + pltpu.roll(mm(everyone, wmod_ref[1]), 2, 0)).reshape(mpart.shape)
    for copy in mod_sends:
        copy.start()
    mgot[f] = mpart[f]

    forward(adapters, z)
    forward(FULL, z)
    for m in (1, 2, 3):
        launch_own(m)
    for m in (FULL + 1, FULL + 2, FULL + 3):
        launch_own(m)
    for k in range(1, n_z):
        arrive(0, k)
    for m in (1, 2, 3):
        arrive(m, 1)
    for k in range(n_z):
        at_distance(k, lambda zz: forward(0, zz))

    finish(adapters, z)
    settle(adapters, z)
    own_copy(adapters).wait()
    hot2 = hot2_ref[...]
    starts = {}
    offset = 0
    for stream in range(2):
        for index in range(5):
            starts[stream, index] = (offset, offset + fans[index] // n_z)
            offset += fans[index] // n_z + cols[index] // n_z

    def pick_a(stream, index):
        at = starts[stream, index][0]
        return mm_t(hot2, row_ref[at:at + fans[index] // n_z, :]).astype(bf16)

    def pick_b(stream, index, s, put):
        at = starts[stream, index][1]
        count = cols[index] // n_z // NAD
        flat = row_ref[at:at + count, :].astype(f32) * picks_ref[s * NAD:s * NAD + 1, :]
        for k in range(1, NAD):
            begin = at + k * count
            flat = flat + row_ref[begin:begin + count, :].astype(f32) * picks_ref[s * NAD + k:s * NAD + k + 1, :]
        fl_ref[:count, :] = flat
        blocks = count // RANK
        for j in range(blocks):
            put(j * 128, fl_ref[pl.ds(j, RANK, stride=blocks), :].astype(bf16))

    spans_a, spans_b = [], []
    offset = 0
    for index in range(1, 5):
        count = fans[index] // n_z
        picked = pick_a(0, index)
        for s in range(2):
            img_msg[s, :, offset:offset + count] = picked[s * RANK:(s + 1) * RANK]
        spans_a.append((offset, count))
        offset += count
    for index in range(1, 5):
        count = cols[index] // n_z
        for s in range(2):
            def put(at, value, s=s, offset=offset):
                img_msg[s, :, offset + at:offset + at + 128] = value
            pick_b(0, index, s, put)
        spans_b.append((offset, count))
        offset += count

    def img_push(s, side):
        return push(img_msg.at[s], img_got.at[z], i_send.at[s, side], i_recv.at[z], (base + side, 2 * core + s))

    for s in range(2):
        for side in range(2):
            self_here = (side == core) & (2 * core + s == z)

            @pl.when(self_here)
            def _():
                img_got[z] = img_msg[s]

            @pl.when(jnp.logical_not(self_here))
            def _():
                img_push(s, side).start()

    share = width // n_z
    for place_at, (stream, index) in enumerate([(0, 0), (1, 0), (1, 1), (1, 3)]):
        txt_msg[:, place_at * share:(place_at + 1) * share] = pick_a(stream, index)
    for place_at, index in ((4, 2), (5, 4)):
        for s in range(2):
            def put(at, value, s=s, place_at=place_at):
                txt_msg[s * RANK:(s + 1) * RANK, place_at * share + at:place_at * share + at + 128] = value
            pick_b(1, index, s, put)
    txt_got[z] = txt_msg[...]
    ring.start(lambda to: txt_msg, txt_got, t_send, t_recv)
    for ref in txt_a + txt_b:
        ref[...] = jnp.zeros_like(ref)
    for index in (2, 4):
        txt_a[index - 1][:rank2, :] = pick_a(1, index)
    for ref, stream, index in ((txt_b[0], 1, 1), (txt_b[2], 1, 3), (modb_out.at[0], 0, 0), (modb_out.at[1], 1, 0)):
        for s in range(2):
            def put(at, value, ref=ref, s=s):
                ref[s * RANK:(s + 1) * RANK, at:at + 128] = value
            pick_b(stream, index, s, put)

    for k in (2, 3):
        for m in (1, 2, 3):
            arrive(m, k)
    for m in (1, 2, 3):
        forward(m, z)
    for m in (FULL + 1, FULL + 2, FULL + 3):
        forward(m, z)

    ring.wait(txt_got, t_send, t_recv)
    for t in range(n_z):
        lanes = slice(t * share, (t + 1) * share)
        got = lambda number: txt_got[t, :, number * share:(number + 1) * share]
        moda_out[0, :, lanes] = got(0)
        moda_out[1, :, lanes] = got(1)
        txt_a[0][:rank2, lanes] = got(2)
        txt_a[2][:rank2, lanes] = got(3)
        txt_b[1][:rank2, lanes] = got(4)
        txt_b[3][:rank2, lanes] = got(5)
    around_wait(mgot, m_send, m_recv)
    mod_sum = mgot[0]
    for j in range(1, n_f):
        mod_sum = mod_sum + mgot[j]
    c8 = c8_ref[...].astype(bf16)
    thin = mm_t(c8, moda_out[0])
    row = lax.broadcasted_iota(jnp.int32, thin.shape, 0)
    middle = (jnp.where(row < 2, thin, mm_t(c8, moda_out[1])) * smask_ref[...]).astype(bf16)
    low = jnp.where(row < 2, middle.astype(f32), 0.0)
    high = jnp.where((row >= 2) & (row < 4), middle.astype(f32), 0.0)
    midm_out[0] = low
    midm_out[1] = high
    own_mod[...] = mod_sum + mm(low.astype(bf16), modb_out[0]) + mm(high.astype(bf16), modb_out[1])

    def mod_push(index, peer):
        return push(own_mod, mod_got.at[core * n_z + z], d_send.at[index], d_recv.at[core * n_z + z], peer)

    for index, peer in enumerate(column):
        mod_push(index, peer).start()
    mod_got[core * n_z + z] = own_mod[...]

    for t in range(n_z):
        @pl.when(jnp.logical_not((z // 2 == core) & (t == z)))
        def _():
            push(img_got.at[t], img_got.at[t], i_send.at[0, 0], i_recv.at[t], (base + z // 2, t)).wait_recv()
    for t in range(n_z):
        for refs_of, spans in ((img_a, spans_a), (img_b, spans_b)):
            for ref, (begin, count) in zip(refs_of, spans):
                ref[:, t * count:(t + 1) * count] = img_got[t, :, begin:begin + count]

    for index, peer in enumerate(column):
        place_at = peer[0] % 2 * n_z + peer[1]
        push(mod_got.at[place_at], mod_got.at[place_at], d_send.at[index], d_recv.at[place_at], peer).wait_recv()
    step = width // 2
    per = own_mod.shape[1] // step
    imod_out[...] = jnp.zeros_like(imod_out)
    tmod_out[...] = jnp.zeros_like(tmod_out)
    for q in range(12):
        t, lanes = q // per, slice(q % per * step, (q % per + 1) * step)
        into = slice(q % 2 * step, (q % 2 + 1) * step)
        here = mod_got[z // 2 * n_z + t]
        imod_out[q // 2:q // 2 + 1, into] = jnp.where(z % 2 == 0, here[0:1, lanes], here[1:2, lanes])
        ours = mod_got[core * n_z + t]
        for s in range(2):
            tmod_out[8 * s + q // 2:8 * s + q // 2 + 1, into] = ours[2 + s:3 + s, lanes]

    own = own_ref[...]
    pick = lambda r: jnp.where(own > 0, tmod_out[r:r + 1, :], tmod_out[8 + r:9 + r, :])
    hat, _inv = norm_rows(xt_ref[...].astype(f32))
    th_out[z] = (hat * (1.0 + pick(1)) + pick(0)).astype(bf16)
    ring.start(lambda to: th_out.at[z], th_out, a_send, a_recv)
    dm_out[z] = (pick(5) * gt_ref[...].astype(f32)).astype(bf16)
    ring.start(lambda to: dm_out.at[z], dm_out, dm_send, dm_recv)
    tokens_wait(x_ref, x_out, x_send, x_recv)
    quarter = x_ref.shape[1]
    for i in range(2):
        def norm(r, _):
            sl = pl.ds(pl.multiple_of(r * ROWS, ROWS), ROWS)
            hat, _inv = norm_rows(x_out[i, sl, :].astype(f32))
            h_out[pl.ds(pl.multiple_of(i * quarter + r * ROWS, ROWS), ROWS), :] = (
                hat * (1.0 + imod_out[1:2, :]) + imod_out[0:1, :]).astype(bf16)
            return 0

        lax.fori_loop(0, quarter // ROWS, norm, 0)
    tokens_start(g_ref, g_out, g_send, g_recv)

    for m in (1, 2, 3):
        at_distance(1, lambda zz: forward(m, zz))

    finish(FULL, z)
    settle(FULL, z)
    own_copy(FULL).wait()
    load = pltpu.make_async_copy(outs[FULL], wtxt, tw_sem)
    load.start()
    ring.wait(th_out, a_send, a_recv)
    pad = xt_ref.shape[0]
    h_txt = th_out[...].reshape(n_z * pad, width)
    tmid = (mm_t(h_txt, txt_a[0][...]) * tmask_ref[...]).astype(bf16)
    tmid_out[...] = tmid
    load.wait()
    tq_ref[...] = (mm(h_txt, wtxt[...].reshape(width, wtxt.shape[2])) + mm(tmid, txt_b[0][...])).astype(bf16)
    for s in range(2):
        @pl.when(is_here(s))
        def _():
            copy = pltpu.make_async_copy(tq_ref, theads_out.at[z % 2], q_recv.at[z % 2])
            copy.start()
            copy.wait()

        @pl.when(jnp.logical_not(is_here(s)))
        def _():
            push(tq_ref, theads_out.at[z % 2], q_send.at[s], q_recv.at[z % 2], there[s]).start()

    every_z(0, finish)
    every_z(0, settle)
    own_copy(0).wait()
    mid = mm_t(h_out[...], img_a[0][...]).astype(bf16)
    mid_out[...] = mid
    tn = wtile.shape[3]
    per_half = stage.shape[2] // tn

    def tile_of(n):
        side = 1 - core if n < per_half else core
        return side, side * per_half + n % per_half

    def tile_load(n):
        at = pl.ds(pl.multiple_of(tile_of(n)[1] * tn, 128), tn)
        return pltpu.make_async_copy(outs[0].at[:, :, at], wtile.at[n % 2], w_sem.at[n % 2])

    def heads_push():
        return push(stage.at[0], heads_out.at[core], h_send, h_recv, (partner, z))

    tile_load(0).start()
    for n in range(2 * per_half):
        if n + 1 < 2 * per_half:
            tile_load(n + 1).start()
        tile_load(n).wait()
        at = pl.ds(pl.multiple_of(tile_of(n)[1] * tn, 128), tn)
        lanes = slice(n % per_half * tn, (n % per_half + 1) * tn)
        stage[n // per_half, :, lanes] = (
            mm(h_out[...], wtile[n % 2].reshape(width, tn)) + mm(mid, img_b[0][:, at])).astype(bf16)
        if n == per_half - 1:
            heads_push().start()
    keep = pltpu.make_async_copy(stage.at[1], heads_out.at[core], h_sem)
    keep.start()

    sign_push.wait_recv()
    chip_sign = jnp.where(z // 2 == core, sign_ref[...], sign_got[...])
    chip_sign = jnp.where(z % 2 == 0, chip_sign, -chip_sign)
    bias_out[...] = jnp.where(chip_sign > 0, 0.0, -1e30)
    hot_push.wait_recv()
    hot4_out[:rank2, :] = jnp.where(core == 0, hot2_ref[...].astype(f32), hot_got[...].astype(f32)).astype(bf16)
    hot4_out[rank2:, :] = jnp.where(core == 0, hot_got[...].astype(f32), hot2_ref[...].astype(f32)).astype(bf16)
    keep.wait()
    push(stage.at[0], heads_out.at[1 - core], h_send, h_recv, (partner, z)).wait_recv()
    for s in range(2):
        @pl.when(jnp.logical_not(is_here(s)))
        def _():
            push(theads_out.at[s], theads_out.at[s], q_send.at[s], q_recv.at[s], there[s]).wait_recv()
    pairs = heads_out.shape[2] // (6 * HD)
    per_part = pairs // 2

    def pair_loads(i):
        lanes = pl.ds(pl.multiple_of(i * (6 * HD), 128), 6 * HD)
        part = pl.ds(pl.multiple_of(i % per_part * (6 * HD), 128), 6 * HD)
        return [pltpu.make_async_copy(heads_out.at[:, :, lanes], img_buf.at[i % 2], b_sem.at[i % 2, 0]),
                pltpu.make_async_copy(theads_out.at[i // per_part, :, part], txt_buf.at[i % 2], b_sem.at[i % 2, 1])]

    def pair_lanes(i):
        return pl.ds(pl.multiple_of((core * pairs + i) * (2 * HD), 128), 2 * HD)

    def o_keep(i):
        return pltpu.make_async_copy(o_stage.at[i, core], att_out.at[:, pair_lanes(i)], o_sem.at[i])

    def o_push(i):
        return push(o_stage.at[i, 1 - core], att_out.at[:, pair_lanes(i)], o_send.at[i], o_recv.at[i], (partner, z))

    for copy in pair_loads(0):
        copy.start()
    tokens = img_buf.shape[1] * img_buf.shape[2]

    def pair_step(i, _):
        at = i % 2

        @pl.when(i + 1 < pairs)
        def _():
            for copy in pair_loads(i + 1):
                copy.start()

        for copy in pair_loads(i):
            copy.wait()
        bias = bias_out[:, 0:1]
        for h in range(2):
            low = 3 * HD * h
            ki = img_buf[at, :, :, low + HD:low + 2 * HD].reshape(tokens, HD)
            vi = img_buf[at, :, :, low + 2 * HD:low + 3 * HD].reshape(tokens, HD)
            kt = txt_buf[at, :, low + HD:low + 2 * HD]
            vt = txt_buf[at, :, low + 2 * HD:low + 3 * HD]
            for b in range(3):
                q = img_buf[at, b, :, low:low + HD] if b < 2 else txt_buf[at, :, low:low + HD]
                o, lse = attend_block(q, ki, vi, kt, vt, bias)
                rows = img_buf.shape[2]
                if b < 2:
                    o_stage[i, b, :, h * HD:(h + 1) * HD] = o
                    lse_out[i, h:h + 1, b * rows:(b + 1) * rows] = lse
                else:
                    ot_stage = o
                    lse_out[i, h:h + 1, tokens:tokens + q.shape[0]] = lse
            if h == 0:
                first = ot_stage
        both = jnp.concatenate([first, ot_stage], axis=1)
        ot_out[i // per_part, :, pl.ds(pl.multiple_of(i % per_part * (2 * HD), 128), 2 * HD)] = both
        o_keep(i).start()
        o_push(i).start()
        return 0

    lax.fori_loop(0, pairs // 2, pair_step, 0)
    for m in (1, 2, 3):
        at_distance(2, lambda zz: forward(m, zz))
    lax.fori_loop(pairs // 2, pairs, pair_step, 0)

    for m in (1, 2, 3):
        at_distance(n_z - 1, lambda zz: forward(m, zz))
    for m in range(total - 1):
        if m not in (0, FULL):
            every_z(m, finish)
    for m in range(total - 1):
        if m not in (0, FULL):
            every_z(m, settle)
            own_copy(m).wait()
    for m in range(total):
        every_z(m, drain)
        if m < FULL:
            def sent(zz, _):
                @pl.when((zz <= z) & (z < n_z - 1))
                def _():
                    z_copy(m, zz, 1).wait_send()

                @pl.when((zz >= z) & (z > 0))
                def _():
                    z_copy(m, zz, 0).wait_send()

                return 0

            lax.fori_loop(0, n_z, sent, 0)
    for copy in cond_sends + lane_sends + mod_sends:
        copy.wait_send()
    around_wait(cond_out, l_send, l_recv)
    ring.drain(lambda to: txt_msg, txt_got, t_send, t_recv)
    ring.drain(lambda to: th_out.at[z], th_out, a_send, a_recv)
    ring.wait(dm_out, dm_send, dm_recv)
    ring.drain(lambda to: dm_out.at[z], dm_out, dm_send, dm_recv)
    for index, peer in enumerate(column):
        mod_push(index, peer).wait_send()
    for s in range(2):
        for side in range(2):
            @pl.when(jnp.logical_not((side == core) & (2 * core + s == z)))
            def _():
                img_push(s, side).wait_send()
    tokens_wait(g_ref, g_out, g_send, g_recv)
    tokens_drain(x_ref, x_out, x_send, x_recv)
    tokens_drain(g_ref, g_out, g_send, g_recv)
    heads_push().wait_send()
    sign_push.wait_send()
    hot_push.wait_send()

    def o_done(i, _):
        o_keep(i).wait()
        o_push(i).wait_send()
        other = pl.ds(pl.multiple_of(((1 - core) * pairs + i) * (2 * HD), 128), 2 * HD)
        push(o_stage.at[i, 0], att_out.at[:, other], o_send.at[i], o_recv.at[i], (partner, z)).wait_recv()
        return 0

    lax.fori_loop(0, pairs, o_done, 0)
    for s in range(2):
        @pl.when(jnp.logical_not(is_here(s)))
        def _():
            push(tq_ref, theads_out.at[z % 2], q_send.at[s], q_recv.at[z % 2], there[s]).wait_send()


def front(full, part, adapter_rows, x, g, picks, hot2, cond, wmod, x_txt, g_txt, own, tmask, smask, sign_rows, n_f, n_z, fans, cols, cid):
    f32, bf16 = jnp.float32, jnp.bfloat16
    vmem, dma = pltpu.VMEM, pltpu.SemaphoreType.DMA
    shape = jax.ShapeDtypeStruct
    slots, width = cond.shape
    k_local = wmod.shape[1]
    z = lax.axis_index("tp")
    blocks = jnp.pad(jnp.swapaxes(cond.reshape(slots, n_f, k_local), 0, 1), ((0, 0), (0, 6), (0, 256 - k_local)))
    cond8 = jnp.concatenate([cond, cond, jnp.zeros((4, width), f32)])
    lane = jnp.pad(lax.dynamic_slice_in_dim(cond, z * (width // n_z), width // n_z, 1), ((0, 6), (0, 0)))
    chosen = (picks[:, None] == jnp.arange(NAD)[None, :]).astype(f32).reshape(-1, 1)
    smalls = (jnp.broadcast_to(chosen, (slots * NAD, 128)), hot2, blocks, lane, cond8, smask, wmod, x_txt, g_txt, own, tmask, sign_rows)
    args = (*full, *part, adapter_rows, x, g, *smalls)
    any_spec, in_vmem = pl.BlockSpec(memory_space=pl.ANY), pl.BlockSpec(memory_space=vmem)
    rows = 2 * (sum(fans) + sum(cols)) // n_z
    chips = n_f // 2
    nbits = bits_of(chips)
    total = len(full) + len(part) + 1
    pad = x_txt.shape[0]
    img_rows = 2 * x.shape[1]
    cut = cols[0] // n_z
    qkv_part = cols[1] // n_z
    thick = tmask.shape[1]
    rank2 = hot2.shape[0]
    own_a = [fans[1], fans[2] // n_z, fans[3], fans[4] // n_z]
    own_b = [cols[1] // n_z, cols[2], cols[3] // n_z, cols[4]]
    lanes = (sum(fans[1:]) + sum(cols[1:])) // n_z
    share = width // n_z
    outs = [shape((n_f,) + a.shape[:-1] + (a.shape[-1] * (n_z if i < len(full) else 1),), a.dtype) for i, a in enumerate(full + part)]
    in_hbm = len(outs)
    outs += [shape(x.shape, bf16), shape(g.shape, bf16), shape((8, width), f32), shape((16, width), f32)]
    outs += [shape((RANK, n), bf16) for n in fans[1:]] + [shape((RANK, n), bf16) for n in cols[1:]]
    outs += [shape((thick, n), bf16) for n in own_a] + [shape((thick, n), bf16) for n in own_b]
    outs += [shape((2, rank2, width), bf16), shape((2, rank2, cut), bf16), shape((2, 8, rank2), f32), shape((n_f, 8, share), f32), shape((n_z, pad, width), bf16)]
    heads_half = cols[1] // (6 * HD)
    pairs = heads_half // 2
    outs += [shape((2, n_z * pad, width // n_z), bf16), shape((pairs, 2, 2 * img_rows + n_z * pad), f32), shape(sign_rows.shape, f32),
             shape((2 * rank2, NAD * RANK), bf16)]
    outs += [shape((img_rows, width), bf16), shape((img_rows, RANK), bf16), shape((2, img_rows, cols[1] // 2), bf16),
             shape((n_z, pad, width), bf16), shape((n_z * pad, thick), bf16), shape((2, n_z * pad, qkv_part), bf16), shape((img_rows, width), bf16)]
    specs = [any_spec] * in_hbm + [in_vmem, any_spec] + [in_vmem] * (len(outs) - in_hbm - 2)
    for place in (1, 2, 5):
        specs[len(outs) - place] = any_spec
    return pl.pallas_call(
        functools.partial(front_kernel, n_f, n_z, tuple(fans), tuple(cols)),
        out_shape=outs,
        in_specs=[any_spec] * (total + 2) + [in_vmem] * len(smalls),
        out_specs=specs,
        scratch_shapes=[
            vmem((rows, 128), bf16), vmem((cut // NAD, 128), f32), vmem((2, RANK, lanes), bf16), vmem((n_z, RANK, lanes), bf16),
            vmem((rank2, 6 * share), bf16), vmem((n_z, rank2, 6 * share), bf16), vmem((n_f, 8, 256), f32),
            vmem((n_f, 8, cut), f32), vmem((n_f, 8, cut), f32), vmem((8, cut), f32), vmem((2 * n_z, 8, cut), f32),
            vmem((2, n_f, k_local, 768), bf16), vmem((n_f, k_local, qkv_part), bf16), vmem((2, img_rows, cols[1] // 2), bf16),
            vmem((n_z * pad, qkv_part), bf16), vmem(sign_rows.shape, f32), vmem((rank2, NAD * RANK), bf16),
            vmem((2, 2, img_rows, 6 * HD), bf16), vmem((2, n_z * pad, 6 * HD), bf16), vmem((pairs, 2, img_rows, 2 * HD), bf16),
            dma((total, n_z, 2)), dma((total, n_z)), dma((total, n_z, 2, chips, nbits)), dma((total, n_z, 2, chips)),
            dma((total, n_z, 2, chips)), dma((total, n_z, 2, chips)), dma((total,)),
            dma((2,)), dma((2,)), dma((2,)), dma((2,)), dma((n_f,)), dma((n_f,)), dma((n_f,)), dma((n_f,)), dma((n_f,)), dma((n_f,)),
            dma((2, 2)), dma((n_z,)), dma((n_z,)), dma((n_z,)), dma((2 * n_z,)), dma((2 * n_z,)), dma((n_z,)), dma((n_z,)),
            dma((2,)), dma, dma, dma, dma, dma((2,)), dma((2,)), dma((n_z,)), dma((n_z,)),
            dma((2,)), dma((2,)), dma((2, 2)), dma((pairs,)), dma((pairs,)), dma((pairs,)),
        ],
        compiler_params=pltpu.CompilerParams(collective_id=cid, has_side_effects=True, vmem_limit_bytes=58 * 1024 * 1024),
        name="front",
    )(*args)

HD = 64
FF = 6144
NAD = 8
RANK = 16
EPS = 1e-06
HIGH = lax.Precision.HIGHEST
F32 = jnp.float32
BF16 = jnp.bfloat16
BOTH = ("fsdp", "tp")


def matmul(left, right):
    return jnp.dot(left, right, preferred_element_type=F32)


def exact(left, right):
    return jnp.dot(left, right, precision=HIGH, preferred_element_type=F32)


def inner_left(left, right):
    return lax.dot_general(left, right, (((0,), (0,)), ((), ())), preferred_element_type=F32)


def inner_right(left, right):
    return lax.dot_general(
        left, right, (((left.ndim - 1,), (right.ndim - 1,)), ((), ())), preferred_element_type=F32
    )


def layer_norm(values):
    center = values - jnp.mean(values, axis=-1, keepdims=True)
    inverse = lax.rsqrt(jnp.mean(center * center, axis=-1, keepdims=True) + EPS)
    return (center * inverse, inverse)


def norm_back(grad_normed, normed, inverse, scale):
    grad_hat = grad_normed * (1.0 + scale)
    return inverse * (
        grad_hat
        - jnp.mean(grad_hat, axis=-1, keepdims=True)
        - normed * jnp.mean(grad_hat * normed, axis=-1, keepdims=True)
    )


def gelu(value):
    return jax.nn.gelu(value, approximate=True)


def gelu_back(value, grad):
    return jax.vjp(gelu, value)[1](grad)[0]


def shards(
    image_tokens,
    text_tokens,
    conditioning,
    text_lengths,
    adapter_index,
    adapters,
    mod_weight,
    qkv_weight,
    out_weight,
    fc1_weight,
    fc2_weight,
    image_cot,
    text_cot,
):
    n_f, n_z = lax.axis_size("fsdp"), lax.axis_size("tp")
    f, z = lax.axis_index("fsdp"), lax.axis_index("tp")
    core = f % 2
    slots, quarter, width = image_tokens.shape
    txt_local = text_tokens.shape[0]
    txt_group = txt_local * n_z
    img_half = 2 * quarter
    img_n = 2 * img_half
    cols = [6 * width, 3 * width, width, FF, width]
    fans = [width, width, width, width, FF]

    def round_pairs(r):
        pairs = []
        for fa in range(n_f):
            for t in range(n_z):
                there = (fa // 2 * 2 + t // 2) * n_z + 2 * (fa % 2) + (r ^ (t % 2))
                pairs.append((fa * n_z + t, there))
        return pairs

    low_bit = z % 2

    def pick(stack, bit):
        return lax.dynamic_index_in_dim(stack, bit, 0, keepdims=False)

    def flip(r):
        return low_bit if r == 0 else 1 - low_bit

    def to_chip(parts):
        got = [lax.ppermute(parts[r], BOTH, round_pairs(r)) for r in range(2)]
        return jnp.where(low_bit == 0, got[0], got[1]), jnp.where(low_bit == 0, got[1], got[0])

    def from_chip(pieces):
        got = []
        for r in range(2):
            mine = jnp.where(flip(r) == 0, pieces[0], pieces[1])
            got.append(lax.ppermute(mine, BOTH, [(b, a) for a, b in round_pairs(r)]))
        return jnp.where(low_bit == 0, got[0], got[1]), jnp.where(low_bit == 0, got[1], got[0])

    def reshard(values):
        return jnp.concatenate(to_chip([pick(values, flip(r)) for r in range(2)]), axis=0)

    def unshard(values):
        return jnp.stack(from_chip([values[:quarter], values[quarter:]]))

    def swap_core(values):
        return lax.ppermute(values, "fsdp", [(i, i ^ 1) for i in range(n_f)])

    def by_core(mine, other, axis):
        first = jnp.where(core == 0, mine, other)
        second = jnp.where(core == 0, other, mine)
        return jnp.concatenate([first, second], axis=axis)

    def z_swap(values, step):
        return lax.ppermute(values, "tp", [(i, i ^ step) for i in range(n_z)])

    def z_order(pieces):
        stack = jnp.stack(pieces)
        return [pick(stack, z ^ a) for a in range(n_z)]

    def z_gather(values):
        return z_order([values] + [z_swap(values, j) for j in range(1, n_z)])

    def z_exchange(blocks):
        return z_order([pick(blocks, z ^ j) if j == 0 else z_swap(pick(blocks, z ^ j), j) for j in range(n_z)])

    def z_scatter(values):
        count = values.shape[0] // n_z
        mine = lax.dynamic_slice_in_dim(values, z * count, count, 0)
        for j in range(1, n_z):
            part = lax.dynamic_slice_in_dim(values, (z ^ j) * count, count, 0)
            mine = mine + z_swap(part.astype(BF16), j).astype(F32)
        return mine

    def to_heads(values):
        half = values.shape[1] // 2
        low, high = values[:, :half], values[:, half:]
        mine = jnp.where(core == 0, low, high)
        return by_core(mine, swap_core(jnp.where(core == 0, high, low)), 0)

    def to_tokens(values):
        low, high = values[:img_half], values[img_half:]
        mine = jnp.where(core == 0, low, high)
        return by_core(mine, swap_core(jnp.where(core == 0, high, low)), 1)

    out_t = jnp.swapaxes(out_weight, 1, 2)
    fc2_t = jnp.swapaxes(fc2_weight, 1, 2)
    local = [qkv_weight, out_t, fc1_weight, fc2_t]
    adapter_rows = lax.optimization_barrier(adapters.reshape(-1, 128)).astype(BF16)
    txt_pad = (txt_local + 15) // 16 * 16

    def padded(values):
        return jnp.pad(values, ((0, txt_pad - txt_local), (0, 0)))

    x_txt_low, g_txt_low = padded(text_tokens), padded(text_cot)
    x_txt = x_txt_low.astype(F32)

    seg_ends = jnp.cumsum(text_lengths[0])
    slot_ids = jnp.arange(slots)

    def owner_of(position):
        segment = jnp.sum((position[:, None] >= seg_ends[None, :]).astype(jnp.int32), axis=1)
        return (segment[:, None] == slot_ids[None, :]).astype(F32)

    def real(owner):
        place = jnp.arange(owner.shape[0]) % txt_pad
        return jnp.where((place < txt_local)[:, None], owner, 0.0)

    def position(rows):
        return rows // txt_pad * txt_local + rows % txt_pad

    txt_rows = jnp.arange(n_z * txt_pad)
    owner_group = real(owner_of(position(txt_rows)))
    owner_local = real(owner_of(z * txt_local + jnp.arange(txt_pad)))
    txt_mask = jnp.repeat(owner_group, RANK, axis=1)
    txt_mask_local = jnp.repeat(owner_local, RANK, axis=1)
    rank_cols = slots * RANK
    seq_mask = jnp.repeat(jnp.eye(slots, dtype=F32), RANK, axis=1)

    def by_group(mine, other):
        return by_core(mine, other, 0)

    def stretch(stream, index):
        if stream == 0:
            return img_mod[:, index * width : (index + 1) * width]
        return exact(owner_local, txt_mods[:, index * width : (index + 1) * width])

    def collapse(stream, values):
        if stream == 0:
            return jnp.sum(values, axis=0, keepdims=True)
        return exact(owner_local.T, values)

    def share(values):
        return jnp.concatenate(z_gather(values), axis=0)

    def give(values, rank_part):
        got = z_scatter(jnp.concatenate([values, rank_part], axis=1))
        return got[:, :width], (got[:, width:] * txt_mask_local).astype(BF16)

    def lanes(values):
        count = values.shape[1] // n_z
        return lax.dynamic_slice_in_dim(values, z * count, count, 1)

    def project(values, weight, pair, mask, flipped):
        middle = inner_right(values, pair[0])
        if mask is not None:
            middle = middle * mask
        middle = middle.astype(BF16)
        main = inner_right(values, weight) if flipped else matmul(values, weight)
        return middle, main + matmul(middle, pair[1])

    own_hot = (
        jnp.arange(NAD * RANK)[:, None]
        == (adapter_index[:, None] * RANK + jnp.arange(RANK)[None, :]).reshape(1, -1)
    ).astype(F32)
    k_local = mod_weight.shape[1]
    cond_act = jax.nn.silu(conditioning).astype(BF16)
    thick = 128

    def thicker(part):
        return jnp.concatenate([part, jnp.zeros((thick - part.shape[0], part.shape[1]), part.dtype)], axis=0)

    def sign(owner):
        return owner[:, 0:1] - owner[:, 1:2]

    def lanes_pad(mask):
        return jnp.pad(mask, ((0, 0), (0, thick - mask.shape[1])))

    if n_f == 8:
        slot_mask = jnp.pad(jnp.concatenate([seq_mask, seq_mask]), ((0, 4), (0, 0)))
        made = front(
            [w[0] for w in local], [w[1] for w in local], adapter_rows, image_tokens, image_cot,
            adapter_index, own_hot.T.astype(BF16), cond_act.astype(F32), mod_weight, x_txt_low,
            g_txt_low, sign(owner_local), lanes_pad(txt_mask), slot_mask,
            jnp.broadcast_to(sign(owner_group), (owner_group.shape[0], thick)), n_f, n_z, fans, cols, 1,
        )
        made = iter(made)
        take = lambda count: [next(made) for _ in range(count)]
        img_w = [w.reshape(-1, w.shape[-1]) for w in take(4)]
        txt_w = [w.reshape(-1, w.shape[-1]) for w in take(4)]
        x_img, g_img = [v.reshape(-1, width) for v in take(2)]
        img_rows_mod, txt_mod = take(2)
        img_pairs = [None] + list(zip(take(4), take(4)))
        thick_pairs = [None] + list(zip(take(4), take(4)))
        mod_a, mod_b, tmod, cond_own, txt_dm = take(5)
        o_txt, lse, bias, hot_four = take(4)
        bias = bias[:, :1]
        img_in, img_qkv_mid, img_heads, txt_in, txt_qkv_mid, txt_heads, attended = take(7)
        img_heads = img_heads.reshape(img_n, -1)
        txt_in = txt_in.reshape(-1, width)
        txt_pairs = [None, tuple(part[:rank_cols] for part in thick_pairs[1])]
        img_mod = img_rows_mod[:6].reshape(1, -1)
        txt_mods = txt_mod.reshape(slots, 8, width)[:, :6].reshape(slots, -1)
    else:
        column_picks = by_group(adapter_index, swap_core(adapter_index))
        column_count = 2 * slots
        one_hot = (
            jnp.arange(NAD * RANK)[:, None]
            == (column_picks[:, None] * RANK + jnp.arange(RANK)[None, :]).reshape(1, -1)
        ).astype(F32)
        got = gather([w[0] for w in local], [w[1] for w in local] + [adapter_rows], n_f, n_z)
        got = [g.reshape(-1, g.shape[-1]) for g in got]
        img_w, txt_w, row = got[:4], got[4:8], got[8]
        x_img = reshard(image_tokens)
        g_img = reshard(image_cot)
        own_picks = adapter_index

        a_rows = [[None] * 5 for stream in range(2)]
        b_rows = [[None] * 5 for stream in range(2)]
        offset = 0
        for stream in range(2):
            for index in range(5):
                count = fans[index] // n_z
                a_rows[stream][index] = row[offset : offset + count]
                offset += count
                count = cols[index] // n_z
                b_rows[stream][index] = row[offset : offset + count]
                offset += count

        def b_pick(stream, index, pick_index):
            part = b_rows[stream][index]
            count = part.shape[0] // NAD
            return lax.dynamic_slice_in_dim(part, pick_index * count, count, 0).reshape(RANK, -1)

        def a_pick(rows, hot):
            return inner_right(hot.T.astype(BF16), rows).astype(BF16)

        img_a = a_pick(jnp.concatenate(a_rows[0], axis=0), one_hot)
        fan_share = sum(fans) // n_z
        img_a = img_a.reshape(column_count, RANK, fan_share)
        img_b = [
            jnp.concatenate([b_pick(0, index, column_picks[s]) for index in range(1, 5)], axis=1)
            for s in range(column_count)
        ]
        img_msg = jnp.concatenate([img_a, jnp.stack(img_b)], axis=2)
        txt_a_rows = jnp.concatenate(
            [a_rows[0][0], a_rows[1][0], a_rows[1][1], a_rows[1][3]], axis=0
        )
        txt_a = a_pick(txt_a_rows, own_hot).reshape(slots, RANK, -1)
        txt_b_own = [
            [b_pick(stream, index, own_picks[s]) for s in range(slots)]
            for stream, index in [(0, 0), (1, 0), (1, 1), (1, 2), (1, 3), (1, 4)]
        ]
        txt_b_own = [jnp.concatenate(parts, axis=0) for parts in txt_b_own]
        txt_a_own = a_pick(jnp.concatenate([a_rows[1][2], a_rows[1][4]], axis=0), own_hot)
        txt_msg = jnp.concatenate(
            [txt_a.reshape(slots * RANK, -1), txt_b_own[3], txt_b_own[5]], axis=1
        )
        img_got = jnp.stack(z_exchange(img_msg))
        txt_got = jnp.stack(z_gather(txt_msg))

        def join(part):
            return jnp.swapaxes(part, 0, 1).reshape(part.shape[1], -1)

        img_pairs = []
        offset, b_offset = 0, fan_share
        for index in range(5):
            count = fans[index] // n_z
            a_full = join(img_got[:, :, offset : offset + count])
            offset += count
            if index == 0:
                img_pairs.append(None)
                continue
            count = cols[index] // n_z
            b_full = join(img_got[:, :, b_offset : b_offset + count])
            b_offset += count
            img_pairs.append((a_full, b_full))
        txt_full = []
        offset = 0
        for count in [width // n_z] * 6:
            txt_full.append(join(txt_got[:, :, offset : offset + count]))
            offset += count
        mod_a = [txt_full[0], txt_full[1]]
        mod_b = [txt_b_own[0], txt_b_own[1]]
        txt_pairs = [
            None,
            (txt_full[2], txt_b_own[2]),
            (txt_a_own[:, : width // n_z], txt_full[4]),
            (txt_full[3], txt_b_own[4]),
            (txt_a_own[:, width // n_z :], txt_full[5]),
        ]

        cond_all = lax.all_gather(cond_act, "fsdp", axis=0, tiled=True)
        cond_slice = lax.dynamic_slice_in_dim(cond_all, f * k_local, k_local, 1)
        mod_part = jnp.stack([matmul(cond_slice, mod_weight[stream]) for stream in range(2)], axis=1)
        mod_part = lax.psum_scatter(mod_part, "fsdp", scatter_dimension=0, tiled=True)
        mod_mid = []
        mod_terms = []
        for stream in range(2):
            middle = (inner_right(cond_act, mod_a[stream]) * seq_mask).astype(BF16)
            mod_mid.append(middle)
            mod_terms.append(mod_part[:, stream] + matmul(middle, mod_b[stream]))
        mods = jnp.concatenate(z_gather(jnp.stack(mod_terms, axis=1)), axis=2)
        img_mods = by_group(mods[:, 0], swap_core(mods[:, 0]))
        img_mod = lax.dynamic_slice_in_dim(img_mods, z, 1, 0)
        txt_mods = mods[:, 1]

        img_rows_mod = jnp.concatenate([img_mod.reshape(6, width), jnp.zeros((2, width), F32)], axis=0)
        txt_mod = jnp.pad(txt_mods.reshape(slots, 6, width), ((0, 0), (0, 2), (0, 0))).reshape(-1, width)
        thick_pairs = [None] + [tuple(thicker(part) for part in txt_pairs[index]) for index in range(1, 5)]
        norm_first = [layer_norm(v.astype(F32)) for v in (x_img, x_txt)]
        heads_in = [
            (norm_first[s][0] * (1.0 + stretch(s, 1)) + stretch(s, 0)).astype(BF16) for s in range(2)
        ]

        txt_in = share(heads_in[1])
        txt_qkv_mid, txt_qkv = project(txt_in, txt_w[0], txt_pairs[1], txt_mask, False)
        img_qkv_mid, img_qkv = project(heads_in[0], img_w[0], img_pairs[1], None, False)
        txt_qkv, img_qkv = txt_qkv.astype(BF16), img_qkv.astype(BF16)
        img_heads = to_heads(img_qkv)
        txt_heads = jnp.stack(to_chip([txt_qkv, txt_qkv]))
        img_in = heads_in[0]
        txt_dm = jnp.stack(z_gather((stretch(1, 5) * g_txt_low.astype(F32)).astype(BF16)))

    inputs = [x_img.astype(F32), x_txt]
    norm_one = [layer_norm(values) for values in inputs]
    def txt_home(values):
        got = from_chip([values[0], values[1]])
        return jnp.where(owner_group[:, 0:1] > 0, got[0], jnp.where(owner_group[:, 1:2] > 0, got[1], 0))

    if n_f != 8:
        lengths = by_group(text_lengths[0:1], swap_core(text_lengths[0:1]))
        chip_lengths = jnp.cumsum(lax.dynamic_index_in_dim(lengths, z // slots, 0, keepdims=False))
        chip_slot = z % slots
        chip_segment = jnp.sum(
            (position(txt_rows)[:, None] >= chip_lengths[None, :]).astype(jnp.int32),
            axis=1,
            keepdims=True,
        )
        chip_owner = (chip_segment == chip_slot) & (txt_rows % txt_pad < txt_local)[:, None]
        bias = jnp.where(chip_owner, 0.0, -1e30).astype(F32)
        o_img, o_txt, lse = attend(img_heads, txt_heads, bias, HD)

        attended = to_tokens(o_img)
    (img_branch, img_after, img_mlp, img_pre, img_result, *img_mids, img_gate, txt_mlp, txt_att, txt_after, txt_branch) = both_fwd(
        attended, x_img, g_img, img_rows_mod, img_w[1], img_pairs[2], img_pairs[3], img_w[2], img_pairs[4], img_w[3],
        o_txt, x_txt_low, txt_mod, sign(owner_group), sign(owner_local), lanes_pad(txt_mask_local), txt_w[1], thick_pairs[2],
        n_z, 2,
    )
    made = both_back(
        g_img, img_after, img_branch, img_mlp, attended, img_rows_mod, img_pre, img_w[3], img_pairs[4], img_w[2], img_pairs[3],
        img_w[1], img_pairs[2], img_mids, g_txt_low, txt_after, txt_branch, txt_mod, sign(owner_local), lanes_pad(txt_mask),
        lanes_pad(txt_mask_local), txt_mlp, txt_att, txt_dm, txt_w[1], txt_w[2], txt_w[3], thick_pairs[2], thick_pairs[3],
        thick_pairs[4], n_z, 4,
    )
    img_grad_after, img_grad_att, img_sums, *sides = made[:9]
    txt_result, txt_grad_after, do_txt, txt_sums, *txt_sides = made[9:]
    if n_f != 8:
        txt_sides = [part[:rank_cols] for part in txt_sides]
    txt_sum_rows = txt_sums
    txt_sums = txt_sums.reshape(4, slots, width)
    image_out = unshard(img_result)

    grads = [[None] * 5 for stream in range(2)]

    def project_back(grad, weight, pair, mask, flipped):
        middle = inner_right(grad, pair[1])
        if mask is not None:
            middle = middle * mask
        middle = middle.astype(BF16)
        main = matmul(grad, weight) if flipped else inner_right(grad, weight)
        return middle, main + matmul(middle, pair[0])

    grads[0][4] = (sides[0], sides[3])
    grads[0][3] = (sides[2], sides[1])
    grads[0][2] = (sides[4], sides[5])
    mod_parts = [[None] * 6 for stream in range(2)]
    for place in range(4):
        mod_parts[1][2 + place] = txt_sums[place]
    grads[1][2] = (txt_sides[0], txt_sides[1])
    grads[1][3] = (txt_sides[2], txt_sides[3])
    grads[1][4] = (txt_sides[4], txt_sides[5])
    img_sum_rows = img_sums
    img_sums = jnp.sum(jnp.concatenate([img_sums, img_gate]).reshape(4, 8, width), axis=1)
    for place in range(4):
        mod_parts[0][2 + place] = img_sums[place : place + 1]
    grad_after = [img_grad_after, txt_grad_after]

    do_img = to_heads(img_grad_att)
    d_img, d_txt = attend_back(img_heads, txt_heads, bias, do_img, do_txt, lse, HD)
    if n_f == 8:
        sides_of = lambda stream, side: [grads[stream][index][side] for index in range(2, 5)]
        smalls = (
            x_img, img_grad_after, img_in, img_rows_mod, img_qkv_mid, *img_pairs[1], img_sum_rows, img_gate,
            x_txt_low, txt_grad_after, txt_in.reshape(n_z, txt_pad, width), txt_mod, sign(owner_group), sign(owner_local),
            lanes_pad(txt_mask_local), txt_qkv_mid, txt_w[0], *thick_pairs[1], txt_sum_rows,
        )
        image_low, txt_grad, cond_slices, mod_rank, shard = tail(
            d_img.reshape(2, img_half, -1), d_txt, img_w[0].reshape(n_f, k_local, -1), smalls,
            sides_of(0, 0), sides_of(0, 1), sides_of(1, 0), sides_of(1, 1),
            hot_four, own_hot.T.astype(BF16), mod_weight, mod_b, tmod, cond_own, slot_mask,
            n_f, n_z, fans, cols, 3,
        )
        image_grad = image_low.astype(F32)
        cond_rows = jnp.swapaxes(cond_slices[:, :slots, :k_local], 0, 1).reshape(slots, width)
        for s in range(2):
            cond_rows = cond_rows + matmul(mod_rank[2 * s : 2 * s + 2].astype(BF16), mod_a[s])
        cond_grad = jax.vjp(jax.nn.silu, conditioning)[1](cond_rows)[0]
        adapter_grad = shard.reshape(1, -1)
        return (image_out, txt_result[:txt_local], image_grad, txt_grad[:txt_local], cond_grad, adapter_grad)
    img_grad_qkv = to_tokens(d_img)
    txt_grad_qkv = txt_home(d_txt)

    img_back_mid, img_grad_norm = project_back(img_grad_qkv, img_w[0], img_pairs[1], None, False)
    grads[0][1] = (inner_left(img_back_mid, img_in), inner_left(img_qkv_mid, img_grad_qkv))
    txt_grad_norm, txt_qkv_back = give(
        inner_right(txt_grad_qkv, txt_w[0]), inner_right(txt_grad_qkv, txt_pairs[1][1])
    )
    txt_grad_norm = txt_grad_norm + matmul(txt_qkv_back, txt_pairs[1][0])
    grads[1][1] = (
        inner_left(share(txt_qkv_back), lanes(txt_in)),
        inner_left(txt_qkv_mid, txt_grad_qkv),
    )
    grad_norm = [img_grad_norm, txt_grad_norm]
    grad_inputs = []
    for s in range(2):
        grad_inputs.append(
            grad_after[s]
            + norm_back(grad_norm[s], norm_one[s][0], norm_one[s][1], stretch(s, 1))
        )
        mod_parts[s][0] = collapse(s, grad_norm[s])
        mod_parts[s][1] = collapse(s, grad_norm[s] * norm_one[s][0])
    img_dmod = jnp.concatenate(mod_parts[0], axis=1)
    txt_dmod = jnp.concatenate(mod_parts[1], axis=1)
    image_grad = unshard(grad_inputs[0].astype(BF16)).astype(F32)

    img_dmod = (img_dmod + swap_core(img_dmod)).astype(BF16)
    def lane_blocks(values):
        return jnp.swapaxes(values.reshape(values.shape[0], n_z, -1), 0, 1)

    img_dmods = jnp.concatenate(z_exchange(lane_blocks(img_dmod)), axis=0)
    img_dmods = lax.dynamic_slice_in_dim(img_dmods, core * slots, slots, 0)
    txt_dmods = sum(z_exchange(lane_blocks(txt_dmod))).astype(BF16)
    dmods = jnp.stack([img_dmods, txt_dmods], axis=1)
    dmods_all = lax.all_gather(dmods, "fsdp", axis=0, tiled=True)
    cond_part = sum(inner_right(dmods_all[:, s], mod_weight[s]) for s in range(2))
    mod_back = [inner_right(dmods[:, s], mod_b[s]) for s in range(2)]
    cond_part = cond_part.reshape(-1, width // n_f)
    joined = jnp.concatenate([cond_part.reshape(-1), jnp.stack(mod_back).reshape(-1)])
    joined = sum(z_gather(joined))
    cond_slices = joined[: cond_part.size].reshape(n_f, -1, width // n_f)
    mod_rank = joined[cond_part.size :].reshape(2, slots, -1)
    cond_rows = lax.all_to_all(cond_slices, "fsdp", 0, 2, tiled=True)[0]
    for s in range(2):
        back_mid = (mod_rank[s] * seq_mask).astype(BF16)
        cond_rows = cond_rows + matmul(back_mid, mod_a[s])
        grads[s][0] = (inner_left(back_mid, lanes(cond_act)), inner_left(mod_mid[s], dmods[:, s]))
    cond_grad = jax.vjp(jax.nn.silu, conditioning)[1](cond_rows)[0]

    def spread(values):
        return jnp.swapaxes(values.reshape(RANK, n_z, -1), 0, 1)

    img_rows = {}
    for group in ((2, 3, 4), (1,)):
        parts = [spread(grads[0][index][side]) for side in range(2) for index in group]
        parts = jnp.concatenate(z_exchange(jnp.concatenate(parts, axis=2)), axis=0)
        offset = 0
        for side, sizes in enumerate((fans, cols)):
            for index in group:
                count = sizes[index] // n_z
                img_rows[side, index] = parts[:, offset : offset + count]
                offset += count
    flat = []
    for stream in range(2):
        for index in range(5):
            if stream == 0 and index > 0:
                part_a, part_b = img_rows[0, index], img_rows[1, index]
                hot = one_hot
            else:
                part_a, part_b = grads[stream][index]
                hot = own_hot
            flat.append(
                lax.dot_general(
                    part_a, hot, (((0,), (1,)), ((), ())),
                    precision=HIGH, preferred_element_type=F32,
                )
            )
            flat.append(exact(hot, part_b).reshape(-1, 128))
    total = jnp.concatenate(flat, axis=0).reshape(n_f, -1, 128)
    step = 1
    while step < n_f:
        bit = (f // step) % 2
        pairs = total.reshape((-1, 2) + total.shape[1:])
        keep = lax.dynamic_index_in_dim(pairs, bit, 1, keepdims=False)
        send = lax.dynamic_index_in_dim(pairs, 1 - bit, 1, keepdims=False)
        sent = lax.ppermute(send.astype(BF16), "fsdp", [(i, i ^ step) for i in range(n_f)])
        total = keep + sent.astype(F32)
        step *= 2
    adapter_grad = total.reshape(1, -1)
    return (
        image_out, txt_result[:txt_local], image_grad, grad_inputs[1][:txt_local], cond_grad, adapter_grad
    )


def solution(mesh):
    return jax.shard_map(
        shards,
        mesh=mesh,
        in_specs=(
            P("fsdp", "tp", None),
            P(("fsdp", "tp"), None),
            P("fsdp", None),
            P("fsdp", None),
            P("fsdp"),
            P("tp", "fsdp"),
            P(None, "fsdp", "tp"),
            P(None, "fsdp", "tp"),
            P(None, "tp", "fsdp"),
            P(None, "fsdp", "tp"),
            P(None, "tp", "fsdp"),
            P("fsdp", "tp", None),
            P(("fsdp", "tp"), None),
        ),
        out_specs=(
            P("fsdp", "tp", None),
            P(("fsdp", "tp"), None),
            P("fsdp", "tp", None),
            P(("fsdp", "tp"), None),
            P("fsdp", None),
            P("tp", "fsdp"),
        ),
        check_vma=False,
    )
```

```python
import functools

import jax
import jax.numpy as jnp
from jax import lax
from jax.experimental import pallas as pl
from jax.experimental.pallas import tpu as pltpu
from jax.sharding import PartitionSpec as P

MESH = pl.DeviceIdType.MESH

def bits_of(count):
    return max(count.bit_length() - 1, 0)

def halves(width):
    tiles = width // 128
    first = (tiles + 1) // 2 * 128
    return [(0, first), (first, width - first)]

def gather_kernel(n_f, n_z, full_count, part_count, *refs):
    total = full_count + part_count
    ins, outs = refs[:total], refs[total:2 * total]
    z_send, z_recv, xy_send, xy_recv, core_send, core_recv, own_sem = refs[2 * total:]
    f = lax.axis_index("fsdp")
    z = lax.axis_index("tp")
    chip, core = f // 2, f % 2
    chips = n_f // 2
    nbits = bits_of(chips)
    partner = chip * 2 + (1 - core)

    def peer_of(mask):
        other = 0
        for bit in range(nbits):
            have = (chip // (1 << bit)) % 2
            want = 1 - have if (mask >> bit) & 1 else have
            other = other + want * (1 << bit)
        return other * 2 + core

    barrier = pltpu.get_barrier_semaphore()
    for bit in range(nbits):
        pl.semaphore_signal(barrier, inc=1, device_id=(peer_of(1 << bit), z), device_id_type=MESH)
    pl.semaphore_signal(barrier, inc=1, device_id=(partner, z), device_id_type=MESH)
    @pl.when(z > 0)
    def _():
        pl.semaphore_signal(barrier, inc=1, device_id=(f, z - 1), device_id_type=MESH)
    @pl.when(z < n_z - 1)
    def _():
        pl.semaphore_signal(barrier, inc=1, device_id=(f, z + 1), device_id_type=MESH)
    peers = nbits + 1 + (z > 0).astype(jnp.int32) + (z < n_z - 1).astype(jnp.int32)
    pl.semaphore_wait(barrier, peers)

    def width(m):
        return ins[m].shape[-1]

    def place(m, who, zz, off=0, w=None):
        w = width(m) if w is None else w
        if m < full_count:
            return outs[m].at[who, :, pl.ds(pl.multiple_of(zz * width(m) + off, 128), w)]
        if w == width(m):
            return outs[m].at[who]
        return outs[m].at[who, :, pl.ds(off, w)]

    def piece(m, off, w):
        return ins[m] if w == width(m) else ins[m].at[:, pl.ds(off, w)]

    def remote(src, dst, ssem, rsem, dev):
        return pltpu.make_async_remote_copy(src_ref=src, dst_ref=dst, send_sem=ssem, recv_sem=rsem, device_id=dev, device_id_type=MESH)

    def order_of(half):
        order = list(range(nbits))
        return order if half == 0 else order[::-1]

    def cuts(m):
        if width(m) >= 256:
            return list(enumerate(halves(width(m))))
        return [(m % 2, (0, width(m)))]

    def slot(m, zz):
        return zz if m < full_count else 0

    def xy_copy(m, zz, half, cut, mask, bit, own_piece=False):
        off, w = cut
        who = peer_of(mask)
        source = piece(m, off, w) if own_piece and mask == 0 else place(m, who, zz, off, w)
        return remote(source, place(m, who, zz, off, w),
                      xy_send.at[m, slot(m, zz), half, mask, bit], xy_recv.at[m, slot(m, zz), half, mask | (1 << bit)],
                      (peer_of(1 << bit), z))

    def xy_wait(m, zz, half, cut, mask):
        off, w = cut
        who = peer_of(mask)
        remote(place(m, who, zz, off, w), place(m, who, zz, off, w), xy_send.at[m, slot(m, zz), half, 0, 0],
               xy_recv.at[m, slot(m, zz), half, mask], (partner, z)).wait_recv()

    def core_copy(m, zz, half, cut, mask, own_piece=False):
        off, w = cut
        who = peer_of(mask)
        source = piece(m, off, w) if own_piece and mask == 0 else place(m, who, zz, off, w)
        return remote(source, place(m, who, zz, off, w),
                      core_send.at[m, slot(m, zz), half, mask], core_recv.at[m, slot(m, zz), half, mask], (partner, z))

    def core_wait_recv(m, zz, half, cut, mask):
        off, w = cut
        who = peer_of(mask) - core + (1 - core)
        remote(place(m, who, zz, off, w), place(m, who, zz, off, w),
               core_send.at[m, slot(m, zz), half, mask], core_recv.at[m, slot(m, zz), half, mask], (partner, z)).wait_recv()

    def own(m):
        return pltpu.make_async_copy(ins[m], place(m, f, z), own_sem.at[m])

    def z_copy(m, zz, up, own_piece=False):
        return remote(ins[m] if own_piece else place(m, f, zz), place(m, f, zz), z_send.at[m, zz, up], z_recv.at[m, zz], (f, z + 1 if up else z - 1))

    def launch(m, zz, own_piece=False):
        for half, cut in cuts(m):
            for bit in order_of(half):
                xy_copy(m, zz, half, cut, 0, bit, own_piece).start()
            core_copy(m, zz, half, cut, 0, own_piece).start()

    def masks_in_order(half):
        order = order_of(half)
        def rank(mask):
            return [1 if (mask >> b) & 1 else 0 for b in reversed(order)]
        return sorted(range(1, 1 << nbits), key=rank)

    def forward(m, zz):
        for half, cut in cuts(m):
            order = order_of(half)
            for mask in masks_in_order(half):
                last = max(i for i, b in enumerate(order) if (mask >> b) & 1)
                if last == nbits - 1:
                    continue
                xy_wait(m, zz, half, cut, mask)
                for b in order[last + 1:]:
                    xy_copy(m, zz, half, cut, mask, b).start()
                core_copy(m, zz, half, cut, mask).start()

    def finish(m, zz):
        for half, cut in cuts(m):
            order = order_of(half)
            for mask in masks_in_order(half):
                last = max(i for i, b in enumerate(order) if (mask >> b) & 1)
                if last == nbits - 1:
                    xy_wait(m, zz, half, cut, mask)
                    core_copy(m, zz, half, cut, mask).start()

    def drain(m, zz):
        for half, cut in cuts(m):
            order = order_of(half)
            for mask in [0] + masks_in_order(half):
                last = max([i for i, b in enumerate(order) if (mask >> b) & 1], default=-1)
                for b in order[last + 1:]:
                    xy_copy(m, zz, half, cut, mask, b).wait_send()
                core_copy(m, zz, half, cut, mask).wait_send()
                core_wait_recv(m, zz, half, cut, mask)

    for m in range(total):
        own(m).start()
    for m in range(total):
        if m < full_count:
            @pl.when(z < n_z - 1)
            def _():
                z_copy(m, z, 1, True).start()
            @pl.when(z > 0)
            def _():
                z_copy(m, z, 0, True).start()
        launch(m, z, True)
    for m in range(full_count, total):
        forward(m, z)
    for k in range(1, n_z):
        for m in range(full_count):
            @pl.when(z - k >= 0)
            def _():
                zz = z - k
                z_copy(m, zz, 1).wait_recv()
                @pl.when(z < n_z - 1)
                def _():
                    z_copy(m, zz, 1).start()
                launch(m, zz)
            @pl.when(z + k < n_z)
            def _():
                zz = z + k
                z_copy(m, zz, 0).wait_recv()
                @pl.when(z > 0)
                def _():
                    z_copy(m, zz, 0).start()
                launch(m, zz)
            for sign in ((-1, 1) if k > 1 else (1,)):
                zz = z + sign * (k - 1)
                @pl.when((zz >= 0) & (zz < n_z))
                def _():
                    forward(m, zz)
    for m in range(full_count):
        for sign in (-1, 1):
            zz = z + sign * (n_z - 1)
            @pl.when((zz >= 0) & (zz < n_z))
            def _():
                forward(m, zz)
    for m in range(total):
        if m < full_count:
            def body(zz, _):
                finish(m, zz)
                return 0
            lax.fori_loop(0, n_z, body, 0)
        else:
            finish(m, z)
    for m in range(total):
        own(m).wait()
        if m < full_count:
            def body(zz, _):
                drain(m, zz)
                @pl.when((zz <= z) & (z < n_z - 1))
                def _():
                    z_copy(m, zz, 1).wait_send()
                @pl.when((zz >= z) & (z > 0))
                def _():
                    z_copy(m, zz, 0).wait_send()
                return 0
            lax.fori_loop(0, n_z, body, 0)
        else:
            drain(m, z)

def gather(full, part, n_f, n_z, cid=1):
    arrays = list(full) + list(part)
    total = len(arrays)
    if n_f > 8:
        rows = [lax.all_gather(a, "fsdp", axis=0, tiled=True) for a in arrays]
        return [
            lax.all_gather(a, "tp", axis=1, tiled=True) if i < len(full) else a
            for i, a in enumerate(rows)
        ]
    chips = n_f // 2
    nbits = bits_of(chips)
    shapes = [jax.ShapeDtypeStruct((n_f,) + a.shape[:-1] + (a.shape[-1] * (n_z if i < len(full) else 1),), a.dtype) for i, a in enumerate(arrays)]
    dma = pltpu.SemaphoreType.DMA
    return pl.pallas_call(
        functools.partial(gather_kernel, n_f, n_z, len(full), len(part)),
        out_shape=shapes,
        in_specs=[pl.BlockSpec(memory_space=pl.ANY)] * total,
        out_specs=[pl.BlockSpec(memory_space=pl.ANY)] * total,
        scratch_shapes=[
            dma((total, n_z, 2)), dma((total, n_z)),
            dma((total, n_z, 2, chips, max(nbits, 1))), dma((total, n_z, 2, chips)),
            dma((total, n_z, 2, chips)), dma((total, n_z, 2, chips)), dma((total,)),
        ],
        compiler_params=pltpu.CompilerParams(collective_id=cid, has_side_effects=True),
        name="weight_gather",
    )(*arrays)

def dots(left, right, lc, rc):
    return lax.dot_general(left, right, (((lc,), (rc,)), ((), ())), preferred_element_type=jnp.float32)

def attend_block(q, ki, vi, kt, vt, bias):
    q = q * jnp.bfloat16(0.125)
    si = dots(ki, q, 1, 1)
    st = dots(kt, q, 1, 1) + bias
    top = jnp.maximum(jnp.max(si, axis=0, keepdims=True), jnp.max(st, axis=0, keepdims=True))
    ei = jnp.exp(si - top)
    et = jnp.exp(st - top)
    total = jnp.sum(ei, axis=0, keepdims=True) + jnp.sum(et, axis=0, keepdims=True)
    o = dots(vi, ei.astype(jnp.bfloat16), 0, 0) + dots(vt, et.astype(jnp.bfloat16), 0, 0)
    return (o / total).T.astype(jnp.bfloat16), top + jnp.log(total)


def attend_kernel(hd, bq, img_ref, txt_ref, bias_ref, oi_ref, ot_ref, lse_ref):
    img_n, txt_n = img_ref.shape[0], txt_ref.shape[1]
    heads = img_ref.shape[1] // (3 * hd)
    bias = bias_ref[...]
    for h in range(heads):
        base = 3 * hd * h
        ki = img_ref[:, base + hd:base + 2 * hd]
        vi = img_ref[:, base + 2 * hd:base + 3 * hd]
        kt = txt_ref[0, :, base + hd:base + 2 * hd]
        vt = txt_ref[0, :, base + 2 * hd:base + 3 * hd]

        def block(q):
            q = q * jnp.bfloat16(0.125)
            si = dots(ki, q, 1, 1)
            st = dots(kt, q, 1, 1) + bias
            top = jnp.maximum(jnp.max(si, axis=0, keepdims=True), jnp.max(st, axis=0, keepdims=True))
            ei = jnp.exp(si - top)
            et = jnp.exp(st - top)
            total = jnp.sum(ei, axis=0, keepdims=True) + jnp.sum(et, axis=0, keepdims=True)
            o = dots(vi, ei.astype(jnp.bfloat16), 0, 0) + dots(vt, et.astype(jnp.bfloat16), 0, 0)
            return (o / total).T.astype(jnp.bfloat16), top + jnp.log(total)

        for i in range(img_n // bq):
            o, lse = block(img_ref[i * bq:(i + 1) * bq, base:base + hd])
            oi_ref[i * bq:(i + 1) * bq, h * hd:(h + 1) * hd] = o
            lse_ref[0, h:h + 1, i * bq:(i + 1) * bq] = lse
        o, lse = block(txt_ref[0, :, base:base + hd])
        ot_ref[0, :, h * hd:(h + 1) * hd] = o
        lse_ref[0, h:h + 1, img_n:img_n + txt_n] = lse

def attend(img, txt, bias, hd, bq=512):
    img_n, cols = img.shape
    parts, txt_n, _ = txt.shape
    pairs = cols // (6 * hd)
    per = pairs // parts
    return pl.pallas_call(
        functools.partial(attend_kernel, hd, bq),
        grid=(pairs,),
        in_specs=[
            pl.BlockSpec((img_n, 6 * hd), lambda i: (0, i)),
            pl.BlockSpec((1, txt_n, 6 * hd), lambda i: (i // per, 0, i % per)),
            pl.BlockSpec((txt_n, 1), lambda i: (0, 0)),
        ],
        out_specs=[
            pl.BlockSpec((img_n, 2 * hd), lambda i: (0, i)),
            pl.BlockSpec((1, txt_n, 2 * hd), lambda i: (i // per, 0, i % per)),
            pl.BlockSpec((1, 2, img_n + txt_n), lambda i: (i, 0, 0)),
        ],
        out_shape=[
            jax.ShapeDtypeStruct((img_n, pairs * 2 * hd), jnp.bfloat16),
            jax.ShapeDtypeStruct((parts, txt_n, per * 2 * hd), jnp.bfloat16),
            jax.ShapeDtypeStruct((pairs, 2, img_n + txt_n), jnp.float32),
        ],
        compiler_params=pltpu.CompilerParams(vmem_limit_bytes=48 * 1024 * 1024),
        name="attend",
    )(img, txt, bias)

def attend_back_kernel(hd, bq, img_ref, txt_ref, bias_ref, doi_ref, dot_ref, lse_ref, di_ref, dt_ref, acc_i, acc_t):
    img_n, txt_n = img_ref.shape[0], txt_ref.shape[1]
    heads = img_ref.shape[1] // (3 * hd)
    bias = bias_ref[...]
    for h in range(heads):
        base = 3 * hd * h
        ki = img_ref[:, base + hd:base + 2 * hd]
        vi = img_ref[:, base + 2 * hd:base + 3 * hd]
        kt = txt_ref[0, :, base + hd:base + 2 * hd]
        vt = txt_ref[0, :, base + 2 * hd:base + 3 * hd]

        def block(q, do, lse, first):
            q = q * jnp.bfloat16(0.125)
            pi = jnp.exp(dots(ki, q, 1, 1) - lse)
            pt = jnp.exp(dots(kt, q, 1, 1) + bias - lse)
            dwi = dots(vi, do, 1, 1)
            dwt = dots(vt, do, 1, 1)
            delta = jnp.sum(pi * dwi, axis=0, keepdims=True) + jnp.sum(pt * dwt, axis=0, keepdims=True)
            dsi = (pi * (dwi - delta)).astype(jnp.bfloat16)
            dst = (pt * (dwt - delta)).astype(jnp.bfloat16)
            dvi = dots(pi.astype(jnp.bfloat16), do, 1, 0)
            dvt = dots(pt.astype(jnp.bfloat16), do, 1, 0)
            dki = dots(dsi, q, 1, 0)
            dkt = dots(dst, q, 1, 0)
            if first:
                acc_i[0], acc_i[1], acc_t[0], acc_t[1] = dki, dvi, dkt, dvt
            else:
                acc_i[0] += dki
                acc_i[1] += dvi
                acc_t[0] += dkt
                acc_t[1] += dvt
            dq = dots(ki, dsi, 0, 0) + dots(kt, dst, 0, 0)
            return (dq.T * 0.125).astype(jnp.bfloat16)

        for i in range(img_n // bq):
            rows = slice(i * bq, (i + 1) * bq)
            di_ref[rows, base:base + hd] = block(
                img_ref[rows, base:base + hd], doi_ref[rows, h * hd:(h + 1) * hd], lse_ref[0, h:h + 1, rows], i == 0)
        grad = jnp.where(bias < 0, 0.0, dot_ref[0, :, h * hd:(h + 1) * hd].astype(jnp.float32)).astype(jnp.bfloat16)
        dt_ref[0, :, base:base + hd] = block(
            txt_ref[0, :, base:base + hd], grad, lse_ref[0, h:h + 1, img_n:img_n + txt_n], False)
        di_ref[:, base + hd:base + 2 * hd] = acc_i[0].astype(jnp.bfloat16)
        di_ref[:, base + 2 * hd:base + 3 * hd] = acc_i[1].astype(jnp.bfloat16)
        dt_ref[0, :, base + hd:base + 2 * hd] = acc_t[0].astype(jnp.bfloat16)
        dt_ref[0, :, base + 2 * hd:base + 3 * hd] = acc_t[1].astype(jnp.bfloat16)

def attend_back_far_kernel(hd, bq, n_z, fans, cols, img_ref, txt_ref, bias_ref, doi_ref, dot_ref, lse_ref, y_ref, *refs):
    img_a, img_b, rest = refs[:3], refs[3:6], refs[6:]
    di_ref, dt_ref, y_out, z_out, acc_i, acc_t, zmsg, y_send, y_recv, z_send, z_recv = rest
    step = pl.program_id(0)
    f, z, core, base, column = column_peers(n_z)
    ring = ZRing(f, z, n_z)
    there = [(base + z // 2, 2 * core + i) for i in range(2)]

    def is_here(i):
        return (z // 2 == core) & (2 * core + i == z)

    def y_keep(i):
        return pltpu.make_async_copy(y_ref.at[i], y_out.at[z % 2], y_recv.at[z % 2])

    def y_push(i):
        return push(y_ref.at[i], y_out.at[z % 2], y_send.at[i], y_recv.at[z % 2], there[i])

    def z_keep():
        return pltpu.make_async_copy(zmsg.at[z], z_out.at[z], z_recv.at[z])

    @pl.when(step == 0)
    def _():
        meet(column)
        offset = 0
        for part, sizes in ((img_a, fans), (img_b, cols)):
            for index in range(3):
                count = sizes[index + 2] // n_z
                for t in range(n_z):
                    zmsg[t, :, offset:offset + count] = part[index][:, t * count:(t + 1) * count].astype(jnp.bfloat16)
                offset += count
        ring.start(lambda to: zmsg.at[to], z_out, z_send, z_recv)
        z_keep().start()
        for i in range(2):
            @pl.when(is_here(i))
            def _():
                y_keep(i).start()

            @pl.when(jnp.logical_not(is_here(i)))
            def _():
                y_push(i).start()

    attend_back_kernel(hd, bq, img_ref, txt_ref, bias_ref, doi_ref, dot_ref, lse_ref, di_ref, dt_ref, acc_i, acc_t)

    @pl.when(step == pl.num_programs(0) - 1)
    def _():
        z_keep().wait()
        ring.wait(z_out, z_send, z_recv)
        ring.drain(lambda to: zmsg.at[to], z_out, z_send, z_recv)
        for i in range(2):
            @pl.when(is_here(i))
            def _():
                y_keep(i).wait()

            @pl.when(jnp.logical_not(is_here(i)))
            def _():
                push(y_out.at[i], y_out.at[i], y_send.at[i], y_recv.at[i], there[i]).wait_recv()
                y_push(i).wait_send()


def attend_back_far(img, txt, bias, doi, dot, lse, hd, y, img_a, img_b, n_z, fans, cols, cid, bq=512):
    img_n, wide_n = img.shape
    parts, txt_n, _ = txt.shape
    pairs = wide_n // (6 * hd)
    per = pairs // parts
    vmem, dma = pltpu.VMEM, pltpu.SemaphoreType.DMA
    bf16, shape = jnp.bfloat16, jax.ShapeDtypeStruct
    wide = pl.BlockSpec((img_n, 6 * hd), lambda i: (0, i))
    wide_t = pl.BlockSpec((1, txt_n, 6 * hd), lambda i: (i // per, 0, i % per))
    outside = pl.BlockSpec(memory_space=pl.ANY)
    sides = (*img_a, *img_b)
    lanes = (sum(fans[2:]) + sum(cols[2:])) // n_z
    return pl.pallas_call(
        functools.partial(attend_back_far_kernel, hd, bq, n_z, tuple(fans), tuple(cols)),
        grid=(pairs,),
        in_specs=[
            wide, wide_t,
            pl.BlockSpec((txt_n, 1), lambda i: (0, 0)),
            pl.BlockSpec((img_n, 2 * hd), lambda i: (0, i)),
            pl.BlockSpec((1, txt_n, 2 * hd), lambda i: (i // per, 0, i % per)),
            pl.BlockSpec((1, 2, img_n + txt_n), lambda i: (i, 0, 0)),
            outside,
        ] + [pl.BlockSpec(v.shape, lambda i: (0, 0)) for v in sides],
        out_specs=[wide, wide_t, outside, outside],
        out_shape=[shape(img.shape, bf16), shape(txt.shape, bf16), shape(y.shape, bf16), shape((n_z, RANK, lanes), bf16)],
        scratch_shapes=[vmem((2, img_n, hd), jnp.float32), vmem((2, txt_n, hd), jnp.float32), vmem((n_z, RANK, lanes), bf16),
                        dma((2,)), dma((2,)), dma((n_z,)), dma((n_z,))],
        compiler_params=pltpu.CompilerParams(collective_id=cid, has_side_effects=True, vmem_limit_bytes=56 * 1024 * 1024),
        name="attend_back",
    )(img, txt, bias, doi, dot, lse, y, *sides)


def attend_back(img, txt, bias, doi, dot, lse, hd, bq=512):
    img_n, cols = img.shape
    parts, txt_n, _ = txt.shape
    pairs = cols // (6 * hd)
    per = pairs // parts
    wide = pl.BlockSpec((img_n, 6 * hd), lambda i: (0, i))
    wide_t = pl.BlockSpec((1, txt_n, 6 * hd), lambda i: (i // per, 0, i % per))
    return pl.pallas_call(
        functools.partial(attend_back_kernel, hd, bq),
        grid=(pairs,),
        in_specs=[
            wide, wide_t,
            pl.BlockSpec((txt_n, 1), lambda i: (0, 0)),
            pl.BlockSpec((img_n, 2 * hd), lambda i: (0, i)),
            pl.BlockSpec((1, txt_n, 2 * hd), lambda i: (i // per, 0, i % per)),
            pl.BlockSpec((1, 2, img_n + txt_n), lambda i: (i, 0, 0)),
        ],
        out_specs=[wide, wide_t],
        out_shape=[jax.ShapeDtypeStruct(img.shape, jnp.bfloat16), jax.ShapeDtypeStruct(txt.shape, jnp.bfloat16)],
        scratch_shapes=[pltpu.VMEM((2, img_n, hd), jnp.float32), pltpu.VMEM((2, txt_n, hd), jnp.float32)],
        compiler_params=pltpu.CompilerParams(vmem_limit_bytes=48 * 1024 * 1024),
        name="attend_back",
    )(img, txt, bias, doi, dot, lse)

ROWS = 64


def mm(left, right):
    return dots(left, right, 1, 0)


def mm_t(left, right):
    return dots(left, right, 1, 1)


def t_mm(left, right):
    return dots(left, right, 0, 0)


def gelu_parts(u):
    scale = 0.7978845608028654
    square = u * u
    tanh = jnp.tanh(scale * (u + 0.044715 * u * square))
    half = 0.5 * (1.0 + tanh)
    slope = half + 0.5 * u * (1.0 - tanh * tanh) * (scale * (1.0 + 3 * 0.044715 * square))
    return u * half, slope


def norm_rows(v):
    center = v - jnp.mean(v, axis=-1, keepdims=True)
    inverse = lax.rsqrt(jnp.mean(center * center, axis=-1, keepdims=True) + 1e-06)
    return center * inverse, inverse


def column_peers(n_z):
    f, z = lax.axis_index("fsdp"), lax.axis_index("tp")
    core = f % 2
    base = f - core
    peers = [(f, (z + j) % n_z) for j in range(1, n_z)]
    peers += [(base + 1 - core, (z + j) % n_z) for j in range(n_z)]
    return f, z, core, base, peers


def meet(peers):
    barrier = pltpu.get_barrier_semaphore()
    for peer in peers:
        pl.semaphore_signal(barrier, inc=1, device_id=peer, device_id_type=MESH)
    pl.semaphore_wait(barrier, len(peers))


def push(src, dst, send, recv, peer):
    return pltpu.make_async_remote_copy(
        src_ref=src, dst_ref=dst, send_sem=send, recv_sem=recv, device_id=peer, device_id_type=MESH)


class ZRing:
    def __init__(self, f, z, n_z):
        self.f, self.z, self.n_z = f, z, n_z

    def start(self, source_of, buf, send, recv):
        for j in range(1, self.n_z):
            to = (self.z + j) % self.n_z
            push(source_of(to), buf.at[self.z], send.at[j], recv.at[self.z], (self.f, to)).start()

    def wait(self, buf, send, recv):
        for j in range(1, self.n_z):
            came = (self.z + j) % self.n_z
            push(buf.at[came], buf.at[came], send.at[j], recv.at[came], (self.f, came)).wait_recv()

    def drain(self, source_of, buf, send, recv):
        for j in range(1, self.n_z):
            to = (self.z + j) % self.n_z
            push(source_of(to), buf.at[self.z], send.at[j], recv.at[self.z], (self.f, to)).wait_send()


def text_tools(n_z, pad, width, f, z, lmask_ref, part_ref, mine_ref, out_buf, in_buf, rs_send, rs_recv, ag_send, ag_recv):
    ring = ZRing(f, z, n_z)
    bf16, f32 = jnp.bfloat16, jnp.float32

    def scatter(turn, main, rank_part):
        full = jnp.concatenate([main, rank_part], axis=1)
        full = full.reshape(n_z, pad, full.shape[1])
        part_ref[...] = full
        mine_ref[turn] = part_ref[z]
        out_buf[turn] = full.astype(bf16)
        ring.start(lambda to: out_buf.at[turn, to], in_buf.at[turn], rs_send.at[turn], rs_recv.at[turn])

    def collect(turn):
        ring.wait(in_buf.at[turn], rs_send.at[turn], rs_recv.at[turn])
        total = mine_ref[turn]
        for j in range(1, n_z):
            total = total + in_buf[turn, (z + j) % n_z].astype(f32)
        ring.drain(lambda to: out_buf.at[turn, to], in_buf.at[turn], rs_send.at[turn], rs_recv.at[turn])
        return total[:, :width], (total[:, width:] * lmask_ref[...]).astype(bf16)

    def spread(ref, *parts):
        offset = 0
        for part in parts:
            ref[z, :, offset:offset + part.shape[1]] = part
            offset += part.shape[1]
        ring.start(lambda to: ref.at[z], ref, ag_send, ag_recv)

    def spread_end(ref):
        ring.wait(ref, ag_send, ag_recv)
        ring.drain(lambda to: ref.at[z], ref, ag_send, ag_recv)

    def gathered(ref, start, count):
        return ref[:, :, start:start + count].reshape(n_z * pad, count)

    def own_lanes(ref, share):
        at = pl.ds(pl.multiple_of(z * share, 128), share)
        return ref[:, :, at].reshape(n_z * pad, share)

    return scatter, collect, spread, spread_end, gathered, own_lanes


def rows_of(mod_ref, own_ref):
    return lambda row: jnp.where(own_ref[...] > 0, mod_ref[row:row + 1, :], mod_ref[8 + row:9 + row, :])


def both_fwd_kernel(tiles, n_z, turns, o_ref, x_ref, g_ref, mod_ref, wo_ref, ao_ref, bo_ref, a1_ref, b1_ref, w1_ref, a2_ref, w2_ref, b2_ref,
                    ot_ref, xt_ref, tmod_ref, owner_ref, own_ref, lmask_ref, two_ref, tao_ref, tbo_ref,
                    a_out, x1_out, h2_out, u_out, y_out, to_out, t1_out, t2_out, gate_out,
                    tall_out, att_out, tx1_out, tbr_out,
                    m_acc, t2_acc, o_got, part_ref, mine_ref, out_buf, in_buf, ag_ref, o_send, o_recv, rs_send, rs_recv, ag_send, ag_recv):
    step = pl.program_id(0)
    f, z, core, base, column = column_peers(n_z)
    pad, width_t = xt_ref.shape
    f32, bf16 = jnp.float32, jnp.bfloat16
    scatter, collect, spread, spread_end, gathered, own_lanes = text_tools(
        n_z, pad, width_t, f, z, lmask_ref, part_ref, mine_ref, out_buf, in_buf, rs_send, rs_recv, ag_send, ag_recv)
    home = [(base + z // 2, 2 * core + i) for i in range(2)]

    def is_here(i):
        return (z // 2 == core) & (2 * core + i == z)

    def o_push(i):
        return push(ot_ref.at[i], o_got.at[z % 2], o_send.at[i], o_recv.at[z % 2], home[i])

    @pl.when(step == 0)
    def _():
        meet(column)
        for i in range(2):
            @pl.when(is_here(i))
            def _():
                copy = pltpu.make_async_copy(ot_ref.at[i], o_got.at[z % 2], o_recv.at[z % 2])
                copy.start()
                copy.wait()

            @pl.when(jnp.logical_not(is_here(i)))
            def _():
                o_push(i).start()

    rows = o_ref.shape[0]
    width = o_ref.shape[1]


    @pl.when(step == 0)
    def _():
        to = mm_t(o_ref[...], ao_ref[...]).astype(jnp.bfloat16)
        to_out[...] = to

        def cols(n, _):
            sl = pl.ds(pl.multiple_of(n * 256, 256), 256)
            a = mm_t(o_ref[...], wo_ref[sl, :]) + mm(to_out[...], bo_ref[:, sl])
            a_out[:, sl] = a.astype(jnp.bfloat16)
            x1_out[:, sl] = x_ref[:, sl].astype(jnp.float32) + mod_ref[2:3, sl] * a
            return 0

        lax.fori_loop(0, width // 256, cols, 0)

        def norm(r, _):
            sl = pl.ds(pl.multiple_of(r * ROWS, ROWS), ROWS)
            xh, _inv = norm_rows(x1_out[sl, :])
            h2_out[sl, :] = (xh * (1.0 + mod_ref[4:5, :]) + mod_ref[3:4, :]).astype(jnp.bfloat16)
            return 0

        lax.fori_loop(0, rows // ROWS, norm, 0)
        t1_out[...] = mm_t(h2_out[...], a1_ref[...]).astype(jnp.bfloat16)
        m_acc[...] = jnp.zeros_like(m_acc)
        t2_acc[...] = jnp.zeros_like(t2_acc)

    u = mm(h2_out[...], w1_ref[...]) + mm(t1_out[...], b1_ref[...])
    u_out[...] = u
    f = gelu_parts(u)[0].astype(jnp.bfloat16)
    m_acc[...] += mm_t(f, w2_ref[...])
    t2_acc[...] += mm_t(f, a2_ref[...])


    @pl.when(step == turns[0])
    def _():
        for i in range(2):
            @pl.when(jnp.logical_not(is_here(i)))
            def _():
                push(o_got.at[i], o_got.at[i], o_send.at[i], o_recv.at[i], home[i]).wait_recv()
                o_push(i).wait_send()
        owner = owner_ref[...]
        att = jnp.where(owner > 0, o_got[0].astype(f32), jnp.where(owner < 0, o_got[1].astype(f32), 0.0)).astype(bf16)
        att_out[...] = att
        scatter(0, mm_t(att, two_ref[...]), mm_t(att, tao_ref[...]))

    @pl.when(step == turns[1])
    def _():
        modulation = rows_of(tmod_ref, own_ref)
        branch, to_mine = collect(0)
        branch = branch + mm(to_mine, tbo_ref[...])
        tbr_out[...] = branch
        x1 = xt_ref[...].astype(f32) + modulation(2) * branch
        tx1_out[...] = x1
        hat, _inv = norm_rows(x1)
        spread(ag_ref, (hat * (1.0 + modulation(4)) + modulation(3)).astype(bf16), to_mine)

    @pl.when(step == tiles - 1)
    def _():
        spread_end(ag_ref)
        tall_out[...] = ag_ref[...]

    @pl.when(step == tiles - 1)
    def _():
        t2_out[...] = t2_acc[...].astype(jnp.bfloat16)
        gate_out[...] = jnp.zeros_like(gate_out)

        def last(r, _):
            sl = pl.ds(pl.multiple_of(r * ROWS, ROWS), ROWS)
            m = m_acc[sl, :] + mm(t2_out[sl, :], b2_ref[...])
            y_out[sl, :] = (x1_out[sl, :] + mod_ref[5:6, :] * m).astype(jnp.bfloat16)
            gm = g_ref[sl, :].astype(jnp.float32) * m
            gate_out[...] += sum(gm[8 * i:8 * i + 8, :] for i in range(ROWS // 8))
            return 0

        lax.fori_loop(0, rows // ROWS, last, 0)


def both_back_kernel(tiles, n_z, turns, g_ref, x1_ref, a_ref, h2_ref, o_ref, mod_ref, u_ref, w2_ref, a2_ref, b2_ref, w1_ref, a1_ref, b1_ref,
                     wo_ref, ao_ref, bo_ref, to_ref, t1_ref, t2_ref,
                     gt_ref, tx1_ref, tbr_ref, tmod_ref, own_ref, mask_ref, lmask_ref, tall_ref, att_ref, tdm_ref, two_ref, tw1_ref, tw2_ref,
                     tao_ref, tbo_ref, ta1_ref, tb1_ref, ta2_ref, tb2_ref,
                     dx1_out, do_out, sums_out, ga2_out, gb1_out, ga1_out, gb2_out, gao_out, gbo_out,
                     ty_out, tdx1_out, tdo_out, tsums_out, tgao_out, tgbo_out, tga1_out, tgb1_out, tga2_out, tgb2_out,
                     dm_ref, dt2_ref, dh_acc, dt1_acc, part_ref, mine_ref, out_buf, in_buf, tda_ref, tdo_buf, heads_buf,
                     do_send, do_recv, rs_send, rs_recv, ag_send, ag_recv, hd_send, hd_recv, hd_own):
    step = pl.program_id(0)
    f, z, core, base, column = column_peers(n_z)
    pad, width_t = gt_ref.shape
    rank = tao_ref.shape[0]
    share = tao_ref.shape[1]
    f32, bf16 = jnp.float32, jnp.bfloat16
    scatter, collect, spread, spread_end, gathered, own_lanes = text_tools(
        n_z, pad, width_t, f, z, lmask_ref, part_ref, mine_ref, out_buf, in_buf, rs_send, rs_recv, ag_send, ag_recv)
    home = [(base + z // 2, 2 * core + i) for i in range(2)]

    def is_here(i):
        return (z // 2 == core) & (2 * core + i == z)

    def do_push(s):
        return push(tdo_buf, tdo_out.at[z % 2], do_send.at[s], do_recv.at[z % 2], home[s])

    def collapse(place, values):
        for s in range(2):
            tsums_out[2 * place + s:2 * place + s + 1, :] = jnp.sum(
                jnp.where(own_ref[...] == (1.0 if s == 0 else -1.0), values, 0.0), axis=0, keepdims=True)

    @pl.when(step == 0)
    def _():
        meet(column)
        h2_all = gathered(tall_ref, 0, width_t)
        t1 = (mm_t(h2_all, ta1_ref[...]) * mask_ref[...]).astype(bf16)
        u = mm(h2_all, tw1_ref[...]) + mm(t1, tb1_ref[...])
        act, slope = gelu_parts(u)
        act = act.astype(bf16)
        dm_all = tdm_ref[...].reshape(n_z * pad, width_t)
        dt2 = (mm_t(dm_all, tb2_ref[...]) * mask_ref[...]).astype(bf16)
        du = ((mm(dm_all, tw2_ref[...]) + mm(dt2, ta2_ref[...])) * slope).astype(bf16)
        scatter(1, mm_t(du, tw1_ref[...]), mm_t(du, tb1_ref[...]))
        scatter(0, mm_t(act, tw2_ref[...]), mm_t(act, ta2_ref[...]))
        tga2_out[...] = t_mm(dt2, act)
        tgb1_out[...] = t_mm(t1, du)

    rows, width = g_ref.shape
    bf16 = jnp.bfloat16


    @pl.when(step == 0)
    def _():
        def start(r, _):
            sl = pl.ds(pl.multiple_of(r * ROWS, ROWS), ROWS)
            dm_ref[sl, :] = (mod_ref[5:6, :] * g_ref[sl, :].astype(jnp.float32)).astype(bf16)
            return 0

        lax.fori_loop(0, rows // ROWS, start, 0)
        dt2_ref[...] = mm_t(dm_ref[...], b2_ref[...]).astype(bf16)
        gb2_out[...] = t_mm(t2_ref[...], dm_ref[...])
        dh_acc[...] = jnp.zeros_like(dh_acc)
        dt1_acc[...] = jnp.zeros_like(dt1_acc)

    act, slope = gelu_parts(u_ref[...])
    df = mm(dm_ref[...], w2_ref[...]) + mm(dt2_ref[...], a2_ref[...])
    ga2_out[...] = t_mm(dt2_ref[...], act.astype(bf16))
    du = (df * slope).astype(bf16)
    gb1_out[...] = t_mm(t1_ref[...], du)
    dh_acc[...] += mm_t(du, w1_ref[...])
    dt1_acc[...] += mm_t(du, b1_ref[...])


    @pl.when(step == turns[0])
    def _():
        modulation = rows_of(tmod_ref, own_ref)
        dh, dt1_mine = collect(1)
        dh = dh + mm(dt1_mine, ta1_ref[...])
        hat, inverse = norm_rows(tx1_ref[...])
        dz = dh * (1.0 + modulation(4))
        dx1 = gt_ref[...].astype(f32) + inverse * (
            dz - jnp.mean(dz, axis=-1, keepdims=True) - hat * jnp.mean(dz * hat, axis=-1, keepdims=True))
        feed, t2_mine = collect(0)
        spread(tda_ref, (modulation(2) * dx1).astype(bf16), dt1_mine, t2_mine)
        tdx1_out[...] = dx1
        collapse(0, dx1 * tbr_ref[...])
        collapse(1, dh)
        collapse(2, dh * hat)
        feed = feed + mm(t2_mine, tb2_ref[...])
        ty_out[...] = (tx1_ref[...] + modulation(5) * feed).astype(bf16)
        collapse(3, gt_ref[...].astype(f32) * feed)

    @pl.when(step == turns[1])
    def _():
        spread_end(tda_ref)
        da_all = gathered(tda_ref, 0, width_t)
        dt1 = gathered(tda_ref, width_t, rank)
        t2 = gathered(tda_ref, width_t + rank, rank)
        dto = (mm_t(da_all, tbo_ref[...]) * mask_ref[...]).astype(bf16)
        tdo_buf[...] = (mm(da_all, two_ref[...]) + mm(dto, tao_ref[...])).astype(bf16)
        for s in range(2):
            @pl.when(is_here(s))
            def _():
                copy = pltpu.make_async_copy(tdo_buf, tdo_out.at[z % 2], do_recv.at[z % 2])
                copy.start()
                copy.wait()

            @pl.when(jnp.logical_not(is_here(s)))
            def _():
                do_push(s).start()
        tgao_out[...] = t_mm(dto, att_ref[...])
        tgbo_out[...] = t_mm(gathered(tall_ref, width_t, rank), own_lanes(tda_ref, share))
        tgb2_out[...] = t_mm(t2, own_lanes(tdm_ref, share))
        tga1_out[...] = t_mm(dt1, own_lanes(tall_ref, share))

    @pl.when(step == tiles - 1)
    def _():
        dt1 = dt1_acc[...].astype(bf16)
        dt2_ref[...] = dt1
        ga1_out[...] = t_mm(dt1, h2_ref[...])
        sums_out[...] = jnp.zeros_like(sums_out)

        def last(r, _):
            sl = pl.ds(pl.multiple_of(r * ROWS, ROWS), ROWS)
            dh = dh_acc[sl, :] + mm(dt2_ref[sl, :], a1_ref[...])
            xh, inverse = norm_rows(x1_ref[sl, :])
            dz = dh * (1.0 + mod_ref[4:5, :])
            dx1 = g_ref[sl, :].astype(jnp.float32) + inverse * (
                dz - jnp.mean(dz, axis=-1, keepdims=True) - xh * jnp.mean(dz * xh, axis=-1, keepdims=True))
            dx1_out[sl, :] = dx1
            dm_ref[sl, :] = (mod_ref[2:3, :] * dx1).astype(bf16)
            fold = lambda v: sum(v[8 * i:8 * i + 8, :] for i in range(ROWS // 8))
            sums_out[0:8, :] += fold(dx1 * a_ref[sl, :].astype(jnp.float32))
            sums_out[8:16, :] += fold(dh)
            sums_out[16:24, :] += fold(dh * xh)
            return 0

        lax.fori_loop(0, rows // ROWS, last, 0)
        dto = mm_t(dm_ref[...], bo_ref[...]).astype(bf16)
        dt2_ref[...] = dto
        gao_out[...] = t_mm(dto, o_ref[...])
        gbo_out[...] = t_mm(to_ref[...], dm_ref[...])

        per_half = width // 512

        def cols(n, _):
            sl = pl.ds(pl.multiple_of(n * 256, 256), 256)
            into = pl.ds(pl.multiple_of(n % per_half * 256, 256), 256)
            heads_buf[n // per_half, :, into] = (mm(dm_ref[...], wo_ref[:, sl]) + mm(dt2_ref[...], ao_ref[:, sl])).astype(bf16)
            return 0

        lax.fori_loop(0, width // 256, cols, 0)
        partner = base + 1 - core
        swap = push(heads_buf.at[1 - core], do_out.at[core], hd_send, hd_recv, (partner, z))
        swap.start()
        keep = pltpu.make_async_copy(heads_buf.at[core], do_out.at[core], hd_own)
        keep.start()
        keep.wait()
        swap.wait_send()
        push(heads_buf.at[0], do_out.at[1 - core], hd_send, hd_recv, (partner, z)).wait_recv()

    @pl.when(step == tiles - 1)
    def _():
        for i in range(2):
            @pl.when(jnp.logical_not(is_here(i)))
            def _():
                push(tdo_out.at[i], tdo_out.at[i], do_send.at[i], do_recv.at[i], home[i]).wait_recv()
                do_push(i).wait_send()


def both_fwd(o, x, g, mod, wo, pair_o, pair_1, w1, pair_2, w2, ot, xt, tmod, owner, own, lmask, two, tpair_o, n_z, cid, tn=512, turns=(2, 7)):
    rows, width = o.shape
    hidden = w1.shape[1]
    tiles = hidden // tn
    rank = pair_o[0].shape[0]
    once = lambda shape: pl.BlockSpec(shape, lambda n: (0,) * len(shape), pipeline_mode=pl.Buffered(1))
    whole = once
    tile = lambda height: pl.BlockSpec((height, tn), lambda n: (0, n))
    f32, bf16 = jnp.float32, jnp.bfloat16
    shape, vmem, dma = jax.ShapeDtypeStruct, pltpu.VMEM, pltpu.SemaphoreType.DMA
    act = (rows, width)
    pad = xt.shape[0]
    total, share = n_z * pad, two.shape[1]
    thick = tpair_o[0].shape[0]
    wide = width + thick
    texts = (xt, tmod, owner, own, lmask, two, *tpair_o)
    return pl.pallas_call(
        functools.partial(both_fwd_kernel, tiles, n_z, turns),
        grid=(tiles,),
        in_specs=[once(act), once(act), once(act), once(mod.shape), once((width, width)), once((rank, width)), once((rank, width)),
                  once((rank, width)), tile(rank), tile(width), tile(rank), tile(width), once((rank, width)),
                  pl.BlockSpec(memory_space=pl.ANY)] + [once(v.shape) for v in texts],
        out_specs=[whole(act), whole(act), whole(act), tile(rows), whole(act), whole((rows, rank)), whole((rows, rank)),
                   whole((rows, rank)), whole((8, width)), whole((n_z, pad, wide)), whole((total, share)), whole((pad, width)),
                   whole((pad, width))],
        out_shape=[shape(act, bf16), shape(act, f32), shape(act, bf16), shape((rows, hidden), f32), shape(act, bf16)]
        + [shape((rows, rank), bf16)] * 3
        + [shape((8, width), f32), shape((n_z, pad, wide), bf16), shape((total, share), bf16), shape((pad, width), f32),
           shape((pad, width), f32)],
        scratch_shapes=[vmem(act, f32), vmem((rows, rank), f32), vmem((2, total, share), bf16), vmem((n_z, pad, wide), f32), vmem((1, pad, wide), f32),
                        vmem((1, n_z, pad, wide), bf16), vmem((1, n_z, pad, wide), bf16), vmem((n_z, pad, wide), bf16),
                        dma((2,)), dma((2,)), dma((1, n_z)), dma((1, n_z)), dma((n_z,)), dma((n_z,))],
        compiler_params=pltpu.CompilerParams(collective_id=cid, has_side_effects=True, vmem_limit_bytes=60 * 1024 * 1024),
        name="block_forward",
    )(o, x, g, mod, wo, *pair_o, pair_1[0], pair_1[1], w1, pair_2[0], w2, pair_2[1], ot, *texts)


def both_back(g, x1, a, h2, o, mod, u, w2, pair_2, w1, pair_1, wo, pair_o, mids,
              gt, tx1, tbr, tmod, own, mask, lmask, tall, att, tdm, two, tw1, tw2, tpair_o, tpair_1, tpair_2, n_z, cid, tn=512, turns=(8, 11)):
    rows, width = o.shape
    hidden = w1.shape[1]
    tiles = hidden // tn
    rank = pair_o[0].shape[0]
    once = lambda shape: pl.BlockSpec(shape, lambda n: (0,) * len(shape), pipeline_mode=pl.Buffered(1))
    whole = once
    tile = lambda height: pl.BlockSpec((height, tn), lambda n: (0, n))
    f32, bf16 = jnp.float32, jnp.bfloat16
    shape, vmem, dma = jax.ShapeDtypeStruct, pltpu.VMEM, pltpu.SemaphoreType.DMA
    act = (rows, width)
    side = (rank, width)
    thin = (rows, rank)
    pad = gt.shape[0]
    total, share = n_z * pad, two.shape[1]
    thick = tpair_o[0].shape[0]
    t_hidden = tw1.shape[1]
    wide = width + thick
    texts = (gt, tx1, tbr, tmod, own, mask, lmask, tall, att, tdm, two, tw1, tw2, *tpair_o, *tpair_1, *tpair_2)
    return pl.pallas_call(
        functools.partial(both_back_kernel, tiles, n_z, turns),
        grid=(tiles,),
        in_specs=[once(act)] * 5 + [once(mod.shape), tile(rows), tile(width), tile(rank), once(side), tile(width), once(side), tile(rank),
                  once((width, width)), once(side), once(side)] + [once(thin)] * 3 + [once(v.shape) for v in texts],
        out_specs=[whole(act), pl.BlockSpec(memory_space=pl.ANY), whole((24, width)), tile(rank), tile(rank)] + [whole(side)] * 4
        + [whole((pad, width)), whole((pad, width)), pl.BlockSpec(memory_space=pl.ANY), whole((8, width)), whole((thick, share)),
           whole((thick, share)), whole((thick, share)), whole((thick, t_hidden)), whole((thick, t_hidden)), whole((thick, share))],
        out_shape=[shape(act, f32), shape((2, rows, width // 2), bf16), shape((24, width), f32)] + [shape((rank, hidden), f32)] * 2 + [shape(side, f32)] * 4
        + [shape((pad, width), bf16), shape((pad, width), f32), shape((2, total, share), bf16), shape((8, width), f32),
           shape((thick, share), f32), shape((thick, share), f32), shape((thick, share), f32), shape((thick, t_hidden), f32),
           shape((thick, t_hidden), f32), shape((thick, share), f32)],
        scratch_shapes=[vmem(act, bf16), vmem(thin, bf16), vmem(act, f32), vmem(thin, f32),
                        vmem((n_z, pad, wide), f32), vmem((2, pad, wide), f32), vmem((2, n_z, pad, wide), bf16), vmem((2, n_z, pad, wide), bf16),
                        vmem((n_z, pad, wide + thick), bf16), vmem((total, share), bf16), vmem((2, rows, width // 2), bf16),
                        dma((2,)), dma((2,)), dma((2, n_z)), dma((2, n_z)), dma((n_z,)), dma((n_z,)), dma, dma, dma],
        compiler_params=pltpu.CompilerParams(collective_id=cid, has_side_effects=True, vmem_limit_bytes=60 * 1024 * 1024),
        name="block_backward",
    )(g, x1, a, h2, o, mod, u, w2, pair_2[0], pair_2[1], w1, pair_1[0], pair_1[1], wo, *pair_o, *mids, *texts)


def flip_bits(chip, mask, nbits):
    other = 0
    for bit in range(nbits):
        have = (chip // (1 << bit)) % 2
        other = other + (1 - have if (mask >> bit) & 1 else have) * (1 << bit)
    return other


def tail_kernel(n_f, n_z, fans, cols, *refs):
    it = iter(refs)
    take = lambda count: [next(it) for _ in range(count)]
    dq_in, tdq_in, wq_ref = take(3)
    (x_ref, dx1_ref, h_ref, imod_ref, mid_ref, qa_ref, qb_ref, isum_ref, igate_ref, tx_ref, tdx1_ref, th_ref, tmodr_ref, owner_ref,
     own_ref, lmask_ref, tmid_ref, twq_ref, tqa_ref, tqb_ref, tsum_ref) = take(21)
    early_ref, = take(1)
    txt_a, txt_b = take(3), take(3)
    hot4_ref, hot2_ref, wmod_ref, bmod_ref, tmod_ref, cond_ref, smask_ref = take(7)
    grad_out, tgrad_out, cond_out, rank_out, shard_out = take(5)
    (dq_ref, wtile, dh_ref, dt_ref, grad_ref, gaq_ref, gbq_ref, tgot, part_ref, mine_ref, out_buf, in_buf, dt_ag, tgb_ref, dmod_ref,
     isums) = take(16)
    zmsg, zgot, dense, snd1, rcv1, snd2, rcv2, dgot, own_dm, all_dm, cpart, cgot, zsum, zall, dts = take(15)
    (g_send, g_recv, z_send, z_recv, c_send, c_recv, s_send, s_recv, d_send, d_recv, f_send, f_recv, p_send, p_recv,
     q_send, q_recv, t_send, t_recv, dq_send, dq_recv, dq_own, w_sem, h_send, h_recv, rs_send, rs_recv, ag_send, ag_recv) = take(28)
    f32, bf16 = jnp.float32, jnp.bfloat16
    f, z, core, base, column = column_peers(n_z)
    chip = f // 2
    chips = n_f // 2
    nbits = bits_of(chips)
    partner = base + 1 - core
    around = [((f + j) % n_f, z) for j in range(1, n_f)]
    others = [(flip_bits(chip, mask, nbits) * 2 + side, z) for mask in range(1, chips) for side in range(2)]
    meet(column + others)
    ring = ZRing(f, z, n_z)
    blk = shard_out.shape[0]
    hidden_rank = hot2_ref.shape[0]

    home = [(base + z // 2, 2 * core + i) for i in range(2)]

    def is_here(i):
        return (z // 2 == core) & (2 * core + i == z)

    swap = push(dq_in.at[1 - core], dq_ref.at[core], dq_send, dq_recv, (partner, z))
    swap.start()
    keep = pltpu.make_async_copy(dq_in.at[core], dq_ref.at[core], dq_own)
    keep.start()

    def t_push(i):
        return push(tdq_in.at[i], tgot.at[z % 2], h_send.at[i], h_recv.at[z % 2], home[i])

    for i in range(2):
        @pl.when(is_here(i))
        def _():
            copy = pltpu.make_async_copy(tdq_in.at[i], tgot.at[z % 2], h_recv.at[z % 2])
            copy.start()
            copy.wait()

        @pl.when(jnp.logical_not(is_here(i)))
        def _():
            t_push(i).start()

    pad, width = tx_ref.shape
    thick = tqa_ref.shape[0]
    scatter, collect, spread, spread_end, gathered, own_lanes = text_tools(
        n_z, pad, width, f, z, lmask_ref, part_ref, mine_ref, out_buf, in_buf, rs_send, rs_recv, ag_send, ag_recv)
    tn = wtile.shape[3]
    per_half = dq_ref.shape[2] // tn

    def tile_of(n):
        side = core if n < per_half else 1 - core
        return side, side * per_half + n % per_half

    def tile_load(n):
        at = pl.ds(pl.multiple_of(tile_of(n)[1] * tn, 128), tn)
        return pltpu.make_async_copy(wq_ref.at[:, :, at], wtile.at[n % 2], w_sem.at[n % 2])

    def tile_back(n):
        if n + 1 < 2 * per_half:
            tile_load(n + 1).start()
        tile_load(n).wait()
        side, number = tile_of(n)
        at = pl.ds(pl.multiple_of(number * tn, 128), tn)
        part = dq_ref[side, :, n % per_half * tn:(n % per_half + 1) * tn]
        main = mm_t(part, wtile[n % 2].reshape(width, tn))
        thin = mm_t(part, qb_ref[:, at])
        if n == 0:
            dh_ref[...] = main
            dt_ref[...] = thin
        else:
            dh_ref[...] += main
            dt_ref[...] += thin
        gbq_ref[:, at] = t_mm(mid_ref[...], part)

    tile_load(0).start()
    keep.wait()
    for n in range(per_half):
        tile_back(n)

    for i in range(2):
        @pl.when(jnp.logical_not(is_here(i)))
        def _():
            push(tgot.at[i], tgot.at[i], h_send.at[i], h_recv.at[i], home[i]).wait_recv()
            t_push(i).wait_send()
    owner = owner_ref[...]
    tdq = jnp.where(owner > 0, tgot[0].astype(f32), jnp.where(owner < 0, tgot[1].astype(f32), 0.0)).astype(bf16)
    scatter(0, mm_t(tdq, twq_ref[...]), mm_t(tdq, tqb_ref[...]))
    tgb_ref[...] = t_mm(tmid_ref[...], tdq)

    push(dq_in.at[1 - core], dq_ref.at[1 - core], dq_send, dq_recv, (partner, z)).wait_recv()
    for n in range(per_half, 2 * per_half):
        tile_back(n)
    dt_low = dt_ref[...].astype(bf16)
    gaq_ref[...] = t_mm(dt_low, h_ref[...])

    spans = {}
    offset = 0
    for part, count, name in ((gaq_ref, fans[1] // n_z, (0, 1)), (gbq_ref, cols[1] // n_z, (1, 1))):
        for t in range(n_z):
            zmsg[t, :, offset:offset + count] = part[:, t * count:(t + 1) * count].astype(bf16)
        spans[name] = (offset, count)
        offset += count
    ring.start(lambda to: zmsg.at[to], zgot, z_send, z_recv)
    zgot[z] = zmsg[z]
    offset = 0
    for side, sizes in ((0, fans), (1, cols)):
        for index in range(2, 5):
            spans[side, index] = (offset, sizes[index] // n_z)
            offset += sizes[index] // n_z

    isums[...] = jnp.zeros_like(isums)
    quarter = grad_ref.shape[1]
    dh_ref[...] += mm(dt_low, qa_ref[...])
    for i in range(2):
        def last(r, _):
            sl = pl.ds(pl.multiple_of(i * quarter + r * ROWS, ROWS), ROWS)
            dh = dh_ref[sl, :]
            xh, inverse = norm_rows(x_ref[sl, :].astype(f32))
            dz = dh * (1.0 + imod_ref[1:2, :])
            dx = dx1_ref[sl, :] + inverse * (
                dz - jnp.mean(dz, axis=-1, keepdims=True) - xh * jnp.mean(dz * xh, axis=-1, keepdims=True))
            grad_ref[i, pl.ds(pl.multiple_of(r * ROWS, ROWS), ROWS), :] = dx.astype(bf16)
            fold = lambda v: sum(v[8 * j:8 * j + 8, :] for j in range(ROWS // 8))
            isums[0:8, :] += fold(dh)
            isums[8:16, :] += fold(dh * xh)
            return 0

        lax.fori_loop(0, quarter // ROWS, last, 0)

    pick = rows_of(tmodr_ref, own_ref)
    tdh, tdt = collect(0)
    spread(dt_ag, tdt)
    tdh = tdh + mm(tdt, tqa_ref[...])
    hat, inverse = norm_rows(tx_ref[...].astype(f32))
    dz = tdh * (1.0 + pick(1))
    tgrad_out[...] = tdx1_ref[...] + inverse * (
        dz - jnp.mean(dz, axis=-1, keepdims=True) - hat * jnp.mean(dz * hat, axis=-1, keepdims=True))

    def total_of(v):
        return jnp.sum(v, axis=0, keepdims=True)

    rows_img = [total_of(isums[0:8, :]), total_of(isums[8:16, :])]
    rows_img += [total_of(isum_ref[8 * p:8 * p + 8, :]) for p in range(3)] + [total_of(igate_ref[...])]
    rows_txt = []
    for s in range(2):
        chosen = own_ref[...] == (1.0 if s == 0 else -1.0)
        rows_txt.append([total_of(jnp.where(chosen, tdh, 0.0)), total_of(jnp.where(chosen, tdh * hat, 0.0))]
                        + [tsum_ref[2 * p + s:2 * p + s + 1, :] for p in range(4)])
    dmod_ref[...] = jnp.zeros_like(dmod_ref)
    chunk = dmod_ref.shape[-1]
    per_row = width // chunk
    per_block = 6 * per_row // n_z
    for r, parts in enumerate([rows_img] + rows_txt):
        for q in range(6 * per_row):
            dmod_ref[q // per_block, r, q % per_block:q % per_block + 1, :] = (
                parts[q // per_row][:, q % per_row * chunk:(q % per_row + 1) * chunk])

    def dmod_copy(index, peer):
        return push(dmod_ref.at[peer[1]], dgot.at[core * n_z + z], d_send.at[index], d_recv.at[core * n_z + z], peer)

    for index, peer in enumerate(column):
        dmod_copy(index, peer).start()
    dgot[core * n_z + z] = dmod_ref[z]

    hot2, hot4 = hot2_ref[...], hot4_ref[...]
    starts = []
    offset = 0
    for stream in range(2):
        for index in range(5):
            starts.append((stream, index, offset, offset + fans[index] // n_z))
            offset += fans[index] // n_z + cols[index] // n_z

    def put_a(at, part, hot):
        dense[at:at + part.shape[1], :] = dots(part, hot, 0, 0)

    def put_b(at, part, hot):
        full = dots(hot, part, 0, 0)
        blocks = part.shape[1] // 128
        for j in range(blocks):
            dense[pl.ds(at + j, 128, stride=blocks), :] = full[:, j * 128:(j + 1) * 128]

    def put_image(index, ref):
        for side, put in ((0, put_a), (1, put_b)):
            begin, count = spans[side, index]
            put(starts[index][2 + side], ref[:, :, begin:begin + count].reshape(hot4.shape[0], count), hot4)

    for index in range(2, 5):
        put_image(index, early_ref)
        put_a(starts[5 + index][2], txt_a[index - 2][:hidden_rank, :].astype(bf16), hot2)
        put_b(starts[5 + index][3], txt_b[index - 2][:hidden_rank, :].astype(bf16), hot2)

    for index, peer in enumerate(column):
        place = peer[0] % 2 * n_z + peer[1]
        push(dgot.at[place], dgot.at[place], d_send.at[index], d_recv.at[place], peer).wait_recv()
    rows = []
    for slot in range(2):
        rows.append(dgot[2 * core + slot, 0] + dgot[n_z + 2 * core + slot, 0])
    for slot in range(2):
        total = dgot[core * n_z, 1 + slot]
        for t in range(1, n_z):
            total = total + dgot[core * n_z + t, 1 + slot]
        rows.append(total)
    own_dm[...] = jnp.zeros_like(own_dm)
    for r, total in enumerate(rows):
        for j in range(own_dm.shape[1] // chunk):
            own_dm[r:r + 1, j * chunk:(j + 1) * chunk] = total[j:j + 1, :].astype(bf16).astype(f32)
    for j in range(1, n_f):
        push(own_dm, all_dm.at[f], f_send.at[j], f_recv.at[f], around[j - 1]).start()
    all_dm[f] = own_dm[...]
    dm_low = own_dm[...].astype(bf16)
    tmod = [tmod_ref[s].astype(bf16) for s in range(2)]
    gb_mod = [t_mm(tmod[s], dm_low) for s in range(2)]
    rank_img = mm_t(dm_low, bmod_ref[0])
    rank_txt = mm_t(dm_low, bmod_ref[1])
    row = lax.broadcasted_iota(jnp.int32, rank_img.shape, 0)
    rank_part = jnp.where(row < 2, rank_img, rank_txt)

    spread_end(dt_ag)
    tga = t_mm(gathered(dt_ag, 0, thick), own_lanes(th_ref, cols[2] // n_z))
    for stream, index, at_a, at_b in starts:
        if index == 0:
            dense[at_a:at_b, :] = jnp.zeros((at_b - at_a, 128), f32)
            put_b(at_b, gb_mod[stream].astype(bf16), hot2)
        elif index == 1 and stream == 1:
            put_a(at_a, tga[:hidden_rank].astype(bf16), hot2)
            put_b(at_b, tgb_ref[:hidden_rank, :].astype(bf16), hot2)
    ring.wait(zgot, z_send, z_recv)
    put_image(1, zgot)

    for i in range(2):
        @pl.when(is_here(i))
        def _():
            pltpu.make_async_copy(grad_ref.at[i], grad_out.at[z % 2], g_recv.at[z % 2]).start()

        @pl.when(jnp.logical_not(is_here(i)))
        def _():
            push(grad_ref.at[i], grad_out.at[z % 2], g_send.at[i], g_recv.at[z % 2], home[i]).start()

    def block(number):
        return pl.ds(pl.multiple_of(number * blk, 16), blk)

    for p in range(chips):
        snd1[p] = dense[block(2 * p + 1 - core), :].astype(bf16)
        push(snd1.at[p], rcv1.at[p], c_send.at[p], c_recv.at[p], (partner, z)).start()

    for j in range(1, n_f):
        came = (f - j + n_f) % n_f
        push(own_dm, all_dm.at[came], f_send.at[j], f_recv.at[came], (came, z)).wait_recv()
    everyone = all_dm[...].reshape(n_f * 8, own_dm.shape[1]).astype(bf16)
    part = mm_t(everyone, wmod_ref[0]) + pltpu.roll(mm_t(everyone, wmod_ref[1]), n_f * 8 - 2, 0)
    k_local = part.shape[1]
    cpart[...] = jnp.zeros_like(cpart)
    cpart[:, :, :k_local] = part.reshape(n_f, 8, k_local)
    for j in range(1, n_f):
        to = (f + j) % n_f
        push(cpart.at[to], cgot.at[f], p_send.at[j], p_recv.at[f], (to, z)).start()
    cgot[f] = cpart[f]

    for p in range(chips):
        push(snd1.at[p], rcv1.at[p], c_send.at[p], c_recv.at[p], (partner, z)).wait_recv()

    def mine_of(p):
        return block(2 * p + core)

    for p in range(chips):
        dense[mine_of(p), :] += rcv1[p].astype(f32)

    half = blk // 2
    orders = [list(range(nbits)), list(range(nbits))[::-1]]

    def masks_at(side, turn):
        left = orders[side][turn:]
        return [sum(1 << b for i, b in enumerate(left) if (m >> i) & 1) for m in range(1 << len(left))]

    def rs_copy(side, turn, index):
        slot = turn * 2 + index
        peer = flip_bits(chip, 1 << orders[side][turn], nbits) * 2 + core
        return push(snd2.at[side, slot], rcv2.at[side, slot], s_send.at[side, slot], s_recv.at[side, slot], (peer, z))

    def half_of(number, side):
        return pl.ds(pl.multiple_of((2 * number + core) * blk + side * half, 16), half)

    def rs_start(turn):
        for side in range(2):
            bit = 1 << orders[side][turn]
            for index, mask in enumerate(masks_at(side, turn + 1)):
                number = flip_bits(chip, bit | mask, nbits)
                snd2[side, turn * 2 + index] = dense[half_of(number, side), :].astype(bf16)
                rs_copy(side, turn, index).start()

    def rs_end(turn):
        for side in range(2):
            for index, mask in enumerate(masks_at(side, turn + 1)):
                number = flip_bits(chip, mask, nbits)
                rs_copy(side, turn, index).wait_recv()
                dense[half_of(number, side), :] += rcv2[side, turn * 2 + index].astype(f32)

    rs_start(0)

    for j in range(1, n_f):
        came = (f - j + n_f) % n_f
        push(cpart.at[came], cgot.at[came], p_send.at[j], p_recv.at[came], (came, z)).wait_recv()
    zsum[:n_f] = cgot[...]
    zsum[n_f] = jnp.zeros(zsum.shape[1:], f32)
    zsum[n_f, :, :hidden_rank] = rank_part
    zall[z] = zsum[...]
    ring.start(lambda to: zsum, zall, q_send, q_recv)
    ring.wait(zall, q_send, q_recv)
    total = zall[0]
    for t in range(1, n_z):
        total = total + zall[t]
    cond_out[...] = total[:n_f]
    dt = (total[n_f][:, :hidden_rank] * smask_ref[...]).astype(bf16)
    rank_out[...] = dt.astype(f32)
    wide = mm(dt, hot2)
    dts[f] = wide
    for j in range(1, n_f):
        push(dts.at[f], dts.at[f], t_send.at[j], t_recv.at[f], around[j - 1]).start()

    rs_end(0)
    if nbits > 1:
        rs_start(1)
    for j in range(1, n_f):
        came = (f - j + n_f) % n_f
        push(dts.at[came], dts.at[came], t_send.at[j], t_recv.at[came], (came, z)).wait_recv()
    all_dt = dts[...].reshape(n_f * 8, 128)
    row = lax.broadcasted_iota(jnp.int32, all_dt.shape, 0) % 8
    act = cond_ref[...].reshape(n_f * 8, cond_ref.shape[-1]).astype(bf16)
    mod_a = [
        dots(act, jnp.where(row < 2, all_dt, 0.0).astype(bf16), 0, 0),
        dots(act, pltpu.roll(jnp.where((row >= 2) & (row < 4), all_dt, 0.0), n_f * 8 - 2, 0).astype(bf16), 0, 0),
    ]
    if nbits > 1:
        rs_end(1)
    shard_out[...] = dense[block(f), :]
    for stream in range(2):
        first = starts[5 * stream][2]
        own = jnp.where(f == first // blk, 1.0, 0.0)
        count = mod_a[stream].shape[0]
        shard_out[:count, :] += own * mod_a[stream]

    swap.wait_send()
    ring.drain(lambda to: zmsg.at[to], zgot, z_send, z_recv)
    ring.drain(lambda to: zsum, zall, q_send, q_recv)
    for index, peer in enumerate(column):
        dmod_copy(index, peer).wait_send()
    for j in range(1, n_f):
        to = (f + j) % n_f
        push(own_dm, all_dm.at[f], f_send.at[j], f_recv.at[f], (to, z)).wait_send()
        push(cpart.at[to], cgot.at[f], p_send.at[j], p_recv.at[f], (to, z)).wait_send()
        push(dts.at[f], dts.at[f], t_send.at[j], t_recv.at[f], (to, z)).wait_send()
    for p in range(chips):
        push(snd1.at[p], rcv1.at[p], c_send.at[p], c_recv.at[p], (partner, z)).wait_send()
    for turn in range(nbits):
        for side in range(2):
            for index in range(len(masks_at(side, turn + 1))):
                rs_copy(side, turn, index).wait_send()
    for i in range(2):
        @pl.when(is_here(i))
        def _():
            pltpu.make_async_copy(grad_ref.at[i], grad_out.at[z % 2], g_recv.at[z % 2]).wait()

        @pl.when(jnp.logical_not(is_here(i)))
        def _():
            push(grad_out.at[i], grad_out.at[i], g_send.at[i], g_recv.at[i], home[i]).wait_recv()
            push(grad_ref.at[i], grad_out.at[z % 2], g_send.at[i], g_recv.at[z % 2], home[i]).wait_send()


def tail(dq, tdq, wq, smalls, early, txt_a, txt_b, hot4, hot2, wmod, bmod, tmod, cond, smask, n_f, n_z, fans, cols, cid, tn=768):
    f32, bf16 = jnp.float32, jnp.bfloat16
    vmem, dma = pltpu.VMEM, pltpu.SemaphoreType.DMA
    shape = jax.ShapeDtypeStruct
    args = (dq, tdq, wq, *smalls, early, *txt_a, *txt_b, hot4, hot2, wmod, bmod, tmod, cond, smask)
    lanes = (fans[1] + cols[1]) // n_z
    rows = 2 * (sum(fans) + sum(cols)) // n_z
    blk = rows // n_f
    chips = n_f // 2
    cut = cols[0] // n_z
    rank = hot2.shape[0]
    _, img_rows, half = dq.shape
    _, k_local, _ = wq.shape
    width = cols[2]
    tx = smalls[9]
    thick = smalls[18].shape[0]
    pad = tx.shape[0]
    wide = width + thick
    inside, outside = pl.BlockSpec(memory_space=vmem), pl.BlockSpec(memory_space=pl.ANY)
    return pl.pallas_call(
        functools.partial(tail_kernel, n_f, n_z, tuple(fans), tuple(cols)),
        out_shape=[shape((2, img_rows // 2, width), bf16), shape((pad, width), f32), shape((n_f, 8, 256), f32), shape((8, rank), f32),
                   shape((blk, 128), f32)],
        in_specs=[outside] * 3 + [inside] * (len(args) - 3),
        out_specs=[outside] + [inside] * 4,
        scratch_shapes=[
            vmem((2, img_rows, half), bf16), vmem((2, n_f, k_local, tn), bf16), vmem((img_rows, width), f32), vmem((img_rows, RANK), f32),
            vmem((2, img_rows // 2, width), bf16), vmem((RANK, fans[1]), f32), vmem((RANK, cols[1]), f32), vmem(tdq.shape, bf16),
            vmem((n_z, pad, wide), f32), vmem((1, pad, wide), f32), vmem((1, n_z, pad, wide), bf16), vmem((1, n_z, pad, wide), bf16),
            vmem((n_z, pad, thick), bf16), vmem((thick, cols[1] // n_z), f32), vmem((n_z, 3, 8, width // n_z), f32), vmem((16, width), f32),
            vmem((n_z, RANK, lanes), bf16), vmem((n_z, RANK, lanes), bf16), vmem((rows, 128), f32),
            vmem((chips, blk, 128), bf16), vmem((chips, blk, 128), bf16),
            vmem((2, 3, blk // 2, 128), bf16), vmem((2, 3, blk // 2, 128), bf16),
            vmem((2 * n_z, 3, 8, width // n_z), f32), vmem((8, cut), f32), vmem((n_f, 8, cut), f32),
            vmem((n_f, 8, 256), f32), vmem((n_f, 8, 256), f32), vmem((n_f + 1, 8, 256), f32),
            vmem((n_z, n_f + 1, 8, 256), f32), vmem((n_f, 8, 128), f32),
            dma((2,)), dma((2,)), dma((n_z,)), dma((n_z,)), dma((chips,)), dma((chips,)), dma((2, 3)), dma((2, 3)),
            dma((2 * n_z,)), dma((2 * n_z,)), dma((n_f,)), dma((n_f,)), dma((n_f,)), dma((n_f,)), dma((n_z,)), dma((n_z,)),
            dma((n_f,)), dma((n_f,)), dma, dma, dma, dma((2,)), dma((2,)), dma((2,)), dma((1, n_z)), dma((1, n_z)), dma((n_z,)), dma((n_z,)),
        ],
        compiler_params=pltpu.CompilerParams(collective_id=cid, has_side_effects=True, vmem_limit_bytes=60 * 1024 * 1024),
        name="gradient_exchange",
    )(*args)

FULL = 4
PART = 4


def front_kernel(n_f, n_z, fans, cols, *refs):
    it = iter(refs)
    take = lambda count: [next(it) for _ in range(count)]
    ins = take(FULL + PART + 1)
    (x_ref, g_ref, picks_ref, hot2_ref, cblk_ref, clane_ref, c8_ref, smask_ref, wmod_ref, xt_ref, gt_ref, own_ref, tmask_ref, sign_ref) = take(14)
    outs = take(FULL + PART)
    x_out, g_out, imod_out, tmod_out = take(4)
    img_a, img_b, txt_a, txt_b = take(4), take(4), take(4), take(4)
    moda_out, modb_out, midm_out, cond_out, dm_out = take(5)
    ot_out, lse_out, bias_out, hot4_out = take(4)
    h_out, mid_out, heads_out, th_out, tmid_out, theads_out, att_out = take(7)
    (row_ref, fl_ref, img_msg, img_got, txt_msg, txt_got, cgot, mpart, mgot, own_mod, mod_got, wtile, wtxt, stage, tq_ref, sign_got, hot_got, img_buf, txt_buf, o_stage) = take(20)
    (z_send, z_recv, xy_send, xy_recv, core_send, core_recv, own_sem, x_send, x_recv, g_send, g_recv, c_send, c_recv, l_send,
     l_recv, m_send, m_recv, i_send, i_recv, t_send, t_recv, d_send, d_recv, a_send, a_recv, w_sem, tw_sem, h_send, h_recv,
     h_sem, q_send, q_recv, dm_send, dm_recv, s_send, s_recv, b_sem, o_send, o_recv, o_sem) = take(40)
    f32, bf16 = jnp.float32, jnp.bfloat16
    f, z, core, base, column = column_peers(n_z)
    chip = f // 2
    chips = n_f // 2
    nbits = bits_of(chips)
    partner = base + 1 - core
    others = [(flip_bits(chip, mask, nbits) * 2 + side, z) for mask in range(1, chips) for side in range(2)]
    meet(column + others)
    ring = ZRing(f, z, n_z)
    total = FULL + PART + 1
    adapters = total - 1
    blk = ins[adapters].shape[0]
    width = x_ref.shape[2]
    rank2 = hot2_ref.shape[0]

    def peer_of(mask):
        return flip_bits(chip, mask, nbits) * 2 + core

    def wide_of(m):
        return ins[m].shape[-1]

    def cuts(m):
        if m == adapters:
            return [(0, (0, blk // 2)), (1, (blk // 2, blk // 2))]
        return list(enumerate(halves(wide_of(m))))

    def place(m, who, zz, cut):
        off, w = cut
        if m == adapters:
            return row_ref.at[pl.ds(pl.multiple_of(who * blk + off, 16), w), :]
        if m < FULL:
            return outs[m].at[who, :, pl.ds(pl.multiple_of(zz * wide_of(m) + off, 128), w)]
        return outs[m].at[who, :, pl.ds(off, w)]

    def piece(m, cut):
        off, w = cut
        if m == adapters:
            return ins[m].at[pl.ds(off, w), :]
        return ins[m].at[:, pl.ds(off, w)]

    def whole_place(m, who, zz):
        return place(m, who, zz, (0, blk if m == adapters else wide_of(m)))

    def slot(m, zz):
        return zz if m < FULL else 0

    def order_of(half):
        order = list(range(nbits))
        return order if half == 0 else order[::-1]

    def xy_copy(m, zz, half, cut, mask, bit, own_piece=False):
        where = place(m, peer_of(mask), zz, cut)
        return push(piece(m, cut) if own_piece else where, where, xy_send.at[m, slot(m, zz), half, mask, bit],
                    xy_recv.at[m, slot(m, zz), half, mask | (1 << bit)], (peer_of(1 << bit), z))

    def xy_wait(m, zz, half, cut, mask):
        where = place(m, peer_of(mask), zz, cut)
        push(where, where, xy_send.at[m, slot(m, zz), half, 0, 0], xy_recv.at[m, slot(m, zz), half, mask], (partner, z)).wait_recv()

    def core_copy(m, zz, half, cut, mask, own_piece=False):
        where = place(m, peer_of(mask), zz, cut)
        return push(piece(m, cut) if own_piece else where, where, core_send.at[m, slot(m, zz), half, mask],
                    core_recv.at[m, slot(m, zz), half, mask], (partner, z))

    def core_wait(m, zz, half, cut, mask):
        where = place(m, peer_of(mask) - core + (1 - core), zz, cut)
        push(where, where, core_send.at[m, slot(m, zz), half, mask], core_recv.at[m, slot(m, zz), half, mask], (partner, z)).wait_recv()

    def own_copy(m):
        return pltpu.make_async_copy(ins[m], whole_place(m, f, z), own_sem.at[m])

    def z_copy(m, zz, up, own_piece=False):
        where = whole_place(m, f, zz)
        return push(ins[m] if own_piece else where, where, z_send.at[m, zz, up], z_recv.at[m, zz], (f, z + 1 if up else z - 1))

    def last_of(order, mask):
        return max([i for i, b in enumerate(order) if (mask >> b) & 1], default=-1)

    def masks_in_order(half):
        order = order_of(half)
        return sorted(range(1, 1 << nbits), key=lambda mask: [1 if (mask >> b) & 1 else 0 for b in reversed(order)])

    def launch(m, zz, own_piece=False):
        for half, cut in cuts(m):
            for bit in order_of(half):
                xy_copy(m, zz, half, cut, 0, bit, own_piece).start()
            core_copy(m, zz, half, cut, 0, own_piece).start()

    def launch_own(m):
        if m < FULL:
            @pl.when(z < n_z - 1)
            def _():
                z_copy(m, z, 1, True).start()

            @pl.when(z > 0)
            def _():
                z_copy(m, z, 0, True).start()
        launch(m, z, True)
        own_copy(m).start()

    def forward(m, zz):
        for half, cut in cuts(m):
            order = order_of(half)
            for mask in masks_in_order(half):
                if last_of(order, mask) < nbits - 1:
                    xy_wait(m, zz, half, cut, mask)
                    for b in order[last_of(order, mask) + 1:]:
                        xy_copy(m, zz, half, cut, mask, b).start()
                    core_copy(m, zz, half, cut, mask).start()

    def finish(m, zz):
        for half, cut in cuts(m):
            order = order_of(half)
            for mask in masks_in_order(half):
                if last_of(order, mask) == nbits - 1:
                    xy_wait(m, zz, half, cut, mask)
                    core_copy(m, zz, half, cut, mask).start()

    def settle(m, zz):
        for half, cut in cuts(m):
            for mask in range(1 << nbits):
                core_wait(m, zz, half, cut, mask)

    def drain(m, zz):
        for half, cut in cuts(m):
            order = order_of(half)
            for mask in range(1 << nbits):
                for b in order[last_of(order, mask) + 1:]:
                    xy_copy(m, zz, half, cut, mask, b).wait_send()
                core_copy(m, zz, half, cut, mask).wait_send()

    def at_distance(k, body):
        for sign in ((-1, 1) if k else (1,)):
            zz = z + sign * k

            @pl.when((zz >= 0) & (zz < n_z))
            def _():
                body(zz)

    def arrive(m, k):
        @pl.when(z - k >= 0)
        def _():
            zz = z - k
            z_copy(m, zz, 1).wait_recv()

            @pl.when(z < n_z - 1)
            def _():
                z_copy(m, zz, 1).start()

            launch(m, zz)

        @pl.when(z + k < n_z)
        def _():
            zz = z + k
            z_copy(m, zz, 0).wait_recv()

            @pl.when(z > 0)
            def _():
                z_copy(m, zz, 0).start()

            launch(m, zz)

    def every_z(m, body):
        if m < FULL:
            def step(zz, _):
                body(m, zz)
                return 0

            lax.fori_loop(0, n_z, step, 0)
        else:
            body(m, z)

    there = [(base + z // 2, 2 * core + s) for s in range(2)]

    def is_here(s):
        return (z // 2 == core) & (2 * core + s == z)

    def token_push(src, dst, send, recv, s):
        return push(src.at[s], dst.at[z % 2], send.at[s], recv.at[z % 2], there[s])

    def tokens_start(src, dst, send, recv):
        for s in range(2):
            @pl.when(is_here(s))
            def _():
                pltpu.make_async_copy(src.at[s], dst.at[z % 2], recv.at[z % 2]).start()

            @pl.when(jnp.logical_not(is_here(s)))
            def _():
                token_push(src, dst, send, recv, s).start()

    def tokens_wait(src, dst, send, recv):
        for i in range(2):
            @pl.when(is_here(i))
            def _():
                pltpu.make_async_copy(src.at[i], dst.at[z % 2], recv.at[z % 2]).wait()

            @pl.when(jnp.logical_not(is_here(i)))
            def _():
                push(dst.at[i], dst.at[i], send.at[i], recv.at[i], there[i]).wait_recv()

    def tokens_drain(src, dst, send, recv):
        for s in range(2):
            @pl.when(jnp.logical_not(is_here(s)))
            def _():
                token_push(src, dst, send, recv, s).wait_send()

    def around(src_of, dst, send, recv):
        return [push(src_of((f + j) % n_f), dst.at[f], send.at[j], recv.at[f], ((f + j) % n_f, z)) for j in range(1, n_f)]

    def around_wait(dst, send, recv):
        for j in range(1, n_f):
            came = (f - j + n_f) % n_f
            push(dst.at[came], dst.at[came], send.at[j], recv.at[came], (came, z)).wait_recv()

    cond_sends = around(lambda to: cblk_ref.at[to], cgot, c_send, c_recv)
    lane_sends = around(lambda to: clane_ref, cond_out, l_send, l_recv)
    mod_sends = around(lambda to: mpart.at[to], mgot, m_send, m_recv)

    sign_push = push(sign_ref, sign_got, s_send.at[0], s_recv.at[0], (partner, z))
    hot_push = push(hot2_ref, hot_got, s_send.at[1], s_recv.at[1], (partner, z))

    sign_push.start()
    hot_push.start()
    for copy in cond_sends + lane_sends:
        copy.start()
    launch_own(adapters)
    tokens_start(x_ref, x_out, x_send, x_recv)
    launch_own(FULL)
    launch_own(0)
    cgot[f] = cblk_ref[f]
    cond_out[f] = clane_ref[...]

    around_wait(cgot, c_send, c_recv)
    k_local = wmod_ref.shape[1]
    everyone = cgot[...].reshape(n_f * 8, cgot.shape[2])[:, :k_local].astype(bf16)
    mpart[...] = (mm(everyone, wmod_ref[0]) + pltpu.roll(mm(everyone, wmod_ref[1]), 2, 0)).reshape(mpart.shape)
    for copy in mod_sends:
        copy.start()
    mgot[f] = mpart[f]

    forward(adapters, z)
    forward(FULL, z)
    for m in (1, 2, 3):
        launch_own(m)
    for m in (FULL + 1, FULL + 2, FULL + 3):
        launch_own(m)
    for k in range(1, n_z):
        arrive(0, k)
    for m in (1, 2, 3):
        arrive(m, 1)
    for k in range(n_z):
        at_distance(k, lambda zz: forward(0, zz))

    finish(adapters, z)
    settle(adapters, z)
    own_copy(adapters).wait()
    hot2 = hot2_ref[...]
    starts = {}
    offset = 0
    for stream in range(2):
        for index in range(5):
            starts[stream, index] = (offset, offset + fans[index] // n_z)
            offset += fans[index] // n_z + cols[index] // n_z

    def pick_a(stream, index):
        at = starts[stream, index][0]
        return mm_t(hot2, row_ref[at:at + fans[index] // n_z, :]).astype(bf16)

    def pick_b(stream, index, s, put):
        at = starts[stream, index][1]
        count = cols[index] // n_z // NAD
        flat = row_ref[at:at + count, :].astype(f32) * picks_ref[s * NAD:s * NAD + 1, :]
        for k in range(1, NAD):
            begin = at + k * count
            flat = flat + row_ref[begin:begin + count, :].astype(f32) * picks_ref[s * NAD + k:s * NAD + k + 1, :]
        fl_ref[:count, :] = flat
        blocks = count // RANK
        for j in range(blocks):
            put(j * 128, fl_ref[pl.ds(j, RANK, stride=blocks), :].astype(bf16))

    spans_a, spans_b = [], []
    offset = 0
    for index in range(1, 5):
        count = fans[index] // n_z
        picked = pick_a(0, index)
        for s in range(2):
            img_msg[s, :, offset:offset + count] = picked[s * RANK:(s + 1) * RANK]
        spans_a.append((offset, count))
        offset += count
    for index in range(1, 5):
        count = cols[index] // n_z
        for s in range(2):
            def put(at, value, s=s, offset=offset):
                img_msg[s, :, offset + at:offset + at + 128] = value
            pick_b(0, index, s, put)
        spans_b.append((offset, count))
        offset += count

    def img_push(s, side):
        return push(img_msg.at[s], img_got.at[z], i_send.at[s, side], i_recv.at[z], (base + side, 2 * core + s))

    for s in range(2):
        for side in range(2):
            self_here = (side == core) & (2 * core + s == z)

            @pl.when(self_here)
            def _():
                img_got[z] = img_msg[s]

            @pl.when(jnp.logical_not(self_here))
            def _():
                img_push(s, side).start()

    share = width // n_z
    for place_at, (stream, index) in enumerate([(0, 0), (1, 0), (1, 1), (1, 3)]):
        txt_msg[:, place_at * share:(place_at + 1) * share] = pick_a(stream, index)
    for place_at, index in ((4, 2), (5, 4)):
        for s in range(2):
            def put(at, value, s=s, place_at=place_at):
                txt_msg[s * RANK:(s + 1) * RANK, place_at * share + at:place_at * share + at + 128] = value
            pick_b(1, index, s, put)
    txt_got[z] = txt_msg[...]
    ring.start(lambda to: txt_msg, txt_got, t_send, t_recv)
    for ref in txt_a + txt_b:
        ref[...] = jnp.zeros_like(ref)
    for index in (2, 4):
        txt_a[index - 1][:rank2, :] = pick_a(1, index)
    for ref, stream, index in ((txt_b[0], 1, 1), (txt_b[2], 1, 3), (modb_out.at[0], 0, 0), (modb_out.at[1], 1, 0)):
        for s in range(2):
            def put(at, value, ref=ref, s=s):
                ref[s * RANK:(s + 1) * RANK, at:at + 128] = value
            pick_b(stream, index, s, put)

    for k in (2, 3):
        for m in (1, 2, 3):
            arrive(m, k)
    for m in (1, 2, 3):
        forward(m, z)
    for m in (FULL + 1, FULL + 2, FULL + 3):
        forward(m, z)

    ring.wait(txt_got, t_send, t_recv)
    for t in range(n_z):
        lanes = slice(t * share, (t + 1) * share)
        got = lambda number: txt_got[t, :, number * share:(number + 1) * share]
        moda_out[0, :, lanes] = got(0)
        moda_out[1, :, lanes] = got(1)
        txt_a[0][:rank2, lanes] = got(2)
        txt_a[2][:rank2, lanes] = got(3)
        txt_b[1][:rank2, lanes] = got(4)
        txt_b[3][:rank2, lanes] = got(5)
    around_wait(mgot, m_send, m_recv)
    mod_sum = mgot[0]
    for j in range(1, n_f):
        mod_sum = mod_sum + mgot[j]
    c8 = c8_ref[...].astype(bf16)
    thin = mm_t(c8, moda_out[0])
    row = lax.broadcasted_iota(jnp.int32, thin.shape, 0)
    middle = (jnp.where(row < 2, thin, mm_t(c8, moda_out[1])) * smask_ref[...]).astype(bf16)
    low = jnp.where(row < 2, middle.astype(f32), 0.0)
    high = jnp.where((row >= 2) & (row < 4), middle.astype(f32), 0.0)
    midm_out[0] = low
    midm_out[1] = high
    own_mod[...] = mod_sum + mm(low.astype(bf16), modb_out[0]) + mm(high.astype(bf16), modb_out[1])

    def mod_push(index, peer):
        return push(own_mod, mod_got.at[core * n_z + z], d_send.at[index], d_recv.at[core * n_z + z], peer)

    for index, peer in enumerate(column):
        mod_push(index, peer).start()
    mod_got[core * n_z + z] = own_mod[...]

    for t in range(n_z):
        @pl.when(jnp.logical_not((z // 2 == core) & (t == z)))
        def _():
            push(img_got.at[t], img_got.at[t], i_send.at[0, 0], i_recv.at[t], (base + z // 2, t)).wait_recv()
    for t in range(n_z):
        for refs_of, spans in ((img_a, spans_a), (img_b, spans_b)):
            for ref, (begin, count) in zip(refs_of, spans):
                ref[:, t * count:(t + 1) * count] = img_got[t, :, begin:begin + count]

    for index, peer in enumerate(column):
        place_at = peer[0] % 2 * n_z + peer[1]
        push(mod_got.at[place_at], mod_got.at[place_at], d_send.at[index], d_recv.at[place_at], peer).wait_recv()
    step = width // 2
    per = own_mod.shape[1] // step
    imod_out[...] = jnp.zeros_like(imod_out)
    tmod_out[...] = jnp.zeros_like(tmod_out)
    for q in range(12):
        t, lanes = q // per, slice(q % per * step, (q % per + 1) * step)
        into = slice(q % 2 * step, (q % 2 + 1) * step)
        here = mod_got[z // 2 * n_z + t]
        imod_out[q // 2:q // 2 + 1, into] = jnp.where(z % 2 == 0, here[0:1, lanes], here[1:2, lanes])
        ours = mod_got[core * n_z + t]
        for s in range(2):
            tmod_out[8 * s + q // 2:8 * s + q // 2 + 1, into] = ours[2 + s:3 + s, lanes]

    own = own_ref[...]
    pick = lambda r: jnp.where(own > 0, tmod_out[r:r + 1, :], tmod_out[8 + r:9 + r, :])
    hat, _inv = norm_rows(xt_ref[...].astype(f32))
    th_out[z] = (hat * (1.0 + pick(1)) + pick(0)).astype(bf16)
    ring.start(lambda to: th_out.at[z], th_out, a_send, a_recv)
    dm_out[z] = (pick(5) * gt_ref[...].astype(f32)).astype(bf16)
    ring.start(lambda to: dm_out.at[z], dm_out, dm_send, dm_recv)
    tokens_wait(x_ref, x_out, x_send, x_recv)
    quarter = x_ref.shape[1]
    for i in range(2):
        def norm(r, _):
            sl = pl.ds(pl.multiple_of(r * ROWS, ROWS), ROWS)
            hat, _inv = norm_rows(x_out[i, sl, :].astype(f32))
            h_out[pl.ds(pl.multiple_of(i * quarter + r * ROWS, ROWS), ROWS), :] = (
                hat * (1.0 + imod_out[1:2, :]) + imod_out[0:1, :]).astype(bf16)
            return 0

        lax.fori_loop(0, quarter // ROWS, norm, 0)
    tokens_start(g_ref, g_out, g_send, g_recv)

    for m in (1, 2, 3):
        at_distance(1, lambda zz: forward(m, zz))

    finish(FULL, z)
    settle(FULL, z)
    own_copy(FULL).wait()
    load = pltpu.make_async_copy(outs[FULL], wtxt, tw_sem)
    load.start()
    ring.wait(th_out, a_send, a_recv)
    pad = xt_ref.shape[0]
    h_txt = th_out[...].reshape(n_z * pad, width)
    tmid = (mm_t(h_txt, txt_a[0][...]) * tmask_ref[...]).astype(bf16)
    tmid_out[...] = tmid
    load.wait()
    tq_ref[...] = (mm(h_txt, wtxt[...].reshape(width, wtxt.shape[2])) + mm(tmid, txt_b[0][...])).astype(bf16)
    for s in range(2):
        @pl.when(is_here(s))
        def _():
            copy = pltpu.make_async_copy(tq_ref, theads_out.at[z % 2], q_recv.at[z % 2])
            copy.start()
            copy.wait()

        @pl.when(jnp.logical_not(is_here(s)))
        def _():
            push(tq_ref, theads_out.at[z % 2], q_send.at[s], q_recv.at[z % 2], there[s]).start()

    every_z(0, finish)
    every_z(0, settle)
    own_copy(0).wait()
    mid = mm_t(h_out[...], img_a[0][...]).astype(bf16)
    mid_out[...] = mid
    tn = wtile.shape[3]
    per_half = stage.shape[2] // tn

    def tile_of(n):
        side = 1 - core if n < per_half else core
        return side, side * per_half + n % per_half

    def tile_load(n):
        at = pl.ds(pl.multiple_of(tile_of(n)[1] * tn, 128), tn)
        return pltpu.make_async_copy(outs[0].at[:, :, at], wtile.at[n % 2], w_sem.at[n % 2])

    def heads_push():
        return push(stage.at[0], heads_out.at[core], h_send, h_recv, (partner, z))

    tile_load(0).start()
    for n in range(2 * per_half):
        if n + 1 < 2 * per_half:
            tile_load(n + 1).start()
        tile_load(n).wait()
        at = pl.ds(pl.multiple_of(tile_of(n)[1] * tn, 128), tn)
        lanes = slice(n % per_half * tn, (n % per_half + 1) * tn)
        stage[n // per_half, :, lanes] = (
            mm(h_out[...], wtile[n % 2].reshape(width, tn)) + mm(mid, img_b[0][:, at])).astype(bf16)
        if n == per_half - 1:
            heads_push().start()
    keep = pltpu.make_async_copy(stage.at[1], heads_out.at[core], h_sem)
    keep.start()

    sign_push.wait_recv()
    chip_sign = jnp.where(z // 2 == core, sign_ref[...], sign_got[...])
    chip_sign = jnp.where(z % 2 == 0, chip_sign, -chip_sign)
    bias_out[...] = jnp.where(chip_sign > 0, 0.0, -1e30)
    hot_push.wait_recv()
    hot4_out[:rank2, :] = jnp.where(core == 0, hot2_ref[...].astype(f32), hot_got[...].astype(f32)).astype(bf16)
    hot4_out[rank2:, :] = jnp.where(core == 0, hot_got[...].astype(f32), hot2_ref[...].astype(f32)).astype(bf16)
    keep.wait()
    push(stage.at[0], heads_out.at[1 - core], h_send, h_recv, (partner, z)).wait_recv()
    for s in range(2):
        @pl.when(jnp.logical_not(is_here(s)))
        def _():
            push(theads_out.at[s], theads_out.at[s], q_send.at[s], q_recv.at[s], there[s]).wait_recv()
    pairs = heads_out.shape[2] // (6 * HD)
    per_part = pairs // 2

    def pair_loads(i):
        lanes = pl.ds(pl.multiple_of(i * (6 * HD), 128), 6 * HD)
        part = pl.ds(pl.multiple_of(i % per_part * (6 * HD), 128), 6 * HD)
        return [pltpu.make_async_copy(heads_out.at[:, :, lanes], img_buf.at[i % 2], b_sem.at[i % 2, 0]),
                pltpu.make_async_copy(theads_out.at[i // per_part, :, part], txt_buf.at[i % 2], b_sem.at[i % 2, 1])]

    def pair_lanes(i):
        return pl.ds(pl.multiple_of((core * pairs + i) * (2 * HD), 128), 2 * HD)

    def o_keep(i):
        return pltpu.make_async_copy(o_stage.at[i, core], att_out.at[:, pair_lanes(i)], o_sem.at[i])

    def o_push(i):
        return push(o_stage.at[i, 1 - core], att_out.at[:, pair_lanes(i)], o_send.at[i], o_recv.at[i], (partner, z))

    for copy in pair_loads(0):
        copy.start()
    tokens = img_buf.shape[1] * img_buf.shape[2]

    def pair_step(i, _):
        at = i % 2

        @pl.when(i + 1 < pairs)
        def _():
            for copy in pair_loads(i + 1):
                copy.start()

        for copy in pair_loads(i):
            copy.wait()
        bias = bias_out[:, 0:1]
        for h in range(2):
            low = 3 * HD * h
            ki = img_buf[at, :, :, low + HD:low + 2 * HD].reshape(tokens, HD)
            vi = img_buf[at, :, :, low + 2 * HD:low + 3 * HD].reshape(tokens, HD)
            kt = txt_buf[at, :, low + HD:low + 2 * HD]
            vt = txt_buf[at, :, low + 2 * HD:low + 3 * HD]
            for b in range(3):
                q = img_buf[at, b, :, low:low + HD] if b < 2 else txt_buf[at, :, low:low + HD]
                o, lse = attend_block(q, ki, vi, kt, vt, bias)
                rows = img_buf.shape[2]
                if b < 2:
                    o_stage[i, b, :, h * HD:(h + 1) * HD] = o
                    lse_out[i, h:h + 1, b * rows:(b + 1) * rows] = lse
                else:
                    ot_stage = o
                    lse_out[i, h:h + 1, tokens:tokens + q.shape[0]] = lse
            if h == 0:
                first = ot_stage
        both = jnp.concatenate([first, ot_stage], axis=1)
        ot_out[i // per_part, :, pl.ds(pl.multiple_of(i % per_part * (2 * HD), 128), 2 * HD)] = both
        o_keep(i).start()
        o_push(i).start()
        return 0

    lax.fori_loop(0, pairs // 2, pair_step, 0)
    for m in (1, 2, 3):
        at_distance(2, lambda zz: forward(m, zz))
    lax.fori_loop(pairs // 2, pairs, pair_step, 0)

    for m in (1, 2, 3):
        at_distance(n_z - 1, lambda zz: forward(m, zz))
    for m in range(total - 1):
        if m not in (0, FULL):
            every_z(m, finish)
    for m in range(total - 1):
        if m not in (0, FULL):
            every_z(m, settle)
            own_copy(m).wait()
    for m in range(total):
        every_z(m, drain)
        if m < FULL:
            def sent(zz, _):
                @pl.when((zz <= z) & (z < n_z - 1))
                def _():
                    z_copy(m, zz, 1).wait_send()

                @pl.when((zz >= z) & (z > 0))
                def _():
                    z_copy(m, zz, 0).wait_send()

                return 0

            lax.fori_loop(0, n_z, sent, 0)
    for copy in cond_sends + lane_sends + mod_sends:
        copy.wait_send()
    around_wait(cond_out, l_send, l_recv)
    ring.drain(lambda to: txt_msg, txt_got, t_send, t_recv)
    ring.drain(lambda to: th_out.at[z], th_out, a_send, a_recv)
    ring.wait(dm_out, dm_send, dm_recv)
    ring.drain(lambda to: dm_out.at[z], dm_out, dm_send, dm_recv)
    for index, peer in enumerate(column):
        mod_push(index, peer).wait_send()
    for s in range(2):
        for side in range(2):
            @pl.when(jnp.logical_not((side == core) & (2 * core + s == z)))
            def _():
                img_push(s, side).wait_send()
    tokens_wait(g_ref, g_out, g_send, g_recv)
    tokens_drain(x_ref, x_out, x_send, x_recv)
    tokens_drain(g_ref, g_out, g_send, g_recv)
    heads_push().wait_send()
    sign_push.wait_send()
    hot_push.wait_send()

    def o_done(i, _):
        o_keep(i).wait()
        o_push(i).wait_send()
        other = pl.ds(pl.multiple_of(((1 - core) * pairs + i) * (2 * HD), 128), 2 * HD)
        push(o_stage.at[i, 0], att_out.at[:, other], o_send.at[i], o_recv.at[i], (partner, z)).wait_recv()
        return 0

    lax.fori_loop(0, pairs, o_done, 0)
    for s in range(2):
        @pl.when(jnp.logical_not(is_here(s)))
        def _():
            push(tq_ref, theads_out.at[z % 2], q_send.at[s], q_recv.at[z % 2], there[s]).wait_send()


def front(full, part, adapter_rows, x, g, picks, hot2, cond, wmod, x_txt, g_txt, own, tmask, smask, sign_rows, n_f, n_z, fans, cols, cid):
    f32, bf16 = jnp.float32, jnp.bfloat16
    vmem, dma = pltpu.VMEM, pltpu.SemaphoreType.DMA
    shape = jax.ShapeDtypeStruct
    slots, width = cond.shape
    k_local = wmod.shape[1]
    z = lax.axis_index("tp")
    blocks = jnp.pad(jnp.swapaxes(cond.reshape(slots, n_f, k_local), 0, 1), ((0, 0), (0, 6), (0, 256 - k_local)))
    cond8 = jnp.concatenate([cond, cond, jnp.zeros((4, width), f32)])
    lane = jnp.pad(lax.dynamic_slice_in_dim(cond, z * (width // n_z), width // n_z, 1), ((0, 6), (0, 0)))
    chosen = (picks[:, None] == jnp.arange(NAD)[None, :]).astype(f32).reshape(-1, 1)
    smalls = (jnp.broadcast_to(chosen, (slots * NAD, 128)), hot2, blocks, lane, cond8, smask, wmod, x_txt, g_txt, own, tmask, sign_rows)
    args = (*full, *part, adapter_rows, x, g, *smalls)
    any_spec, in_vmem = pl.BlockSpec(memory_space=pl.ANY), pl.BlockSpec(memory_space=vmem)
    rows = 2 * (sum(fans) + sum(cols)) // n_z
    chips = n_f // 2
    nbits = bits_of(chips)
    total = len(full) + len(part) + 1
    pad = x_txt.shape[0]
    img_rows = 2 * x.shape[1]
    cut = cols[0] // n_z
    qkv_part = cols[1] // n_z
    thick = tmask.shape[1]
    rank2 = hot2.shape[0]
    own_a = [fans[1], fans[2] // n_z, fans[3], fans[4] // n_z]
    own_b = [cols[1] // n_z, cols[2], cols[3] // n_z, cols[4]]
    lanes = (sum(fans[1:]) + sum(cols[1:])) // n_z
    share = width // n_z
    outs = [shape((n_f,) + a.shape[:-1] + (a.shape[-1] * (n_z if i < len(full) else 1),), a.dtype) for i, a in enumerate(full + part)]
    in_hbm = len(outs)
    outs += [shape(x.shape, bf16), shape(g.shape, bf16), shape((8, width), f32), shape((16, width), f32)]
    outs += [shape((RANK, n), bf16) for n in fans[1:]] + [shape((RANK, n), bf16) for n in cols[1:]]
    outs += [shape((thick, n), bf16) for n in own_a] + [shape((thick, n), bf16) for n in own_b]
    outs += [shape((2, rank2, width), bf16), shape((2, rank2, cut), bf16), shape((2, 8, rank2), f32), shape((n_f, 8, share), f32), shape((n_z, pad, width), bf16)]
    heads_half = cols[1] // (6 * HD)
    pairs = heads_half // 2
    outs += [shape((2, n_z * pad, width // n_z), bf16), shape((pairs, 2, 2 * img_rows + n_z * pad), f32), shape(sign_rows.shape, f32),
             shape((2 * rank2, NAD * RANK), bf16)]
    outs += [shape((img_rows, width), bf16), shape((img_rows, RANK), bf16), shape((2, img_rows, cols[1] // 2), bf16),
             shape((n_z, pad, width), bf16), shape((n_z * pad, thick), bf16), shape((2, n_z * pad, qkv_part), bf16), shape((img_rows, width), bf16)]
    specs = [any_spec] * in_hbm + [in_vmem, any_spec] + [in_vmem] * (len(outs) - in_hbm - 2)
    for place in (1, 2, 5):
        specs[len(outs) - place] = any_spec
    return pl.pallas_call(
        functools.partial(front_kernel, n_f, n_z, tuple(fans), tuple(cols)),
        out_shape=outs,
        in_specs=[any_spec] * (total + 2) + [in_vmem] * len(smalls),
        out_specs=specs,
        scratch_shapes=[
            vmem((rows, 128), bf16), vmem((cut // NAD, 128), f32), vmem((2, RANK, lanes), bf16), vmem((n_z, RANK, lanes), bf16),
            vmem((rank2, 6 * share), bf16), vmem((n_z, rank2, 6 * share), bf16), vmem((n_f, 8, 256), f32),
            vmem((n_f, 8, cut), f32), vmem((n_f, 8, cut), f32), vmem((8, cut), f32), vmem((2 * n_z, 8, cut), f32),
            vmem((2, n_f, k_local, 768), bf16), vmem((n_f, k_local, qkv_part), bf16), vmem((2, img_rows, cols[1] // 2), bf16),
            vmem((n_z * pad, qkv_part), bf16), vmem(sign_rows.shape, f32), vmem((rank2, NAD * RANK), bf16),
            vmem((2, 2, img_rows, 6 * HD), bf16), vmem((2, n_z * pad, 6 * HD), bf16), vmem((pairs, 2, img_rows, 2 * HD), bf16),
            dma((total, n_z, 2)), dma((total, n_z)), dma((total, n_z, 2, chips, nbits)), dma((total, n_z, 2, chips)),
            dma((total, n_z, 2, chips)), dma((total, n_z, 2, chips)), dma((total,)),
            dma((2,)), dma((2,)), dma((2,)), dma((2,)), dma((n_f,)), dma((n_f,)), dma((n_f,)), dma((n_f,)), dma((n_f,)), dma((n_f,)),
            dma((2, 2)), dma((n_z,)), dma((n_z,)), dma((n_z,)), dma((2 * n_z,)), dma((2 * n_z,)), dma((n_z,)), dma((n_z,)),
            dma((2,)), dma, dma, dma, dma, dma((2,)), dma((2,)), dma((n_z,)), dma((n_z,)),
            dma((2,)), dma((2,)), dma((2, 2)), dma((pairs,)), dma((pairs,)), dma((pairs,)),
        ],
        compiler_params=pltpu.CompilerParams(collective_id=cid, has_side_effects=True, vmem_limit_bytes=58 * 1024 * 1024),
        name="front",
    )(*args)

HD = 64
FF = 6144
NAD = 8
RANK = 16
EPS = 1e-06
HIGH = lax.Precision.HIGHEST
F32 = jnp.float32
BF16 = jnp.bfloat16
BOTH = ("fsdp", "tp")


def matmul(left, right):
    return jnp.dot(left, right, preferred_element_type=F32)


def exact(left, right):
    return jnp.dot(left, right, precision=HIGH, preferred_element_type=F32)


def inner_left(left, right):
    return lax.dot_general(left, right, (((0,), (0,)), ((), ())), preferred_element_type=F32)


def inner_right(left, right):
    return lax.dot_general(
        left, right, (((left.ndim - 1,), (right.ndim - 1,)), ((), ())), preferred_element_type=F32
    )


def layer_norm(values):
    center = values - jnp.mean(values, axis=-1, keepdims=True)
    inverse = lax.rsqrt(jnp.mean(center * center, axis=-1, keepdims=True) + EPS)
    return (center * inverse, inverse)


def norm_back(grad_normed, normed, inverse, scale):
    grad_hat = grad_normed * (1.0 + scale)
    return inverse * (
        grad_hat
        - jnp.mean(grad_hat, axis=-1, keepdims=True)
        - normed * jnp.mean(grad_hat * normed, axis=-1, keepdims=True)
    )


def gelu(value):
    return jax.nn.gelu(value, approximate=True)


def gelu_back(value, grad):
    return jax.vjp(gelu, value)[1](grad)[0]


def shards(
    image_tokens,
    text_tokens,
    conditioning,
    text_lengths,
    adapter_index,
    adapters,
    mod_weight,
    qkv_weight,
    out_weight,
    fc1_weight,
    fc2_weight,
    image_cot,
    text_cot,
):
    n_f, n_z = lax.axis_size("fsdp"), lax.axis_size("tp")
    f, z = lax.axis_index("fsdp"), lax.axis_index("tp")
    core = f % 2
    slots, quarter, width = image_tokens.shape
    txt_local = text_tokens.shape[0]
    txt_group = txt_local * n_z
    img_half = 2 * quarter
    img_n = 2 * img_half
    cols = [6 * width, 3 * width, width, FF, width]
    fans = [width, width, width, width, FF]

    def round_pairs(r):
        pairs = []
        for fa in range(n_f):
            for t in range(n_z):
                there = (fa // 2 * 2 + t // 2) * n_z + 2 * (fa % 2) + (r ^ (t % 2))
                pairs.append((fa * n_z + t, there))
        return pairs

    low_bit = z % 2

    def pick(stack, bit):
        return lax.dynamic_index_in_dim(stack, bit, 0, keepdims=False)

    def flip(r):
        return low_bit if r == 0 else 1 - low_bit

    def to_chip(parts):
        got = [lax.ppermute(parts[r], BOTH, round_pairs(r)) for r in range(2)]
        return jnp.where(low_bit == 0, got[0], got[1]), jnp.where(low_bit == 0, got[1], got[0])

    def from_chip(pieces):
        got = []
        for r in range(2):
            mine = jnp.where(flip(r) == 0, pieces[0], pieces[1])
            got.append(lax.ppermute(mine, BOTH, [(b, a) for a, b in round_pairs(r)]))
        return jnp.where(low_bit == 0, got[0], got[1]), jnp.where(low_bit == 0, got[1], got[0])

    def reshard(values):
        return jnp.concatenate(to_chip([pick(values, flip(r)) for r in range(2)]), axis=0)

    def unshard(values):
        return jnp.stack(from_chip([values[:quarter], values[quarter:]]))

    def swap_core(values):
        return lax.ppermute(values, "fsdp", [(i, i ^ 1) for i in range(n_f)])

    def by_core(mine, other, axis):
        first = jnp.where(core == 0, mine, other)
        second = jnp.where(core == 0, other, mine)
        return jnp.concatenate([first, second], axis=axis)

    def z_swap(values, step):
        return lax.ppermute(values, "tp", [(i, i ^ step) for i in range(n_z)])

    def z_order(pieces):
        stack = jnp.stack(pieces)
        return [pick(stack, z ^ a) for a in range(n_z)]

    def z_gather(values):
        return z_order([values] + [z_swap(values, j) for j in range(1, n_z)])

    def z_exchange(blocks):
        return z_order([pick(blocks, z ^ j) if j == 0 else z_swap(pick(blocks, z ^ j), j) for j in range(n_z)])

    def z_scatter(values):
        count = values.shape[0] // n_z
        mine = lax.dynamic_slice_in_dim(values, z * count, count, 0)
        for j in range(1, n_z):
            part = lax.dynamic_slice_in_dim(values, (z ^ j) * count, count, 0)
            mine = mine + z_swap(part.astype(BF16), j).astype(F32)
        return mine

    def to_heads(values):
        half = values.shape[1] // 2
        low, high = values[:, :half], values[:, half:]
        mine = jnp.where(core == 0, low, high)
        return by_core(mine, swap_core(jnp.where(core == 0, high, low)), 0)

    def to_tokens(values):
        low, high = values[:img_half], values[img_half:]
        mine = jnp.where(core == 0, low, high)
        return by_core(mine, swap_core(jnp.where(core == 0, high, low)), 1)

    out_t = jnp.swapaxes(out_weight, 1, 2)
    fc2_t = jnp.swapaxes(fc2_weight, 1, 2)
    local = [qkv_weight, out_t, fc1_weight, fc2_t]
    adapter_rows = lax.optimization_barrier(adapters.reshape(-1, 128)).astype(BF16)
    txt_pad = (txt_local + 15) // 16 * 16

    def padded(values):
        return jnp.pad(values, ((0, txt_pad - txt_local), (0, 0)))

    x_txt_low, g_txt_low = padded(text_tokens), padded(text_cot)
    x_txt = x_txt_low.astype(F32)

    seg_ends = jnp.cumsum(text_lengths[0])
    slot_ids = jnp.arange(slots)

    def owner_of(position):
        segment = jnp.sum((position[:, None] >= seg_ends[None, :]).astype(jnp.int32), axis=1)
        return (segment[:, None] == slot_ids[None, :]).astype(F32)

    def real(owner):
        place = jnp.arange(owner.shape[0]) % txt_pad
        return jnp.where((place < txt_local)[:, None], owner, 0.0)

    def position(rows):
        return rows // txt_pad * txt_local + rows % txt_pad

    txt_rows = jnp.arange(n_z * txt_pad)
    owner_group = real(owner_of(position(txt_rows)))
    owner_local = real(owner_of(z * txt_local + jnp.arange(txt_pad)))
    txt_mask = jnp.repeat(owner_group, RANK, axis=1)
    txt_mask_local = jnp.repeat(owner_local, RANK, axis=1)
    rank_cols = slots * RANK
    seq_mask = jnp.repeat(jnp.eye(slots, dtype=F32), RANK, axis=1)

    def by_group(mine, other):
        return by_core(mine, other, 0)

    def stretch(stream, index):
        if stream == 0:
            return img_mod[:, index * width : (index + 1) * width]
        return exact(owner_local, txt_mods[:, index * width : (index + 1) * width])

    def collapse(stream, values):
        if stream == 0:
            return jnp.sum(values, axis=0, keepdims=True)
        return exact(owner_local.T, values)

    def share(values):
        return jnp.concatenate(z_gather(values), axis=0)

    def give(values, rank_part):
        got = z_scatter(jnp.concatenate([values, rank_part], axis=1))
        return got[:, :width], (got[:, width:] * txt_mask_local).astype(BF16)

    def lanes(values):
        count = values.shape[1] // n_z
        return lax.dynamic_slice_in_dim(values, z * count, count, 1)

    def project(values, weight, pair, mask, flipped):
        middle = inner_right(values, pair[0])
        if mask is not None:
            middle = middle * mask
        middle = middle.astype(BF16)
        main = inner_right(values, weight) if flipped else matmul(values, weight)
        return middle, main + matmul(middle, pair[1])

    own_hot = (
        jnp.arange(NAD * RANK)[:, None]
        == (adapter_index[:, None] * RANK + jnp.arange(RANK)[None, :]).reshape(1, -1)
    ).astype(F32)
    k_local = mod_weight.shape[1]
    cond_act = jax.nn.silu(conditioning).astype(BF16)
    thick = 128

    def thicker(part):
        return jnp.concatenate([part, jnp.zeros((thick - part.shape[0], part.shape[1]), part.dtype)], axis=0)

    def sign(owner):
        return owner[:, 0:1] - owner[:, 1:2]

    def lanes_pad(mask):
        return jnp.pad(mask, ((0, 0), (0, thick - mask.shape[1])))

    if n_f == 8:
        slot_mask = jnp.pad(jnp.concatenate([seq_mask, seq_mask]), ((0, 4), (0, 0)))
        made = front(
            [w[0] for w in local], [w[1] for w in local], adapter_rows, image_tokens, image_cot,
            adapter_index, own_hot.T.astype(BF16), cond_act.astype(F32), mod_weight, x_txt_low,
            g_txt_low, sign(owner_local), lanes_pad(txt_mask), slot_mask,
            jnp.broadcast_to(sign(owner_group), (owner_group.shape[0], thick)), n_f, n_z, fans, cols, 1,
        )
        made = iter(made)
        take = lambda count: [next(made) for _ in range(count)]
        img_w = [w.reshape(-1, w.shape[-1]) for w in take(4)]
        txt_w = [w.reshape(-1, w.shape[-1]) for w in take(4)]
        x_img, g_img = [v.reshape(-1, width) for v in take(2)]
        img_rows_mod, txt_mod = take(2)
        img_pairs = [None] + list(zip(take(4), take(4)))
        thick_pairs = [None] + list(zip(take(4), take(4)))
        mod_a, mod_b, tmod, cond_own, txt_dm = take(5)
        o_txt, lse, bias, hot_four = take(4)
        bias = bias[:, :1]
        img_in, img_qkv_mid, img_heads, txt_in, txt_qkv_mid, txt_heads, attended = take(7)
        img_heads = img_heads.reshape(img_n, -1)
        txt_in = txt_in.reshape(-1, width)
        txt_pairs = [None, tuple(part[:rank_cols] for part in thick_pairs[1])]
        img_mod = img_rows_mod[:6].reshape(1, -1)
        txt_mods = txt_mod.reshape(slots, 8, width)[:, :6].reshape(slots, -1)
    else:
        column_picks = by_group(adapter_index, swap_core(adapter_index))
        column_count = 2 * slots
        one_hot = (
            jnp.arange(NAD * RANK)[:, None]
            == (column_picks[:, None] * RANK + jnp.arange(RANK)[None, :]).reshape(1, -1)
        ).astype(F32)
        got = gather([w[0] for w in local], [w[1] for w in local] + [adapter_rows], n_f, n_z)
        got = [g.reshape(-1, g.shape[-1]) for g in got]
        img_w, txt_w, row = got[:4], got[4:8], got[8]
        x_img = reshard(image_tokens)
        g_img = reshard(image_cot)
        own_picks = adapter_index

        a_rows = [[None] * 5 for stream in range(2)]
        b_rows = [[None] * 5 for stream in range(2)]
        offset = 0
        for stream in range(2):
            for index in range(5):
                count = fans[index] // n_z
                a_rows[stream][index] = row[offset : offset + count]
                offset += count
                count = cols[index] // n_z
                b_rows[stream][index] = row[offset : offset + count]
                offset += count

        def b_pick(stream, index, pick_index):
            part = b_rows[stream][index]
            count = part.shape[0] // NAD
            return lax.dynamic_slice_in_dim(part, pick_index * count, count, 0).reshape(RANK, -1)

        def a_pick(rows, hot):
            return inner_right(hot.T.astype(BF16), rows).astype(BF16)

        img_a = a_pick(jnp.concatenate(a_rows[0], axis=0), one_hot)
        fan_share = sum(fans) // n_z
        img_a = img_a.reshape(column_count, RANK, fan_share)
        img_b = [
            jnp.concatenate([b_pick(0, index, column_picks[s]) for index in range(1, 5)], axis=1)
            for s in range(column_count)
        ]
        img_msg = jnp.concatenate([img_a, jnp.stack(img_b)], axis=2)
        txt_a_rows = jnp.concatenate(
            [a_rows[0][0], a_rows[1][0], a_rows[1][1], a_rows[1][3]], axis=0
        )
        txt_a = a_pick(txt_a_rows, own_hot).reshape(slots, RANK, -1)
        txt_b_own = [
            [b_pick(stream, index, own_picks[s]) for s in range(slots)]
            for stream, index in [(0, 0), (1, 0), (1, 1), (1, 2), (1, 3), (1, 4)]
        ]
        txt_b_own = [jnp.concatenate(parts, axis=0) for parts in txt_b_own]
        txt_a_own = a_pick(jnp.concatenate([a_rows[1][2], a_rows[1][4]], axis=0), own_hot)
        txt_msg = jnp.concatenate(
            [txt_a.reshape(slots * RANK, -1), txt_b_own[3], txt_b_own[5]], axis=1
        )
        img_got = jnp.stack(z_exchange(img_msg))
        txt_got = jnp.stack(z_gather(txt_msg))

        def join(part):
            return jnp.swapaxes(part, 0, 1).reshape(part.shape[1], -1)

        img_pairs = []
        offset, b_offset = 0, fan_share
        for index in range(5):
            count = fans[index] // n_z
            a_full = join(img_got[:, :, offset : offset + count])
            offset += count
            if index == 0:
                img_pairs.append(None)
                continue
            count = cols[index] // n_z
            b_full = join(img_got[:, :, b_offset : b_offset + count])
            b_offset += count
            img_pairs.append((a_full, b_full))
        txt_full = []
        offset = 0
        for count in [width // n_z] * 6:
            txt_full.append(join(txt_got[:, :, offset : offset + count]))
            offset += count
        mod_a = [txt_full[0], txt_full[1]]
        mod_b = [txt_b_own[0], txt_b_own[1]]
        txt_pairs = [
            None,
            (txt_full[2], txt_b_own[2]),
            (txt_a_own[:, : width // n_z], txt_full[4]),
            (txt_full[3], txt_b_own[4]),
            (txt_a_own[:, width // n_z :], txt_full[5]),
        ]

        cond_all = lax.all_gather(cond_act, "fsdp", axis=0, tiled=True)
        cond_slice = lax.dynamic_slice_in_dim(cond_all, f * k_local, k_local, 1)
        mod_part = jnp.stack([matmul(cond_slice, mod_weight[stream]) for stream in range(2)], axis=1)
        mod_part = lax.psum_scatter(mod_part, "fsdp", scatter_dimension=0, tiled=True)
        mod_mid = []
        mod_terms = []
        for stream in range(2):
            middle = (inner_right(cond_act, mod_a[stream]) * seq_mask).astype(BF16)
            mod_mid.append(middle)
            mod_terms.append(mod_part[:, stream] + matmul(middle, mod_b[stream]))
        mods = jnp.concatenate(z_gather(jnp.stack(mod_terms, axis=1)), axis=2)
        img_mods = by_group(mods[:, 0], swap_core(mods[:, 0]))
        img_mod = lax.dynamic_slice_in_dim(img_mods, z, 1, 0)
        txt_mods = mods[:, 1]

        img_rows_mod = jnp.concatenate([img_mod.reshape(6, width), jnp.zeros((2, width), F32)], axis=0)
        txt_mod = jnp.pad(txt_mods.reshape(slots, 6, width), ((0, 0), (0, 2), (0, 0))).reshape(-1, width)
        thick_pairs = [None] + [tuple(thicker(part) for part in txt_pairs[index]) for index in range(1, 5)]
        norm_first = [layer_norm(v.astype(F32)) for v in (x_img, x_txt)]
        heads_in = [
            (norm_first[s][0] * (1.0 + stretch(s, 1)) + stretch(s, 0)).astype(BF16) for s in range(2)
        ]

        txt_in = share(heads_in[1])
        txt_qkv_mid, txt_qkv = project(txt_in, txt_w[0], txt_pairs[1], txt_mask, False)
        img_qkv_mid, img_qkv = project(heads_in[0], img_w[0], img_pairs[1], None, False)
        txt_qkv, img_qkv = txt_qkv.astype(BF16), img_qkv.astype(BF16)
        img_heads = to_heads(img_qkv)
        txt_heads = jnp.stack(to_chip([txt_qkv, txt_qkv]))
        img_in = heads_in[0]
        txt_dm = jnp.stack(z_gather((stretch(1, 5) * g_txt_low.astype(F32)).astype(BF16)))

    inputs = [x_img.astype(F32), x_txt]
    norm_one = [layer_norm(values) for values in inputs]
    def txt_home(values):
        got = from_chip([values[0], values[1]])
        return jnp.where(owner_group[:, 0:1] > 0, got[0], jnp.where(owner_group[:, 1:2] > 0, got[1], 0))

    if n_f != 8:
        lengths = by_group(text_lengths[0:1], swap_core(text_lengths[0:1]))
        chip_lengths = jnp.cumsum(lax.dynamic_index_in_dim(lengths, z // slots, 0, keepdims=False))
        chip_slot = z % slots
        chip_segment = jnp.sum(
            (position(txt_rows)[:, None] >= chip_lengths[None, :]).astype(jnp.int32),
            axis=1,
            keepdims=True,
        )
        chip_owner = (chip_segment == chip_slot) & (txt_rows % txt_pad < txt_local)[:, None]
        bias = jnp.where(chip_owner, 0.0, -1e30).astype(F32)
        o_img, o_txt, lse = attend(img_heads, txt_heads, bias, HD)

        attended = to_tokens(o_img)
    (img_branch, img_after, img_mlp, img_pre, img_result, *img_mids, img_gate, txt_mlp, txt_att, txt_after, txt_branch) = both_fwd(
        attended, x_img, g_img, img_rows_mod, img_w[1], img_pairs[2], img_pairs[3], img_w[2], img_pairs[4], img_w[3],
        o_txt, x_txt_low, txt_mod, sign(owner_group), sign(owner_local), lanes_pad(txt_mask_local), txt_w[1], thick_pairs[2],
        n_z, 2,
    )
    made = both_back(
        g_img, img_after, img_branch, img_mlp, attended, img_rows_mod, img_pre, img_w[3], img_pairs[4], img_w[2], img_pairs[3],
        img_w[1], img_pairs[2], img_mids, g_txt_low, txt_after, txt_branch, txt_mod, sign(owner_local), lanes_pad(txt_mask),
        lanes_pad(txt_mask_local), txt_mlp, txt_att, txt_dm, txt_w[1], txt_w[2], txt_w[3], thick_pairs[2], thick_pairs[3],
        thick_pairs[4], n_z, 4,
    )
    img_grad_after, img_grad_att, img_sums, *sides = made[:9]
    txt_result, txt_grad_after, do_txt, txt_sums, *txt_sides = made[9:]
    if n_f != 8:
        txt_sides = [part[:rank_cols] for part in txt_sides]
    txt_sum_rows = txt_sums
    txt_sums = txt_sums.reshape(4, slots, width)
    if n_f != 8:
        image_out = unshard(img_result)

    grads = [[None] * 5 for stream in range(2)]

    def project_back(grad, weight, pair, mask, flipped):
        middle = inner_right(grad, pair[1])
        if mask is not None:
            middle = middle * mask
        middle = middle.astype(BF16)
        main = matmul(grad, weight) if flipped else inner_right(grad, weight)
        return middle, main + matmul(middle, pair[0])

    grads[0][4] = (sides[0], sides[3])
    grads[0][3] = (sides[2], sides[1])
    grads[0][2] = (sides[4], sides[5])
    mod_parts = [[None] * 6 for stream in range(2)]
    for place in range(4):
        mod_parts[1][2 + place] = txt_sums[place]
    grads[1][2] = (txt_sides[0], txt_sides[1])
    grads[1][3] = (txt_sides[2], txt_sides[3])
    grads[1][4] = (txt_sides[4], txt_sides[5])
    img_sum_rows = img_sums
    img_sums = jnp.sum(jnp.concatenate([img_sums, img_gate]).reshape(4, 8, width), axis=1)
    for place in range(4):
        mod_parts[0][2 + place] = img_sums[place : place + 1]
    grad_after = [img_grad_after, txt_grad_after]

    do_img = img_grad_att.reshape(img_n, -1)
    if n_f != 8:
        d_img, d_txt = attend_back(img_heads, txt_heads, bias, do_img, do_txt, lse, HD)
    if n_f == 8:
        sides_of = lambda stream, side: [grads[stream][index][side] for index in range(2, 5)]
        d_img, d_txt, image_out, early = attend_back_far(
            img_heads, txt_heads, bias, do_img, do_txt, lse, HD, img_result.reshape(2, quarter, width),
            sides_of(0, 0), sides_of(0, 1), n_z, fans, cols, 5,
        )
        smalls = (
            x_img, img_grad_after, img_in, img_rows_mod, img_qkv_mid, *img_pairs[1], img_sum_rows, img_gate,
            x_txt_low, txt_grad_after, txt_in.reshape(n_z, txt_pad, width), txt_mod, sign(owner_group), sign(owner_local),
            lanes_pad(txt_mask_local), txt_qkv_mid, txt_w[0], *thick_pairs[1], txt_sum_rows,
        )
        image_low, txt_grad, cond_slices, mod_rank, shard = tail(
            d_img.reshape(2, img_half, -1), d_txt, img_w[0].reshape(n_f, k_local, -1), smalls,
            early, sides_of(1, 0), sides_of(1, 1),
            hot_four, own_hot.T.astype(BF16), mod_weight, mod_b, tmod, cond_own, slot_mask,
            n_f, n_z, fans, cols, 3,
        )
        image_grad = image_low.astype(F32)
        cond_rows = jnp.swapaxes(cond_slices[:, :slots, :k_local], 0, 1).reshape(slots, width)
        for s in range(2):
            cond_rows = cond_rows + matmul(mod_rank[2 * s : 2 * s + 2].astype(BF16), mod_a[s])
        cond_grad = jax.vjp(jax.nn.silu, conditioning)[1](cond_rows)[0]
        adapter_grad = shard.reshape(1, -1)
        return (image_out, txt_result[:txt_local], image_grad, txt_grad[:txt_local], cond_grad, adapter_grad)
    img_grad_qkv = to_tokens(d_img)
    txt_grad_qkv = txt_home(d_txt)

    img_back_mid, img_grad_norm = project_back(img_grad_qkv, img_w[0], img_pairs[1], None, False)
    grads[0][1] = (inner_left(img_back_mid, img_in), inner_left(img_qkv_mid, img_grad_qkv))
    txt_grad_norm, txt_qkv_back = give(
        inner_right(txt_grad_qkv, txt_w[0]), inner_right(txt_grad_qkv, txt_pairs[1][1])
    )
    txt_grad_norm = txt_grad_norm + matmul(txt_qkv_back, txt_pairs[1][0])
    grads[1][1] = (
        inner_left(share(txt_qkv_back), lanes(txt_in)),
        inner_left(txt_qkv_mid, txt_grad_qkv),
    )
    grad_norm = [img_grad_norm, txt_grad_norm]
    grad_inputs = []
    for s in range(2):
        grad_inputs.append(
            grad_after[s]
            + norm_back(grad_norm[s], norm_one[s][0], norm_one[s][1], stretch(s, 1))
        )
        mod_parts[s][0] = collapse(s, grad_norm[s])
        mod_parts[s][1] = collapse(s, grad_norm[s] * norm_one[s][0])
    img_dmod = jnp.concatenate(mod_parts[0], axis=1)
    txt_dmod = jnp.concatenate(mod_parts[1], axis=1)
    image_grad = unshard(grad_inputs[0].astype(BF16)).astype(F32)

    img_dmod = (img_dmod + swap_core(img_dmod)).astype(BF16)
    def lane_blocks(values):
        return jnp.swapaxes(values.reshape(values.shape[0], n_z, -1), 0, 1)

    img_dmods = jnp.concatenate(z_exchange(lane_blocks(img_dmod)), axis=0)
    img_dmods = lax.dynamic_slice_in_dim(img_dmods, core * slots, slots, 0)
    txt_dmods = sum(z_exchange(lane_blocks(txt_dmod))).astype(BF16)
    dmods = jnp.stack([img_dmods, txt_dmods], axis=1)
    dmods_all = lax.all_gather(dmods, "fsdp", axis=0, tiled=True)
    cond_part = sum(inner_right(dmods_all[:, s], mod_weight[s]) for s in range(2))
    mod_back = [inner_right(dmods[:, s], mod_b[s]) for s in range(2)]
    cond_part = cond_part.reshape(-1, width // n_f)
    joined = jnp.concatenate([cond_part.reshape(-1), jnp.stack(mod_back).reshape(-1)])
    joined = sum(z_gather(joined))
    cond_slices = joined[: cond_part.size].reshape(n_f, -1, width // n_f)
    mod_rank = joined[cond_part.size :].reshape(2, slots, -1)
    cond_rows = lax.all_to_all(cond_slices, "fsdp", 0, 2, tiled=True)[0]
    for s in range(2):
        back_mid = (mod_rank[s] * seq_mask).astype(BF16)
        cond_rows = cond_rows + matmul(back_mid, mod_a[s])
        grads[s][0] = (inner_left(back_mid, lanes(cond_act)), inner_left(mod_mid[s], dmods[:, s]))
    cond_grad = jax.vjp(jax.nn.silu, conditioning)[1](cond_rows)[0]

    def spread(values):
        return jnp.swapaxes(values.reshape(RANK, n_z, -1), 0, 1)

    img_rows = {}
    for group in ((2, 3, 4), (1,)):
        parts = [spread(grads[0][index][side]) for side in range(2) for index in group]
        parts = jnp.concatenate(z_exchange(jnp.concatenate(parts, axis=2)), axis=0)
        offset = 0
        for side, sizes in enumerate((fans, cols)):
            for index in group:
                count = sizes[index] // n_z
                img_rows[side, index] = parts[:, offset : offset + count]
                offset += count
    flat = []
    for stream in range(2):
        for index in range(5):
            if stream == 0 and index > 0:
                part_a, part_b = img_rows[0, index], img_rows[1, index]
                hot = one_hot
            else:
                part_a, part_b = grads[stream][index]
                hot = own_hot
            flat.append(
                lax.dot_general(
                    part_a, hot, (((0,), (1,)), ((), ())),
                    precision=HIGH, preferred_element_type=F32,
                )
            )
            flat.append(exact(hot, part_b).reshape(-1, 128))
    total = jnp.concatenate(flat, axis=0).reshape(n_f, -1, 128)
    step = 1
    while step < n_f:
        bit = (f // step) % 2
        pairs = total.reshape((-1, 2) + total.shape[1:])
        keep = lax.dynamic_index_in_dim(pairs, bit, 1, keepdims=False)
        send = lax.dynamic_index_in_dim(pairs, 1 - bit, 1, keepdims=False)
        sent = lax.ppermute(send.astype(BF16), "fsdp", [(i, i ^ step) for i in range(n_f)])
        total = keep + sent.astype(F32)
        step *= 2
    adapter_grad = total.reshape(1, -1)
    return (
        image_out, txt_result[:txt_local], image_grad, grad_inputs[1][:txt_local], cond_grad, adapter_grad
    )


def solution(mesh):
    return jax.shard_map(
        shards,
        mesh=mesh,
        in_specs=(
            P("fsdp", "tp", None),
            P(("fsdp", "tp"), None),
            P("fsdp", None),
            P("fsdp", None),
            P("fsdp"),
            P("tp", "fsdp"),
            P(None, "fsdp", "tp"),
            P(None, "fsdp", "tp"),
            P(None, "tp", "fsdp"),
            P(None, "fsdp", "tp"),
            P(None, "tp", "fsdp"),
            P("fsdp", "tp", None),
            P(("fsdp", "tp"), None),
        ),
        out_specs=(
            P("fsdp", "tp", None),
            P(("fsdp", "tp"), None),
            P("fsdp", "tp", None),
            P(("fsdp", "tp"), None),
            P("fsdp", None),
            P("tp", "fsdp"),
        ),
        check_vma=False,
    )
```

```python
import functools

import jax
import jax.numpy as jnp
from jax import lax
from jax.experimental import pallas as pl
from jax.experimental.pallas import tpu as pltpu
from jax.sharding import PartitionSpec as P

MESH = pl.DeviceIdType.MESH

def bits_of(count):
    return max(count.bit_length() - 1, 0)

def halves(width):
    tiles = width // 128
    first = (tiles + 1) // 2 * 128
    return [(0, first), (first, width - first)]

def gather_kernel(n_f, n_z, full_count, part_count, *refs):
    total = full_count + part_count
    ins, outs = refs[:total], refs[total:2 * total]
    z_send, z_recv, xy_send, xy_recv, core_send, core_recv, own_sem = refs[2 * total:]
    f = lax.axis_index("fsdp")
    z = lax.axis_index("tp")
    chip, core = f // 2, f % 2
    chips = n_f // 2
    nbits = bits_of(chips)
    partner = chip * 2 + (1 - core)

    def peer_of(mask):
        other = 0
        for bit in range(nbits):
            have = (chip // (1 << bit)) % 2
            want = 1 - have if (mask >> bit) & 1 else have
            other = other + want * (1 << bit)
        return other * 2 + core

    barrier = pltpu.get_barrier_semaphore()
    for bit in range(nbits):
        pl.semaphore_signal(barrier, inc=1, device_id=(peer_of(1 << bit), z), device_id_type=MESH)
    pl.semaphore_signal(barrier, inc=1, device_id=(partner, z), device_id_type=MESH)
    @pl.when(z > 0)
    def _():
        pl.semaphore_signal(barrier, inc=1, device_id=(f, z - 1), device_id_type=MESH)
    @pl.when(z < n_z - 1)
    def _():
        pl.semaphore_signal(barrier, inc=1, device_id=(f, z + 1), device_id_type=MESH)
    peers = nbits + 1 + (z > 0).astype(jnp.int32) + (z < n_z - 1).astype(jnp.int32)
    pl.semaphore_wait(barrier, peers)

    def width(m):
        return ins[m].shape[-1]

    def place(m, who, zz, off=0, w=None):
        w = width(m) if w is None else w
        if m < full_count:
            return outs[m].at[who, :, pl.ds(pl.multiple_of(zz * width(m) + off, 128), w)]
        if w == width(m):
            return outs[m].at[who]
        return outs[m].at[who, :, pl.ds(off, w)]

    def piece(m, off, w):
        return ins[m] if w == width(m) else ins[m].at[:, pl.ds(off, w)]

    def remote(src, dst, ssem, rsem, dev):
        return pltpu.make_async_remote_copy(src_ref=src, dst_ref=dst, send_sem=ssem, recv_sem=rsem, device_id=dev, device_id_type=MESH)

    def order_of(half):
        order = list(range(nbits))
        return order if half == 0 else order[::-1]

    def cuts(m):
        if width(m) >= 256:
            return list(enumerate(halves(width(m))))
        return [(m % 2, (0, width(m)))]

    def slot(m, zz):
        return zz if m < full_count else 0

    def xy_copy(m, zz, half, cut, mask, bit, own_piece=False):
        off, w = cut
        who = peer_of(mask)
        source = piece(m, off, w) if own_piece and mask == 0 else place(m, who, zz, off, w)
        return remote(source, place(m, who, zz, off, w),
                      xy_send.at[m, slot(m, zz), half, mask, bit], xy_recv.at[m, slot(m, zz), half, mask | (1 << bit)],
                      (peer_of(1 << bit), z))

    def xy_wait(m, zz, half, cut, mask):
        off, w = cut
        who = peer_of(mask)
        remote(place(m, who, zz, off, w), place(m, who, zz, off, w), xy_send.at[m, slot(m, zz), half, 0, 0],
               xy_recv.at[m, slot(m, zz), half, mask], (partner, z)).wait_recv()

    def core_copy(m, zz, half, cut, mask, own_piece=False):
        off, w = cut
        who = peer_of(mask)
        source = piece(m, off, w) if own_piece and mask == 0 else place(m, who, zz, off, w)
        return remote(source, place(m, who, zz, off, w),
                      core_send.at[m, slot(m, zz), half, mask], core_recv.at[m, slot(m, zz), half, mask], (partner, z))

    def core_wait_recv(m, zz, half, cut, mask):
        off, w = cut
        who = peer_of(mask) - core + (1 - core)
        remote(place(m, who, zz, off, w), place(m, who, zz, off, w),
               core_send.at[m, slot(m, zz), half, mask], core_recv.at[m, slot(m, zz), half, mask], (partner, z)).wait_recv()

    def own(m):
        return pltpu.make_async_copy(ins[m], place(m, f, z), own_sem.at[m])

    def z_copy(m, zz, up, own_piece=False):
        return remote(ins[m] if own_piece else place(m, f, zz), place(m, f, zz), z_send.at[m, zz, up], z_recv.at[m, zz], (f, z + 1 if up else z - 1))

    def launch(m, zz, own_piece=False):
        for half, cut in cuts(m):
            for bit in order_of(half):
                xy_copy(m, zz, half, cut, 0, bit, own_piece).start()
            core_copy(m, zz, half, cut, 0, own_piece).start()

    def masks_in_order(half):
        order = order_of(half)
        def rank(mask):
            return [1 if (mask >> b) & 1 else 0 for b in reversed(order)]
        return sorted(range(1, 1 << nbits), key=rank)

    def forward(m, zz):
        for half, cut in cuts(m):
            order = order_of(half)
            for mask in masks_in_order(half):
                last = max(i for i, b in enumerate(order) if (mask >> b) & 1)
                if last == nbits - 1:
                    continue
                xy_wait(m, zz, half, cut, mask)
                for b in order[last + 1:]:
                    xy_copy(m, zz, half, cut, mask, b).start()
                core_copy(m, zz, half, cut, mask).start()

    def finish(m, zz):
        for half, cut in cuts(m):
            order = order_of(half)
            for mask in masks_in_order(half):
                last = max(i for i, b in enumerate(order) if (mask >> b) & 1)
                if last == nbits - 1:
                    xy_wait(m, zz, half, cut, mask)
                    core_copy(m, zz, half, cut, mask).start()

    def drain(m, zz):
        for half, cut in cuts(m):
            order = order_of(half)
            for mask in [0] + masks_in_order(half):
                last = max([i for i, b in enumerate(order) if (mask >> b) & 1], default=-1)
                for b in order[last + 1:]:
                    xy_copy(m, zz, half, cut, mask, b).wait_send()
                core_copy(m, zz, half, cut, mask).wait_send()
                core_wait_recv(m, zz, half, cut, mask)

    for m in range(total):
        own(m).start()
    for m in range(total):
        if m < full_count:
            @pl.when(z < n_z - 1)
            def _():
                z_copy(m, z, 1, True).start()
            @pl.when(z > 0)
            def _():
                z_copy(m, z, 0, True).start()
        launch(m, z, True)
    for m in range(full_count, total):
        forward(m, z)
    for k in range(1, n_z):
        for m in range(full_count):
            @pl.when(z - k >= 0)
            def _():
                zz = z - k
                z_copy(m, zz, 1).wait_recv()
                @pl.when(z < n_z - 1)
                def _():
                    z_copy(m, zz, 1).start()
                launch(m, zz)
            @pl.when(z + k < n_z)
            def _():
                zz = z + k
                z_copy(m, zz, 0).wait_recv()
                @pl.when(z > 0)
                def _():
                    z_copy(m, zz, 0).start()
                launch(m, zz)
            for sign in ((-1, 1) if k > 1 else (1,)):
                zz = z + sign * (k - 1)
                @pl.when((zz >= 0) & (zz < n_z))
                def _():
                    forward(m, zz)
    for m in range(full_count):
        for sign in (-1, 1):
            zz = z + sign * (n_z - 1)
            @pl.when((zz >= 0) & (zz < n_z))
            def _():
                forward(m, zz)
    for m in range(total):
        if m < full_count:
            def body(zz, _):
                finish(m, zz)
                return 0
            lax.fori_loop(0, n_z, body, 0)
        else:
            finish(m, z)
    for m in range(total):
        own(m).wait()
        if m < full_count:
            def body(zz, _):
                drain(m, zz)
                @pl.when((zz <= z) & (z < n_z - 1))
                def _():
                    z_copy(m, zz, 1).wait_send()
                @pl.when((zz >= z) & (z > 0))
                def _():
                    z_copy(m, zz, 0).wait_send()
                return 0
            lax.fori_loop(0, n_z, body, 0)
        else:
            drain(m, z)

def gather(full, part, n_f, n_z, cid=1):
    arrays = list(full) + list(part)
    total = len(arrays)
    if n_f > 8:
        rows = [lax.all_gather(a, "fsdp", axis=0, tiled=True) for a in arrays]
        return [
            lax.all_gather(a, "tp", axis=1, tiled=True) if i < len(full) else a
            for i, a in enumerate(rows)
        ]
    chips = n_f // 2
    nbits = bits_of(chips)
    shapes = [jax.ShapeDtypeStruct((n_f,) + a.shape[:-1] + (a.shape[-1] * (n_z if i < len(full) else 1),), a.dtype) for i, a in enumerate(arrays)]
    dma = pltpu.SemaphoreType.DMA
    return pl.pallas_call(
        functools.partial(gather_kernel, n_f, n_z, len(full), len(part)),
        out_shape=shapes,
        in_specs=[pl.BlockSpec(memory_space=pl.ANY)] * total,
        out_specs=[pl.BlockSpec(memory_space=pl.ANY)] * total,
        scratch_shapes=[
            dma((total, n_z, 2)), dma((total, n_z)),
            dma((total, n_z, 2, chips, max(nbits, 1))), dma((total, n_z, 2, chips)),
            dma((total, n_z, 2, chips)), dma((total, n_z, 2, chips)), dma((total,)),
        ],
        compiler_params=pltpu.CompilerParams(collective_id=cid, has_side_effects=True),
        name="weight_gather",
    )(*arrays)

def dots(left, right, lc, rc):
    return lax.dot_general(left, right, (((lc,), (rc,)), ((), ())), preferred_element_type=jnp.float32)

def attend_block(q, ki, vi, kt, vt, bias):
    q = q * jnp.bfloat16(0.125)
    si = dots(ki, q, 1, 1)
    st = dots(kt, q, 1, 1) + bias
    top = jnp.maximum(jnp.max(si, axis=0, keepdims=True), jnp.max(st, axis=0, keepdims=True))
    ei = jnp.exp(si - top)
    et = jnp.exp(st - top)
    total = jnp.sum(ei, axis=0, keepdims=True) + jnp.sum(et, axis=0, keepdims=True)
    o = dots(vi, ei.astype(jnp.bfloat16), 0, 0) + dots(vt, et.astype(jnp.bfloat16), 0, 0)
    return (o / total).T.astype(jnp.bfloat16), top + jnp.log(total)


def attend_kernel(hd, bq, img_ref, txt_ref, bias_ref, oi_ref, ot_ref, lse_ref):
    img_n, txt_n = img_ref.shape[0], txt_ref.shape[1]
    heads = img_ref.shape[1] // (3 * hd)
    bias = bias_ref[...]
    for h in range(heads):
        base = 3 * hd * h
        ki = img_ref[:, base + hd:base + 2 * hd]
        vi = img_ref[:, base + 2 * hd:base + 3 * hd]
        kt = txt_ref[0, :, base + hd:base + 2 * hd]
        vt = txt_ref[0, :, base + 2 * hd:base + 3 * hd]

        def block(q):
            q = q * jnp.bfloat16(0.125)
            si = dots(ki, q, 1, 1)
            st = dots(kt, q, 1, 1) + bias
            top = jnp.maximum(jnp.max(si, axis=0, keepdims=True), jnp.max(st, axis=0, keepdims=True))
            ei = jnp.exp(si - top)
            et = jnp.exp(st - top)
            total = jnp.sum(ei, axis=0, keepdims=True) + jnp.sum(et, axis=0, keepdims=True)
            o = dots(vi, ei.astype(jnp.bfloat16), 0, 0) + dots(vt, et.astype(jnp.bfloat16), 0, 0)
            return (o / total).T.astype(jnp.bfloat16), top + jnp.log(total)

        for i in range(img_n // bq):
            o, lse = block(img_ref[i * bq:(i + 1) * bq, base:base + hd])
            oi_ref[i * bq:(i + 1) * bq, h * hd:(h + 1) * hd] = o
            lse_ref[0, h:h + 1, i * bq:(i + 1) * bq] = lse
        o, lse = block(txt_ref[0, :, base:base + hd])
        ot_ref[0, :, h * hd:(h + 1) * hd] = o
        lse_ref[0, h:h + 1, img_n:img_n + txt_n] = lse

def attend(img, txt, bias, hd, bq=512):
    img_n, cols = img.shape
    parts, txt_n, _ = txt.shape
    pairs = cols // (6 * hd)
    per = pairs // parts
    return pl.pallas_call(
        functools.partial(attend_kernel, hd, bq),
        grid=(pairs,),
        in_specs=[
            pl.BlockSpec((img_n, 6 * hd), lambda i: (0, i)),
            pl.BlockSpec((1, txt_n, 6 * hd), lambda i: (i // per, 0, i % per)),
            pl.BlockSpec((txt_n, 1), lambda i: (0, 0)),
        ],
        out_specs=[
            pl.BlockSpec((img_n, 2 * hd), lambda i: (0, i)),
            pl.BlockSpec((1, txt_n, 2 * hd), lambda i: (i // per, 0, i % per)),
            pl.BlockSpec((1, 2, img_n + txt_n), lambda i: (i, 0, 0)),
        ],
        out_shape=[
            jax.ShapeDtypeStruct((img_n, pairs * 2 * hd), jnp.bfloat16),
            jax.ShapeDtypeStruct((parts, txt_n, per * 2 * hd), jnp.bfloat16),
            jax.ShapeDtypeStruct((pairs, 2, img_n + txt_n), jnp.float32),
        ],
        compiler_params=pltpu.CompilerParams(vmem_limit_bytes=48 * 1024 * 1024),
        name="attend",
    )(img, txt, bias)

def attend_back_kernel(hd, bq, img_ref, txt_ref, bias_ref, doi_ref, dot_ref, lse_ref, di_ref, dt_ref, acc_i, acc_t):
    img_n, txt_n = img_ref.shape[0], txt_ref.shape[1]
    heads = img_ref.shape[1] // (3 * hd)
    bias = bias_ref[...]
    for h in range(heads):
        base = 3 * hd * h
        ki = img_ref[:, base + hd:base + 2 * hd]
        vi = img_ref[:, base + 2 * hd:base + 3 * hd]
        kt = txt_ref[0, :, base + hd:base + 2 * hd]
        vt = txt_ref[0, :, base + 2 * hd:base + 3 * hd]

        def block(q, do, lse, first):
            q = q * jnp.bfloat16(0.125)
            pi = jnp.exp(dots(ki, q, 1, 1) - lse)
            pt = jnp.exp(dots(kt, q, 1, 1) + bias - lse)
            dwi = dots(vi, do, 1, 1)
            dwt = dots(vt, do, 1, 1)
            delta = jnp.sum(pi * dwi, axis=0, keepdims=True) + jnp.sum(pt * dwt, axis=0, keepdims=True)
            dsi = (pi * (dwi - delta)).astype(jnp.bfloat16)
            dst = (pt * (dwt - delta)).astype(jnp.bfloat16)
            dvi = dots(pi.astype(jnp.bfloat16), do, 1, 0)
            dvt = dots(pt.astype(jnp.bfloat16), do, 1, 0)
            dki = dots(dsi, q, 1, 0)
            dkt = dots(dst, q, 1, 0)
            if first:
                acc_i[0], acc_i[1], acc_t[0], acc_t[1] = dki, dvi, dkt, dvt
            else:
                acc_i[0] += dki
                acc_i[1] += dvi
                acc_t[0] += dkt
                acc_t[1] += dvt
            dq = dots(ki, dsi, 0, 0) + dots(kt, dst, 0, 0)
            return (dq.T * 0.125).astype(jnp.bfloat16)

        for i in range(img_n // bq):
            rows = slice(i * bq, (i + 1) * bq)
            di_ref[rows, base:base + hd] = block(
                img_ref[rows, base:base + hd], doi_ref[rows, h * hd:(h + 1) * hd], lse_ref[0, h:h + 1, rows], i == 0)
        grad = jnp.where(bias < 0, 0.0, dot_ref[0, :, h * hd:(h + 1) * hd].astype(jnp.float32)).astype(jnp.bfloat16)
        dt_ref[0, :, base:base + hd] = block(
            txt_ref[0, :, base:base + hd], grad, lse_ref[0, h:h + 1, img_n:img_n + txt_n], False)
        di_ref[:, base + hd:base + 2 * hd] = acc_i[0].astype(jnp.bfloat16)
        di_ref[:, base + 2 * hd:base + 3 * hd] = acc_i[1].astype(jnp.bfloat16)
        dt_ref[0, :, base + hd:base + 2 * hd] = acc_t[0].astype(jnp.bfloat16)
        dt_ref[0, :, base + 2 * hd:base + 3 * hd] = acc_t[1].astype(jnp.bfloat16)

def attend_back_far_kernel(hd, bq, n_z, fans, cols, img_ref, txt_ref, bias_ref, doi_ref, dot_ref, lse_ref, y_ref, *refs):
    img_a, img_b, rest = refs[:3], refs[3:6], refs[6:]
    di_ref, dt_ref, y_out, z_out, acc_i, acc_t, zmsg, y_send, y_recv, z_send, z_recv = rest
    step = pl.program_id(0)
    f, z, core, base, column = column_peers(n_z)
    ring = ZRing(f, z, n_z)
    there = [(base + z // 2, 2 * core + i) for i in range(2)]

    def is_here(i):
        return (z // 2 == core) & (2 * core + i == z)

    def y_keep(i):
        return pltpu.make_async_copy(y_ref.at[i], y_out.at[z % 2], y_recv.at[z % 2])

    def y_push(i):
        return push(y_ref.at[i], y_out.at[z % 2], y_send.at[i], y_recv.at[z % 2], there[i])

    def z_keep():
        return pltpu.make_async_copy(zmsg.at[z], z_out.at[z], z_recv.at[z])

    @pl.when(step == 0)
    def _():
        meet(column)
        offset = 0
        for part, sizes in ((img_a, fans), (img_b, cols)):
            for index in range(3):
                count = sizes[index + 2] // n_z
                for t in range(n_z):
                    zmsg[t, :, offset:offset + count] = part[index][:, t * count:(t + 1) * count].astype(jnp.bfloat16)
                offset += count
        ring.start(lambda to: zmsg.at[to], z_out, z_send, z_recv)
        z_keep().start()
        for i in range(2):
            @pl.when(is_here(i))
            def _():
                y_keep(i).start()

            @pl.when(jnp.logical_not(is_here(i)))
            def _():
                y_push(i).start()

    attend_back_kernel(hd, bq, img_ref, txt_ref, bias_ref, doi_ref, dot_ref, lse_ref, di_ref, dt_ref, acc_i, acc_t)

    @pl.when(step == pl.num_programs(0) - 1)
    def _():
        z_keep().wait()
        ring.wait(z_out, z_send, z_recv)
        ring.drain(lambda to: zmsg.at[to], z_out, z_send, z_recv)
        for i in range(2):
            @pl.when(is_here(i))
            def _():
                y_keep(i).wait()

            @pl.when(jnp.logical_not(is_here(i)))
            def _():
                push(y_out.at[i], y_out.at[i], y_send.at[i], y_recv.at[i], there[i]).wait_recv()
                y_push(i).wait_send()


def attend_back_far(img, txt, bias, doi, dot, lse, hd, y, img_a, img_b, n_z, fans, cols, cid, bq=512):
    img_n, wide_n = img.shape
    parts, txt_n, _ = txt.shape
    pairs = wide_n // (6 * hd)
    per = pairs // parts
    vmem, dma = pltpu.VMEM, pltpu.SemaphoreType.DMA
    bf16, shape = jnp.bfloat16, jax.ShapeDtypeStruct
    wide = pl.BlockSpec((img_n, 6 * hd), lambda i: (0, i))
    wide_t = pl.BlockSpec((1, txt_n, 6 * hd), lambda i: (i // per, 0, i % per))
    outside = pl.BlockSpec(memory_space=pl.ANY)
    sides = (*img_a, *img_b)
    lanes = (sum(fans[2:]) + sum(cols[2:])) // n_z
    return pl.pallas_call(
        functools.partial(attend_back_far_kernel, hd, bq, n_z, tuple(fans), tuple(cols)),
        grid=(pairs,),
        in_specs=[
            wide, wide_t,
            pl.BlockSpec((txt_n, 1), lambda i: (0, 0)),
            pl.BlockSpec((img_n, 2 * hd), lambda i: (0, i)),
            pl.BlockSpec((1, txt_n, 2 * hd), lambda i: (i // per, 0, i % per)),
            pl.BlockSpec((1, 2, img_n + txt_n), lambda i: (i, 0, 0)),
            outside,
        ] + [pl.BlockSpec(v.shape, lambda i: (0, 0)) for v in sides],
        out_specs=[wide, wide_t, outside, outside],
        out_shape=[shape(img.shape, bf16), shape(txt.shape, bf16), shape(y.shape, bf16), shape((n_z, RANK, lanes), bf16)],
        scratch_shapes=[vmem((2, img_n, hd), jnp.float32), vmem((2, txt_n, hd), jnp.float32), vmem((n_z, RANK, lanes), bf16),
                        dma((2,)), dma((2,)), dma((n_z,)), dma((n_z,))],
        compiler_params=pltpu.CompilerParams(collective_id=cid, has_side_effects=True, vmem_limit_bytes=56 * 1024 * 1024),
        name="attend_back",
    )(img, txt, bias, doi, dot, lse, y, *sides)


def attend_back(img, txt, bias, doi, dot, lse, hd, bq=512):
    img_n, cols = img.shape
    parts, txt_n, _ = txt.shape
    pairs = cols // (6 * hd)
    per = pairs // parts
    wide = pl.BlockSpec((img_n, 6 * hd), lambda i: (0, i))
    wide_t = pl.BlockSpec((1, txt_n, 6 * hd), lambda i: (i // per, 0, i % per))
    return pl.pallas_call(
        functools.partial(attend_back_kernel, hd, bq),
        grid=(pairs,),
        in_specs=[
            wide, wide_t,
            pl.BlockSpec((txt_n, 1), lambda i: (0, 0)),
            pl.BlockSpec((img_n, 2 * hd), lambda i: (0, i)),
            pl.BlockSpec((1, txt_n, 2 * hd), lambda i: (i // per, 0, i % per)),
            pl.BlockSpec((1, 2, img_n + txt_n), lambda i: (i, 0, 0)),
        ],
        out_specs=[wide, wide_t],
        out_shape=[jax.ShapeDtypeStruct(img.shape, jnp.bfloat16), jax.ShapeDtypeStruct(txt.shape, jnp.bfloat16)],
        scratch_shapes=[pltpu.VMEM((2, img_n, hd), jnp.float32), pltpu.VMEM((2, txt_n, hd), jnp.float32)],
        compiler_params=pltpu.CompilerParams(vmem_limit_bytes=48 * 1024 * 1024),
        name="attend_back",
    )(img, txt, bias, doi, dot, lse)

ROWS = 64


def mm(left, right):
    return dots(left, right, 1, 0)


def mm_t(left, right):
    return dots(left, right, 1, 1)


def t_mm(left, right):
    return dots(left, right, 0, 0)


def gelu_parts(u):
    scale = 0.7978845608028654
    square = u * u
    tanh = jnp.tanh(scale * (u + 0.044715 * u * square))
    half = 0.5 * (1.0 + tanh)
    slope = half + 0.5 * u * (1.0 - tanh * tanh) * (scale * (1.0 + 3 * 0.044715 * square))
    return u * half, slope


def norm_rows(v):
    center = v - jnp.mean(v, axis=-1, keepdims=True)
    inverse = lax.rsqrt(jnp.mean(center * center, axis=-1, keepdims=True) + 1e-06)
    return center * inverse, inverse


def column_peers(n_z):
    f, z = lax.axis_index("fsdp"), lax.axis_index("tp")
    core = f % 2
    base = f - core
    peers = [(f, (z + j) % n_z) for j in range(1, n_z)]
    peers += [(base + 1 - core, (z + j) % n_z) for j in range(n_z)]
    return f, z, core, base, peers


def meet(peers):
    barrier = pltpu.get_barrier_semaphore()
    for peer in peers:
        pl.semaphore_signal(barrier, inc=1, device_id=peer, device_id_type=MESH)
    pl.semaphore_wait(barrier, len(peers))


def push(src, dst, send, recv, peer):
    return pltpu.make_async_remote_copy(
        src_ref=src, dst_ref=dst, send_sem=send, recv_sem=recv, device_id=peer, device_id_type=MESH)


class ZRing:
    def __init__(self, f, z, n_z):
        self.f, self.z, self.n_z = f, z, n_z

    def start(self, source_of, buf, send, recv):
        for j in range(1, self.n_z):
            to = (self.z + j) % self.n_z
            push(source_of(to), buf.at[self.z], send.at[j], recv.at[self.z], (self.f, to)).start()

    def wait(self, buf, send, recv):
        for j in range(1, self.n_z):
            came = (self.z + j) % self.n_z
            push(buf.at[came], buf.at[came], send.at[j], recv.at[came], (self.f, came)).wait_recv()

    def drain(self, source_of, buf, send, recv):
        for j in range(1, self.n_z):
            to = (self.z + j) % self.n_z
            push(source_of(to), buf.at[self.z], send.at[j], recv.at[self.z], (self.f, to)).wait_send()


def text_tools(n_z, pad, width, f, z, lmask_ref, part_ref, mine_ref, out_buf, in_buf, rs_send, rs_recv, ag_send, ag_recv):
    ring = ZRing(f, z, n_z)
    bf16, f32 = jnp.bfloat16, jnp.float32

    def scatter(turn, main, rank_part):
        full = jnp.concatenate([main, rank_part], axis=1)
        full = full.reshape(n_z, pad, full.shape[1])
        part_ref[...] = full
        mine_ref[turn] = part_ref[z]
        out_buf[turn] = full.astype(bf16)
        ring.start(lambda to: out_buf.at[turn, to], in_buf.at[turn], rs_send.at[turn], rs_recv.at[turn])

    def collect(turn):
        ring.wait(in_buf.at[turn], rs_send.at[turn], rs_recv.at[turn])
        total = mine_ref[turn]
        for j in range(1, n_z):
            total = total + in_buf[turn, (z + j) % n_z].astype(f32)
        ring.drain(lambda to: out_buf.at[turn, to], in_buf.at[turn], rs_send.at[turn], rs_recv.at[turn])
        return total[:, :width], (total[:, width:] * lmask_ref[...]).astype(bf16)

    def spread(ref, *parts):
        offset = 0
        for part in parts:
            ref[z, :, offset:offset + part.shape[1]] = part
            offset += part.shape[1]
        ring.start(lambda to: ref.at[z], ref, ag_send, ag_recv)

    def spread_end(ref):
        ring.wait(ref, ag_send, ag_recv)
        ring.drain(lambda to: ref.at[z], ref, ag_send, ag_recv)

    def gathered(ref, start, count):
        return ref[:, :, start:start + count].reshape(n_z * pad, count)

    def own_lanes(ref, share):
        at = pl.ds(pl.multiple_of(z * share, 128), share)
        return ref[:, :, at].reshape(n_z * pad, share)

    return scatter, collect, spread, spread_end, gathered, own_lanes


def rows_of(mod_ref, own_ref):
    return lambda row: jnp.where(own_ref[...] > 0, mod_ref[row:row + 1, :], mod_ref[8 + row:9 + row, :])


def both_fwd_kernel(tiles, n_z, turns, o_ref, x_ref, g_ref, mod_ref, wo_ref, ao_ref, bo_ref, a1_ref, b1_ref, w1_ref, a2_ref, w2_ref, b2_ref,
                    ot_ref, xt_ref, tmod_ref, owner_ref, own_ref, lmask_ref, two_ref, tao_ref, tbo_ref,
                    a_out, x1_out, h2_out, u_out, y_out, to_out, t1_out, t2_out, gate_out,
                    tall_out, att_out, tx1_out, tbr_out,
                    m_acc, t2_acc, o_got, part_ref, mine_ref, out_buf, in_buf, ag_ref, o_send, o_recv, rs_send, rs_recv, ag_send, ag_recv):
    step = pl.program_id(0)
    f, z, core, base, column = column_peers(n_z)
    pad, width_t = xt_ref.shape
    f32, bf16 = jnp.float32, jnp.bfloat16
    scatter, collect, spread, spread_end, gathered, own_lanes = text_tools(
        n_z, pad, width_t, f, z, lmask_ref, part_ref, mine_ref, out_buf, in_buf, rs_send, rs_recv, ag_send, ag_recv)
    home = [(base + z // 2, 2 * core + i) for i in range(2)]

    def is_here(i):
        return (z // 2 == core) & (2 * core + i == z)

    def o_push(i):
        return push(ot_ref.at[i], o_got.at[z % 2], o_send.at[i], o_recv.at[z % 2], home[i])

    @pl.when(step == 0)
    def _():
        meet(column)
        for i in range(2):
            @pl.when(is_here(i))
            def _():
                copy = pltpu.make_async_copy(ot_ref.at[i], o_got.at[z % 2], o_recv.at[z % 2])
                copy.start()
                copy.wait()

            @pl.when(jnp.logical_not(is_here(i)))
            def _():
                o_push(i).start()

    rows = o_ref.shape[0]
    width = o_ref.shape[1]


    @pl.when(step == 0)
    def _():
        to = mm_t(o_ref[...], ao_ref[...]).astype(jnp.bfloat16)
        to_out[...] = to

        def cols(n, _):
            sl = pl.ds(pl.multiple_of(n * 256, 256), 256)
            a = mm_t(o_ref[...], wo_ref[sl, :]) + mm(to_out[...], bo_ref[:, sl])
            a_out[:, sl] = a.astype(jnp.bfloat16)
            x1_out[:, sl] = x_ref[:, sl].astype(jnp.float32) + mod_ref[2:3, sl] * a
            return 0

        lax.fori_loop(0, width // 256, cols, 0)

        def norm(r, _):
            sl = pl.ds(pl.multiple_of(r * ROWS, ROWS), ROWS)
            xh, _inv = norm_rows(x1_out[sl, :])
            h2_out[sl, :] = (xh * (1.0 + mod_ref[4:5, :]) + mod_ref[3:4, :]).astype(jnp.bfloat16)
            return 0

        lax.fori_loop(0, rows // ROWS, norm, 0)
        t1_out[...] = mm_t(h2_out[...], a1_ref[...]).astype(jnp.bfloat16)
        m_acc[...] = jnp.zeros_like(m_acc)
        t2_acc[...] = jnp.zeros_like(t2_acc)

    u = mm(h2_out[...], w1_ref[...]) + mm(t1_out[...], b1_ref[...])
    u_out[...] = u
    f = gelu_parts(u)[0].astype(jnp.bfloat16)
    m_acc[...] += mm_t(f, w2_ref[...])
    t2_acc[...] += mm_t(f, a2_ref[...])


    @pl.when(step == turns[0])
    def _():
        for i in range(2):
            @pl.when(jnp.logical_not(is_here(i)))
            def _():
                push(o_got.at[i], o_got.at[i], o_send.at[i], o_recv.at[i], home[i]).wait_recv()
                o_push(i).wait_send()
        owner = owner_ref[...]
        att = jnp.where(owner > 0, o_got[0].astype(f32), jnp.where(owner < 0, o_got[1].astype(f32), 0.0)).astype(bf16)
        att_out[...] = att
        scatter(0, mm_t(att, two_ref[...]), mm_t(att, tao_ref[...]))

    @pl.when(step == turns[1])
    def _():
        modulation = rows_of(tmod_ref, own_ref)
        branch, to_mine = collect(0)
        branch = branch + mm(to_mine, tbo_ref[...])
        tbr_out[...] = branch
        x1 = xt_ref[...].astype(f32) + modulation(2) * branch
        tx1_out[...] = x1
        hat, _inv = norm_rows(x1)
        spread(ag_ref, (hat * (1.0 + modulation(4)) + modulation(3)).astype(bf16), to_mine)

    @pl.when(step == tiles - 1)
    def _():
        spread_end(ag_ref)
        tall_out[...] = ag_ref[...]

    @pl.when(step == tiles - 1)
    def _():
        t2_out[...] = t2_acc[...].astype(jnp.bfloat16)
        gate_out[...] = jnp.zeros_like(gate_out)

        def last(r, _):
            sl = pl.ds(pl.multiple_of(r * ROWS, ROWS), ROWS)
            m = m_acc[sl, :] + mm(t2_out[sl, :], b2_ref[...])
            y_out[sl, :] = (x1_out[sl, :] + mod_ref[5:6, :] * m).astype(jnp.bfloat16)
            gm = g_ref[sl, :].astype(jnp.float32) * m
            gate_out[...] += sum(gm[8 * i:8 * i + 8, :] for i in range(ROWS // 8))
            return 0

        lax.fori_loop(0, rows // ROWS, last, 0)


def both_back_kernel(tiles, n_z, turns, g_ref, x1_ref, a_ref, h2_ref, o_ref, mod_ref, u_ref, w2_ref, a2_ref, b2_ref, w1_ref, a1_ref, b1_ref,
                     wo_ref, ao_ref, bo_ref, to_ref, t1_ref, t2_ref,
                     gt_ref, tx1_ref, tbr_ref, tmod_ref, own_ref, mask_ref, lmask_ref, tall_ref, att_ref, tdm_ref, two_ref, tw1_ref, tw2_ref,
                     tao_ref, tbo_ref, ta1_ref, tb1_ref, ta2_ref, tb2_ref,
                     dx1_out, do_out, sums_out, ga2_out, gb1_out, ga1_out, gb2_out, gao_out, gbo_out,
                     ty_out, tdx1_out, tdo_out, tsums_out, tgao_out, tgbo_out, tga1_out, tgb1_out, tga2_out, tgb2_out,
                     dm_ref, dt2_ref, dh_acc, dt1_acc, part_ref, mine_ref, out_buf, in_buf, tda_ref, tdo_buf, heads_buf,
                     do_send, do_recv, rs_send, rs_recv, ag_send, ag_recv, hd_send, hd_recv, hd_own):
    step = pl.program_id(0)
    f, z, core, base, column = column_peers(n_z)
    pad, width_t = gt_ref.shape
    rank = tao_ref.shape[0]
    share = tao_ref.shape[1]
    f32, bf16 = jnp.float32, jnp.bfloat16
    scatter, collect, spread, spread_end, gathered, own_lanes = text_tools(
        n_z, pad, width_t, f, z, lmask_ref, part_ref, mine_ref, out_buf, in_buf, rs_send, rs_recv, ag_send, ag_recv)
    home = [(base + z // 2, 2 * core + i) for i in range(2)]

    def is_here(i):
        return (z // 2 == core) & (2 * core + i == z)

    def do_push(s):
        return push(tdo_buf, tdo_out.at[z % 2], do_send.at[s], do_recv.at[z % 2], home[s])

    def collapse(place, values):
        for s in range(2):
            tsums_out[2 * place + s:2 * place + s + 1, :] = jnp.sum(
                jnp.where(own_ref[...] == (1.0 if s == 0 else -1.0), values, 0.0), axis=0, keepdims=True)

    @pl.when(step == 0)
    def _():
        meet(column)
        h2_all = gathered(tall_ref, 0, width_t)
        t1 = (mm_t(h2_all, ta1_ref[...]) * mask_ref[...]).astype(bf16)
        u = mm(h2_all, tw1_ref[...]) + mm(t1, tb1_ref[...])
        act, slope = gelu_parts(u)
        act = act.astype(bf16)
        dm_all = tdm_ref[...].reshape(n_z * pad, width_t)
        dt2 = (mm_t(dm_all, tb2_ref[...]) * mask_ref[...]).astype(bf16)
        du = ((mm(dm_all, tw2_ref[...]) + mm(dt2, ta2_ref[...])) * slope).astype(bf16)
        scatter(1, mm_t(du, tw1_ref[...]), mm_t(du, tb1_ref[...]))
        scatter(0, mm_t(act, tw2_ref[...]), mm_t(act, ta2_ref[...]))
        tga2_out[...] = t_mm(dt2, act)
        tgb1_out[...] = t_mm(t1, du)

    rows, width = g_ref.shape
    bf16 = jnp.bfloat16


    @pl.when(step == 0)
    def _():
        def start(r, _):
            sl = pl.ds(pl.multiple_of(r * ROWS, ROWS), ROWS)
            dm_ref[sl, :] = (mod_ref[5:6, :] * g_ref[sl, :].astype(jnp.float32)).astype(bf16)
            return 0

        lax.fori_loop(0, rows // ROWS, start, 0)
        dt2_ref[...] = mm_t(dm_ref[...], b2_ref[...]).astype(bf16)
        gb2_out[...] = t_mm(t2_ref[...], dm_ref[...])
        dh_acc[...] = jnp.zeros_like(dh_acc)
        dt1_acc[...] = jnp.zeros_like(dt1_acc)

    act, slope = gelu_parts(u_ref[...])
    df = mm(dm_ref[...], w2_ref[...]) + mm(dt2_ref[...], a2_ref[...])
    ga2_out[...] = t_mm(dt2_ref[...], act.astype(bf16))
    du = (df * slope).astype(bf16)
    gb1_out[...] = t_mm(t1_ref[...], du)
    dh_acc[...] += mm_t(du, w1_ref[...])
    dt1_acc[...] += mm_t(du, b1_ref[...])


    @pl.when(step == turns[0])
    def _():
        modulation = rows_of(tmod_ref, own_ref)
        dh, dt1_mine = collect(1)
        dh = dh + mm(dt1_mine, ta1_ref[...])
        hat, inverse = norm_rows(tx1_ref[...])
        dz = dh * (1.0 + modulation(4))
        dx1 = gt_ref[...].astype(f32) + inverse * (
            dz - jnp.mean(dz, axis=-1, keepdims=True) - hat * jnp.mean(dz * hat, axis=-1, keepdims=True))
        feed, t2_mine = collect(0)
        spread(tda_ref, (modulation(2) * dx1).astype(bf16), dt1_mine, t2_mine)
        tdx1_out[...] = dx1
        collapse(0, dx1 * tbr_ref[...])
        collapse(1, dh)
        collapse(2, dh * hat)
        feed = feed + mm(t2_mine, tb2_ref[...])
        ty_out[...] = (tx1_ref[...] + modulation(5) * feed).astype(bf16)
        collapse(3, gt_ref[...].astype(f32) * feed)

    @pl.when(step == turns[1])
    def _():
        spread_end(tda_ref)
        da_all = gathered(tda_ref, 0, width_t)
        dt1 = gathered(tda_ref, width_t, rank)
        t2 = gathered(tda_ref, width_t + rank, rank)
        dto = (mm_t(da_all, tbo_ref[...]) * mask_ref[...]).astype(bf16)
        tdo_buf[...] = (mm(da_all, two_ref[...]) + mm(dto, tao_ref[...])).astype(bf16)
        for s in range(2):
            @pl.when(is_here(s))
            def _():
                copy = pltpu.make_async_copy(tdo_buf, tdo_out.at[z % 2], do_recv.at[z % 2])
                copy.start()
                copy.wait()

            @pl.when(jnp.logical_not(is_here(s)))
            def _():
                do_push(s).start()
        tgao_out[...] = t_mm(dto, att_ref[...])
        tgbo_out[...] = t_mm(gathered(tall_ref, width_t, rank), own_lanes(tda_ref, share))
        tgb2_out[...] = t_mm(t2, own_lanes(tdm_ref, share))
        tga1_out[...] = t_mm(dt1, own_lanes(tall_ref, share))

    @pl.when(step == tiles - 1)
    def _():
        dt1 = dt1_acc[...].astype(bf16)
        dt2_ref[...] = dt1
        ga1_out[...] = t_mm(dt1, h2_ref[...])
        sums_out[...] = jnp.zeros_like(sums_out)

        def last(r, _):
            sl = pl.ds(pl.multiple_of(r * ROWS, ROWS), ROWS)
            dh = dh_acc[sl, :] + mm(dt2_ref[sl, :], a1_ref[...])
            xh, inverse = norm_rows(x1_ref[sl, :])
            dz = dh * (1.0 + mod_ref[4:5, :])
            dx1 = g_ref[sl, :].astype(jnp.float32) + inverse * (
                dz - jnp.mean(dz, axis=-1, keepdims=True) - xh * jnp.mean(dz * xh, axis=-1, keepdims=True))
            dx1_out[sl, :] = dx1
            dm_ref[sl, :] = (mod_ref[2:3, :] * dx1).astype(bf16)
            fold = lambda v: sum(v[8 * i:8 * i + 8, :] for i in range(ROWS // 8))
            sums_out[0:8, :] += fold(dx1 * a_ref[sl, :].astype(jnp.float32))
            sums_out[8:16, :] += fold(dh)
            sums_out[16:24, :] += fold(dh * xh)
            return 0

        lax.fori_loop(0, rows // ROWS, last, 0)
        dto = mm_t(dm_ref[...], bo_ref[...]).astype(bf16)
        dt2_ref[...] = dto
        gao_out[...] = t_mm(dto, o_ref[...])
        gbo_out[...] = t_mm(to_ref[...], dm_ref[...])

        per_half = width // 512

        def cols(n, _):
            sl = pl.ds(pl.multiple_of(n * 256, 256), 256)
            into = pl.ds(pl.multiple_of(n % per_half * 256, 256), 256)
            heads_buf[n // per_half, :, into] = (mm(dm_ref[...], wo_ref[:, sl]) + mm(dt2_ref[...], ao_ref[:, sl])).astype(bf16)
            return 0

        lax.fori_loop(0, width // 256, cols, 0)
        partner = base + 1 - core
        swap = push(heads_buf.at[1 - core], do_out.at[core], hd_send, hd_recv, (partner, z))
        swap.start()
        keep = pltpu.make_async_copy(heads_buf.at[core], do_out.at[core], hd_own)
        keep.start()
        keep.wait()
        swap.wait_send()
        push(heads_buf.at[0], do_out.at[1 - core], hd_send, hd_recv, (partner, z)).wait_recv()

    @pl.when(step == tiles - 1)
    def _():
        for i in range(2):
            @pl.when(jnp.logical_not(is_here(i)))
            def _():
                push(tdo_out.at[i], tdo_out.at[i], do_send.at[i], do_recv.at[i], home[i]).wait_recv()
                do_push(i).wait_send()


def both_fwd(o, x, g, mod, wo, pair_o, pair_1, w1, pair_2, w2, ot, xt, tmod, owner, own, lmask, two, tpair_o, n_z, cid, tn=512, turns=(2, 7)):
    rows, width = o.shape
    hidden = w1.shape[1]
    tiles = hidden // tn
    rank = pair_o[0].shape[0]
    once = lambda shape: pl.BlockSpec(shape, lambda n: (0,) * len(shape), pipeline_mode=pl.Buffered(1))
    whole = once
    tile = lambda height: pl.BlockSpec((height, tn), lambda n: (0, n))
    f32, bf16 = jnp.float32, jnp.bfloat16
    shape, vmem, dma = jax.ShapeDtypeStruct, pltpu.VMEM, pltpu.SemaphoreType.DMA
    act = (rows, width)
    pad = xt.shape[0]
    total, share = n_z * pad, two.shape[1]
    thick = tpair_o[0].shape[0]
    wide = width + thick
    texts = (xt, tmod, owner, own, lmask, two, *tpair_o)
    return pl.pallas_call(
        functools.partial(both_fwd_kernel, tiles, n_z, turns),
        grid=(tiles,),
        in_specs=[once(act), once(act), once(act), once(mod.shape), once((width, width)), once((rank, width)), once((rank, width)),
                  once((rank, width)), tile(rank), tile(width), tile(rank), tile(width), once((rank, width)),
                  pl.BlockSpec(memory_space=pl.ANY)] + [once(v.shape) for v in texts],
        out_specs=[whole(act), whole(act), whole(act), tile(rows), whole(act), whole((rows, rank)), whole((rows, rank)),
                   whole((rows, rank)), whole((8, width)), whole((n_z, pad, wide)), whole((total, share)), whole((pad, width)),
                   whole((pad, width))],
        out_shape=[shape(act, bf16), shape(act, f32), shape(act, bf16), shape((rows, hidden), f32), shape(act, bf16)]
        + [shape((rows, rank), bf16)] * 3
        + [shape((8, width), f32), shape((n_z, pad, wide), bf16), shape((total, share), bf16), shape((pad, width), f32),
           shape((pad, width), f32)],
        scratch_shapes=[vmem(act, f32), vmem((rows, rank), f32), vmem((2, total, share), bf16), vmem((n_z, pad, wide), f32), vmem((1, pad, wide), f32),
                        vmem((1, n_z, pad, wide), bf16), vmem((1, n_z, pad, wide), bf16), vmem((n_z, pad, wide), bf16),
                        dma((2,)), dma((2,)), dma((1, n_z)), dma((1, n_z)), dma((n_z,)), dma((n_z,))],
        compiler_params=pltpu.CompilerParams(collective_id=cid, has_side_effects=True, vmem_limit_bytes=60 * 1024 * 1024),
        name="block_forward",
    )(o, x, g, mod, wo, *pair_o, pair_1[0], pair_1[1], w1, pair_2[0], w2, pair_2[1], ot, *texts)


def both_back(g, x1, a, h2, o, mod, u, w2, pair_2, w1, pair_1, wo, pair_o, mids,
              gt, tx1, tbr, tmod, own, mask, lmask, tall, att, tdm, two, tw1, tw2, tpair_o, tpair_1, tpair_2, n_z, cid, tn=512, turns=(8, 11)):
    rows, width = o.shape
    hidden = w1.shape[1]
    tiles = hidden // tn
    rank = pair_o[0].shape[0]
    once = lambda shape: pl.BlockSpec(shape, lambda n: (0,) * len(shape), pipeline_mode=pl.Buffered(1))
    whole = once
    tile = lambda height: pl.BlockSpec((height, tn), lambda n: (0, n))
    f32, bf16 = jnp.float32, jnp.bfloat16
    shape, vmem, dma = jax.ShapeDtypeStruct, pltpu.VMEM, pltpu.SemaphoreType.DMA
    act = (rows, width)
    side = (rank, width)
    thin = (rows, rank)
    pad = gt.shape[0]
    total, share = n_z * pad, two.shape[1]
    thick = tpair_o[0].shape[0]
    t_hidden = tw1.shape[1]
    wide = width + thick
    texts = (gt, tx1, tbr, tmod, own, mask, lmask, tall, att, tdm, two, tw1, tw2, *tpair_o, *tpair_1, *tpair_2)
    return pl.pallas_call(
        functools.partial(both_back_kernel, tiles, n_z, turns),
        grid=(tiles,),
        in_specs=[once(act)] * 5 + [once(mod.shape), tile(rows), tile(width), tile(rank), once(side), tile(width), once(side), tile(rank),
                  once((width, width)), once(side), once(side)] + [once(thin)] * 3 + [once(v.shape) for v in texts],
        out_specs=[whole(act), pl.BlockSpec(memory_space=pl.ANY), whole((24, width)), tile(rank), tile(rank)] + [whole(side)] * 4
        + [whole((pad, width)), whole((pad, width)), pl.BlockSpec(memory_space=pl.ANY), whole((8, width)), whole((thick, share)),
           whole((thick, share)), whole((thick, share)), whole((thick, t_hidden)), whole((thick, t_hidden)), whole((thick, share))],
        out_shape=[shape(act, f32), shape((2, rows, width // 2), bf16), shape((24, width), f32)] + [shape((rank, hidden), f32)] * 2 + [shape(side, f32)] * 4
        + [shape((pad, width), bf16), shape((pad, width), f32), shape((2, total, share), bf16), shape((8, width), f32),
           shape((thick, share), f32), shape((thick, share), f32), shape((thick, share), f32), shape((thick, t_hidden), f32),
           shape((thick, t_hidden), f32), shape((thick, share), f32)],
        scratch_shapes=[vmem(act, bf16), vmem(thin, bf16), vmem(act, f32), vmem(thin, f32),
                        vmem((n_z, pad, wide), f32), vmem((2, pad, wide), f32), vmem((2, n_z, pad, wide), bf16), vmem((2, n_z, pad, wide), bf16),
                        vmem((n_z, pad, wide + thick), bf16), vmem((total, share), bf16), vmem((2, rows, width // 2), bf16),
                        dma((2,)), dma((2,)), dma((2, n_z)), dma((2, n_z)), dma((n_z,)), dma((n_z,)), dma, dma, dma],
        compiler_params=pltpu.CompilerParams(collective_id=cid, has_side_effects=True, vmem_limit_bytes=60 * 1024 * 1024),
        name="block_backward",
    )(g, x1, a, h2, o, mod, u, w2, pair_2[0], pair_2[1], w1, pair_1[0], pair_1[1], wo, *pair_o, *mids, *texts)


def flip_bits(chip, mask, nbits):
    other = 0
    for bit in range(nbits):
        have = (chip // (1 << bit)) % 2
        other = other + (1 - have if (mask >> bit) & 1 else have) * (1 << bit)
    return other


def tail_kernel(n_f, n_z, fans, cols, *refs):
    it = iter(refs)
    take = lambda count: [next(it) for _ in range(count)]
    dq_in, tdq_in, wq_ref = take(3)
    (x_ref, dx1_ref, h_ref, imod_ref, mid_ref, qa_ref, qb_ref, isum_ref, igate_ref, tx_ref, tdx1_ref, th_ref, tmodr_ref, owner_ref,
     own_ref, lmask_ref, tmid_ref, twq_ref, tqa_ref, tqb_ref, tsum_ref) = take(21)
    early_ref, = take(1)
    txt_a, txt_b = take(3), take(3)
    hot4_ref, hot2_ref, wmod_ref, bmod_ref, tmod_ref, cond_ref, smask_ref = take(7)
    grad_out, tgrad_out, cond_out, rank_out, shard_out = take(5)
    (dq_ref, wtile, dh_ref, dt_ref, grad_ref, gaq_ref, gbq_ref, tgot, part_ref, mine_ref, out_buf, in_buf, dt_ag, tgb_ref, dmod_ref,
     isums) = take(16)
    zmsg, zgot, dense, snd1, rcv1, snd2, rcv2, dgot, own_dm, all_dm, cpart, cgot, zsum, zall, dts = take(15)
    (g_send, g_recv, z_send, z_recv, c_send, c_recv, s_send, s_recv, d_send, d_recv, f_send, f_recv, p_send, p_recv,
     q_send, q_recv, t_send, t_recv, dq_send, dq_recv, dq_own, w_sem, h_send, h_recv, rs_send, rs_recv, ag_send, ag_recv) = take(28)
    f32, bf16 = jnp.float32, jnp.bfloat16
    f, z, core, base, column = column_peers(n_z)
    chip = f // 2
    chips = n_f // 2
    nbits = bits_of(chips)
    partner = base + 1 - core
    around = [((f + j) % n_f, z) for j in range(1, n_f)]
    others = [(flip_bits(chip, mask, nbits) * 2 + side, z) for mask in range(1, chips) for side in range(2)]
    meet(column + others)
    ring = ZRing(f, z, n_z)
    blk = shard_out.shape[0]
    hidden_rank = hot2_ref.shape[0]

    home = [(base + z // 2, 2 * core + i) for i in range(2)]

    def is_here(i):
        return (z // 2 == core) & (2 * core + i == z)

    swap = push(dq_in.at[1 - core], dq_ref.at[core], dq_send, dq_recv, (partner, z))
    swap.start()
    keep = pltpu.make_async_copy(dq_in.at[core], dq_ref.at[core], dq_own)
    keep.start()

    def t_push(i):
        return push(tdq_in.at[i], tgot.at[z % 2], h_send.at[i], h_recv.at[z % 2], home[i])

    for i in range(2):
        @pl.when(is_here(i))
        def _():
            copy = pltpu.make_async_copy(tdq_in.at[i], tgot.at[z % 2], h_recv.at[z % 2])
            copy.start()
            copy.wait()

        @pl.when(jnp.logical_not(is_here(i)))
        def _():
            t_push(i).start()

    pad, width = tx_ref.shape
    thick = tqa_ref.shape[0]
    scatter, collect, spread, spread_end, gathered, own_lanes = text_tools(
        n_z, pad, width, f, z, lmask_ref, part_ref, mine_ref, out_buf, in_buf, rs_send, rs_recv, ag_send, ag_recv)
    tn = wtile.shape[3]
    per_half = dq_ref.shape[2] // tn

    def tile_of(n):
        side = core if n < per_half else 1 - core
        return side, side * per_half + n % per_half

    def tile_load(n):
        at = pl.ds(pl.multiple_of(tile_of(n)[1] * tn, 128), tn)
        return pltpu.make_async_copy(wq_ref.at[:, :, at], wtile.at[n % 2], w_sem.at[n % 2])

    def tile_back(n):
        if n + 1 < 2 * per_half:
            tile_load(n + 1).start()
        tile_load(n).wait()
        side, number = tile_of(n)
        at = pl.ds(pl.multiple_of(number * tn, 128), tn)
        part = dq_ref[side, :, n % per_half * tn:(n % per_half + 1) * tn]
        main = mm_t(part, wtile[n % 2].reshape(width, tn))
        thin = mm_t(part, qb_ref[:, at])
        if n == 0:
            dh_ref[...] = main
            dt_ref[...] = thin
        else:
            dh_ref[...] += main
            dt_ref[...] += thin
        gbq_ref[:, at] = t_mm(mid_ref[...], part)

    tile_load(0).start()
    keep.wait()
    for n in range(per_half):
        tile_back(n)

    for i in range(2):
        @pl.when(jnp.logical_not(is_here(i)))
        def _():
            push(tgot.at[i], tgot.at[i], h_send.at[i], h_recv.at[i], home[i]).wait_recv()
            t_push(i).wait_send()
    owner = owner_ref[...]
    tdq = jnp.where(owner > 0, tgot[0].astype(f32), jnp.where(owner < 0, tgot[1].astype(f32), 0.0)).astype(bf16)
    scatter(0, mm_t(tdq, twq_ref[...]), mm_t(tdq, tqb_ref[...]))
    tgb_ref[...] = t_mm(tmid_ref[...], tdq)

    push(dq_in.at[1 - core], dq_ref.at[1 - core], dq_send, dq_recv, (partner, z)).wait_recv()
    for n in range(per_half, 2 * per_half):
        tile_back(n)
    dt_low = dt_ref[...].astype(bf16)
    gaq_ref[...] = t_mm(dt_low, h_ref[...])

    spans = {}
    offset = 0
    for part, count, name in ((gaq_ref, fans[1] // n_z, (0, 1)), (gbq_ref, cols[1] // n_z, (1, 1))):
        for t in range(n_z):
            zmsg[t, :, offset:offset + count] = part[:, t * count:(t + 1) * count].astype(bf16)
        spans[name] = (offset, count)
        offset += count
    ring.start(lambda to: zmsg.at[to], zgot, z_send, z_recv)
    zgot[z] = zmsg[z]
    offset = 0
    for side, sizes in ((0, fans), (1, cols)):
        for index in range(2, 5):
            spans[side, index] = (offset, sizes[index] // n_z)
            offset += sizes[index] // n_z

    isums[...] = jnp.zeros_like(isums)
    quarter = grad_ref.shape[1]
    dh_ref[...] += mm(dt_low, qa_ref[...])
    for i in range(2):
        def last(r, _):
            sl = pl.ds(pl.multiple_of(i * quarter + r * ROWS, ROWS), ROWS)
            dh = dh_ref[sl, :]
            xh, inverse = norm_rows(x_ref[sl, :].astype(f32))
            dz = dh * (1.0 + imod_ref[1:2, :])
            dx = dx1_ref[sl, :] + inverse * (
                dz - jnp.mean(dz, axis=-1, keepdims=True) - xh * jnp.mean(dz * xh, axis=-1, keepdims=True))
            grad_ref[i, pl.ds(pl.multiple_of(r * ROWS, ROWS), ROWS), :] = dx.astype(bf16)
            fold = lambda v: sum(v[8 * j:8 * j + 8, :] for j in range(ROWS // 8))
            isums[0:8, :] += fold(dh)
            isums[8:16, :] += fold(dh * xh)
            return 0

        lax.fori_loop(0, quarter // ROWS, last, 0)

    pick = rows_of(tmodr_ref, own_ref)
    tdh, tdt = collect(0)
    spread(dt_ag, tdt)
    tdh = tdh + mm(tdt, tqa_ref[...])
    hat, inverse = norm_rows(tx_ref[...].astype(f32))
    dz = tdh * (1.0 + pick(1))
    tgrad_out[...] = tdx1_ref[...] + inverse * (
        dz - jnp.mean(dz, axis=-1, keepdims=True) - hat * jnp.mean(dz * hat, axis=-1, keepdims=True))

    def total_of(v):
        return jnp.sum(v, axis=0, keepdims=True)

    rows_img = [total_of(isums[0:8, :]), total_of(isums[8:16, :])]
    rows_img += [total_of(isum_ref[8 * p:8 * p + 8, :]) for p in range(3)] + [total_of(igate_ref[...])]
    rows_txt = []
    for s in range(2):
        chosen = own_ref[...] == (1.0 if s == 0 else -1.0)
        rows_txt.append([total_of(jnp.where(chosen, tdh, 0.0)), total_of(jnp.where(chosen, tdh * hat, 0.0))]
                        + [tsum_ref[2 * p + s:2 * p + s + 1, :] for p in range(4)])
    dmod_ref[...] = jnp.zeros_like(dmod_ref)
    chunk = dmod_ref.shape[-1]
    per_row = width // chunk
    per_block = 6 * per_row // n_z
    for r, parts in enumerate([rows_img] + rows_txt):
        for q in range(6 * per_row):
            dmod_ref[q // per_block, r, q % per_block:q % per_block + 1, :] = (
                parts[q // per_row][:, q % per_row * chunk:(q % per_row + 1) * chunk])

    def dmod_copy(index, peer):
        return push(dmod_ref.at[peer[1]], dgot.at[core * n_z + z], d_send.at[index], d_recv.at[core * n_z + z], peer)

    for index, peer in enumerate(column):
        dmod_copy(index, peer).start()
    dgot[core * n_z + z] = dmod_ref[z]

    hot2, hot4 = hot2_ref[...], hot4_ref[...]
    starts = []
    offset = 0
    for stream in range(2):
        for index in range(5):
            starts.append((stream, index, offset, offset + fans[index] // n_z))
            offset += fans[index] // n_z + cols[index] // n_z

    def put_a(at, part, hot):
        dense[at:at + part.shape[1], :] = dots(part, hot, 0, 0)

    def put_b(at, part, hot):
        full = dots(hot, part, 0, 0)
        blocks = part.shape[1] // 128
        for j in range(blocks):
            dense[pl.ds(at + j, 128, stride=blocks), :] = full[:, j * 128:(j + 1) * 128]

    def put_image(index, ref):
        for side, put in ((0, put_a), (1, put_b)):
            begin, count = spans[side, index]
            put(starts[index][2 + side], ref[:, :, begin:begin + count].reshape(hot4.shape[0], count), hot4)

    for index in range(2, 5):
        put_image(index, early_ref)
        put_a(starts[5 + index][2], txt_a[index - 2][:hidden_rank, :].astype(bf16), hot2)
        put_b(starts[5 + index][3], txt_b[index - 2][:hidden_rank, :].astype(bf16), hot2)

    for index, peer in enumerate(column):
        place = peer[0] % 2 * n_z + peer[1]
        push(dgot.at[place], dgot.at[place], d_send.at[index], d_recv.at[place], peer).wait_recv()
    rows = []
    for slot in range(2):
        rows.append(dgot[2 * core + slot, 0] + dgot[n_z + 2 * core + slot, 0])
    for slot in range(2):
        total = dgot[core * n_z, 1 + slot]
        for t in range(1, n_z):
            total = total + dgot[core * n_z + t, 1 + slot]
        rows.append(total)
    own_dm[...] = jnp.zeros_like(own_dm)
    for r, total in enumerate(rows):
        for j in range(own_dm.shape[1] // chunk):
            own_dm[r:r + 1, j * chunk:(j + 1) * chunk] = total[j:j + 1, :].astype(bf16).astype(f32)
    for j in range(1, n_f):
        push(own_dm, all_dm.at[f], f_send.at[j], f_recv.at[f], around[j - 1]).start()
    all_dm[f] = own_dm[...]
    dm_low = own_dm[...].astype(bf16)
    tmod = [tmod_ref[s].astype(bf16) for s in range(2)]
    gb_mod = [t_mm(tmod[s], dm_low) for s in range(2)]
    rank_img = mm_t(dm_low, bmod_ref[0])
    rank_txt = mm_t(dm_low, bmod_ref[1])
    row = lax.broadcasted_iota(jnp.int32, rank_img.shape, 0)
    rank_part = jnp.where(row < 2, rank_img, rank_txt)

    spread_end(dt_ag)
    tga = t_mm(gathered(dt_ag, 0, thick), own_lanes(th_ref, cols[2] // n_z))
    for stream, index, at_a, at_b in starts:
        if index == 0:
            dense[at_a:at_b, :] = jnp.zeros((at_b - at_a, 128), f32)
            put_b(at_b, gb_mod[stream].astype(bf16), hot2)
        elif index == 1 and stream == 1:
            put_a(at_a, tga[:hidden_rank].astype(bf16), hot2)
            put_b(at_b, tgb_ref[:hidden_rank, :].astype(bf16), hot2)
    ring.wait(zgot, z_send, z_recv)
    put_image(1, zgot)

    for i in range(2):
        @pl.when(is_here(i))
        def _():
            pltpu.make_async_copy(grad_ref.at[i], grad_out.at[z % 2], g_recv.at[z % 2]).start()

        @pl.when(jnp.logical_not(is_here(i)))
        def _():
            push(grad_ref.at[i], grad_out.at[z % 2], g_send.at[i], g_recv.at[z % 2], home[i]).start()

    def block(number):
        return pl.ds(pl.multiple_of(number * blk, 16), blk)

    for p in range(chips):
        snd1[p] = dense[block(2 * p + 1 - core), :].astype(bf16)
        push(snd1.at[p], rcv1.at[p], c_send.at[p], c_recv.at[p], (partner, z)).start()

    for j in range(1, n_f):
        came = (f - j + n_f) % n_f
        push(own_dm, all_dm.at[came], f_send.at[j], f_recv.at[came], (came, z)).wait_recv()
    everyone = all_dm[...].reshape(n_f * 8, own_dm.shape[1]).astype(bf16)
    part = mm_t(everyone, wmod_ref[0]) + pltpu.roll(mm_t(everyone, wmod_ref[1]), n_f * 8 - 2, 0)
    k_local = part.shape[1]
    cpart[...] = jnp.zeros_like(cpart)
    cpart[:, :, :k_local] = part.reshape(n_f, 8, k_local)
    for j in range(1, n_f):
        to = (f + j) % n_f
        push(cpart.at[to], cgot.at[f], p_send.at[j], p_recv.at[f], (to, z)).start()
    cgot[f] = cpart[f]

    for p in range(chips):
        push(snd1.at[p], rcv1.at[p], c_send.at[p], c_recv.at[p], (partner, z)).wait_recv()

    def mine_of(p):
        return block(2 * p + core)

    for p in range(chips):
        dense[mine_of(p), :] += rcv1[p].astype(f32)

    half = blk // 2
    orders = [list(range(nbits)), list(range(nbits))[::-1]]

    def masks_at(side, turn):
        left = orders[side][turn:]
        return [sum(1 << b for i, b in enumerate(left) if (m >> i) & 1) for m in range(1 << len(left))]

    def rs_copy(side, turn, index):
        slot = turn * 2 + index
        peer = flip_bits(chip, 1 << orders[side][turn], nbits) * 2 + core
        return push(snd2.at[side, slot], rcv2.at[side, slot], s_send.at[side, slot], s_recv.at[side, slot], (peer, z))

    def half_of(number, side):
        return pl.ds(pl.multiple_of((2 * number + core) * blk + side * half, 16), half)

    def rs_start(turn):
        for side in range(2):
            bit = 1 << orders[side][turn]
            for index, mask in enumerate(masks_at(side, turn + 1)):
                number = flip_bits(chip, bit | mask, nbits)
                snd2[side, turn * 2 + index] = dense[half_of(number, side), :].astype(bf16)
                rs_copy(side, turn, index).start()

    def rs_end(turn):
        for side in range(2):
            for index, mask in enumerate(masks_at(side, turn + 1)):
                number = flip_bits(chip, mask, nbits)
                rs_copy(side, turn, index).wait_recv()
                dense[half_of(number, side), :] += rcv2[side, turn * 2 + index].astype(f32)

    rs_start(0)

    for j in range(1, n_f):
        came = (f - j + n_f) % n_f
        push(cpart.at[came], cgot.at[came], p_send.at[j], p_recv.at[came], (came, z)).wait_recv()
    zsum[:n_f] = cgot[...]
    zsum[n_f] = jnp.zeros(zsum.shape[1:], f32)
    zsum[n_f, :, :hidden_rank] = rank_part
    zall[z] = zsum[...]
    ring.start(lambda to: zsum, zall, q_send, q_recv)
    ring.wait(zall, q_send, q_recv)
    total = zall[0]
    for t in range(1, n_z):
        total = total + zall[t]
    cond_out[...] = total[:n_f]
    dt = (total[n_f][:, :hidden_rank] * smask_ref[...]).astype(bf16)
    rank_out[...] = dt.astype(f32)
    wide = mm(dt, hot2)
    dts[f] = wide
    for j in range(1, n_f):
        push(dts.at[f], dts.at[f], t_send.at[j], t_recv.at[f], around[j - 1]).start()

    rs_end(0)
    if nbits > 1:
        rs_start(1)
    for j in range(1, n_f):
        came = (f - j + n_f) % n_f
        push(dts.at[came], dts.at[came], t_send.at[j], t_recv.at[came], (came, z)).wait_recv()
    all_dt = dts[...].reshape(n_f * 8, 128)
    row = lax.broadcasted_iota(jnp.int32, all_dt.shape, 0) % 8
    act = cond_ref[...].reshape(n_f * 8, cond_ref.shape[-1]).astype(bf16)
    mod_a = [
        dots(act, jnp.where(row < 2, all_dt, 0.0).astype(bf16), 0, 0),
        dots(act, pltpu.roll(jnp.where((row >= 2) & (row < 4), all_dt, 0.0), n_f * 8 - 2, 0).astype(bf16), 0, 0),
    ]
    if nbits > 1:
        rs_end(1)
    shard_out[...] = dense[block(f), :]
    for stream in range(2):
        first = starts[5 * stream][2]
        own = jnp.where(f == first // blk, 1.0, 0.0)
        count = mod_a[stream].shape[0]
        shard_out[:count, :] += own * mod_a[stream]

    swap.wait_send()
    ring.drain(lambda to: zmsg.at[to], zgot, z_send, z_recv)
    ring.drain(lambda to: zsum, zall, q_send, q_recv)
    for index, peer in enumerate(column):
        dmod_copy(index, peer).wait_send()
    for j in range(1, n_f):
        to = (f + j) % n_f
        push(own_dm, all_dm.at[f], f_send.at[j], f_recv.at[f], (to, z)).wait_send()
        push(cpart.at[to], cgot.at[f], p_send.at[j], p_recv.at[f], (to, z)).wait_send()
        push(dts.at[f], dts.at[f], t_send.at[j], t_recv.at[f], (to, z)).wait_send()
    for p in range(chips):
        push(snd1.at[p], rcv1.at[p], c_send.at[p], c_recv.at[p], (partner, z)).wait_send()
    for turn in range(nbits):
        for side in range(2):
            for index in range(len(masks_at(side, turn + 1))):
                rs_copy(side, turn, index).wait_send()
    for i in range(2):
        @pl.when(is_here(i))
        def _():
            pltpu.make_async_copy(grad_ref.at[i], grad_out.at[z % 2], g_recv.at[z % 2]).wait()

        @pl.when(jnp.logical_not(is_here(i)))
        def _():
            push(grad_out.at[i], grad_out.at[i], g_send.at[i], g_recv.at[i], home[i]).wait_recv()
            push(grad_ref.at[i], grad_out.at[z % 2], g_send.at[i], g_recv.at[z % 2], home[i]).wait_send()


def tail(dq, tdq, wq, smalls, early, txt_a, txt_b, hot4, hot2, wmod, bmod, tmod, cond, smask, n_f, n_z, fans, cols, cid, tn=768):
    f32, bf16 = jnp.float32, jnp.bfloat16
    vmem, dma = pltpu.VMEM, pltpu.SemaphoreType.DMA
    shape = jax.ShapeDtypeStruct
    args = (dq, tdq, wq, *smalls, early, *txt_a, *txt_b, hot4, hot2, wmod, bmod, tmod, cond, smask)
    lanes = (fans[1] + cols[1]) // n_z
    rows = 2 * (sum(fans) + sum(cols)) // n_z
    blk = rows // n_f
    chips = n_f // 2
    cut = cols[0] // n_z
    rank = hot2.shape[0]
    _, img_rows, half = dq.shape
    _, k_local, _ = wq.shape
    width = cols[2]
    tx = smalls[9]
    thick = smalls[18].shape[0]
    pad = tx.shape[0]
    wide = width + thick
    inside, outside = pl.BlockSpec(memory_space=vmem), pl.BlockSpec(memory_space=pl.ANY)
    return pl.pallas_call(
        functools.partial(tail_kernel, n_f, n_z, tuple(fans), tuple(cols)),
        out_shape=[shape((2, img_rows // 2, width), bf16), shape((pad, width), f32), shape((n_f, 8, 256), f32), shape((8, rank), f32),
                   shape((blk, 128), f32)],
        in_specs=[outside] * 3 + [inside] * (len(args) - 3),
        out_specs=[outside] + [inside] * 4,
        scratch_shapes=[
            vmem((2, img_rows, half), bf16), vmem((2, n_f, k_local, tn), bf16), vmem((img_rows, width), f32), vmem((img_rows, RANK), f32),
            vmem((2, img_rows // 2, width), bf16), vmem((RANK, fans[1]), f32), vmem((RANK, cols[1]), f32), vmem(tdq.shape, bf16),
            vmem((n_z, pad, wide), f32), vmem((1, pad, wide), f32), vmem((1, n_z, pad, wide), bf16), vmem((1, n_z, pad, wide), bf16),
            vmem((n_z, pad, thick), bf16), vmem((thick, cols[1] // n_z), f32), vmem((n_z, 3, 8, width // n_z), f32), vmem((16, width), f32),
            vmem((n_z, RANK, lanes), bf16), vmem((n_z, RANK, lanes), bf16), vmem((rows, 128), f32),
            vmem((chips, blk, 128), bf16), vmem((chips, blk, 128), bf16),
            vmem((2, 3, blk // 2, 128), bf16), vmem((2, 3, blk // 2, 128), bf16),
            vmem((2 * n_z, 3, 8, width // n_z), f32), vmem((8, cut), f32), vmem((n_f, 8, cut), f32),
            vmem((n_f, 8, 256), f32), vmem((n_f, 8, 256), f32), vmem((n_f + 1, 8, 256), f32),
            vmem((n_z, n_f + 1, 8, 256), f32), vmem((n_f, 8, 128), f32),
            dma((2,)), dma((2,)), dma((n_z,)), dma((n_z,)), dma((chips,)), dma((chips,)), dma((2, 3)), dma((2, 3)),
            dma((2 * n_z,)), dma((2 * n_z,)), dma((n_f,)), dma((n_f,)), dma((n_f,)), dma((n_f,)), dma((n_z,)), dma((n_z,)),
            dma((n_f,)), dma((n_f,)), dma, dma, dma, dma((2,)), dma((2,)), dma((2,)), dma((1, n_z)), dma((1, n_z)), dma((n_z,)), dma((n_z,)),
        ],
        compiler_params=pltpu.CompilerParams(collective_id=cid, has_side_effects=True, vmem_limit_bytes=60 * 1024 * 1024),
        name="gradient_exchange",
    )(*args)

FULL = 4
PART = 4


def front_kernel(n_f, n_z, fans, cols, *refs):
    it = iter(refs)
    take = lambda count: [next(it) for _ in range(count)]
    ins = take(FULL + PART + 1)
    (x_ref, g_ref, picks_ref, hot2_ref, cblk_ref, clane_ref, c8_ref, smask_ref, wmod_ref, xt_ref, gt_ref, own_ref, tmask_ref, sign_ref) = take(14)
    outs = take(FULL + PART)
    x_out, g_out, imod_out, tmod_out = take(4)
    img_a, img_b, txt_a, txt_b = take(4), take(4), take(4), take(4)
    moda_out, modb_out, midm_out, cond_out, dm_out = take(5)
    ot_out, lse_out, bias_out, hot4_out = take(4)
    h_out, mid_out, heads_out, th_out, tmid_out, theads_out, att_out = take(7)
    (row_ref, fl_ref, img_msg, img_got, txt_msg, txt_got, cgot, mpart, mgot, own_mod, mod_got, wtile, wtxt, stage, tq_ref, sign_got, hot_got, img_buf, txt_buf, o_stage) = take(20)
    (z_send, z_recv, xy_send, xy_recv, core_send, core_recv, own_sem, x_send, x_recv, g_send, g_recv, c_send, c_recv, l_send,
     l_recv, m_send, m_recv, i_send, i_recv, t_send, t_recv, d_send, d_recv, a_send, a_recv, w_sem, tw_sem, h_send, h_recv,
     h_sem, q_send, q_recv, dm_send, dm_recv, s_send, s_recv, b_sem, o_send, o_recv, o_sem) = take(40)
    f32, bf16 = jnp.float32, jnp.bfloat16
    f, z, core, base, column = column_peers(n_z)
    chip = f // 2
    chips = n_f // 2
    nbits = bits_of(chips)
    partner = base + 1 - core
    others = [(flip_bits(chip, mask, nbits) * 2 + side, z) for mask in range(1, chips) for side in range(2)]
    meet(column + others)
    ring = ZRing(f, z, n_z)
    total = FULL + PART + 1
    adapters = total - 1
    blk = ins[adapters].shape[0]
    width = x_ref.shape[2]
    rank2 = hot2_ref.shape[0]

    def peer_of(mask):
        return flip_bits(chip, mask, nbits) * 2 + core

    def wide_of(m):
        return ins[m].shape[-1]

    def cuts(m):
        if m == adapters:
            return [(0, (0, blk // 2)), (1, (blk // 2, blk // 2))]
        parts = halves(wide_of(m))
        if m % FULL == 1:
            parts = [(0, parts[1][1]), (parts[1][1], parts[0][1])]
        return list(enumerate(parts))

    def place(m, who, zz, cut):
        off, w = cut
        if m == adapters:
            return row_ref.at[pl.ds(pl.multiple_of(who * blk + off, 16), w), :]
        if m < FULL:
            return outs[m].at[who, :, pl.ds(pl.multiple_of(zz * wide_of(m) + off, 128), w)]
        return outs[m].at[who, :, pl.ds(off, w)]

    def piece(m, cut):
        off, w = cut
        if m == adapters:
            return ins[m].at[pl.ds(off, w), :]
        return ins[m].at[:, pl.ds(off, w)]

    def whole_place(m, who, zz):
        return place(m, who, zz, (0, blk if m == adapters else wide_of(m)))

    def slot(m, zz):
        return zz if m < FULL else 0

    def order_of(half):
        order = list(range(nbits))
        return order if half == 0 else order[::-1]

    def xy_copy(m, zz, half, cut, mask, bit, own_piece=False):
        where = place(m, peer_of(mask), zz, cut)
        return push(piece(m, cut) if own_piece else where, where, xy_send.at[m, slot(m, zz), half, mask, bit],
                    xy_recv.at[m, slot(m, zz), half, mask | (1 << bit)], (peer_of(1 << bit), z))

    def xy_wait(m, zz, half, cut, mask):
        where = place(m, peer_of(mask), zz, cut)
        push(where, where, xy_send.at[m, slot(m, zz), half, 0, 0], xy_recv.at[m, slot(m, zz), half, mask], (partner, z)).wait_recv()

    def core_copy(m, zz, half, cut, mask, own_piece=False):
        where = place(m, peer_of(mask), zz, cut)
        return push(piece(m, cut) if own_piece else where, where, core_send.at[m, slot(m, zz), half, mask],
                    core_recv.at[m, slot(m, zz), half, mask], (partner, z))

    def core_wait(m, zz, half, cut, mask):
        where = place(m, peer_of(mask) - core + (1 - core), zz, cut)
        push(where, where, core_send.at[m, slot(m, zz), half, mask], core_recv.at[m, slot(m, zz), half, mask], (partner, z)).wait_recv()

    def own_copy(m):
        return pltpu.make_async_copy(ins[m], whole_place(m, f, z), own_sem.at[m])

    def z_copy(m, zz, up, own_piece=False):
        where = whole_place(m, f, zz)
        return push(ins[m] if own_piece else where, where, z_send.at[m, zz, up], z_recv.at[m, zz], (f, z + 1 if up else z - 1))

    def last_of(order, mask):
        return max([i for i, b in enumerate(order) if (mask >> b) & 1], default=-1)

    def masks_in_order(half):
        order = order_of(half)
        return sorted(range(1, 1 << nbits), key=lambda mask: [1 if (mask >> b) & 1 else 0 for b in reversed(order)])

    def launch(m, zz, own_piece=False):
        for half, cut in cuts(m):
            for bit in order_of(half):
                xy_copy(m, zz, half, cut, 0, bit, own_piece).start()
            core_copy(m, zz, half, cut, 0, own_piece).start()

    def launch_own(m):
        if m < FULL:
            @pl.when(z < n_z - 1)
            def _():
                z_copy(m, z, 1, True).start()

            @pl.when(z > 0)
            def _():
                z_copy(m, z, 0, True).start()
        launch(m, z, True)
        own_copy(m).start()

    def forward(m, zz):
        for half, cut in cuts(m):
            order = order_of(half)
            for mask in masks_in_order(half):
                if last_of(order, mask) < nbits - 1:
                    xy_wait(m, zz, half, cut, mask)
                    for b in order[last_of(order, mask) + 1:]:
                        xy_copy(m, zz, half, cut, mask, b).start()
                    core_copy(m, zz, half, cut, mask).start()

    def finish(m, zz):
        for half, cut in cuts(m):
            order = order_of(half)
            for mask in masks_in_order(half):
                if last_of(order, mask) == nbits - 1:
                    xy_wait(m, zz, half, cut, mask)
                    core_copy(m, zz, half, cut, mask).start()

    def settle(m, zz):
        for half, cut in cuts(m):
            for mask in range(1 << nbits):
                core_wait(m, zz, half, cut, mask)

    def drain(m, zz):
        for half, cut in cuts(m):
            order = order_of(half)
            for mask in range(1 << nbits):
                for b in order[last_of(order, mask) + 1:]:
                    xy_copy(m, zz, half, cut, mask, b).wait_send()
                core_copy(m, zz, half, cut, mask).wait_send()

    def at_distance(k, body):
        for sign in ((-1, 1) if k else (1,)):
            zz = z + sign * k

            @pl.when((zz >= 0) & (zz < n_z))
            def _():
                body(zz)

    def arrive(m, k):
        @pl.when(z - k >= 0)
        def _():
            zz = z - k
            z_copy(m, zz, 1).wait_recv()

            @pl.when(z < n_z - 1)
            def _():
                z_copy(m, zz, 1).start()

            launch(m, zz)

        @pl.when(z + k < n_z)
        def _():
            zz = z + k
            z_copy(m, zz, 0).wait_recv()

            @pl.when(z > 0)
            def _():
                z_copy(m, zz, 0).start()

            launch(m, zz)

    def every_z(m, body):
        if m < FULL:
            def step(zz, _):
                body(m, zz)
                return 0

            lax.fori_loop(0, n_z, step, 0)
        else:
            body(m, z)

    there = [(base + z // 2, 2 * core + s) for s in range(2)]

    def is_here(s):
        return (z // 2 == core) & (2 * core + s == z)

    def token_push(src, dst, send, recv, s):
        return push(src.at[s], dst.at[z % 2], send.at[s], recv.at[z % 2], there[s])

    def tokens_start(src, dst, send, recv):
        for s in range(2):
            @pl.when(is_here(s))
            def _():
                pltpu.make_async_copy(src.at[s], dst.at[z % 2], recv.at[z % 2]).start()

            @pl.when(jnp.logical_not(is_here(s)))
            def _():
                token_push(src, dst, send, recv, s).start()

    def tokens_wait(src, dst, send, recv):
        for i in range(2):
            @pl.when(is_here(i))
            def _():
                pltpu.make_async_copy(src.at[i], dst.at[z % 2], recv.at[z % 2]).wait()

            @pl.when(jnp.logical_not(is_here(i)))
            def _():
                push(dst.at[i], dst.at[i], send.at[i], recv.at[i], there[i]).wait_recv()

    def tokens_drain(src, dst, send, recv):
        for s in range(2):
            @pl.when(jnp.logical_not(is_here(s)))
            def _():
                token_push(src, dst, send, recv, s).wait_send()

    def around(src_of, dst, send, recv):
        return [push(src_of((f + j) % n_f), dst.at[f], send.at[j], recv.at[f], ((f + j) % n_f, z)) for j in range(1, n_f)]

    def around_wait(dst, send, recv):
        for j in range(1, n_f):
            came = (f - j + n_f) % n_f
            push(dst.at[came], dst.at[came], send.at[j], recv.at[came], (came, z)).wait_recv()

    cond_sends = around(lambda to: cblk_ref.at[to], cgot, c_send, c_recv)
    lane_sends = around(lambda to: clane_ref, cond_out, l_send, l_recv)
    mod_sends = around(lambda to: mpart.at[to], mgot, m_send, m_recv)

    sign_push = push(sign_ref, sign_got, s_send.at[0], s_recv.at[0], (partner, z))
    hot_push = push(hot2_ref, hot_got, s_send.at[1], s_recv.at[1], (partner, z))

    sign_push.start()
    hot_push.start()
    for copy in cond_sends + lane_sends:
        copy.start()
    launch_own(adapters)
    tokens_start(x_ref, x_out, x_send, x_recv)
    launch_own(FULL)
    launch_own(0)
    cgot[f] = cblk_ref[f]
    cond_out[f] = clane_ref[...]

    around_wait(cgot, c_send, c_recv)
    k_local = wmod_ref.shape[1]
    everyone = cgot[...].reshape(n_f * 8, cgot.shape[2])[:, :k_local].astype(bf16)
    mpart[...] = (mm(everyone, wmod_ref[0]) + pltpu.roll(mm(everyone, wmod_ref[1]), 2, 0)).reshape(mpart.shape)
    for copy in mod_sends:
        copy.start()
    mgot[f] = mpart[f]

    forward(adapters, z)
    forward(FULL, z)
    for k in range(1, n_z):
        arrive(0, k)
    forward(0, z)
    for m in (1, 2, 3):
        launch_own(m)
    for m in (FULL + 1, FULL + 2, FULL + 3):
        launch_own(m)
    at_distance(1, lambda zz: forward(0, zz))
    for m in (1, 2, 3):
        arrive(m, 1)
    for k in range(2, n_z):
        at_distance(k, lambda zz: forward(0, zz))

    finish(adapters, z)
    settle(adapters, z)
    own_copy(adapters).wait()
    hot2 = hot2_ref[...]
    starts = {}
    offset = 0
    for stream in range(2):
        for index in range(5):
            starts[stream, index] = (offset, offset + fans[index] // n_z)
            offset += fans[index] // n_z + cols[index] // n_z

    def pick_a(stream, index):
        at = starts[stream, index][0]
        return mm_t(hot2, row_ref[at:at + fans[index] // n_z, :]).astype(bf16)

    def pick_b(stream, index, s, put):
        at = starts[stream, index][1]
        count = cols[index] // n_z // NAD
        flat = row_ref[at:at + count, :].astype(f32) * picks_ref[s * NAD:s * NAD + 1, :]
        for k in range(1, NAD):
            begin = at + k * count
            flat = flat + row_ref[begin:begin + count, :].astype(f32) * picks_ref[s * NAD + k:s * NAD + k + 1, :]
        fl_ref[:count, :] = flat
        blocks = count // RANK
        for j in range(blocks):
            put(j * 128, fl_ref[pl.ds(j, RANK, stride=blocks), :].astype(bf16))

    spans_a, spans_b = [], []
    offset = 0
    for index in range(1, 5):
        count = fans[index] // n_z
        picked = pick_a(0, index)
        for s in range(2):
            img_msg[s, :, offset:offset + count] = picked[s * RANK:(s + 1) * RANK]
        spans_a.append((offset, count))
        offset += count
    for index in range(1, 5):
        count = cols[index] // n_z
        for s in range(2):
            def put(at, value, s=s, offset=offset):
                img_msg[s, :, offset + at:offset + at + 128] = value
            pick_b(0, index, s, put)
        spans_b.append((offset, count))
        offset += count

    def img_push(s, side):
        return push(img_msg.at[s], img_got.at[z], i_send.at[s, side], i_recv.at[z], (base + side, 2 * core + s))

    for s in range(2):
        for side in range(2):
            self_here = (side == core) & (2 * core + s == z)

            @pl.when(self_here)
            def _():
                img_got[z] = img_msg[s]

            @pl.when(jnp.logical_not(self_here))
            def _():
                img_push(s, side).start()

    share = width // n_z
    for place_at, (stream, index) in enumerate([(0, 0), (1, 0), (1, 1), (1, 3)]):
        txt_msg[:, place_at * share:(place_at + 1) * share] = pick_a(stream, index)
    for place_at, index in ((4, 2), (5, 4)):
        for s in range(2):
            def put(at, value, s=s, place_at=place_at):
                txt_msg[s * RANK:(s + 1) * RANK, place_at * share + at:place_at * share + at + 128] = value
            pick_b(1, index, s, put)
    txt_got[z] = txt_msg[...]
    ring.start(lambda to: txt_msg, txt_got, t_send, t_recv)
    for ref in txt_a + txt_b:
        ref[...] = jnp.zeros_like(ref)
    for index in (2, 4):
        txt_a[index - 1][:rank2, :] = pick_a(1, index)
    for ref, stream, index in ((txt_b[0], 1, 1), (txt_b[2], 1, 3), (modb_out.at[0], 0, 0), (modb_out.at[1], 1, 0)):
        for s in range(2):
            def put(at, value, ref=ref, s=s):
                ref[s * RANK:(s + 1) * RANK, at:at + 128] = value
            pick_b(stream, index, s, put)

    for k in (2, 3):
        for m in (1, 2, 3):
            arrive(m, k)
    for m in (1, 2, 3):
        forward(m, z)
    for m in (FULL + 1, FULL + 2, FULL + 3):
        forward(m, z)

    ring.wait(txt_got, t_send, t_recv)
    for t in range(n_z):
        lanes = slice(t * share, (t + 1) * share)
        got = lambda number: txt_got[t, :, number * share:(number + 1) * share]
        moda_out[0, :, lanes] = got(0)
        moda_out[1, :, lanes] = got(1)
        txt_a[0][:rank2, lanes] = got(2)
        txt_a[2][:rank2, lanes] = got(3)
        txt_b[1][:rank2, lanes] = got(4)
        txt_b[3][:rank2, lanes] = got(5)
    around_wait(mgot, m_send, m_recv)
    mod_sum = mgot[0]
    for j in range(1, n_f):
        mod_sum = mod_sum + mgot[j]
    c8 = c8_ref[...].astype(bf16)
    thin = mm_t(c8, moda_out[0])
    row = lax.broadcasted_iota(jnp.int32, thin.shape, 0)
    middle = (jnp.where(row < 2, thin, mm_t(c8, moda_out[1])) * smask_ref[...]).astype(bf16)
    low = jnp.where(row < 2, middle.astype(f32), 0.0)
    high = jnp.where((row >= 2) & (row < 4), middle.astype(f32), 0.0)
    midm_out[0] = low
    midm_out[1] = high
    own_mod[...] = mod_sum + mm(low.astype(bf16), modb_out[0]) + mm(high.astype(bf16), modb_out[1])

    def mod_push(index, peer):
        return push(own_mod, mod_got.at[core * n_z + z], d_send.at[index], d_recv.at[core * n_z + z], peer)

    for index, peer in enumerate(column):
        mod_push(index, peer).start()
    mod_got[core * n_z + z] = own_mod[...]

    for t in range(n_z):
        @pl.when(jnp.logical_not((z // 2 == core) & (t == z)))
        def _():
            push(img_got.at[t], img_got.at[t], i_send.at[0, 0], i_recv.at[t], (base + z // 2, t)).wait_recv()
    for t in range(n_z):
        for refs_of, spans in ((img_a, spans_a), (img_b, spans_b)):
            for ref, (begin, count) in zip(refs_of, spans):
                ref[:, t * count:(t + 1) * count] = img_got[t, :, begin:begin + count]

    for index, peer in enumerate(column):
        place_at = peer[0] % 2 * n_z + peer[1]
        push(mod_got.at[place_at], mod_got.at[place_at], d_send.at[index], d_recv.at[place_at], peer).wait_recv()
    step = width // 2
    per = own_mod.shape[1] // step
    imod_out[...] = jnp.zeros_like(imod_out)
    tmod_out[...] = jnp.zeros_like(tmod_out)
    for q in range(12):
        t, lanes = q // per, slice(q % per * step, (q % per + 1) * step)
        into = slice(q % 2 * step, (q % 2 + 1) * step)
        here = mod_got[z // 2 * n_z + t]
        imod_out[q // 2:q // 2 + 1, into] = jnp.where(z % 2 == 0, here[0:1, lanes], here[1:2, lanes])
        ours = mod_got[core * n_z + t]
        for s in range(2):
            tmod_out[8 * s + q // 2:8 * s + q // 2 + 1, into] = ours[2 + s:3 + s, lanes]

    own = own_ref[...]
    pick = lambda r: jnp.where(own > 0, tmod_out[r:r + 1, :], tmod_out[8 + r:9 + r, :])
    hat, _inv = norm_rows(xt_ref[...].astype(f32))
    th_out[z] = (hat * (1.0 + pick(1)) + pick(0)).astype(bf16)
    ring.start(lambda to: th_out.at[z], th_out, a_send, a_recv)
    dm_out[z] = (pick(5) * gt_ref[...].astype(f32)).astype(bf16)
    ring.start(lambda to: dm_out.at[z], dm_out, dm_send, dm_recv)
    tokens_wait(x_ref, x_out, x_send, x_recv)
    quarter = x_ref.shape[1]
    for i in range(2):
        def norm(r, _):
            sl = pl.ds(pl.multiple_of(r * ROWS, ROWS), ROWS)
            hat, _inv = norm_rows(x_out[i, sl, :].astype(f32))
            h_out[pl.ds(pl.multiple_of(i * quarter + r * ROWS, ROWS), ROWS), :] = (
                hat * (1.0 + imod_out[1:2, :]) + imod_out[0:1, :]).astype(bf16)
            return 0

        lax.fori_loop(0, quarter // ROWS, norm, 0)
    tokens_start(g_ref, g_out, g_send, g_recv)


    finish(FULL, z)
    settle(FULL, z)
    own_copy(FULL).wait()
    load = pltpu.make_async_copy(outs[FULL], wtxt, tw_sem)
    load.start()
    ring.wait(th_out, a_send, a_recv)
    pad = xt_ref.shape[0]
    h_txt = th_out[...].reshape(n_z * pad, width)
    tmid = (mm_t(h_txt, txt_a[0][...]) * tmask_ref[...]).astype(bf16)
    tmid_out[...] = tmid
    load.wait()
    tq_ref[...] = (mm(h_txt, wtxt[...].reshape(width, wtxt.shape[2])) + mm(tmid, txt_b[0][...])).astype(bf16)
    for s in range(2):
        @pl.when(is_here(s))
        def _():
            copy = pltpu.make_async_copy(tq_ref, theads_out.at[z % 2], q_recv.at[z % 2])
            copy.start()
            copy.wait()

        @pl.when(jnp.logical_not(is_here(s)))
        def _():
            push(tq_ref, theads_out.at[z % 2], q_send.at[s], q_recv.at[z % 2], there[s]).start()

    every_z(0, finish)
    every_z(0, settle)
    own_copy(0).wait()
    mid = mm_t(h_out[...], img_a[0][...]).astype(bf16)
    mid_out[...] = mid
    tn = wtile.shape[3]
    per_half = stage.shape[2] // tn

    def tile_of(n):
        side = 1 - core if n < per_half else core
        return side, side * per_half + n % per_half

    def tile_load(n):
        at = pl.ds(pl.multiple_of(tile_of(n)[1] * tn, 128), tn)
        return pltpu.make_async_copy(outs[0].at[:, :, at], wtile.at[n % 2], w_sem.at[n % 2])

    def heads_push():
        return push(stage.at[0], heads_out.at[core], h_send, h_recv, (partner, z))

    tile_load(0).start()
    for n in range(2 * per_half):
        if n + 1 < 2 * per_half:
            tile_load(n + 1).start()
        tile_load(n).wait()
        at = pl.ds(pl.multiple_of(tile_of(n)[1] * tn, 128), tn)
        lanes = slice(n % per_half * tn, (n % per_half + 1) * tn)
        stage[n // per_half, :, lanes] = (
            mm(h_out[...], wtile[n % 2].reshape(width, tn)) + mm(mid, img_b[0][:, at])).astype(bf16)
        if n == per_half - 1:
            heads_push().start()
    keep = pltpu.make_async_copy(stage.at[1], heads_out.at[core], h_sem)
    keep.start()

    for m in (1, 2, 3):
        at_distance(1, lambda zz: forward(m, zz))

    sign_push.wait_recv()
    chip_sign = jnp.where(z // 2 == core, sign_ref[...], sign_got[...])
    chip_sign = jnp.where(z % 2 == 0, chip_sign, -chip_sign)
    bias_out[...] = jnp.where(chip_sign > 0, 0.0, -1e30)
    hot_push.wait_recv()
    hot4_out[:rank2, :] = jnp.where(core == 0, hot2_ref[...].astype(f32), hot_got[...].astype(f32)).astype(bf16)
    hot4_out[rank2:, :] = jnp.where(core == 0, hot_got[...].astype(f32), hot2_ref[...].astype(f32)).astype(bf16)
    keep.wait()
    push(stage.at[0], heads_out.at[1 - core], h_send, h_recv, (partner, z)).wait_recv()
    for s in range(2):
        @pl.when(jnp.logical_not(is_here(s)))
        def _():
            push(theads_out.at[s], theads_out.at[s], q_send.at[s], q_recv.at[s], there[s]).wait_recv()
    pairs = heads_out.shape[2] // (6 * HD)
    per_part = pairs // 2

    def pair_loads(i):
        lanes = pl.ds(pl.multiple_of(i * (6 * HD), 128), 6 * HD)
        part = pl.ds(pl.multiple_of(i % per_part * (6 * HD), 128), 6 * HD)
        return [pltpu.make_async_copy(heads_out.at[:, :, lanes], img_buf.at[i % 2], b_sem.at[i % 2, 0]),
                pltpu.make_async_copy(theads_out.at[i // per_part, :, part], txt_buf.at[i % 2], b_sem.at[i % 2, 1])]

    def pair_lanes(i):
        return pl.ds(pl.multiple_of((core * pairs + i) * (2 * HD), 128), 2 * HD)

    def o_keep(i):
        return pltpu.make_async_copy(o_stage.at[i, core], att_out.at[:, pair_lanes(i)], o_sem.at[i])

    def o_push(i):
        return push(o_stage.at[i, 1 - core], att_out.at[:, pair_lanes(i)], o_send.at[i], o_recv.at[i], (partner, z))

    for copy in pair_loads(0):
        copy.start()
    tokens = img_buf.shape[1] * img_buf.shape[2]

    def pair_step(i, _):
        at = i % 2

        @pl.when(i + 1 < pairs)
        def _():
            for copy in pair_loads(i + 1):
                copy.start()

        for copy in pair_loads(i):
            copy.wait()
        bias = bias_out[:, 0:1]
        for h in range(2):
            low = 3 * HD * h
            ki = img_buf[at, :, :, low + HD:low + 2 * HD].reshape(tokens, HD)
            vi = img_buf[at, :, :, low + 2 * HD:low + 3 * HD].reshape(tokens, HD)
            kt = txt_buf[at, :, low + HD:low + 2 * HD]
            vt = txt_buf[at, :, low + 2 * HD:low + 3 * HD]
            for b in range(3):
                q = img_buf[at, b, :, low:low + HD] if b < 2 else txt_buf[at, :, low:low + HD]
                o, lse = attend_block(q, ki, vi, kt, vt, bias)
                rows = img_buf.shape[2]
                if b < 2:
                    o_stage[i, b, :, h * HD:(h + 1) * HD] = o
                    lse_out[i, h:h + 1, b * rows:(b + 1) * rows] = lse
                else:
                    ot_stage = o
                    lse_out[i, h:h + 1, tokens:tokens + q.shape[0]] = lse
            if h == 0:
                first = ot_stage
        both = jnp.concatenate([first, ot_stage], axis=1)
        ot_out[i // per_part, :, pl.ds(pl.multiple_of(i % per_part * (2 * HD), 128), 2 * HD)] = both
        o_keep(i).start()
        o_push(i).start()
        return 0

    for m in (1, 2, 3):
        at_distance(2, lambda zz: forward(m, zz))
    lax.fori_loop(0, pairs // 2, pair_step, 0)
    for m in (1, 2, 3):
        at_distance(n_z - 1, lambda zz: forward(m, zz))
    lax.fori_loop(pairs // 2, pairs, pair_step, 0)

    for m in range(total - 1):
        if m not in (0, FULL):
            every_z(m, finish)
    for m in range(total - 1):
        if m not in (0, FULL):
            every_z(m, settle)
            own_copy(m).wait()
    for m in range(total):
        every_z(m, drain)
        if m < FULL:
            def sent(zz, _):
                @pl.when((zz <= z) & (z < n_z - 1))
                def _():
                    z_copy(m, zz, 1).wait_send()

                @pl.when((zz >= z) & (z > 0))
                def _():
                    z_copy(m, zz, 0).wait_send()

                return 0

            lax.fori_loop(0, n_z, sent, 0)
    for copy in cond_sends + lane_sends + mod_sends:
        copy.wait_send()
    around_wait(cond_out, l_send, l_recv)
    ring.drain(lambda to: txt_msg, txt_got, t_send, t_recv)
    ring.drain(lambda to: th_out.at[z], th_out, a_send, a_recv)
    ring.wait(dm_out, dm_send, dm_recv)
    ring.drain(lambda to: dm_out.at[z], dm_out, dm_send, dm_recv)
    for index, peer in enumerate(column):
        mod_push(index, peer).wait_send()
    for s in range(2):
        for side in range(2):
            @pl.when(jnp.logical_not((side == core) & (2 * core + s == z)))
            def _():
                img_push(s, side).wait_send()
    tokens_wait(g_ref, g_out, g_send, g_recv)
    tokens_drain(x_ref, x_out, x_send, x_recv)
    tokens_drain(g_ref, g_out, g_send, g_recv)
    heads_push().wait_send()
    sign_push.wait_send()
    hot_push.wait_send()

    def o_done(i, _):
        o_keep(i).wait()
        o_push(i).wait_send()
        other = pl.ds(pl.multiple_of(((1 - core) * pairs + i) * (2 * HD), 128), 2 * HD)
        push(o_stage.at[i, 0], att_out.at[:, other], o_send.at[i], o_recv.at[i], (partner, z)).wait_recv()
        return 0

    lax.fori_loop(0, pairs, o_done, 0)
    for s in range(2):
        @pl.when(jnp.logical_not(is_here(s)))
        def _():
            push(tq_ref, theads_out.at[z % 2], q_send.at[s], q_recv.at[z % 2], there[s]).wait_send()


def front(full, part, adapter_rows, x, g, picks, hot2, cond, wmod, x_txt, g_txt, own, tmask, smask, sign_rows, n_f, n_z, fans, cols, cid):
    f32, bf16 = jnp.float32, jnp.bfloat16
    vmem, dma = pltpu.VMEM, pltpu.SemaphoreType.DMA
    shape = jax.ShapeDtypeStruct
    slots, width = cond.shape
    k_local = wmod.shape[1]
    z = lax.axis_index("tp")
    blocks = jnp.pad(jnp.swapaxes(cond.reshape(slots, n_f, k_local), 0, 1), ((0, 0), (0, 6), (0, 256 - k_local)))
    cond8 = jnp.concatenate([cond, cond, jnp.zeros((4, width), f32)])
    lane = jnp.pad(lax.dynamic_slice_in_dim(cond, z * (width // n_z), width // n_z, 1), ((0, 6), (0, 0)))
    chosen = (picks[:, None] == jnp.arange(NAD)[None, :]).astype(f32).reshape(-1, 1)
    smalls = (jnp.broadcast_to(chosen, (slots * NAD, 128)), hot2, blocks, lane, cond8, smask, wmod, x_txt, g_txt, own, tmask, sign_rows)
    args = (*full, *part, adapter_rows, x, g, *smalls)
    any_spec, in_vmem = pl.BlockSpec(memory_space=pl.ANY), pl.BlockSpec(memory_space=vmem)
    rows = 2 * (sum(fans) + sum(cols)) // n_z
    chips = n_f // 2
    nbits = bits_of(chips)
    total = len(full) + len(part) + 1
    pad = x_txt.shape[0]
    img_rows = 2 * x.shape[1]
    cut = cols[0] // n_z
    qkv_part = cols[1] // n_z
    thick = tmask.shape[1]
    rank2 = hot2.shape[0]
    own_a = [fans[1], fans[2] // n_z, fans[3], fans[4] // n_z]
    own_b = [cols[1] // n_z, cols[2], cols[3] // n_z, cols[4]]
    lanes = (sum(fans[1:]) + sum(cols[1:])) // n_z
    share = width // n_z
    outs = [shape((n_f,) + a.shape[:-1] + (a.shape[-1] * (n_z if i < len(full) else 1),), a.dtype) for i, a in enumerate(full + part)]
    in_hbm = len(outs)
    outs += [shape(x.shape, bf16), shape(g.shape, bf16), shape((8, width), f32), shape((16, width), f32)]
    outs += [shape((RANK, n), bf16) for n in fans[1:]] + [shape((RANK, n), bf16) for n in cols[1:]]
    outs += [shape((thick, n), bf16) for n in own_a] + [shape((thick, n), bf16) for n in own_b]
    outs += [shape((2, rank2, width), bf16), shape((2, rank2, cut), bf16), shape((2, 8, rank2), f32), shape((n_f, 8, share), f32), shape((n_z, pad, width), bf16)]
    heads_half = cols[1] // (6 * HD)
    pairs = heads_half // 2
    outs += [shape((2, n_z * pad, width // n_z), bf16), shape((pairs, 2, 2 * img_rows + n_z * pad), f32), shape(sign_rows.shape, f32),
             shape((2 * rank2, NAD * RANK), bf16)]
    outs += [shape((img_rows, width), bf16), shape((img_rows, RANK), bf16), shape((2, img_rows, cols[1] // 2), bf16),
             shape((n_z, pad, width), bf16), shape((n_z * pad, thick), bf16), shape((2, n_z * pad, qkv_part), bf16), shape((img_rows, width), bf16)]
    specs = [any_spec] * in_hbm + [in_vmem, any_spec] + [in_vmem] * (len(outs) - in_hbm - 2)
    for place in (1, 2, 5):
        specs[len(outs) - place] = any_spec
    return pl.pallas_call(
        functools.partial(front_kernel, n_f, n_z, tuple(fans), tuple(cols)),
        out_shape=outs,
        in_specs=[any_spec] * (total + 2) + [in_vmem] * len(smalls),
        out_specs=specs,
        scratch_shapes=[
            vmem((rows, 128), bf16), vmem((cut // NAD, 128), f32), vmem((2, RANK, lanes), bf16), vmem((n_z, RANK, lanes), bf16),
            vmem((rank2, 6 * share), bf16), vmem((n_z, rank2, 6 * share), bf16), vmem((n_f, 8, 256), f32),
            vmem((n_f, 8, cut), f32), vmem((n_f, 8, cut), f32), vmem((8, cut), f32), vmem((2 * n_z, 8, cut), f32),
            vmem((2, n_f, k_local, 768), bf16), vmem((n_f, k_local, qkv_part), bf16), vmem((2, img_rows, cols[1] // 2), bf16),
            vmem((n_z * pad, qkv_part), bf16), vmem(sign_rows.shape, f32), vmem((rank2, NAD * RANK), bf16),
            vmem((2, 2, img_rows, 6 * HD), bf16), vmem((2, n_z * pad, 6 * HD), bf16), vmem((pairs, 2, img_rows, 2 * HD), bf16),
            dma((total, n_z, 2)), dma((total, n_z)), dma((total, n_z, 2, chips, nbits)), dma((total, n_z, 2, chips)),
            dma((total, n_z, 2, chips)), dma((total, n_z, 2, chips)), dma((total,)),
            dma((2,)), dma((2,)), dma((2,)), dma((2,)), dma((n_f,)), dma((n_f,)), dma((n_f,)), dma((n_f,)), dma((n_f,)), dma((n_f,)),
            dma((2, 2)), dma((n_z,)), dma((n_z,)), dma((n_z,)), dma((2 * n_z,)), dma((2 * n_z,)), dma((n_z,)), dma((n_z,)),
            dma((2,)), dma, dma, dma, dma, dma((2,)), dma((2,)), dma((n_z,)), dma((n_z,)),
            dma((2,)), dma((2,)), dma((2, 2)), dma((pairs,)), dma((pairs,)), dma((pairs,)),
        ],
        compiler_params=pltpu.CompilerParams(collective_id=cid, has_side_effects=True, vmem_limit_bytes=58 * 1024 * 1024),
        name="front",
    )(*args)

HD = 64
FF = 6144
NAD = 8
RANK = 16
EPS = 1e-06
HIGH = lax.Precision.HIGHEST
F32 = jnp.float32
BF16 = jnp.bfloat16
BOTH = ("fsdp", "tp")


def matmul(left, right):
    return jnp.dot(left, right, preferred_element_type=F32)


def exact(left, right):
    return jnp.dot(left, right, precision=HIGH, preferred_element_type=F32)


def inner_left(left, right):
    return lax.dot_general(left, right, (((0,), (0,)), ((), ())), preferred_element_type=F32)


def inner_right(left, right):
    return lax.dot_general(
        left, right, (((left.ndim - 1,), (right.ndim - 1,)), ((), ())), preferred_element_type=F32
    )


def layer_norm(values):
    center = values - jnp.mean(values, axis=-1, keepdims=True)
    inverse = lax.rsqrt(jnp.mean(center * center, axis=-1, keepdims=True) + EPS)
    return (center * inverse, inverse)


def norm_back(grad_normed, normed, inverse, scale):
    grad_hat = grad_normed * (1.0 + scale)
    return inverse * (
        grad_hat
        - jnp.mean(grad_hat, axis=-1, keepdims=True)
        - normed * jnp.mean(grad_hat * normed, axis=-1, keepdims=True)
    )


def gelu(value):
    return jax.nn.gelu(value, approximate=True)


def gelu_back(value, grad):
    return jax.vjp(gelu, value)[1](grad)[0]


def shards(
    image_tokens,
    text_tokens,
    conditioning,
    text_lengths,
    adapter_index,
    adapters,
    mod_weight,
    qkv_weight,
    out_weight,
    fc1_weight,
    fc2_weight,
    image_cot,
    text_cot,
):
    n_f, n_z = lax.axis_size("fsdp"), lax.axis_size("tp")
    f, z = lax.axis_index("fsdp"), lax.axis_index("tp")
    core = f % 2
    slots, quarter, width = image_tokens.shape
    txt_local = text_tokens.shape[0]
    txt_group = txt_local * n_z
    img_half = 2 * quarter
    img_n = 2 * img_half
    cols = [6 * width, 3 * width, width, FF, width]
    fans = [width, width, width, width, FF]

    def round_pairs(r):
        pairs = []
        for fa in range(n_f):
            for t in range(n_z):
                there = (fa // 2 * 2 + t // 2) * n_z + 2 * (fa % 2) + (r ^ (t % 2))
                pairs.append((fa * n_z + t, there))
        return pairs

    low_bit = z % 2

    def pick(stack, bit):
        return lax.dynamic_index_in_dim(stack, bit, 0, keepdims=False)

    def flip(r):
        return low_bit if r == 0 else 1 - low_bit

    def to_chip(parts):
        got = [lax.ppermute(parts[r], BOTH, round_pairs(r)) for r in range(2)]
        return jnp.where(low_bit == 0, got[0], got[1]), jnp.where(low_bit == 0, got[1], got[0])

    def from_chip(pieces):
        got = []
        for r in range(2):
            mine = jnp.where(flip(r) == 0, pieces[0], pieces[1])
            got.append(lax.ppermute(mine, BOTH, [(b, a) for a, b in round_pairs(r)]))
        return jnp.where(low_bit == 0, got[0], got[1]), jnp.where(low_bit == 0, got[1], got[0])

    def reshard(values):
        return jnp.concatenate(to_chip([pick(values, flip(r)) for r in range(2)]), axis=0)

    def unshard(values):
        return jnp.stack(from_chip([values[:quarter], values[quarter:]]))

    def swap_core(values):
        return lax.ppermute(values, "fsdp", [(i, i ^ 1) for i in range(n_f)])

    def by_core(mine, other, axis):
        first = jnp.where(core == 0, mine, other)
        second = jnp.where(core == 0, other, mine)
        return jnp.concatenate([first, second], axis=axis)

    def z_swap(values, step):
        return lax.ppermute(values, "tp", [(i, i ^ step) for i in range(n_z)])

    def z_order(pieces):
        stack = jnp.stack(pieces)
        return [pick(stack, z ^ a) for a in range(n_z)]

    def z_gather(values):
        return z_order([values] + [z_swap(values, j) for j in range(1, n_z)])

    def z_exchange(blocks):
        return z_order([pick(blocks, z ^ j) if j == 0 else z_swap(pick(blocks, z ^ j), j) for j in range(n_z)])

    def z_scatter(values):
        count = values.shape[0] // n_z
        mine = lax.dynamic_slice_in_dim(values, z * count, count, 0)
        for j in range(1, n_z):
            part = lax.dynamic_slice_in_dim(values, (z ^ j) * count, count, 0)
            mine = mine + z_swap(part.astype(BF16), j).astype(F32)
        return mine

    def to_heads(values):
        half = values.shape[1] // 2
        low, high = values[:, :half], values[:, half:]
        mine = jnp.where(core == 0, low, high)
        return by_core(mine, swap_core(jnp.where(core == 0, high, low)), 0)

    def to_tokens(values):
        low, high = values[:img_half], values[img_half:]
        mine = jnp.where(core == 0, low, high)
        return by_core(mine, swap_core(jnp.where(core == 0, high, low)), 1)

    out_t = jnp.swapaxes(out_weight, 1, 2)
    fc2_t = jnp.swapaxes(fc2_weight, 1, 2)
    local = [qkv_weight, out_t, fc1_weight, fc2_t]
    adapter_rows = lax.optimization_barrier(adapters.reshape(-1, 128)).astype(BF16)
    txt_pad = (txt_local + 15) // 16 * 16

    def padded(values):
        return jnp.pad(values, ((0, txt_pad - txt_local), (0, 0)))

    x_txt_low, g_txt_low = padded(text_tokens), padded(text_cot)
    x_txt = x_txt_low.astype(F32)

    seg_ends = jnp.cumsum(text_lengths[0])
    slot_ids = jnp.arange(slots)

    def owner_of(position):
        segment = jnp.sum((position[:, None] >= seg_ends[None, :]).astype(jnp.int32), axis=1)
        return (segment[:, None] == slot_ids[None, :]).astype(F32)

    def real(owner):
        place = jnp.arange(owner.shape[0]) % txt_pad
        return jnp.where((place < txt_local)[:, None], owner, 0.0)

    def position(rows):
        return rows // txt_pad * txt_local + rows % txt_pad

    txt_rows = jnp.arange(n_z * txt_pad)
    owner_group = real(owner_of(position(txt_rows)))
    owner_local = real(owner_of(z * txt_local + jnp.arange(txt_pad)))
    txt_mask = jnp.repeat(owner_group, RANK, axis=1)
    txt_mask_local = jnp.repeat(owner_local, RANK, axis=1)
    rank_cols = slots * RANK
    seq_mask = jnp.repeat(jnp.eye(slots, dtype=F32), RANK, axis=1)

    def by_group(mine, other):
        return by_core(mine, other, 0)

    def stretch(stream, index):
        if stream == 0:
            return img_mod[:, index * width : (index + 1) * width]
        return exact(owner_local, txt_mods[:, index * width : (index + 1) * width])

    def collapse(stream, values):
        if stream == 0:
            return jnp.sum(values, axis=0, keepdims=True)
        return exact(owner_local.T, values)

    def share(values):
        return jnp.concatenate(z_gather(values), axis=0)

    def give(values, rank_part):
        got = z_scatter(jnp.concatenate([values, rank_part], axis=1))
        return got[:, :width], (got[:, width:] * txt_mask_local).astype(BF16)

    def lanes(values):
        count = values.shape[1] // n_z
        return lax.dynamic_slice_in_dim(values, z * count, count, 1)

    def project(values, weight, pair, mask, flipped):
        middle = inner_right(values, pair[0])
        if mask is not None:
            middle = middle * mask
        middle = middle.astype(BF16)
        main = inner_right(values, weight) if flipped else matmul(values, weight)
        return middle, main + matmul(middle, pair[1])

    own_hot = (
        jnp.arange(NAD * RANK)[:, None]
        == (adapter_index[:, None] * RANK + jnp.arange(RANK)[None, :]).reshape(1, -1)
    ).astype(F32)
    k_local = mod_weight.shape[1]
    cond_act = jax.nn.silu(conditioning).astype(BF16)
    thick = 128

    def thicker(part):
        return jnp.concatenate([part, jnp.zeros((thick - part.shape[0], part.shape[1]), part.dtype)], axis=0)

    def sign(owner):
        return owner[:, 0:1] - owner[:, 1:2]

    def lanes_pad(mask):
        return jnp.pad(mask, ((0, 0), (0, thick - mask.shape[1])))

    if n_f == 8:
        slot_mask = jnp.pad(jnp.concatenate([seq_mask, seq_mask]), ((0, 4), (0, 0)))
        made = front(
            [w[0] for w in local], [w[1] for w in local], adapter_rows, image_tokens, image_cot,
            adapter_index, own_hot.T.astype(BF16), cond_act.astype(F32), mod_weight, x_txt_low,
            g_txt_low, sign(owner_local), lanes_pad(txt_mask), slot_mask,
            jnp.broadcast_to(sign(owner_group), (owner_group.shape[0], thick)), n_f, n_z, fans, cols, 1,
        )
        made = iter(made)
        take = lambda count: [next(made) for _ in range(count)]
        img_w = [w.reshape(-1, w.shape[-1]) for w in take(4)]
        txt_w = [w.reshape(-1, w.shape[-1]) for w in take(4)]
        x_img, g_img = [v.reshape(-1, width) for v in take(2)]
        img_rows_mod, txt_mod = take(2)
        img_pairs = [None] + list(zip(take(4), take(4)))
        thick_pairs = [None] + list(zip(take(4), take(4)))
        mod_a, mod_b, tmod, cond_own, txt_dm = take(5)
        o_txt, lse, bias, hot_four = take(4)
        bias = bias[:, :1]
        img_in, img_qkv_mid, img_heads, txt_in, txt_qkv_mid, txt_heads, attended = take(7)
        img_heads = img_heads.reshape(img_n, -1)
        txt_in = txt_in.reshape(-1, width)
        txt_pairs = [None, tuple(part[:rank_cols] for part in thick_pairs[1])]
        img_mod = img_rows_mod[:6].reshape(1, -1)
        txt_mods = txt_mod.reshape(slots, 8, width)[:, :6].reshape(slots, -1)
    else:
        column_picks = by_group(adapter_index, swap_core(adapter_index))
        column_count = 2 * slots
        one_hot = (
            jnp.arange(NAD * RANK)[:, None]
            == (column_picks[:, None] * RANK + jnp.arange(RANK)[None, :]).reshape(1, -1)
        ).astype(F32)
        got = gather([w[0] for w in local], [w[1] for w in local] + [adapter_rows], n_f, n_z)
        got = [g.reshape(-1, g.shape[-1]) for g in got]
        img_w, txt_w, row = got[:4], got[4:8], got[8]
        x_img = reshard(image_tokens)
        g_img = reshard(image_cot)
        own_picks = adapter_index

        a_rows = [[None] * 5 for stream in range(2)]
        b_rows = [[None] * 5 for stream in range(2)]
        offset = 0
        for stream in range(2):
            for index in range(5):
                count = fans[index] // n_z
                a_rows[stream][index] = row[offset : offset + count]
                offset += count
                count = cols[index] // n_z
                b_rows[stream][index] = row[offset : offset + count]
                offset += count

        def b_pick(stream, index, pick_index):
            part = b_rows[stream][index]
            count = part.shape[0] // NAD
            return lax.dynamic_slice_in_dim(part, pick_index * count, count, 0).reshape(RANK, -1)

        def a_pick(rows, hot):
            return inner_right(hot.T.astype(BF16), rows).astype(BF16)

        img_a = a_pick(jnp.concatenate(a_rows[0], axis=0), one_hot)
        fan_share = sum(fans) // n_z
        img_a = img_a.reshape(column_count, RANK, fan_share)
        img_b = [
            jnp.concatenate([b_pick(0, index, column_picks[s]) for index in range(1, 5)], axis=1)
            for s in range(column_count)
        ]
        img_msg = jnp.concatenate([img_a, jnp.stack(img_b)], axis=2)
        txt_a_rows = jnp.concatenate(
            [a_rows[0][0], a_rows[1][0], a_rows[1][1], a_rows[1][3]], axis=0
        )
        txt_a = a_pick(txt_a_rows, own_hot).reshape(slots, RANK, -1)
        txt_b_own = [
            [b_pick(stream, index, own_picks[s]) for s in range(slots)]
            for stream, index in [(0, 0), (1, 0), (1, 1), (1, 2), (1, 3), (1, 4)]
        ]
        txt_b_own = [jnp.concatenate(parts, axis=0) for parts in txt_b_own]
        txt_a_own = a_pick(jnp.concatenate([a_rows[1][2], a_rows[1][4]], axis=0), own_hot)
        txt_msg = jnp.concatenate(
            [txt_a.reshape(slots * RANK, -1), txt_b_own[3], txt_b_own[5]], axis=1
        )
        img_got = jnp.stack(z_exchange(img_msg))
        txt_got = jnp.stack(z_gather(txt_msg))

        def join(part):
            return jnp.swapaxes(part, 0, 1).reshape(part.shape[1], -1)

        img_pairs = []
        offset, b_offset = 0, fan_share
        for index in range(5):
            count = fans[index] // n_z
            a_full = join(img_got[:, :, offset : offset + count])
            offset += count
            if index == 0:
                img_pairs.append(None)
                continue
            count = cols[index] // n_z
            b_full = join(img_got[:, :, b_offset : b_offset + count])
            b_offset += count
            img_pairs.append((a_full, b_full))
        txt_full = []
        offset = 0
        for count in [width // n_z] * 6:
            txt_full.append(join(txt_got[:, :, offset : offset + count]))
            offset += count
        mod_a = [txt_full[0], txt_full[1]]
        mod_b = [txt_b_own[0], txt_b_own[1]]
        txt_pairs = [
            None,
            (txt_full[2], txt_b_own[2]),
            (txt_a_own[:, : width // n_z], txt_full[4]),
            (txt_full[3], txt_b_own[4]),
            (txt_a_own[:, width // n_z :], txt_full[5]),
        ]

        cond_all = lax.all_gather(cond_act, "fsdp", axis=0, tiled=True)
        cond_slice = lax.dynamic_slice_in_dim(cond_all, f * k_local, k_local, 1)
        mod_part = jnp.stack([matmul(cond_slice, mod_weight[stream]) for stream in range(2)], axis=1)
        mod_part = lax.psum_scatter(mod_part, "fsdp", scatter_dimension=0, tiled=True)
        mod_mid = []
        mod_terms = []
        for stream in range(2):
            middle = (inner_right(cond_act, mod_a[stream]) * seq_mask).astype(BF16)
            mod_mid.append(middle)
            mod_terms.append(mod_part[:, stream] + matmul(middle, mod_b[stream]))
        mods = jnp.concatenate(z_gather(jnp.stack(mod_terms, axis=1)), axis=2)
        img_mods = by_group(mods[:, 0], swap_core(mods[:, 0]))
        img_mod = lax.dynamic_slice_in_dim(img_mods, z, 1, 0)
        txt_mods = mods[:, 1]

        img_rows_mod = jnp.concatenate([img_mod.reshape(6, width), jnp.zeros((2, width), F32)], axis=0)
        txt_mod = jnp.pad(txt_mods.reshape(slots, 6, width), ((0, 0), (0, 2), (0, 0))).reshape(-1, width)
        thick_pairs = [None] + [tuple(thicker(part) for part in txt_pairs[index]) for index in range(1, 5)]
        norm_first = [layer_norm(v.astype(F32)) for v in (x_img, x_txt)]
        heads_in = [
            (norm_first[s][0] * (1.0 + stretch(s, 1)) + stretch(s, 0)).astype(BF16) for s in range(2)
        ]

        txt_in = share(heads_in[1])
        txt_qkv_mid, txt_qkv = project(txt_in, txt_w[0], txt_pairs[1], txt_mask, False)
        img_qkv_mid, img_qkv = project(heads_in[0], img_w[0], img_pairs[1], None, False)
        txt_qkv, img_qkv = txt_qkv.astype(BF16), img_qkv.astype(BF16)
        img_heads = to_heads(img_qkv)
        txt_heads = jnp.stack(to_chip([txt_qkv, txt_qkv]))
        img_in = heads_in[0]
        txt_dm = jnp.stack(z_gather((stretch(1, 5) * g_txt_low.astype(F32)).astype(BF16)))

    inputs = [x_img.astype(F32), x_txt]
    norm_one = [layer_norm(values) for values in inputs]
    def txt_home(values):
        got = from_chip([values[0], values[1]])
        return jnp.where(owner_group[:, 0:1] > 0, got[0], jnp.where(owner_group[:, 1:2] > 0, got[1], 0))

    if n_f != 8:
        lengths = by_group(text_lengths[0:1], swap_core(text_lengths[0:1]))
        chip_lengths = jnp.cumsum(lax.dynamic_index_in_dim(lengths, z // slots, 0, keepdims=False))
        chip_slot = z % slots
        chip_segment = jnp.sum(
            (position(txt_rows)[:, None] >= chip_lengths[None, :]).astype(jnp.int32),
            axis=1,
            keepdims=True,
        )
        chip_owner = (chip_segment == chip_slot) & (txt_rows % txt_pad < txt_local)[:, None]
        bias = jnp.where(chip_owner, 0.0, -1e30).astype(F32)
        o_img, o_txt, lse = attend(img_heads, txt_heads, bias, HD)

        attended = to_tokens(o_img)
    (img_branch, img_after, img_mlp, img_pre, img_result, *img_mids, img_gate, txt_mlp, txt_att, txt_after, txt_branch) = both_fwd(
        attended, x_img, g_img, img_rows_mod, img_w[1], img_pairs[2], img_pairs[3], img_w[2], img_pairs[4], img_w[3],
        o_txt, x_txt_low, txt_mod, sign(owner_group), sign(owner_local), lanes_pad(txt_mask_local), txt_w[1], thick_pairs[2],
        n_z, 2,
    )
    made = both_back(
        g_img, img_after, img_branch, img_mlp, attended, img_rows_mod, img_pre, img_w[3], img_pairs[4], img_w[2], img_pairs[3],
        img_w[1], img_pairs[2], img_mids, g_txt_low, txt_after, txt_branch, txt_mod, sign(owner_local), lanes_pad(txt_mask),
        lanes_pad(txt_mask_local), txt_mlp, txt_att, txt_dm, txt_w[1], txt_w[2], txt_w[3], thick_pairs[2], thick_pairs[3],
        thick_pairs[4], n_z, 4,
    )
    img_grad_after, img_grad_att, img_sums, *sides = made[:9]
    txt_result, txt_grad_after, do_txt, txt_sums, *txt_sides = made[9:]
    if n_f != 8:
        txt_sides = [part[:rank_cols] for part in txt_sides]
    txt_sum_rows = txt_sums
    txt_sums = txt_sums.reshape(4, slots, width)
    if n_f != 8:
        image_out = unshard(img_result)

    grads = [[None] * 5 for stream in range(2)]

    def project_back(grad, weight, pair, mask, flipped):
        middle = inner_right(grad, pair[1])
        if mask is not None:
            middle = middle * mask
        middle = middle.astype(BF16)
        main = matmul(grad, weight) if flipped else inner_right(grad, weight)
        return middle, main + matmul(middle, pair[0])

    grads[0][4] = (sides[0], sides[3])
    grads[0][3] = (sides[2], sides[1])
    grads[0][2] = (sides[4], sides[5])
    mod_parts = [[None] * 6 for stream in range(2)]
    for place in range(4):
        mod_parts[1][2 + place] = txt_sums[place]
    grads[1][2] = (txt_sides[0], txt_sides[1])
    grads[1][3] = (txt_sides[2], txt_sides[3])
    grads[1][4] = (txt_sides[4], txt_sides[5])
    img_sum_rows = img_sums
    img_sums = jnp.sum(jnp.concatenate([img_sums, img_gate]).reshape(4, 8, width), axis=1)
    for place in range(4):
        mod_parts[0][2 + place] = img_sums[place : place + 1]
    grad_after = [img_grad_after, txt_grad_after]

    do_img = img_grad_att.reshape(img_n, -1)
    if n_f != 8:
        d_img, d_txt = attend_back(img_heads, txt_heads, bias, do_img, do_txt, lse, HD)
    if n_f == 8:
        sides_of = lambda stream, side: [grads[stream][index][side] for index in range(2, 5)]
        d_img, d_txt, image_out, early = attend_back_far(
            img_heads, txt_heads, bias, do_img, do_txt, lse, HD, img_result.reshape(2, quarter, width),
            sides_of(0, 0), sides_of(0, 1), n_z, fans, cols, 5,
        )
        smalls = (
            x_img, img_grad_after, img_in, img_rows_mod, img_qkv_mid, *img_pairs[1], img_sum_rows, img_gate,
            x_txt_low, txt_grad_after, txt_in.reshape(n_z, txt_pad, width), txt_mod, sign(owner_group), sign(owner_local),
            lanes_pad(txt_mask_local), txt_qkv_mid, txt_w[0], *thick_pairs[1], txt_sum_rows,
        )
        image_low, txt_grad, cond_slices, mod_rank, shard = tail(
            d_img.reshape(2, img_half, -1), d_txt, img_w[0].reshape(n_f, k_local, -1), smalls,
            early, sides_of(1, 0), sides_of(1, 1),
            hot_four, own_hot.T.astype(BF16), mod_weight, mod_b, tmod, cond_own, slot_mask,
            n_f, n_z, fans, cols, 3,
        )
        image_grad = image_low.astype(F32)
        cond_rows = jnp.swapaxes(cond_slices[:, :slots, :k_local], 0, 1).reshape(slots, width)
        for s in range(2):
            cond_rows = cond_rows + matmul(mod_rank[2 * s : 2 * s + 2].astype(BF16), mod_a[s])
        cond_grad = jax.vjp(jax.nn.silu, conditioning)[1](cond_rows)[0]
        adapter_grad = shard.reshape(1, -1)
        return (image_out, txt_result[:txt_local], image_grad, txt_grad[:txt_local], cond_grad, adapter_grad)
    img_grad_qkv = to_tokens(d_img)
    txt_grad_qkv = txt_home(d_txt)

    img_back_mid, img_grad_norm = project_back(img_grad_qkv, img_w[0], img_pairs[1], None, False)
    grads[0][1] = (inner_left(img_back_mid, img_in), inner_left(img_qkv_mid, img_grad_qkv))
    txt_grad_norm, txt_qkv_back = give(
        inner_right(txt_grad_qkv, txt_w[0]), inner_right(txt_grad_qkv, txt_pairs[1][1])
    )
    txt_grad_norm = txt_grad_norm + matmul(txt_qkv_back, txt_pairs[1][0])
    grads[1][1] = (
        inner_left(share(txt_qkv_back), lanes(txt_in)),
        inner_left(txt_qkv_mid, txt_grad_qkv),
    )
    grad_norm = [img_grad_norm, txt_grad_norm]
    grad_inputs = []
    for s in range(2):
        grad_inputs.append(
            grad_after[s]
            + norm_back(grad_norm[s], norm_one[s][0], norm_one[s][1], stretch(s, 1))
        )
        mod_parts[s][0] = collapse(s, grad_norm[s])
        mod_parts[s][1] = collapse(s, grad_norm[s] * norm_one[s][0])
    img_dmod = jnp.concatenate(mod_parts[0], axis=1)
    txt_dmod = jnp.concatenate(mod_parts[1], axis=1)
    image_grad = unshard(grad_inputs[0].astype(BF16)).astype(F32)

    img_dmod = (img_dmod + swap_core(img_dmod)).astype(BF16)
    def lane_blocks(values):
        return jnp.swapaxes(values.reshape(values.shape[0], n_z, -1), 0, 1)

    img_dmods = jnp.concatenate(z_exchange(lane_blocks(img_dmod)), axis=0)
    img_dmods = lax.dynamic_slice_in_dim(img_dmods, core * slots, slots, 0)
    txt_dmods = sum(z_exchange(lane_blocks(txt_dmod))).astype(BF16)
    dmods = jnp.stack([img_dmods, txt_dmods], axis=1)
    dmods_all = lax.all_gather(dmods, "fsdp", axis=0, tiled=True)
    cond_part = sum(inner_right(dmods_all[:, s], mod_weight[s]) for s in range(2))
    mod_back = [inner_right(dmods[:, s], mod_b[s]) for s in range(2)]
    cond_part = cond_part.reshape(-1, width // n_f)
    joined = jnp.concatenate([cond_part.reshape(-1), jnp.stack(mod_back).reshape(-1)])
    joined = sum(z_gather(joined))
    cond_slices = joined[: cond_part.size].reshape(n_f, -1, width // n_f)
    mod_rank = joined[cond_part.size :].reshape(2, slots, -1)
    cond_rows = lax.all_to_all(cond_slices, "fsdp", 0, 2, tiled=True)[0]
    for s in range(2):
        back_mid = (mod_rank[s] * seq_mask).astype(BF16)
        cond_rows = cond_rows + matmul(back_mid, mod_a[s])
        grads[s][0] = (inner_left(back_mid, lanes(cond_act)), inner_left(mod_mid[s], dmods[:, s]))
    cond_grad = jax.vjp(jax.nn.silu, conditioning)[1](cond_rows)[0]

    def spread(values):
        return jnp.swapaxes(values.reshape(RANK, n_z, -1), 0, 1)

    img_rows = {}
    for group in ((2, 3, 4), (1,)):
        parts = [spread(grads[0][index][side]) for side in range(2) for index in group]
        parts = jnp.concatenate(z_exchange(jnp.concatenate(parts, axis=2)), axis=0)
        offset = 0
        for side, sizes in enumerate((fans, cols)):
            for index in group:
                count = sizes[index] // n_z
                img_rows[side, index] = parts[:, offset : offset + count]
                offset += count
    flat = []
    for stream in range(2):
        for index in range(5):
            if stream == 0 and index > 0:
                part_a, part_b = img_rows[0, index], img_rows[1, index]
                hot = one_hot
            else:
                part_a, part_b = grads[stream][index]
                hot = own_hot
            flat.append(
                lax.dot_general(
                    part_a, hot, (((0,), (1,)), ((), ())),
                    precision=HIGH, preferred_element_type=F32,
                )
            )
            flat.append(exact(hot, part_b).reshape(-1, 128))
    total = jnp.concatenate(flat, axis=0).reshape(n_f, -1, 128)
    step = 1
    while step < n_f:
        bit = (f // step) % 2
        pairs = total.reshape((-1, 2) + total.shape[1:])
        keep = lax.dynamic_index_in_dim(pairs, bit, 1, keepdims=False)
        send = lax.dynamic_index_in_dim(pairs, 1 - bit, 1, keepdims=False)
        sent = lax.ppermute(send.astype(BF16), "fsdp", [(i, i ^ step) for i in range(n_f)])
        total = keep + sent.astype(F32)
        step *= 2
    adapter_grad = total.reshape(1, -1)
    return (
        image_out, txt_result[:txt_local], image_grad, grad_inputs[1][:txt_local], cond_grad, adapter_grad
    )


def solution(mesh):
    return jax.shard_map(
        shards,
        mesh=mesh,
        in_specs=(
            P("fsdp", "tp", None),
            P(("fsdp", "tp"), None),
            P("fsdp", None),
            P("fsdp", None),
            P("fsdp"),
            P("tp", "fsdp"),
            P(None, "fsdp", "tp"),
            P(None, "fsdp", "tp"),
            P(None, "tp", "fsdp"),
            P(None, "fsdp", "tp"),
            P(None, "tp", "fsdp"),
            P("fsdp", "tp", None),
            P(("fsdp", "tp"), None),
        ),
        out_specs=(
            P("fsdp", "tp", None),
            P(("fsdp", "tp"), None),
            P("fsdp", "tp", None),
            P(("fsdp", "tp"), None),
            P("fsdp", None),
            P("tp", "fsdp"),
        ),
        check_vma=False,
    )
```

```python
import functools

import jax
import jax.numpy as jnp
from jax import lax
from jax.experimental import pallas as pl
from jax.experimental.pallas import tpu as pltpu
from jax.sharding import PartitionSpec as P

MESH = pl.DeviceIdType.MESH

def bits_of(count):
    return max(count.bit_length() - 1, 0)

def halves(width):
    tiles = width // 128
    first = (tiles + 1) // 2 * 128
    return [(0, first), (first, width - first)]

def gather_kernel(n_f, n_z, full_count, part_count, *refs):
    total = full_count + part_count
    ins, outs = refs[:total], refs[total:2 * total]
    z_send, z_recv, xy_send, xy_recv, core_send, core_recv, own_sem = refs[2 * total:]
    f = lax.axis_index("fsdp")
    z = lax.axis_index("tp")
    chip, core = f // 2, f % 2
    chips = n_f // 2
    nbits = bits_of(chips)
    partner = chip * 2 + (1 - core)

    def peer_of(mask):
        other = 0
        for bit in range(nbits):
            have = (chip // (1 << bit)) % 2
            want = 1 - have if (mask >> bit) & 1 else have
            other = other + want * (1 << bit)
        return other * 2 + core

    barrier = pltpu.get_barrier_semaphore()
    for bit in range(nbits):
        pl.semaphore_signal(barrier, inc=1, device_id=(peer_of(1 << bit), z), device_id_type=MESH)
    pl.semaphore_signal(barrier, inc=1, device_id=(partner, z), device_id_type=MESH)
    @pl.when(z > 0)
    def _():
        pl.semaphore_signal(barrier, inc=1, device_id=(f, z - 1), device_id_type=MESH)
    @pl.when(z < n_z - 1)
    def _():
        pl.semaphore_signal(barrier, inc=1, device_id=(f, z + 1), device_id_type=MESH)
    peers = nbits + 1 + (z > 0).astype(jnp.int32) + (z < n_z - 1).astype(jnp.int32)
    pl.semaphore_wait(barrier, peers)

    def width(m):
        return ins[m].shape[-1]

    def place(m, who, zz, off=0, w=None):
        w = width(m) if w is None else w
        if m < full_count:
            return outs[m].at[who, :, pl.ds(pl.multiple_of(zz * width(m) + off, 128), w)]
        if w == width(m):
            return outs[m].at[who]
        return outs[m].at[who, :, pl.ds(off, w)]

    def piece(m, off, w):
        return ins[m] if w == width(m) else ins[m].at[:, pl.ds(off, w)]

    def remote(src, dst, ssem, rsem, dev):
        return pltpu.make_async_remote_copy(src_ref=src, dst_ref=dst, send_sem=ssem, recv_sem=rsem, device_id=dev, device_id_type=MESH)

    def order_of(half):
        order = list(range(nbits))
        return order if half == 0 else order[::-1]

    def cuts(m):
        if width(m) >= 256:
            return list(enumerate(halves(width(m))))
        return [(m % 2, (0, width(m)))]

    def slot(m, zz):
        return zz if m < full_count else 0

    def xy_copy(m, zz, half, cut, mask, bit, own_piece=False):
        off, w = cut
        who = peer_of(mask)
        source = piece(m, off, w) if own_piece and mask == 0 else place(m, who, zz, off, w)
        return remote(source, place(m, who, zz, off, w),
                      xy_send.at[m, slot(m, zz), half, mask, bit], xy_recv.at[m, slot(m, zz), half, mask | (1 << bit)],
                      (peer_of(1 << bit), z))

    def xy_wait(m, zz, half, cut, mask):
        off, w = cut
        who = peer_of(mask)
        remote(place(m, who, zz, off, w), place(m, who, zz, off, w), xy_send.at[m, slot(m, zz), half, 0, 0],
               xy_recv.at[m, slot(m, zz), half, mask], (partner, z)).wait_recv()

    def core_copy(m, zz, half, cut, mask, own_piece=False):
        off, w = cut
        who = peer_of(mask)
        source = piece(m, off, w) if own_piece and mask == 0 else place(m, who, zz, off, w)
        return remote(source, place(m, who, zz, off, w),
                      core_send.at[m, slot(m, zz), half, mask], core_recv.at[m, slot(m, zz), half, mask], (partner, z))

    def core_wait_recv(m, zz, half, cut, mask):
        off, w = cut
        who = peer_of(mask) - core + (1 - core)
        remote(place(m, who, zz, off, w), place(m, who, zz, off, w),
               core_send.at[m, slot(m, zz), half, mask], core_recv.at[m, slot(m, zz), half, mask], (partner, z)).wait_recv()

    def own(m):
        return pltpu.make_async_copy(ins[m], place(m, f, z), own_sem.at[m])

    def z_copy(m, zz, up, own_piece=False):
        return remote(ins[m] if own_piece else place(m, f, zz), place(m, f, zz), z_send.at[m, zz, up], z_recv.at[m, zz], (f, z + 1 if up else z - 1))

    def launch(m, zz, own_piece=False):
        for half, cut in cuts(m):
            for bit in order_of(half):
                xy_copy(m, zz, half, cut, 0, bit, own_piece).start()
            core_copy(m, zz, half, cut, 0, own_piece).start()

    def masks_in_order(half):
        order = order_of(half)
        def rank(mask):
            return [1 if (mask >> b) & 1 else 0 for b in reversed(order)]
        return sorted(range(1, 1 << nbits), key=rank)

    def forward(m, zz):
        for half, cut in cuts(m):
            order = order_of(half)
            for mask in masks_in_order(half):
                last = max(i for i, b in enumerate(order) if (mask >> b) & 1)
                if last == nbits - 1:
                    continue
                xy_wait(m, zz, half, cut, mask)
                for b in order[last + 1:]:
                    xy_copy(m, zz, half, cut, mask, b).start()
                core_copy(m, zz, half, cut, mask).start()

    def finish(m, zz):
        for half, cut in cuts(m):
            order = order_of(half)
            for mask in masks_in_order(half):
                last = max(i for i, b in enumerate(order) if (mask >> b) & 1)
                if last == nbits - 1:
                    xy_wait(m, zz, half, cut, mask)
                    core_copy(m, zz, half, cut, mask).start()

    def drain(m, zz):
        for half, cut in cuts(m):
            order = order_of(half)
            for mask in [0] + masks_in_order(half):
                last = max([i for i, b in enumerate(order) if (mask >> b) & 1], default=-1)
                for b in order[last + 1:]:
                    xy_copy(m, zz, half, cut, mask, b).wait_send()
                core_copy(m, zz, half, cut, mask).wait_send()
                core_wait_recv(m, zz, half, cut, mask)

    for m in range(total):
        own(m).start()
    for m in range(total):
        if m < full_count:
            @pl.when(z < n_z - 1)
            def _():
                z_copy(m, z, 1, True).start()
            @pl.when(z > 0)
            def _():
                z_copy(m, z, 0, True).start()
        launch(m, z, True)
    for m in range(full_count, total):
        forward(m, z)
    for k in range(1, n_z):
        for m in range(full_count):
            @pl.when(z - k >= 0)
            def _():
                zz = z - k
                z_copy(m, zz, 1).wait_recv()
                @pl.when(z < n_z - 1)
                def _():
                    z_copy(m, zz, 1).start()
                launch(m, zz)
            @pl.when(z + k < n_z)
            def _():
                zz = z + k
                z_copy(m, zz, 0).wait_recv()
                @pl.when(z > 0)
                def _():
                    z_copy(m, zz, 0).start()
                launch(m, zz)
            for sign in ((-1, 1) if k > 1 else (1,)):
                zz = z + sign * (k - 1)
                @pl.when((zz >= 0) & (zz < n_z))
                def _():
                    forward(m, zz)
    for m in range(full_count):
        for sign in (-1, 1):
            zz = z + sign * (n_z - 1)
            @pl.when((zz >= 0) & (zz < n_z))
            def _():
                forward(m, zz)
    for m in range(total):
        if m < full_count:
            def body(zz, _):
                finish(m, zz)
                return 0
            lax.fori_loop(0, n_z, body, 0)
        else:
            finish(m, z)
    for m in range(total):
        own(m).wait()
        if m < full_count:
            def body(zz, _):
                drain(m, zz)
                @pl.when((zz <= z) & (z < n_z - 1))
                def _():
                    z_copy(m, zz, 1).wait_send()
                @pl.when((zz >= z) & (z > 0))
                def _():
                    z_copy(m, zz, 0).wait_send()
                return 0
            lax.fori_loop(0, n_z, body, 0)
        else:
            drain(m, z)

def gather(full, part, n_f, n_z, cid=1):
    arrays = list(full) + list(part)
    total = len(arrays)
    if n_f > 8:
        rows = [lax.all_gather(a, "fsdp", axis=0, tiled=True) for a in arrays]
        return [
            lax.all_gather(a, "tp", axis=1, tiled=True) if i < len(full) else a
            for i, a in enumerate(rows)
        ]
    chips = n_f // 2
    nbits = bits_of(chips)
    shapes = [jax.ShapeDtypeStruct((n_f,) + a.shape[:-1] + (a.shape[-1] * (n_z if i < len(full) else 1),), a.dtype) for i, a in enumerate(arrays)]
    dma = pltpu.SemaphoreType.DMA
    return pl.pallas_call(
        functools.partial(gather_kernel, n_f, n_z, len(full), len(part)),
        out_shape=shapes,
        in_specs=[pl.BlockSpec(memory_space=pl.ANY)] * total,
        out_specs=[pl.BlockSpec(memory_space=pl.ANY)] * total,
        scratch_shapes=[
            dma((total, n_z, 2)), dma((total, n_z)),
            dma((total, n_z, 2, chips, max(nbits, 1))), dma((total, n_z, 2, chips)),
            dma((total, n_z, 2, chips)), dma((total, n_z, 2, chips)), dma((total,)),
        ],
        compiler_params=pltpu.CompilerParams(collective_id=cid, has_side_effects=True),
        name="weight_gather",
    )(*arrays)

def dots(left, right, lc, rc):
    return lax.dot_general(left, right, (((lc,), (rc,)), ((), ())), preferred_element_type=jnp.float32)

def attend_block(q, ki, vi, kt, vt, bias):
    q = q * jnp.bfloat16(0.125)
    si = dots(ki, q, 1, 1)
    st = dots(kt, q, 1, 1) + bias
    top = jnp.maximum(jnp.max(si, axis=0, keepdims=True), jnp.max(st, axis=0, keepdims=True))
    ei = jnp.exp(si - top)
    et = jnp.exp(st - top)
    total = jnp.sum(ei, axis=0, keepdims=True) + jnp.sum(et, axis=0, keepdims=True)
    o = dots(vi, ei.astype(jnp.bfloat16), 0, 0) + dots(vt, et.astype(jnp.bfloat16), 0, 0)
    return (o / total).T.astype(jnp.bfloat16), top + jnp.log(total)


def attend_kernel(hd, bq, img_ref, txt_ref, bias_ref, oi_ref, ot_ref, lse_ref):
    img_n, txt_n = img_ref.shape[0], txt_ref.shape[1]
    heads = img_ref.shape[1] // (3 * hd)
    bias = bias_ref[...]
    for h in range(heads):
        base = 3 * hd * h
        ki = img_ref[:, base + hd:base + 2 * hd]
        vi = img_ref[:, base + 2 * hd:base + 3 * hd]
        kt = txt_ref[0, :, base + hd:base + 2 * hd]
        vt = txt_ref[0, :, base + 2 * hd:base + 3 * hd]

        def block(q):
            q = q * jnp.bfloat16(0.125)
            si = dots(ki, q, 1, 1)
            st = dots(kt, q, 1, 1) + bias
            top = jnp.maximum(jnp.max(si, axis=0, keepdims=True), jnp.max(st, axis=0, keepdims=True))
            ei = jnp.exp(si - top)
            et = jnp.exp(st - top)
            total = jnp.sum(ei, axis=0, keepdims=True) + jnp.sum(et, axis=0, keepdims=True)
            o = dots(vi, ei.astype(jnp.bfloat16), 0, 0) + dots(vt, et.astype(jnp.bfloat16), 0, 0)
            return (o / total).T.astype(jnp.bfloat16), top + jnp.log(total)

        for i in range(img_n // bq):
            o, lse = block(img_ref[i * bq:(i + 1) * bq, base:base + hd])
            oi_ref[i * bq:(i + 1) * bq, h * hd:(h + 1) * hd] = o
            lse_ref[0, h:h + 1, i * bq:(i + 1) * bq] = lse
        o, lse = block(txt_ref[0, :, base:base + hd])
        ot_ref[0, :, h * hd:(h + 1) * hd] = o
        lse_ref[0, h:h + 1, img_n:img_n + txt_n] = lse

def attend(img, txt, bias, hd, bq=512):
    img_n, cols = img.shape
    parts, txt_n, _ = txt.shape
    pairs = cols // (6 * hd)
    per = pairs // parts
    return pl.pallas_call(
        functools.partial(attend_kernel, hd, bq),
        grid=(pairs,),
        in_specs=[
            pl.BlockSpec((img_n, 6 * hd), lambda i: (0, i)),
            pl.BlockSpec((1, txt_n, 6 * hd), lambda i: (i // per, 0, i % per)),
            pl.BlockSpec((txt_n, 1), lambda i: (0, 0)),
        ],
        out_specs=[
            pl.BlockSpec((img_n, 2 * hd), lambda i: (0, i)),
            pl.BlockSpec((1, txt_n, 2 * hd), lambda i: (i // per, 0, i % per)),
            pl.BlockSpec((1, 2, img_n + txt_n), lambda i: (i, 0, 0)),
        ],
        out_shape=[
            jax.ShapeDtypeStruct((img_n, pairs * 2 * hd), jnp.bfloat16),
            jax.ShapeDtypeStruct((parts, txt_n, per * 2 * hd), jnp.bfloat16),
            jax.ShapeDtypeStruct((pairs, 2, img_n + txt_n), jnp.float32),
        ],
        compiler_params=pltpu.CompilerParams(vmem_limit_bytes=48 * 1024 * 1024),
        name="attend",
    )(img, txt, bias)

def attend_back_kernel(hd, bq, img_ref, txt_ref, bias_ref, doi_ref, dot_ref, lse_ref, di_ref, dt_ref, acc_i, acc_t):
    img_n, txt_n = img_ref.shape[0], txt_ref.shape[1]
    heads = img_ref.shape[1] // (3 * hd)
    bias = bias_ref[...]
    for h in range(heads):
        base = 3 * hd * h
        ki = img_ref[:, base + hd:base + 2 * hd]
        vi = img_ref[:, base + 2 * hd:base + 3 * hd]
        kt = txt_ref[0, :, base + hd:base + 2 * hd]
        vt = txt_ref[0, :, base + 2 * hd:base + 3 * hd]

        def block(q, do, lse, first):
            q = q * jnp.bfloat16(0.125)
            pi = jnp.exp(dots(ki, q, 1, 1) - lse)
            pt = jnp.exp(dots(kt, q, 1, 1) + bias - lse)
            dwi = dots(vi, do, 1, 1)
            dwt = dots(vt, do, 1, 1)
            delta = jnp.sum(pi * dwi, axis=0, keepdims=True) + jnp.sum(pt * dwt, axis=0, keepdims=True)
            dsi = (pi * (dwi - delta)).astype(jnp.bfloat16)
            dst = (pt * (dwt - delta)).astype(jnp.bfloat16)
            dvi = dots(pi.astype(jnp.bfloat16), do, 1, 0)
            dvt = dots(pt.astype(jnp.bfloat16), do, 1, 0)
            dki = dots(dsi, q, 1, 0)
            dkt = dots(dst, q, 1, 0)
            if first:
                acc_i[0], acc_i[1], acc_t[0], acc_t[1] = dki, dvi, dkt, dvt
            else:
                acc_i[0] += dki
                acc_i[1] += dvi
                acc_t[0] += dkt
                acc_t[1] += dvt
            dq = dots(ki, dsi, 0, 0) + dots(kt, dst, 0, 0)
            return (dq.T * 0.125).astype(jnp.bfloat16)

        for i in range(img_n // bq):
            rows = slice(i * bq, (i + 1) * bq)
            di_ref[rows, base:base + hd] = block(
                img_ref[rows, base:base + hd], doi_ref[rows, h * hd:(h + 1) * hd], lse_ref[0, h:h + 1, rows], i == 0)
        grad = jnp.where(bias < 0, 0.0, dot_ref[0, :, h * hd:(h + 1) * hd].astype(jnp.float32)).astype(jnp.bfloat16)
        dt_ref[0, :, base:base + hd] = block(
            txt_ref[0, :, base:base + hd], grad, lse_ref[0, h:h + 1, img_n:img_n + txt_n], False)
        di_ref[:, base + hd:base + 2 * hd] = acc_i[0].astype(jnp.bfloat16)
        di_ref[:, base + 2 * hd:base + 3 * hd] = acc_i[1].astype(jnp.bfloat16)
        dt_ref[0, :, base + hd:base + 2 * hd] = acc_t[0].astype(jnp.bfloat16)
        dt_ref[0, :, base + 2 * hd:base + 3 * hd] = acc_t[1].astype(jnp.bfloat16)

def attend_back_far_kernel(hd, bq, n_z, fans, cols, img_ref, txt_ref, bias_ref, doi_ref, dot_ref, lse_ref, y_ref, *refs):
    img_a, img_b, rest = refs[:3], refs[3:6], refs[6:]
    di_ref, dt_ref, y_out, z_out, acc_i, acc_t, zmsg, y_send, y_recv, z_send, z_recv = rest
    step = pl.program_id(0)
    f, z, core, base, column = column_peers(n_z)
    ring = ZRing(f, z, n_z)
    there = [(base + z // 2, 2 * core + i) for i in range(2)]

    def is_here(i):
        return (z // 2 == core) & (2 * core + i == z)

    def y_keep(i):
        return pltpu.make_async_copy(y_ref.at[i], y_out.at[z % 2], y_recv.at[z % 2])

    def y_push(i):
        return push(y_ref.at[i], y_out.at[z % 2], y_send.at[i], y_recv.at[z % 2], there[i])

    def z_keep():
        return pltpu.make_async_copy(zmsg.at[z], z_out.at[z], z_recv.at[z])

    @pl.when(step == 0)
    def _():
        meet(column)
        offset = 0
        for part, sizes in ((img_a, fans), (img_b, cols)):
            for index in range(3):
                count = sizes[index + 2] // n_z
                for t in range(n_z):
                    zmsg[t, :, offset:offset + count] = part[index][:, t * count:(t + 1) * count].astype(jnp.bfloat16)
                offset += count
        ring.start(lambda to: zmsg.at[to], z_out, z_send, z_recv)
        z_keep().start()
        for i in range(2):
            @pl.when(is_here(i))
            def _():
                y_keep(i).start()

            @pl.when(jnp.logical_not(is_here(i)))
            def _():
                y_push(i).start()

    attend_back_kernel(hd, bq, img_ref, txt_ref, bias_ref, doi_ref, dot_ref, lse_ref, di_ref, dt_ref, acc_i, acc_t)

    @pl.when(step == pl.num_programs(0) - 1)
    def _():
        z_keep().wait()
        ring.wait(z_out, z_send, z_recv)
        ring.drain(lambda to: zmsg.at[to], z_out, z_send, z_recv)
        for i in range(2):
            @pl.when(is_here(i))
            def _():
                y_keep(i).wait()

            @pl.when(jnp.logical_not(is_here(i)))
            def _():
                push(y_out.at[i], y_out.at[i], y_send.at[i], y_recv.at[i], there[i]).wait_recv()
                y_push(i).wait_send()


def attend_back_far(img, txt, bias, doi, dot, lse, hd, y, img_a, img_b, n_z, fans, cols, cid, bq=512):
    img_n, wide_n = img.shape
    parts, txt_n, _ = txt.shape
    pairs = wide_n // (6 * hd)
    per = pairs // parts
    vmem, dma = pltpu.VMEM, pltpu.SemaphoreType.DMA
    bf16, shape = jnp.bfloat16, jax.ShapeDtypeStruct
    wide = pl.BlockSpec((img_n, 6 * hd), lambda i: (0, i))
    wide_t = pl.BlockSpec((1, txt_n, 6 * hd), lambda i: (i // per, 0, i % per))
    outside = pl.BlockSpec(memory_space=pl.ANY)
    sides = (*img_a, *img_b)
    lanes = (sum(fans[2:]) + sum(cols[2:])) // n_z
    return pl.pallas_call(
        functools.partial(attend_back_far_kernel, hd, bq, n_z, tuple(fans), tuple(cols)),
        grid=(pairs,),
        in_specs=[
            wide, wide_t,
            pl.BlockSpec((txt_n, 1), lambda i: (0, 0)),
            pl.BlockSpec((img_n, 2 * hd), lambda i: (0, i)),
            pl.BlockSpec((1, txt_n, 2 * hd), lambda i: (i // per, 0, i % per)),
            pl.BlockSpec((1, 2, img_n + txt_n), lambda i: (i, 0, 0)),
            outside,
        ] + [pl.BlockSpec(v.shape, lambda i: (0, 0)) for v in sides],
        out_specs=[wide, wide_t, outside, outside],
        out_shape=[shape(img.shape, bf16), shape(txt.shape, bf16), shape(y.shape, bf16), shape((n_z, RANK, lanes), bf16)],
        scratch_shapes=[vmem((2, img_n, hd), jnp.float32), vmem((2, txt_n, hd), jnp.float32), vmem((n_z, RANK, lanes), bf16),
                        dma((2,)), dma((2,)), dma((n_z,)), dma((n_z,))],
        compiler_params=pltpu.CompilerParams(collective_id=cid, has_side_effects=True, vmem_limit_bytes=56 * 1024 * 1024),
        name="attend_back",
    )(img, txt, bias, doi, dot, lse, y, *sides)


def attend_back(img, txt, bias, doi, dot, lse, hd, bq=512):
    img_n, cols = img.shape
    parts, txt_n, _ = txt.shape
    pairs = cols // (6 * hd)
    per = pairs // parts
    wide = pl.BlockSpec((img_n, 6 * hd), lambda i: (0, i))
    wide_t = pl.BlockSpec((1, txt_n, 6 * hd), lambda i: (i // per, 0, i % per))
    return pl.pallas_call(
        functools.partial(attend_back_kernel, hd, bq),
        grid=(pairs,),
        in_specs=[
            wide, wide_t,
            pl.BlockSpec((txt_n, 1), lambda i: (0, 0)),
            pl.BlockSpec((img_n, 2 * hd), lambda i: (0, i)),
            pl.BlockSpec((1, txt_n, 2 * hd), lambda i: (i // per, 0, i % per)),
            pl.BlockSpec((1, 2, img_n + txt_n), lambda i: (i, 0, 0)),
        ],
        out_specs=[wide, wide_t],
        out_shape=[jax.ShapeDtypeStruct(img.shape, jnp.bfloat16), jax.ShapeDtypeStruct(txt.shape, jnp.bfloat16)],
        scratch_shapes=[pltpu.VMEM((2, img_n, hd), jnp.float32), pltpu.VMEM((2, txt_n, hd), jnp.float32)],
        compiler_params=pltpu.CompilerParams(vmem_limit_bytes=48 * 1024 * 1024),
        name="attend_back",
    )(img, txt, bias, doi, dot, lse)

ROWS = 64


def mm(left, right):
    return dots(left, right, 1, 0)


def mm_t(left, right):
    return dots(left, right, 1, 1)


def t_mm(left, right):
    return dots(left, right, 0, 0)


def gelu_parts(u):
    scale = 0.7978845608028654
    square = u * u
    tanh = jnp.tanh(scale * (u + 0.044715 * u * square))
    half = 0.5 * (1.0 + tanh)
    slope = half + 0.5 * u * (1.0 - tanh * tanh) * (scale * (1.0 + 3 * 0.044715 * square))
    return u * half, slope


def norm_rows(v):
    center = v - jnp.mean(v, axis=-1, keepdims=True)
    inverse = lax.rsqrt(jnp.mean(center * center, axis=-1, keepdims=True) + 1e-06)
    return center * inverse, inverse


def column_peers(n_z):
    f, z = lax.axis_index("fsdp"), lax.axis_index("tp")
    core = f % 2
    base = f - core
    peers = [(f, (z + j) % n_z) for j in range(1, n_z)]
    peers += [(base + 1 - core, (z + j) % n_z) for j in range(n_z)]
    return f, z, core, base, peers


def meet(peers):
    barrier = pltpu.get_barrier_semaphore()
    for peer in peers:
        pl.semaphore_signal(barrier, inc=1, device_id=peer, device_id_type=MESH)
    pl.semaphore_wait(barrier, len(peers))


def push(src, dst, send, recv, peer):
    return pltpu.make_async_remote_copy(
        src_ref=src, dst_ref=dst, send_sem=send, recv_sem=recv, device_id=peer, device_id_type=MESH)


class ZRing:
    def __init__(self, f, z, n_z):
        self.f, self.z, self.n_z = f, z, n_z

    def start(self, source_of, buf, send, recv):
        for j in range(1, self.n_z):
            to = (self.z + j) % self.n_z
            push(source_of(to), buf.at[self.z], send.at[j], recv.at[self.z], (self.f, to)).start()

    def wait(self, buf, send, recv):
        for j in range(1, self.n_z):
            came = (self.z + j) % self.n_z
            push(buf.at[came], buf.at[came], send.at[j], recv.at[came], (self.f, came)).wait_recv()

    def drain(self, source_of, buf, send, recv):
        for j in range(1, self.n_z):
            to = (self.z + j) % self.n_z
            push(source_of(to), buf.at[self.z], send.at[j], recv.at[self.z], (self.f, to)).wait_send()


def text_tools(n_z, pad, width, f, z, lmask_ref, part_ref, mine_ref, out_buf, in_buf, rs_send, rs_recv, ag_send, ag_recv):
    ring = ZRing(f, z, n_z)
    bf16, f32 = jnp.bfloat16, jnp.float32

    def scatter(turn, main, rank_part):
        full = jnp.concatenate([main, rank_part], axis=1)
        full = full.reshape(n_z, pad, full.shape[1])
        part_ref[...] = full
        mine_ref[turn] = part_ref[z]
        out_buf[turn] = full.astype(bf16)
        ring.start(lambda to: out_buf.at[turn, to], in_buf.at[turn], rs_send.at[turn], rs_recv.at[turn])

    def collect(turn):
        ring.wait(in_buf.at[turn], rs_send.at[turn], rs_recv.at[turn])
        total = mine_ref[turn]
        for j in range(1, n_z):
            total = total + in_buf[turn, (z + j) % n_z].astype(f32)
        ring.drain(lambda to: out_buf.at[turn, to], in_buf.at[turn], rs_send.at[turn], rs_recv.at[turn])
        return total[:, :width], (total[:, width:] * lmask_ref[...]).astype(bf16)

    def spread(ref, *parts):
        offset = 0
        for part in parts:
            ref[z, :, offset:offset + part.shape[1]] = part
            offset += part.shape[1]
        ring.start(lambda to: ref.at[z], ref, ag_send, ag_recv)

    def spread_end(ref):
        ring.wait(ref, ag_send, ag_recv)
        ring.drain(lambda to: ref.at[z], ref, ag_send, ag_recv)

    def gathered(ref, start, count):
        return ref[:, :, start:start + count].reshape(n_z * pad, count)

    def own_lanes(ref, share):
        at = pl.ds(pl.multiple_of(z * share, 128), share)
        return ref[:, :, at].reshape(n_z * pad, share)

    return scatter, collect, spread, spread_end, gathered, own_lanes


def rows_of(mod_ref, own_ref):
    return lambda row: jnp.where(own_ref[...] > 0, mod_ref[row:row + 1, :], mod_ref[8 + row:9 + row, :])


def both_fwd_kernel(tiles, n_z, turns, o_ref, x_ref, g_ref, mod_ref, wo_ref, ao_ref, bo_ref, a1_ref, b1_ref, w1_ref, a2_ref, w2_ref, b2_ref,
                    ot_ref, xt_ref, tmod_ref, owner_ref, own_ref, lmask_ref, two_ref, tao_ref, tbo_ref,
                    a_out, x1_out, h2_out, u_out, y_out, to_out, t1_out, t2_out, gate_out,
                    tall_out, att_out, tx1_out, tbr_out,
                    m_acc, t2_acc, o_got, part_ref, mine_ref, out_buf, in_buf, ag_ref, o_send, o_recv, rs_send, rs_recv, ag_send, ag_recv):
    step = pl.program_id(0)
    f, z, core, base, column = column_peers(n_z)
    pad, width_t = xt_ref.shape
    f32, bf16 = jnp.float32, jnp.bfloat16
    scatter, collect, spread, spread_end, gathered, own_lanes = text_tools(
        n_z, pad, width_t, f, z, lmask_ref, part_ref, mine_ref, out_buf, in_buf, rs_send, rs_recv, ag_send, ag_recv)
    home = [(base + z // 2, 2 * core + i) for i in range(2)]

    def is_here(i):
        return (z // 2 == core) & (2 * core + i == z)

    def o_push(i):
        return push(ot_ref.at[i], o_got.at[z % 2], o_send.at[i], o_recv.at[z % 2], home[i])

    @pl.when(step == 0)
    def _():
        meet(column)
        for i in range(2):
            @pl.when(is_here(i))
            def _():
                copy = pltpu.make_async_copy(ot_ref.at[i], o_got.at[z % 2], o_recv.at[z % 2])
                copy.start()
                copy.wait()

            @pl.when(jnp.logical_not(is_here(i)))
            def _():
                o_push(i).start()

    rows = o_ref.shape[0]
    width = o_ref.shape[1]


    @pl.when(step == 0)
    def _():
        to = mm_t(o_ref[...], ao_ref[...]).astype(jnp.bfloat16)
        to_out[...] = to

        def cols(n, _):
            sl = pl.ds(pl.multiple_of(n * 256, 256), 256)
            a = mm_t(o_ref[...], wo_ref[sl, :]) + mm(to_out[...], bo_ref[:, sl])
            a_out[:, sl] = a.astype(jnp.bfloat16)
            x1_out[:, sl] = x_ref[:, sl].astype(jnp.float32) + mod_ref[2:3, sl] * a
            return 0

        lax.fori_loop(0, width // 256, cols, 0)

        def norm(r, _):
            sl = pl.ds(pl.multiple_of(r * ROWS, ROWS), ROWS)
            xh, _inv = norm_rows(x1_out[sl, :])
            h2_out[sl, :] = (xh * (1.0 + mod_ref[4:5, :]) + mod_ref[3:4, :]).astype(jnp.bfloat16)
            return 0

        lax.fori_loop(0, rows // ROWS, norm, 0)
        t1_out[...] = mm_t(h2_out[...], a1_ref[...]).astype(jnp.bfloat16)
        m_acc[...] = jnp.zeros_like(m_acc)
        t2_acc[...] = jnp.zeros_like(t2_acc)

    u = mm(h2_out[...], w1_ref[...]) + mm(t1_out[...], b1_ref[...])
    u_out[...] = u
    f = gelu_parts(u)[0].astype(jnp.bfloat16)
    m_acc[...] += mm_t(f, w2_ref[...])
    t2_acc[...] += mm_t(f, a2_ref[...])


    @pl.when(step == turns[0])
    def _():
        for i in range(2):
            @pl.when(jnp.logical_not(is_here(i)))
            def _():
                push(o_got.at[i], o_got.at[i], o_send.at[i], o_recv.at[i], home[i]).wait_recv()
                o_push(i).wait_send()
        owner = owner_ref[...]
        att = jnp.where(owner > 0, o_got[0].astype(f32), jnp.where(owner < 0, o_got[1].astype(f32), 0.0)).astype(bf16)
        att_out[...] = att
        scatter(0, mm_t(att, two_ref[...]), mm_t(att, tao_ref[...]))

    @pl.when(step == turns[1])
    def _():
        modulation = rows_of(tmod_ref, own_ref)
        branch, to_mine = collect(0)
        branch = branch + mm(to_mine, tbo_ref[...])
        tbr_out[...] = branch
        x1 = xt_ref[...].astype(f32) + modulation(2) * branch
        tx1_out[...] = x1
        hat, _inv = norm_rows(x1)
        spread(ag_ref, (hat * (1.0 + modulation(4)) + modulation(3)).astype(bf16), to_mine)

    @pl.when(step == tiles - 1)
    def _():
        spread_end(ag_ref)
        tall_out[...] = ag_ref[...]

    @pl.when(step == tiles - 1)
    def _():
        t2_out[...] = t2_acc[...].astype(jnp.bfloat16)
        gate_out[...] = jnp.zeros_like(gate_out)

        def last(r, _):
            sl = pl.ds(pl.multiple_of(r * ROWS, ROWS), ROWS)
            m = m_acc[sl, :] + mm(t2_out[sl, :], b2_ref[...])
            y_out[sl, :] = (x1_out[sl, :] + mod_ref[5:6, :] * m).astype(jnp.bfloat16)
            gm = g_ref[sl, :].astype(jnp.float32) * m
            gate_out[...] += sum(gm[8 * i:8 * i + 8, :] for i in range(ROWS // 8))
            return 0

        lax.fori_loop(0, rows // ROWS, last, 0)


def both_back_kernel(tiles, n_z, turns, g_ref, x1_ref, a_ref, h2_ref, o_ref, mod_ref, u_ref, w2_ref, a2_ref, b2_ref, w1_ref, a1_ref, b1_ref,
                     wo_ref, ao_ref, bo_ref, to_ref, t1_ref, t2_ref,
                     gt_ref, tx1_ref, tbr_ref, tmod_ref, own_ref, mask_ref, lmask_ref, tall_ref, att_ref, tdm_ref, two_ref, tw1_ref, tw2_ref,
                     tao_ref, tbo_ref, ta1_ref, tb1_ref, ta2_ref, tb2_ref,
                     dx1_out, do_out, sums_out, ga2_out, gb1_out, ga1_out, gb2_out, gao_out, gbo_out,
                     ty_out, tdx1_out, tdo_out, tsums_out, tgao_out, tgbo_out, tga1_out, tgb1_out, tga2_out, tgb2_out,
                     dm_ref, dt2_ref, dh_acc, dt1_acc, part_ref, mine_ref, out_buf, in_buf, tda_ref, tdo_buf, heads_buf,
                     do_send, do_recv, rs_send, rs_recv, ag_send, ag_recv, hd_send, hd_recv, hd_own):
    step = pl.program_id(0)
    f, z, core, base, column = column_peers(n_z)
    pad, width_t = gt_ref.shape
    rank = tao_ref.shape[0]
    share = tao_ref.shape[1]
    f32, bf16 = jnp.float32, jnp.bfloat16
    scatter, collect, spread, spread_end, gathered, own_lanes = text_tools(
        n_z, pad, width_t, f, z, lmask_ref, part_ref, mine_ref, out_buf, in_buf, rs_send, rs_recv, ag_send, ag_recv)
    home = [(base + z // 2, 2 * core + i) for i in range(2)]

    def is_here(i):
        return (z // 2 == core) & (2 * core + i == z)

    def do_push(s):
        return push(tdo_buf, tdo_out.at[z % 2], do_send.at[s], do_recv.at[z % 2], home[s])

    def collapse(place, values):
        for s in range(2):
            tsums_out[2 * place + s:2 * place + s + 1, :] = jnp.sum(
                jnp.where(own_ref[...] == (1.0 if s == 0 else -1.0), values, 0.0), axis=0, keepdims=True)

    @pl.when(step == 0)
    def _():
        meet(column)
        h2_all = gathered(tall_ref, 0, width_t)
        t1 = (mm_t(h2_all, ta1_ref[...]) * mask_ref[...]).astype(bf16)
        u = mm(h2_all, tw1_ref[...]) + mm(t1, tb1_ref[...])
        act, slope = gelu_parts(u)
        act = act.astype(bf16)
        dm_all = tdm_ref[...].reshape(n_z * pad, width_t)
        dt2 = (mm_t(dm_all, tb2_ref[...]) * mask_ref[...]).astype(bf16)
        du = ((mm(dm_all, tw2_ref[...]) + mm(dt2, ta2_ref[...])) * slope).astype(bf16)
        scatter(1, mm_t(du, tw1_ref[...]), mm_t(du, tb1_ref[...]))
        scatter(0, mm_t(act, tw2_ref[...]), mm_t(act, ta2_ref[...]))
        tga2_out[...] = t_mm(dt2, act)
        tgb1_out[...] = t_mm(t1, du)

    rows, width = g_ref.shape
    bf16 = jnp.bfloat16


    @pl.when(step == 0)
    def _():
        def start(r, _):
            sl = pl.ds(pl.multiple_of(r * ROWS, ROWS), ROWS)
            dm_ref[sl, :] = (mod_ref[5:6, :] * g_ref[sl, :].astype(jnp.float32)).astype(bf16)
            return 0

        lax.fori_loop(0, rows // ROWS, start, 0)
        dt2_ref[...] = mm_t(dm_ref[...], b2_ref[...]).astype(bf16)
        gb2_out[...] = t_mm(t2_ref[...], dm_ref[...])
        dh_acc[...] = jnp.zeros_like(dh_acc)
        dt1_acc[...] = jnp.zeros_like(dt1_acc)

    act, slope = gelu_parts(u_ref[...])
    df = mm(dm_ref[...], w2_ref[...]) + mm(dt2_ref[...], a2_ref[...])
    ga2_out[...] = t_mm(dt2_ref[...], act.astype(bf16))
    du = (df * slope).astype(bf16)
    gb1_out[...] = t_mm(t1_ref[...], du)
    dh_acc[...] += mm_t(du, w1_ref[...])
    dt1_acc[...] += mm_t(du, b1_ref[...])


    @pl.when(step == turns[0])
    def _():
        modulation = rows_of(tmod_ref, own_ref)
        dh, dt1_mine = collect(1)
        dh = dh + mm(dt1_mine, ta1_ref[...])
        hat, inverse = norm_rows(tx1_ref[...])
        dz = dh * (1.0 + modulation(4))
        dx1 = gt_ref[...].astype(f32) + inverse * (
            dz - jnp.mean(dz, axis=-1, keepdims=True) - hat * jnp.mean(dz * hat, axis=-1, keepdims=True))
        feed, t2_mine = collect(0)
        spread(tda_ref, (modulation(2) * dx1).astype(bf16), dt1_mine, t2_mine)
        tdx1_out[...] = dx1
        collapse(0, dx1 * tbr_ref[...])
        collapse(1, dh)
        collapse(2, dh * hat)
        feed = feed + mm(t2_mine, tb2_ref[...])
        ty_out[...] = (tx1_ref[...] + modulation(5) * feed).astype(bf16)
        collapse(3, gt_ref[...].astype(f32) * feed)

    @pl.when(step == turns[1])
    def _():
        spread_end(tda_ref)
        da_all = gathered(tda_ref, 0, width_t)
        dt1 = gathered(tda_ref, width_t, rank)
        t2 = gathered(tda_ref, width_t + rank, rank)
        dto = (mm_t(da_all, tbo_ref[...]) * mask_ref[...]).astype(bf16)
        tdo_buf[...] = (mm(da_all, two_ref[...]) + mm(dto, tao_ref[...])).astype(bf16)
        for s in range(2):
            @pl.when(is_here(s))
            def _():
                copy = pltpu.make_async_copy(tdo_buf, tdo_out.at[z % 2], do_recv.at[z % 2])
                copy.start()
                copy.wait()

            @pl.when(jnp.logical_not(is_here(s)))
            def _():
                do_push(s).start()
        tgao_out[...] = t_mm(dto, att_ref[...])
        tgbo_out[...] = t_mm(gathered(tall_ref, width_t, rank), own_lanes(tda_ref, share))
        tgb2_out[...] = t_mm(t2, own_lanes(tdm_ref, share))
        tga1_out[...] = t_mm(dt1, own_lanes(tall_ref, share))

    @pl.when(step == tiles - 1)
    def _():
        dt1 = dt1_acc[...].astype(bf16)
        dt2_ref[...] = dt1
        ga1_out[...] = t_mm(dt1, h2_ref[...])
        sums_out[...] = jnp.zeros_like(sums_out)

        def last(r, _):
            sl = pl.ds(pl.multiple_of(r * ROWS, ROWS), ROWS)
            dh = dh_acc[sl, :] + mm(dt2_ref[sl, :], a1_ref[...])
            xh, inverse = norm_rows(x1_ref[sl, :])
            dz = dh * (1.0 + mod_ref[4:5, :])
            dx1 = g_ref[sl, :].astype(jnp.float32) + inverse * (
                dz - jnp.mean(dz, axis=-1, keepdims=True) - xh * jnp.mean(dz * xh, axis=-1, keepdims=True))
            dx1_out[sl, :] = dx1
            dm_ref[sl, :] = (mod_ref[2:3, :] * dx1).astype(bf16)
            fold = lambda v: sum(v[8 * i:8 * i + 8, :] for i in range(ROWS // 8))
            sums_out[0:8, :] += fold(dx1 * a_ref[sl, :].astype(jnp.float32))
            sums_out[8:16, :] += fold(dh)
            sums_out[16:24, :] += fold(dh * xh)
            return 0

        lax.fori_loop(0, rows // ROWS, last, 0)
        dto = mm_t(dm_ref[...], bo_ref[...]).astype(bf16)
        dt2_ref[...] = dto
        gao_out[...] = t_mm(dto, o_ref[...])
        gbo_out[...] = t_mm(to_ref[...], dm_ref[...])

        per_half = width // 512

        def cols(n, _):
            sl = pl.ds(pl.multiple_of(n * 256, 256), 256)
            into = pl.ds(pl.multiple_of(n % per_half * 256, 256), 256)
            heads_buf[n // per_half, :, into] = (mm(dm_ref[...], wo_ref[:, sl]) + mm(dt2_ref[...], ao_ref[:, sl])).astype(bf16)
            return 0

        lax.fori_loop(0, width // 256, cols, 0)
        partner = base + 1 - core
        swap = push(heads_buf.at[1 - core], do_out.at[core], hd_send, hd_recv, (partner, z))
        swap.start()
        keep = pltpu.make_async_copy(heads_buf.at[core], do_out.at[core], hd_own)
        keep.start()
        keep.wait()
        swap.wait_send()
        push(heads_buf.at[0], do_out.at[1 - core], hd_send, hd_recv, (partner, z)).wait_recv()

    @pl.when(step == tiles - 1)
    def _():
        for i in range(2):
            @pl.when(jnp.logical_not(is_here(i)))
            def _():
                push(tdo_out.at[i], tdo_out.at[i], do_send.at[i], do_recv.at[i], home[i]).wait_recv()
                do_push(i).wait_send()


def both_fwd(o, x, g, mod, wo, pair_o, pair_1, w1, pair_2, w2, ot, xt, tmod, owner, own, lmask, two, tpair_o, n_z, cid, tn=512, turns=(2, 7)):
    rows, width = o.shape
    hidden = w1.shape[1]
    tiles = hidden // tn
    rank = pair_o[0].shape[0]
    once = lambda shape: pl.BlockSpec(shape, lambda n: (0,) * len(shape), pipeline_mode=pl.Buffered(1))
    whole = once
    tile = lambda height: pl.BlockSpec((height, tn), lambda n: (0, n))
    f32, bf16 = jnp.float32, jnp.bfloat16
    shape, vmem, dma = jax.ShapeDtypeStruct, pltpu.VMEM, pltpu.SemaphoreType.DMA
    act = (rows, width)
    pad = xt.shape[0]
    total, share = n_z * pad, two.shape[1]
    thick = tpair_o[0].shape[0]
    wide = width + thick
    texts = (xt, tmod, owner, own, lmask, two, *tpair_o)
    return pl.pallas_call(
        functools.partial(both_fwd_kernel, tiles, n_z, turns),
        grid=(tiles,),
        in_specs=[once(act), once(act), once(act), once(mod.shape), once((width, width)), once((rank, width)), once((rank, width)),
                  once((rank, width)), tile(rank), tile(width), tile(rank), tile(width), once((rank, width)),
                  pl.BlockSpec(memory_space=pl.ANY)] + [once(v.shape) for v in texts],
        out_specs=[whole(act), whole(act), whole(act), tile(rows), whole(act), whole((rows, rank)), whole((rows, rank)),
                   whole((rows, rank)), whole((8, width)), whole((n_z, pad, wide)), whole((total, share)), whole((pad, width)),
                   whole((pad, width))],
        out_shape=[shape(act, bf16), shape(act, f32), shape(act, bf16), shape((rows, hidden), f32), shape(act, bf16)]
        + [shape((rows, rank), bf16)] * 3
        + [shape((8, width), f32), shape((n_z, pad, wide), bf16), shape((total, share), bf16), shape((pad, width), f32),
           shape((pad, width), f32)],
        scratch_shapes=[vmem(act, f32), vmem((rows, rank), f32), vmem((2, total, share), bf16), vmem((n_z, pad, wide), f32), vmem((1, pad, wide), f32),
                        vmem((1, n_z, pad, wide), bf16), vmem((1, n_z, pad, wide), bf16), vmem((n_z, pad, wide), bf16),
                        dma((2,)), dma((2,)), dma((1, n_z)), dma((1, n_z)), dma((n_z,)), dma((n_z,))],
        compiler_params=pltpu.CompilerParams(collective_id=cid, has_side_effects=True, vmem_limit_bytes=60 * 1024 * 1024),
        name="block_forward",
    )(o, x, g, mod, wo, *pair_o, pair_1[0], pair_1[1], w1, pair_2[0], w2, pair_2[1], ot, *texts)


def both_back(g, x1, a, h2, o, mod, u, w2, pair_2, w1, pair_1, wo, pair_o, mids,
              gt, tx1, tbr, tmod, own, mask, lmask, tall, att, tdm, two, tw1, tw2, tpair_o, tpair_1, tpair_2, n_z, cid, tn=512, turns=(8, 11)):
    rows, width = o.shape
    hidden = w1.shape[1]
    tiles = hidden // tn
    rank = pair_o[0].shape[0]
    once = lambda shape: pl.BlockSpec(shape, lambda n: (0,) * len(shape), pipeline_mode=pl.Buffered(1))
    whole = once
    tile = lambda height: pl.BlockSpec((height, tn), lambda n: (0, n))
    f32, bf16 = jnp.float32, jnp.bfloat16
    shape, vmem, dma = jax.ShapeDtypeStruct, pltpu.VMEM, pltpu.SemaphoreType.DMA
    act = (rows, width)
    side = (rank, width)
    thin = (rows, rank)
    pad = gt.shape[0]
    total, share = n_z * pad, two.shape[1]
    thick = tpair_o[0].shape[0]
    t_hidden = tw1.shape[1]
    wide = width + thick
    texts = (gt, tx1, tbr, tmod, own, mask, lmask, tall, att, tdm, two, tw1, tw2, *tpair_o, *tpair_1, *tpair_2)
    return pl.pallas_call(
        functools.partial(both_back_kernel, tiles, n_z, turns),
        grid=(tiles,),
        in_specs=[once(act)] * 5 + [once(mod.shape), tile(rows), tile(width), tile(rank), once(side), tile(width), once(side), tile(rank),
                  once((width, width)), once(side), once(side)] + [once(thin)] * 3 + [once(v.shape) for v in texts],
        out_specs=[whole(act), pl.BlockSpec(memory_space=pl.ANY), whole((24, width)), tile(rank), tile(rank)] + [whole(side)] * 4
        + [whole((pad, width)), whole((pad, width)), pl.BlockSpec(memory_space=pl.ANY), whole((8, width)), whole((thick, share)),
           whole((thick, share)), whole((thick, share)), whole((thick, t_hidden)), whole((thick, t_hidden)), whole((thick, share))],
        out_shape=[shape(act, f32), shape((2, rows, width // 2), bf16), shape((24, width), f32)] + [shape((rank, hidden), f32)] * 2 + [shape(side, f32)] * 4
        + [shape((pad, width), bf16), shape((pad, width), f32), shape((2, total, share), bf16), shape((8, width), f32),
           shape((thick, share), f32), shape((thick, share), f32), shape((thick, share), f32), shape((thick, t_hidden), f32),
           shape((thick, t_hidden), f32), shape((thick, share), f32)],
        scratch_shapes=[vmem(act, bf16), vmem(thin, bf16), vmem(act, f32), vmem(thin, f32),
                        vmem((n_z, pad, wide), f32), vmem((2, pad, wide), f32), vmem((2, n_z, pad, wide), bf16), vmem((2, n_z, pad, wide), bf16),
                        vmem((n_z, pad, wide + thick), bf16), vmem((total, share), bf16), vmem((2, rows, width // 2), bf16),
                        dma((2,)), dma((2,)), dma((2, n_z)), dma((2, n_z)), dma((n_z,)), dma((n_z,)), dma, dma, dma],
        compiler_params=pltpu.CompilerParams(collective_id=cid, has_side_effects=True, vmem_limit_bytes=60 * 1024 * 1024),
        name="block_backward",
    )(g, x1, a, h2, o, mod, u, w2, pair_2[0], pair_2[1], w1, pair_1[0], pair_1[1], wo, *pair_o, *mids, *texts)


def flip_bits(chip, mask, nbits):
    other = 0
    for bit in range(nbits):
        have = (chip // (1 << bit)) % 2
        other = other + (1 - have if (mask >> bit) & 1 else have) * (1 << bit)
    return other


def tail_kernel(n_f, n_z, fans, cols, *refs):
    it = iter(refs)
    take = lambda count: [next(it) for _ in range(count)]
    dq_in, tdq_in, wq_ref = take(3)
    (x_ref, dx1_ref, h_ref, imod_ref, mid_ref, qa_ref, qb_ref, isum_ref, igate_ref, tx_ref, tdx1_ref, th_ref, tmodr_ref, owner_ref,
     own_ref, lmask_ref, tmid_ref, twq_ref, tqa_ref, tqb_ref, tsum_ref) = take(21)
    early_ref, = take(1)
    txt_a, txt_b = take(3), take(3)
    hot4_ref, hot2_ref, wmod_ref, bmod_ref, tmod_ref, cond_ref, smask_ref = take(7)
    grad_out, tgrad_out, cond_out, rank_out, shard_out = take(5)
    (dq_ref, wtile, dh_ref, dt_ref, grad_ref, gaq_ref, gbq_ref, tgot, part_ref, mine_ref, out_buf, in_buf, dt_ag, tgb_ref, dmod_ref,
     isums) = take(16)
    zmsg, zgot, dense, snd1, rcv1, snd2, rcv2, dgot, own_dm, all_dm, cpart, cgot, zsum, zall, dts = take(15)
    (g_send, g_recv, z_send, z_recv, c_send, c_recv, s_send, s_recv, d_send, d_recv, f_send, f_recv, p_send, p_recv,
     q_send, q_recv, t_send, t_recv, dq_send, dq_recv, dq_own, w_sem, h_send, h_recv, rs_send, rs_recv, ag_send, ag_recv) = take(28)
    f32, bf16 = jnp.float32, jnp.bfloat16
    f, z, core, base, column = column_peers(n_z)
    chip = f // 2
    chips = n_f // 2
    nbits = bits_of(chips)
    partner = base + 1 - core
    around = [((f + j) % n_f, z) for j in range(1, n_f)]
    others = [(flip_bits(chip, mask, nbits) * 2 + side, z) for mask in range(1, chips) for side in range(2)]
    meet(column + others)
    ring = ZRing(f, z, n_z)
    blk = shard_out.shape[0]
    hidden_rank = hot2_ref.shape[0]

    home = [(base + z // 2, 2 * core + i) for i in range(2)]

    def is_here(i):
        return (z // 2 == core) & (2 * core + i == z)

    swap = push(dq_in.at[1 - core], dq_ref.at[core], dq_send, dq_recv, (partner, z))
    swap.start()
    keep = pltpu.make_async_copy(dq_in.at[core], dq_ref.at[core], dq_own)
    keep.start()

    def t_push(i):
        return push(tdq_in.at[i], tgot.at[z % 2], h_send.at[i], h_recv.at[z % 2], home[i])

    for i in range(2):
        @pl.when(is_here(i))
        def _():
            copy = pltpu.make_async_copy(tdq_in.at[i], tgot.at[z % 2], h_recv.at[z % 2])
            copy.start()
            copy.wait()

        @pl.when(jnp.logical_not(is_here(i)))
        def _():
            t_push(i).start()

    pad, width = tx_ref.shape
    thick = tqa_ref.shape[0]
    scatter, collect, spread, spread_end, gathered, own_lanes = text_tools(
        n_z, pad, width, f, z, lmask_ref, part_ref, mine_ref, out_buf, in_buf, rs_send, rs_recv, ag_send, ag_recv)
    tn = wtile.shape[3]
    per_half = dq_ref.shape[2] // tn

    def tile_of(n):
        side = core if n < per_half else 1 - core
        return side, side * per_half + n % per_half

    def tile_load(n):
        at = pl.ds(pl.multiple_of(tile_of(n)[1] * tn, 128), tn)
        return pltpu.make_async_copy(wq_ref.at[:, :, at], wtile.at[n % 2], w_sem.at[n % 2])

    def tile_back(n):
        if n + 1 < 2 * per_half:
            tile_load(n + 1).start()
        tile_load(n).wait()
        side, number = tile_of(n)
        at = pl.ds(pl.multiple_of(number * tn, 128), tn)
        part = dq_ref[side, :, n % per_half * tn:(n % per_half + 1) * tn]
        main = mm_t(part, wtile[n % 2].reshape(width, tn))
        thin = mm_t(part, qb_ref[:, at])
        if n == 0:
            dh_ref[...] = main
            dt_ref[...] = thin
        else:
            dh_ref[...] += main
            dt_ref[...] += thin
        gbq_ref[:, at] = t_mm(mid_ref[...], part)

    tile_load(0).start()
    keep.wait()
    for n in range(per_half):
        tile_back(n)

    for i in range(2):
        @pl.when(jnp.logical_not(is_here(i)))
        def _():
            push(tgot.at[i], tgot.at[i], h_send.at[i], h_recv.at[i], home[i]).wait_recv()
            t_push(i).wait_send()
    owner = owner_ref[...]
    tdq = jnp.where(owner > 0, tgot[0].astype(f32), jnp.where(owner < 0, tgot[1].astype(f32), 0.0)).astype(bf16)
    scatter(0, mm_t(tdq, twq_ref[...]), mm_t(tdq, tqb_ref[...]))
    tgb_ref[...] = t_mm(tmid_ref[...], tdq)

    push(dq_in.at[1 - core], dq_ref.at[1 - core], dq_send, dq_recv, (partner, z)).wait_recv()
    for n in range(per_half, 2 * per_half):
        tile_back(n)
    dt_low = dt_ref[...].astype(bf16)
    gaq_ref[...] = t_mm(dt_low, h_ref[...])

    spans = {}
    offset = 0
    for part, count, name in ((gaq_ref, fans[1] // n_z, (0, 1)), (gbq_ref, cols[1] // n_z, (1, 1))):
        for t in range(n_z):
            zmsg[t, :, offset:offset + count] = part[:, t * count:(t + 1) * count].astype(bf16)
        spans[name] = (offset, count)
        offset += count
    ring.start(lambda to: zmsg.at[to], zgot, z_send, z_recv)
    zgot[z] = zmsg[z]
    offset = 0
    for side, sizes in ((0, fans), (1, cols)):
        for index in range(2, 5):
            spans[side, index] = (offset, sizes[index] // n_z)
            offset += sizes[index] // n_z

    isums[...] = jnp.zeros_like(isums)
    quarter = grad_ref.shape[1]
    dh_ref[...] += mm(dt_low, qa_ref[...])
    for i in range(2):
        def last(r, _):
            sl = pl.ds(pl.multiple_of(i * quarter + r * ROWS, ROWS), ROWS)
            dh = dh_ref[sl, :]
            xh, inverse = norm_rows(x_ref[sl, :].astype(f32))
            dz = dh * (1.0 + imod_ref[1:2, :])
            dx = dx1_ref[sl, :] + inverse * (
                dz - jnp.mean(dz, axis=-1, keepdims=True) - xh * jnp.mean(dz * xh, axis=-1, keepdims=True))
            grad_ref[i, pl.ds(pl.multiple_of(r * ROWS, ROWS), ROWS), :] = dx.astype(bf16)
            fold = lambda v: sum(v[8 * j:8 * j + 8, :] for j in range(ROWS // 8))
            isums[0:8, :] += fold(dh)
            isums[8:16, :] += fold(dh * xh)
            return 0

        lax.fori_loop(0, quarter // ROWS, last, 0)

    pick = rows_of(tmodr_ref, own_ref)
    tdh, tdt = collect(0)
    spread(dt_ag, tdt)
    tdh = tdh + mm(tdt, tqa_ref[...])
    hat, inverse = norm_rows(tx_ref[...].astype(f32))
    dz = tdh * (1.0 + pick(1))
    tgrad_out[...] = tdx1_ref[...] + inverse * (
        dz - jnp.mean(dz, axis=-1, keepdims=True) - hat * jnp.mean(dz * hat, axis=-1, keepdims=True))

    def total_of(v):
        return jnp.sum(v, axis=0, keepdims=True)

    rows_img = [total_of(isums[0:8, :]), total_of(isums[8:16, :])]
    rows_img += [total_of(isum_ref[8 * p:8 * p + 8, :]) for p in range(3)] + [total_of(igate_ref[...])]
    rows_txt = []
    for s in range(2):
        chosen = own_ref[...] == (1.0 if s == 0 else -1.0)
        rows_txt.append([total_of(jnp.where(chosen, tdh, 0.0)), total_of(jnp.where(chosen, tdh * hat, 0.0))]
                        + [tsum_ref[2 * p + s:2 * p + s + 1, :] for p in range(4)])
    dmod_ref[...] = jnp.zeros_like(dmod_ref)
    chunk = dmod_ref.shape[-1]
    per_row = width // chunk
    per_block = 6 * per_row // n_z
    for r, parts in enumerate([rows_img] + rows_txt):
        for q in range(6 * per_row):
            dmod_ref[q // per_block, r, q % per_block:q % per_block + 1, :] = (
                parts[q // per_row][:, q % per_row * chunk:(q % per_row + 1) * chunk])

    def dmod_copy(index, peer):
        return push(dmod_ref.at[peer[1]], dgot.at[core * n_z + z], d_send.at[index], d_recv.at[core * n_z + z], peer)

    for index, peer in enumerate(column):
        dmod_copy(index, peer).start()
    dgot[core * n_z + z] = dmod_ref[z]

    hot2, hot4 = hot2_ref[...], hot4_ref[...]
    starts = []
    offset = 0
    for stream in range(2):
        for index in range(5):
            starts.append((stream, index, offset, offset + fans[index] // n_z))
            offset += fans[index] // n_z + cols[index] // n_z

    def put_a(at, part, hot):
        dense[at:at + part.shape[1], :] = dots(part, hot, 0, 0)

    def put_b(at, part, hot):
        full = dots(hot, part, 0, 0)
        blocks = part.shape[1] // 128
        for j in range(blocks):
            dense[pl.ds(at + j, 128, stride=blocks), :] = full[:, j * 128:(j + 1) * 128]

    def put_image(index, ref):
        for side, put in ((0, put_a), (1, put_b)):
            begin, count = spans[side, index]
            put(starts[index][2 + side], ref[:, :, begin:begin + count].reshape(hot4.shape[0], count), hot4)

    for index in range(2, 5):
        put_image(index, early_ref)
        put_a(starts[5 + index][2], txt_a[index - 2][:hidden_rank, :].astype(bf16), hot2)
        put_b(starts[5 + index][3], txt_b[index - 2][:hidden_rank, :].astype(bf16), hot2)

    for index, peer in enumerate(column):
        place = peer[0] % 2 * n_z + peer[1]
        push(dgot.at[place], dgot.at[place], d_send.at[index], d_recv.at[place], peer).wait_recv()
    rows = []
    for slot in range(2):
        rows.append(dgot[2 * core + slot, 0] + dgot[n_z + 2 * core + slot, 0])
    for slot in range(2):
        total = dgot[core * n_z, 1 + slot]
        for t in range(1, n_z):
            total = total + dgot[core * n_z + t, 1 + slot]
        rows.append(total)
    own_dm[...] = jnp.zeros_like(own_dm)
    for r, total in enumerate(rows):
        for j in range(own_dm.shape[1] // chunk):
            own_dm[r:r + 1, j * chunk:(j + 1) * chunk] = total[j:j + 1, :].astype(bf16).astype(f32)
    for j in range(1, n_f):
        push(own_dm, all_dm.at[f], f_send.at[j], f_recv.at[f], around[j - 1]).start()
    all_dm[f] = own_dm[...]
    dm_low = own_dm[...].astype(bf16)
    tmod = [tmod_ref[s].astype(bf16) for s in range(2)]
    gb_mod = [t_mm(tmod[s], dm_low) for s in range(2)]
    rank_img = mm_t(dm_low, bmod_ref[0])
    rank_txt = mm_t(dm_low, bmod_ref[1])
    row = lax.broadcasted_iota(jnp.int32, rank_img.shape, 0)
    rank_part = jnp.where(row < 2, rank_img, rank_txt)

    spread_end(dt_ag)
    tga = t_mm(gathered(dt_ag, 0, thick), own_lanes(th_ref, cols[2] // n_z))
    for stream, index, at_a, at_b in starts:
        if index == 0:
            dense[at_a:at_b, :] = jnp.zeros((at_b - at_a, 128), f32)
            put_b(at_b, gb_mod[stream].astype(bf16), hot2)
        elif index == 1 and stream == 1:
            put_a(at_a, tga[:hidden_rank].astype(bf16), hot2)
            put_b(at_b, tgb_ref[:hidden_rank, :].astype(bf16), hot2)
    ring.wait(zgot, z_send, z_recv)
    put_image(1, zgot)

    for i in range(2):
        @pl.when(is_here(i))
        def _():
            pltpu.make_async_copy(grad_ref.at[i], grad_out.at[z % 2], g_recv.at[z % 2]).start()

        @pl.when(jnp.logical_not(is_here(i)))
        def _():
            push(grad_ref.at[i], grad_out.at[z % 2], g_send.at[i], g_recv.at[z % 2], home[i]).start()

    def block(number):
        return pl.ds(pl.multiple_of(number * blk, 16), blk)

    for p in range(chips):
        snd1[p] = dense[block(2 * p + 1 - core), :].astype(bf16)
        push(snd1.at[p], rcv1.at[p], c_send.at[p], c_recv.at[p], (partner, z)).start()

    for j in range(1, n_f):
        came = (f - j + n_f) % n_f
        push(own_dm, all_dm.at[came], f_send.at[j], f_recv.at[came], (came, z)).wait_recv()
    everyone = all_dm[...].reshape(n_f * 8, own_dm.shape[1]).astype(bf16)
    part = mm_t(everyone, wmod_ref[0]) + pltpu.roll(mm_t(everyone, wmod_ref[1]), n_f * 8 - 2, 0)
    k_local = part.shape[1]
    cpart[...] = jnp.zeros_like(cpart)
    cpart[:, :, :k_local] = part.reshape(n_f, 8, k_local)
    for j in range(1, n_f):
        to = (f + j) % n_f
        push(cpart.at[to], cgot.at[f], p_send.at[j], p_recv.at[f], (to, z)).start()
    cgot[f] = cpart[f]

    for p in range(chips):
        push(snd1.at[p], rcv1.at[p], c_send.at[p], c_recv.at[p], (partner, z)).wait_recv()

    def mine_of(p):
        return block(2 * p + core)

    for p in range(chips):
        dense[mine_of(p), :] += rcv1[p].astype(f32)

    half = blk // 2
    orders = [list(range(nbits)), list(range(nbits))[::-1]]

    def masks_at(side, turn):
        left = orders[side][turn:]
        return [sum(1 << b for i, b in enumerate(left) if (m >> i) & 1) for m in range(1 << len(left))]

    def rs_copy(side, turn, index):
        slot = turn * 2 + index
        peer = flip_bits(chip, 1 << orders[side][turn], nbits) * 2 + core
        return push(snd2.at[side, slot], rcv2.at[side, slot], s_send.at[side, slot], s_recv.at[side, slot], (peer, z))

    def half_of(number, side):
        return pl.ds(pl.multiple_of((2 * number + core) * blk + side * half, 16), half)

    def rs_start(turn):
        for side in range(2):
            bit = 1 << orders[side][turn]
            for index, mask in enumerate(masks_at(side, turn + 1)):
                number = flip_bits(chip, bit | mask, nbits)
                snd2[side, turn * 2 + index] = dense[half_of(number, side), :].astype(bf16)
                rs_copy(side, turn, index).start()

    def rs_end(turn):
        for side in range(2):
            for index, mask in enumerate(masks_at(side, turn + 1)):
                number = flip_bits(chip, mask, nbits)
                rs_copy(side, turn, index).wait_recv()
                dense[half_of(number, side), :] += rcv2[side, turn * 2 + index].astype(f32)

    rs_start(0)

    for j in range(1, n_f):
        came = (f - j + n_f) % n_f
        push(cpart.at[came], cgot.at[came], p_send.at[j], p_recv.at[came], (came, z)).wait_recv()
    zsum[:n_f] = cgot[...]
    zsum[n_f] = jnp.zeros(zsum.shape[1:], f32)
    zsum[n_f, :, :hidden_rank] = rank_part
    zall[z] = zsum[...]
    ring.start(lambda to: zsum, zall, q_send, q_recv)
    ring.wait(zall, q_send, q_recv)
    total = zall[0]
    for t in range(1, n_z):
        total = total + zall[t]
    cond_out[...] = total[:n_f]
    dt = (total[n_f][:, :hidden_rank] * smask_ref[...]).astype(bf16)
    rank_out[...] = dt.astype(f32)
    wide = mm(dt, hot2)
    dts[f] = wide
    for j in range(1, n_f):
        push(dts.at[f], dts.at[f], t_send.at[j], t_recv.at[f], around[j - 1]).start()

    rs_end(0)
    if nbits > 1:
        rs_start(1)
    for j in range(1, n_f):
        came = (f - j + n_f) % n_f
        push(dts.at[came], dts.at[came], t_send.at[j], t_recv.at[came], (came, z)).wait_recv()
    all_dt = dts[...].reshape(n_f * 8, 128)
    row = lax.broadcasted_iota(jnp.int32, all_dt.shape, 0) % 8
    act = cond_ref[...].reshape(n_f * 8, cond_ref.shape[-1]).astype(bf16)
    mod_a = [
        dots(act, jnp.where(row < 2, all_dt, 0.0).astype(bf16), 0, 0),
        dots(act, pltpu.roll(jnp.where((row >= 2) & (row < 4), all_dt, 0.0), n_f * 8 - 2, 0).astype(bf16), 0, 0),
    ]
    if nbits > 1:
        rs_end(1)
    shard_out[...] = dense[block(f), :]
    for stream in range(2):
        first = starts[5 * stream][2]
        own = jnp.where(f == first // blk, 1.0, 0.0)
        count = mod_a[stream].shape[0]
        shard_out[:count, :] += own * mod_a[stream]

    swap.wait_send()
    ring.drain(lambda to: zmsg.at[to], zgot, z_send, z_recv)
    ring.drain(lambda to: zsum, zall, q_send, q_recv)
    for index, peer in enumerate(column):
        dmod_copy(index, peer).wait_send()
    for j in range(1, n_f):
        to = (f + j) % n_f
        push(own_dm, all_dm.at[f], f_send.at[j], f_recv.at[f], (to, z)).wait_send()
        push(cpart.at[to], cgot.at[f], p_send.at[j], p_recv.at[f], (to, z)).wait_send()
        push(dts.at[f], dts.at[f], t_send.at[j], t_recv.at[f], (to, z)).wait_send()
    for p in range(chips):
        push(snd1.at[p], rcv1.at[p], c_send.at[p], c_recv.at[p], (partner, z)).wait_send()
    for turn in range(nbits):
        for side in range(2):
            for index in range(len(masks_at(side, turn + 1))):
                rs_copy(side, turn, index).wait_send()
    for i in range(2):
        @pl.when(is_here(i))
        def _():
            pltpu.make_async_copy(grad_ref.at[i], grad_out.at[z % 2], g_recv.at[z % 2]).wait()

        @pl.when(jnp.logical_not(is_here(i)))
        def _():
            push(grad_out.at[i], grad_out.at[i], g_send.at[i], g_recv.at[i], home[i]).wait_recv()
            push(grad_ref.at[i], grad_out.at[z % 2], g_send.at[i], g_recv.at[z % 2], home[i]).wait_send()


def tail(dq, tdq, wq, smalls, early, txt_a, txt_b, hot4, hot2, wmod, bmod, tmod, cond, smask, n_f, n_z, fans, cols, cid, tn=768):
    f32, bf16 = jnp.float32, jnp.bfloat16
    vmem, dma = pltpu.VMEM, pltpu.SemaphoreType.DMA
    shape = jax.ShapeDtypeStruct
    args = (dq, tdq, wq, *smalls, early, *txt_a, *txt_b, hot4, hot2, wmod, bmod, tmod, cond, smask)
    lanes = (fans[1] + cols[1]) // n_z
    rows = 2 * (sum(fans) + sum(cols)) // n_z
    blk = rows // n_f
    chips = n_f // 2
    cut = cols[0] // n_z
    rank = hot2.shape[0]
    _, img_rows, half = dq.shape
    _, k_local, _ = wq.shape
    width = cols[2]
    tx = smalls[9]
    thick = smalls[18].shape[0]
    pad = tx.shape[0]
    wide = width + thick
    inside, outside = pl.BlockSpec(memory_space=vmem), pl.BlockSpec(memory_space=pl.ANY)
    return pl.pallas_call(
        functools.partial(tail_kernel, n_f, n_z, tuple(fans), tuple(cols)),
        out_shape=[shape((2, img_rows // 2, width), bf16), shape((pad, width), f32), shape((n_f, 8, 256), f32), shape((8, rank), f32),
                   shape((blk, 128), f32)],
        in_specs=[outside] * 3 + [inside] * (len(args) - 3),
        out_specs=[outside] + [inside] * 4,
        scratch_shapes=[
            vmem((2, img_rows, half), bf16), vmem((2, n_f, k_local, tn), bf16), vmem((img_rows, width), f32), vmem((img_rows, RANK), f32),
            vmem((2, img_rows // 2, width), bf16), vmem((RANK, fans[1]), f32), vmem((RANK, cols[1]), f32), vmem(tdq.shape, bf16),
            vmem((n_z, pad, wide), f32), vmem((1, pad, wide), f32), vmem((1, n_z, pad, wide), bf16), vmem((1, n_z, pad, wide), bf16),
            vmem((n_z, pad, thick), bf16), vmem((thick, cols[1] // n_z), f32), vmem((n_z, 3, 8, width // n_z), f32), vmem((16, width), f32),
            vmem((n_z, RANK, lanes), bf16), vmem((n_z, RANK, lanes), bf16), vmem((rows, 128), f32),
            vmem((chips, blk, 128), bf16), vmem((chips, blk, 128), bf16),
            vmem((2, 3, blk // 2, 128), bf16), vmem((2, 3, blk // 2, 128), bf16),
            vmem((2 * n_z, 3, 8, width // n_z), f32), vmem((8, cut), f32), vmem((n_f, 8, cut), f32),
            vmem((n_f, 8, 256), f32), vmem((n_f, 8, 256), f32), vmem((n_f + 1, 8, 256), f32),
            vmem((n_z, n_f + 1, 8, 256), f32), vmem((n_f, 8, 128), f32),
            dma((2,)), dma((2,)), dma((n_z,)), dma((n_z,)), dma((chips,)), dma((chips,)), dma((2, 3)), dma((2, 3)),
            dma((2 * n_z,)), dma((2 * n_z,)), dma((n_f,)), dma((n_f,)), dma((n_f,)), dma((n_f,)), dma((n_z,)), dma((n_z,)),
            dma((n_f,)), dma((n_f,)), dma, dma, dma, dma((2,)), dma((2,)), dma((2,)), dma((1, n_z)), dma((1, n_z)), dma((n_z,)), dma((n_z,)),
        ],
        compiler_params=pltpu.CompilerParams(collective_id=cid, has_side_effects=True, vmem_limit_bytes=60 * 1024 * 1024),
        name="gradient_exchange",
    )(*args)

FULL = 4
PART = 4


def front_kernel(n_f, n_z, fans, cols, *refs):
    it = iter(refs)
    take = lambda count: [next(it) for _ in range(count)]
    ins = take(FULL + PART + 1)
    (x_ref, g_ref, picks_ref, hot2_ref, cblk_ref, clane_ref, c8_ref, smask_ref, wmod_ref, xt_ref, gt_ref, own_ref, tmask_ref, sign_ref) = take(14)
    outs = take(FULL + PART)
    x_out, g_out, imod_out, tmod_out = take(4)
    img_a, img_b, txt_a, txt_b = take(4), take(4), take(4), take(4)
    moda_out, modb_out, midm_out, cond_out, dm_out = take(5)
    ot_out, lse_out, bias_out, hot4_out = take(4)
    h_out, mid_out, heads_out, th_out, tmid_out, theads_out, att_out = take(7)
    (row_ref, fl_ref, img_msg, img_got, txt_msg, txt_got, cgot, mpart, mgot, own_mod, mod_got, wtile, wtxt, stage, tq_ref, sign_got, hot_got, img_buf, txt_buf, o_stage) = take(20)
    (z_send, z_recv, xy_send, xy_recv, core_send, core_recv, own_sem, x_send, x_recv, g_send, g_recv, c_send, c_recv, l_send,
     l_recv, m_send, m_recv, i_send, i_recv, t_send, t_recv, d_send, d_recv, a_send, a_recv, w_sem, tw_sem, h_send, h_recv,
     h_sem, q_send, q_recv, dm_send, dm_recv, s_send, s_recv, b_sem, o_send, o_recv, o_sem) = take(40)
    f32, bf16 = jnp.float32, jnp.bfloat16
    f, z, core, base, column = column_peers(n_z)
    chip = f // 2
    chips = n_f // 2
    nbits = bits_of(chips)
    partner = base + 1 - core
    others = [(flip_bits(chip, mask, nbits) * 2 + side, z) for mask in range(1, chips) for side in range(2)]
    meet(column + others)
    ring = ZRing(f, z, n_z)
    total = FULL + PART + 1
    adapters = total - 1
    blk = ins[adapters].shape[0]
    width = x_ref.shape[2]
    rank2 = hot2_ref.shape[0]

    def peer_of(mask):
        return flip_bits(chip, mask, nbits) * 2 + core

    def wide_of(m):
        return ins[m].shape[-1]

    def cuts(m):
        if m == adapters:
            return [(0, (0, blk // 2)), (1, (blk // 2, blk // 2))]
        parts = halves(wide_of(m))
        if m % FULL == 1:
            parts = [(0, parts[1][1]), (parts[1][1], parts[0][1])]
        return list(enumerate(parts))

    def place(m, who, zz, cut):
        off, w = cut
        if m == adapters:
            return row_ref.at[pl.ds(pl.multiple_of(who * blk + off, 16), w), :]
        if m < FULL:
            return outs[m].at[who, :, pl.ds(pl.multiple_of(zz * wide_of(m) + off, 128), w)]
        return outs[m].at[who, :, pl.ds(off, w)]

    def piece(m, cut):
        off, w = cut
        if m == adapters:
            return ins[m].at[pl.ds(off, w), :]
        return ins[m].at[:, pl.ds(off, w)]

    def whole_place(m, who, zz):
        return place(m, who, zz, (0, blk if m == adapters else wide_of(m)))

    def slot(m, zz):
        return zz if m < FULL else 0

    def order_of(half):
        order = list(range(nbits))
        return order if half == 0 else order[::-1]

    def xy_copy(m, zz, half, cut, mask, bit, own_piece=False):
        where = place(m, peer_of(mask), zz, cut)
        return push(piece(m, cut) if own_piece else where, where, xy_send.at[m, slot(m, zz), half, mask, bit],
                    xy_recv.at[m, slot(m, zz), half, mask | (1 << bit)], (peer_of(1 << bit), z))

    def xy_wait(m, zz, half, cut, mask):
        where = place(m, peer_of(mask), zz, cut)
        push(where, where, xy_send.at[m, slot(m, zz), half, 0, 0], xy_recv.at[m, slot(m, zz), half, mask], (partner, z)).wait_recv()

    def core_copy(m, zz, half, cut, mask, own_piece=False):
        where = place(m, peer_of(mask), zz, cut)
        return push(piece(m, cut) if own_piece else where, where, core_send.at[m, slot(m, zz), half, mask],
                    core_recv.at[m, slot(m, zz), half, mask], (partner, z))

    def core_wait(m, zz, half, cut, mask):
        where = place(m, peer_of(mask) - core + (1 - core), zz, cut)
        push(where, where, core_send.at[m, slot(m, zz), half, mask], core_recv.at[m, slot(m, zz), half, mask], (partner, z)).wait_recv()

    def own_copy(m):
        return pltpu.make_async_copy(ins[m], whole_place(m, f, z), own_sem.at[m])

    def z_copy(m, zz, up, own_piece=False):
        where = whole_place(m, f, zz)
        return push(ins[m] if own_piece else where, where, z_send.at[m, zz, up], z_recv.at[m, zz], (f, z + 1 if up else z - 1))

    def last_of(order, mask):
        return max([i for i, b in enumerate(order) if (mask >> b) & 1], default=-1)

    def masks_in_order(half):
        order = order_of(half)
        return sorted(range(1, 1 << nbits), key=lambda mask: [1 if (mask >> b) & 1 else 0 for b in reversed(order)])

    def launch(m, zz, own_piece=False):
        for half, cut in cuts(m):
            for bit in order_of(half):
                xy_copy(m, zz, half, cut, 0, bit, own_piece).start()
            core_copy(m, zz, half, cut, 0, own_piece).start()

    def launch_own(m):
        if m < FULL:
            @pl.when(z < n_z - 1)
            def _():
                z_copy(m, z, 1, True).start()

            @pl.when(z > 0)
            def _():
                z_copy(m, z, 0, True).start()
        launch(m, z, True)
        own_copy(m).start()

    def forward(m, zz):
        for half, cut in cuts(m):
            order = order_of(half)
            for mask in masks_in_order(half):
                if last_of(order, mask) < nbits - 1:
                    xy_wait(m, zz, half, cut, mask)
                    for b in order[last_of(order, mask) + 1:]:
                        xy_copy(m, zz, half, cut, mask, b).start()
                    core_copy(m, zz, half, cut, mask).start()

    def finish(m, zz):
        for half, cut in cuts(m):
            order = order_of(half)
            for mask in masks_in_order(half):
                if last_of(order, mask) == nbits - 1:
                    xy_wait(m, zz, half, cut, mask)
                    core_copy(m, zz, half, cut, mask).start()

    def settle(m, zz):
        for half, cut in cuts(m):
            for mask in range(1 << nbits):
                core_wait(m, zz, half, cut, mask)

    def drain(m, zz):
        for half, cut in cuts(m):
            order = order_of(half)
            for mask in range(1 << nbits):
                for b in order[last_of(order, mask) + 1:]:
                    xy_copy(m, zz, half, cut, mask, b).wait_send()
                core_copy(m, zz, half, cut, mask).wait_send()

    def at_distance(k, body):
        for sign in ((-1, 1) if k else (1,)):
            zz = z + sign * k

            @pl.when((zz >= 0) & (zz < n_z))
            def _():
                body(zz)

    def arrive(m, k):
        @pl.when(z - k >= 0)
        def _():
            zz = z - k
            z_copy(m, zz, 1).wait_recv()

            @pl.when(z < n_z - 1)
            def _():
                z_copy(m, zz, 1).start()

            launch(m, zz)

        @pl.when(z + k < n_z)
        def _():
            zz = z + k
            z_copy(m, zz, 0).wait_recv()

            @pl.when(z > 0)
            def _():
                z_copy(m, zz, 0).start()

            launch(m, zz)

    def every_z(m, body):
        if m < FULL:
            def step(zz, _):
                body(m, zz)
                return 0

            lax.fori_loop(0, n_z, step, 0)
        else:
            body(m, z)

    there = [(base + z // 2, 2 * core + s) for s in range(2)]

    def is_here(s):
        return (z // 2 == core) & (2 * core + s == z)

    def token_push(src, dst, send, recv, s):
        return push(src.at[s], dst.at[z % 2], send.at[s], recv.at[z % 2], there[s])

    def tokens_start(src, dst, send, recv):
        for s in range(2):
            @pl.when(is_here(s))
            def _():
                pltpu.make_async_copy(src.at[s], dst.at[z % 2], recv.at[z % 2]).start()

            @pl.when(jnp.logical_not(is_here(s)))
            def _():
                token_push(src, dst, send, recv, s).start()

    def tokens_wait(src, dst, send, recv):
        for i in range(2):
            @pl.when(is_here(i))
            def _():
                pltpu.make_async_copy(src.at[i], dst.at[z % 2], recv.at[z % 2]).wait()

            @pl.when(jnp.logical_not(is_here(i)))
            def _():
                push(dst.at[i], dst.at[i], send.at[i], recv.at[i], there[i]).wait_recv()

    def tokens_drain(src, dst, send, recv):
        for s in range(2):
            @pl.when(jnp.logical_not(is_here(s)))
            def _():
                token_push(src, dst, send, recv, s).wait_send()

    def around(src_of, dst, send, recv):
        return [push(src_of((f + j) % n_f), dst.at[f], send.at[j], recv.at[f], ((f + j) % n_f, z)) for j in range(1, n_f)]

    def around_wait(dst, send, recv):
        for j in range(1, n_f):
            came = (f - j + n_f) % n_f
            push(dst.at[came], dst.at[came], send.at[j], recv.at[came], (came, z)).wait_recv()

    cond_sends = around(lambda to: cblk_ref.at[to], cgot, c_send, c_recv)
    lane_sends = around(lambda to: clane_ref, cond_out, l_send, l_recv)
    mod_sends = around(lambda to: mpart.at[to], mgot, m_send, m_recv)

    sign_push = push(sign_ref, sign_got, s_send.at[0], s_recv.at[0], (partner, z))
    hot_push = push(hot2_ref, hot_got, s_send.at[1], s_recv.at[1], (partner, z))

    sign_push.start()
    hot_push.start()
    for copy in cond_sends + lane_sends:
        copy.start()
    launch_own(adapters)
    tokens_start(x_ref, x_out, x_send, x_recv)
    launch_own(FULL)
    launch_own(0)
    cgot[f] = cblk_ref[f]
    cond_out[f] = clane_ref[...]

    around_wait(cgot, c_send, c_recv)
    k_local = wmod_ref.shape[1]
    everyone = cgot[...].reshape(n_f * 8, cgot.shape[2])[:, :k_local].astype(bf16)
    mpart[...] = (mm(everyone, wmod_ref[0]) + pltpu.roll(mm(everyone, wmod_ref[1]), 2, 0)).reshape(mpart.shape)
    for copy in mod_sends:
        copy.start()
    mgot[f] = mpart[f]

    forward(adapters, z)
    forward(FULL, z)
    for k in range(1, n_z):
        arrive(0, k)
    forward(0, z)
    for m in (FULL + 1, FULL + 2, FULL + 3):
        launch_own(m)
    for m in (1, 2, 3):
        launch_own(m)
    at_distance(1, lambda zz: forward(0, zz))
    for m in (1, 2, 3):
        arrive(m, 1)
    for k in range(2, n_z):
        at_distance(k, lambda zz: forward(0, zz))

    finish(adapters, z)
    settle(adapters, z)
    own_copy(adapters).wait()
    hot2 = hot2_ref[...]
    starts = {}
    offset = 0
    for stream in range(2):
        for index in range(5):
            starts[stream, index] = (offset, offset + fans[index] // n_z)
            offset += fans[index] // n_z + cols[index] // n_z

    def pick_a(stream, index):
        at = starts[stream, index][0]
        return mm_t(hot2, row_ref[at:at + fans[index] // n_z, :]).astype(bf16)

    def pick_b(stream, index, s, put):
        at = starts[stream, index][1]
        count = cols[index] // n_z // NAD
        flat = row_ref[at:at + count, :].astype(f32) * picks_ref[s * NAD:s * NAD + 1, :]
        for k in range(1, NAD):
            begin = at + k * count
            flat = flat + row_ref[begin:begin + count, :].astype(f32) * picks_ref[s * NAD + k:s * NAD + k + 1, :]
        fl_ref[:count, :] = flat
        blocks = count // RANK
        for j in range(blocks):
            put(j * 128, fl_ref[pl.ds(j, RANK, stride=blocks), :].astype(bf16))

    spans_a, spans_b = [], []
    offset = 0
    for index in range(1, 5):
        count = fans[index] // n_z
        picked = pick_a(0, index)
        for s in range(2):
            img_msg[s, :, offset:offset + count] = picked[s * RANK:(s + 1) * RANK]
        spans_a.append((offset, count))
        offset += count
    for index in range(1, 5):
        count = cols[index] // n_z
        for s in range(2):
            def put(at, value, s=s, offset=offset):
                img_msg[s, :, offset + at:offset + at + 128] = value
            pick_b(0, index, s, put)
        spans_b.append((offset, count))
        offset += count

    def img_push(s, side):
        return push(img_msg.at[s], img_got.at[z], i_send.at[s, side], i_recv.at[z], (base + side, 2 * core + s))

    for s in range(2):
        for side in range(2):
            self_here = (side == core) & (2 * core + s == z)

            @pl.when(self_here)
            def _():
                img_got[z] = img_msg[s]

            @pl.when(jnp.logical_not(self_here))
            def _():
                img_push(s, side).start()

    share = width // n_z
    for place_at, (stream, index) in enumerate([(0, 0), (1, 0), (1, 1), (1, 3)]):
        txt_msg[:, place_at * share:(place_at + 1) * share] = pick_a(stream, index)
    for place_at, index in ((4, 2), (5, 4)):
        for s in range(2):
            def put(at, value, s=s, place_at=place_at):
                txt_msg[s * RANK:(s + 1) * RANK, place_at * share + at:place_at * share + at + 128] = value
            pick_b(1, index, s, put)
    txt_got[z] = txt_msg[...]
    ring.start(lambda to: txt_msg, txt_got, t_send, t_recv)
    for ref in txt_a + txt_b:
        ref[...] = jnp.zeros_like(ref)
    for index in (2, 4):
        txt_a[index - 1][:rank2, :] = pick_a(1, index)
    for ref, stream, index in ((txt_b[0], 1, 1), (txt_b[2], 1, 3), (modb_out.at[0], 0, 0), (modb_out.at[1], 1, 0)):
        for s in range(2):
            def put(at, value, ref=ref, s=s):
                ref[s * RANK:(s + 1) * RANK, at:at + 128] = value
            pick_b(stream, index, s, put)

    for k in (2, 3):
        for m in (1, 2, 3):
            arrive(m, k)
    for m in (1, 2, 3):
        forward(m, z)
    for m in (FULL + 1, FULL + 2, FULL + 3):
        forward(m, z)

    ring.wait(txt_got, t_send, t_recv)
    for t in range(n_z):
        lanes = slice(t * share, (t + 1) * share)
        got = lambda number: txt_got[t, :, number * share:(number + 1) * share]
        moda_out[0, :, lanes] = got(0)
        moda_out[1, :, lanes] = got(1)
        txt_a[0][:rank2, lanes] = got(2)
        txt_a[2][:rank2, lanes] = got(3)
        txt_b[1][:rank2, lanes] = got(4)
        txt_b[3][:rank2, lanes] = got(5)
    around_wait(mgot, m_send, m_recv)
    mod_sum = mgot[0]
    for j in range(1, n_f):
        mod_sum = mod_sum + mgot[j]
    c8 = c8_ref[...].astype(bf16)
    thin = mm_t(c8, moda_out[0])
    row = lax.broadcasted_iota(jnp.int32, thin.shape, 0)
    middle = (jnp.where(row < 2, thin, mm_t(c8, moda_out[1])) * smask_ref[...]).astype(bf16)
    low = jnp.where(row < 2, middle.astype(f32), 0.0)
    high = jnp.where((row >= 2) & (row < 4), middle.astype(f32), 0.0)
    midm_out[0] = low
    midm_out[1] = high
    own_mod[...] = mod_sum + mm(low.astype(bf16), modb_out[0]) + mm(high.astype(bf16), modb_out[1])

    def mod_push(index, peer):
        return push(own_mod, mod_got.at[core * n_z + z], d_send.at[index], d_recv.at[core * n_z + z], peer)

    for index, peer in enumerate(column):
        mod_push(index, peer).start()
    mod_got[core * n_z + z] = own_mod[...]

    for t in range(n_z):
        @pl.when(jnp.logical_not((z // 2 == core) & (t == z)))
        def _():
            push(img_got.at[t], img_got.at[t], i_send.at[0, 0], i_recv.at[t], (base + z // 2, t)).wait_recv()
    for t in range(n_z):
        for refs_of, spans in ((img_a, spans_a), (img_b, spans_b)):
            for ref, (begin, count) in zip(refs_of, spans):
                ref[:, t * count:(t + 1) * count] = img_got[t, :, begin:begin + count]

    for index, peer in enumerate(column):
        place_at = peer[0] % 2 * n_z + peer[1]
        push(mod_got.at[place_at], mod_got.at[place_at], d_send.at[index], d_recv.at[place_at], peer).wait_recv()
    step = width // 2
    per = own_mod.shape[1] // step
    imod_out[...] = jnp.zeros_like(imod_out)
    tmod_out[...] = jnp.zeros_like(tmod_out)
    for q in range(12):
        t, lanes = q // per, slice(q % per * step, (q % per + 1) * step)
        into = slice(q % 2 * step, (q % 2 + 1) * step)
        here = mod_got[z // 2 * n_z + t]
        imod_out[q // 2:q // 2 + 1, into] = jnp.where(z % 2 == 0, here[0:1, lanes], here[1:2, lanes])
        ours = mod_got[core * n_z + t]
        for s in range(2):
            tmod_out[8 * s + q // 2:8 * s + q // 2 + 1, into] = ours[2 + s:3 + s, lanes]

    own = own_ref[...]
    pick = lambda r: jnp.where(own > 0, tmod_out[r:r + 1, :], tmod_out[8 + r:9 + r, :])
    hat, _inv = norm_rows(xt_ref[...].astype(f32))
    th_out[z] = (hat * (1.0 + pick(1)) + pick(0)).astype(bf16)
    ring.start(lambda to: th_out.at[z], th_out, a_send, a_recv)
    dm_out[z] = (pick(5) * gt_ref[...].astype(f32)).astype(bf16)
    ring.start(lambda to: dm_out.at[z], dm_out, dm_send, dm_recv)
    tokens_wait(x_ref, x_out, x_send, x_recv)
    quarter = x_ref.shape[1]
    for i in range(2):
        def norm(r, _):
            sl = pl.ds(pl.multiple_of(r * ROWS, ROWS), ROWS)
            hat, _inv = norm_rows(x_out[i, sl, :].astype(f32))
            h_out[pl.ds(pl.multiple_of(i * quarter + r * ROWS, ROWS), ROWS), :] = (
                hat * (1.0 + imod_out[1:2, :]) + imod_out[0:1, :]).astype(bf16)
            return 0

        lax.fori_loop(0, quarter // ROWS, norm, 0)
    tokens_start(g_ref, g_out, g_send, g_recv)


    finish(FULL, z)
    settle(FULL, z)
    own_copy(FULL).wait()
    load = pltpu.make_async_copy(outs[FULL], wtxt, tw_sem)
    load.start()
    ring.wait(th_out, a_send, a_recv)
    pad = xt_ref.shape[0]
    h_txt = th_out[...].reshape(n_z * pad, width)
    tmid = (mm_t(h_txt, txt_a[0][...]) * tmask_ref[...]).astype(bf16)
    tmid_out[...] = tmid
    load.wait()
    tq_ref[...] = (mm(h_txt, wtxt[...].reshape(width, wtxt.shape[2])) + mm(tmid, txt_b[0][...])).astype(bf16)
    for s in range(2):
        @pl.when(is_here(s))
        def _():
            copy = pltpu.make_async_copy(tq_ref, theads_out.at[z % 2], q_recv.at[z % 2])
            copy.start()
            copy.wait()

        @pl.when(jnp.logical_not(is_here(s)))
        def _():
            push(tq_ref, theads_out.at[z % 2], q_send.at[s], q_recv.at[z % 2], there[s]).start()

    every_z(0, finish)
    every_z(0, settle)
    own_copy(0).wait()
    mid = mm_t(h_out[...], img_a[0][...]).astype(bf16)
    mid_out[...] = mid
    tn = wtile.shape[3]
    per_half = stage.shape[2] // tn

    def tile_of(n):
        side = 1 - core if n < per_half else core
        return side, side * per_half + n % per_half

    def tile_load(n):
        at = pl.ds(pl.multiple_of(tile_of(n)[1] * tn, 128), tn)
        return pltpu.make_async_copy(outs[0].at[:, :, at], wtile.at[n % 2], w_sem.at[n % 2])

    def heads_push():
        return push(stage.at[0], heads_out.at[core], h_send, h_recv, (partner, z))

    tile_load(0).start()
    for n in range(2 * per_half):
        if n + 1 < 2 * per_half:
            tile_load(n + 1).start()
        tile_load(n).wait()
        at = pl.ds(pl.multiple_of(tile_of(n)[1] * tn, 128), tn)
        lanes = slice(n % per_half * tn, (n % per_half + 1) * tn)
        stage[n // per_half, :, lanes] = (
            mm(h_out[...], wtile[n % 2].reshape(width, tn)) + mm(mid, img_b[0][:, at])).astype(bf16)
        if n == per_half - 1:
            heads_push().start()
    keep = pltpu.make_async_copy(stage.at[1], heads_out.at[core], h_sem)
    keep.start()

    for m in (1, 2, 3):
        at_distance(1, lambda zz: forward(m, zz))

    sign_push.wait_recv()
    chip_sign = jnp.where(z // 2 == core, sign_ref[...], sign_got[...])
    chip_sign = jnp.where(z % 2 == 0, chip_sign, -chip_sign)
    bias_out[...] = jnp.where(chip_sign > 0, 0.0, -1e30)
    hot_push.wait_recv()
    hot4_out[:rank2, :] = jnp.where(core == 0, hot2_ref[...].astype(f32), hot_got[...].astype(f32)).astype(bf16)
    hot4_out[rank2:, :] = jnp.where(core == 0, hot_got[...].astype(f32), hot2_ref[...].astype(f32)).astype(bf16)
    keep.wait()
    push(stage.at[0], heads_out.at[1 - core], h_send, h_recv, (partner, z)).wait_recv()
    for s in range(2):
        @pl.when(jnp.logical_not(is_here(s)))
        def _():
            push(theads_out.at[s], theads_out.at[s], q_send.at[s], q_recv.at[s], there[s]).wait_recv()
    pairs = heads_out.shape[2] // (6 * HD)
    per_part = pairs // 2

    def pair_loads(i):
        lanes = pl.ds(pl.multiple_of(i * (6 * HD), 128), 6 * HD)
        part = pl.ds(pl.multiple_of(i % per_part * (6 * HD), 128), 6 * HD)
        return [pltpu.make_async_copy(heads_out.at[:, :, lanes], img_buf.at[i % 2], b_sem.at[i % 2, 0]),
                pltpu.make_async_copy(theads_out.at[i // per_part, :, part], txt_buf.at[i % 2], b_sem.at[i % 2, 1])]

    def pair_lanes(i):
        return pl.ds(pl.multiple_of((core * pairs + i) * (2 * HD), 128), 2 * HD)

    def o_keep(i):
        return pltpu.make_async_copy(o_stage.at[i, core], att_out.at[:, pair_lanes(i)], o_sem.at[i])

    def o_push(i):
        return push(o_stage.at[i, 1 - core], att_out.at[:, pair_lanes(i)], o_send.at[i], o_recv.at[i], (partner, z))

    for copy in pair_loads(0):
        copy.start()
    tokens = img_buf.shape[1] * img_buf.shape[2]

    def pair_step(i, _):
        at = i % 2

        @pl.when(i + 1 < pairs)
        def _():
            for copy in pair_loads(i + 1):
                copy.start()

        for copy in pair_loads(i):
            copy.wait()
        bias = bias_out[:, 0:1]
        for h in range(2):
            low = 3 * HD * h
            ki = img_buf[at, :, :, low + HD:low + 2 * HD].reshape(tokens, HD)
            vi = img_buf[at, :, :, low + 2 * HD:low + 3 * HD].reshape(tokens, HD)
            kt = txt_buf[at, :, low + HD:low + 2 * HD]
            vt = txt_buf[at, :, low + 2 * HD:low + 3 * HD]
            for b in range(3):
                q = img_buf[at, b, :, low:low + HD] if b < 2 else txt_buf[at, :, low:low + HD]
                o, lse = attend_block(q, ki, vi, kt, vt, bias)
                rows = img_buf.shape[2]
                if b < 2:
                    o_stage[i, b, :, h * HD:(h + 1) * HD] = o
                    lse_out[i, h:h + 1, b * rows:(b + 1) * rows] = lse
                else:
                    ot_stage = o
                    lse_out[i, h:h + 1, tokens:tokens + q.shape[0]] = lse
            if h == 0:
                first = ot_stage
        both = jnp.concatenate([first, ot_stage], axis=1)
        ot_out[i // per_part, :, pl.ds(pl.multiple_of(i % per_part * (2 * HD), 128), 2 * HD)] = both
        o_keep(i).start()
        o_push(i).start()
        return 0

    for m in (1, 2, 3):
        at_distance(2, lambda zz: forward(m, zz))
    lax.fori_loop(0, pairs // 2, pair_step, 0)
    for m in (1, 2, 3):
        at_distance(n_z - 1, lambda zz: forward(m, zz))
    lax.fori_loop(pairs // 2, pairs, pair_step, 0)

    for m in range(total - 1):
        if m not in (0, FULL):
            every_z(m, finish)
    for m in range(total - 1):
        if m not in (0, FULL):
            every_z(m, settle)
            own_copy(m).wait()
    for m in range(total):
        every_z(m, drain)
        if m < FULL:
            def sent(zz, _):
                @pl.when((zz <= z) & (z < n_z - 1))
                def _():
                    z_copy(m, zz, 1).wait_send()

                @pl.when((zz >= z) & (z > 0))
                def _():
                    z_copy(m, zz, 0).wait_send()

                return 0

            lax.fori_loop(0, n_z, sent, 0)
    for copy in cond_sends + lane_sends + mod_sends:
        copy.wait_send()
    around_wait(cond_out, l_send, l_recv)
    ring.drain(lambda to: txt_msg, txt_got, t_send, t_recv)
    ring.drain(lambda to: th_out.at[z], th_out, a_send, a_recv)
    ring.wait(dm_out, dm_send, dm_recv)
    ring.drain(lambda to: dm_out.at[z], dm_out, dm_send, dm_recv)
    for index, peer in enumerate(column):
        mod_push(index, peer).wait_send()
    for s in range(2):
        for side in range(2):
            @pl.when(jnp.logical_not((side == core) & (2 * core + s == z)))
            def _():
                img_push(s, side).wait_send()
    tokens_wait(g_ref, g_out, g_send, g_recv)
    tokens_drain(x_ref, x_out, x_send, x_recv)
    tokens_drain(g_ref, g_out, g_send, g_recv)
    heads_push().wait_send()
    sign_push.wait_send()
    hot_push.wait_send()

    def o_done(i, _):
        o_keep(i).wait()
        o_push(i).wait_send()
        other = pl.ds(pl.multiple_of(((1 - core) * pairs + i) * (2 * HD), 128), 2 * HD)
        push(o_stage.at[i, 0], att_out.at[:, other], o_send.at[i], o_recv.at[i], (partner, z)).wait_recv()
        return 0

    lax.fori_loop(0, pairs, o_done, 0)
    for s in range(2):
        @pl.when(jnp.logical_not(is_here(s)))
        def _():
            push(tq_ref, theads_out.at[z % 2], q_send.at[s], q_recv.at[z % 2], there[s]).wait_send()


def front(full, part, adapter_rows, x, g, picks, hot2, cond, wmod, x_txt, g_txt, own, tmask, smask, sign_rows, n_f, n_z, fans, cols, cid):
    f32, bf16 = jnp.float32, jnp.bfloat16
    vmem, dma = pltpu.VMEM, pltpu.SemaphoreType.DMA
    shape = jax.ShapeDtypeStruct
    slots, width = cond.shape
    k_local = wmod.shape[1]
    z = lax.axis_index("tp")
    blocks = jnp.pad(jnp.swapaxes(cond.reshape(slots, n_f, k_local), 0, 1), ((0, 0), (0, 6), (0, 256 - k_local)))
    cond8 = jnp.concatenate([cond, cond, jnp.zeros((4, width), f32)])
    lane = jnp.pad(lax.dynamic_slice_in_dim(cond, z * (width // n_z), width // n_z, 1), ((0, 6), (0, 0)))
    chosen = (picks[:, None] == jnp.arange(NAD)[None, :]).astype(f32).reshape(-1, 1)
    smalls = (jnp.broadcast_to(chosen, (slots * NAD, 128)), hot2, blocks, lane, cond8, smask, wmod, x_txt, g_txt, own, tmask, sign_rows)
    args = (*full, *part, adapter_rows, x, g, *smalls)
    any_spec, in_vmem = pl.BlockSpec(memory_space=pl.ANY), pl.BlockSpec(memory_space=vmem)
    rows = 2 * (sum(fans) + sum(cols)) // n_z
    chips = n_f // 2
    nbits = bits_of(chips)
    total = len(full) + len(part) + 1
    pad = x_txt.shape[0]
    img_rows = 2 * x.shape[1]
    cut = cols[0] // n_z
    qkv_part = cols[1] // n_z
    thick = tmask.shape[1]
    rank2 = hot2.shape[0]
    own_a = [fans[1], fans[2] // n_z, fans[3], fans[4] // n_z]
    own_b = [cols[1] // n_z, cols[2], cols[3] // n_z, cols[4]]
    lanes = (sum(fans[1:]) + sum(cols[1:])) // n_z
    share = width // n_z
    outs = [shape((n_f,) + a.shape[:-1] + (a.shape[-1] * (n_z if i < len(full) else 1),), a.dtype) for i, a in enumerate(full + part)]
    in_hbm = len(outs)
    outs += [shape(x.shape, bf16), shape(g.shape, bf16), shape((8, width), f32), shape((16, width), f32)]
    outs += [shape((RANK, n), bf16) for n in fans[1:]] + [shape((RANK, n), bf16) for n in cols[1:]]
    outs += [shape((thick, n), bf16) for n in own_a] + [shape((thick, n), bf16) for n in own_b]
    outs += [shape((2, rank2, width), bf16), shape((2, rank2, cut), bf16), shape((2, 8, rank2), f32), shape((n_f, 8, share), f32), shape((n_z, pad, width), bf16)]
    heads_half = cols[1] // (6 * HD)
    pairs = heads_half // 2
    outs += [shape((2, n_z * pad, width // n_z), bf16), shape((pairs, 2, 2 * img_rows + n_z * pad), f32), shape(sign_rows.shape, f32),
             shape((2 * rank2, NAD * RANK), bf16)]
    outs += [shape((img_rows, width), bf16), shape((img_rows, RANK), bf16), shape((2, img_rows, cols[1] // 2), bf16),
             shape((n_z, pad, width), bf16), shape((n_z * pad, thick), bf16), shape((2, n_z * pad, qkv_part), bf16), shape((img_rows, width), bf16)]
    specs = [any_spec] * in_hbm + [in_vmem, any_spec] + [in_vmem] * (len(outs) - in_hbm - 2)
    for place in (1, 2, 5):
        specs[len(outs) - place] = any_spec
    return pl.pallas_call(
        functools.partial(front_kernel, n_f, n_z, tuple(fans), tuple(cols)),
        out_shape=outs,
        in_specs=[any_spec] * (total + 2) + [in_vmem] * len(smalls),
        out_specs=specs,
        scratch_shapes=[
            vmem((rows, 128), bf16), vmem((cut // NAD, 128), f32), vmem((2, RANK, lanes), bf16), vmem((n_z, RANK, lanes), bf16),
            vmem((rank2, 6 * share), bf16), vmem((n_z, rank2, 6 * share), bf16), vmem((n_f, 8, 256), f32),
            vmem((n_f, 8, cut), f32), vmem((n_f, 8, cut), f32), vmem((8, cut), f32), vmem((2 * n_z, 8, cut), f32),
            vmem((2, n_f, k_local, 768), bf16), vmem((n_f, k_local, qkv_part), bf16), vmem((2, img_rows, cols[1] // 2), bf16),
            vmem((n_z * pad, qkv_part), bf16), vmem(sign_rows.shape, f32), vmem((rank2, NAD * RANK), bf16),
            vmem((2, 2, img_rows, 6 * HD), bf16), vmem((2, n_z * pad, 6 * HD), bf16), vmem((pairs, 2, img_rows, 2 * HD), bf16),
            dma((total, n_z, 2)), dma((total, n_z)), dma((total, n_z, 2, chips, nbits)), dma((total, n_z, 2, chips)),
            dma((total, n_z, 2, chips)), dma((total, n_z, 2, chips)), dma((total,)),
            dma((2,)), dma((2,)), dma((2,)), dma((2,)), dma((n_f,)), dma((n_f,)), dma((n_f,)), dma((n_f,)), dma((n_f,)), dma((n_f,)),
            dma((2, 2)), dma((n_z,)), dma((n_z,)), dma((n_z,)), dma((2 * n_z,)), dma((2 * n_z,)), dma((n_z,)), dma((n_z,)),
            dma((2,)), dma, dma, dma, dma, dma((2,)), dma((2,)), dma((n_z,)), dma((n_z,)),
            dma((2,)), dma((2,)), dma((2, 2)), dma((pairs,)), dma((pairs,)), dma((pairs,)),
        ],
        compiler_params=pltpu.CompilerParams(collective_id=cid, has_side_effects=True, vmem_limit_bytes=58 * 1024 * 1024),
        name="front",
    )(*args)

HD = 64
FF = 6144
NAD = 8
RANK = 16
EPS = 1e-06
HIGH = lax.Precision.HIGHEST
F32 = jnp.float32
BF16 = jnp.bfloat16
BOTH = ("fsdp", "tp")


def matmul(left, right):
    return jnp.dot(left, right, preferred_element_type=F32)


def exact(left, right):
    return jnp.dot(left, right, precision=HIGH, preferred_element_type=F32)


def inner_left(left, right):
    return lax.dot_general(left, right, (((0,), (0,)), ((), ())), preferred_element_type=F32)


def inner_right(left, right):
    return lax.dot_general(
        left, right, (((left.ndim - 1,), (right.ndim - 1,)), ((), ())), preferred_element_type=F32
    )


def layer_norm(values):
    center = values - jnp.mean(values, axis=-1, keepdims=True)
    inverse = lax.rsqrt(jnp.mean(center * center, axis=-1, keepdims=True) + EPS)
    return (center * inverse, inverse)


def norm_back(grad_normed, normed, inverse, scale):
    grad_hat = grad_normed * (1.0 + scale)
    return inverse * (
        grad_hat
        - jnp.mean(grad_hat, axis=-1, keepdims=True)
        - normed * jnp.mean(grad_hat * normed, axis=-1, keepdims=True)
    )


def gelu(value):
    return jax.nn.gelu(value, approximate=True)


def gelu_back(value, grad):
    return jax.vjp(gelu, value)[1](grad)[0]


def shards(
    image_tokens,
    text_tokens,
    conditioning,
    text_lengths,
    adapter_index,
    adapters,
    mod_weight,
    qkv_weight,
    out_weight,
    fc1_weight,
    fc2_weight,
    image_cot,
    text_cot,
):
    n_f, n_z = lax.axis_size("fsdp"), lax.axis_size("tp")
    f, z = lax.axis_index("fsdp"), lax.axis_index("tp")
    core = f % 2
    slots, quarter, width = image_tokens.shape
    txt_local = text_tokens.shape[0]
    txt_group = txt_local * n_z
    img_half = 2 * quarter
    img_n = 2 * img_half
    cols = [6 * width, 3 * width, width, FF, width]
    fans = [width, width, width, width, FF]

    def round_pairs(r):
        pairs = []
        for fa in range(n_f):
            for t in range(n_z):
                there = (fa // 2 * 2 + t // 2) * n_z + 2 * (fa % 2) + (r ^ (t % 2))
                pairs.append((fa * n_z + t, there))
        return pairs

    low_bit = z % 2

    def pick(stack, bit):
        return lax.dynamic_index_in_dim(stack, bit, 0, keepdims=False)

    def flip(r):
        return low_bit if r == 0 else 1 - low_bit

    def to_chip(parts):
        got = [lax.ppermute(parts[r], BOTH, round_pairs(r)) for r in range(2)]
        return jnp.where(low_bit == 0, got[0], got[1]), jnp.where(low_bit == 0, got[1], got[0])

    def from_chip(pieces):
        got = []
        for r in range(2):
            mine = jnp.where(flip(r) == 0, pieces[0], pieces[1])
            got.append(lax.ppermute(mine, BOTH, [(b, a) for a, b in round_pairs(r)]))
        return jnp.where(low_bit == 0, got[0], got[1]), jnp.where(low_bit == 0, got[1], got[0])

    def reshard(values):
        return jnp.concatenate(to_chip([pick(values, flip(r)) for r in range(2)]), axis=0)

    def unshard(values):
        return jnp.stack(from_chip([values[:quarter], values[quarter:]]))

    def swap_core(values):
        return lax.ppermute(values, "fsdp", [(i, i ^ 1) for i in range(n_f)])

    def by_core(mine, other, axis):
        first = jnp.where(core == 0, mine, other)
        second = jnp.where(core == 0, other, mine)
        return jnp.concatenate([first, second], axis=axis)

    def z_swap(values, step):
        return lax.ppermute(values, "tp", [(i, i ^ step) for i in range(n_z)])

    def z_order(pieces):
        stack = jnp.stack(pieces)
        return [pick(stack, z ^ a) for a in range(n_z)]

    def z_gather(values):
        return z_order([values] + [z_swap(values, j) for j in range(1, n_z)])

    def z_exchange(blocks):
        return z_order([pick(blocks, z ^ j) if j == 0 else z_swap(pick(blocks, z ^ j), j) for j in range(n_z)])

    def z_scatter(values):
        count = values.shape[0] // n_z
        mine = lax.dynamic_slice_in_dim(values, z * count, count, 0)
        for j in range(1, n_z):
            part = lax.dynamic_slice_in_dim(values, (z ^ j) * count, count, 0)
            mine = mine + z_swap(part.astype(BF16), j).astype(F32)
        return mine

    def to_heads(values):
        half = values.shape[1] // 2
        low, high = values[:, :half], values[:, half:]
        mine = jnp.where(core == 0, low, high)
        return by_core(mine, swap_core(jnp.where(core == 0, high, low)), 0)

    def to_tokens(values):
        low, high = values[:img_half], values[img_half:]
        mine = jnp.where(core == 0, low, high)
        return by_core(mine, swap_core(jnp.where(core == 0, high, low)), 1)

    out_t = jnp.swapaxes(out_weight, 1, 2)
    fc2_t = jnp.swapaxes(fc2_weight, 1, 2)
    local = [qkv_weight, out_t, fc1_weight, fc2_t]
    adapter_rows = lax.optimization_barrier(adapters.reshape(-1, 128)).astype(BF16)
    txt_pad = (txt_local + 15) // 16 * 16

    def padded(values):
        return jnp.pad(values, ((0, txt_pad - txt_local), (0, 0)))

    x_txt_low, g_txt_low = padded(text_tokens), padded(text_cot)
    x_txt = x_txt_low.astype(F32)

    seg_ends = jnp.cumsum(text_lengths[0])
    slot_ids = jnp.arange(slots)

    def owner_of(position):
        segment = jnp.sum((position[:, None] >= seg_ends[None, :]).astype(jnp.int32), axis=1)
        return (segment[:, None] == slot_ids[None, :]).astype(F32)

    def real(owner):
        place = jnp.arange(owner.shape[0]) % txt_pad
        return jnp.where((place < txt_local)[:, None], owner, 0.0)

    def position(rows):
        return rows // txt_pad * txt_local + rows % txt_pad

    txt_rows = jnp.arange(n_z * txt_pad)
    owner_group = real(owner_of(position(txt_rows)))
    owner_local = real(owner_of(z * txt_local + jnp.arange(txt_pad)))
    txt_mask = jnp.repeat(owner_group, RANK, axis=1)
    txt_mask_local = jnp.repeat(owner_local, RANK, axis=1)
    rank_cols = slots * RANK
    seq_mask = jnp.repeat(jnp.eye(slots, dtype=F32), RANK, axis=1)

    def by_group(mine, other):
        return by_core(mine, other, 0)

    def stretch(stream, index):
        if stream == 0:
            return img_mod[:, index * width : (index + 1) * width]
        return exact(owner_local, txt_mods[:, index * width : (index + 1) * width])

    def collapse(stream, values):
        if stream == 0:
            return jnp.sum(values, axis=0, keepdims=True)
        return exact(owner_local.T, values)

    def share(values):
        return jnp.concatenate(z_gather(values), axis=0)

    def give(values, rank_part):
        got = z_scatter(jnp.concatenate([values, rank_part], axis=1))
        return got[:, :width], (got[:, width:] * txt_mask_local).astype(BF16)

    def lanes(values):
        count = values.shape[1] // n_z
        return lax.dynamic_slice_in_dim(values, z * count, count, 1)

    def project(values, weight, pair, mask, flipped):
        middle = inner_right(values, pair[0])
        if mask is not None:
            middle = middle * mask
        middle = middle.astype(BF16)
        main = inner_right(values, weight) if flipped else matmul(values, weight)
        return middle, main + matmul(middle, pair[1])

    own_hot = (
        jnp.arange(NAD * RANK)[:, None]
        == (adapter_index[:, None] * RANK + jnp.arange(RANK)[None, :]).reshape(1, -1)
    ).astype(F32)
    k_local = mod_weight.shape[1]
    cond_act = jax.nn.silu(conditioning).astype(BF16)
    thick = 128

    def thicker(part):
        return jnp.concatenate([part, jnp.zeros((thick - part.shape[0], part.shape[1]), part.dtype)], axis=0)

    def sign(owner):
        return owner[:, 0:1] - owner[:, 1:2]

    def lanes_pad(mask):
        return jnp.pad(mask, ((0, 0), (0, thick - mask.shape[1])))

    if n_f == 8:
        slot_mask = jnp.pad(jnp.concatenate([seq_mask, seq_mask]), ((0, 4), (0, 0)))
        made = front(
            [w[0] for w in local], [w[1] for w in local], adapter_rows, image_tokens, image_cot,
            adapter_index, own_hot.T.astype(BF16), cond_act.astype(F32), mod_weight, x_txt_low,
            g_txt_low, sign(owner_local), lanes_pad(txt_mask), slot_mask,
            jnp.broadcast_to(sign(owner_group), (owner_group.shape[0], thick)), n_f, n_z, fans, cols, 1,
        )
        made = iter(made)
        take = lambda count: [next(made) for _ in range(count)]
        img_w = [w.reshape(-1, w.shape[-1]) for w in take(4)]
        txt_w = [w.reshape(-1, w.shape[-1]) for w in take(4)]
        x_img, g_img = [v.reshape(-1, width) for v in take(2)]
        img_rows_mod, txt_mod = take(2)
        img_pairs = [None] + list(zip(take(4), take(4)))
        thick_pairs = [None] + list(zip(take(4), take(4)))
        mod_a, mod_b, tmod, cond_own, txt_dm = take(5)
        o_txt, lse, bias, hot_four = take(4)
        bias = bias[:, :1]
        img_in, img_qkv_mid, img_heads, txt_in, txt_qkv_mid, txt_heads, attended = take(7)
        img_heads = img_heads.reshape(img_n, -1)
        txt_in = txt_in.reshape(-1, width)
        txt_pairs = [None, tuple(part[:rank_cols] for part in thick_pairs[1])]
        img_mod = img_rows_mod[:6].reshape(1, -1)
        txt_mods = txt_mod.reshape(slots, 8, width)[:, :6].reshape(slots, -1)
    else:
        column_picks = by_group(adapter_index, swap_core(adapter_index))
        column_count = 2 * slots
        one_hot = (
            jnp.arange(NAD * RANK)[:, None]
            == (column_picks[:, None] * RANK + jnp.arange(RANK)[None, :]).reshape(1, -1)
        ).astype(F32)
        got = gather([w[0] for w in local], [w[1] for w in local] + [adapter_rows], n_f, n_z)
        got = [g.reshape(-1, g.shape[-1]) for g in got]
        img_w, txt_w, row = got[:4], got[4:8], got[8]
        x_img = reshard(image_tokens)
        g_img = reshard(image_cot)
        own_picks = adapter_index

        a_rows = [[None] * 5 for stream in range(2)]
        b_rows = [[None] * 5 for stream in range(2)]
        offset = 0
        for stream in range(2):
            for index in range(5):
                count = fans[index] // n_z
                a_rows[stream][index] = row[offset : offset + count]
                offset += count
                count = cols[index] // n_z
                b_rows[stream][index] = row[offset : offset + count]
                offset += count

        def b_pick(stream, index, pick_index):
            part = b_rows[stream][index]
            count = part.shape[0] // NAD
            return lax.dynamic_slice_in_dim(part, pick_index * count, count, 0).reshape(RANK, -1)

        def a_pick(rows, hot):
            return inner_right(hot.T.astype(BF16), rows).astype(BF16)

        img_a = a_pick(jnp.concatenate(a_rows[0], axis=0), one_hot)
        fan_share = sum(fans) // n_z
        img_a = img_a.reshape(column_count, RANK, fan_share)
        img_b = [
            jnp.concatenate([b_pick(0, index, column_picks[s]) for index in range(1, 5)], axis=1)
            for s in range(column_count)
        ]
        img_msg = jnp.concatenate([img_a, jnp.stack(img_b)], axis=2)
        txt_a_rows = jnp.concatenate(
            [a_rows[0][0], a_rows[1][0], a_rows[1][1], a_rows[1][3]], axis=0
        )
        txt_a = a_pick(txt_a_rows, own_hot).reshape(slots, RANK, -1)
        txt_b_own = [
            [b_pick(stream, index, own_picks[s]) for s in range(slots)]
            for stream, index in [(0, 0), (1, 0), (1, 1), (1, 2), (1, 3), (1, 4)]
        ]
        txt_b_own = [jnp.concatenate(parts, axis=0) for parts in txt_b_own]
        txt_a_own = a_pick(jnp.concatenate([a_rows[1][2], a_rows[1][4]], axis=0), own_hot)
        txt_msg = jnp.concatenate(
            [txt_a.reshape(slots * RANK, -1), txt_b_own[3], txt_b_own[5]], axis=1
        )
        img_got = jnp.stack(z_exchange(img_msg))
        txt_got = jnp.stack(z_gather(txt_msg))

        def join(part):
            return jnp.swapaxes(part, 0, 1).reshape(part.shape[1], -1)

        img_pairs = []
        offset, b_offset = 0, fan_share
        for index in range(5):
            count = fans[index] // n_z
            a_full = join(img_got[:, :, offset : offset + count])
            offset += count
            if index == 0:
                img_pairs.append(None)
                continue
            count = cols[index] // n_z
            b_full = join(img_got[:, :, b_offset : b_offset + count])
            b_offset += count
            img_pairs.append((a_full, b_full))
        txt_full = []
        offset = 0
        for count in [width // n_z] * 6:
            txt_full.append(join(txt_got[:, :, offset : offset + count]))
            offset += count
        mod_a = [txt_full[0], txt_full[1]]
        mod_b = [txt_b_own[0], txt_b_own[1]]
        txt_pairs = [
            None,
            (txt_full[2], txt_b_own[2]),
            (txt_a_own[:, : width // n_z], txt_full[4]),
            (txt_full[3], txt_b_own[4]),
            (txt_a_own[:, width // n_z :], txt_full[5]),
        ]

        cond_all = lax.all_gather(cond_act, "fsdp", axis=0, tiled=True)
        cond_slice = lax.dynamic_slice_in_dim(cond_all, f * k_local, k_local, 1)
        mod_part = jnp.stack([matmul(cond_slice, mod_weight[stream]) for stream in range(2)], axis=1)
        mod_part = lax.psum_scatter(mod_part, "fsdp", scatter_dimension=0, tiled=True)
        mod_mid = []
        mod_terms = []
        for stream in range(2):
            middle = (inner_right(cond_act, mod_a[stream]) * seq_mask).astype(BF16)
            mod_mid.append(middle)
            mod_terms.append(mod_part[:, stream] + matmul(middle, mod_b[stream]))
        mods = jnp.concatenate(z_gather(jnp.stack(mod_terms, axis=1)), axis=2)
        img_mods = by_group(mods[:, 0], swap_core(mods[:, 0]))
        img_mod = lax.dynamic_slice_in_dim(img_mods, z, 1, 0)
        txt_mods = mods[:, 1]

        img_rows_mod = jnp.concatenate([img_mod.reshape(6, width), jnp.zeros((2, width), F32)], axis=0)
        txt_mod = jnp.pad(txt_mods.reshape(slots, 6, width), ((0, 0), (0, 2), (0, 0))).reshape(-1, width)
        thick_pairs = [None] + [tuple(thicker(part) for part in txt_pairs[index]) for index in range(1, 5)]
        norm_first = [layer_norm(v.astype(F32)) for v in (x_img, x_txt)]
        heads_in = [
            (norm_first[s][0] * (1.0 + stretch(s, 1)) + stretch(s, 0)).astype(BF16) for s in range(2)
        ]

        txt_in = share(heads_in[1])
        txt_qkv_mid, txt_qkv = project(txt_in, txt_w[0], txt_pairs[1], txt_mask, False)
        img_qkv_mid, img_qkv = project(heads_in[0], img_w[0], img_pairs[1], None, False)
        txt_qkv, img_qkv = txt_qkv.astype(BF16), img_qkv.astype(BF16)
        img_heads = to_heads(img_qkv)
        txt_heads = jnp.stack(to_chip([txt_qkv, txt_qkv]))
        img_in = heads_in[0]
        txt_dm = jnp.stack(z_gather((stretch(1, 5) * g_txt_low.astype(F32)).astype(BF16)))

    inputs = [x_img.astype(F32), x_txt]
    norm_one = [layer_norm(values) for values in inputs]
    def txt_home(values):
        got = from_chip([values[0], values[1]])
        return jnp.where(owner_group[:, 0:1] > 0, got[0], jnp.where(owner_group[:, 1:2] > 0, got[1], 0))

    if n_f != 8:
        lengths = by_group(text_lengths[0:1], swap_core(text_lengths[0:1]))
        chip_lengths = jnp.cumsum(lax.dynamic_index_in_dim(lengths, z // slots, 0, keepdims=False))
        chip_slot = z % slots
        chip_segment = jnp.sum(
            (position(txt_rows)[:, None] >= chip_lengths[None, :]).astype(jnp.int32),
            axis=1,
            keepdims=True,
        )
        chip_owner = (chip_segment == chip_slot) & (txt_rows % txt_pad < txt_local)[:, None]
        bias = jnp.where(chip_owner, 0.0, -1e30).astype(F32)
        o_img, o_txt, lse = attend(img_heads, txt_heads, bias, HD)

        attended = to_tokens(o_img)
    (img_branch, img_after, img_mlp, img_pre, img_result, *img_mids, img_gate, txt_mlp, txt_att, txt_after, txt_branch) = both_fwd(
        attended, x_img, g_img, img_rows_mod, img_w[1], img_pairs[2], img_pairs[3], img_w[2], img_pairs[4], img_w[3],
        o_txt, x_txt_low, txt_mod, sign(owner_group), sign(owner_local), lanes_pad(txt_mask_local), txt_w[1], thick_pairs[2],
        n_z, 2,
    )
    made = both_back(
        g_img, img_after, img_branch, img_mlp, attended, img_rows_mod, img_pre, img_w[3], img_pairs[4], img_w[2], img_pairs[3],
        img_w[1], img_pairs[2], img_mids, g_txt_low, txt_after, txt_branch, txt_mod, sign(owner_local), lanes_pad(txt_mask),
        lanes_pad(txt_mask_local), txt_mlp, txt_att, txt_dm, txt_w[1], txt_w[2], txt_w[3], thick_pairs[2], thick_pairs[3],
        thick_pairs[4], n_z, 4,
    )
    img_grad_after, img_grad_att, img_sums, *sides = made[:9]
    txt_result, txt_grad_after, do_txt, txt_sums, *txt_sides = made[9:]
    if n_f != 8:
        txt_sides = [part[:rank_cols] for part in txt_sides]
    txt_sum_rows = txt_sums
    txt_sums = txt_sums.reshape(4, slots, width)
    if n_f != 8:
        image_out = unshard(img_result)

    grads = [[None] * 5 for stream in range(2)]

    def project_back(grad, weight, pair, mask, flipped):
        middle = inner_right(grad, pair[1])
        if mask is not None:
            middle = middle * mask
        middle = middle.astype(BF16)
        main = matmul(grad, weight) if flipped else inner_right(grad, weight)
        return middle, main + matmul(middle, pair[0])

    grads[0][4] = (sides[0], sides[3])
    grads[0][3] = (sides[2], sides[1])
    grads[0][2] = (sides[4], sides[5])
    mod_parts = [[None] * 6 for stream in range(2)]
    for place in range(4):
        mod_parts[1][2 + place] = txt_sums[place]
    grads[1][2] = (txt_sides[0], txt_sides[1])
    grads[1][3] = (txt_sides[2], txt_sides[3])
    grads[1][4] = (txt_sides[4], txt_sides[5])
    img_sum_rows = img_sums
    img_sums = jnp.sum(jnp.concatenate([img_sums, img_gate]).reshape(4, 8, width), axis=1)
    for place in range(4):
        mod_parts[0][2 + place] = img_sums[place : place + 1]
    grad_after = [img_grad_after, txt_grad_after]

    do_img = img_grad_att.reshape(img_n, -1)
    if n_f != 8:
        d_img, d_txt = attend_back(img_heads, txt_heads, bias, do_img, do_txt, lse, HD)
    if n_f == 8:
        sides_of = lambda stream, side: [grads[stream][index][side] for index in range(2, 5)]
        d_img, d_txt, image_out, early = attend_back_far(
            img_heads, txt_heads, bias, do_img, do_txt, lse, HD, img_result.reshape(2, quarter, width),
            sides_of(0, 0), sides_of(0, 1), n_z, fans, cols, 5,
        )
        smalls = (
            x_img, img_grad_after, img_in, img_rows_mod, img_qkv_mid, *img_pairs[1], img_sum_rows, img_gate,
            x_txt_low, txt_grad_after, txt_in.reshape(n_z, txt_pad, width), txt_mod, sign(owner_group), sign(owner_local),
            lanes_pad(txt_mask_local), txt_qkv_mid, txt_w[0], *thick_pairs[1], txt_sum_rows,
        )
        image_low, txt_grad, cond_slices, mod_rank, shard = tail(
            d_img.reshape(2, img_half, -1), d_txt, img_w[0].reshape(n_f, k_local, -1), smalls,
            early, sides_of(1, 0), sides_of(1, 1),
            hot_four, own_hot.T.astype(BF16), mod_weight, mod_b, tmod, cond_own, slot_mask,
            n_f, n_z, fans, cols, 3,
        )
        image_grad = image_low.astype(F32)
        cond_rows = jnp.swapaxes(cond_slices[:, :slots, :k_local], 0, 1).reshape(slots, width)
        for s in range(2):
            cond_rows = cond_rows + matmul(mod_rank[2 * s : 2 * s + 2].astype(BF16), mod_a[s])
        cond_grad = jax.vjp(jax.nn.silu, conditioning)[1](cond_rows)[0]
        adapter_grad = shard.reshape(1, -1)
        return (image_out, txt_result[:txt_local], image_grad, txt_grad[:txt_local], cond_grad, adapter_grad)
    img_grad_qkv = to_tokens(d_img)
    txt_grad_qkv = txt_home(d_txt)

    img_back_mid, img_grad_norm = project_back(img_grad_qkv, img_w[0], img_pairs[1], None, False)
    grads[0][1] = (inner_left(img_back_mid, img_in), inner_left(img_qkv_mid, img_grad_qkv))
    txt_grad_norm, txt_qkv_back = give(
        inner_right(txt_grad_qkv, txt_w[0]), inner_right(txt_grad_qkv, txt_pairs[1][1])
    )
    txt_grad_norm = txt_grad_norm + matmul(txt_qkv_back, txt_pairs[1][0])
    grads[1][1] = (
        inner_left(share(txt_qkv_back), lanes(txt_in)),
        inner_left(txt_qkv_mid, txt_grad_qkv),
    )
    grad_norm = [img_grad_norm, txt_grad_norm]
    grad_inputs = []
    for s in range(2):
        grad_inputs.append(
            grad_after[s]
            + norm_back(grad_norm[s], norm_one[s][0], norm_one[s][1], stretch(s, 1))
        )
        mod_parts[s][0] = collapse(s, grad_norm[s])
        mod_parts[s][1] = collapse(s, grad_norm[s] * norm_one[s][0])
    img_dmod = jnp.concatenate(mod_parts[0], axis=1)
    txt_dmod = jnp.concatenate(mod_parts[1], axis=1)
    image_grad = unshard(grad_inputs[0].astype(BF16)).astype(F32)

    img_dmod = (img_dmod + swap_core(img_dmod)).astype(BF16)
    def lane_blocks(values):
        return jnp.swapaxes(values.reshape(values.shape[0], n_z, -1), 0, 1)

    img_dmods = jnp.concatenate(z_exchange(lane_blocks(img_dmod)), axis=0)
    img_dmods = lax.dynamic_slice_in_dim(img_dmods, core * slots, slots, 0)
    txt_dmods = sum(z_exchange(lane_blocks(txt_dmod))).astype(BF16)
    dmods = jnp.stack([img_dmods, txt_dmods], axis=1)
    dmods_all = lax.all_gather(dmods, "fsdp", axis=0, tiled=True)
    cond_part = sum(inner_right(dmods_all[:, s], mod_weight[s]) for s in range(2))
    mod_back = [inner_right(dmods[:, s], mod_b[s]) for s in range(2)]
    cond_part = cond_part.reshape(-1, width // n_f)
    joined = jnp.concatenate([cond_part.reshape(-1), jnp.stack(mod_back).reshape(-1)])
    joined = sum(z_gather(joined))
    cond_slices = joined[: cond_part.size].reshape(n_f, -1, width // n_f)
    mod_rank = joined[cond_part.size :].reshape(2, slots, -1)
    cond_rows = lax.all_to_all(cond_slices, "fsdp", 0, 2, tiled=True)[0]
    for s in range(2):
        back_mid = (mod_rank[s] * seq_mask).astype(BF16)
        cond_rows = cond_rows + matmul(back_mid, mod_a[s])
        grads[s][0] = (inner_left(back_mid, lanes(cond_act)), inner_left(mod_mid[s], dmods[:, s]))
    cond_grad = jax.vjp(jax.nn.silu, conditioning)[1](cond_rows)[0]

    def spread(values):
        return jnp.swapaxes(values.reshape(RANK, n_z, -1), 0, 1)

    img_rows = {}
    for group in ((2, 3, 4), (1,)):
        parts = [spread(grads[0][index][side]) for side in range(2) for index in group]
        parts = jnp.concatenate(z_exchange(jnp.concatenate(parts, axis=2)), axis=0)
        offset = 0
        for side, sizes in enumerate((fans, cols)):
            for index in group:
                count = sizes[index] // n_z
                img_rows[side, index] = parts[:, offset : offset + count]
                offset += count
    flat = []
    for stream in range(2):
        for index in range(5):
            if stream == 0 and index > 0:
                part_a, part_b = img_rows[0, index], img_rows[1, index]
                hot = one_hot
            else:
                part_a, part_b = grads[stream][index]
                hot = own_hot
            flat.append(
                lax.dot_general(
                    part_a, hot, (((0,), (1,)), ((), ())),
                    precision=HIGH, preferred_element_type=F32,
                )
            )
            flat.append(exact(hot, part_b).reshape(-1, 128))
    total = jnp.concatenate(flat, axis=0).reshape(n_f, -1, 128)
    step = 1
    while step < n_f:
        bit = (f // step) % 2
        pairs = total.reshape((-1, 2) + total.shape[1:])
        keep = lax.dynamic_index_in_dim(pairs, bit, 1, keepdims=False)
        send = lax.dynamic_index_in_dim(pairs, 1 - bit, 1, keepdims=False)
        sent = lax.ppermute(send.astype(BF16), "fsdp", [(i, i ^ step) for i in range(n_f)])
        total = keep + sent.astype(F32)
        step *= 2
    adapter_grad = total.reshape(1, -1)
    return (
        image_out, txt_result[:txt_local], image_grad, grad_inputs[1][:txt_local], cond_grad, adapter_grad
    )


def solution(mesh):
    return jax.shard_map(
        shards,
        mesh=mesh,
        in_specs=(
            P("fsdp", "tp", None),
            P(("fsdp", "tp"), None),
            P("fsdp", None),
            P("fsdp", None),
            P("fsdp"),
            P("tp", "fsdp"),
            P(None, "fsdp", "tp"),
            P(None, "fsdp", "tp"),
            P(None, "tp", "fsdp"),
            P(None, "fsdp", "tp"),
            P(None, "tp", "fsdp"),
            P("fsdp", "tp", None),
            P(("fsdp", "tp"), None),
        ),
        out_specs=(
            P("fsdp", "tp", None),
            P(("fsdp", "tp"), None),
            P("fsdp", "tp", None),
            P(("fsdp", "tp"), None),
            P("fsdp", None),
            P("tp", "fsdp"),
        ),
        check_vma=False,
    )
```
